32 devices in a mesh: grp: 8 (over y, x, core), rep: 4 (over z).
Axes of the slice: x: 2, y: 2, z: 4, core: 2. Of those that a mesh axis runs over, the one named last changes fastest.
Arguments:
- layer_input: bfloat16 [4, 2048, 2048], P('rep', 'grp'), may hold values from -6 to 6
- cotangent: bfloat16 [4, 2048, 2048], P('rep', 'grp'), may hold values from -6 to 6
- cut_order: int32 [4, 16], P('rep'), may hold values from 0 to 15, each once within a row
- piece_ids: int32 [4, 2048], P('rep'), may hold values from 0 to 8, as said below
- w_query: bfloat16 [2048, 2048], P('grp'), may hold values from -0.1875 to 0.1875
- w_key: bfloat16 [2048, 1024], P('grp'), may hold values from -0.1875 to 0.1875
- w_value: bfloat16 [2048, 1024], P('grp'), may hold values from -0.125 to 0.125
- w_out: bfloat16 [2048, 2048], P('grp'), may hold values from -0.5 to 0.5
- w_gate: bfloat16 [2048, 8192], P('grp'), may hold values from -0.125 to 0.125
- w_up: bfloat16 [2048, 8192], P('grp'), may hold values from -0.125 to 0.125
- w_down: bfloat16 [8192, 2048], P('grp'), may hold values from -0.125 to 0.125
- gain_attn: float32 [2048], replicated, may hold values from 0.25 to 1.75
- gain_ffn: float32 [2048], replicated, may hold values from 0.25 to 1.75
Outputs:
- layer_output: bfloat16 [4, 2048, 2048], P('rep', 'grp')
- grad_x: bfloat16 [4, 2048, 2048], P('rep', 'grp')
- grad_w_query: float32 [2048, 2048], P('grp')
- grad_w_key: float32 [2048, 1024], P('grp')
- grad_w_value: float32 [2048, 1024], P('grp')
- grad_w_out: float32 [2048, 2048], P('grp')
- grad_w_gate: float32 [2048, 8192], P('grp')
- grad_w_up: float32 [2048, 8192], P('grp')
- grad_w_down: float32 [8192, 2048], P('grp')
- grad_gain_attn: float32 [2048], P('grp')
- grad_gain_ffn: float32 [2048], P('grp')
The draws below stay inside these ranges and needn't reach their ends.
Inputs may be any that keep to these rules, and one draw needn't show every extreme that they name: `cut_order`: each row is a permutation of the 16 cut numbers. `piece_ids`: A sequence is cut into aligned runs of 256 positions; run k carries id k + 1 on all its positions if it is a picture, else 0; the last run of every sequence is a picture.
All inputs are finite; a program needn't handle non-finite values.
Results may differ from the reference program's by a relative error of at most 0.024.
Values may be sent and summed in bfloat16 or wider, within the bound.
A program may use at most 640 MiB of HBM per device.

```python
import jax
import jax.numpy as jnp
from jax import lax

D = 2048
H = 16
HD = 128
FF = 8192
LEN = 2048
PIECE = 256
KV = 1024
SEQ_ALL = 4
CUTS = 16


def draw_piece_ids(key, part):
    slot_count = LEN // PIECE
    picture_flags = jax.random.randint(jax.random.fold_in(key, 11), (SEQ_ALL, slot_count), 0, 2)
    slot_ids = jnp.arange(slot_count, dtype=jnp.int32)
    picture_flags = jnp.where(slot_ids[None, :] == slot_count - 1, 1, picture_flags)
    labels = (picture_flags * (slot_ids[None, :] + 1)).astype(jnp.int32)
    return jnp.repeat(labels, PIECE, axis=1)


def strengthened(values, key, source, target, blocks, factor):
    def block_of(axis_at):
        return (jnp.arange(values.shape[axis_at]) // (values.shape[axis_at] // blocks)).reshape((-1,) + (1,) * (values.ndim - 1 - axis_at))

    near = jax.random.permutation(key, blocks)[block_of(target)]
    second = (block_of(target) + blocks // 2) % blocks
    return jnp.where((block_of(source) == near) | (block_of(source) == second), factor * values, values)


def shard_levels(own_key, dims, cuts, low, largest):
    def one(position, parts):
        heights = jax.random.uniform(jax.random.fold_in(jax.random.fold_in(own_key, 6), position), (parts,), jnp.float32, low / len(cuts), largest / len(cuts))
        return jnp.repeat(jnp.exp(heights), dims[position] // parts).reshape((-1,) + (1,) * (len(dims) - position - 1))

    level = one(*cuts[0])
    for cut in cuts[1:]:
        level = level * one(*cut)
    return level


def noise(key, dims, scale, limit, cuts=(), held_as=jnp.bfloat16):
    level = shard_levels(key, dims, cuts, -0.22, 0.18) if cuts else 1.0
    drawn = jax.random.normal(key, dims, jnp.float32) * scale * level
    return jnp.minimum(jnp.maximum(drawn, -limit), limit).astype(held_as)


def heavy_noise(rng, extent, width, limit, cuts, heavy, held_as=jnp.bfloat16):
    result = width * jax.random.normal(rng, extent, jnp.float32)
    if cuts:
        result = result * shard_levels(rng, extent, cuts, -0.22, 0.18)
    return jnp.clip(strengthened(result, jax.random.fold_in(rng, 3), *heavy), -limit, limit).astype(held_as)


def setup_inputs(seed: int = 0) -> dict:
    key_of = jax.random.split(jax.random.key(seed), 14)
    layer_input = heavy_noise(key_of[0], (SEQ_ALL, LEN, D), 1.0, 6.0, ((0, 4), (1, 8)), (1, 2, 8, 2.0))
    cotangent = noise(key_of[1], (SEQ_ALL, LEN, D), 1.0, 6.0, ((0, 4), (1, 8)))
    cut_order = jax.vmap(lambda own: jax.random.permutation(own, CUTS))(jax.random.split(key_of[2], SEQ_ALL)).reshape((SEQ_ALL, CUTS)).astype(jnp.int32)
    piece_ids = draw_piece_ids(jax.random.fold_in(key_of[13], 71), 0)
    w_query = noise(key_of[4], (D, H * HD), (D // 2) ** -0.5, 0.1875, ((0, 8),))
    w_key = noise(key_of[5], (D, KV), (D // 2) ** -0.5, 0.1875, ((0, 8),))
    w_value = noise(key_of[6], (D, KV), D ** -0.5, 0.125, ((0, 8),))
    w_out = noise(key_of[7], (H * HD, D), (D // 16) ** -0.5, 0.5, ((0, 8),))
    w_gate = noise(key_of[8], (D, FF), D ** -0.5, 0.125, ((0, 8),))
    w_up = noise(key_of[9], (D, FF), D ** -0.5, 0.125, ((0, 8),))
    w_down = noise(key_of[10], (FF, D), (FF // 4) ** -0.5, 0.125, ((0, 8),))
    gain_attn = jnp.clip(1.0 + 0.15 * jax.random.normal(key_of[11], (D,), jnp.float32), 0.25, 1.75)
    gain_ffn = jnp.clip(1.0 + 0.15 * jax.random.normal(key_of[12], (D,), jnp.float32), 0.25, 1.75)
    return {"layer_input": layer_input, "cotangent": cotangent, "cut_order": cut_order, "piece_ids": piece_ids, "w_query": w_query, "w_key": w_key, "w_value": w_value, "w_out": w_out, "w_gate": w_gate, "w_up": w_up, "w_down": w_down, "gain_attn": gain_attn, "gain_ffn": gain_ffn}


EPS = 1e-05
ROPE_BASE = 1000000.0

@jax.custom_vjp
def low(v):
    return lax.optimization_barrier(v.astype(jnp.bfloat16)).astype(jnp.float32)

@jax.custom_vjp
def low_back(v):
    return v

def low_keep(v):
    return (low(v), None)

def low_pass(kept, grad):
    return (grad,)

def back_keep(v):
    return (v, None)

def back_low(kept, grad):
    return (low(grad),)
low.defvjp(low_keep, low_pass)
low_back.defvjp(back_keep, back_low)

def matmul_high(first, second):
    return jnp.dot(first, second, precision=lax.Precision.HIGHEST, preferred_element_type=jnp.float32)

def rms_scale(rows_in, gain):
    inv_root = lax.rsqrt(lax.optimization_barrier(jnp.mean(rows_in * rows_in, axis=-1, keepdims=True)) + EPS)
    return rows_in * inv_root * gain

def rotary(features, places):
    half_size = features.shape[-1] // 2
    inverse = ROPE_BASE ** (-(jnp.arange(half_size, dtype=jnp.float32) * 2.0) / features.shape[-1])
    angles = places.astype(jnp.float32)[:, None] * inverse[None, :]
    cosine = jnp.concatenate([jnp.cos(angles), jnp.cos(angles)], -1)[:, None, :]
    sine_table = jnp.concatenate([jnp.sin(angles), jnp.sin(angles)], -1)[:, None, :]
    turned = jnp.concatenate([-features[..., half_size:], features[..., :half_size]], -1)
    return features * cosine + turned * sine_table

def attention_ref(query, key_rows, value_rows, places, piece_of):
    length = query.shape[0]
    kv_heads = key_rows.shape[1]
    head_size = query.shape[2]
    group_size = query.shape[1] // kv_heads
    row_block = min(512, length)
    block_count = length // row_block
    score_scale = head_size ** (-0.5)
    grouped = query.reshape(block_count, row_block, kv_heads, group_size, head_size)
    query_places = places.reshape(block_count, row_block)
    query_pieces = piece_of.reshape(block_count, row_block)

    def one_block(inputs):
        block_query, block_places, block_pieces = inputs
        scores = low_back(jnp.einsum('qkgd,nkd->kgqn', block_query, key_rows, precision=lax.Precision.HIGHEST) * score_scale)
        allowed = (places[None, :] <= block_places[:, None]) | (block_pieces[:, None] != 0) & (piece_of[None, :] == block_pieces[:, None])
        scores = jnp.where(allowed[None, None], scores, -1e+30)
        row_max = lax.optimization_barrier(jnp.max(scores, axis=-1, keepdims=True))
        log_total = row_max + jnp.log(lax.optimization_barrier(jnp.sum(jnp.exp(scores - row_max), axis=-1, keepdims=True)))
        probabilities = low(jnp.exp(scores - log_total))
        mixed_heads = jnp.einsum('kgqn,nkd->qkgd', probabilities, value_rows, precision=lax.Precision.HIGHEST)
        return mixed_heads.reshape(row_block, -1)
    out_blocks = lax.map(jax.checkpoint(one_block), (grouped, query_places, query_pieces))
    return out_blocks.reshape(length, -1)

def layer_forward(x_rows, w_query, w_key, w_value, w_out, w_gate, w_up, w_down, gain_attn, gain_ffn, places, piece_of):
    length = x_rows.shape[0]
    normed_one = low(rms_scale(x_rows, gain_attn))
    query = low(rotary(low_back(matmul_high(normed_one, w_query)).reshape(length, -1, HD), places))
    key_rows = low(rotary(low_back(matmul_high(normed_one, w_key)).reshape(length, -1, HD), places))
    value_rows = low(low_back(matmul_high(normed_one, w_value))).reshape(length, -1, HD)
    attended = low(low_back(attention_ref(query, key_rows, value_rows, places, piece_of)))
    residual_mid = x_rows + low_back(matmul_high(attended, w_out))
    normed_two = low(rms_scale(residual_mid, gain_ffn))
    gate_proj = low_back(matmul_high(normed_two, w_gate))
    up_proj = low_back(matmul_high(normed_two, w_up))
    hidden = low(jax.nn.silu(gate_proj) * up_proj)
    return residual_mid + low_back(matmul_high(hidden, w_down))

def reference(layer_input, cotangent, cut_order, piece_ids, w_query, w_key, w_value, w_out, w_gate, w_up, w_down, gain_attn, gain_ffn):
    weights = tuple((weight.astype(jnp.float32) for weight in (w_query, w_key, w_value, w_out, w_gate, w_up, w_down, gain_attn, gain_ffn)))
    length = layer_input.shape[1]
    cut_len = length // cut_order.shape[1]
    rows_all = jnp.arange(length, dtype=jnp.int32)

    def one_sequence(totals, inputs):
        x_seq, grad_seq, order_seq, piece_seq = inputs
        places = (order_seq[rows_all // cut_len] * cut_len + rows_all % cut_len).astype(jnp.int32)
        piece_of = piece_seq[places]

        def forward_fn(x_rows, *params):
            return layer_forward(x_rows, *params, places, piece_of)
        output_rows, pull_back = jax.vjp(forward_fn, x_seq.astype(jnp.float32), *weights)
        grads_all = pull_back(grad_seq.astype(jnp.float32))
        totals = tuple((held + fresh for held, fresh in zip(totals, grads_all[1:])))
        return (totals, (output_rows.astype(jnp.bfloat16), grads_all[0].astype(jnp.bfloat16)))
    zeros_all = tuple((jnp.zeros(weight.shape, jnp.float32) for weight in weights))
    totals, (outputs, grad_inputs) = lax.scan(one_sequence, zeros_all, (layer_input, cotangent, cut_order, piece_ids))
    return (outputs, grad_inputs, totals[0], totals[1], totals[2], totals[3], totals[4], totals[5], totals[6], totals[7], totals[8])
```

```python
import functools

import jax
import jax.numpy as jnp
from jax import lax
from jax.experimental import pallas as pl
from jax.experimental.pallas import tpu as pltpu
from jax.sharding import PartitionSpec as P

HD = 128
EPS = 1e-05
ROPE_BASE = 1000000.0
SCORE_SCALE = HD**-0.5
LOG2E = 1.4426950408889634
TO_EXP2 = SCORE_SCALE * LOG2E
NEG = -1e30

f32 = jnp.float32
bf16 = jnp.bfloat16


def matmul_f32(first, second):
    return jnp.dot(first, second, preferred_element_type=f32)


def against_rows(first, second):
    return lax.dot_general(first, second, (((1,), (1,)), ((), ())), preferred_element_type=f32)


def over_tokens(first, second):
    return lax.dot_general(first, second, (((0,), (0,)), ((), ())), preferred_element_type=f32)


def turn_tables(length):
    half_size = HD // 2
    inverse = ROPE_BASE ** (-(jnp.arange(half_size, dtype=f32) * 2.0) / HD)
    angles = jnp.arange(length, dtype=jnp.int32).astype(f32)[:, None] * inverse
    cosine, sine = jnp.cos(angles), jnp.sin(angles)
    return jnp.concatenate([cosine, cosine], -1), jnp.concatenate([-sine, sine], -1)


def norm_back(upstream, grad_normed, unit_rows, inv_root, gain):
    scaled = grad_normed * gain
    center_term = jnp.mean(scaled * unit_rows, -1, keepdims=True)
    return (
        upstream + inv_root * (scaled - unit_rows * center_term),
        jnp.sum(grad_normed * unit_rows, 0),
    )


def fold_lanes(values, op):
    out = values[:, :HD]
    for at in range(HD, values.shape[1], HD):
        out = op(out, values[:, at : at + HD])
    return out


def as_row(column):
    return jnp.broadcast_to(column, (column.shape[0], HD)).T[0:1, :]


def attend_kernel(
    heads, cuts, block,
    order_ref, qkv_ref, cos_ref, sin_ref, piece_ref, piece_col_ref,
    out_ref, q_ref, k_ref, v_ref, lse_ref,
    scores, placed,
):
    length = qkv_ref.shape[0]
    cut = length // cuts
    blocks = length // block

    def place_cut(r, _):
        src = pl.ds(pl.multiple_of(r * cut, cut), cut)
        dst = pl.ds(pl.multiple_of(order_ref[0, r] * cut, cut), cut)
        cosine, sine = cos_ref[dst, :], sin_ref[dst, :]
        for h in range(heads + 1):
            part = qkv_ref[src, h * HD : (h + 1) * HD]
            turned = (part * cosine + pltpu.roll(part, HD // 2, 1) * sine).astype(bf16)
            if h < heads:
                q_ref[h, dst, :] = turned
            else:
                k_ref[dst, :] = turned
        v_ref[dst, :] = qkv_ref[src, (heads + 1) * HD :].astype(bf16)
        return 0

    lax.fori_loop(0, cuts, place_cut, 0)

    def one_block(i, _):
        rows = pl.ds(pl.multiple_of(i * block, block), block)
        query = q_ref[:, rows, :].reshape(heads * block, HD)

        def score(j, high):
            cols = pl.ds(pl.multiple_of(j * block, block), block)
            tile = against_rows(query, k_ref[cols, :])
            scores[j] = tile
            return jnp.maximum(high, fold_lanes(tile, jnp.maximum))

        high = lax.fori_loop(0, i, score, jnp.full((heads * block, HD), NEG, f32))
        tile = against_rows(query, k_ref[rows, :])
        q_at = lax.broadcasted_iota(jnp.int32, (block, block), 0)
        k_at = lax.broadcasted_iota(jnp.int32, (block, block), 1)
        q_piece, k_piece = piece_col_ref[rows, 0:1], piece_ref[0:1, rows]
        allowed = (k_at <= q_at) | ((q_piece != 0) & (q_piece == k_piece))
        tile = jnp.concatenate(
            [jnp.where(allowed, tile[h * block : (h + 1) * block], NEG) for h in range(heads)], 0
        )
        scores[i] = tile
        high = jnp.max(jnp.maximum(high, fold_lanes(tile, jnp.maximum)), 1, keepdims=True)

        def weigh(j, state):
            total, mixed = state
            cols = pl.ds(pl.multiple_of(j * block, block), block)
            prob = jnp.exp2((scores[j] - high) * TO_EXP2)
            total = total + fold_lanes(prob, jnp.add)
            return total, mixed + matmul_f32(prob.astype(bf16), v_ref[cols, :])

        zero = jnp.zeros((heads * block, HD), f32)
        total, mixed = lax.fori_loop(0, i + 1, weigh, (zero, zero))
        total = jnp.sum(total, 1, keepdims=True)
        mixed = (mixed / total).astype(bf16)
        log_total = high * TO_EXP2 + jnp.log2(total)
        for h in range(heads):
            placed[rows, h * HD : (h + 1) * HD] = mixed[h * block : (h + 1) * block]
            lse_ref[h : h + 1, rows] = as_row(log_total[h * block : (h + 1) * block])
        return 0

    lax.fori_loop(0, blocks, one_block, 0)

    def store_cut(r, _):
        dst = pl.ds(pl.multiple_of(r * cut, cut), cut)
        src = pl.ds(pl.multiple_of(order_ref[0, r] * cut, cut), cut)
        out_ref[dst, :] = placed[src, :]
        return 0

    lax.fori_loop(0, cuts, store_cut, 0)


def vmem_specs(count):
    return [pl.BlockSpec(memory_space=pltpu.VMEM)] * count


def attend(order, qkv, cosine, sine, piece, piece_col, heads):
    length = qkv.shape[0]
    block = min(512, length)
    return pl.pallas_call(
        functools.partial(attend_kernel, heads, order.shape[1], block),
        out_shape=(
            jax.ShapeDtypeStruct((length, heads * HD), bf16),
            jax.ShapeDtypeStruct((heads, length, HD), bf16),
            jax.ShapeDtypeStruct((length, HD), bf16),
            jax.ShapeDtypeStruct((length, HD), bf16),
            jax.ShapeDtypeStruct((heads, length), f32),
        ),
        in_specs=[pl.BlockSpec(memory_space=pltpu.SMEM)] + vmem_specs(5),
        out_specs=tuple(vmem_specs(5)),
        scratch_shapes=[
            pltpu.VMEM((length // block, heads * block, block), f32),
            pltpu.VMEM((length, heads * HD), bf16),
        ],
        compiler_params=pltpu.CompilerParams(vmem_limit_bytes=48 * 2**20),
        cost_estimate=pl.CostEstimate(
            flops=3 * heads * length * length * HD, bytes_accessed=10 * length * HD * heads * 4,
            transcendentals=heads * length * length // 2,
        ),
    )(order, qkv, cosine, sine, piece, piece_col)


def attend_back_kernel(
    heads, cuts, block,
    order_ref, grad_ref, out_ref, q_ref, k_ref, v_ref, lse_ref, cos_ref, sin_ref,
    piece_ref, piece_col_ref,
    grad_qkv_ref,
    grads, centers, grad_q, placed,
):
    length = grad_ref.shape[0]
    cut = length // cuts
    blocks = length // block

    def place_cut(r, _):
        src = pl.ds(pl.multiple_of(r * cut, cut), cut)
        dst = pl.ds(pl.multiple_of(order_ref[0, r] * cut, cut), cut)
        for h in range(heads):
            grad = grad_ref[src, h * HD : (h + 1) * HD].astype(bf16)
            grads[h, dst, :] = grad
            product = grad.astype(f32) * out_ref[src, h * HD : (h + 1) * HD].astype(f32)
            centers[h, dst, :] = jnp.broadcast_to(
                jnp.sum(product, 1, keepdims=True), (cut, HD)
            )
        return 0

    lax.fori_loop(0, cuts, place_cut, 0)
    grad_q[...] = jnp.zeros_like(grad_q)

    def key_block(j, _):
        cols = pl.ds(pl.multiple_of(j * block, block), block)
        key, value = k_ref[cols, :], v_ref[cols, :]

        def one(i, state, diagonal):
            grad_key, grad_value = state
            rows = pl.ds(pl.multiple_of(i * block, block), block)
            for h in range(heads):
                query, grad = q_ref[h, rows, :], grads[h, rows, :]
                log_total = lse_ref[h : h + 1, rows]
                center = centers[h, rows, :].T[0:1, :]
                prob = jnp.exp2(against_rows(key, query) * TO_EXP2 - log_total)
                if diagonal:
                    k_at = lax.broadcasted_iota(jnp.int32, (block, block), 0)
                    q_at = lax.broadcasted_iota(jnp.int32, (block, block), 1)
                    k_piece, q_piece = piece_col_ref[cols, 0:1], piece_ref[0:1, cols]
                    allowed = (k_at <= q_at) | ((q_piece != 0) & (q_piece == k_piece))
                    prob = jnp.where(allowed, prob, 0.0)
                grad_prob = against_rows(value, grad)
                grad_score = (prob * (grad_prob - center)).astype(bf16)
                grad_value = grad_value + matmul_f32(prob.astype(bf16), grad)
                grad_key = grad_key + matmul_f32(grad_score, query)
                grad_q[h, rows, :] += over_tokens(grad_score, key)
            return grad_key, grad_value

        zero = jnp.zeros((block, HD), f32)
        state = one(j, (zero, zero), True)
        grad_key, grad_value = lax.fori_loop(
            j + 1, blocks, functools.partial(one, diagonal=False), state
        )
        grad_key = grad_key * SCORE_SCALE
        grad_key = grad_key * cos_ref[cols, :] - pltpu.roll(grad_key, HD // 2, 1) * sin_ref[cols, :]
        placed[cols, heads * HD : (heads + 1) * HD] = grad_key.astype(bf16)
        placed[cols, (heads + 1) * HD :] = grad_value.astype(bf16)
        return 0

    lax.fori_loop(0, blocks, key_block, 0)

    def store_cut(r, _):
        dst = pl.ds(pl.multiple_of(r * cut, cut), cut)
        src = pl.ds(pl.multiple_of(order_ref[0, r] * cut, cut), cut)
        for h in range(heads):
            grad = grad_q[h, src, :] * SCORE_SCALE
            grad = grad * cos_ref[src, :] - pltpu.roll(grad, HD // 2, 1) * sin_ref[src, :]
            grad_qkv_ref[dst, h * HD : (h + 1) * HD] = grad.astype(bf16)
        grad_qkv_ref[dst, heads * HD :] = placed[src, heads * HD :]
        return 0

    lax.fori_loop(0, cuts, store_cut, 0)


def attend_back(order, grad, out, query, key, value, lse, cosine, sine, piece, piece_col, heads):
    length = grad.shape[0]
    block = min(512, length)
    return pl.pallas_call(
        functools.partial(attend_back_kernel, heads, order.shape[1], block),
        out_shape=jax.ShapeDtypeStruct((length, (heads + 2) * HD), bf16),
        in_specs=[pl.BlockSpec(memory_space=pltpu.SMEM)] + vmem_specs(10),
        out_specs=pl.BlockSpec(memory_space=pltpu.VMEM),
        scratch_shapes=[
            pltpu.VMEM((heads, length, HD), bf16),
            pltpu.VMEM((heads, length, HD), f32),
            pltpu.VMEM((heads, length, HD), f32),
            pltpu.VMEM((length, (heads + 2) * HD), bf16),
        ],
        compiler_params=pltpu.CompilerParams(vmem_limit_bytes=48 * 2**20),
        cost_estimate=pl.CostEstimate(
            flops=8 * heads * length * length * HD, bytes_accessed=14 * length * HD * heads * 4,
            transcendentals=heads * length * length // 2,
        ),
    )(order, grad, out, query, key, value, lse, cosine, sine, piece, piece_col)


def sum_over_sequences(term, reps):
    if reps != 4:
        return lax.psum(term, "rep").astype(f32)
    rank = lax.axis_index("rep")
    inward = lax.ppermute(term, "rep", [(0, 1), (3, 2)])
    pair = (term.astype(f32) + inward.astype(f32)).astype(bf16)
    other = lax.ppermute(pair, "rep", [(1, 2), (2, 1)])
    total = (pair.astype(f32) + other.astype(f32)).astype(bf16)
    outward = lax.ppermute(total, "rep", [(1, 0), (2, 3)])
    return jnp.where((rank == 0) | (rank == 3), outward, total).astype(f32)


def on_device(
    layer_input,
    cotangent,
    cut_order,
    piece_ids,
    w_query,
    w_key,
    w_value,
    w_out,
    w_gate,
    w_up,
    w_down,
    gain_attn,
    gain_ffn,
):
    groups = lax.axis_size("grp")
    reps = lax.axis_size("rep")
    own_index = lax.axis_index("grp")
    _, local_rows, model_width = layer_input.shape
    length = piece_ids.shape[1]
    rows_here = w_query.shape[0]
    q_width = w_query.shape[1]
    kv_heads = w_key.shape[1] // HD
    heads = q_width // HD // groups
    copies = groups // kv_heads
    hidden_here = w_down.shape[0]
    piece_col = jnp.broadcast_to(piece_ids.reshape(length, 1), (length, HD))
    cosine, sine = turn_tables(length)

    def gather(rows):
        return lax.all_gather(rows, "grp", axis=0, tiled=True)

    def scatter(terms):
        return lax.psum_scatter(terms.astype(bf16), "grp", scatter_dimension=0, tiled=True)

    def to_columns(parts):
        return lax.all_to_all(parts, "grp", 1, 0, tiled=True).reshape(-1, parts.shape[-1])

    def per_group(weight):
        return weight.reshape(rows_here, groups, -1)

    def per_kv_head(weight):
        return jnp.repeat(weight.reshape(rows_here, kv_heads, HD), copies, axis=1)

    x_flat = layer_input.reshape(local_rows, model_width).astype(f32)
    inv_one = lax.rsqrt(jnp.mean(x_flat * x_flat, -1, keepdims=True) + EPS)
    unit_one = x_flat * inv_one
    normed_one = gather((unit_one * gain_attn).astype(bf16))
    cols_qkv = to_columns(
        jnp.concatenate([per_group(w_query), per_kv_head(w_key), per_kv_head(w_value)], -1)
    )
    qkv = matmul_f32(normed_one, cols_qkv)
    attended, query, key, value, lse = attend(
        cut_order, qkv, cosine, sine, piece_ids, piece_col, heads
    )
    cols_gate_up = to_columns(jnp.concatenate([per_group(w_gate), per_group(w_up)], -1))
    mid = x_flat + scatter(matmul_f32(attended, w_out)).astype(f32)
    inv_two = lax.rsqrt(jnp.mean(mid * mid, -1, keepdims=True) + EPS)
    unit_two = mid * inv_two
    normed_two = gather((unit_two * gain_ffn).astype(bf16))
    grad_out = cotangent.reshape(local_rows, model_width)
    grad_all = gather(grad_out)
    gate_up = matmul_f32(normed_two, cols_gate_up)
    gate_proj, up_proj = gate_up[:, :hidden_here], gate_up[:, hidden_here:]
    sigmoid_gate = jax.nn.sigmoid(gate_proj)
    swish = gate_proj * sigmoid_gate
    hidden = (swish * up_proj).astype(bf16)
    down_term = sum_over_sequences(over_tokens(hidden, grad_all).astype(bf16), reps)
    grad_hidden = against_rows(grad_all, w_down)
    grad_gate = (
        grad_hidden * up_proj * sigmoid_gate * (1.0 + gate_proj * (1.0 - sigmoid_gate))
    ).astype(bf16)
    grad_up = (grad_hidden * swish).astype(bf16)
    grad_gate_up = jnp.concatenate([grad_gate, grad_up], 1)
    grad_two = scatter(against_rows(grad_gate_up, cols_gate_up)).astype(f32)
    grad_mid, gain_ffn_term = norm_back(
        grad_out.astype(f32), grad_two, unit_two, inv_two, gain_ffn
    )
    grad_mid_low = gather(grad_mid.astype(bf16))
    grad_attended = against_rows(grad_mid_low, w_out).astype(bf16)

    def to_rows(term):
        return lax.all_to_all(
            term.astype(bf16).reshape(groups, rows_here, -1), "grp", 0, 0, tiled=True
        )

    gate_up_term = sum_over_sequences(to_rows(over_tokens(normed_two, grad_gate_up)), reps)
    result = (mid + scatter(matmul_f32(hidden, w_down)).astype(f32)).astype(bf16)
    grad_qkv = attend_back(
        cut_order, grad_attended, attended, query, key, value, lse, cosine, sine,
        piece_ids, piece_col, heads,
    )
    out_term = sum_over_sequences(over_tokens(attended, grad_mid_low).astype(bf16), reps)
    qkv_term = sum_over_sequences(to_rows(over_tokens(normed_one, grad_qkv)), reps)
    grad_one = scatter(against_rows(grad_qkv, cols_qkv)).astype(f32)
    grad_input, gain_attn_term = norm_back(grad_mid, grad_one, unit_one, inv_one, gain_attn)
    gain_total = lax.psum(jnp.stack([gain_attn_term, gain_ffn_term]), ("grp", "rep"))
    own_gains = lax.dynamic_slice_in_dim(gain_total, own_index * rows_here, rows_here, 1)

    def whole_rows(term):
        return jnp.moveaxis(term, 0, 1).reshape(rows_here, -1)

    def kv_rows(term):
        return jnp.sum(
            jnp.moveaxis(term, 0, 1).reshape(rows_here, kv_heads, copies, HD), 2
        ).reshape(rows_here, -1)

    q_here = heads * HD
    return (
        result.reshape(layer_input.shape),
        grad_input.astype(bf16).reshape(layer_input.shape),
        whole_rows(qkv_term[..., :q_here]),
        kv_rows(qkv_term[..., q_here : q_here + HD]),
        kv_rows(qkv_term[..., q_here + HD :]),
        out_term,
        whole_rows(gate_up_term[..., :hidden_here]),
        whole_rows(gate_up_term[..., hidden_here:]),
        down_term,
        own_gains[0],
        own_gains[1],
    )


def solution(mesh):
    tokens, table, rows, whole = P("rep", "grp", None), P("rep", None), P("grp", None), P()
    return jax.shard_map(
        on_device,
        mesh=mesh,
        in_specs=(tokens, tokens, table, table) + (rows,) * 7 + (whole,) * 2,
        out_specs=(tokens, tokens) + (rows,) * 7 + (P("grp"),) * 2,
        check_vma=False,
    )
```

```python
import functools

import jax
import jax.numpy as jnp
from jax import lax
from jax.experimental import pallas as pl
from jax.experimental.pallas import tpu as pltpu
from jax.sharding import PartitionSpec as P

HD = 128
EPS = 1e-05
ROPE_BASE = 1000000.0
SCORE_SCALE = HD**-0.5
LOG2E = 1.4426950408889634
TO_EXP2 = SCORE_SCALE * LOG2E
NEG = -1e30

f32 = jnp.float32
bf16 = jnp.bfloat16


def matmul_f32(first, second):
    return jnp.dot(first, second, preferred_element_type=f32)


def against_rows(first, second):
    return lax.dot_general(first, second, (((1,), (1,)), ((), ())), preferred_element_type=f32)


def over_tokens(first, second):
    return lax.dot_general(first, second, (((0,), (0,)), ((), ())), preferred_element_type=f32)


def turn_tables(length):
    half_size = HD // 2
    inverse = ROPE_BASE ** (-(jnp.arange(half_size, dtype=f32) * 2.0) / HD)
    angles = jnp.arange(length, dtype=jnp.int32).astype(f32)[:, None] * inverse
    cosine, sine = jnp.cos(angles), jnp.sin(angles)
    return jnp.concatenate([cosine, cosine], -1), jnp.concatenate([-sine, sine], -1)


def norm_back(upstream, grad_normed, unit_rows, inv_root, gain):
    scaled = grad_normed * gain
    center_term = jnp.mean(scaled * unit_rows, -1, keepdims=True)
    return (
        upstream + inv_root * (scaled - unit_rows * center_term),
        jnp.sum(grad_normed * unit_rows, 0),
    )


def fold_lanes(values, op):
    out = values[:, :HD]
    for at in range(HD, values.shape[1], HD):
        out = op(out, values[:, at : at + HD])
    return out


def as_row(column):
    return jnp.broadcast_to(column, (column.shape[0], HD)).T[0:1, :]


def attend_kernel(
    heads, cuts, block,
    order_ref, qkv_ref, cos_ref, sin_ref, piece_ref, piece_col_ref,
    out_ref, q_ref, k_ref, v_ref, lse_ref,
    scores, placed,
):
    length = qkv_ref.shape[0]
    cut = length // cuts
    blocks = length // block

    def place_cut(r, _):
        src = pl.ds(pl.multiple_of(r * cut, cut), cut)
        dst = pl.ds(pl.multiple_of(order_ref[0, r] * cut, cut), cut)
        cosine, sine = cos_ref[dst, :], sin_ref[dst, :]
        for h in range(heads + 1):
            part = qkv_ref[src, h * HD : (h + 1) * HD]
            turned = (part * cosine + pltpu.roll(part, HD // 2, 1) * sine).astype(bf16)
            if h < heads:
                q_ref[h, dst, :] = turned
            else:
                k_ref[dst, :] = turned
        v_ref[dst, :] = qkv_ref[src, (heads + 1) * HD :].astype(bf16)
        return 0

    lax.fori_loop(0, cuts, place_cut, 0)

    def one_block(i, _):
        rows = pl.ds(pl.multiple_of(i * block, block), block)
        query = q_ref[:, rows, :].reshape(heads * block, HD)

        def score(j, high):
            cols = pl.ds(pl.multiple_of(j * block, block), block)
            tile = against_rows(query, k_ref[cols, :])
            scores[j] = tile
            return jnp.maximum(high, fold_lanes(tile, jnp.maximum))

        high = lax.fori_loop(0, i, score, jnp.full((heads * block, HD), NEG, f32))
        tile = against_rows(query, k_ref[rows, :])
        q_at = lax.broadcasted_iota(jnp.int32, (block, block), 0)
        k_at = lax.broadcasted_iota(jnp.int32, (block, block), 1)
        q_piece, k_piece = piece_col_ref[rows, 0:1], piece_ref[0:1, rows]
        allowed = (k_at <= q_at) | ((q_piece != 0) & (q_piece == k_piece))
        tile = jnp.concatenate(
            [jnp.where(allowed, tile[h * block : (h + 1) * block], NEG) for h in range(heads)], 0
        )
        scores[i] = tile
        high = jnp.max(jnp.maximum(high, fold_lanes(tile, jnp.maximum)), 1, keepdims=True)

        def weigh(j, state):
            total, mixed = state
            cols = pl.ds(pl.multiple_of(j * block, block), block)
            prob = jnp.exp2((scores[j] - high) * TO_EXP2)
            total = total + fold_lanes(prob, jnp.add)
            return total, mixed + matmul_f32(prob.astype(bf16), v_ref[cols, :])

        zero = jnp.zeros((heads * block, HD), f32)
        total, mixed = lax.fori_loop(0, i + 1, weigh, (zero, zero))
        total = jnp.sum(total, 1, keepdims=True)
        mixed = (mixed / total).astype(bf16)
        log_total = high * TO_EXP2 + jnp.log2(total)
        for h in range(heads):
            placed[rows, h * HD : (h + 1) * HD] = mixed[h * block : (h + 1) * block]
            lse_ref[h : h + 1, rows] = as_row(log_total[h * block : (h + 1) * block])
        return 0

    lax.fori_loop(0, blocks, one_block, 0)

    def store_cut(r, _):
        dst = pl.ds(pl.multiple_of(r * cut, cut), cut)
        src = pl.ds(pl.multiple_of(order_ref[0, r] * cut, cut), cut)
        out_ref[dst, :] = placed[src, :]
        return 0

    lax.fori_loop(0, cuts, store_cut, 0)


def vmem_specs(count):
    return [pl.BlockSpec(memory_space=pltpu.VMEM)] * count


def attend(order, qkv, cosine, sine, piece, piece_col, heads):
    length = qkv.shape[0]
    block = min(512, length)
    return pl.pallas_call(
        functools.partial(attend_kernel, heads, order.shape[1], block),
        out_shape=(
            jax.ShapeDtypeStruct((length, heads * HD), bf16),
            jax.ShapeDtypeStruct((heads, length, HD), bf16),
            jax.ShapeDtypeStruct((length, HD), bf16),
            jax.ShapeDtypeStruct((length, HD), bf16),
            jax.ShapeDtypeStruct((heads, length), f32),
        ),
        in_specs=[pl.BlockSpec(memory_space=pltpu.SMEM)] + vmem_specs(5),
        out_specs=tuple(vmem_specs(5)),
        scratch_shapes=[
            pltpu.VMEM((length // block, heads * block, block), f32),
            pltpu.VMEM((length, heads * HD), bf16),
        ],
        compiler_params=pltpu.CompilerParams(vmem_limit_bytes=48 * 2**20),
        cost_estimate=pl.CostEstimate(
            flops=3 * heads * length * length * HD, bytes_accessed=10 * length * HD * heads * 4,
            transcendentals=heads * length * length // 2,
        ),
    )(order, qkv, cosine, sine, piece, piece_col)


def attend_back_kernel(
    heads, cuts, block,
    order_ref, grad_ref, out_ref, q_ref, k_ref, v_ref, lse_ref, cos_ref, sin_ref,
    piece_ref, piece_col_ref,
    grad_qkv_ref,
    grads, centers, grad_q, placed,
):
    length = grad_ref.shape[0]
    cut = length // cuts
    blocks = length // block

    def place_cut(r, _):
        src = pl.ds(pl.multiple_of(r * cut, cut), cut)
        dst = pl.ds(pl.multiple_of(order_ref[0, r] * cut, cut), cut)
        for h in range(heads):
            grad = grad_ref[src, h * HD : (h + 1) * HD].astype(bf16)
            grads[h, dst, :] = grad
            product = grad.astype(f32) * out_ref[src, h * HD : (h + 1) * HD].astype(f32)
            centers[h, dst, :] = jnp.broadcast_to(
                jnp.sum(product, 1, keepdims=True), (cut, HD)
            )
        return 0

    lax.fori_loop(0, cuts, place_cut, 0)
    grad_q[...] = jnp.zeros_like(grad_q)

    def key_block(j, _):
        cols = pl.ds(pl.multiple_of(j * block, block), block)
        key, value = k_ref[cols, :], v_ref[cols, :]

        def one(i, state, diagonal):
            grad_key, grad_value = state
            rows = pl.ds(pl.multiple_of(i * block, block), block)
            for h in range(heads):
                query, grad = q_ref[h, rows, :], grads[h, rows, :]
                log_total = lse_ref[h : h + 1, rows]
                center = centers[h, rows, :].T[0:1, :]
                prob = jnp.exp2(against_rows(key, query) * TO_EXP2 - log_total)
                if diagonal:
                    k_at = lax.broadcasted_iota(jnp.int32, (block, block), 0)
                    q_at = lax.broadcasted_iota(jnp.int32, (block, block), 1)
                    k_piece, q_piece = piece_col_ref[cols, 0:1], piece_ref[0:1, cols]
                    allowed = (k_at <= q_at) | ((q_piece != 0) & (q_piece == k_piece))
                    prob = jnp.where(allowed, prob, 0.0)
                grad_prob = against_rows(value, grad)
                grad_score = (prob * (grad_prob - center)).astype(bf16)
                grad_value = grad_value + matmul_f32(prob.astype(bf16), grad)
                grad_key = grad_key + matmul_f32(grad_score, query)
                grad_q[h, rows, :] += over_tokens(grad_score, key)
            return grad_key, grad_value

        zero = jnp.zeros((block, HD), f32)
        state = one(j, (zero, zero), True)
        grad_key, grad_value = lax.fori_loop(
            j + 1, blocks, functools.partial(one, diagonal=False), state
        )
        grad_key = grad_key * SCORE_SCALE
        grad_key = grad_key * cos_ref[cols, :] - pltpu.roll(grad_key, HD // 2, 1) * sin_ref[cols, :]
        placed[cols, heads * HD : (heads + 1) * HD] = grad_key.astype(bf16)
        placed[cols, (heads + 1) * HD :] = grad_value.astype(bf16)
        return 0

    lax.fori_loop(0, blocks, key_block, 0)

    def store_cut(r, _):
        dst = pl.ds(pl.multiple_of(r * cut, cut), cut)
        src = pl.ds(pl.multiple_of(order_ref[0, r] * cut, cut), cut)
        for h in range(heads):
            grad = grad_q[h, src, :] * SCORE_SCALE
            grad = grad * cos_ref[src, :] - pltpu.roll(grad, HD // 2, 1) * sin_ref[src, :]
            grad_qkv_ref[dst, h * HD : (h + 1) * HD] = grad.astype(bf16)
        grad_qkv_ref[dst, heads * HD :] = placed[src, heads * HD :]
        return 0

    lax.fori_loop(0, cuts, store_cut, 0)


def attend_back(order, grad, out, query, key, value, lse, cosine, sine, piece, piece_col, heads):
    length = grad.shape[0]
    block = min(512, length)
    return pl.pallas_call(
        functools.partial(attend_back_kernel, heads, order.shape[1], block),
        out_shape=jax.ShapeDtypeStruct((length, (heads + 2) * HD), bf16),
        in_specs=[pl.BlockSpec(memory_space=pltpu.SMEM)] + vmem_specs(10),
        out_specs=pl.BlockSpec(memory_space=pltpu.VMEM),
        scratch_shapes=[
            pltpu.VMEM((heads, length, HD), bf16),
            pltpu.VMEM((heads, length, HD), f32),
            pltpu.VMEM((heads, length, HD), f32),
            pltpu.VMEM((length, (heads + 2) * HD), bf16),
        ],
        compiler_params=pltpu.CompilerParams(vmem_limit_bytes=48 * 2**20),
        cost_estimate=pl.CostEstimate(
            flops=8 * heads * length * length * HD, bytes_accessed=14 * length * HD * heads * 4,
            transcendentals=heads * length * length // 2,
        ),
    )(order, grad, out, query, key, value, lse, cosine, sine, piece, piece_col)


MESH = pl.DeviceIdType.MESH


def place_in_group():
    me = lax.axis_index("grp")
    return me // 4, (me // 2) % 2, me % 2


def other(flip_y, flip_x, flip_core):
    y, x, core = place_in_group()
    return ((y + flip_y) % 2) * 4 + ((x + flip_x) % 2) * 2 + (core + flip_core) % 2


def chip_rows(flip_y, flip_x, rows):
    y, x, _ = place_in_group()
    first = (((y + flip_y) % 2) * 2 + (x + flip_x) % 2) * (2 * rows)
    return pl.ds(pl.multiple_of(first, 2 * rows), 2 * rows)


def greet_group():
    barrier = pltpu.get_barrier_semaphore()
    for flips in ((0, 0, 1), (0, 1, 0), (1, 0, 0)):
        pl.semaphore_signal(barrier, inc=1, device_id={"grp": other(*flips)}, device_id_type=MESH)
    pl.semaphore_wait(barrier, 3)


SIBLING, ALONG_X, ALONG_Y, ACROSS = (0, 0), (0, 1), (1, 0), (1, 1)


def gather_rows(rows, all_ref, sends, recvs, on_chip):
    half = rows // 2

    def block(chip, core, part=None):
        first = other(*chip, core) * rows
        if part is None:
            return pl.ds(pl.multiple_of(first, rows), rows)
        return pl.ds(pl.multiple_of(first + part * half, half), half)

    def copy(number, chip, core, part, target):
        where = all_ref.at[block(chip, core, part), :]
        return pltpu.make_async_remote_copy(
            src_ref=where, dst_ref=where, send_sem=sends.at[number], recv_sem=recvs.at[number],
            device_id={"grp": other(*target)}, device_id_type=MESH,
        )

    def landed(number, chip, core, part):
        where = all_ref.at[block(chip, core, part), :]
        pltpu.make_async_remote_copy(
            src_ref=where, dst_ref=where, send_sem=sends.at[number], recv_sem=recvs.at[number],
            device_id={"grp": other(0, 0, 1)}, device_id_type=MESH,
        ).wait_recv()

    to_s, to_x, to_y = (0, 0, 1), (0, 1, 0), (1, 0, 0)
    started = []

    def send(*what):
        one = copy(*what)
        one.start()
        started.append(one)

    send(1, SIBLING, 0, 1, to_x)
    send(3, SIBLING, 0, 0, to_y)
    send(0, SIBLING, 0, None, to_s)
    send(2, SIBLING, 0, 0, to_x)
    send(4, SIBLING, 0, 1, to_y)
    landed(0, SIBLING, 1, None)
    on_chip(*SIBLING)
    landed(1, ALONG_X, 0, 1)
    send(6, ALONG_X, 0, 1, to_y)
    landed(3, ALONG_Y, 0, 0)
    send(5, ALONG_Y, 0, 0, to_x)
    send(7, ALONG_X, 0, 1, to_s)
    send(8, ALONG_Y, 0, 0, to_s)
    landed(2, ALONG_X, 0, 0)
    send(9, ALONG_X, 0, 0, to_s)
    landed(4, ALONG_Y, 0, 1)
    send(10, ALONG_Y, 0, 1, to_s)
    landed(7, ALONG_X, 1, 1)
    landed(9, ALONG_X, 1, 0)
    on_chip(*ALONG_X)
    landed(5, ACROSS, 0, 0)
    send(11, ACROSS, 0, 0, to_s)
    landed(6, ACROSS, 0, 1)
    send(12, ACROSS, 0, 1, to_s)
    landed(8, ALONG_Y, 1, 0)
    landed(10, ALONG_Y, 1, 1)
    on_chip(*ALONG_Y)
    landed(11, ACROSS, 1, 0)
    landed(12, ACROSS, 1, 1)
    on_chip(*ACROSS)
    for one in started:
        one.wait_send()


GATHER_COPIES = 13


def rms_normed(values, gain):
    return values * lax.rsqrt(jnp.mean(values * values, -1, keepdims=True) + EPS) * gain


class Moves:
    def __init__(self, sems):
        self.sems, self.count, self.open = sems, 0, []

    def start(self, src, dst):
        one = pltpu.make_async_copy(src, dst, self.sems.at[self.count])
        self.count += 1
        one.start()
        return one

    def later(self, src, dst):
        self.open.append(self.start(src, dst))

    def finish(self):
        for one in self.open:
            one.wait()


def comm_params(number, vmem=56):
    return pltpu.CompilerParams(
        collective_id=number, has_side_effects=True, vmem_limit_bytes=vmem * 2**20
    )


def gather_scratch(rows, width, moves):
    return [
        pltpu.VMEM((8 * rows, width), bf16),
        pltpu.SemaphoreType.DMA((GATHER_COPIES,)),
        pltpu.SemaphoreType.DMA((GATHER_COPIES,)),
        pltpu.SemaphoreType.DMA((moves,)),
    ]


def any_specs(count):
    return [pl.BlockSpec(memory_space=pl.ANY)] * count


def own_rows(rows):
    return pl.ds(pl.multiple_of(other(0, 0, 0) * rows, rows), rows)


def gather_normed_kernel(x_ref, gain_ref, all_ref, held, sends, recvs, sems):
    rows = x_ref.shape[0]
    moves = Moves(sems)
    held[own_rows(rows), :] = rms_normed(x_ref[...].astype(f32), gain_ref[...]).astype(bf16)
    greet_group()

    def on_chip(*chip):
        where = chip_rows(*chip, rows)
        moves.later(held.at[where, :], all_ref.at[where, :])

    gather_rows(rows, held, sends, recvs, on_chip)
    moves.finish()


def gather_normed(x, gain, number):
    rows, width = x.shape
    return pl.pallas_call(
        gather_normed_kernel,
        out_shape=jax.ShapeDtypeStruct((8 * rows, width), bf16),
        in_specs=vmem_specs(2),
        out_specs=pl.BlockSpec(memory_space=pl.ANY),
        scratch_shapes=gather_scratch(rows, width, 4),
        compiler_params=comm_params(number),
        cost_estimate=pl.CostEstimate(
            flops=0, bytes_accessed=150 * rows * width * 2, transcendentals=0
        ),
    )(x, gain)


def feed_forward_kernel(
    tile, mid_ref, gain_ref, w_ref, all_ref, hidden_ref, up_part_ref, gate_part_ref,
    held, sends, recvs, sems, weight, hidden, up_part, gate_part,
):
    rows = mid_ref.shape[0]
    inner = hidden.shape[1]
    moves = Moves(sems)
    weight_copy = moves.start(w_ref, weight)
    held[own_rows(rows), :] = rms_normed(mid_ref[...], gain_ref[...]).astype(bf16)
    greet_group()

    def on_chip(*chip):
        where = chip_rows(*chip, rows)
        moves.later(held.at[where, :], all_ref.at[where, :])
        if chip == SIBLING:
            weight_copy.wait()

        def column(t, _):
            cols = pl.ds(pl.multiple_of(t * tile, tile), tile)
            up_cols = pl.ds(pl.multiple_of(inner + t * tile, tile), tile)
            lhs = held[where, :]
            gate = matmul_f32(lhs, weight[:, cols])
            up = matmul_f32(lhs, weight[:, up_cols])
            sigma = 1.0 / (1.0 + jnp.exp(-gate))
            swish = gate * sigma
            hidden[where, cols] = (swish * up).astype(bf16)
            up_part[where, cols] = swish.astype(bf16)
            gate_part[where, cols] = (up * sigma * (1.0 + gate * (1.0 - sigma))).astype(bf16)
            return 0

        lax.fori_loop(0, inner // tile, column, 0)
        for src, dst in ((hidden, hidden_ref), (up_part, up_part_ref), (gate_part, gate_part_ref)):
            moves.later(src.at[where, :], dst.at[where, :])

    gather_rows(rows, held, sends, recvs, on_chip)
    moves.finish()


def feed_forward(mid, gain, cols_gate_up, number):
    rows, width = mid.shape
    inner = cols_gate_up.shape[1] // 2
    tall = jax.ShapeDtypeStruct((8 * rows, inner), bf16)
    return pl.pallas_call(
        functools.partial(feed_forward_kernel, min(256, inner)),
        out_shape=(jax.ShapeDtypeStruct((8 * rows, width), bf16), tall, tall, tall),
        in_specs=vmem_specs(2) + any_specs(1),
        out_specs=tuple(any_specs(4)),
        scratch_shapes=gather_scratch(rows, width, 17)
        + [pltpu.VMEM(cols_gate_up.shape, bf16)]
        + [pltpu.VMEM((8 * rows, inner), bf16)] * 3,
        compiler_params=comm_params(number),
        cost_estimate=pl.CostEstimate(
            flops=32 * rows * width * inner, bytes_accessed=150 * rows * width * 2,
            transcendentals=8 * rows * inner,
        ),
    )(mid, gain, cols_gate_up)


def feed_forward_back_kernel(
    tile, grad_ref, w_ref, hidden_ref, up_part_ref, gate_part_ref, grad_gate_up_ref, down_ref,
    held, sends, recvs, sems, weight, hidden, up_part, gate_part, grads, down, down_low,
):
    rows = grad_ref.shape[0]
    inner, width = weight.shape
    moves = Moves(sems)
    loads = [
        moves.start(src, dst)
        for src, dst in (
            (w_ref, weight), (hidden_ref, hidden), (up_part_ref, up_part), (gate_part_ref, gate_part)
        )
    ]
    held[own_rows(rows), :] = grad_ref[...]
    greet_group()

    def on_chip(*chip):
        where = chip_rows(*chip, rows)
        if chip == SIBLING:
            for one in loads:
                one.wait()

        def column(t, _):
            cols = pl.ds(pl.multiple_of(t * tile, tile), tile)
            up_cols = pl.ds(pl.multiple_of(inner + t * tile, tile), tile)
            incoming = held[where, :]
            grad_hidden = against_rows(incoming, weight[cols, :])
            grads[where, cols] = (grad_hidden * gate_part[where, cols].astype(f32)).astype(bf16)
            grads[where, up_cols] = (grad_hidden * up_part[where, cols].astype(f32)).astype(bf16)
            term = over_tokens(hidden[where, cols], incoming)
            if chip == SIBLING:
                down[cols, :] = term
            elif chip == ACROSS:
                down_low[cols, :] = (down[cols, :] + term).astype(bf16)
            else:
                down[cols, :] += term
            return 0

        lax.fori_loop(0, inner // tile, column, 0)
        moves.later(grads.at[where, :], grad_gate_up_ref.at[where, :])

    gather_rows(rows, held, sends, recvs, on_chip)
    moves.later(down_low, down_ref)
    moves.finish()


def feed_forward_back(grad, w_down, hidden, up_part, gate_part, number):
    rows, width = grad.shape
    inner = w_down.shape[0]
    return pl.pallas_call(
        functools.partial(feed_forward_back_kernel, min(256, inner)),
        out_shape=(
            jax.ShapeDtypeStruct((8 * rows, 2 * inner), bf16),
            jax.ShapeDtypeStruct((inner, width), bf16),
        ),
        in_specs=vmem_specs(1) + any_specs(4),
        out_specs=tuple(any_specs(2)),
        scratch_shapes=gather_scratch(rows, width, 9)
        + [pltpu.VMEM(w_down.shape, bf16)]
        + [pltpu.VMEM((8 * rows, inner), bf16)] * 3
        + [
            pltpu.VMEM((8 * rows, 2 * inner), bf16),
            pltpu.VMEM(w_down.shape, f32),
            pltpu.VMEM(w_down.shape, bf16),
        ],
        compiler_params=comm_params(number, 62),
        cost_estimate=pl.CostEstimate(
            flops=32 * rows * width * inner, bytes_accessed=150 * rows * width * 2,
            transcendentals=0,
        ),
    )(grad, w_down, hidden, up_part, gate_part)


def attended_back_kernel(
    grad_ref, w_ref, attended_ref, grad_attended_ref, out_term_ref,
    held, sends, recvs, sems, total,
):
    rows = grad_ref.shape[0]
    moves = Moves(sems)
    held[own_rows(rows), :] = grad_ref[...]
    greet_group()

    def on_chip(*chip):
        where = chip_rows(*chip, rows)
        incoming = held[where, :]
        grad_attended_ref[where, :] = against_rows(incoming, w_ref[...]).astype(bf16)
        term = over_tokens(attended_ref[where, :], incoming)
        if chip == SIBLING:
            total[...] = term
        elif chip == ACROSS:
            out_term_ref[...] = (total[...] + term).astype(bf16)
        else:
            total[...] += term

    gather_rows(rows, held, sends, recvs, on_chip)
    moves.finish()


def attended_back(grad, w_out, attended, number):
    rows, width = grad.shape
    return pl.pallas_call(
        attended_back_kernel,
        out_shape=(
            jax.ShapeDtypeStruct(attended.shape, bf16),
            jax.ShapeDtypeStruct(w_out.shape, bf16),
        ),
        in_specs=vmem_specs(3),
        out_specs=tuple(vmem_specs(2)),
        scratch_shapes=gather_scratch(rows, width, 1) + [pltpu.VMEM(w_out.shape, f32)],
        compiler_params=comm_params(number),
        cost_estimate=pl.CostEstimate(
            flops=32 * rows * width * w_out.shape[0], bytes_accessed=150 * rows * width * 2,
            transcendentals=0,
        ),
    )(grad, w_out, attended)


def scatter_kernel(
    turned, tile,
    a_ref, b_ref, out_ref,
    part, to_s, from_s, to_chip, held, relay, last, sends, recvs,
):
    rows, width = out_ref.shape
    half = rows // 2
    _, _, core = place_in_group()
    greet_group()
    own_at = pl.multiple_of(core * rows, rows)
    other_at = pl.multiple_of((1 - core) * rows, rows)
    started = []

    def send(number, src, dst, target):
        one = pltpu.make_async_remote_copy(
            src_ref=src, dst_ref=dst, send_sem=sends.at[number], recv_sem=recvs.at[number],
            device_id={"grp": other(*target)}, device_id_type=MESH,
        )
        one.start()
        started.append(one)
        return one

    def landed(number, where):
        pltpu.make_async_remote_copy(
            src_ref=where, dst_ref=where, send_sem=sends.at[number], recv_sem=recvs.at[number],
            device_id={"grp": other(0, 0, 1)}, device_id_type=MESH,
        ).wait_recv()

    to_sib, to_x, to_y = (0, 0, 1), (0, 1, 0), (1, 0, 0)

    def make(number, chip):
        where = chip_rows(*chip, rows)

        def column(t, _):
            cols = pl.ds(pl.multiple_of(t * tile, tile), tile)
            lhs = a_ref[where, :]
            if turned:
                part[:, cols] = against_rows(lhs, b_ref[cols, :])
            else:
                part[:, cols] = matmul_f32(lhs, b_ref[:, cols])
            return 0

        lax.fori_loop(0, width // tile, column, 0)
        to_s[number] = part[pl.ds(other_at, rows), :].astype(bf16)
        send(number, to_s.at[number], from_s.at[number], to_sib)

    def own(low, number):
        at = pl.ds(pl.multiple_of(core * rows + low * half, half), half)
        return part[at, :] + from_s[number, low * half : (low + 1) * half, :].astype(f32)

    first, second = slice(0, half), slice(half, rows)
    make(0, ACROSS)
    landed(0, from_s.at[0])
    to_chip[0, first, :] = own(0, 0).astype(bf16)
    send(4, to_chip.at[0, first, :], relay.at[0], to_x)
    to_chip[0, second, :] = own(1, 0).astype(bf16)
    send(5, to_chip.at[0, second, :], relay.at[1], to_y)
    make(1, ALONG_X)
    landed(1, from_s.at[1])
    to_chip[1, first, :] = own(0, 1).astype(bf16)
    send(6, to_chip.at[1, first, :], last.at[0, first, :], to_x)
    held[0] = own(1, 1)
    make(2, ALONG_Y)
    landed(2, from_s.at[2])
    to_chip[2, second, :] = own(1, 2).astype(bf16)
    send(7, to_chip.at[2, second, :], last.at[1, second, :], to_y)
    held[1] = own(0, 2)
    landed(5, relay.at[1])
    to_chip[1, second, :] = (held[0] + relay[1].astype(f32)).astype(bf16)
    send(8, to_chip.at[1, second, :], last.at[0, second, :], to_x)
    landed(4, relay.at[0])
    to_chip[2, first, :] = (held[1] + relay[0].astype(f32)).astype(bf16)
    send(9, to_chip.at[2, first, :], last.at[1, first, :], to_y)
    make(3, SIBLING)
    landed(3, from_s.at[3])
    for low in (0, 1):
        out_ref[low * half : (low + 1) * half, :] = own(low, 3)
    landed(6, last.at[0, first, :])
    out_ref[first, :] += last[0, first, :].astype(f32)
    landed(7, last.at[1, second, :])
    out_ref[second, :] += last[1, second, :].astype(f32)
    landed(8, last.at[0, second, :])
    out_ref[second, :] += last[0, second, :].astype(f32)
    landed(9, last.at[1, first, :])
    out_ref[first, :] += last[1, first, :].astype(f32)
    for one in started:
        one.wait_send()


def product_scattered(a, b, turned, number):
    length, depth = a.shape
    width = b.shape[0] if turned else b.shape[1]
    rows = length // 8
    tile = min(256, width)
    return pl.pallas_call(
        functools.partial(scatter_kernel, turned, tile),
        out_shape=jax.ShapeDtypeStruct((rows, width), f32),
        in_specs=vmem_specs(2),
        out_specs=pl.BlockSpec(memory_space=pltpu.VMEM),
        scratch_shapes=[
            pltpu.VMEM((2 * rows, width), f32),
            pltpu.VMEM((4, rows, width), bf16),
            pltpu.VMEM((4, rows, width), bf16),
            pltpu.VMEM((3, rows, width), bf16),
            pltpu.VMEM((2, rows // 2, width), f32),
            pltpu.VMEM((2, rows // 2, width), bf16),
            pltpu.VMEM((2, rows, width), bf16),
            pltpu.SemaphoreType.DMA((10,)),
            pltpu.SemaphoreType.DMA((10,)),
        ],
        compiler_params=pltpu.CompilerParams(
            collective_id=number, has_side_effects=True, vmem_limit_bytes=56 * 2**20
        ),
        cost_estimate=pl.CostEstimate(
            flops=2 * length * depth * width,
            bytes_accessed=100 * rows * width * 2, transcendentals=0,
        ),
    )(a, b)


def sum_over_sequences(term, reps):
    if reps != 4:
        return lax.psum(term, "rep").astype(f32)
    rank = lax.axis_index("rep")
    inward = lax.ppermute(term, "rep", [(0, 1), (3, 2)])
    pair = (term.astype(f32) + inward.astype(f32)).astype(bf16)
    other = lax.ppermute(pair, "rep", [(1, 2), (2, 1)])
    total = (pair.astype(f32) + other.astype(f32)).astype(bf16)
    outward = lax.ppermute(total, "rep", [(1, 0), (2, 3)])
    return jnp.where((rank == 0) | (rank == 3), outward, total).astype(f32)


def on_device(
    layer_input,
    cotangent,
    cut_order,
    piece_ids,
    w_query,
    w_key,
    w_value,
    w_out,
    w_gate,
    w_up,
    w_down,
    gain_attn,
    gain_ffn,
):
    groups = lax.axis_size("grp")
    reps = lax.axis_size("rep")
    own_index = lax.axis_index("grp")
    _, local_rows, model_width = layer_input.shape
    length = piece_ids.shape[1]
    rows_here = w_query.shape[0]
    q_width = w_query.shape[1]
    kv_heads = w_key.shape[1] // HD
    heads = q_width // HD // groups
    copies = groups // kv_heads
    hidden_here = w_down.shape[0]
    piece_col = jnp.broadcast_to(piece_ids.reshape(length, 1), (length, HD))
    cosine, sine = turn_tables(length)

    near = groups == 8

    def gather(rows):
        return lax.all_gather(rows, "grp", axis=0, tiled=True)

    def scatter(first, second, turned, number):
        if near:
            return product_scattered(first, second, turned, number)
        term = against_rows(first, second) if turned else matmul_f32(first, second)
        return lax.psum_scatter(
            term.astype(bf16), "grp", scatter_dimension=0, tiled=True
        ).astype(f32)

    def to_columns(parts):
        return lax.all_to_all(parts, "grp", 1, 0, tiled=True).reshape(-1, parts.shape[-1])

    def per_group(weight):
        return weight.reshape(rows_here, groups, -1)

    def per_kv_head(weight):
        return jnp.repeat(weight.reshape(rows_here, kv_heads, HD), copies, axis=1)

    x_rows = layer_input.reshape(local_rows, model_width)
    x_flat = x_rows.astype(f32)
    inv_one = lax.rsqrt(jnp.mean(x_flat * x_flat, -1, keepdims=True) + EPS)
    unit_one = x_flat * inv_one
    attn_gain, ffn_gain = gain_attn.reshape(1, -1), gain_ffn.reshape(1, -1)
    cols_qkv = to_columns(
        jnp.concatenate([per_group(w_query), per_kv_head(w_key), per_kv_head(w_value)], -1)
    )
    if near:
        normed_one = gather_normed(x_rows, attn_gain, 1)
    else:
        normed_one = gather(rms_normed(x_flat, attn_gain).astype(bf16))
    qkv = matmul_f32(normed_one, cols_qkv)
    attended, query, key, value, lse = attend(
        cut_order, qkv, cosine, sine, piece_ids, piece_col, heads
    )
    cols_gate_up = to_columns(jnp.concatenate([per_group(w_gate), per_group(w_up)], -1))
    mid = x_flat + scatter(attended, w_out, False, 2)
    inv_two = lax.rsqrt(jnp.mean(mid * mid, -1, keepdims=True) + EPS)
    unit_two = mid * inv_two
    grad_out = cotangent.reshape(local_rows, model_width)
    if near:
        normed_two, hidden, up_part, gate_part = feed_forward(mid, ffn_gain, cols_gate_up, 3)
        grad_gate_up, down_term = feed_forward_back(
            grad_out, w_down, hidden, up_part, gate_part, 4
        )
    else:
        normed_two = gather((unit_two * ffn_gain).astype(bf16))
        grad_all = gather(grad_out)
        gate_up = matmul_f32(normed_two, cols_gate_up)
        gate_proj, up_proj = gate_up[:, :hidden_here], gate_up[:, hidden_here:]
        sigmoid_gate = jax.nn.sigmoid(gate_proj)
        swish = gate_proj * sigmoid_gate
        hidden = (swish * up_proj).astype(bf16)
        gate_part = up_proj * sigmoid_gate * (1.0 + gate_proj * (1.0 - sigmoid_gate))
        down_term = over_tokens(hidden, grad_all).astype(bf16)
        grad_hidden = against_rows(grad_all, w_down)
        grad_gate_up = jnp.concatenate([grad_hidden * gate_part, grad_hidden * swish], 1)
        grad_gate_up = grad_gate_up.astype(bf16)
    down_term = sum_over_sequences(down_term, reps)
    grad_two = scatter(grad_gate_up, cols_gate_up, True, 5)
    grad_mid, gain_ffn_term = norm_back(
        grad_out.astype(f32), grad_two, unit_two, inv_two, gain_ffn
    )
    grad_mid_low = grad_mid.astype(bf16)
    if near:
        grad_attended, out_term = attended_back(grad_mid_low, w_out, attended, 6)
    else:
        grad_mid_low = gather(grad_mid_low)
        grad_attended = against_rows(grad_mid_low, w_out).astype(bf16)
        out_term = over_tokens(attended, grad_mid_low).astype(bf16)

    def to_rows(term):
        return lax.all_to_all(
            term.astype(bf16).reshape(groups, rows_here, -1), "grp", 0, 0, tiled=True
        )

    gate_up_term = sum_over_sequences(to_rows(over_tokens(normed_two, grad_gate_up)), reps)
    grad_qkv = attend_back(
        cut_order, grad_attended, attended, query, key, value, lse, cosine, sine,
        piece_ids, piece_col, heads,
    )
    out_term = sum_over_sequences(out_term, reps)
    qkv_term = sum_over_sequences(to_rows(over_tokens(normed_one, grad_qkv)), reps)
    grad_one = scatter(grad_qkv, cols_qkv, True, 7)
    grad_input, gain_attn_term = norm_back(grad_mid, grad_one, unit_one, inv_one, gain_attn)
    result = (mid + scatter(hidden, w_down, False, 8)).astype(bf16)
    gain_total = lax.psum(jnp.stack([gain_attn_term, gain_ffn_term]), ("grp", "rep"))
    own_gains = lax.dynamic_slice_in_dim(gain_total, own_index * rows_here, rows_here, 1)

    def whole_rows(term):
        return jnp.moveaxis(term, 0, 1).reshape(rows_here, -1)

    def kv_rows(term):
        return jnp.sum(
            jnp.moveaxis(term, 0, 1).reshape(rows_here, kv_heads, copies, HD), 2
        ).reshape(rows_here, -1)

    q_here = heads * HD
    return (
        result.reshape(layer_input.shape),
        grad_input.astype(bf16).reshape(layer_input.shape),
        whole_rows(qkv_term[..., :q_here]),
        kv_rows(qkv_term[..., q_here : q_here + HD]),
        kv_rows(qkv_term[..., q_here + HD :]),
        out_term,
        whole_rows(gate_up_term[..., :hidden_here]),
        whole_rows(gate_up_term[..., hidden_here:]),
        down_term,
        own_gains[0],
        own_gains[1],
    )


def solution(mesh):
    tokens, table, rows, whole = P("rep", "grp", None), P("rep", None), P("grp", None), P()
    return jax.shard_map(
        on_device,
        mesh=mesh,
        in_specs=(tokens, tokens, table, table) + (rows,) * 7 + (whole,) * 2,
        out_specs=(tokens, tokens) + (rows,) * 7 + (P("grp"),) * 2,
        check_vma=False,
    )
```

```python
import functools

import jax
import jax.numpy as jnp
from jax import lax
from jax.experimental import pallas as pl
from jax.experimental.pallas import tpu as pltpu
from jax.sharding import PartitionSpec as P

HD = 128
EPS = 1e-05
ROPE_BASE = 1000000.0
SCORE_SCALE = HD**-0.5
LOG2E = 1.4426950408889634
TO_EXP2 = SCORE_SCALE * LOG2E
NEG = -1e30

MESH = pl.DeviceIdType.MESH
f32 = jnp.float32
bf16 = jnp.bfloat16


def matmul_f32(first, second):
    return jnp.dot(first, second, preferred_element_type=f32)


def against_rows(first, second):
    return lax.dot_general(first, second, (((1,), (1,)), ((), ())), preferred_element_type=f32)


def over_tokens(first, second):
    return lax.dot_general(first, second, (((0,), (0,)), ((), ())), preferred_element_type=f32)


def turn_tables(length):
    half_size = HD // 2
    inverse = ROPE_BASE ** (-(jnp.arange(half_size, dtype=f32) * 2.0) / HD)
    angles = jnp.arange(length, dtype=jnp.int32).astype(f32)[:, None] * inverse
    cosine, sine = jnp.cos(angles), jnp.sin(angles)
    return jnp.concatenate([cosine, cosine], -1), jnp.concatenate([-sine, sine], -1)


def norm_back(upstream, grad_normed, unit_rows, inv_root, gain):
    scaled = grad_normed * gain
    center_term = jnp.mean(scaled * unit_rows, -1, keepdims=True)
    return (
        upstream + inv_root * (scaled - unit_rows * center_term),
        jnp.sum(grad_normed * unit_rows, 0),
    )


def fold_lanes(values, op):
    out = values[:, :HD]
    for at in range(HD, values.shape[1], HD):
        out = op(out, values[:, at : at + HD])
    return out


def as_row(column):
    return jnp.broadcast_to(column, (column.shape[0], HD)).T[0:1, :]


def attend_kernel(
    heads, cuts, block,
    order_ref, qkv_ref, cos_ref, sin_ref, piece_ref, piece_col_ref,
    out_ref, q_ref, k_ref, v_ref, lse_ref, placed,
    scores,
):
    length = qkv_ref.shape[0]
    cut = length // cuts
    blocks = length // block

    def place_cut(r, _):
        src = pl.ds(pl.multiple_of(r * cut, cut), cut)
        dst = pl.ds(pl.multiple_of(order_ref[0, r] * cut, cut), cut)
        cosine, sine = cos_ref[dst, :], sin_ref[dst, :]
        for h in range(heads + 1):
            part = qkv_ref[src, h * HD : (h + 1) * HD]
            turned = (part * cosine + pltpu.roll(part, HD // 2, 1) * sine).astype(bf16)
            if h < heads:
                q_ref[h, dst, :] = turned
            else:
                k_ref[dst, :] = turned
        v_ref[dst, :] = qkv_ref[src, (heads + 1) * HD :].astype(bf16)
        return 0

    lax.fori_loop(0, cuts, place_cut, 0)

    def one_block(i, _):
        rows = pl.ds(pl.multiple_of(i * block, block), block)
        query = q_ref[:, rows, :].reshape(heads * block, HD)

        def score(j, high):
            cols = pl.ds(pl.multiple_of(j * block, block), block)
            tile = against_rows(query, k_ref[cols, :])
            scores[j] = tile
            return jnp.maximum(high, fold_lanes(tile, jnp.maximum))

        high = lax.fori_loop(0, i, score, jnp.full((heads * block, HD), NEG, f32))
        tile = against_rows(query, k_ref[rows, :])
        q_at = lax.broadcasted_iota(jnp.int32, (block, block), 0)
        k_at = lax.broadcasted_iota(jnp.int32, (block, block), 1)
        q_piece, k_piece = piece_col_ref[rows, 0:1], piece_ref[0:1, rows]
        allowed = (k_at <= q_at) | ((q_piece != 0) & (q_piece == k_piece))
        tile = jnp.concatenate(
            [jnp.where(allowed, tile[h * block : (h + 1) * block], NEG) for h in range(heads)], 0
        )
        scores[i] = tile
        high = jnp.max(jnp.maximum(high, fold_lanes(tile, jnp.maximum)), 1, keepdims=True)

        def weigh(j, state):
            total, mixed = state
            cols = pl.ds(pl.multiple_of(j * block, block), block)
            prob = jnp.exp2((scores[j] - high) * TO_EXP2)
            total = total + fold_lanes(prob, jnp.add)
            return total, mixed + matmul_f32(prob.astype(bf16), v_ref[cols, :])

        zero = jnp.zeros((heads * block, HD), f32)
        total, mixed = lax.fori_loop(0, i + 1, weigh, (zero, zero))
        total = jnp.sum(total, 1, keepdims=True)
        mixed = (mixed / total).astype(bf16)
        log_total = high * TO_EXP2 + jnp.log2(total)
        for h in range(heads):
            placed[rows, h * HD : (h + 1) * HD] = mixed[h * block : (h + 1) * block]
            lse_ref[h : h + 1, rows] = as_row(log_total[h * block : (h + 1) * block])
        return 0

    lax.fori_loop(0, blocks, one_block, 0)

    def store_cut(r, _):
        dst = pl.ds(pl.multiple_of(r * cut, cut), cut)
        src = pl.ds(pl.multiple_of(order_ref[0, r] * cut, cut), cut)
        out_ref[dst, :] = placed[src, :]
        return 0

    lax.fori_loop(0, cuts, store_cut, 0)


def vmem_specs(count):
    return [pl.BlockSpec(memory_space=pltpu.VMEM)] * count


def attend(order, qkv, cosine, sine, piece, piece_col, heads):
    length = qkv.shape[0]
    block = min(512, length)
    return pl.pallas_call(
        functools.partial(attend_kernel, heads, order.shape[1], block),
        out_shape=(
            jax.ShapeDtypeStruct((length, heads * HD), bf16),
            jax.ShapeDtypeStruct((heads, length, HD), bf16),
            jax.ShapeDtypeStruct((length, HD), bf16),
            jax.ShapeDtypeStruct((length, HD), bf16),
            jax.ShapeDtypeStruct((heads, length), f32),
            jax.ShapeDtypeStruct((length, heads * HD), bf16),
        ),
        in_specs=[pl.BlockSpec(memory_space=pltpu.SMEM)] + vmem_specs(5),
        out_specs=tuple(vmem_specs(6)),
        scratch_shapes=[pltpu.VMEM((length // block, heads * block, block), f32)],
        compiler_params=pltpu.CompilerParams(vmem_limit_bytes=48 * 2**20),
        cost_estimate=pl.CostEstimate(
            flops=3 * heads * length * length * HD, bytes_accessed=10 * length * HD * heads * 4,
            transcendentals=heads * length * length // 2,
        ),
    )(order, qkv, cosine, sine, piece, piece_col)


CHUNKS = 15


def is_middle():
    rank = lax.axis_index("rep")
    return (rank == 1) | (rank == 2)


def is_end():
    rank = lax.axis_index("rep")
    return (rank == 0) | (rank == 3)


class NoLine:
    ticks = 0

    def greet(self, barrier, others):
        if others:
            pl.semaphore_wait(barrier, others)

    def open(self, number):
        pass

    def close(self, number):
        pass

    def finish(self):
        pass


class Line:
    def __init__(self, first, ticks, picks, refs, outs, scratch):
        self.first, self.ticks, self.picks, self.refs, self.outs = first, ticks, picks, refs, outs
        self.inward, self.across, self.own, self.pair, self.total, self.sems, self.local = scratch
        rank = lax.axis_index("rep")
        self.partner = {"rep": rank + 1 - 2 * (rank % 2)}
        self.peer = {"rep": 3 - rank}
        self.slots = line_slots(first, ticks)

    def greet(self, barrier, others):
        pl.semaphore_signal(barrier, inc=1, device_id=self.partner, device_id_type=MESH)

        @pl.when(is_middle())
        def _():
            pl.semaphore_signal(barrier, inc=1, device_id=self.peer, device_id_type=MESH)
            pl.semaphore_wait(barrier, others + 2)

        @pl.when(is_end())
        def _():
            pl.semaphore_wait(barrier, others + 1)

    def remote(self, hop, number, src, dst, device):
        return pltpu.make_async_remote_copy(
            src_ref=src, dst_ref=dst, send_sem=self.sems.at[0, hop, number],
            recv_sem=self.sems.at[1, hop, number], device_id=device, device_id_type=MESH,
        )

    def hops(self, number):
        tick = self.first + number
        term = pair = total = None
        if tick < CHUNKS:
            which, pick = self.picks[tick]
            term = (
                lambda: self.remote(
                    0, number, pick(self.refs[which]), self.inward.at[number], self.partner
                ),
                lambda: pltpu.make_async_copy(
                    pick(self.refs[which]), self.own.at[number % 2], self.local.at[0, number]
                ),
            )
        if 1 <= tick <= CHUNKS:
            before = self.refs["pair"] if number == 0 else self.pair.at[(number - 1) % 2]
            pair = (
                lambda: self.remote(1, number, before, self.across.at[number], self.peer),
                lambda: pltpu.make_async_copy(before, self.pair.at[2], self.local.at[1, number]),
            )
        if 2 <= tick <= CHUNKS + 1:
            done = self.refs["total"] if number == 0 else self.total.at[(number - 1) % 2]
            slot = self.outs[tick - 2]
            total = (
                lambda: self.remote(2, number, done, slot, self.partner),
                lambda: pltpu.make_async_copy(done, slot, self.local.at[2, number]),
            )
        return term, pair, total

    def open(self, number):
        if number >= self.ticks:
            return
        term, pair, total = self.hops(number)

        @pl.when(is_end())
        def _():
            if term:
                term[0]().start()

        @pl.when(is_middle())
        def _():
            if pair:
                pair[0]().start()
            if total:
                total[0]().start()
                total[1]().start()
            if term:
                term[1]().start()
            if pair and number == 0:
                pair[1]().start()

    def close(self, number):
        if number >= self.ticks:
            return
        term, pair, total = self.hops(number)

        def add(into, first, second):
            def one(g, _):
                into[g] = (first[g].astype(f32) + second[g].astype(f32)).astype(bf16)
                return 0

            lax.fori_loop(0, into.shape[0], one, 0)

        @pl.when(is_end())
        def _():
            if term:
                term[0]().wait_send()
            if total:
                total[0]().wait_recv()

        @pl.when(is_middle())
        def _():
            if total:
                total[0]().wait_send()
                total[1]().wait()
            if pair:
                pair[0]().wait_send()
                pair[0]().wait_recv()
                if number == 0:
                    pair[1]().wait()
                before = 2 if number == 0 else (number - 1) % 2
                add(self.total.at[number % 2], self.pair.at[before], self.across.at[number])
            if term:
                term[1]().wait()
                term[0]().wait_recv()
                add(self.pair.at[number % 2], self.own.at[number % 2], self.inward.at[number])

    def finish(self):
        last = self.ticks - 1
        tick = self.first + last

        @pl.when(is_middle())
        def _():
            if tick < CHUNKS:
                keep = pltpu.make_async_copy(
                    self.pair.at[last % 2], self.outs["pair"], self.local.at[0, last]
                )
                keep.start()
                keep.wait()
            if 1 <= tick <= CHUNKS:
                keep = pltpu.make_async_copy(
                    self.total.at[last % 2], self.outs["total"], self.local.at[1, last]
                )
                keep.start()
                keep.wait()


def line_slots(first, ticks):
    return [t - 2 for t in range(first, first + ticks) if 2 <= t <= CHUNKS + 1]


class Sums:
    def __init__(self, shape):
        self.shape, self.tick, self.pair, self.total, self.done = shape, 0, None, None, {}


def run(kernel, ins, outs, scratch, number, cost, sums=None, ticks=0, arrays=(), picks=None, vmem=58):
    ins, outs, scratch = list(ins), list(outs), list(scratch)
    counts = (len(ins), len(outs), len(scratch))
    first = sums.tick if ticks else 0
    names_in, names_out = [], []
    if ticks:
        last = first + ticks - 1
        chunk = jax.ShapeDtypeStruct(sums.shape, bf16)
        for name, array in arrays:
            names_in.append(name)
            ins.append((array, pl.ANY))
        if 1 <= first <= CHUNKS:
            names_in.append("pair")
            ins.append((sums.pair, pl.ANY))
        if 2 <= first <= CHUNKS + 1:
            names_in.append("total")
            ins.append((sums.total, pl.ANY))
        names_out = line_slots(first, ticks)
        if last < CHUNKS:
            names_out.append("pair")
        if 1 <= last <= CHUNKS:
            names_out.append("total")
        outs += [(chunk, pl.ANY)] * len(names_out)
        scratch += [
            pltpu.VMEM((ticks,) + sums.shape, bf16),
            pltpu.VMEM((ticks,) + sums.shape, bf16),
            pltpu.VMEM((2,) + sums.shape, bf16),
            pltpu.VMEM((3,) + sums.shape, bf16),
            pltpu.VMEM((2,) + sums.shape, bf16),
            pltpu.SemaphoreType.DMA((2, 3, ticks)),
            pltpu.SemaphoreType.DMA((3, ticks)),
        ]

    def body(*refs):
        in_refs, rest = refs[: len(ins)], refs[len(ins) :]
        out_refs, scratch_refs = rest[: len(outs)], rest[len(outs) :]
        line = NoLine()
        if ticks:
            line = Line(
                first, ticks, picks, dict(zip(names_in, in_refs[counts[0] :])),
                dict(zip(names_out, out_refs[counts[1] :])), scratch_refs[counts[2] :],
            )
        kernel(in_refs[: counts[0]], out_refs[: counts[1]], scratch_refs[: counts[2]], line)

    results = pl.pallas_call(
        body,
        out_shape=tuple(shape for shape, _ in outs),
        in_specs=[pl.BlockSpec(memory_space=space) for _, space in ins],
        out_specs=tuple(pl.BlockSpec(memory_space=space) for _, space in outs),
        scratch_shapes=scratch,
        compiler_params=pltpu.CompilerParams(
            vmem_limit_bytes=vmem * 2**20,
            **({} if number is None else {"collective_id": number, "has_side_effects": True}),
        ),
        cost_estimate=pl.CostEstimate(
            flops=cost[0], bytes_accessed=cost[1], transcendentals=cost[2]
        ),
    )(*[array for array, _ in ins])
    for name, result in zip(names_out, results[counts[1] :]):
        if name == "pair":
            sums.pair = result
        elif name == "total":
            sums.total = result
        else:
            sums.done[name] = result
    if ticks:
        sums.tick += ticks
    return results[: counts[1]]


SMEM, VMEM, ANY = pltpu.SMEM, pltpu.VMEM, pl.ANY


def attend_back_kernel(
    heads, block, ins, outs, scratch, line
):
    grad_ref, out_ref, q_ref, k_ref, v_ref, lse_ref, cos_ref, sin_ref, piece_ref, piece_col_ref = ins
    (grad_qkv_ref,) = outs
    grads, centers, grad_q = scratch
    if line.ticks:
        line.greet(pltpu.get_barrier_semaphore(), 0)
        line.open(0)
    length = grad_ref.shape[0]
    blocks = length // block

    def take_block(i, _):
        rows = pl.ds(pl.multiple_of(i * block, block), block)
        for h in range(heads):
            grad = grad_ref[rows, h * HD : (h + 1) * HD].astype(bf16)
            grads[h, rows, :] = grad
            product = grad.astype(f32) * out_ref[rows, h * HD : (h + 1) * HD].astype(f32)
            centers[h, rows, :] = jnp.broadcast_to(
                jnp.sum(product, 1, keepdims=True), (block, HD)
            )
        return 0

    lax.fori_loop(0, blocks, take_block, 0)
    grad_q[...] = jnp.zeros_like(grad_q)

    def key_block(j, _):
        cols = pl.ds(pl.multiple_of(j * block, block), block)
        key, value = k_ref[cols, :], v_ref[cols, :]

        def one(i, state, diagonal):
            grad_key, grad_value = state
            rows = pl.ds(pl.multiple_of(i * block, block), block)
            for h in range(heads):
                query, grad = q_ref[h, rows, :], grads[h, rows, :]
                log_total = lse_ref[h : h + 1, rows]
                center = centers[h, rows, :].T[0:1, :]
                prob = jnp.exp2(against_rows(key, query) * TO_EXP2 - log_total)
                if diagonal:
                    k_at = lax.broadcasted_iota(jnp.int32, (block, block), 0)
                    q_at = lax.broadcasted_iota(jnp.int32, (block, block), 1)
                    k_piece, q_piece = piece_col_ref[cols, 0:1], piece_ref[0:1, cols]
                    allowed = (k_at <= q_at) | ((q_piece != 0) & (q_piece == k_piece))
                    prob = jnp.where(allowed, prob, 0.0)
                grad_prob = against_rows(value, grad)
                grad_score = (prob * (grad_prob - center)).astype(bf16)
                grad_value = grad_value + matmul_f32(prob.astype(bf16), grad)
                grad_key = grad_key + matmul_f32(grad_score, query)
                grad_q[h, rows, :] += over_tokens(grad_score, key)
            return grad_key, grad_value

        zero = jnp.zeros((block, HD), f32)
        state = one(j, (zero, zero), True)
        grad_key, grad_value = lax.fori_loop(
            j + 1, blocks, functools.partial(one, diagonal=False), state
        )
        grad_key = grad_key * SCORE_SCALE
        grad_key = grad_key * cos_ref[cols, :] - pltpu.roll(grad_key, HD // 2, 1) * sin_ref[cols, :]
        grad_qkv_ref[cols, heads * HD : (heads + 1) * HD] = grad_key.astype(bf16)
        grad_qkv_ref[cols, (heads + 1) * HD :] = grad_value.astype(bf16)
        return 0

    lax.fori_loop(0, blocks, key_block, 0)

    def turn_back(i, _):
        rows = pl.ds(pl.multiple_of(i * block, block), block)
        for h in range(heads):
            grad = grad_q[h, rows, :] * SCORE_SCALE
            grad = grad * cos_ref[rows, :] - pltpu.roll(grad, HD // 2, 1) * sin_ref[rows, :]
            grad_qkv_ref[rows, h * HD : (h + 1) * HD] = grad.astype(bf16)
        return 0

    lax.fori_loop(0, blocks, turn_back, 0)
    if line.ticks:
        line.close(0)
        line.finish()


def take_cuts_kernel(cuts, holder_ref, rows_ref, out_ref):
    cut = out_ref.shape[0] // cuts

    def one(p, _):
        src = pl.ds(pl.multiple_of(holder_ref[0, p] * cut, cut), cut)
        out_ref[pl.ds(pl.multiple_of(p * cut, cut), cut), :] = rows_ref[src, :]
        return 0

    lax.fori_loop(0, cuts, one, 0)


def take_cuts(holder, rows):
    return pl.pallas_call(
        functools.partial(take_cuts_kernel, holder.shape[1]),
        out_shape=jax.ShapeDtypeStruct(rows.shape, rows.dtype),
        in_specs=[pl.BlockSpec(memory_space=pltpu.SMEM)] + vmem_specs(1),
        out_specs=pl.BlockSpec(memory_space=pltpu.VMEM),
        cost_estimate=pl.CostEstimate(
            flops=0, bytes_accessed=2 * rows.size * rows.dtype.itemsize, transcendentals=0
        ),
    )(holder, rows)


def attend_back(
    order, grad, out, query, key, value, lse, cosine, sine, piece, piece_col, heads, **line
):
    cuts = jnp.arange(order.shape[1], dtype=order.dtype)
    holder = jnp.sum(jnp.where(order[0][None, :] == cuts[:, None], cuts[None, :], 0), 1)[None, :]
    length = grad.shape[0]
    block = min(512, length)
    tall = [take_cuts(holder, grad), out, query, key, value, lse, cosine, sine, piece, piece_col]
    grad_qkv = run(
        functools.partial(attend_back_kernel, heads, block),
        [(array, VMEM) for array in tall],
        [(jax.ShapeDtypeStruct((length, (heads + 2) * HD), bf16), VMEM)],
        [
            pltpu.VMEM((heads, length, HD), bf16),
            pltpu.VMEM((heads, length, HD), f32),
            pltpu.VMEM((heads, length, HD), f32),
        ],
        line.pop("number", None),
        (8 * heads * length * length * HD, 14 * length * HD * heads * 4, heads * length * length // 2),
        **line,
    )[0]
    return take_cuts(order, grad_qkv)


def place_in_group():
    me = lax.axis_index("grp")
    return me // 4, (me // 2) % 2, me % 2


def other(flip_y, flip_x, flip_core):
    y, x, core = place_in_group()
    return ((y + flip_y) % 2) * 4 + ((x + flip_x) % 2) * 2 + (core + flip_core) % 2


def chip_rows(flip_y, flip_x, rows):
    y, x, _ = place_in_group()
    first = (((y + flip_y) % 2) * 2 + (x + flip_x) % 2) * (2 * rows)
    return pl.ds(pl.multiple_of(first, 2 * rows), 2 * rows)


NEIGHBOURS = ((0, 0, 1), (0, 1, 0), (1, 0, 0))
EVERYONE = tuple((n // 4, (n // 2) % 2, n % 2) for n in range(1, 8))


def greet_group(line, flips=NEIGHBOURS):
    barrier = pltpu.get_barrier_semaphore()
    for flip in flips:
        pl.semaphore_signal(barrier, inc=1, device_id={"grp": other(*flip)}, device_id_type=MESH)
    line.greet(barrier, len(flips))


SIBLING, ALONG_X, ALONG_Y, ACROSS = (0, 0), (0, 1), (1, 0), (1, 1)


def gather_rows(rows, all_ref, sends, recvs, on_chip, line):
    half = rows // 2

    def block(chip, core, part=None):
        first = other(*chip, core) * rows
        if part is None:
            return pl.ds(pl.multiple_of(first, rows), rows)
        return pl.ds(pl.multiple_of(first + part * half, half), half)

    def copy(number, chip, core, part, target):
        where = all_ref.at[block(chip, core, part), :]
        return pltpu.make_async_remote_copy(
            src_ref=where, dst_ref=where, send_sem=sends.at[number], recv_sem=recvs.at[number],
            device_id={"grp": other(*target)}, device_id_type=MESH,
        )

    def landed(number, chip, core, part):
        where = all_ref.at[block(chip, core, part), :]
        pltpu.make_async_remote_copy(
            src_ref=where, dst_ref=where, send_sem=sends.at[number], recv_sem=recvs.at[number],
            device_id={"grp": other(0, 0, 1)}, device_id_type=MESH,
        ).wait_recv()

    to_s, to_x, to_y = (0, 0, 1), (0, 1, 0), (1, 0, 0)
    started = []

    def send(*what):
        one = copy(*what)
        one.start()
        started.append(one)

    send(1, SIBLING, 0, 1, to_x)
    send(3, SIBLING, 0, 0, to_y)
    send(0, SIBLING, 0, None, to_s)
    send(2, SIBLING, 0, 0, to_x)
    send(4, SIBLING, 0, 1, to_y)
    landed(0, SIBLING, 1, None)
    on_chip(*SIBLING)
    landed(1, ALONG_X, 0, 1)
    send(6, ALONG_X, 0, 1, to_y)
    landed(3, ALONG_Y, 0, 0)
    send(5, ALONG_Y, 0, 0, to_x)
    send(7, ALONG_X, 0, 1, to_s)
    send(8, ALONG_Y, 0, 0, to_s)
    landed(2, ALONG_X, 0, 0)
    send(9, ALONG_X, 0, 0, to_s)
    landed(4, ALONG_Y, 0, 1)
    send(10, ALONG_Y, 0, 1, to_s)
    line.close(0)
    line.open(1)
    landed(7, ALONG_X, 1, 1)
    landed(9, ALONG_X, 1, 0)
    on_chip(*ALONG_X)
    landed(5, ACROSS, 0, 0)
    send(11, ACROSS, 0, 0, to_s)
    landed(6, ACROSS, 0, 1)
    send(12, ACROSS, 0, 1, to_s)
    landed(8, ALONG_Y, 1, 0)
    landed(10, ALONG_Y, 1, 1)
    on_chip(*ALONG_Y)
    landed(11, ACROSS, 1, 0)
    landed(12, ACROSS, 1, 1)
    on_chip(*ACROSS)
    for one in started:
        one.wait_send()
    line.close(1)
    line.finish()


GATHER_COPIES = 13


def rms_normed(values, gain):
    return values * lax.rsqrt(jnp.mean(values * values, -1, keepdims=True) + EPS) * gain


class Moves:
    def __init__(self, sems):
        self.sems, self.count, self.open = sems, 0, []

    def start(self, src, dst):
        one = pltpu.make_async_copy(src, dst, self.sems.at[self.count])
        self.count += 1
        one.start()
        return one

    def later(self, src, dst):
        self.open.append(self.start(src, dst))

    def finish(self):
        for one in self.open:
            one.wait()


def gather_scratch(rows, width, moves):
    return [
        pltpu.VMEM((8 * rows, width), bf16),
        pltpu.SemaphoreType.DMA((GATHER_COPIES,)),
        pltpu.SemaphoreType.DMA((GATHER_COPIES,)),
        pltpu.SemaphoreType.DMA((moves,)),
    ]


def own_rows(rows):
    return pl.ds(pl.multiple_of(other(0, 0, 0) * rows, rows), rows)


def gather_normed_kernel(ins, outs, scratch, line):
    x_ref, gain_ref = ins
    (all_ref,) = outs
    held, sends, recvs, sems = scratch
    rows = x_ref.shape[0]
    moves = Moves(sems)
    held[own_rows(rows), :] = rms_normed(x_ref[...].astype(f32), gain_ref[...]).astype(bf16)
    greet_group(line)
    line.open(0)

    def on_chip(*chip):
        where = chip_rows(*chip, rows)
        moves.later(held.at[where, :], all_ref.at[where, :])

    gather_rows(rows, held, sends, recvs, on_chip, line)
    moves.finish()


def gather_normed(x, gain, **line):
    rows, width = x.shape
    return run(
        gather_normed_kernel,
        [(x, VMEM), (gain, VMEM)],
        [(jax.ShapeDtypeStruct((8 * rows, width), bf16), ANY)],
        gather_scratch(rows, width, 4),
        line.pop("number"),
        (0, 150 * rows * width * 2, 0),
        **line,
    )[0]


def feed_forward_kernel(tile, ins, outs, scratch, line):
    mid_ref, gain_ref, w_ref = ins
    all_ref, hidden_ref, up_part_ref, gate_part_ref = outs
    held, sends, recvs, sems, weight, hidden, up_part, gate_part = scratch
    rows = mid_ref.shape[0]
    inner = hidden.shape[1]
    moves = Moves(sems)
    weight_copy = moves.start(w_ref, weight)
    held[own_rows(rows), :] = rms_normed(mid_ref[...], gain_ref[...]).astype(bf16)
    greet_group(line)
    line.open(0)

    def on_chip(*chip):
        where = chip_rows(*chip, rows)
        moves.later(held.at[where, :], all_ref.at[where, :])
        if chip == SIBLING:
            weight_copy.wait()

        def column(t, _):
            cols = pl.ds(pl.multiple_of(t * tile, tile), tile)
            up_cols = pl.ds(pl.multiple_of(inner + t * tile, tile), tile)
            lhs = held[where, :]
            gate = matmul_f32(lhs, weight[:, cols])
            up = matmul_f32(lhs, weight[:, up_cols])
            sigma = 1.0 / (1.0 + jnp.exp(-gate))
            swish = gate * sigma
            hidden[where, cols] = (swish * up).astype(bf16)
            up_part[where, cols] = swish.astype(bf16)
            gate_part[where, cols] = (up * sigma * (1.0 + gate * (1.0 - sigma))).astype(bf16)
            return 0

        lax.fori_loop(0, inner // tile, column, 0)
        for src, dst in ((hidden, hidden_ref), (up_part, up_part_ref), (gate_part, gate_part_ref)):
            moves.later(src.at[where, :], dst.at[where, :])

    gather_rows(rows, held, sends, recvs, on_chip, line)
    moves.finish()


def feed_forward(mid, gain, cols_gate_up, **line):
    rows, width = mid.shape
    inner = cols_gate_up.shape[1] // 2
    tall = jax.ShapeDtypeStruct((8 * rows, inner), bf16)
    return run(
        functools.partial(feed_forward_kernel, min(256, inner)),
        [(mid, VMEM), (gain, VMEM), (cols_gate_up, ANY)],
        [(jax.ShapeDtypeStruct((8 * rows, width), bf16), ANY)] + [(tall, ANY)] * 3,
        gather_scratch(rows, width, 17)
        + [pltpu.VMEM(cols_gate_up.shape, bf16)]
        + [pltpu.VMEM((8 * rows, inner), bf16)] * 3,
        line.pop("number"),
        (32 * rows * width * inner, 150 * rows * width * 2, 8 * rows * inner),
        **line,
    )


def feed_forward_back_kernel(tile, ins, outs, scratch, line):
    grad_ref, w_ref, hidden_ref, up_part_ref, gate_part_ref = ins
    grad_gate_up_ref, down_ref = outs
    held, sends, recvs, sems, weight, hidden, up_part, gate_part, grads, down, down_low = scratch
    rows = grad_ref.shape[0]
    inner, width = weight.shape
    moves = Moves(sems)
    loads = [
        moves.start(src, dst)
        for src, dst in (
            (w_ref, weight), (hidden_ref, hidden), (up_part_ref, up_part), (gate_part_ref, gate_part)
        )
    ]
    held[own_rows(rows), :] = grad_ref[...]
    greet_group(line)
    line.open(0)

    def on_chip(*chip):
        where = chip_rows(*chip, rows)
        if chip == SIBLING:
            for one in loads:
                one.wait()

        def column(t, _):
            cols = pl.ds(pl.multiple_of(t * tile, tile), tile)
            up_cols = pl.ds(pl.multiple_of(inner + t * tile, tile), tile)
            incoming = held[where, :]
            grad_hidden = against_rows(incoming, weight[cols, :])
            grads[where, cols] = (grad_hidden * gate_part[where, cols].astype(f32)).astype(bf16)
            grads[where, up_cols] = (grad_hidden * up_part[where, cols].astype(f32)).astype(bf16)
            term = over_tokens(hidden[where, cols], incoming)
            if chip == SIBLING:
                down[cols, :] = term
            elif chip == ACROSS:
                down_low[cols, :] = (down[cols, :] + term).astype(bf16)
            else:
                down[cols, :] += term
            return 0

        lax.fori_loop(0, inner // tile, column, 0)
        moves.later(grads.at[where, :], grad_gate_up_ref.at[where, :])

    gather_rows(rows, held, sends, recvs, on_chip, line)
    moves.later(down_low, down_ref)
    moves.finish()


def feed_forward_back(grad, w_down, hidden, up_part, gate_part, **line):
    rows, width = grad.shape
    inner = w_down.shape[0]
    return run(
        functools.partial(feed_forward_back_kernel, min(256, inner)),
        [(grad, VMEM)] + [(array, ANY) for array in (w_down, hidden, up_part, gate_part)],
        [
            (jax.ShapeDtypeStruct((8 * rows, 2 * inner), bf16), ANY),
            (jax.ShapeDtypeStruct((inner, width), bf16), ANY),
        ],
        gather_scratch(rows, width, 9)
        + [pltpu.VMEM(w_down.shape, bf16)]
        + [pltpu.VMEM((8 * rows, inner), bf16)] * 3
        + [
            pltpu.VMEM((8 * rows, 2 * inner), bf16),
            pltpu.VMEM(w_down.shape, f32),
            pltpu.VMEM(w_down.shape, bf16),
        ],
        line.pop("number"),
        (32 * rows * width * inner, 150 * rows * width * 2, 0),
        vmem=62,
        **line,
    )


def attended_back_kernel(ins, outs, scratch, line):
    grad_ref, w_ref, attended_ref = ins
    grad_attended_ref, out_term_ref = outs
    held, sends, recvs, sems, total = scratch
    rows = grad_ref.shape[0]
    moves = Moves(sems)
    held[own_rows(rows), :] = grad_ref[...]
    greet_group(line)
    line.open(0)

    def on_chip(*chip):
        where = chip_rows(*chip, rows)
        incoming = held[where, :]
        grad_attended_ref[where, :] = against_rows(incoming, w_ref[...]).astype(bf16)
        term = over_tokens(attended_ref[where, :], incoming)
        if chip == SIBLING:
            total[...] = term
        elif chip == ACROSS:
            out_term_ref[...] = (total[...] + term).astype(bf16)
        else:
            total[...] += term

    gather_rows(rows, held, sends, recvs, on_chip, line)
    moves.finish()


def attended_back(grad, w_out, attended, **line):
    rows, width = grad.shape
    return run(
        attended_back_kernel,
        [(array, VMEM) for array in (grad, w_out, attended)],
        [
            (jax.ShapeDtypeStruct(attended.shape, bf16), VMEM),
            (jax.ShapeDtypeStruct(w_out.shape, bf16), VMEM),
        ],
        gather_scratch(rows, width, 1) + [pltpu.VMEM(w_out.shape, f32)],
        line.pop("number"),
        (32 * rows * width * w_out.shape[0], 150 * rows * width * 2, 0),
        **line,
    )


class WeightTerm:
    def __init__(self, rows_ref, columns_ref, term_ref, scratch):
        self.rows_ref, self.columns_ref, self.term_ref = rows_ref, columns_ref, term_ref
        self.loaded, self.ready, self.sems = scratch
        self.tile = self.loaded.shape[2]
        for number in (0, 1):
            self.load(number).start()

    def load(self, number):
        cols = slice(number * self.tile, (number + 1) * self.tile)
        return pltpu.make_async_copy(
            self.rows_ref.at[:, cols], self.loaded.at[number % 2], self.sems.at[0, number % 2]
        )

    def store(self, number):
        return pltpu.make_async_copy(
            self.ready.at[number % 2], self.term_ref.at[number], self.sems.at[1, number % 2]
        )

    def work(self, numbers):
        for number in numbers:
            at = number % 2
            self.load(number).wait()
            if number >= 2:
                self.store(number - 2).wait()
            width = self.columns_ref.shape[1]
            step = min(256, width)

            def column(t, _):
                cols = pl.ds(pl.multiple_of(t * step, step), step)
                term = over_tokens(self.loaded[at], self.columns_ref[:, cols])
                self.ready[at, :, cols] = term.astype(bf16)
                return 0

            lax.fori_loop(0, width // step, column, 0)
            self.store(number).start()
            if number + 2 < 8:
                self.load(number + 2).start()

    def finish(self):
        for number in (6, 7):
            self.store(number).wait()


def scatter_kernel(turned, tile, extra, ins, outs, scratch, line):
    a_ref, b_ref = ins[:2]
    out_ref = outs[0]
    part, to_s, from_s, to_chip, held, relay, last, sends, recvs = scratch[:9]
    rows, width = out_ref.shape
    half = rows // 2
    _, _, core = place_in_group()
    greet_group(line)
    line.open(0)
    if extra:
        columns_ref = a_ref
        if extra == "loaded":
            columns_ref = scratch[12]
            columns_copy = pltpu.make_async_copy(ins[3], columns_ref, scratch[13].at[0])
            columns_copy.start()
        term = WeightTerm(ins[2], columns_ref, outs[1], scratch[9:12])
    own_at = pl.multiple_of(core * rows, rows)
    other_at = pl.multiple_of((1 - core) * rows, rows)
    started = []

    def send(number, src, dst, target):
        one = pltpu.make_async_remote_copy(
            src_ref=src, dst_ref=dst, send_sem=sends.at[number], recv_sem=recvs.at[number],
            device_id={"grp": other(*target)}, device_id_type=MESH,
        )
        one.start()
        started.append(one)
        return one

    def landed(number, where):
        pltpu.make_async_remote_copy(
            src_ref=where, dst_ref=where, send_sem=sends.at[number], recv_sem=recvs.at[number],
            device_id={"grp": other(0, 0, 1)}, device_id_type=MESH,
        ).wait_recv()

    to_sib, to_x, to_y = (0, 0, 1), (0, 1, 0), (1, 0, 0)

    def make(number, chip):
        where = chip_rows(*chip, rows)

        def column(t, _):
            cols = pl.ds(pl.multiple_of(t * tile, tile), tile)
            lhs = a_ref[where, :]
            if turned:
                part[:, cols] = against_rows(lhs, b_ref[cols, :])
            else:
                part[:, cols] = matmul_f32(lhs, b_ref[:, cols])
            return 0

        lax.fori_loop(0, width // tile, column, 0)
        to_s[number] = part[pl.ds(other_at, rows), :].astype(bf16)
        send(number, to_s.at[number], from_s.at[number], to_sib)

    def own(low, number):
        at = pl.ds(pl.multiple_of(core * rows + low * half, half), half)
        return part[at, :] + from_s[number, low * half : (low + 1) * half, :].astype(f32)

    first, second = slice(0, half), slice(half, rows)
    make(0, ACROSS)
    landed(0, from_s.at[0])
    to_chip[0, first, :] = own(0, 0).astype(bf16)
    send(4, to_chip.at[0, first, :], relay.at[0], to_x)
    to_chip[0, second, :] = own(1, 0).astype(bf16)
    send(5, to_chip.at[0, second, :], relay.at[1], to_y)
    make(1, ALONG_X)
    landed(1, from_s.at[1])
    to_chip[1, first, :] = own(0, 1).astype(bf16)
    send(6, to_chip.at[1, first, :], last.at[0, first, :], to_x)
    held[0] = own(1, 1)
    make(2, ALONG_Y)
    landed(2, from_s.at[2])
    to_chip[2, second, :] = own(1, 2).astype(bf16)
    send(7, to_chip.at[2, second, :], last.at[1, second, :], to_y)
    held[1] = own(0, 2)
    if extra:
        if extra == "loaded":
            columns_copy.wait()
        term.work((0, 1, 2))
    landed(5, relay.at[1])
    to_chip[1, second, :] = (held[0] + relay[1].astype(f32)).astype(bf16)
    send(8, to_chip.at[1, second, :], last.at[0, second, :], to_x)
    landed(4, relay.at[0])
    to_chip[2, first, :] = (held[1] + relay[0].astype(f32)).astype(bf16)
    send(9, to_chip.at[2, first, :], last.at[1, first, :], to_y)
    line.close(0)
    line.open(1)
    make(3, SIBLING)
    if extra:
        term.work((3, 4, 5, 6, 7))
    landed(3, from_s.at[3])
    for low in (0, 1):
        out_ref[low * half : (low + 1) * half, :] = own(low, 3)
    landed(6, last.at[0, first, :])
    out_ref[first, :] += last[0, first, :].astype(f32)
    landed(7, last.at[1, second, :])
    out_ref[second, :] += last[1, second, :].astype(f32)
    landed(8, last.at[0, second, :])
    out_ref[second, :] += last[0, second, :].astype(f32)
    landed(9, last.at[1, first, :])
    out_ref[first, :] += last[1, first, :].astype(f32)
    for one in started:
        one.wait_send()
    if extra:
        term.finish()
    line.close(1)
    line.finish()


def product_scattered(a, b, turned, extra=None, **line):
    length, depth = a.shape
    width = b.shape[0] if turned else b.shape[1]
    rows = length // 8
    tile = min(256, width)
    ins = [(a, VMEM), (b, VMEM)]
    outs = [(jax.ShapeDtypeStruct((rows, width), f32), VMEM)]
    scratch = [
        pltpu.VMEM((2 * rows, width), f32),
        pltpu.VMEM((4, rows, width), bf16),
        pltpu.VMEM((4, rows, width), bf16),
        pltpu.VMEM((3, rows, width), bf16),
        pltpu.VMEM((2, rows // 2, width), f32),
        pltpu.VMEM((2, rows // 2, width), bf16),
        pltpu.VMEM((2, rows, width), bf16),
        pltpu.SemaphoreType.DMA((10,)),
        pltpu.SemaphoreType.DMA((10,)),
    ]
    flops, kind = 2 * length * depth * width, None
    if extra:
        first, second = extra
        kind = "own" if second is None else "loaded"
        ins.append((first, ANY))
        columns = a if second is None else second
        tall = first.shape[1] // 8
        outs.append((jax.ShapeDtypeStruct((8, tall, columns.shape[1]), bf16), ANY))
        scratch += [
            pltpu.VMEM((2, length, tall), bf16),
            pltpu.VMEM((2, tall, columns.shape[1]), bf16),
            pltpu.SemaphoreType.DMA((2, 2)),
        ]
        if second is not None:
            ins.append((second, ANY))
            scratch += [pltpu.VMEM(second.shape, bf16), pltpu.SemaphoreType.DMA((1,))]
        flops += 2 * length * first.shape[1] * columns.shape[1]
    return run(
        functools.partial(scatter_kernel, turned, tile, kind), ins, outs, scratch,
        line.pop("number"), (flops, 150 * rows * width * 2, 0), vmem=60, **line,
    )


def tail_kernel(ready, later, ins, outs, scratch, line):
    qkv_ref, gains_ref = ins[:2]
    chunk_refs = dict(zip(ready, ins[2:]))
    gate_ref, up_ref, qkv_rows_ref, gains_out_ref = outs
    from_group, mine, from_rep, sends, recvs, chunk_sems, local = scratch
    me, rank = other(0, 0, 0), lax.axis_index("rep")
    inner = gate_ref.shape[1] // 8
    part = qkv_ref.shape[-1]
    high = line.outs[later[0]].shape[1]
    barrier = pltpu.get_barrier_semaphore()
    for flip in range(1, 4):
        pl.semaphore_signal(
            barrier, inc=1, device_id={"rep": (rank + flip) % 4}, device_id_type=MESH
        )
    for flip in EVERYONE:
        pl.semaphore_signal(barrier, inc=1, device_id={"grp": other(*flip)}, device_id_type=MESH)
    pl.semaphore_wait(barrier, 10)
    waits, moves = [], Moves(local)
    line.refs["qkv"] = qkv_rows_ref

    def send(kind, number, src, dst, device):
        return pltpu.make_async_remote_copy(
            src_ref=src, dst_ref=dst, send_sem=sends.at[kind, number],
            recv_sem=recvs.at[kind, number], device_id=device, device_id_type=MESH,
        )

    own_qkv = qkv_rows_ref.at[me // 4, :, :, pl.ds(pl.multiple_of((me % 4) * part, part), part)]
    qkv_copies, gain_copies = [], []
    for number, flip in enumerate(EVERYONE):
        target = other(*flip)
        qkv_copies.append(send(0, number, qkv_ref.at[target], own_qkv, {"grp": target}))
        qkv_copies[-1].start()
    moves.later(qkv_ref.at[me], own_qkv)
    line.open(0)
    for number, flip in enumerate(EVERYONE):
        target = other(*flip)
        gain_copies.append(
            send(1, number, gains_ref.at[target], from_group.at[me], {"grp": target})
        )
        gain_copies[-1].start()
    from_group[me] = gains_ref[me]

    def spread(chunk):
        src = chunk_refs[chunk] if chunk in chunk_refs else line.outs[chunk]
        number = chunk - 4
        rows = slice(number * high, (number + 1) * high)
        cols = pl.ds(pl.multiple_of(me * inner, inner), inner)
        for which, dst in enumerate((gate_ref, up_ref)):
            there = dst.at[rows, cols]
            for flip in EVERYONE:
                target = other(*flip)
                pltpu.make_async_remote_copy(
                    src_ref=src.at[target, :, which * inner : (which + 1) * inner], dst_ref=there,
                    send_sem=chunk_sems.at[0, which, number], recv_sem=chunk_sems.at[1, which, number],
                    device_id={"grp": target}, device_id_type=MESH,
                ).start()
            moves.later(src.at[me, :, which * inner : (which + 1) * inner], there)
            seven = dst.at[rows, : 7 * inner]
            waits.append(
                pltpu.make_async_remote_copy(
                    src_ref=seven, dst_ref=seven, send_sem=chunk_sems.at[0, which, number],
                    recv_sem=chunk_sems.at[1, which, number],
                    device_id={"grp": other(0, 0, 1)}, device_id_type=MESH,
                )
            )

    for chunk in ready:
        spread(chunk)
    for one in gain_copies:
        one.wait()
    mine[rank] = sum(from_group[g] for g in range(8))
    rep_copies = []
    for step in range(1, 4):
        target = (rank + step) % 4
        rep_copies.append(
            send(2, step, mine.at[rank], from_rep.at[step], {"rep": target})
        )
        rep_copies[-1].start()
    for step, one in zip(range(1, 4), rep_copies):
        one.wait()
        mine[(rank + 4 - step) % 4] = from_rep[step]
    gains_out_ref[...] = (mine[0] + mine[1]) + (mine[2] + mine[3])
    line.close(0)
    for number in range(1, line.ticks):
        if line.first + number == CHUNKS - 2:
            for one in qkv_copies:
                one.wait()
            moves.open.pop(0).wait()
        line.open(number)
        chunk = line.first + number - 3
        if chunk in later:
            spread(chunk)
        line.close(number)
    for one in waits:
        one.wait_send()
        one.wait_recv()
    moves.finish()


def tail(qkv_term, gains, chunks, inner, number, sums, ticks, arrays, picks):
    first = sums.tick
    ready = sorted(chunks)
    later = [c for c in line_slots(first, ticks) if c < 12]
    _, high, width = sums.shape
    part = qkv_term.shape[-1]
    wide = jax.ShapeDtypeStruct((8 * high, 8 * inner), bf16)
    moved = jax.ShapeDtypeStruct((2,) + sums.shape, bf16)
    picks = dict(picks)
    for half in (0, 1):
        picks[CHUNKS - 2 + half] = ("qkv", lambda ref, half=half: ref.at[half])
    return run(
        functools.partial(tail_kernel, ready, later),
        [(qkv_term, ANY), (gains, VMEM)] + [(chunks[c], ANY) for c in ready],
        [(wide, ANY), (wide, ANY), (moved, ANY), (jax.ShapeDtypeStruct(gains.shape[1:], f32), VMEM)],
        [
            pltpu.VMEM(gains.shape, f32),
            pltpu.VMEM((4,) + gains.shape[1:], f32),
            pltpu.VMEM((4,) + gains.shape[1:], f32),
            pltpu.SemaphoreType.DMA((3, 7)),
            pltpu.SemaphoreType.DMA((3, 7)),
            pltpu.SemaphoreType.DMA((2, 2, 8)),
            pltpu.SemaphoreType.DMA((17,)),
        ],
        number, (0, 200 * 8 * high * width * 2, 0), sums=sums, ticks=ticks, arrays=arrays, picks=picks,
    )


def sum_over_sequences(term):
    return lax.psum(term, "rep").astype(f32)


def on_device(
    layer_input,
    cotangent,
    cut_order,
    piece_ids,
    w_query,
    w_key,
    w_value,
    w_out,
    w_gate,
    w_up,
    w_down,
    gain_attn,
    gain_ffn,
):
    groups = lax.axis_size("grp")
    reps = lax.axis_size("rep")
    own_index = lax.axis_index("grp")
    _, local_rows, model_width = layer_input.shape
    length = piece_ids.shape[1]
    rows_here = w_query.shape[0]
    q_width = w_query.shape[1]
    kv_heads = w_key.shape[1] // HD
    heads = q_width // HD // groups
    copies = groups // kv_heads
    hidden_here = w_down.shape[0]
    piece_col = jnp.broadcast_to(piece_ids.reshape(length, 1), (length, HD))
    cosine, sine = turn_tables(length)

    near = groups == 8 and reps == 4 and copies == 1

    def gather(rows):
        return lax.all_gather(rows, "grp", axis=0, tiled=True)

    def scatter(first, second, turned):
        term = against_rows(first, second) if turned else matmul_f32(first, second)
        return lax.psum_scatter(
            term.astype(bf16), "grp", scatter_dimension=0, tiled=True
        ).astype(f32)

    def to_columns(parts):
        return lax.all_to_all(parts, "grp", 1, 0, tiled=True).reshape(-1, parts.shape[-1])

    def per_group(weight):
        return weight.reshape(rows_here, groups, -1)

    def per_kv_head(weight):
        return jnp.repeat(weight.reshape(rows_here, kv_heads, HD), copies, axis=1)

    x_rows = layer_input.reshape(local_rows, model_width)
    x_flat = x_rows.astype(f32)
    inv_one = lax.rsqrt(jnp.mean(x_flat * x_flat, -1, keepdims=True) + EPS)
    unit_one = x_flat * inv_one
    attn_gain, ffn_gain = gain_attn.reshape(1, -1), gain_ffn.reshape(1, -1)
    cols_qkv = to_columns(
        jnp.concatenate([per_group(w_query), per_kv_head(w_key), per_kv_head(w_value)], -1)
    )
    if near:
        normed_one = gather_normed(x_rows, attn_gain, number=1)
    else:
        normed_one = gather(rms_normed(x_flat, attn_gain).astype(bf16))
    qkv = matmul_f32(normed_one, cols_qkv)
    attended, query, key, value, lse, attended_placed = attend(
        cut_order, qkv, cosine, sine, piece_ids, piece_col, heads
    )
    cols_gate_up = to_columns(jnp.concatenate([per_group(w_gate), per_group(w_up)], -1))
    if near:
        out_sum = product_scattered(attended, w_out, False, number=2)[0]
    else:
        out_sum = scatter(attended, w_out, False)
    mid = x_flat + out_sum
    inv_two = lax.rsqrt(jnp.mean(mid * mid, -1, keepdims=True) + EPS)
    unit_two = mid * inv_two
    grad_out = cotangent.reshape(local_rows, model_width)

    def finish_two(grad_two):
        return norm_back(grad_out.astype(f32), grad_two, unit_two, inv_two, gain_ffn)

    def finish_one(grad_mid, grad_one):
        grad_input, gain_term = norm_back(grad_mid, grad_one, unit_one, inv_one, gain_attn)
        return grad_input.astype(bf16).reshape(layer_input.shape), gain_term

    def back_through_attention(grad_attended, **line):
        return attend_back(
            cut_order, grad_attended, attended_placed, query, key, value, lse, cosine, sine,
            piece_ids, piece_col, heads, **line,
        )

    def result_of(down_sum):
        return (mid + down_sum).astype(bf16).reshape(layer_input.shape)

    q_here = heads * HD
    if near:
        normed_two, hidden, up_part, gate_part = feed_forward(
            mid, ffn_gain, cols_gate_up, number=3
        )
        grad_gate_up, down_term = feed_forward_back(
            grad_out, w_down, hidden, up_part, gate_part, number=4
        )
        high = rows_here // 8
        sums = Sums((8, high, model_width))
        terms = {"down": down_term.reshape((4,) + sums.shape)}

        def pick_down(number):
            return "down", lambda ref: ref.at[number]

        def pick_gate_up(number):
            return "gate_up", lambda ref: ref.at[:, number * high : (number + 1) * high, :]

        picks = [pick_down(n) for n in range(4)] + [pick_gate_up(n) for n in range(8)]
        picks += [("out", lambda ref: ref)]

        def line(number, ticks):
            names = sorted(
                {picks[t][0] for t in range(sums.tick, sums.tick + ticks) if t < len(picks)}
            )
            return dict(
                number=number, ticks=ticks, sums=sums, picks=dict(enumerate(picks)),
                arrays=[(name, terms[name]) for name in names],
            )

        down_sum, terms["gate_up"] = product_scattered(
            hidden, w_down, False, extra=(normed_two, grad_gate_up), **line(5, 2)
        )
        result = result_of(down_sum)
        grad_two = product_scattered(grad_gate_up, cols_gate_up, True, **line(6, 2))[0]
        grad_mid, gain_ffn_term = finish_two(grad_two)
        grad_attended, out_term = attended_back(
            grad_mid.astype(bf16), w_out, attended, **line(7, 2)
        )
        terms["out"] = out_term.reshape(sums.shape)
        grad_qkv = back_through_attention(grad_attended, **line(8, 1))
        grad_one, qkv_term = product_scattered(
            grad_qkv, cols_qkv, True, extra=(normed_one, None), **line(9, 2)
        )
        grad_x, gain_attn_term = finish_one(grad_mid, grad_one)
        gains = jnp.stack([gain_attn_term, gain_ffn_term]).reshape(2, groups, rows_here)
        gains = jnp.pad(jnp.moveaxis(gains, 0, 1), ((0, 0), (0, 6), (0, 0)))
        rest = line(10, 8)
        gate_rows, up_rows, qkv_rows, own_gains = tail(
            qkv_term.reshape(8, 8, high, -1), gains,
            {c: sums.done[c] for c in range(4, 7)}, hidden_here, **rest,
        )
        qkv_rows = jnp.stack([sums.done[13], sums.done[14]], 2).astype(f32)
        qkv_rows = qkv_rows.reshape(8, high, 2, 4, -1)

        def columns(low, above):
            return qkv_rows[..., low:above].reshape(rows_here, -1)

        return (
            result,
            grad_x,
            columns(0, q_here),
            columns(q_here, q_here + HD),
            columns(q_here + HD, q_here + 2 * HD),
            sums.done[12].reshape(rows_here, model_width).astype(f32),
            gate_rows.astype(f32),
            up_rows.astype(f32),
            jnp.stack([sums.done[n] for n in range(4)]).reshape(hidden_here, -1).astype(f32),
            own_gains[0],
            own_gains[1],
        )

    normed_two = gather((unit_two * ffn_gain).astype(bf16))
    grad_all = gather(grad_out)
    gate_up = matmul_f32(normed_two, cols_gate_up)
    gate_proj, up_proj = gate_up[:, :hidden_here], gate_up[:, hidden_here:]
    sigmoid_gate = jax.nn.sigmoid(gate_proj)
    swish = gate_proj * sigmoid_gate
    hidden = (swish * up_proj).astype(bf16)
    gate_part = up_proj * sigmoid_gate * (1.0 + gate_proj * (1.0 - sigmoid_gate))
    down_term = over_tokens(hidden, grad_all).astype(bf16)
    grad_hidden = against_rows(grad_all, w_down)
    grad_gate_up = jnp.concatenate([grad_hidden * gate_part, grad_hidden * swish], 1).astype(bf16)
    grad_mid, gain_ffn_term = finish_two(scatter(grad_gate_up, cols_gate_up, True))
    grad_mid_low = gather(grad_mid.astype(bf16))
    grad_qkv = back_through_attention(against_rows(grad_mid_low, w_out).astype(bf16))
    grad_x, gain_attn_term = finish_one(grad_mid, scatter(grad_qkv, cols_qkv, True))

    def to_rows(term):
        return lax.all_to_all(
            term.astype(bf16).reshape(groups, rows_here, -1), "grp", 0, 0, tiled=True
        )

    def whole_rows(term):
        return jnp.moveaxis(term, 0, 1).reshape(rows_here, -1)

    def kv_rows(term):
        return jnp.sum(
            jnp.moveaxis(term, 0, 1).reshape(rows_here, kv_heads, copies, HD), 2
        ).reshape(rows_here, -1)

    gate_up_term = sum_over_sequences(to_rows(over_tokens(normed_two, grad_gate_up)))
    out_term = sum_over_sequences(over_tokens(attended, grad_mid_low).astype(bf16))
    qkv_term = sum_over_sequences(to_rows(over_tokens(normed_one, grad_qkv)))
    gain_total = lax.psum(jnp.stack([gain_attn_term, gain_ffn_term]), ("grp", "rep"))
    own_gains = lax.dynamic_slice_in_dim(gain_total, own_index * rows_here, rows_here, 1)
    return (
        result_of(scatter(hidden, w_down, False)),
        grad_x,
        whole_rows(qkv_term[..., :q_here]),
        kv_rows(qkv_term[..., q_here : q_here + HD]),
        kv_rows(qkv_term[..., q_here + HD :]),
        out_term,
        whole_rows(gate_up_term[..., :hidden_here]),
        whole_rows(gate_up_term[..., hidden_here:]),
        sum_over_sequences(down_term),
        own_gains[0],
        own_gains[1],
    )


def solution(mesh):
    tokens, table, rows, whole = P("rep", "grp", None), P("rep", None), P("grp", None), P()
    return jax.shard_map(
        on_device,
        mesh=mesh,
        in_specs=(tokens, tokens, table, table) + (rows,) * 7 + (whole,) * 2,
        out_specs=(tokens, tokens) + (rows,) * 7 + (P("grp"),) * 2,
        check_vma=False,
    )
```

```python
import functools

import jax
import jax.numpy as jnp
from jax import lax
from jax.experimental import pallas as pl
from jax.experimental.pallas import tpu as pltpu
from jax.sharding import PartitionSpec as P

HD = 128
EPS = 1e-05
ROPE_BASE = 1000000.0
SCORE_SCALE = HD**-0.5
LOG2E = 1.4426950408889634
TO_EXP2 = SCORE_SCALE * LOG2E
NEG = -1e30

MESH = pl.DeviceIdType.MESH
f32 = jnp.float32
bf16 = jnp.bfloat16


def matmul_f32(first, second):
    return jnp.dot(first, second, preferred_element_type=f32)


def against_rows(first, second):
    return lax.dot_general(first, second, (((1,), (1,)), ((), ())), preferred_element_type=f32)


def over_tokens(first, second):
    return lax.dot_general(first, second, (((0,), (0,)), ((), ())), preferred_element_type=f32)


def turn_tables(length):
    half_size = HD // 2
    inverse = ROPE_BASE ** (-(jnp.arange(half_size, dtype=f32) * 2.0) / HD)
    angles = jnp.arange(length, dtype=jnp.int32).astype(f32)[:, None] * inverse
    cosine, sine = jnp.cos(angles), jnp.sin(angles)
    return jnp.concatenate([cosine, cosine], -1), jnp.concatenate([-sine, sine], -1)


def norm_back(upstream, grad_normed, unit_rows, inv_root, gain):
    scaled = grad_normed * gain
    center_term = jnp.mean(scaled * unit_rows, -1, keepdims=True)
    return (
        upstream + inv_root * (scaled - unit_rows * center_term),
        jnp.sum(grad_normed * unit_rows, 0),
    )


def fold_lanes(values, op):
    out = values[:, :HD]
    for at in range(HD, values.shape[1], HD):
        out = op(out, values[:, at : at + HD])
    return out


def as_row(column):
    return jnp.broadcast_to(column, (column.shape[0], HD)).T[0:1, :]


def attend_kernel(
    heads, cuts, block,
    order_ref, qkv_ref, cos_ref, sin_ref, piece_ref, piece_col_ref,
    out_ref, q_ref, k_ref, v_ref, lse_ref, placed,
    scores,
):
    length = qkv_ref.shape[0]
    cut = length // cuts
    blocks = length // block

    def place_cut(r, _):
        src = pl.ds(pl.multiple_of(r * cut, cut), cut)
        dst = pl.ds(pl.multiple_of(order_ref[0, r] * cut, cut), cut)
        cosine, sine = cos_ref[dst, :], sin_ref[dst, :]
        for h in range(heads + 1):
            part = qkv_ref[src, h * HD : (h + 1) * HD]
            turned = (part * cosine + pltpu.roll(part, HD // 2, 1) * sine).astype(bf16)
            if h < heads:
                q_ref[h, dst, :] = turned
            else:
                k_ref[dst, :] = turned
        v_ref[dst, :] = qkv_ref[src, (heads + 1) * HD :].astype(bf16)
        return 0

    lax.fori_loop(0, cuts, place_cut, 0)

    def one_block(i, _):
        rows = pl.ds(pl.multiple_of(i * block, block), block)
        query = q_ref[:, rows, :].reshape(heads * block, HD)

        def score(j, high):
            cols = pl.ds(pl.multiple_of(j * block, block), block)
            tile = against_rows(query, k_ref[cols, :])
            scores[j] = tile
            return jnp.maximum(high, fold_lanes(tile, jnp.maximum))

        high = lax.fori_loop(0, i, score, jnp.full((heads * block, HD), NEG, f32))
        tile = against_rows(query, k_ref[rows, :])
        q_at = lax.broadcasted_iota(jnp.int32, (block, block), 0)
        k_at = lax.broadcasted_iota(jnp.int32, (block, block), 1)
        q_piece, k_piece = piece_col_ref[rows, 0:1], piece_ref[0:1, rows]
        allowed = (k_at <= q_at) | ((q_piece != 0) & (q_piece == k_piece))
        tile = jnp.concatenate(
            [jnp.where(allowed, tile[h * block : (h + 1) * block], NEG) for h in range(heads)], 0
        )
        scores[i] = tile
        high = jnp.max(jnp.maximum(high, fold_lanes(tile, jnp.maximum)), 1, keepdims=True)

        def weigh(j, state):
            total, mixed = state
            cols = pl.ds(pl.multiple_of(j * block, block), block)
            prob = jnp.exp2((scores[j] - high) * TO_EXP2)
            total = total + fold_lanes(prob, jnp.add)
            return total, mixed + matmul_f32(prob.astype(bf16), v_ref[cols, :])

        zero = jnp.zeros((heads * block, HD), f32)
        total, mixed = lax.fori_loop(0, i + 1, weigh, (zero, zero))
        total = jnp.sum(total, 1, keepdims=True)
        mixed = (mixed / total).astype(bf16)
        log_total = high * TO_EXP2 + jnp.log2(total)
        for h in range(heads):
            placed[rows, h * HD : (h + 1) * HD] = mixed[h * block : (h + 1) * block]
            lse_ref[h : h + 1, rows] = as_row(log_total[h * block : (h + 1) * block])
        return 0

    lax.fori_loop(0, blocks, one_block, 0)

    def store_cut(r, _):
        dst = pl.ds(pl.multiple_of(r * cut, cut), cut)
        src = pl.ds(pl.multiple_of(order_ref[0, r] * cut, cut), cut)
        out_ref[dst, :] = placed[src, :]
        return 0

    lax.fori_loop(0, cuts, store_cut, 0)


def vmem_specs(count):
    return [pl.BlockSpec(memory_space=pltpu.VMEM)] * count


def attend(order, qkv, cosine, sine, piece, piece_col, heads):
    length = qkv.shape[0]
    block = min(512, length)
    return pl.pallas_call(
        functools.partial(attend_kernel, heads, order.shape[1], block),
        out_shape=(
            jax.ShapeDtypeStruct((length, heads * HD), bf16),
            jax.ShapeDtypeStruct((heads, length, HD), bf16),
            jax.ShapeDtypeStruct((length, HD), bf16),
            jax.ShapeDtypeStruct((length, HD), bf16),
            jax.ShapeDtypeStruct((heads, length), f32),
            jax.ShapeDtypeStruct((length, heads * HD), bf16),
        ),
        in_specs=[pl.BlockSpec(memory_space=pltpu.SMEM)] + vmem_specs(5),
        out_specs=tuple(vmem_specs(6)),
        scratch_shapes=[pltpu.VMEM((length // block, heads * block, block), f32)],
        compiler_params=pltpu.CompilerParams(vmem_limit_bytes=48 * 2**20),
        cost_estimate=pl.CostEstimate(
            flops=3 * heads * length * length * HD, bytes_accessed=10 * length * HD * heads * 4,
            transcendentals=heads * length * length // 2,
        ),
    )(order, qkv, cosine, sine, piece, piece_col)


CHUNKS = 15


def is_middle():
    rank = lax.axis_index("rep")
    return (rank == 1) | (rank == 2)


def is_end():
    rank = lax.axis_index("rep")
    return (rank == 0) | (rank == 3)


class NoLine:
    ticks = 0

    def greet(self, barrier, others):
        if others:
            pl.semaphore_wait(barrier, others)

    def open(self, number):
        pass

    def close(self, number):
        pass

    def finish(self):
        pass


class Line:
    def __init__(self, first, ticks, picks, refs, outs, scratch):
        self.first, self.ticks, self.picks, self.refs, self.outs = first, ticks, picks, refs, outs
        self.inward, self.across, self.own, self.pair, self.total, self.sems, self.local = scratch
        rank = lax.axis_index("rep")
        self.partner = {"rep": rank + 1 - 2 * (rank % 2)}
        self.peer = {"rep": 3 - rank}
        self.slots = line_slots(first, ticks)

    def greet(self, barrier, others):
        pl.semaphore_signal(barrier, inc=1, device_id=self.partner, device_id_type=MESH)

        @pl.when(is_middle())
        def _():
            pl.semaphore_signal(barrier, inc=1, device_id=self.peer, device_id_type=MESH)
            pl.semaphore_wait(barrier, others + 2)

        @pl.when(is_end())
        def _():
            pl.semaphore_wait(barrier, others + 1)

    def remote(self, hop, number, src, dst, device):
        return pltpu.make_async_remote_copy(
            src_ref=src, dst_ref=dst, send_sem=self.sems.at[0, hop, number],
            recv_sem=self.sems.at[1, hop, number], device_id=device, device_id_type=MESH,
        )

    def hops(self, number):
        tick = self.first + number
        term = pair = total = None
        if tick < CHUNKS:
            which, pick = self.picks[tick]
            term = (
                lambda: self.remote(
                    0, number, pick(self.refs[which]), self.inward.at[number], self.partner
                ),
                lambda: pltpu.make_async_copy(
                    pick(self.refs[which]), self.own.at[number % 2], self.local.at[0, number]
                ),
            )
        if 1 <= tick <= CHUNKS:
            before = self.refs["pair"] if number == 0 else self.pair.at[(number - 1) % 2]
            pair = (
                lambda: self.remote(1, number, before, self.across.at[number], self.peer),
                lambda: pltpu.make_async_copy(before, self.pair.at[2], self.local.at[1, number]),
            )
        if 2 <= tick <= CHUNKS + 1:
            done = self.refs["total"] if number == 0 else self.total.at[(number - 1) % 2]
            slot = self.outs[tick - 2]
            total = (
                lambda: self.remote(2, number, done, slot, self.partner),
                lambda: pltpu.make_async_copy(done, slot, self.local.at[2, number]),
            )
        return term, pair, total

    def open(self, number):
        if number >= self.ticks:
            return
        term, pair, total = self.hops(number)

        @pl.when(is_end())
        def _():
            if term:
                term[0]().start()

        @pl.when(is_middle())
        def _():
            if pair:
                pair[0]().start()
            if total:
                total[0]().start()
                total[1]().start()
            if term:
                term[1]().start()
            if pair and number == 0:
                pair[1]().start()

    def close(self, number):
        if number >= self.ticks:
            return
        term, pair, total = self.hops(number)

        def add(into, first, second):
            def one(g, _):
                into[g] = (first[g].astype(f32) + second[g].astype(f32)).astype(bf16)
                return 0

            lax.fori_loop(0, into.shape[0], one, 0)

        @pl.when(is_end())
        def _():
            if term:
                term[0]().wait_send()
            if total:
                total[0]().wait_recv()

        @pl.when(is_middle())
        def _():
            if total:
                total[0]().wait_send()
                total[1]().wait()
            if pair:
                pair[0]().wait_send()
                pair[0]().wait_recv()
                if number == 0:
                    pair[1]().wait()
                before = 2 if number == 0 else (number - 1) % 2
                add(self.total.at[number % 2], self.pair.at[before], self.across.at[number])
            if term:
                term[1]().wait()
                term[0]().wait_recv()
                add(self.pair.at[number % 2], self.own.at[number % 2], self.inward.at[number])

    def finish(self):
        last = self.ticks - 1
        tick = self.first + last

        @pl.when(is_middle())
        def _():
            if tick < CHUNKS:
                keep = pltpu.make_async_copy(
                    self.pair.at[last % 2], self.outs["pair"], self.local.at[0, last]
                )
                keep.start()
                keep.wait()
            if 1 <= tick <= CHUNKS:
                keep = pltpu.make_async_copy(
                    self.total.at[last % 2], self.outs["total"], self.local.at[1, last]
                )
                keep.start()
                keep.wait()


def line_slots(first, ticks):
    return [t - 2 for t in range(first, first + ticks) if 2 <= t <= CHUNKS + 1]


class Sums:
    def __init__(self, shape):
        self.shape, self.tick, self.pair, self.total, self.done = shape, 0, None, None, {}


def run(kernel, ins, outs, scratch, number, cost, sums=None, ticks=0, arrays=(), picks=None, vmem=58):
    ins, outs, scratch = list(ins), list(outs), list(scratch)
    counts = (len(ins), len(outs), len(scratch))
    first = sums.tick if ticks else 0
    names_in, names_out = [], []
    if ticks:
        last = first + ticks - 1
        chunk = jax.ShapeDtypeStruct(sums.shape, bf16)
        for name, array in arrays:
            names_in.append(name)
            ins.append((array, pl.ANY))
        if 1 <= first <= CHUNKS:
            names_in.append("pair")
            ins.append((sums.pair, pl.ANY))
        if 2 <= first <= CHUNKS + 1:
            names_in.append("total")
            ins.append((sums.total, pl.ANY))
        names_out = line_slots(first, ticks)
        if last < CHUNKS:
            names_out.append("pair")
        if 1 <= last <= CHUNKS:
            names_out.append("total")
        outs += [(chunk, pl.ANY)] * len(names_out)
        scratch += [
            pltpu.VMEM((ticks,) + sums.shape, bf16),
            pltpu.VMEM((ticks,) + sums.shape, bf16),
            pltpu.VMEM((2,) + sums.shape, bf16),
            pltpu.VMEM((3,) + sums.shape, bf16),
            pltpu.VMEM((2,) + sums.shape, bf16),
            pltpu.SemaphoreType.DMA((2, 3, ticks)),
            pltpu.SemaphoreType.DMA((3, ticks)),
        ]

    def body(*refs):
        in_refs, rest = refs[: len(ins)], refs[len(ins) :]
        out_refs, scratch_refs = rest[: len(outs)], rest[len(outs) :]
        line = NoLine()
        if ticks:
            line = Line(
                first, ticks, picks, dict(zip(names_in, in_refs[counts[0] :])),
                dict(zip(names_out, out_refs[counts[1] :])), scratch_refs[counts[2] :],
            )
        kernel(in_refs[: counts[0]], out_refs[: counts[1]], scratch_refs[: counts[2]], line)

    results = pl.pallas_call(
        body,
        out_shape=tuple(shape for shape, _ in outs),
        in_specs=[pl.BlockSpec(memory_space=space) for _, space in ins],
        out_specs=tuple(pl.BlockSpec(memory_space=space) for _, space in outs),
        scratch_shapes=scratch,
        compiler_params=pltpu.CompilerParams(
            vmem_limit_bytes=vmem * 2**20,
            **({} if number is None else {"collective_id": number, "has_side_effects": True}),
        ),
        cost_estimate=pl.CostEstimate(
            flops=cost[0], bytes_accessed=cost[1], transcendentals=cost[2]
        ),
    )(*[array for array, _ in ins])
    for name, result in zip(names_out, results[counts[1] :]):
        if name == "pair":
            sums.pair = result
        elif name == "total":
            sums.total = result
        else:
            sums.done[name] = result
    if ticks:
        sums.tick += ticks
    return results[: counts[1]]


SMEM, VMEM, ANY = pltpu.SMEM, pltpu.VMEM, pl.ANY


def attend_back_kernel(
    heads, block, ins, outs, scratch, line
):
    grad_ref, out_ref, q_ref, k_ref, v_ref, lse_ref, cos_ref, sin_ref, piece_ref, piece_col_ref = ins
    (grad_qkv_ref,) = outs
    grads, centers, grad_q = scratch
    if line.ticks:
        line.greet(pltpu.get_barrier_semaphore(), 0)
        line.open(0)
    length = grad_ref.shape[0]
    blocks = length // block

    def take_block(i, _):
        rows = pl.ds(pl.multiple_of(i * block, block), block)
        for h in range(heads):
            grad = grad_ref[rows, h * HD : (h + 1) * HD].astype(bf16)
            grads[h, rows, :] = grad
            product = grad.astype(f32) * out_ref[rows, h * HD : (h + 1) * HD].astype(f32)
            centers[h, rows, :] = jnp.broadcast_to(
                jnp.sum(product, 1, keepdims=True), (block, HD)
            )
        return 0

    lax.fori_loop(0, blocks, take_block, 0)
    grad_q[...] = jnp.zeros_like(grad_q)

    def key_block(j, _):
        cols = pl.ds(pl.multiple_of(j * block, block), block)
        key, value = k_ref[cols, :], v_ref[cols, :]

        def one(i, state, diagonal):
            grad_key, grad_value = state
            rows = pl.ds(pl.multiple_of(i * block, block), block)
            for h in range(heads):
                query, grad = q_ref[h, rows, :], grads[h, rows, :]
                log_total = lse_ref[h : h + 1, rows]
                center = centers[h, rows, :].T[0:1, :]
                prob = jnp.exp2(against_rows(key, query) * TO_EXP2 - log_total)
                if diagonal:
                    k_at = lax.broadcasted_iota(jnp.int32, (block, block), 0)
                    q_at = lax.broadcasted_iota(jnp.int32, (block, block), 1)
                    k_piece, q_piece = piece_col_ref[cols, 0:1], piece_ref[0:1, cols]
                    allowed = (k_at <= q_at) | ((q_piece != 0) & (q_piece == k_piece))
                    prob = jnp.where(allowed, prob, 0.0)
                grad_prob = against_rows(value, grad)
                grad_score = (prob * (grad_prob - center)).astype(bf16)
                grad_value = grad_value + matmul_f32(prob.astype(bf16), grad)
                grad_key = grad_key + matmul_f32(grad_score, query)
                grad_q[h, rows, :] += over_tokens(grad_score, key)
            return grad_key, grad_value

        zero = jnp.zeros((block, HD), f32)
        state = one(j, (zero, zero), True)
        grad_key, grad_value = lax.fori_loop(
            j + 1, blocks, functools.partial(one, diagonal=False), state
        )
        grad_key = grad_key * SCORE_SCALE
        grad_key = grad_key * cos_ref[cols, :] - pltpu.roll(grad_key, HD // 2, 1) * sin_ref[cols, :]
        grad_qkv_ref[cols, heads * HD : (heads + 1) * HD] = grad_key.astype(bf16)
        grad_qkv_ref[cols, (heads + 1) * HD :] = grad_value.astype(bf16)
        return 0

    lax.fori_loop(0, blocks, key_block, 0)

    def turn_back(i, _):
        rows = pl.ds(pl.multiple_of(i * block, block), block)
        for h in range(heads):
            grad = grad_q[h, rows, :] * SCORE_SCALE
            grad = grad * cos_ref[rows, :] - pltpu.roll(grad, HD // 2, 1) * sin_ref[rows, :]
            grad_qkv_ref[rows, h * HD : (h + 1) * HD] = grad.astype(bf16)
        return 0

    lax.fori_loop(0, blocks, turn_back, 0)
    if line.ticks:
        line.close(0)
        line.finish()


def take_cuts_kernel(cuts, holder_ref, rows_ref, out_ref):
    cut = out_ref.shape[0] // cuts

    def one(p, _):
        src = pl.ds(pl.multiple_of(holder_ref[0, p] * cut, cut), cut)
        out_ref[pl.ds(pl.multiple_of(p * cut, cut), cut), :] = rows_ref[src, :]
        return 0

    lax.fori_loop(0, cuts, one, 0)


def take_cuts(holder, rows):
    return pl.pallas_call(
        functools.partial(take_cuts_kernel, holder.shape[1]),
        out_shape=jax.ShapeDtypeStruct(rows.shape, rows.dtype),
        in_specs=[pl.BlockSpec(memory_space=pltpu.SMEM)] + vmem_specs(1),
        out_specs=pl.BlockSpec(memory_space=pltpu.VMEM),
        cost_estimate=pl.CostEstimate(
            flops=0, bytes_accessed=2 * rows.size * rows.dtype.itemsize, transcendentals=0
        ),
    )(holder, rows)


def attend_back(
    order, grad, out, query, key, value, lse, cosine, sine, piece, piece_col, heads, **line
):
    cuts = jnp.arange(order.shape[1], dtype=order.dtype)
    holder = jnp.sum(jnp.where(order[0][None, :] == cuts[:, None], cuts[None, :], 0), 1)[None, :]
    length = grad.shape[0]
    block = min(512, length)
    tall = [take_cuts(holder, grad), out, query, key, value, lse, cosine, sine, piece, piece_col]
    grad_qkv = run(
        functools.partial(attend_back_kernel, heads, block),
        [(array, VMEM) for array in tall],
        [(jax.ShapeDtypeStruct((length, (heads + 2) * HD), bf16), VMEM)],
        [
            pltpu.VMEM((heads, length, HD), bf16),
            pltpu.VMEM((heads, length, HD), f32),
            pltpu.VMEM((heads, length, HD), f32),
        ],
        line.pop("number", None),
        (8 * heads * length * length * HD, 14 * length * HD * heads * 4, heads * length * length // 2),
        **line,
    )[0]
    return take_cuts(order, grad_qkv)


def place_in_group():
    me = lax.axis_index("grp")
    return me // 4, (me // 2) % 2, me % 2


def other(flip_y, flip_x, flip_core):
    y, x, core = place_in_group()
    return ((y + flip_y) % 2) * 4 + ((x + flip_x) % 2) * 2 + (core + flip_core) % 2


def chip_rows(flip_y, flip_x, rows):
    y, x, _ = place_in_group()
    first = (((y + flip_y) % 2) * 2 + (x + flip_x) % 2) * (2 * rows)
    return pl.ds(pl.multiple_of(first, 2 * rows), 2 * rows)


NEIGHBOURS = ((0, 0, 1), (0, 1, 0), (1, 0, 0))
EVERYONE = tuple((n // 4, (n // 2) % 2, n % 2) for n in range(1, 8))


def greet_group(line, flips=NEIGHBOURS):
    barrier = pltpu.get_barrier_semaphore()
    for flip in flips:
        pl.semaphore_signal(barrier, inc=1, device_id={"grp": other(*flip)}, device_id_type=MESH)
    line.greet(barrier, len(flips))


SIBLING, ALONG_X, ALONG_Y, ACROSS = (0, 0), (0, 1), (1, 0), (1, 1)


def gather_rows(rows, all_ref, sends, recvs, on_chip, line, then=None):
    half = rows // 2

    def block(chip, core, part=None):
        first = other(*chip, core) * rows
        if part is None:
            return pl.ds(pl.multiple_of(first, rows), rows)
        return pl.ds(pl.multiple_of(first + part * half, half), half)

    def copy(number, chip, core, part, target):
        where = all_ref.at[block(chip, core, part), :]
        return pltpu.make_async_remote_copy(
            src_ref=where, dst_ref=where, send_sem=sends.at[number], recv_sem=recvs.at[number],
            device_id={"grp": other(*target)}, device_id_type=MESH,
        )

    def landed(number, chip, core, part):
        where = all_ref.at[block(chip, core, part), :]
        pltpu.make_async_remote_copy(
            src_ref=where, dst_ref=where, send_sem=sends.at[number], recv_sem=recvs.at[number],
            device_id={"grp": other(0, 0, 1)}, device_id_type=MESH,
        ).wait_recv()

    to_s, to_x, to_y = (0, 0, 1), (0, 1, 0), (1, 0, 0)
    started = []

    def send(*what):
        one = copy(*what)
        one.start()
        started.append(one)

    send(1, SIBLING, 0, 1, to_x)
    send(3, SIBLING, 0, 0, to_y)
    send(0, SIBLING, 0, None, to_s)
    send(2, SIBLING, 0, 0, to_x)
    send(4, SIBLING, 0, 1, to_y)
    if then:
        then()
    landed(0, SIBLING, 1, None)
    on_chip(*SIBLING)
    landed(1, ALONG_X, 0, 1)
    send(6, ALONG_X, 0, 1, to_y)
    landed(3, ALONG_Y, 0, 0)
    send(5, ALONG_Y, 0, 0, to_x)
    send(7, ALONG_X, 0, 1, to_s)
    send(8, ALONG_Y, 0, 0, to_s)
    landed(2, ALONG_X, 0, 0)
    send(9, ALONG_X, 0, 0, to_s)
    landed(4, ALONG_Y, 0, 1)
    send(10, ALONG_Y, 0, 1, to_s)
    line.close(0)
    line.open(1)
    landed(7, ALONG_X, 1, 1)
    landed(9, ALONG_X, 1, 0)
    on_chip(*ALONG_X)
    landed(5, ACROSS, 0, 0)
    send(11, ACROSS, 0, 0, to_s)
    landed(6, ACROSS, 0, 1)
    send(12, ACROSS, 0, 1, to_s)
    landed(8, ALONG_Y, 1, 0)
    landed(10, ALONG_Y, 1, 1)
    on_chip(*ALONG_Y)
    landed(11, ACROSS, 1, 0)
    landed(12, ACROSS, 1, 1)
    on_chip(*ACROSS)
    for one in started:
        one.wait_send()
    line.close(1)
    line.finish()


GATHER_COPIES = 13


def rms_normed(values, gain):
    return values * lax.rsqrt(jnp.mean(values * values, -1, keepdims=True) + EPS) * gain


class Moves:
    def __init__(self, sems):
        self.sems, self.count, self.open = sems, 0, []

    def start(self, src, dst):
        one = pltpu.make_async_copy(src, dst, self.sems.at[self.count])
        self.count += 1
        one.start()
        return one

    def later(self, src, dst):
        self.open.append(self.start(src, dst))

    def finish(self):
        for one in self.open:
            one.wait()


def gather_scratch(rows, width, moves):
    return [
        pltpu.VMEM((8 * rows, width), bf16),
        pltpu.SemaphoreType.DMA((GATHER_COPIES,)),
        pltpu.SemaphoreType.DMA((GATHER_COPIES,)),
        pltpu.SemaphoreType.DMA((moves,)),
    ]


def own_rows(rows):
    return pl.ds(pl.multiple_of(other(0, 0, 0) * rows, rows), rows)


def send_columns(pieces, sends, recvs, moves):
    copies = []
    for which, (rows_ref, width, there) in enumerate(pieces):
        for number, flip in enumerate(EVERYONE):
            target = other(*flip)
            cols = pl.ds(pl.multiple_of(target * width, width), width)
            one = pltpu.make_async_remote_copy(
                src_ref=rows_ref.at[:, cols], dst_ref=there,
                send_sem=sends.at[which, number], recv_sem=recvs.at[which, number],
                device_id={"grp": target}, device_id_type=MESH,
            )
            one.start()
            copies.append(one)
        mine = pl.ds(pl.multiple_of(other(0, 0, 0) * width, width), width)
        moves.later(rows_ref.at[:, mine], there)
    return copies


def gather_normed_kernel(ins, outs, scratch, line):
    x_ref, gain_ref = ins[:2]
    weights = ins[2:]
    all_ref, cols_ref = outs
    held, sends, recvs, sems, col_sends, col_recvs = scratch
    rows = x_ref.shape[0]
    moves = Moves(sems)
    held[own_rows(rows), :] = rms_normed(x_ref[...].astype(f32), gain_ref[...]).astype(bf16)
    greet_group(line, EVERYONE)
    col_copies = []

    def send_weights():
        pieces, low = [], 0
        tall = weights[0].shape[0]
        there = pl.ds(pl.multiple_of(other(0, 0, 0) * tall, tall), tall)
        for weight in weights:
            width = weight.shape[1] // 8
            pieces.append((weight, width, cols_ref.at[there, low : low + width]))
            low += width
        col_copies.extend(send_columns(pieces, col_sends, col_recvs, moves))

    def on_chip(*chip):
        where = chip_rows(*chip, rows)
        moves.later(held.at[where, :], all_ref.at[where, :])

    gather_rows(rows, held, sends, recvs, on_chip, line, send_weights)
    for one in col_copies:
        one.wait()
    moves.finish()


def gather_normed(x, gain, weights, **line):
    rows, width = x.shape
    deep = sum(weight.shape[1] for weight in weights) // 8
    return run(
        gather_normed_kernel,
        [(x, VMEM), (gain, VMEM)] + [(weight, ANY) for weight in weights],
        [
            (jax.ShapeDtypeStruct((8 * rows, width), bf16), ANY),
            (jax.ShapeDtypeStruct((8 * weights[0].shape[0], deep), bf16), ANY),
        ],
        gather_scratch(rows, width, 4 + len(weights))
        + [pltpu.SemaphoreType.DMA((len(weights), 7))] * 2,
        line.pop("number"),
        (0, 150 * rows * width * 2, 0),
        **line,
    )


def columns_kernel(rows_here, ins, outs, scratch, line):
    (cols_ref,) = outs
    sends, recvs, sems = scratch
    moves = Moves(sems)
    barrier = pltpu.get_barrier_semaphore()
    for flip in EVERYONE:
        pl.semaphore_signal(barrier, inc=1, device_id={"grp": other(*flip)}, device_id_type=MESH)
    pl.semaphore_wait(barrier, 7)
    first = pl.multiple_of(lax.axis_index("rep") * rows_here, rows_here)
    me = other(0, 0, 0)
    pieces, low = [], 0
    for weight in ins:
        width = weight.shape[1] // 8
        pieces.append(
            (weight.at[pl.ds(first, rows_here), :], width, cols_ref.at[me, :, low : low + width])
        )
        low += width
    for one in send_columns(pieces, sends, recvs, moves):
        one.wait()
    moves.finish()


def columns_of_some(weights, rows_here, number):
    deep = sum(weight.shape[1] for weight in weights) // 8
    return run(
        functools.partial(columns_kernel, rows_here),
        [(weight, ANY) for weight in weights],
        [(jax.ShapeDtypeStruct((8, rows_here, deep), bf16), ANY)],
        [pltpu.SemaphoreType.DMA((len(weights), 7))] * 2
        + [pltpu.SemaphoreType.DMA((len(weights),))],
        number, (0, 50 * 8 * rows_here * deep, 0),
    )[0]


def feed_forward_kernel(tile, ins, outs, scratch, line):
    mid_ref, gain_ref, spread_ref, rest_ref = ins
    all_ref, hidden_ref, up_part_ref, gate_part_ref, whole_ref = outs
    held, sends, recvs, sems, weight, hidden, up_part, gate_part = scratch
    rows = mid_ref.shape[0]
    inner = hidden.shape[1]
    moves = Moves(sems)
    planes, _, tall, deep = spread_ref.shape
    loads = [
        moves.start(spread_ref.at[z], weight.at[:, z * tall : (z + 1) * tall, :])
        for z in range(planes)
    ]
    loads.append(moves.start(rest_ref, weight.at[:, planes * tall :, :]))
    held[own_rows(rows), :] = rms_normed(mid_ref[...], gain_ref[...]).astype(bf16)
    greet_group(line)
    line.open(0)

    def on_chip(*chip):
        where = chip_rows(*chip, rows)
        moves.later(held.at[where, :], all_ref.at[where, :])
        if chip == SIBLING:
            for one in loads:
                one.wait()
            moves.later(weight, whole_ref)

        def column(t, _):
            cols = pl.ds(pl.multiple_of(t * tile, tile), tile)
            up_cols = pl.ds(pl.multiple_of(inner + t * tile, tile), tile)
            lhs = held[where, :]
            gate = matmul_f32(lhs, weight[:, :, cols].reshape(-1, tile))
            up = matmul_f32(lhs, weight[:, :, up_cols].reshape(-1, tile))
            sigma = 1.0 / (1.0 + jnp.exp(-gate))
            swish = gate * sigma
            hidden[where, cols] = (swish * up).astype(bf16)
            up_part[where, cols] = swish.astype(bf16)
            gate_part[where, cols] = (up * sigma * (1.0 + gate * (1.0 - sigma))).astype(bf16)
            return 0

        lax.fori_loop(0, inner // tile, column, 0)
        for src, dst in ((hidden, hidden_ref), (up_part, up_part_ref), (gate_part, gate_part_ref)):
            moves.later(src.at[where, :], dst.at[where, :])

    gather_rows(rows, held, sends, recvs, on_chip, line)
    moves.finish()


def feed_forward(mid, gain, spread, rest, **line):
    rows, width = mid.shape
    inner = rest.shape[2] // 2
    weight = (8, width // 8, 2 * inner)
    tall = jax.ShapeDtypeStruct((8 * rows, inner), bf16)
    return run(
        functools.partial(feed_forward_kernel, min(256, inner)),
        [(mid, VMEM), (gain, VMEM), (spread, ANY), (rest, ANY)],
        [(jax.ShapeDtypeStruct((8 * rows, width), bf16), ANY)]
        + [(tall, ANY)] * 3
        + [(jax.ShapeDtypeStruct(weight, bf16), ANY)],
        gather_scratch(rows, width, 22)
        + [pltpu.VMEM(weight, bf16)]
        + [pltpu.VMEM((8 * rows, inner), bf16)] * 3,
        line.pop("number"),
        (32 * rows * width * inner, 150 * rows * width * 2, 8 * rows * inner),
        **line,
    )


def feed_forward_back_kernel(tile, ins, outs, scratch, line):
    grad_ref, w_ref, hidden_ref, up_part_ref, gate_part_ref = ins
    grad_gate_up_ref, down_ref = outs
    held, sends, recvs, sems, weight, hidden, up_part, gate_part, grads, down, down_low = scratch
    rows = grad_ref.shape[0]
    inner, width = weight.shape
    moves = Moves(sems)
    loads = [
        moves.start(src, dst)
        for src, dst in (
            (w_ref, weight), (hidden_ref, hidden), (up_part_ref, up_part), (gate_part_ref, gate_part)
        )
    ]
    held[own_rows(rows), :] = grad_ref[...]
    greet_group(line)
    line.open(0)

    def on_chip(*chip):
        where = chip_rows(*chip, rows)
        if chip == SIBLING:
            for one in loads:
                one.wait()

        def column(t, _):
            cols = pl.ds(pl.multiple_of(t * tile, tile), tile)
            up_cols = pl.ds(pl.multiple_of(inner + t * tile, tile), tile)
            incoming = held[where, :]
            grad_hidden = against_rows(incoming, weight[cols, :])
            grads[where, cols] = (grad_hidden * gate_part[where, cols].astype(f32)).astype(bf16)
            grads[where, up_cols] = (grad_hidden * up_part[where, cols].astype(f32)).astype(bf16)
            term = over_tokens(hidden[where, cols], incoming)
            if chip == SIBLING:
                down[cols, :] = term
            elif chip == ACROSS:
                down_low[cols, :] = (down[cols, :] + term).astype(bf16)
            else:
                down[cols, :] += term
            return 0

        lax.fori_loop(0, inner // tile, column, 0)
        moves.later(grads.at[where, :], grad_gate_up_ref.at[where, :])

    gather_rows(rows, held, sends, recvs, on_chip, line)
    moves.later(down_low, down_ref)
    moves.finish()


def feed_forward_back(grad, w_down, hidden, up_part, gate_part, **line):
    rows, width = grad.shape
    inner = w_down.shape[0]
    return run(
        functools.partial(feed_forward_back_kernel, min(256, inner)),
        [(grad, VMEM)] + [(array, ANY) for array in (w_down, hidden, up_part, gate_part)],
        [
            (jax.ShapeDtypeStruct((8 * rows, 2 * inner), bf16), ANY),
            (jax.ShapeDtypeStruct((inner, width), bf16), ANY),
        ],
        gather_scratch(rows, width, 9)
        + [pltpu.VMEM(w_down.shape, bf16)]
        + [pltpu.VMEM((8 * rows, inner), bf16)] * 3
        + [
            pltpu.VMEM((8 * rows, 2 * inner), bf16),
            pltpu.VMEM(w_down.shape, f32),
            pltpu.VMEM(w_down.shape, bf16),
        ],
        line.pop("number"),
        (32 * rows * width * inner, 150 * rows * width * 2, 0),
        vmem=62,
        **line,
    )


def attended_back_kernel(ins, outs, scratch, line):
    grad_ref, w_ref, attended_ref = ins
    grad_attended_ref, out_term_ref = outs
    held, sends, recvs, sems, total = scratch
    rows = grad_ref.shape[0]
    moves = Moves(sems)
    held[own_rows(rows), :] = grad_ref[...]
    greet_group(line)
    line.open(0)

    def on_chip(*chip):
        where = chip_rows(*chip, rows)
        incoming = held[where, :]
        grad_attended_ref[where, :] = against_rows(incoming, w_ref[...]).astype(bf16)
        term = over_tokens(attended_ref[where, :], incoming)
        if chip == SIBLING:
            total[...] = term
        elif chip == ACROSS:
            out_term_ref[...] = (total[...] + term).astype(bf16)
        else:
            total[...] += term

    gather_rows(rows, held, sends, recvs, on_chip, line)
    moves.finish()


def attended_back(grad, w_out, attended, **line):
    rows, width = grad.shape
    return run(
        attended_back_kernel,
        [(array, VMEM) for array in (grad, w_out, attended)],
        [
            (jax.ShapeDtypeStruct(attended.shape, bf16), VMEM),
            (jax.ShapeDtypeStruct(w_out.shape, bf16), VMEM),
        ],
        gather_scratch(rows, width, 1) + [pltpu.VMEM(w_out.shape, f32)],
        line.pop("number"),
        (32 * rows * width * w_out.shape[0], 150 * rows * width * 2, 0),
        **line,
    )


class WeightTerm:
    def __init__(self, rows_ref, columns_ref, term_ref, scratch):
        self.rows_ref, self.columns_ref, self.term_ref = rows_ref, columns_ref, term_ref
        self.loaded, self.ready, self.sems = scratch
        self.tile = self.loaded.shape[2]
        for number in (0, 1):
            self.load(number).start()

    def load(self, number):
        cols = slice(number * self.tile, (number + 1) * self.tile)
        return pltpu.make_async_copy(
            self.rows_ref.at[:, cols], self.loaded.at[number % 2], self.sems.at[0, number % 2]
        )

    def store(self, number):
        return pltpu.make_async_copy(
            self.ready.at[number % 2], self.term_ref.at[number], self.sems.at[1, number % 2]
        )

    def work(self, numbers):
        for number in numbers:
            at = number % 2
            self.load(number).wait()
            if number >= 2:
                self.store(number - 2).wait()
            width = self.columns_ref.shape[1]
            step = min(256, width)

            def column(t, _):
                cols = pl.ds(pl.multiple_of(t * step, step), step)
                term = over_tokens(self.loaded[at], self.columns_ref[:, cols])
                self.ready[at, :, cols] = term.astype(bf16)
                return 0

            lax.fori_loop(0, width // step, column, 0)
            self.store(number).start()
            if number + 2 < 8:
                self.load(number + 2).start()

    def finish(self):
        for number in (6, 7):
            self.store(number).wait()


def scatter_kernel(turned, tile, extra, ins, outs, scratch, line):
    a_ref, b_ref = ins[:2]
    out_ref = outs[0]
    part, to_s, from_s, to_chip, held, relay, last, sends, recvs = scratch[:9]
    rows, width = out_ref.shape
    half = rows // 2
    _, _, core = place_in_group()
    greet_group(line)
    line.open(0)
    if extra:
        columns_ref = a_ref
        if extra == "loaded":
            columns_ref = scratch[12]
            columns_copy = pltpu.make_async_copy(ins[3], columns_ref, scratch[13].at[0])
            columns_copy.start()
        term = WeightTerm(ins[2], columns_ref, outs[1], scratch[9:12])
    own_at = pl.multiple_of(core * rows, rows)
    other_at = pl.multiple_of((1 - core) * rows, rows)
    started = []

    def send(number, src, dst, target):
        one = pltpu.make_async_remote_copy(
            src_ref=src, dst_ref=dst, send_sem=sends.at[number], recv_sem=recvs.at[number],
            device_id={"grp": other(*target)}, device_id_type=MESH,
        )
        one.start()
        started.append(one)
        return one

    def landed(number, where):
        pltpu.make_async_remote_copy(
            src_ref=where, dst_ref=where, send_sem=sends.at[number], recv_sem=recvs.at[number],
            device_id={"grp": other(0, 0, 1)}, device_id_type=MESH,
        ).wait_recv()

    to_sib, to_x, to_y = (0, 0, 1), (0, 1, 0), (1, 0, 0)

    def make(number, chip):
        where = chip_rows(*chip, rows)

        def column(t, _):
            cols = pl.ds(pl.multiple_of(t * tile, tile), tile)
            lhs = a_ref[where, :]
            if turned:
                part[:, cols] = against_rows(lhs, b_ref[cols, :])
            else:
                part[:, cols] = matmul_f32(lhs, b_ref[:, cols])
            return 0

        lax.fori_loop(0, width // tile, column, 0)
        to_s[number] = part[pl.ds(other_at, rows), :].astype(bf16)
        send(number, to_s.at[number], from_s.at[number], to_sib)

    def own(low, number):
        at = pl.ds(pl.multiple_of(core * rows + low * half, half), half)
        return part[at, :] + from_s[number, low * half : (low + 1) * half, :].astype(f32)

    first, second = slice(0, half), slice(half, rows)
    make(0, ACROSS)
    landed(0, from_s.at[0])
    to_chip[0, first, :] = own(0, 0).astype(bf16)
    send(4, to_chip.at[0, first, :], relay.at[0], to_x)
    to_chip[0, second, :] = own(1, 0).astype(bf16)
    send(5, to_chip.at[0, second, :], relay.at[1], to_y)
    make(1, ALONG_X)
    landed(1, from_s.at[1])
    to_chip[1, first, :] = own(0, 1).astype(bf16)
    send(6, to_chip.at[1, first, :], last.at[0, first, :], to_x)
    held[0] = own(1, 1)
    make(2, ALONG_Y)
    landed(2, from_s.at[2])
    to_chip[2, second, :] = own(1, 2).astype(bf16)
    send(7, to_chip.at[2, second, :], last.at[1, second, :], to_y)
    held[1] = own(0, 2)
    if extra:
        if extra == "loaded":
            columns_copy.wait()
        term.work((0, 1, 2))
    landed(5, relay.at[1])
    to_chip[1, second, :] = (held[0] + relay[1].astype(f32)).astype(bf16)
    send(8, to_chip.at[1, second, :], last.at[0, second, :], to_x)
    landed(4, relay.at[0])
    to_chip[2, first, :] = (held[1] + relay[0].astype(f32)).astype(bf16)
    send(9, to_chip.at[2, first, :], last.at[1, first, :], to_y)
    line.close(0)
    line.open(1)
    make(3, SIBLING)
    if extra:
        term.work((3, 4, 5, 6, 7))
    landed(3, from_s.at[3])
    for low in (0, 1):
        out_ref[low * half : (low + 1) * half, :] = own(low, 3)
    landed(6, last.at[0, first, :])
    out_ref[first, :] += last[0, first, :].astype(f32)
    landed(7, last.at[1, second, :])
    out_ref[second, :] += last[1, second, :].astype(f32)
    landed(8, last.at[0, second, :])
    out_ref[second, :] += last[0, second, :].astype(f32)
    landed(9, last.at[1, first, :])
    out_ref[first, :] += last[1, first, :].astype(f32)
    for one in started:
        one.wait_send()
    if extra:
        term.finish()
    line.close(1)
    line.finish()


def product_scattered(a, b, turned, extra=None, **line):
    length, depth = a.shape
    width = b.shape[0] if turned else b.shape[1]
    rows = length // 8
    tile = min(256, width)
    ins = [(a, VMEM), (b, VMEM)]
    outs = [(jax.ShapeDtypeStruct((rows, width), f32), VMEM)]
    scratch = [
        pltpu.VMEM((2 * rows, width), f32),
        pltpu.VMEM((4, rows, width), bf16),
        pltpu.VMEM((4, rows, width), bf16),
        pltpu.VMEM((3, rows, width), bf16),
        pltpu.VMEM((2, rows // 2, width), f32),
        pltpu.VMEM((2, rows // 2, width), bf16),
        pltpu.VMEM((2, rows, width), bf16),
        pltpu.SemaphoreType.DMA((10,)),
        pltpu.SemaphoreType.DMA((10,)),
    ]
    flops, kind = 2 * length * depth * width, None
    if extra:
        first, second = extra
        kind = "own" if second is None else "loaded"
        ins.append((first, ANY))
        columns = a if second is None else second
        tall = first.shape[1] // 8
        outs.append((jax.ShapeDtypeStruct((8, tall, columns.shape[1]), bf16), ANY))
        scratch += [
            pltpu.VMEM((2, length, tall), bf16),
            pltpu.VMEM((2, tall, columns.shape[1]), bf16),
            pltpu.SemaphoreType.DMA((2, 2)),
        ]
        if second is not None:
            ins.append((second, ANY))
            scratch += [pltpu.VMEM(second.shape, bf16), pltpu.SemaphoreType.DMA((1,))]
        flops += 2 * length * first.shape[1] * columns.shape[1]
    return run(
        functools.partial(scatter_kernel, turned, tile, kind), ins, outs, scratch,
        line.pop("number"), (flops, 150 * rows * width * 2, 0), vmem=60, **line,
    )


def tail_kernel(ready, later, ins, outs, scratch, line):
    qkv_ref, gains_ref = ins[:2]
    chunk_refs = dict(zip(ready, ins[2:]))
    gate_ref, up_ref, qkv_rows_ref, gains_out_ref = outs
    from_group, mine, from_rep, sends, recvs, chunk_sems, local = scratch
    me, rank = other(0, 0, 0), lax.axis_index("rep")
    inner = gate_ref.shape[1] // 8
    part = qkv_ref.shape[-1]
    high = line.outs[later[0]].shape[1]
    barrier = pltpu.get_barrier_semaphore()
    for flip in range(1, 4):
        pl.semaphore_signal(
            barrier, inc=1, device_id={"rep": (rank + flip) % 4}, device_id_type=MESH
        )
    for flip in EVERYONE:
        pl.semaphore_signal(barrier, inc=1, device_id={"grp": other(*flip)}, device_id_type=MESH)
    pl.semaphore_wait(barrier, 10)
    waits, moves = [], Moves(local)
    line.refs["qkv"] = qkv_rows_ref

    def send(kind, number, src, dst, device):
        return pltpu.make_async_remote_copy(
            src_ref=src, dst_ref=dst, send_sem=sends.at[kind, number],
            recv_sem=recvs.at[kind, number], device_id=device, device_id_type=MESH,
        )

    own_qkv = qkv_rows_ref.at[me // 4, :, :, pl.ds(pl.multiple_of((me % 4) * part, part), part)]
    qkv_copies, gain_copies = [], []
    for number, flip in enumerate(EVERYONE):
        target = other(*flip)
        qkv_copies.append(send(0, number, qkv_ref.at[target], own_qkv, {"grp": target}))
        qkv_copies[-1].start()
    moves.later(qkv_ref.at[me], own_qkv)
    line.open(0)
    for number, flip in enumerate(EVERYONE):
        target = other(*flip)
        gain_copies.append(
            send(1, number, gains_ref.at[target], from_group.at[me], {"grp": target})
        )
        gain_copies[-1].start()
    from_group[me] = gains_ref[me]

    def spread(chunk):
        src = chunk_refs[chunk] if chunk in chunk_refs else line.outs[chunk]
        number = chunk - 4
        rows = slice(number * high, (number + 1) * high)
        cols = pl.ds(pl.multiple_of(me * inner, inner), inner)
        for which, dst in enumerate((gate_ref, up_ref)):
            there = dst.at[rows, cols]
            for flip in EVERYONE:
                target = other(*flip)
                pltpu.make_async_remote_copy(
                    src_ref=src.at[target, :, which * inner : (which + 1) * inner], dst_ref=there,
                    send_sem=chunk_sems.at[0, which, number], recv_sem=chunk_sems.at[1, which, number],
                    device_id={"grp": target}, device_id_type=MESH,
                ).start()
            moves.later(src.at[me, :, which * inner : (which + 1) * inner], there)
            seven = dst.at[rows, : 7 * inner]
            waits.append(
                pltpu.make_async_remote_copy(
                    src_ref=seven, dst_ref=seven, send_sem=chunk_sems.at[0, which, number],
                    recv_sem=chunk_sems.at[1, which, number],
                    device_id={"grp": other(0, 0, 1)}, device_id_type=MESH,
                )
            )

    for chunk in ready:
        spread(chunk)
    for one in gain_copies:
        one.wait()
    mine[rank] = sum(from_group[g] for g in range(8))
    rep_copies = []
    for step in range(1, 4):
        target = (rank + step) % 4
        rep_copies.append(
            send(2, step, mine.at[rank], from_rep.at[step], {"rep": target})
        )
        rep_copies[-1].start()
    for step, one in zip(range(1, 4), rep_copies):
        one.wait()
        mine[(rank + 4 - step) % 4] = from_rep[step]
    gains_out_ref[...] = (mine[0] + mine[1]) + (mine[2] + mine[3])
    line.close(0)
    for number in range(1, line.ticks):
        if line.first + number == CHUNKS - 2:
            for one in qkv_copies:
                one.wait()
            moves.open.pop(0).wait()
        line.open(number)
        chunk = line.first + number - 3
        if chunk in later:
            spread(chunk)
        line.close(number)
    for one in waits:
        one.wait_send()
        one.wait_recv()
    moves.finish()


def tail(qkv_term, gains, chunks, inner, number, sums, ticks, arrays, picks):
    first = sums.tick
    ready = sorted(chunks)
    later = [c for c in line_slots(first, ticks) if c < 12]
    _, high, width = sums.shape
    part = qkv_term.shape[-1]
    wide = jax.ShapeDtypeStruct((8 * high, 8 * inner), bf16)
    moved = jax.ShapeDtypeStruct((2,) + sums.shape, bf16)
    picks = dict(picks)
    for half in (0, 1):
        picks[CHUNKS - 2 + half] = ("qkv", lambda ref, half=half: ref.at[half])
    return run(
        functools.partial(tail_kernel, ready, later),
        [(qkv_term, ANY), (gains, VMEM)] + [(chunks[c], ANY) for c in ready],
        [(wide, ANY), (wide, ANY), (moved, ANY), (jax.ShapeDtypeStruct(gains.shape[1:], f32), VMEM)],
        [
            pltpu.VMEM(gains.shape, f32),
            pltpu.VMEM((4,) + gains.shape[1:], f32),
            pltpu.VMEM((4,) + gains.shape[1:], f32),
            pltpu.SemaphoreType.DMA((3, 7)),
            pltpu.SemaphoreType.DMA((3, 7)),
            pltpu.SemaphoreType.DMA((2, 2, 8)),
            pltpu.SemaphoreType.DMA((17,)),
        ],
        number, (0, 200 * 8 * high * width * 2, 0), sums=sums, ticks=ticks, arrays=arrays, picks=picks,
    )


def finish_kernel(heads, *refs):
    ins, rest = refs[:9], refs[9:]
    outs, (low, wide, load_sems, store_sems) = rest[:7], rest[7:]
    down_refs, out_sum, qkv_refs, gate_rows, up_rows = ins[:4], ins[4], ins[5:7], ins[7], ins[8]
    query, key, value, out, gate, up, down = outs
    rows, width = down_refs[0].shape
    jobs = []
    for number, ref in enumerate(down_refs):
        jobs.append((ref, [(slice(0, width), down.at[number * rows : (number + 1) * rows, :])]))
    for ref, into in ((gate_rows, gate), (up_rows, up)):
        for low_col in range(0, ref.shape[1], width):
            cols = slice(low_col, low_col + width)
            jobs.append((ref.at[:, cols], [(slice(0, width), into.at[:, cols])]))
    jobs.append((out_sum, [(slice(0, width), out)]))
    part = (heads + 2) * HD
    for number, ref in enumerate(qkv_refs):
        stores = []
        for place in range(width // part):
            at, device = place * part, number * (width // part) + place
            for into, first, size in (
                (query, 0, heads * HD), (key, heads * HD, HD), (value, (heads + 1) * HD, HD)
            ):
                stores.append(
                    (
                        slice(at + first, at + first + size),
                        into.at[:, device * size : (device + 1) * size],
                    )
                )
        jobs.append((ref, stores))

    def load(number):
        return pltpu.make_async_copy(
            jobs[number][0], low.at[number % 3], load_sems.at[number % 3]
        )

    def stores(number):
        return [
            pltpu.make_async_copy(
                wide.at[number % 3, :, cols], into, store_sems.at[number % 3, which]
            )
            for which, (cols, into) in enumerate(jobs[number][1])
        ]

    for number in range(min(2, len(jobs))):
        load(number).start()
    for number in range(len(jobs)):
        if number + 2 < len(jobs):
            load(number + 2).start()
        load(number).wait()
        if number >= 3:
            for one in stores(number - 3):
                one.wait()

        def cast(g, _, at=number % 3):
            some = pl.ds(pl.multiple_of(g * 32, 32), 32)
            wide[at, some, :] = low[at, some, :].astype(f32)
            return 0

        lax.fori_loop(0, rows // 32, cast, 0)
        for one in stores(number):
            one.start()
    for number in range(max(0, len(jobs) - 3), len(jobs)):
        for one in stores(number):
            one.wait()


def finish(downs, out_sum, qkvs, gate_rows, up_rows, heads):
    rows, width = out_sum.shape
    wide = gate_rows.shape[1]
    shapes = [
        (rows, 8 * heads * HD), (rows, 8 * HD), (rows, 8 * HD), (rows, width), (rows, wide),
        (rows, wide), (len(downs) * rows, width),
    ]
    size = len(downs) * rows * width + 2 * rows * wide + 3 * rows * width
    return pl.pallas_call(
        functools.partial(finish_kernel, heads),
        out_shape=tuple(jax.ShapeDtypeStruct(shape, f32) for shape in shapes),
        in_specs=[pl.BlockSpec(memory_space=pl.ANY)] * 9,
        out_specs=tuple([pl.BlockSpec(memory_space=pl.ANY)] * 7),
        scratch_shapes=[
            pltpu.VMEM((3, rows, width), bf16),
            pltpu.VMEM((3, rows, width), f32),
            pltpu.SemaphoreType.DMA((3,)),
            pltpu.SemaphoreType.DMA((3, 12)),
        ],
        compiler_params=pltpu.CompilerParams(vmem_limit_bytes=32 * 2**20),
        cost_estimate=pl.CostEstimate(flops=0, bytes_accessed=6 * size, transcendentals=0),
    )(*downs, out_sum, *qkvs, gate_rows, up_rows)


def sum_over_sequences(term):
    return lax.psum(term, "rep").astype(f32)


def on_device(
    layer_input,
    cotangent,
    cut_order,
    piece_ids,
    w_query,
    w_key,
    w_value,
    w_out,
    w_gate,
    w_up,
    w_down,
    gain_attn,
    gain_ffn,
):
    groups = lax.axis_size("grp")
    reps = lax.axis_size("rep")
    own_index = lax.axis_index("grp")
    _, local_rows, model_width = layer_input.shape
    length = piece_ids.shape[1]
    rows_here = w_query.shape[0]
    q_width = w_query.shape[1]
    kv_heads = w_key.shape[1] // HD
    heads = q_width // HD // groups
    copies = groups // kv_heads
    hidden_here = w_down.shape[0]
    piece_col = jnp.broadcast_to(piece_ids.reshape(length, 1), (length, HD))
    cosine, sine = turn_tables(length)

    near = groups == 8 and reps == 4 and copies == 1

    def gather(rows):
        return lax.all_gather(rows, "grp", axis=0, tiled=True)

    def scatter(first, second, turned):
        term = against_rows(first, second) if turned else matmul_f32(first, second)
        return lax.psum_scatter(
            term.astype(bf16), "grp", scatter_dimension=0, tiled=True
        ).astype(f32)

    def to_columns(parts):
        return lax.all_to_all(parts, "grp", 1, 0, tiled=True).reshape(-1, parts.shape[-1])

    def per_group(weight):
        return weight.reshape(rows_here, groups, -1)

    def per_kv_head(weight):
        return jnp.repeat(weight.reshape(rows_here, kv_heads, HD), copies, axis=1)

    x_rows = layer_input.reshape(local_rows, model_width)
    x_flat = x_rows.astype(f32)
    inv_one = lax.rsqrt(jnp.mean(x_flat * x_flat, -1, keepdims=True) + EPS)
    unit_one = x_flat * inv_one
    attn_gain, ffn_gain = gain_attn.reshape(1, -1), gain_ffn.reshape(1, -1)
    if near:
        share = rows_here // (4 * reps) * 3
        spread = columns_of_some((w_gate, w_up), share, 11)
        x_first, spread = lax.optimization_barrier((x_rows, spread))
        spread = lax.all_gather(spread, "rep", axis=0)
        normed_one, cols_qkv = gather_normed(
            x_first, attn_gain, (w_query, w_key, w_value), number=1
        )
        last_gate, last_up, normed_one = lax.optimization_barrier(
            (w_gate[reps * share :], w_up[reps * share :], normed_one)
        )
        rest = to_columns(
            jnp.concatenate(
                [part.reshape(rows_here - reps * share, groups, -1) for part in (last_gate, last_up)],
                -1,
            )
        ).reshape(groups, rows_here - reps * share, -1)
    else:
        normed_one = gather(rms_normed(x_flat, attn_gain).astype(bf16))
        cols_qkv = to_columns(
            jnp.concatenate([per_group(w_query), per_kv_head(w_key), per_kv_head(w_value)], -1)
        )
        cols_gate_up = to_columns(jnp.concatenate([per_group(w_gate), per_group(w_up)], -1))
    qkv = matmul_f32(normed_one, cols_qkv)
    attended, query, key, value, lse, attended_placed = attend(
        cut_order, qkv, cosine, sine, piece_ids, piece_col, heads
    )
    if near:
        out_sum = product_scattered(attended, w_out, False, number=2)[0]
    else:
        out_sum = scatter(attended, w_out, False)
    mid = x_flat + out_sum
    inv_two = lax.rsqrt(jnp.mean(mid * mid, -1, keepdims=True) + EPS)
    unit_two = mid * inv_two
    grad_out = cotangent.reshape(local_rows, model_width)

    def finish_two(grad_two):
        return norm_back(grad_out.astype(f32), grad_two, unit_two, inv_two, gain_ffn)

    def finish_one(grad_mid, grad_one):
        grad_input, gain_term = norm_back(grad_mid, grad_one, unit_one, inv_one, gain_attn)
        return grad_input.astype(bf16).reshape(layer_input.shape), gain_term

    def back_through_attention(grad_attended, **line):
        return attend_back(
            cut_order, grad_attended, attended_placed, query, key, value, lse, cosine, sine,
            piece_ids, piece_col, heads, **line,
        )

    def result_of(down_sum):
        return (mid + down_sum).astype(bf16).reshape(layer_input.shape)

    q_here = heads * HD
    if near:
        normed_two, hidden, up_part, gate_part, cols_gate_up = feed_forward(
            mid, ffn_gain, spread, rest, number=3
        )
        cols_gate_up = cols_gate_up.reshape(model_width, -1)
        grad_gate_up, down_term = feed_forward_back(
            grad_out, w_down, hidden, up_part, gate_part, number=4
        )
        high = rows_here // 8
        sums = Sums((8, high, model_width))
        terms = {"down": down_term.reshape((4,) + sums.shape)}

        def pick_down(number):
            return "down", lambda ref: ref.at[number]

        def pick_gate_up(number):
            return "gate_up", lambda ref: ref.at[:, number * high : (number + 1) * high, :]

        picks = [pick_down(n) for n in range(4)] + [pick_gate_up(n) for n in range(8)]
        picks += [("out", lambda ref: ref)]

        def line(number, ticks):
            names = sorted(
                {picks[t][0] for t in range(sums.tick, sums.tick + ticks) if t < len(picks)}
            )
            return dict(
                number=number, ticks=ticks, sums=sums, picks=dict(enumerate(picks)),
                arrays=[(name, terms[name]) for name in names],
            )

        down_sum, terms["gate_up"] = product_scattered(
            hidden, w_down, False, extra=(normed_two, grad_gate_up), **line(5, 2)
        )
        result = result_of(down_sum)
        grad_two = product_scattered(grad_gate_up, cols_gate_up, True, **line(6, 2))[0]
        grad_mid, gain_ffn_term = finish_two(grad_two)
        grad_attended, out_term = attended_back(
            grad_mid.astype(bf16), w_out, attended, **line(7, 2)
        )
        terms["out"] = out_term.reshape(sums.shape)
        grad_qkv = back_through_attention(grad_attended, **line(8, 1))
        grad_one, qkv_term = product_scattered(
            grad_qkv, cols_qkv, True, extra=(normed_one, None), **line(9, 2)
        )
        grad_x, gain_attn_term = finish_one(grad_mid, grad_one)
        gains = jnp.stack([gain_attn_term, gain_ffn_term]).reshape(2, groups, rows_here)
        gains = jnp.pad(jnp.moveaxis(gains, 0, 1), ((0, 0), (0, 6), (0, 0)))
        rest = line(10, 8)
        gate_rows, up_rows, qkv_rows, own_gains = tail(
            qkv_term.reshape(8, 8, high, -1), gains,
            {c: sums.done[c] for c in range(4, 7)}, hidden_here, **rest,
        )
        flat = [sums.done[n].reshape(rows_here, model_width) for n in range(4)]
        last = [sums.done[n].reshape(rows_here, model_width) for n in (12, 13, 14)]
        weight_grads = finish(flat, last[0], last[1:], gate_rows, up_rows, heads)
        return (result, grad_x) + tuple(weight_grads) + (own_gains[0], own_gains[1])

    normed_two = gather((unit_two * ffn_gain).astype(bf16))
    grad_all = gather(grad_out)
    gate_up = matmul_f32(normed_two, cols_gate_up)
    gate_proj, up_proj = gate_up[:, :hidden_here], gate_up[:, hidden_here:]
    sigmoid_gate = jax.nn.sigmoid(gate_proj)
    swish = gate_proj * sigmoid_gate
    hidden = (swish * up_proj).astype(bf16)
    gate_part = up_proj * sigmoid_gate * (1.0 + gate_proj * (1.0 - sigmoid_gate))
    down_term = over_tokens(hidden, grad_all).astype(bf16)
    grad_hidden = against_rows(grad_all, w_down)
    grad_gate_up = jnp.concatenate([grad_hidden * gate_part, grad_hidden * swish], 1).astype(bf16)
    grad_mid, gain_ffn_term = finish_two(scatter(grad_gate_up, cols_gate_up, True))
    grad_mid_low = gather(grad_mid.astype(bf16))
    grad_qkv = back_through_attention(against_rows(grad_mid_low, w_out).astype(bf16))
    grad_x, gain_attn_term = finish_one(grad_mid, scatter(grad_qkv, cols_qkv, True))

    def to_rows(term):
        return lax.all_to_all(
            term.astype(bf16).reshape(groups, rows_here, -1), "grp", 0, 0, tiled=True
        )

    def whole_rows(term):
        return jnp.moveaxis(term, 0, 1).reshape(rows_here, -1)

    def kv_rows(term):
        return jnp.sum(
            jnp.moveaxis(term, 0, 1).reshape(rows_here, kv_heads, copies, HD), 2
        ).reshape(rows_here, -1)

    gate_up_term = sum_over_sequences(to_rows(over_tokens(normed_two, grad_gate_up)))
    out_term = sum_over_sequences(over_tokens(attended, grad_mid_low).astype(bf16))
    qkv_term = sum_over_sequences(to_rows(over_tokens(normed_one, grad_qkv)))
    gain_total = lax.psum(jnp.stack([gain_attn_term, gain_ffn_term]), ("grp", "rep"))
    own_gains = lax.dynamic_slice_in_dim(gain_total, own_index * rows_here, rows_here, 1)
    return (
        result_of(scatter(hidden, w_down, False)),
        grad_x,
        whole_rows(qkv_term[..., :q_here]),
        kv_rows(qkv_term[..., q_here : q_here + HD]),
        kv_rows(qkv_term[..., q_here + HD :]),
        out_term,
        whole_rows(gate_up_term[..., :hidden_here]),
        whole_rows(gate_up_term[..., hidden_here:]),
        sum_over_sequences(down_term),
        own_gains[0],
        own_gains[1],
    )


def solution(mesh):
    tokens, table, rows, whole = P("rep", "grp", None), P("rep", None), P("grp", None), P()
    return jax.shard_map(
        on_device,
        mesh=mesh,
        in_specs=(tokens, tokens, table, table) + (rows,) * 7 + (whole,) * 2,
        out_specs=(tokens, tokens) + (rows,) * 7 + (P("grp"),) * 2,
        check_vma=False,
    )
```

```python
import functools

import jax
import jax.numpy as jnp
import numpy as np
from jax import lax
from jax.experimental import pallas as pl
from jax.experimental.pallas import tpu as pltpu
from jax.sharding import PartitionSpec as P

HD = 128
EPS = 1e-05
ROPE_BASE = 1000000.0
SCORE_SCALE = HD**-0.5
LOG2E = 1.4426950408889634
TO_EXP2 = SCORE_SCALE * LOG2E
NEG = -1e30

MESH = pl.DeviceIdType.MESH
f32 = jnp.float32
bf16 = jnp.bfloat16


def matmul_f32(first, second):
    return jnp.dot(first, second, preferred_element_type=f32)


def against_rows(first, second):
    return lax.dot_general(first, second, (((1,), (1,)), ((), ())), preferred_element_type=f32)


def over_tokens(first, second):
    return lax.dot_general(first, second, (((0,), (0,)), ((), ())), preferred_element_type=f32)


def turn_tables(length):
    half_size = HD // 2
    inverse = np.float32(ROPE_BASE) ** (-(np.arange(half_size, dtype=np.float32) * 2) / HD)
    angles = np.arange(length, dtype=np.float32)[:, None] * inverse.astype(np.float32)
    cosine, sine = np.cos(angles), np.sin(angles)
    tables = np.concatenate([cosine, cosine], -1), np.concatenate([-sine, sine], -1)
    return tuple(jnp.asarray(table.astype(np.float32)) for table in tables)


def norm_back(upstream, grad_normed, unit_rows, inv_root, gain):
    scaled = grad_normed * gain
    center_term = jnp.mean(scaled * unit_rows, -1, keepdims=True)
    return (
        upstream + inv_root * (scaled - unit_rows * center_term),
        jnp.sum(grad_normed * unit_rows, 0),
    )


def fold_lanes(values, op):
    out = values[:, :HD]
    for at in range(HD, values.shape[1], HD):
        out = op(out, values[:, at : at + HD])
    return out


def as_row(column):
    return jnp.broadcast_to(column, (column.shape[0], HD)).T[0:1, :]


def attend_kernel(
    heads, cuts, block,
    order_ref, qkv_ref, cos_ref, sin_ref, piece_ref, piece_col_ref,
    out_ref, q_ref, k_ref, v_ref, lse_ref, placed,
    scores,
):
    length = qkv_ref.shape[0]
    cut = length // cuts
    blocks = length // block

    def place_cut(r, _):
        src = pl.ds(pl.multiple_of(r * cut, cut), cut)
        dst = pl.ds(pl.multiple_of(order_ref[0, r] * cut, cut), cut)
        cosine, sine = cos_ref[dst, :], sin_ref[dst, :]
        for h in range(heads + 1):
            part = qkv_ref[src, h * HD : (h + 1) * HD]
            turned = (part * cosine + pltpu.roll(part, HD // 2, 1) * sine).astype(bf16)
            if h < heads:
                q_ref[h, dst, :] = turned
            else:
                k_ref[dst, :] = turned
        v_ref[dst, :] = qkv_ref[src, (heads + 1) * HD :].astype(bf16)
        return 0

    lax.fori_loop(0, cuts, place_cut, 0)

    def one_block(i, _):
        rows = pl.ds(pl.multiple_of(i * block, block), block)
        query = q_ref[:, rows, :].reshape(heads * block, HD)

        def score(j, high):
            cols = pl.ds(pl.multiple_of(j * block, block), block)
            tile = against_rows(query, k_ref[cols, :])
            scores[j] = tile
            return jnp.maximum(high, fold_lanes(tile, jnp.maximum))

        high = lax.fori_loop(0, i, score, jnp.full((heads * block, HD), NEG, f32))
        tile = against_rows(query, k_ref[rows, :])
        q_at = lax.broadcasted_iota(jnp.int32, (block, block), 0)
        k_at = lax.broadcasted_iota(jnp.int32, (block, block), 1)
        q_piece, k_piece = piece_col_ref[rows, 0:1], piece_ref[0:1, rows]
        allowed = (k_at <= q_at) | ((q_piece != 0) & (q_piece == k_piece))
        tile = jnp.concatenate(
            [jnp.where(allowed, tile[h * block : (h + 1) * block], NEG) for h in range(heads)], 0
        )
        scores[i] = tile
        high = jnp.max(jnp.maximum(high, fold_lanes(tile, jnp.maximum)), 1, keepdims=True)

        def weigh(j, state):
            total, mixed = state
            cols = pl.ds(pl.multiple_of(j * block, block), block)
            prob = jnp.exp2((scores[j] - high) * TO_EXP2)
            total = total + fold_lanes(prob, jnp.add)
            return total, mixed + matmul_f32(prob.astype(bf16), v_ref[cols, :])

        zero = jnp.zeros((heads * block, HD), f32)
        total, mixed = lax.fori_loop(0, i + 1, weigh, (zero, zero))
        total = jnp.sum(total, 1, keepdims=True)
        mixed = (mixed / total).astype(bf16)
        log_total = high * TO_EXP2 + jnp.log2(total)
        for h in range(heads):
            placed[rows, h * HD : (h + 1) * HD] = mixed[h * block : (h + 1) * block]
            lse_ref[h : h + 1, rows] = as_row(log_total[h * block : (h + 1) * block])
        return 0

    lax.fori_loop(0, blocks, one_block, 0)

    def store_cut(r, _):
        dst = pl.ds(pl.multiple_of(r * cut, cut), cut)
        src = pl.ds(pl.multiple_of(order_ref[0, r] * cut, cut), cut)
        out_ref[dst, :] = placed[src, :]
        return 0

    lax.fori_loop(0, cuts, store_cut, 0)


def vmem_specs(count):
    return [pl.BlockSpec(memory_space=pltpu.VMEM)] * count


def attend(order, qkv, cosine, sine, piece, piece_col, heads):
    length = qkv.shape[0]
    block = min(512, length)
    return pl.pallas_call(
        functools.partial(attend_kernel, heads, order.shape[1], block),
        out_shape=(
            jax.ShapeDtypeStruct((length, heads * HD), bf16),
            jax.ShapeDtypeStruct((heads, length, HD), bf16),
            jax.ShapeDtypeStruct((length, HD), bf16),
            jax.ShapeDtypeStruct((length, HD), bf16),
            jax.ShapeDtypeStruct((heads, length), f32),
            jax.ShapeDtypeStruct((length, heads * HD), bf16),
        ),
        in_specs=[pl.BlockSpec(memory_space=pltpu.SMEM)] + vmem_specs(5),
        out_specs=tuple(vmem_specs(6)),
        scratch_shapes=[pltpu.VMEM((length // block, heads * block, block), f32)],
        compiler_params=pltpu.CompilerParams(vmem_limit_bytes=60 * 2**20),
        cost_estimate=pl.CostEstimate(
            flops=3 * heads * length * length * HD, bytes_accessed=10 * length * HD * heads * 4,
            transcendentals=heads * length * length // 2,
        ),
    )(order, qkv, cosine, sine, piece, piece_col)


DOWN, GATE_UP, OUT, QKV = 8, 16, 2, 4
CHUNKS = DOWN + GATE_UP + OUT + QKV


def is_chunk(number):
    return 0 <= number < CHUNKS


def is_middle():
    rank = lax.axis_index("rep")
    return (rank == 1) | (rank == 2)


def is_end():
    rank = lax.axis_index("rep")
    return (rank == 0) | (rank == 3)


class NoLine:
    ticks = 0

    def greet(self, barrier, others):
        if others:
            pl.semaphore_wait(barrier, others)

    def start(self):
        pass

    def step(self):
        pass

    def end(self):
        pass


class Line:
    def __init__(self, first, ticks, picks, refs, outs, scratch):
        self.first, self.ticks, self.picks, self.refs, self.outs = first, ticks, picks, refs, outs
        (
            self.inward, self.across, self.own, self.pair, self.total, self.sems, self.local,
            self.carries,
        ) = scratch
        rank = lax.axis_index("rep")
        self.partner = {"rep": rank + 1 - 2 * (rank % 2)}
        self.peer = {"rep": 3 - rank}
        self.now = 0
        self.kept = []

    def greet(self, barrier, others):
        pl.semaphore_signal(barrier, inc=1, device_id=self.partner, device_id_type=MESH)

        @pl.when(is_middle())
        def _():
            pl.semaphore_signal(barrier, inc=1, device_id=self.peer, device_id_type=MESH)
            pl.semaphore_wait(barrier, others + 2)

        @pl.when(is_end())
        def _():
            pl.semaphore_wait(barrier, others + 1)

    def remote(self, hop, number, src, dst, device):
        return pltpu.make_async_remote_copy(
            src_ref=src, dst_ref=dst, send_sem=self.sems.at[0, hop, number],
            recv_sem=self.sems.at[1, hop, number], device_id=device, device_id_type=MESH,
        )

    def hops(self, number):
        tick = self.first + number
        term = pair = total = None
        if is_chunk(tick):
            which, pick = self.picks[tick]
            term = (
                lambda: self.remote(
                    0, number, pick(self.refs[which]), self.inward.at[number], self.partner
                ),
                lambda: pltpu.make_async_copy(
                    pick(self.refs[which]), self.own.at[tick % 2], self.local.at[0, number]
                ),
            )
        if is_chunk(tick - 2):
            before = self.refs[f"pair{number}"] if number < 2 else self.pair.at[(tick - 2) % 3]
            pair = (
                lambda: self.remote(1, number, before, self.across.at[number], self.peer),
                lambda: pltpu.make_async_copy(
                    before, self.pair.at[(tick - 2) % 3], self.carries.at[number]
                ),
            )
        if is_chunk(tick - 4):
            done = self.refs[f"total{number}"] if number < 2 else self.total.at[(tick - 4) % 3]
            slot = self.outs[tick - 4]
            total = (
                lambda: self.remote(2, number, done, slot, self.partner),
                lambda: pltpu.make_async_copy(done, slot, self.local.at[1, number]),
            )
        return term, pair, total

    def open(self, number):
        term, pair, total = self.hops(number)

        @pl.when(is_end())
        def _():
            if term:
                term[0]().start()

        @pl.when(is_middle())
        def _():
            if pair:
                pair[0]().start()
            if total:
                total[0]().start()
            if term:
                term[1]().start()
            if total:
                total[1]().start()
            if pair and number < 2:
                pair[1]().start()

    def close(self, number):
        term, pair, total = self.hops(number)

        @pl.when(is_end())
        def _():
            if term:
                term[0]().wait_send()
            if total:
                total[0]().wait_recv()

        @pl.when(is_middle())
        def _():
            if total:
                total[0]().wait_send()
                total[1]().wait()
            if pair:
                pair[0]().wait_send()
                pair[0]().wait_recv()
            if term:
                term[0]().wait_recv()

    def add(self, number):
        term, pair, _ = self.hops(number)
        tick = self.first + number

        def sum_of(into, first, second):
            def one(g, _):
                into[g] = (first[g].astype(f32) + second[g].astype(f32)).astype(bf16)
                return 0

            lax.fori_loop(0, into.shape[0], one, 0)

        @pl.when(is_middle())
        def _():
            if pair:
                if number < 2:
                    pair[1]().wait()
                sum_of(
                    self.total.at[(tick - 2) % 3], self.pair.at[(tick - 2) % 3],
                    self.across.at[number],
                )
            if term:
                term[1]().wait()
                sum_of(self.pair.at[tick % 3], self.own.at[tick % 2], self.inward.at[number])

    def keep(self, number):
        tick = self.first + number
        which = number - (self.ticks - 2)
        made = []
        if is_chunk(tick):
            made.append((self.pair.at[tick % 3], self.outs[f"pair{which}"], 2 + which))
        if is_chunk(tick - 2):
            made.append((self.total.at[(tick - 2) % 3], self.outs[f"total{which}"], 4 + which))
        copies = [
            lambda src=src, dst=dst, at=at: pltpu.make_async_copy(src, dst, self.carries.at[at])
            for src, dst, at in made
        ]

        @pl.when(is_middle())
        def _():
            for copy in copies:
                copy().start()

        self.kept += copies

    def start(self):
        self.open(0)

    def step(self):
        if self.now + 1 < self.ticks:
            self.close(self.now)
            self.open(self.now + 1)
            self.add(self.now)
            if self.now == self.ticks - 2:
                self.keep(self.now)
            self.now += 1

    def end(self):
        while self.now + 1 < self.ticks:
            self.step()
        self.close(self.now)
        self.add(self.now)
        self.keep(self.now)

        @pl.when(is_middle())
        def _():
            for copy in self.kept:
                copy().wait()


def line_slots(first, ticks):
    return [t - 4 for t in range(first, first + ticks) if is_chunk(t - 4)]


class Sums:
    def __init__(self, shape):
        self.shape, self.tick, self.kept, self.done = shape, 0, {}, {}


def run(kernel, ins, outs, scratch, number, cost, sums=None, ticks=0, arrays=(), picks=None, vmem=58):
    ins, outs, scratch = list(ins), list(outs), list(scratch)
    counts = (len(ins), len(outs), len(scratch))
    first = sums.tick if ticks else 0
    names_in, names_out = [], []
    if ticks:
        last = first + ticks - 1
        chunk = jax.ShapeDtypeStruct(sums.shape, bf16)
        for name, array in arrays:
            names_in.append(name)
            ins.append((array, pl.ANY))
        for which in (0, 1):
            for name, chunk_at in ((f"pair{which}", first - 2), (f"total{which}", first - 4)):
                if is_chunk(chunk_at + which):
                    names_in.append(name)
                    ins.append((sums.kept[name], pl.ANY))
        names_out = line_slots(first, ticks)
        for which in (0, 1):
            for name, chunk_at in ((f"pair{which}", last - 1), (f"total{which}", last - 3)):
                if is_chunk(chunk_at + which):
                    names_out.append(name)
        outs += [(chunk, pl.ANY)] * len(names_out)
        scratch += [
            pltpu.VMEM((ticks,) + sums.shape, bf16),
            pltpu.VMEM((ticks,) + sums.shape, bf16),
            pltpu.VMEM((2,) + sums.shape, bf16),
            pltpu.VMEM((3,) + sums.shape, bf16),
            pltpu.VMEM((3,) + sums.shape, bf16),
            pltpu.SemaphoreType.DMA((2, 3, ticks)),
            pltpu.SemaphoreType.DMA((2, ticks)),
            pltpu.SemaphoreType.DMA((6,)),
        ]

    def body(*refs):
        in_refs, rest = refs[: len(ins)], refs[len(ins) :]
        out_refs, scratch_refs = rest[: len(outs)], rest[len(outs) :]
        line = NoLine()
        if ticks:
            line = Line(
                first, ticks, picks, dict(zip(names_in, in_refs[counts[0] :])),
                dict(zip(names_out, out_refs[counts[1] :])), scratch_refs[counts[2] :],
            )
        kernel(in_refs[: counts[0]], out_refs[: counts[1]], scratch_refs[: counts[2]], line)

    results = pl.pallas_call(
        body,
        out_shape=tuple(shape for shape, _ in outs),
        in_specs=[pl.BlockSpec(memory_space=space) for _, space in ins],
        out_specs=tuple(pl.BlockSpec(memory_space=space) for _, space in outs),
        scratch_shapes=scratch,
        compiler_params=pltpu.CompilerParams(
            vmem_limit_bytes=vmem * 2**20,
            **({} if number is None else {"collective_id": number, "has_side_effects": True}),
        ),
        cost_estimate=pl.CostEstimate(
            flops=cost[0], bytes_accessed=cost[1], transcendentals=cost[2]
        ),
    )(*[array for array, _ in ins])
    for name, result in zip(names_out, results[counts[1] :]):
        if name in line_slots(first, ticks):
            sums.done[name] = result
        else:
            sums.kept[name] = result
    if ticks:
        sums.tick += ticks
    return results[: counts[1]]


SMEM, VMEM, ANY = pltpu.SMEM, pltpu.VMEM, pl.ANY


def attend_back_kernel(
    heads, block, ins, outs, scratch, line
):
    grad_ref, out_ref, q_ref, k_ref, v_ref, lse_ref, cos_ref, sin_ref, piece_ref, piece_col_ref = ins
    (grad_qkv_ref,) = outs
    grads, centers, grad_q = scratch
    if line.ticks:
        line.greet(pltpu.get_barrier_semaphore(), 0)
        line.start()
    length = grad_ref.shape[0]
    blocks = length // block

    def take_block(i, _):
        rows = pl.ds(pl.multiple_of(i * block, block), block)
        for h in range(heads):
            grad = grad_ref[rows, h * HD : (h + 1) * HD].astype(bf16)
            grads[h, rows, :] = grad
            product = grad.astype(f32) * out_ref[rows, h * HD : (h + 1) * HD].astype(f32)
            centers[h, rows, :] = jnp.broadcast_to(
                jnp.sum(product, 1, keepdims=True), (block, HD)
            )
        return 0

    lax.fori_loop(0, blocks, take_block, 0)
    grad_q[...] = jnp.zeros_like(grad_q)

    def key_block(j, _):
        cols = pl.ds(pl.multiple_of(j * block, block), block)
        key, value = k_ref[cols, :], v_ref[cols, :]

        def one(i, state, diagonal):
            grad_key, grad_value = state
            rows = pl.ds(pl.multiple_of(i * block, block), block)
            for h in range(heads):
                query, grad = q_ref[h, rows, :], grads[h, rows, :]
                log_total = lse_ref[h : h + 1, rows]
                center = centers[h, rows, :].T[0:1, :]
                prob = jnp.exp2(against_rows(key, query) * TO_EXP2 - log_total)
                if diagonal:
                    k_at = lax.broadcasted_iota(jnp.int32, (block, block), 0)
                    q_at = lax.broadcasted_iota(jnp.int32, (block, block), 1)
                    k_piece, q_piece = piece_col_ref[cols, 0:1], piece_ref[0:1, cols]
                    allowed = (k_at <= q_at) | ((q_piece != 0) & (q_piece == k_piece))
                    prob = jnp.where(allowed, prob, 0.0)
                grad_prob = against_rows(value, grad)
                grad_score = (prob * (grad_prob - center)).astype(bf16)
                grad_value = grad_value + matmul_f32(prob.astype(bf16), grad)
                grad_key = grad_key + matmul_f32(grad_score, query)
                grad_q[h, rows, :] += over_tokens(grad_score, key)
            return grad_key, grad_value

        zero = jnp.zeros((block, HD), f32)
        state = one(j, (zero, zero), True)
        grad_key, grad_value = lax.fori_loop(
            j + 1, blocks, functools.partial(one, diagonal=False), state
        )
        grad_key = grad_key * SCORE_SCALE
        grad_key = grad_key * cos_ref[cols, :] - pltpu.roll(grad_key, HD // 2, 1) * sin_ref[cols, :]
        grad_qkv_ref[cols, heads * HD : (heads + 1) * HD] = grad_key.astype(bf16)
        grad_qkv_ref[cols, (heads + 1) * HD :] = grad_value.astype(bf16)
        return 0

    for j in range(min(2, blocks - 1)):
        lax.fori_loop(j, j + 1, key_block, 0)
        line.step()
    lax.fori_loop(min(2, blocks - 1), blocks, key_block, 0)

    def turn_back(i, _):
        rows = pl.ds(pl.multiple_of(i * block, block), block)
        for h in range(heads):
            grad = grad_q[h, rows, :] * SCORE_SCALE
            grad = grad * cos_ref[rows, :] - pltpu.roll(grad, HD // 2, 1) * sin_ref[rows, :]
            grad_qkv_ref[rows, h * HD : (h + 1) * HD] = grad.astype(bf16)
        return 0

    lax.fori_loop(0, blocks, turn_back, 0)
    line.end()


def take_cuts_kernel(cuts, holder_ref, rows_ref, out_ref):
    cut = out_ref.shape[0] // cuts

    def one(p, _):
        src = pl.ds(pl.multiple_of(holder_ref[0, p] * cut, cut), cut)
        out_ref[pl.ds(pl.multiple_of(p * cut, cut), cut), :] = rows_ref[src, :]
        return 0

    lax.fori_loop(0, cuts, one, 0)


def take_cuts(holder, rows):
    return pl.pallas_call(
        functools.partial(take_cuts_kernel, holder.shape[1]),
        out_shape=jax.ShapeDtypeStruct(rows.shape, rows.dtype),
        in_specs=[pl.BlockSpec(memory_space=pltpu.SMEM)] + vmem_specs(1),
        out_specs=pl.BlockSpec(memory_space=pltpu.VMEM),
        cost_estimate=pl.CostEstimate(
            flops=0, bytes_accessed=2 * rows.size * rows.dtype.itemsize, transcendentals=0
        ),
    )(holder, rows)


def attend_back(
    order, grad, out, query, key, value, lse, cosine, sine, piece, piece_col, heads, **line
):
    cuts = jnp.arange(order.shape[1], dtype=order.dtype)
    holder = jnp.sum(jnp.where(order[0][None, :] == cuts[:, None], cuts[None, :], 0), 1)[None, :]
    length = grad.shape[0]
    block = min(512, length)
    tall = [take_cuts(holder, grad), out, query, key, value, lse, cosine, sine, piece, piece_col]
    grad_qkv = run(
        functools.partial(attend_back_kernel, heads, block),
        [(array, VMEM) for array in tall],
        [(jax.ShapeDtypeStruct((length, (heads + 2) * HD), bf16), VMEM)],
        [
            pltpu.VMEM((heads, length, HD), bf16),
            pltpu.VMEM((heads, length, HD), f32),
            pltpu.VMEM((heads, length, HD), f32),
        ],
        line.pop("number", None),
        (8 * heads * length * length * HD, 14 * length * HD * heads * 4, heads * length * length // 2),
        **line,
    )[0]
    return take_cuts(order, grad_qkv)


def place_in_group():
    me = lax.axis_index("grp")
    return me // 4, (me // 2) % 2, me % 2


def other(flip_y, flip_x, flip_core):
    y, x, core = place_in_group()
    return ((y + flip_y) % 2) * 4 + ((x + flip_x) % 2) * 2 + (core + flip_core) % 2


def chip_rows(flip_y, flip_x, rows):
    y, x, _ = place_in_group()
    first = (((y + flip_y) % 2) * 2 + (x + flip_x) % 2) * (2 * rows)
    return pl.ds(pl.multiple_of(first, 2 * rows), 2 * rows)


NEIGHBOURS = ((0, 0, 1), (0, 1, 0), (1, 0, 0))
EVERYONE = tuple((n // 4, (n // 2) % 2, n % 2) for n in range(1, 8))


def greet_group(line, flips=NEIGHBOURS):
    barrier = pltpu.get_barrier_semaphore()
    for flip in flips:
        pl.semaphore_signal(barrier, inc=1, device_id={"grp": other(*flip)}, device_id_type=MESH)
    line.greet(barrier, len(flips))


SIBLING, ALONG_X, ALONG_Y, ACROSS = (0, 0), (0, 1), (1, 0), (1, 1)


def gather_rows(rows, all_ref, sends, recvs, on_chip, line, then=None):
    half = rows // 2

    def block(chip, core, part=None):
        first = other(*chip, core) * rows
        if part is None:
            return pl.ds(pl.multiple_of(first, rows), rows)
        return pl.ds(pl.multiple_of(first + part * half, half), half)

    def copy(number, chip, core, part, target):
        where = all_ref.at[block(chip, core, part), :]
        return pltpu.make_async_remote_copy(
            src_ref=where, dst_ref=where, send_sem=sends.at[number], recv_sem=recvs.at[number],
            device_id={"grp": other(*target)}, device_id_type=MESH,
        )

    def landed(number, chip, core, part):
        where = all_ref.at[block(chip, core, part), :]
        pltpu.make_async_remote_copy(
            src_ref=where, dst_ref=where, send_sem=sends.at[number], recv_sem=recvs.at[number],
            device_id={"grp": other(0, 0, 1)}, device_id_type=MESH,
        ).wait_recv()

    to_s, to_x, to_y = (0, 0, 1), (0, 1, 0), (1, 0, 0)
    started = []

    def send(*what):
        one = copy(*what)
        one.start()
        started.append(one)

    send(1, SIBLING, 0, 1, to_x)
    send(3, SIBLING, 0, 0, to_y)
    send(0, SIBLING, 0, None, to_s)
    send(2, SIBLING, 0, 0, to_x)
    send(4, SIBLING, 0, 1, to_y)
    if then:
        then()
    landed(0, SIBLING, 1, None)
    on_chip(*SIBLING)
    landed(1, ALONG_X, 0, 1)
    send(6, ALONG_X, 0, 1, to_y)
    landed(3, ALONG_Y, 0, 0)
    send(5, ALONG_Y, 0, 0, to_x)
    send(7, ALONG_X, 0, 1, to_s)
    send(8, ALONG_Y, 0, 0, to_s)
    line.step()
    landed(2, ALONG_X, 0, 0)
    send(9, ALONG_X, 0, 0, to_s)
    landed(4, ALONG_Y, 0, 1)
    send(10, ALONG_Y, 0, 1, to_s)
    line.step()
    landed(7, ALONG_X, 1, 1)
    landed(9, ALONG_X, 1, 0)
    on_chip(*ALONG_X)
    landed(5, ACROSS, 0, 0)
    send(11, ACROSS, 0, 0, to_s)
    landed(6, ACROSS, 0, 1)
    send(12, ACROSS, 0, 1, to_s)
    line.step()
    landed(8, ALONG_Y, 1, 0)
    landed(10, ALONG_Y, 1, 1)
    on_chip(*ALONG_Y)
    landed(11, ACROSS, 1, 0)
    landed(12, ACROSS, 1, 1)
    on_chip(*ACROSS)
    for one in started:
        one.wait_send()
    line.end()


GATHER_COPIES = 13


def rms_normed(values, gain):
    return values * lax.rsqrt(jnp.mean(values * values, -1, keepdims=True) + EPS) * gain


class Moves:
    def __init__(self, sems):
        self.sems, self.count, self.open = sems, 0, []

    def start(self, src, dst):
        one = pltpu.make_async_copy(src, dst, self.sems.at[self.count])
        self.count += 1
        one.start()
        return one

    def later(self, src, dst):
        self.open.append(self.start(src, dst))

    def finish(self):
        for one in self.open:
            one.wait()


def gather_scratch(rows, width, moves):
    return [
        pltpu.VMEM((8 * rows, width), bf16),
        pltpu.SemaphoreType.DMA((GATHER_COPIES,)),
        pltpu.SemaphoreType.DMA((GATHER_COPIES,)),
        pltpu.SemaphoreType.DMA((moves,)),
    ]


def own_rows(rows):
    return pl.ds(pl.multiple_of(other(0, 0, 0) * rows, rows), rows)


def send_columns(pieces, sends, recvs, moves):
    copies = []
    for which, (rows_ref, width, there) in enumerate(pieces):
        for number, flip in enumerate(EVERYONE):
            target = other(*flip)
            cols = pl.ds(pl.multiple_of(target * width, width), width)
            one = pltpu.make_async_remote_copy(
                src_ref=rows_ref.at[:, cols], dst_ref=there,
                send_sem=sends.at[which, number], recv_sem=recvs.at[which, number],
                device_id={"grp": target}, device_id_type=MESH,
            )
            one.start()
            copies.append(one)
        mine = pl.ds(pl.multiple_of(other(0, 0, 0) * width, width), width)
        moves.later(rows_ref.at[:, mine], there)
    return copies


def gather_normed_kernel(ins, outs, scratch, line):
    x_ref, gain_ref = ins[:2]
    weights = ins[2:]
    all_ref, cols_ref = outs
    held, sends, recvs, sems, col_sends, col_recvs = scratch
    rows = x_ref.shape[0]
    moves = Moves(sems)
    held[own_rows(rows), :] = rms_normed(x_ref[...].astype(f32), gain_ref[...]).astype(bf16)
    greet_group(line, EVERYONE)
    col_copies = []

    def send_weights():
        pieces, low = [], 0
        tall = weights[0].shape[0]
        there = pl.ds(pl.multiple_of(other(0, 0, 0) * tall, tall), tall)
        for weight in weights:
            width = weight.shape[1] // 8
            pieces.append((weight, width, cols_ref.at[there, low : low + width]))
            low += width
        col_copies.extend(send_columns(pieces, col_sends, col_recvs, moves))

    def on_chip(*chip):
        where = chip_rows(*chip, rows)
        moves.later(held.at[where, :], all_ref.at[where, :])

    gather_rows(rows, held, sends, recvs, on_chip, line, send_weights)
    for one in col_copies:
        one.wait()
    moves.finish()


def gather_normed(x, gain, weights, **line):
    rows, width = x.shape
    deep = sum(weight.shape[1] for weight in weights) // 8
    return run(
        gather_normed_kernel,
        [(x, VMEM), (gain, VMEM)] + [(weight, ANY) for weight in weights],
        [
            (jax.ShapeDtypeStruct((8 * rows, width), bf16), ANY),
            (jax.ShapeDtypeStruct((8 * weights[0].shape[0], deep), bf16), ANY),
        ],
        gather_scratch(rows, width, 4 + len(weights))
        + [pltpu.SemaphoreType.DMA((len(weights), 7))] * 2,
        line.pop("number"),
        (0, 150 * rows * width * 2, 0),
        **line,
    )


def columns_kernel(rows_here, ins, outs, scratch, line):
    (cols_ref,) = outs
    sends, recvs, sems = scratch
    moves = Moves(sems)
    barrier = pltpu.get_barrier_semaphore()
    for flip in EVERYONE:
        pl.semaphore_signal(barrier, inc=1, device_id={"grp": other(*flip)}, device_id_type=MESH)
    pl.semaphore_wait(barrier, 7)
    first = pl.multiple_of(lax.axis_index("rep") * rows_here, rows_here)
    me = other(0, 0, 0)
    pieces, low = [], 0
    for weight in ins:
        width = weight.shape[1] // 8
        pieces.append(
            (weight.at[pl.ds(first, rows_here), :], width, cols_ref.at[me, :, low : low + width])
        )
        low += width
    for one in send_columns(pieces, sends, recvs, moves):
        one.wait()
    moves.finish()


def columns_of_some(weights, rows_here, number):
    deep = sum(weight.shape[1] for weight in weights) // 8
    return run(
        functools.partial(columns_kernel, rows_here),
        [(weight, ANY) for weight in weights],
        [(jax.ShapeDtypeStruct((8, rows_here, deep), bf16), ANY)],
        [pltpu.SemaphoreType.DMA((len(weights), 7))] * 2
        + [pltpu.SemaphoreType.DMA((len(weights),))],
        number, (0, 50 * 8 * rows_here * deep, 0),
    )[0]


def feed_forward_kernel(tile, ins, outs, scratch, line):
    mid_ref, gain_ref, spread_ref, rest_ref = ins
    all_ref, hidden_ref, up_part_ref, gate_part_ref, whole_ref = outs
    held, sends, recvs, sems, weight, hidden, up_part, gate_part = scratch
    rows = mid_ref.shape[0]
    inner = hidden.shape[1]
    moves = Moves(sems)
    planes, _, tall, deep = spread_ref.shape
    loads = [
        moves.start(spread_ref.at[z], weight.at[:, z * tall : (z + 1) * tall, :])
        for z in range(planes)
    ]
    loads.append(moves.start(rest_ref, weight.at[:, planes * tall :, :]))
    held[own_rows(rows), :] = rms_normed(mid_ref[...], gain_ref[...]).astype(bf16)
    greet_group(line)
    line.start()

    def on_chip(*chip):
        where = chip_rows(*chip, rows)
        moves.later(held.at[where, :], all_ref.at[where, :])
        if chip == SIBLING:
            for one in loads:
                one.wait()
            moves.later(weight, whole_ref)

        def column(t, _):
            cols = pl.ds(pl.multiple_of(t * tile, tile), tile)
            up_cols = pl.ds(pl.multiple_of(inner + t * tile, tile), tile)
            lhs = held[where, :]
            gate = matmul_f32(lhs, weight[:, :, cols].reshape(-1, tile))
            up = matmul_f32(lhs, weight[:, :, up_cols].reshape(-1, tile))
            sigma = 1.0 / (1.0 + jnp.exp(-gate))
            swish = gate * sigma
            hidden[where, cols] = (swish * up).astype(bf16)
            up_part[where, cols] = swish.astype(bf16)
            gate_part[where, cols] = (up * sigma * (1.0 + gate * (1.0 - sigma))).astype(bf16)
            return 0

        lax.fori_loop(0, inner // tile, column, 0)
        for src, dst in ((hidden, hidden_ref), (up_part, up_part_ref), (gate_part, gate_part_ref)):
            moves.later(src.at[where, :], dst.at[where, :])

    gather_rows(rows, held, sends, recvs, on_chip, line)
    moves.finish()


def feed_forward(mid, gain, spread, rest, **line):
    rows, width = mid.shape
    inner = rest.shape[2] // 2
    weight = (8, width // 8, 2 * inner)
    tall = jax.ShapeDtypeStruct((8 * rows, inner), bf16)
    return run(
        functools.partial(feed_forward_kernel, min(256, inner)),
        [(mid, VMEM), (gain, VMEM), (spread, ANY), (rest, ANY)],
        [(jax.ShapeDtypeStruct((8 * rows, width), bf16), ANY)]
        + [(tall, ANY)] * 3
        + [(jax.ShapeDtypeStruct(weight, bf16), ANY)],
        gather_scratch(rows, width, 22)
        + [pltpu.VMEM(weight, bf16)]
        + [pltpu.VMEM((8 * rows, inner), bf16)] * 3,
        line.pop("number"),
        (32 * rows * width * inner, 150 * rows * width * 2, 8 * rows * inner),
        **line,
    )


def feed_forward_back_kernel(tile, ins, outs, scratch, line):
    grad_ref, w_ref, hidden_ref, up_part_ref, gate_part_ref = ins
    grad_gate_up_ref, down_ref = outs
    held, sends, recvs, sems, weight, hidden, up_part, gate_part, grads, down, down_low = scratch
    rows = grad_ref.shape[0]
    inner, width = weight.shape
    moves = Moves(sems)
    loads = [
        moves.start(src, dst)
        for src, dst in (
            (w_ref, weight), (hidden_ref, hidden), (up_part_ref, up_part), (gate_part_ref, gate_part)
        )
    ]
    held[own_rows(rows), :] = grad_ref[...]
    greet_group(line)
    line.start()

    def on_chip(*chip):
        where = chip_rows(*chip, rows)
        if chip == SIBLING:
            for one in loads:
                one.wait()

        def column(t, _):
            cols = pl.ds(pl.multiple_of(t * tile, tile), tile)
            up_cols = pl.ds(pl.multiple_of(inner + t * tile, tile), tile)
            incoming = held[where, :]
            grad_hidden = against_rows(incoming, weight[cols, :])
            grads[where, cols] = (grad_hidden * gate_part[where, cols].astype(f32)).astype(bf16)
            grads[where, up_cols] = (grad_hidden * up_part[where, cols].astype(f32)).astype(bf16)
            term = over_tokens(hidden[where, cols], incoming)
            if chip == SIBLING:
                down[cols, :] = term
            elif chip == ACROSS:
                down_low[cols, :] = (down[cols, :] + term).astype(bf16)
            else:
                down[cols, :] += term
            return 0

        lax.fori_loop(0, inner // tile, column, 0)
        moves.later(grads.at[where, :], grad_gate_up_ref.at[where, :])

    gather_rows(rows, held, sends, recvs, on_chip, line)
    moves.later(down_low, down_ref)
    moves.finish()


def feed_forward_back(grad, w_down, hidden, up_part, gate_part, **line):
    rows, width = grad.shape
    inner = w_down.shape[0]
    return run(
        functools.partial(feed_forward_back_kernel, min(256, inner)),
        [(grad, VMEM)] + [(array, ANY) for array in (w_down, hidden, up_part, gate_part)],
        [
            (jax.ShapeDtypeStruct((8 * rows, 2 * inner), bf16), ANY),
            (jax.ShapeDtypeStruct((inner, width), bf16), ANY),
        ],
        gather_scratch(rows, width, 9)
        + [pltpu.VMEM(w_down.shape, bf16)]
        + [pltpu.VMEM((8 * rows, inner), bf16)] * 3
        + [
            pltpu.VMEM((8 * rows, 2 * inner), bf16),
            pltpu.VMEM(w_down.shape, f32),
            pltpu.VMEM(w_down.shape, bf16),
        ],
        line.pop("number"),
        (32 * rows * width * inner, 150 * rows * width * 2, 0),
        vmem=62,
        **line,
    )


def attended_back_kernel(ins, outs, scratch, line):
    grad_ref, w_ref, attended_ref = ins
    grad_attended_ref, out_term_ref = outs
    held, sends, recvs, sems, total = scratch
    rows = grad_ref.shape[0]
    moves = Moves(sems)
    held[own_rows(rows), :] = grad_ref[...]
    greet_group(line)
    line.start()

    def on_chip(*chip):
        where = chip_rows(*chip, rows)
        incoming = held[where, :]
        grad_attended_ref[where, :] = against_rows(incoming, w_ref[...]).astype(bf16)
        term = over_tokens(attended_ref[where, :], incoming)
        if chip == SIBLING:
            total[...] = term
        elif chip == ACROSS:
            out_term_ref[...] = (total[...] + term).astype(bf16)
        else:
            total[...] += term

    gather_rows(rows, held, sends, recvs, on_chip, line)
    moves.finish()


def attended_back(grad, w_out, attended, **line):
    rows, width = grad.shape
    return run(
        attended_back_kernel,
        [(array, VMEM) for array in (grad, w_out, attended)],
        [
            (jax.ShapeDtypeStruct(attended.shape, bf16), VMEM),
            (jax.ShapeDtypeStruct(w_out.shape, bf16), VMEM),
        ],
        gather_scratch(rows, width, 1) + [pltpu.VMEM(w_out.shape, f32)],
        line.pop("number"),
        (32 * rows * width * w_out.shape[0], 150 * rows * width * 2, 0),
        **line,
    )


class WeightTerm:
    def __init__(self, rows_ref, columns_ref, term_ref, scratch):
        self.rows_ref, self.columns_ref, self.term_ref = rows_ref, columns_ref, term_ref
        self.loaded, self.ready, self.sems = scratch
        self.tile = self.loaded.shape[2]
        for number in (0, 1):
            self.load(number).start()

    def load(self, number):
        cols = slice(number * self.tile, (number + 1) * self.tile)
        return pltpu.make_async_copy(
            self.rows_ref.at[:, cols], self.loaded.at[number % 2], self.sems.at[0, number % 2]
        )

    def store(self, number):
        return pltpu.make_async_copy(
            self.ready.at[number % 2], self.term_ref.at[number], self.sems.at[1, number % 2]
        )

    def work(self, numbers):
        for number in numbers:
            at = number % 2
            self.load(number).wait()
            if number >= 2:
                self.store(number - 2).wait()
            width = self.columns_ref.shape[1]
            step = min(256, width)

            def column(t, _):
                cols = pl.ds(pl.multiple_of(t * step, step), step)
                term = over_tokens(self.loaded[at], self.columns_ref[:, cols])
                self.ready[at, :, cols] = term.astype(bf16)
                return 0

            lax.fori_loop(0, width // step, column, 0)
            self.store(number).start()
            if number + 2 < 8:
                self.load(number + 2).start()

    def finish(self):
        for number in (6, 7):
            self.store(number).wait()


def scatter_kernel(turned, tile, extra, ins, outs, scratch, line):
    a_ref, b_ref = ins[:2]
    out_ref = outs[0]
    part, to_s, from_s, to_chip, held, relay, last, sends, recvs = scratch[:9]
    rows, width = out_ref.shape
    half = rows // 2
    _, _, core = place_in_group()
    greet_group(line)
    line.start()
    if extra:
        columns_ref = a_ref
        if extra == "loaded":
            columns_ref = scratch[12]
            columns_copy = pltpu.make_async_copy(ins[3], columns_ref, scratch[13].at[0])
            columns_copy.start()
        term = WeightTerm(ins[2], columns_ref, outs[1], scratch[9:12])
    own_at = pl.multiple_of(core * rows, rows)
    other_at = pl.multiple_of((1 - core) * rows, rows)
    started = []

    def send(number, src, dst, target):
        one = pltpu.make_async_remote_copy(
            src_ref=src, dst_ref=dst, send_sem=sends.at[number], recv_sem=recvs.at[number],
            device_id={"grp": other(*target)}, device_id_type=MESH,
        )
        one.start()
        started.append(one)
        return one

    def landed(number, where):
        pltpu.make_async_remote_copy(
            src_ref=where, dst_ref=where, send_sem=sends.at[number], recv_sem=recvs.at[number],
            device_id={"grp": other(0, 0, 1)}, device_id_type=MESH,
        ).wait_recv()

    to_sib, to_x, to_y = (0, 0, 1), (0, 1, 0), (1, 0, 0)

    def make(number, chip):
        where = chip_rows(*chip, rows)

        def column(t, _):
            cols = pl.ds(pl.multiple_of(t * tile, tile), tile)
            lhs = a_ref[where, :]
            if turned:
                part[:, cols] = against_rows(lhs, b_ref[cols, :])
            else:
                part[:, cols] = matmul_f32(lhs, b_ref[:, cols])
            return 0

        lax.fori_loop(0, width // tile, column, 0)
        to_s[number] = part[pl.ds(other_at, rows), :].astype(bf16)
        send(number, to_s.at[number], from_s.at[number], to_sib)

    def own(low, number):
        at = pl.ds(pl.multiple_of(core * rows + low * half, half), half)
        return part[at, :] + from_s[number, low * half : (low + 1) * half, :].astype(f32)

    first, second = slice(0, half), slice(half, rows)
    make(0, ACROSS)
    landed(0, from_s.at[0])
    to_chip[0, first, :] = own(0, 0).astype(bf16)
    send(4, to_chip.at[0, first, :], relay.at[0], to_x)
    to_chip[0, second, :] = own(1, 0).astype(bf16)
    send(5, to_chip.at[0, second, :], relay.at[1], to_y)
    make(1, ALONG_X)
    landed(1, from_s.at[1])
    to_chip[1, first, :] = own(0, 1).astype(bf16)
    send(6, to_chip.at[1, first, :], last.at[0, first, :], to_x)
    held[0] = own(1, 1)
    line.step()
    make(2, ALONG_Y)
    landed(2, from_s.at[2])
    to_chip[2, second, :] = own(1, 2).astype(bf16)
    send(7, to_chip.at[2, second, :], last.at[1, second, :], to_y)
    held[1] = own(0, 2)
    if extra:
        if extra == "loaded":
            columns_copy.wait()
        term.work((0, 1, 2))
    landed(5, relay.at[1])
    to_chip[1, second, :] = (held[0] + relay[1].astype(f32)).astype(bf16)
    send(8, to_chip.at[1, second, :], last.at[0, second, :], to_x)
    landed(4, relay.at[0])
    to_chip[2, first, :] = (held[1] + relay[0].astype(f32)).astype(bf16)
    send(9, to_chip.at[2, first, :], last.at[1, first, :], to_y)
    line.step()
    make(3, SIBLING)
    if extra:
        term.work((3, 4))
        line.step()
        term.work((5, 6, 7))
    landed(3, from_s.at[3])
    for low in (0, 1):
        out_ref[low * half : (low + 1) * half, :] = own(low, 3)
    landed(6, last.at[0, first, :])
    out_ref[first, :] += last[0, first, :].astype(f32)
    landed(7, last.at[1, second, :])
    out_ref[second, :] += last[1, second, :].astype(f32)
    line.step()
    landed(8, last.at[0, second, :])
    out_ref[second, :] += last[0, second, :].astype(f32)
    landed(9, last.at[1, first, :])
    out_ref[first, :] += last[1, first, :].astype(f32)
    for one in started:
        one.wait_send()
    if extra:
        term.finish()
    line.end()


def product_scattered(a, b, turned, extra=None, **line):
    length, depth = a.shape
    width = b.shape[0] if turned else b.shape[1]
    rows = length // 8
    tile = min(256, width)
    ins = [(a, VMEM), (b, VMEM)]
    outs = [(jax.ShapeDtypeStruct((rows, width), f32), VMEM)]
    scratch = [
        pltpu.VMEM((2 * rows, width), f32),
        pltpu.VMEM((4, rows, width), bf16),
        pltpu.VMEM((4, rows, width), bf16),
        pltpu.VMEM((3, rows, width), bf16),
        pltpu.VMEM((2, rows // 2, width), f32),
        pltpu.VMEM((2, rows // 2, width), bf16),
        pltpu.VMEM((2, rows, width), bf16),
        pltpu.SemaphoreType.DMA((10,)),
        pltpu.SemaphoreType.DMA((10,)),
    ]
    flops, kind = 2 * length * depth * width, None
    if extra:
        first, second = extra
        kind = "own" if second is None else "loaded"
        ins.append((first, ANY))
        columns = a if second is None else second
        tall = first.shape[1] // 8
        outs.append((jax.ShapeDtypeStruct((8, tall, columns.shape[1]), bf16), ANY))
        scratch += [
            pltpu.VMEM((2, length, tall), bf16),
            pltpu.VMEM((2, tall, columns.shape[1]), bf16),
            pltpu.SemaphoreType.DMA((2, 2)),
        ]
        if second is not None:
            ins.append((second, ANY))
            scratch += [pltpu.VMEM(second.shape, bf16), pltpu.SemaphoreType.DMA((1,))]
        flops += 2 * length * first.shape[1] * columns.shape[1]
    return run(
        functools.partial(scatter_kernel, turned, tile, kind), ins, outs, scratch,
        line.pop("number"), (flops, 150 * rows * width * 2, 0), vmem=60, **line,
    )


def tail_kernel(ready, later, ins, outs, scratch, line):
    qkv_ref, gains_ref = ins[:2]
    chunk_refs = dict(zip(ready, ins[2:]))
    gate_ref, up_ref, qkv_rows_ref, gains_out_ref = outs
    from_group, mine, from_rep, sends, recvs, chunk_sems, local = scratch
    me, rank = other(0, 0, 0), lax.axis_index("rep")
    inner = gate_ref.shape[1] // 8
    part = qkv_ref.shape[-1]
    high = line.outs[later[0]].shape[1]
    barrier = pltpu.get_barrier_semaphore()
    for flip in range(1, 4):
        pl.semaphore_signal(
            barrier, inc=1, device_id={"rep": (rank + flip) % 4}, device_id_type=MESH
        )
    for flip in EVERYONE:
        pl.semaphore_signal(barrier, inc=1, device_id={"grp": other(*flip)}, device_id_type=MESH)
    pl.semaphore_wait(barrier, 10)
    waits, moves = [], Moves(local)
    line.refs["qkv"] = qkv_rows_ref

    def send(kind, number, src, dst, device):
        return pltpu.make_async_remote_copy(
            src_ref=src, dst_ref=dst, send_sem=sends.at[kind, number],
            recv_sem=recvs.at[kind, number], device_id=device, device_id_type=MESH,
        )

    own_qkv = qkv_rows_ref.at[me // 4, :, :, pl.ds(pl.multiple_of((me % 4) * part, part), part)]
    qkv_copies, gain_copies = [], []
    for number, flip in enumerate(EVERYONE):
        target = other(*flip)
        qkv_copies.append(send(0, number, qkv_ref.at[target], own_qkv, {"grp": target}))
        qkv_copies[-1].start()
    moves.later(qkv_ref.at[me], own_qkv)
    line.start()
    for number, flip in enumerate(EVERYONE):
        target = other(*flip)
        gain_copies.append(
            send(1, number, gains_ref.at[target], from_group.at[me], {"grp": target})
        )
        gain_copies[-1].start()
    from_group[me] = gains_ref[me]

    def spread(chunk):
        src = chunk_refs[chunk] if chunk in chunk_refs else line.outs[chunk]
        number = chunk - DOWN
        rows = slice(number * high, (number + 1) * high)
        cols = pl.ds(pl.multiple_of(me * inner, inner), inner)
        for which, dst in enumerate((gate_ref, up_ref)):
            there = dst.at[rows, cols]
            for flip in EVERYONE:
                target = other(*flip)
                pltpu.make_async_remote_copy(
                    src_ref=src.at[target, :, which * inner : (which + 1) * inner], dst_ref=there,
                    send_sem=chunk_sems.at[0, which, number], recv_sem=chunk_sems.at[1, which, number],
                    device_id={"grp": target}, device_id_type=MESH,
                ).start()
            moves.later(src.at[me, :, which * inner : (which + 1) * inner], there)
            seven = dst.at[rows, : 7 * inner]
            waits.append(
                pltpu.make_async_remote_copy(
                    src_ref=seven, dst_ref=seven, send_sem=chunk_sems.at[0, which, number],
                    recv_sem=chunk_sems.at[1, which, number],
                    device_id={"grp": other(0, 0, 1)}, device_id_type=MESH,
                )
            )

    for chunk in ready:
        spread(chunk)
    for one in gain_copies:
        one.wait()
    mine[rank] = sum(from_group[g] for g in range(8))
    rep_copies = []
    for step in range(1, 4):
        target = (rank + step) % 4
        rep_copies.append(
            send(2, step, mine.at[rank], from_rep.at[step], {"rep": target})
        )
        rep_copies[-1].start()
    for step, one in zip(range(1, 4), rep_copies):
        one.wait()
        mine[(rank + 4 - step) % 4] = from_rep[step]
    gains_out_ref[...] = (mine[0] + mine[1]) + (mine[2] + mine[3])
    for number in range(1, line.ticks):
        if line.first + number == CHUNKS - QKV:
            for one in qkv_copies:
                one.wait()
            moves.open.pop(0).wait()
        line.step()
        chunk = line.first + number - 5
        if chunk in later:
            spread(chunk)
    line.end()
    for one in waits:
        one.wait_send()
        one.wait_recv()
    moves.finish()


def tail(qkv_term, gains, chunks, inner, number, sums, ticks, arrays, picks):
    first = sums.tick
    ready = sorted(chunks)
    later = [c for c in line_slots(first, ticks) if c < DOWN + GATE_UP]
    _, high, width = sums.shape
    wide = jax.ShapeDtypeStruct((GATE_UP * high, 8 * inner), bf16)
    moved = jax.ShapeDtypeStruct((2, 8, 2 * high, width), bf16)
    picks = dict(picks)
    for n in range(QKV):
        picks[CHUNKS - QKV + n] = (
            "qkv",
            lambda ref, n=n: ref.at[n // 2, :, (n % 2) * high : (n % 2 + 1) * high, :],
        )
    return run(
        functools.partial(tail_kernel, ready, later),
        [(qkv_term, ANY), (gains, VMEM)] + [(chunks[c], ANY) for c in ready],
        [(wide, ANY), (wide, ANY), (moved, ANY), (jax.ShapeDtypeStruct(gains.shape[1:], f32), VMEM)],
        [
            pltpu.VMEM(gains.shape, f32),
            pltpu.VMEM((4,) + gains.shape[1:], f32),
            pltpu.VMEM((4,) + gains.shape[1:], f32),
            pltpu.SemaphoreType.DMA((3, 7)),
            pltpu.SemaphoreType.DMA((3, 7)),
            pltpu.SemaphoreType.DMA((2, 2, GATE_UP)),
            pltpu.SemaphoreType.DMA((1 + 2 * GATE_UP,)),
        ],
        number, (0, 200 * 8 * high * width * 2, 0), sums=sums, ticks=ticks, arrays=arrays, picks=picks,
    )


def finish_kernel(heads, *refs):
    chunks, rest = refs[: DOWN + OUT + QKV], refs[DOWN + OUT + QKV :]
    gate_rows, up_rows = rest[:2]
    query, key, value, out, gate, up, down = rest[2:9]
    low, wide, load_sems, store_sems = rest[9:]
    _, high, width = chunks[0].shape
    depth = low.shape[0]

    def half(number):
        return slice(number * high, (number + 1) * high)

    whole = slice(0, width)
    jobs = [(ref, [(whole, down.at[number])]) for number, ref in enumerate(chunks[:DOWN])]
    for ref, into in ((gate_rows, gate), (up_rows, up)):
        for low_col in range(0, ref.shape[2], width):
            cols = slice(low_col, low_col + width)
            for number in (0, 1):
                where = (slice(None), half(number), cols)
                jobs.append((ref.at[where], [(whole, into.at[where])]))
    for number, ref in enumerate(chunks[DOWN : DOWN + OUT]):
        jobs.append((ref, [(whole, out.at[:, half(number), :])]))
    part = (heads + 2) * HD
    for number, ref in enumerate(chunks[DOWN + OUT :]):
        stores = []
        for place in range(width // part):
            at, device = place * part, (number // 2) * (width // part) + place
            for into, first, size in (
                (query, 0, heads * HD), (key, heads * HD, HD), (value, (heads + 1) * HD, HD)
            ):
                there = into.at[:, half(number % 2), device * size : (device + 1) * size]
                stores.append((slice(at + first, at + first + size), there))
        jobs.append((ref, stores))

    def load(number):
        at = number % depth
        return pltpu.make_async_copy(jobs[number][0], low.at[at], load_sems.at[at])

    def stores(number):
        at = number % depth
        return [
            pltpu.make_async_copy(wide.at[at, :, :, cols], into, store_sems.at[at, which])
            for which, (cols, into) in enumerate(jobs[number][1])
        ]

    for number in range(depth - 1):
        load(number).start()
    for number in range(len(jobs)):
        if number + depth - 1 < len(jobs):
            load(number + depth - 1).start()
        load(number).wait()
        if number >= depth:
            for one in stores(number - depth):
                one.wait()

        def cast(g, _, at=number % depth):
            wide[at, g] = low[at, g].astype(f32)
            return 0

        lax.fori_loop(0, low.shape[1], cast, 0)
        for one in stores(number):
            one.start()
    for number in range(len(jobs) - depth, len(jobs)):
        for one in stores(number):
            one.wait()


def finish(chunks, gate_rows, up_rows, heads):
    eight, high, width = chunks[0].shape
    rows, wide = gate_rows.shape

    def split(columns):
        return jax.ShapeDtypeStruct((eight, rows // eight, columns), f32)

    shapes = [split(columns) for columns in (8 * heads * HD, 8 * HD, 8 * HD, width, wide, wide)]
    shapes.append(jax.ShapeDtypeStruct((DOWN, eight, high, width), f32))
    depth = 4
    results = pl.pallas_call(
        functools.partial(finish_kernel, heads),
        out_shape=tuple(shapes),
        in_specs=[pl.BlockSpec(memory_space=pl.ANY)] * (len(chunks) + 2),
        out_specs=tuple([pl.BlockSpec(memory_space=pl.ANY)] * 7),
        scratch_shapes=[
            pltpu.VMEM((depth, eight, high, width), bf16),
            pltpu.VMEM((depth, eight, high, width), f32),
            pltpu.SemaphoreType.DMA((depth,)),
            pltpu.SemaphoreType.DMA((depth, 12)),
        ],
        compiler_params=pltpu.CompilerParams(vmem_limit_bytes=32 * 2**20),
        cost_estimate=pl.CostEstimate(
            flops=0, bytes_accessed=6 * CHUNKS * eight * high * width, transcendentals=0
        ),
    )(
        *chunks, gate_rows.reshape(eight, rows // eight, wide),
        up_rows.reshape(eight, rows // eight, wide),
    )
    flat = [result.reshape(rows, -1) for result in results[:6]]
    return flat + [results[6].reshape(DOWN * eight * high, width)]


def sum_over_sequences(term):
    return lax.psum(term, "rep").astype(f32)


def on_device(
    layer_input,
    cotangent,
    cut_order,
    piece_ids,
    w_query,
    w_key,
    w_value,
    w_out,
    w_gate,
    w_up,
    w_down,
    gain_attn,
    gain_ffn,
):
    groups = lax.axis_size("grp")
    reps = lax.axis_size("rep")
    own_index = lax.axis_index("grp")
    _, local_rows, model_width = layer_input.shape
    length = piece_ids.shape[1]
    rows_here = w_query.shape[0]
    q_width = w_query.shape[1]
    kv_heads = w_key.shape[1] // HD
    heads = q_width // HD // groups
    copies = groups // kv_heads
    hidden_here = w_down.shape[0]
    piece_col = jnp.broadcast_to(piece_ids.reshape(length, 1), (length, HD))
    cosine, sine = turn_tables(length)

    near = groups == 8 and reps == 4 and copies == 1

    def gather(rows):
        return lax.all_gather(rows, "grp", axis=0, tiled=True)

    def scatter(first, second, turned):
        term = against_rows(first, second) if turned else matmul_f32(first, second)
        return lax.psum_scatter(
            term.astype(bf16), "grp", scatter_dimension=0, tiled=True
        ).astype(f32)

    def to_columns(parts):
        return lax.all_to_all(parts, "grp", 1, 0, tiled=True).reshape(-1, parts.shape[-1])

    def per_group(weight):
        return weight.reshape(rows_here, groups, -1)

    def per_kv_head(weight):
        return jnp.repeat(weight.reshape(rows_here, kv_heads, HD), copies, axis=1)

    x_rows = layer_input.reshape(local_rows, model_width)
    x_flat = x_rows.astype(f32)
    inv_one = lax.rsqrt(jnp.mean(x_flat * x_flat, -1, keepdims=True) + EPS)
    unit_one = x_flat * inv_one
    attn_gain, ffn_gain = gain_attn.reshape(1, -1), gain_ffn.reshape(1, -1)
    if near:
        share = rows_here // (4 * reps) * 3
        spread = columns_of_some((w_gate, w_up), share, 11)
        x_first, spread = lax.optimization_barrier((x_rows, spread))
        spread = lax.all_gather(spread, "rep", axis=0)
        normed_one, cols_qkv = gather_normed(
            x_first, attn_gain, (w_query, w_key, w_value), number=1
        )
        last_gate, last_up, normed_one = lax.optimization_barrier(
            (w_gate[reps * share :], w_up[reps * share :], normed_one)
        )
        rest = to_columns(
            jnp.concatenate(
                [part.reshape(rows_here - reps * share, groups, -1) for part in (last_gate, last_up)],
                -1,
            )
        ).reshape(groups, rows_here - reps * share, -1)
    else:
        normed_one = gather(rms_normed(x_flat, attn_gain).astype(bf16))
        cols_qkv = to_columns(
            jnp.concatenate([per_group(w_query), per_kv_head(w_key), per_kv_head(w_value)], -1)
        )
        cols_gate_up = to_columns(jnp.concatenate([per_group(w_gate), per_group(w_up)], -1))
    qkv = matmul_f32(normed_one, cols_qkv)
    attended, query, key, value, lse, attended_placed = attend(
        cut_order, qkv, cosine, sine, piece_ids, piece_col, heads
    )
    if near:
        out_sum = product_scattered(attended, w_out, False, number=2)[0]
    else:
        out_sum = scatter(attended, w_out, False)
    mid = x_flat + out_sum
    inv_two = lax.rsqrt(jnp.mean(mid * mid, -1, keepdims=True) + EPS)
    unit_two = mid * inv_two
    grad_out = cotangent.reshape(local_rows, model_width)

    def finish_two(grad_two):
        return norm_back(grad_out.astype(f32), grad_two, unit_two, inv_two, gain_ffn)

    def finish_one(grad_mid, grad_one):
        grad_input, gain_term = norm_back(grad_mid, grad_one, unit_one, inv_one, gain_attn)
        return grad_input.astype(bf16).reshape(layer_input.shape), gain_term

    def back_through_attention(grad_attended, **line):
        return attend_back(
            cut_order, grad_attended, attended_placed, query, key, value, lse, cosine, sine,
            piece_ids, piece_col, heads, **line,
        )

    def result_of(down_sum):
        return (mid + down_sum).astype(bf16).reshape(layer_input.shape)

    q_here = heads * HD
    if near:
        normed_two, hidden, up_part, gate_part, cols_gate_up = feed_forward(
            mid, ffn_gain, spread, rest, number=3
        )
        cols_gate_up = cols_gate_up.reshape(model_width, -1)
        grad_gate_up, down_term = feed_forward_back(
            grad_out, w_down, hidden, up_part, gate_part, number=4
        )
        high = rows_here // GATE_UP
        sums = Sums((8, high, model_width))
        terms = {"down": down_term.reshape((DOWN,) + sums.shape)}

        def pick_whole(number):
            return "down", lambda ref: ref.at[number]

        def pick_rows(name, number):
            return name, lambda ref: ref.at[:, number * high : (number + 1) * high, :]

        picks = [pick_whole(n) for n in range(DOWN)]
        picks += [pick_rows("gate_up", n) for n in range(GATE_UP)]
        picks += [pick_rows("out", n) for n in range(OUT)]

        def line(number, ticks):
            names = sorted(
                {picks[t][0] for t in range(sums.tick, sums.tick + ticks) if t < len(picks)}
            )
            return dict(
                number=number, ticks=ticks, sums=sums, picks=dict(enumerate(picks)),
                arrays=[(name, terms[name]) for name in names],
            )

        down_sum, terms["gate_up"] = product_scattered(
            hidden, w_down, False, extra=(normed_two, grad_gate_up), **line(5, 4)
        )
        result = result_of(down_sum)
        grad_two = product_scattered(grad_gate_up, cols_gate_up, True, **line(6, 5))[0]
        grad_mid, gain_ffn_term = finish_two(grad_two)
        grad_attended, out_term = attended_back(
            grad_mid.astype(bf16), w_out, attended, **line(7, 4)
        )
        terms["out"] = out_term.reshape(8, OUT * high, model_width)
        grad_qkv = back_through_attention(grad_attended, **line(8, 2))
        grad_one, qkv_term = product_scattered(
            grad_qkv, cols_qkv, True, extra=(normed_one, None), **line(9, 4)
        )
        grad_x, gain_attn_term = finish_one(grad_mid, grad_one)
        gains = jnp.stack([gain_attn_term, gain_ffn_term]).reshape(2, groups, rows_here)
        gains = jnp.pad(jnp.moveaxis(gains, 0, 1), ((0, 0), (0, 6), (0, 0)))
        rest = line(10, CHUNKS + 4 - sums.tick)
        gate_rows, up_rows, qkv_rows, own_gains = tail(
            qkv_term.reshape(8, 8, 2 * high, -1), gains,
            {c: sums.done[c] for c in sums.done if c >= DOWN}, hidden_here, **rest,
        )
        straight = [n for n in range(CHUNKS) if n < DOWN or n >= DOWN + GATE_UP]
        weight_grads = finish([sums.done[n] for n in straight], gate_rows, up_rows, heads)
        return (result, grad_x) + tuple(weight_grads) + (own_gains[0], own_gains[1])

    normed_two = gather((unit_two * ffn_gain).astype(bf16))
    grad_all = gather(grad_out)
    gate_up = matmul_f32(normed_two, cols_gate_up)
    gate_proj, up_proj = gate_up[:, :hidden_here], gate_up[:, hidden_here:]
    sigmoid_gate = jax.nn.sigmoid(gate_proj)
    swish = gate_proj * sigmoid_gate
    hidden = (swish * up_proj).astype(bf16)
    gate_part = up_proj * sigmoid_gate * (1.0 + gate_proj * (1.0 - sigmoid_gate))
    down_term = over_tokens(hidden, grad_all).astype(bf16)
    grad_hidden = against_rows(grad_all, w_down)
    grad_gate_up = jnp.concatenate([grad_hidden * gate_part, grad_hidden * swish], 1).astype(bf16)
    grad_mid, gain_ffn_term = finish_two(scatter(grad_gate_up, cols_gate_up, True))
    grad_mid_low = gather(grad_mid.astype(bf16))
    grad_qkv = back_through_attention(against_rows(grad_mid_low, w_out).astype(bf16))
    grad_x, gain_attn_term = finish_one(grad_mid, scatter(grad_qkv, cols_qkv, True))

    def to_rows(term):
        return lax.all_to_all(
            term.astype(bf16).reshape(groups, rows_here, -1), "grp", 0, 0, tiled=True
        )

    def whole_rows(term):
        return jnp.moveaxis(term, 0, 1).reshape(rows_here, -1)

    def kv_rows(term):
        return jnp.sum(
            jnp.moveaxis(term, 0, 1).reshape(rows_here, kv_heads, copies, HD), 2
        ).reshape(rows_here, -1)

    gate_up_term = sum_over_sequences(to_rows(over_tokens(normed_two, grad_gate_up)))
    out_term = sum_over_sequences(over_tokens(attended, grad_mid_low).astype(bf16))
    qkv_term = sum_over_sequences(to_rows(over_tokens(normed_one, grad_qkv)))
    gain_total = lax.psum(jnp.stack([gain_attn_term, gain_ffn_term]), ("grp", "rep"))
    own_gains = lax.dynamic_slice_in_dim(gain_total, own_index * rows_here, rows_here, 1)
    return (
        result_of(scatter(hidden, w_down, False)),
        grad_x,
        whole_rows(qkv_term[..., :q_here]),
        kv_rows(qkv_term[..., q_here : q_here + HD]),
        kv_rows(qkv_term[..., q_here + HD :]),
        out_term,
        whole_rows(gate_up_term[..., :hidden_here]),
        whole_rows(gate_up_term[..., hidden_here:]),
        sum_over_sequences(down_term),
        own_gains[0],
        own_gains[1],
    )


def solution(mesh):
    tokens, table, rows, whole = P("rep", "grp", None), P("rep", None), P("grp", None), P()
    return jax.shard_map(
        on_device,
        mesh=mesh,
        in_specs=(tokens, tokens, table, table) + (rows,) * 7 + (whole,) * 2,
        out_specs=(tokens, tokens) + (rows,) * 7 + (P("grp"),) * 2,
        check_vma=False,
    )
```

```python
import functools

import jax
import jax.numpy as jnp
import numpy as np
from jax import lax
from jax.experimental import pallas as pl
from jax.experimental.pallas import tpu as pltpu
from jax.sharding import PartitionSpec as P

HD = 128
EPS = 1e-05
ROPE_BASE = 1000000.0
SCORE_SCALE = HD**-0.5
LOG2E = 1.4426950408889634
TO_EXP2 = SCORE_SCALE * LOG2E
NEG = -1e30

MESH = pl.DeviceIdType.MESH
f32 = jnp.float32
bf16 = jnp.bfloat16


def matmul_f32(first, second):
    return jnp.dot(first, second, preferred_element_type=f32)


def against_rows(first, second):
    return lax.dot_general(first, second, (((1,), (1,)), ((), ())), preferred_element_type=f32)


def over_tokens(first, second):
    return lax.dot_general(first, second, (((0,), (0,)), ((), ())), preferred_element_type=f32)


def turn_tables(length):
    half_size = HD // 2
    inverse = np.float32(ROPE_BASE) ** (-(np.arange(half_size, dtype=np.float32) * 2) / HD)
    angles = np.arange(length, dtype=np.float32)[:, None] * inverse.astype(np.float32)
    cosine, sine = np.cos(angles), np.sin(angles)
    tables = np.concatenate([cosine, cosine], -1), np.concatenate([-sine, sine], -1)
    return tuple(jnp.asarray(table.astype(np.float32)) for table in tables)


def norm_back(upstream, grad_normed, unit_rows, inv_root, gain):
    scaled = grad_normed * gain
    center_term = jnp.mean(scaled * unit_rows, -1, keepdims=True)
    return (
        upstream + inv_root * (scaled - unit_rows * center_term),
        jnp.sum(grad_normed * unit_rows, 0),
    )


def fold_lanes(values, op):
    out = values[:, :HD]
    for at in range(HD, values.shape[1], HD):
        out = op(out, values[:, at : at + HD])
    return out


def as_row(column):
    return jnp.broadcast_to(column, (column.shape[0], HD)).T[0:1, :]


def attend_kernel(
    heads, cuts, block,
    order_ref, qkv_ref, cos_ref, sin_ref, piece_ref, piece_col_ref,
    out_ref, q_ref, k_ref, v_ref, lse_ref, placed,
    scores,
):
    length = qkv_ref.shape[0]
    cut = length // cuts
    blocks = length // block

    def place_cut(r, _):
        src = pl.ds(pl.multiple_of(r * cut, cut), cut)
        dst = pl.ds(pl.multiple_of(order_ref[0, r] * cut, cut), cut)
        cosine, sine = cos_ref[dst, :], sin_ref[dst, :]
        for h in range(heads + 1):
            part = qkv_ref[src, h * HD : (h + 1) * HD]
            turned = (part * cosine + pltpu.roll(part, HD // 2, 1) * sine).astype(bf16)
            if h < heads:
                q_ref[h, dst, :] = turned
            else:
                k_ref[dst, :] = turned
        v_ref[dst, :] = qkv_ref[src, (heads + 1) * HD :].astype(bf16)
        return 0

    lax.fori_loop(0, cuts, place_cut, 0)

    def one_block(i, _):
        rows = pl.ds(pl.multiple_of(i * block, block), block)
        query = q_ref[:, rows, :].reshape(heads * block, HD)

        def score(j, high):
            cols = pl.ds(pl.multiple_of(j * block, block), block)
            tile = against_rows(query, k_ref[cols, :])
            scores[j] = tile
            return jnp.maximum(high, fold_lanes(tile, jnp.maximum))

        high = lax.fori_loop(0, i, score, jnp.full((heads * block, HD), NEG, f32))
        tile = against_rows(query, k_ref[rows, :])
        q_at = lax.broadcasted_iota(jnp.int32, (block, block), 0)
        k_at = lax.broadcasted_iota(jnp.int32, (block, block), 1)
        q_piece, k_piece = piece_col_ref[rows, 0:1], piece_ref[0:1, rows]
        allowed = (k_at <= q_at) | ((q_piece != 0) & (q_piece == k_piece))
        tile = jnp.concatenate(
            [jnp.where(allowed, tile[h * block : (h + 1) * block], NEG) for h in range(heads)], 0
        )
        scores[i] = tile
        high = jnp.max(jnp.maximum(high, fold_lanes(tile, jnp.maximum)), 1, keepdims=True)

        def weigh(j, state):
            total, mixed = state
            cols = pl.ds(pl.multiple_of(j * block, block), block)
            prob = jnp.exp2((scores[j] - high) * TO_EXP2)
            total = total + fold_lanes(prob, jnp.add)
            return total, mixed + matmul_f32(prob.astype(bf16), v_ref[cols, :])

        zero = jnp.zeros((heads * block, HD), f32)
        total, mixed = lax.fori_loop(0, i + 1, weigh, (zero, zero))
        total = jnp.sum(total, 1, keepdims=True)
        mixed = (mixed / total).astype(bf16)
        log_total = high * TO_EXP2 + jnp.log2(total)
        for h in range(heads):
            placed[rows, h * HD : (h + 1) * HD] = mixed[h * block : (h + 1) * block]
            lse_ref[h : h + 1, rows] = as_row(log_total[h * block : (h + 1) * block])
        return 0

    lax.fori_loop(0, blocks, one_block, 0)

    def store_cut(r, _):
        dst = pl.ds(pl.multiple_of(r * cut, cut), cut)
        src = pl.ds(pl.multiple_of(order_ref[0, r] * cut, cut), cut)
        out_ref[dst, :] = placed[src, :]
        return 0

    lax.fori_loop(0, cuts, store_cut, 0)


def vmem_specs(count):
    return [pl.BlockSpec(memory_space=pltpu.VMEM)] * count


def attend(order, qkv, cosine, sine, piece, piece_col, heads):
    length = qkv.shape[0]
    block = min(512, length)
    return pl.pallas_call(
        functools.partial(attend_kernel, heads, order.shape[1], block),
        out_shape=(
            jax.ShapeDtypeStruct((length, heads * HD), bf16),
            jax.ShapeDtypeStruct((heads, length, HD), bf16),
            jax.ShapeDtypeStruct((length, HD), bf16),
            jax.ShapeDtypeStruct((length, HD), bf16),
            jax.ShapeDtypeStruct((heads, length), f32),
            jax.ShapeDtypeStruct((length, heads * HD), bf16),
        ),
        in_specs=[pl.BlockSpec(memory_space=pltpu.SMEM)] + vmem_specs(5),
        out_specs=tuple(vmem_specs(6)),
        scratch_shapes=[pltpu.VMEM((length // block, heads * block, block), f32)],
        compiler_params=pltpu.CompilerParams(vmem_limit_bytes=60 * 2**20),
        cost_estimate=pl.CostEstimate(
            flops=3 * heads * length * length * HD, bytes_accessed=10 * length * HD * heads * 4,
            transcendentals=heads * length * length // 2,
        ),
    )(order, qkv, cosine, sine, piece, piece_col)


DOWN, GATE_UP, OUT, QKV = 8, 16, 2, 4
CHUNKS = DOWN + GATE_UP + OUT + QKV


def is_chunk(number):
    return 0 <= number < CHUNKS


def is_middle():
    rank = lax.axis_index("rep")
    return (rank == 1) | (rank == 2)


def is_end():
    rank = lax.axis_index("rep")
    return (rank == 0) | (rank == 3)


class NoLine:
    ticks = 0

    def signal(self, barrier):
        pass

    def greet(self, barrier, others):
        if others:
            pl.semaphore_wait(barrier, others)

    def start(self):
        pass

    def step(self):
        pass

    def end(self):
        pass


class Line:
    def __init__(self, first, ticks, picks, refs, outs, scratch):
        self.first, self.ticks, self.picks, self.refs, self.outs = first, ticks, picks, refs, outs
        (
            self.inward, self.across, self.own, self.pair, self.total, self.sems, self.local,
            self.carries,
        ) = scratch
        rank = lax.axis_index("rep")
        self.partner = {"rep": rank + 1 - 2 * (rank % 2)}
        self.peer = {"rep": 3 - rank}
        self.now = 0
        self.kept = []

    def signal(self, barrier):
        pl.semaphore_signal(barrier, inc=1, device_id=self.partner, device_id_type=MESH)

        @pl.when(is_middle())
        def _():
            pl.semaphore_signal(barrier, inc=1, device_id=self.peer, device_id_type=MESH)

    def greet(self, barrier, others):
        @pl.when(is_middle())
        def _():
            pl.semaphore_wait(barrier, others + 2)

        @pl.when(is_end())
        def _():
            pl.semaphore_wait(barrier, others + 1)

    def remote(self, hop, number, src, dst, device):
        return pltpu.make_async_remote_copy(
            src_ref=src, dst_ref=dst, send_sem=self.sems.at[0, hop, number],
            recv_sem=self.sems.at[1, hop, number], device_id=device, device_id_type=MESH,
        )

    def hops(self, number):
        tick = self.first + number
        term = pair = total = None
        if is_chunk(tick):
            which, pick = self.picks[tick]
            term = (
                lambda: self.remote(
                    0, number, pick(self.refs[which]), self.inward.at[number], self.partner
                ),
                lambda: pltpu.make_async_copy(
                    pick(self.refs[which]), self.own.at[tick % 2], self.local.at[0, number]
                ),
            )
        if is_chunk(tick - 2):
            before = self.refs[f"pair{number}"] if number < 2 else self.pair.at[(tick - 2) % 3]
            pair = (
                lambda: self.remote(1, number, before, self.across.at[number], self.peer),
                lambda: pltpu.make_async_copy(
                    before, self.pair.at[(tick - 2) % 3], self.carries.at[number]
                ),
            )
        if is_chunk(tick - 4):
            done = self.refs[f"total{number}"] if number < 2 else self.total.at[(tick - 4) % 3]
            slot = self.outs[tick - 4]
            total = (
                lambda: self.remote(2, number, done, slot, self.partner),
                lambda: pltpu.make_async_copy(done, slot, self.local.at[1, number]),
            )
        return term, pair, total

    def open(self, number):
        term, pair, total = self.hops(number)

        @pl.when(is_end())
        def _():
            if term:
                term[0]().start()

        @pl.when(is_middle())
        def _():
            if pair:
                pair[0]().start()
            if total:
                total[0]().start()
            if term:
                term[1]().start()
            if total:
                total[1]().start()
            if pair and number < 2:
                pair[1]().start()

    def close(self, number):
        term, pair, total = self.hops(number)

        @pl.when(is_end())
        def _():
            if term:
                term[0]().wait_send()
            if total:
                total[0]().wait_recv()

        @pl.when(is_middle())
        def _():
            if total:
                total[0]().wait_send()
                total[1]().wait()
            if pair:
                pair[0]().wait_send()
                pair[0]().wait_recv()
            if term:
                term[0]().wait_recv()

    def add(self, number):
        term, pair, _ = self.hops(number)
        tick = self.first + number

        def sum_of(into, first, second):
            def one(g, _):
                into[g] = (first[g].astype(f32) + second[g].astype(f32)).astype(bf16)
                return 0

            lax.fori_loop(0, into.shape[0], one, 0)

        @pl.when(is_middle())
        def _():
            if pair:
                if number < 2:
                    pair[1]().wait()
                sum_of(
                    self.total.at[(tick - 2) % 3], self.pair.at[(tick - 2) % 3],
                    self.across.at[number],
                )
            if term:
                term[1]().wait()
                sum_of(self.pair.at[tick % 3], self.own.at[tick % 2], self.inward.at[number])

    def keep(self, number):
        tick = self.first + number
        which = number - (self.ticks - 2)
        made = []
        if is_chunk(tick):
            made.append((self.pair.at[tick % 3], self.outs[f"pair{which}"], 2 + which))
        if is_chunk(tick - 2):
            made.append((self.total.at[(tick - 2) % 3], self.outs[f"total{which}"], 4 + which))
        copies = [
            lambda src=src, dst=dst, at=at: pltpu.make_async_copy(src, dst, self.carries.at[at])
            for src, dst, at in made
        ]

        @pl.when(is_middle())
        def _():
            for copy in copies:
                copy().start()

        self.kept += copies

    def start(self):
        self.open(0)
        if self.ticks > 1:
            self.open(1)

    def step(self):
        if self.now + 2 < self.ticks:
            self.settle()
            self.open(self.now + 1)

    def settle(self):
        self.close(self.now)
        self.add(self.now)
        if self.now >= self.ticks - 2:
            self.keep(self.now)
        self.now += 1

    def end(self):
        while self.now + 2 < self.ticks:
            self.step()
        while self.now < self.ticks:
            self.settle()

        @pl.when(is_middle())
        def _():
            for copy in self.kept:
                copy().wait()


def line_slots(first, ticks):
    return [t - 4 for t in range(first, first + ticks) if is_chunk(t - 4)]


class Sums:
    def __init__(self, shape):
        self.shape, self.tick, self.kept, self.done = shape, 0, {}, {}


def run(kernel, ins, outs, scratch, number, cost, sums=None, ticks=0, arrays=(), picks=None, vmem=58):
    ins, outs, scratch = list(ins), list(outs), list(scratch)
    counts = (len(ins), len(outs), len(scratch))
    first = sums.tick if ticks else 0
    names_in, names_out = [], []
    if ticks:
        last = first + ticks - 1
        chunk = jax.ShapeDtypeStruct(sums.shape, bf16)
        for name, array in arrays:
            names_in.append(name)
            ins.append((array, pl.ANY))
        for which in (0, 1):
            for name, chunk_at in ((f"pair{which}", first - 2), (f"total{which}", first - 4)):
                if is_chunk(chunk_at + which):
                    names_in.append(name)
                    ins.append((sums.kept[name], pl.ANY))
        names_out = line_slots(first, ticks)
        for which in (0, 1):
            for name, chunk_at in ((f"pair{which}", last - 1), (f"total{which}", last - 3)):
                if is_chunk(chunk_at + which):
                    names_out.append(name)
        outs += [(chunk, pl.ANY)] * len(names_out)
        scratch += [
            pltpu.VMEM((ticks,) + sums.shape, bf16),
            pltpu.VMEM((ticks,) + sums.shape, bf16),
            pltpu.VMEM((2,) + sums.shape, bf16),
            pltpu.VMEM((3,) + sums.shape, bf16),
            pltpu.VMEM((3,) + sums.shape, bf16),
            pltpu.SemaphoreType.DMA((2, 3, ticks)),
            pltpu.SemaphoreType.DMA((2, ticks)),
            pltpu.SemaphoreType.DMA((6,)),
        ]

    def body(*refs):
        in_refs, rest = refs[: len(ins)], refs[len(ins) :]
        out_refs, scratch_refs = rest[: len(outs)], rest[len(outs) :]
        line = NoLine()
        if ticks:
            line = Line(
                first, ticks, picks, dict(zip(names_in, in_refs[counts[0] :])),
                dict(zip(names_out, out_refs[counts[1] :])), scratch_refs[counts[2] :],
            )
        kernel(in_refs[: counts[0]], out_refs[: counts[1]], scratch_refs[: counts[2]], line)

    results = pl.pallas_call(
        body,
        out_shape=tuple(shape for shape, _ in outs),
        in_specs=[pl.BlockSpec(memory_space=space) for _, space in ins],
        out_specs=tuple(pl.BlockSpec(memory_space=space) for _, space in outs),
        scratch_shapes=scratch,
        compiler_params=pltpu.CompilerParams(
            vmem_limit_bytes=vmem * 2**20,
            **({} if number is None else {"collective_id": number, "has_side_effects": True}),
        ),
        cost_estimate=pl.CostEstimate(
            flops=cost[0], bytes_accessed=cost[1], transcendentals=cost[2]
        ),
    )(*[array for array, _ in ins])
    for name, result in zip(names_out, results[counts[1] :]):
        if name in line_slots(first, ticks):
            sums.done[name] = result
        else:
            sums.kept[name] = result
    if ticks:
        sums.tick += ticks
    return results[: counts[1]]


SMEM, VMEM, ANY = pltpu.SMEM, pltpu.VMEM, pl.ANY


def attend_back_kernel(
    heads, block, ins, outs, scratch, line
):
    grad_ref, out_ref, q_ref, k_ref, v_ref, lse_ref, cos_ref, sin_ref, piece_ref, piece_col_ref = ins
    (grad_qkv_ref,) = outs
    grads, centers, grad_q = scratch
    if line.ticks:
        line.signal(pltpu.get_barrier_semaphore())
        line.greet(pltpu.get_barrier_semaphore(), 0)
        line.start()
    length = grad_ref.shape[0]
    blocks = length // block

    def take_block(i, _):
        rows = pl.ds(pl.multiple_of(i * block, block), block)
        for h in range(heads):
            grad = grad_ref[rows, h * HD : (h + 1) * HD].astype(bf16)
            grads[h, rows, :] = grad
            product = grad.astype(f32) * out_ref[rows, h * HD : (h + 1) * HD].astype(f32)
            centers[h, rows, :] = jnp.broadcast_to(
                jnp.sum(product, 1, keepdims=True), (block, HD)
            )
        return 0

    lax.fori_loop(0, blocks, take_block, 0)
    grad_q[...] = jnp.zeros_like(grad_q)

    def key_block(j, _):
        cols = pl.ds(pl.multiple_of(j * block, block), block)
        key, value = k_ref[cols, :], v_ref[cols, :]

        def one(i, state, diagonal):
            grad_key, grad_value = state
            rows = pl.ds(pl.multiple_of(i * block, block), block)
            for h in range(heads):
                query, grad = q_ref[h, rows, :], grads[h, rows, :]
                log_total = lse_ref[h : h + 1, rows]
                center = centers[h, rows, :].T[0:1, :]
                prob = jnp.exp2(against_rows(key, query) * TO_EXP2 - log_total)
                if diagonal:
                    k_at = lax.broadcasted_iota(jnp.int32, (block, block), 0)
                    q_at = lax.broadcasted_iota(jnp.int32, (block, block), 1)
                    k_piece, q_piece = piece_col_ref[cols, 0:1], piece_ref[0:1, cols]
                    allowed = (k_at <= q_at) | ((q_piece != 0) & (q_piece == k_piece))
                    prob = jnp.where(allowed, prob, 0.0)
                grad_prob = against_rows(value, grad)
                grad_score = (prob * (grad_prob - center)).astype(bf16)
                grad_value = grad_value + matmul_f32(prob.astype(bf16), grad)
                grad_key = grad_key + matmul_f32(grad_score, query)
                grad_q[h, rows, :] += over_tokens(grad_score, key)
            return grad_key, grad_value

        zero = jnp.zeros((block, HD), f32)
        state = one(j, (zero, zero), True)
        grad_key, grad_value = lax.fori_loop(
            j + 1, blocks, functools.partial(one, diagonal=False), state
        )
        grad_key = grad_key * SCORE_SCALE
        grad_key = grad_key * cos_ref[cols, :] - pltpu.roll(grad_key, HD // 2, 1) * sin_ref[cols, :]
        grad_qkv_ref[cols, heads * HD : (heads + 1) * HD] = grad_key.astype(bf16)
        grad_qkv_ref[cols, (heads + 1) * HD :] = grad_value.astype(bf16)
        return 0

    for j in range(min(2, blocks - 1)):
        lax.fori_loop(j, j + 1, key_block, 0)
        line.step()
    lax.fori_loop(min(2, blocks - 1), blocks, key_block, 0)

    def turn_back(i, _):
        rows = pl.ds(pl.multiple_of(i * block, block), block)
        for h in range(heads):
            grad = grad_q[h, rows, :] * SCORE_SCALE
            grad = grad * cos_ref[rows, :] - pltpu.roll(grad, HD // 2, 1) * sin_ref[rows, :]
            grad_qkv_ref[rows, h * HD : (h + 1) * HD] = grad.astype(bf16)
        return 0

    lax.fori_loop(0, blocks, turn_back, 0)
    line.end()


def take_cuts_kernel(cuts, holder_ref, rows_ref, out_ref):
    cut = out_ref.shape[0] // cuts

    def one(p, _):
        src = pl.ds(pl.multiple_of(holder_ref[0, p] * cut, cut), cut)
        out_ref[pl.ds(pl.multiple_of(p * cut, cut), cut), :] = rows_ref[src, :]
        return 0

    lax.fori_loop(0, cuts, one, 0)


def take_cuts(holder, rows):
    return pl.pallas_call(
        functools.partial(take_cuts_kernel, holder.shape[1]),
        out_shape=jax.ShapeDtypeStruct(rows.shape, rows.dtype),
        in_specs=[pl.BlockSpec(memory_space=pltpu.SMEM)] + vmem_specs(1),
        out_specs=pl.BlockSpec(memory_space=pltpu.VMEM),
        cost_estimate=pl.CostEstimate(
            flops=0, bytes_accessed=2 * rows.size * rows.dtype.itemsize, transcendentals=0
        ),
    )(holder, rows)


def attend_back(
    order, grad, out, query, key, value, lse, cosine, sine, piece, piece_col, heads, **line
):
    cuts = jnp.arange(order.shape[1], dtype=order.dtype)
    holder = jnp.sum(jnp.where(order[0][None, :] == cuts[:, None], cuts[None, :], 0), 1)[None, :]
    length = grad.shape[0]
    block = min(512, length)
    tall = [take_cuts(holder, grad), out, query, key, value, lse, cosine, sine, piece, piece_col]
    grad_qkv = run(
        functools.partial(attend_back_kernel, heads, block),
        [(array, VMEM) for array in tall],
        [(jax.ShapeDtypeStruct((length, (heads + 2) * HD), bf16), VMEM)],
        [
            pltpu.VMEM((heads, length, HD), bf16),
            pltpu.VMEM((heads, length, HD), f32),
            pltpu.VMEM((heads, length, HD), f32),
        ],
        line.pop("number", None),
        (8 * heads * length * length * HD, 14 * length * HD * heads * 4, heads * length * length // 2),
        **line,
    )[0]
    return take_cuts(order, grad_qkv)


def place_in_group():
    me = lax.axis_index("grp")
    return me // 4, (me // 2) % 2, me % 2


def other(flip_y, flip_x, flip_core):
    y, x, core = place_in_group()
    return ((y + flip_y) % 2) * 4 + ((x + flip_x) % 2) * 2 + (core + flip_core) % 2


def chip_rows(flip_y, flip_x, rows):
    y, x, _ = place_in_group()
    first = (((y + flip_y) % 2) * 2 + (x + flip_x) % 2) * (2 * rows)
    return pl.ds(pl.multiple_of(first, 2 * rows), 2 * rows)


NEIGHBOURS = ((0, 0, 1), (0, 1, 0), (1, 0, 0))
EVERYONE = tuple((n // 4, (n // 2) % 2, n % 2) for n in range(1, 8))


def greet_group(line, flips=NEIGHBOURS, between=None):
    barrier = pltpu.get_barrier_semaphore()
    for flip in flips:
        pl.semaphore_signal(barrier, inc=1, device_id={"grp": other(*flip)}, device_id_type=MESH)
    line.signal(barrier)
    if between:
        between()
    line.greet(barrier, len(flips))


SIBLING, ALONG_X, ALONG_Y, ACROSS = (0, 0), (0, 1), (1, 0), (1, 1)


def gather_rows(rows, all_ref, sends, recvs, on_chip, line, then=None):
    half = rows // 2

    def block(chip, core, part=None):
        first = other(*chip, core) * rows
        if part is None:
            return pl.ds(pl.multiple_of(first, rows), rows)
        return pl.ds(pl.multiple_of(first + part * half, half), half)

    def copy(number, chip, core, part, target):
        where = all_ref.at[block(chip, core, part), :]
        return pltpu.make_async_remote_copy(
            src_ref=where, dst_ref=where, send_sem=sends.at[number], recv_sem=recvs.at[number],
            device_id={"grp": other(*target)}, device_id_type=MESH,
        )

    def landed(number, chip, core, part):
        where = all_ref.at[block(chip, core, part), :]
        pltpu.make_async_remote_copy(
            src_ref=where, dst_ref=where, send_sem=sends.at[number], recv_sem=recvs.at[number],
            device_id={"grp": other(0, 0, 1)}, device_id_type=MESH,
        ).wait_recv()

    to_s, to_x, to_y = (0, 0, 1), (0, 1, 0), (1, 0, 0)
    started = []

    def send(*what):
        one = copy(*what)
        one.start()
        started.append(one)

    send(1, SIBLING, 0, 1, to_x)
    send(3, SIBLING, 0, 0, to_y)
    send(0, SIBLING, 0, None, to_s)
    send(2, SIBLING, 0, 0, to_x)
    send(4, SIBLING, 0, 1, to_y)
    if then:
        then()
    landed(0, SIBLING, 1, None)
    on_chip(*SIBLING)
    landed(1, ALONG_X, 0, 1)
    send(6, ALONG_X, 0, 1, to_y)
    landed(3, ALONG_Y, 0, 0)
    send(5, ALONG_Y, 0, 0, to_x)
    send(7, ALONG_X, 0, 1, to_s)
    send(8, ALONG_Y, 0, 0, to_s)
    line.step()
    landed(2, ALONG_X, 0, 0)
    send(9, ALONG_X, 0, 0, to_s)
    landed(4, ALONG_Y, 0, 1)
    send(10, ALONG_Y, 0, 1, to_s)
    line.step()
    landed(7, ALONG_X, 1, 1)
    landed(9, ALONG_X, 1, 0)
    on_chip(*ALONG_X)
    landed(5, ACROSS, 0, 0)
    send(11, ACROSS, 0, 0, to_s)
    landed(6, ACROSS, 0, 1)
    send(12, ACROSS, 0, 1, to_s)
    line.step()
    landed(8, ALONG_Y, 1, 0)
    landed(10, ALONG_Y, 1, 1)
    on_chip(*ALONG_Y)
    landed(11, ACROSS, 1, 0)
    landed(12, ACROSS, 1, 1)
    on_chip(*ACROSS)
    for one in started:
        one.wait_send()
    line.end()


GATHER_COPIES = 13


def rms_normed(values, gain):
    return values * lax.rsqrt(jnp.mean(values * values, -1, keepdims=True) + EPS) * gain


class Moves:
    def __init__(self, sems):
        self.sems, self.count, self.open = sems, 0, []

    def start(self, src, dst):
        one = pltpu.make_async_copy(src, dst, self.sems.at[self.count])
        self.count += 1
        one.start()
        return one

    def later(self, src, dst):
        self.open.append(self.start(src, dst))

    def finish(self):
        for one in self.open:
            one.wait()


def gather_scratch(rows, width, moves):
    return [
        pltpu.VMEM((8 * rows, width), bf16),
        pltpu.SemaphoreType.DMA((GATHER_COPIES,)),
        pltpu.SemaphoreType.DMA((GATHER_COPIES,)),
        pltpu.SemaphoreType.DMA((moves,)),
    ]


def own_rows(rows):
    return pl.ds(pl.multiple_of(other(0, 0, 0) * rows, rows), rows)


def send_columns(pieces, sends, recvs, moves):
    copies = []
    for which, (rows_ref, width, there) in enumerate(pieces):
        for number, flip in enumerate(EVERYONE):
            target = other(*flip)
            cols = pl.ds(pl.multiple_of(target * width, width), width)
            one = pltpu.make_async_remote_copy(
                src_ref=rows_ref.at[:, cols], dst_ref=there,
                send_sem=sends.at[which, number], recv_sem=recvs.at[which, number],
                device_id={"grp": target}, device_id_type=MESH,
            )
            one.start()
            copies.append(one)
        mine = pl.ds(pl.multiple_of(other(0, 0, 0) * width, width), width)
        moves.later(rows_ref.at[:, mine], there)
    return copies


def gather_normed_kernel(ins, outs, scratch, line):
    x_ref, gain_ref = ins[:2]
    weights = ins[2:]
    all_ref, cols_ref = outs
    held, sends, recvs, sems, col_sends, col_recvs = scratch
    rows = x_ref.shape[0]
    moves = Moves(sems)

    def fill():
        held[own_rows(rows), :] = rms_normed(x_ref[...].astype(f32), gain_ref[...]).astype(bf16)

    greet_group(line, EVERYONE, fill)
    col_copies = []

    def send_weights():
        pieces, low = [], 0
        tall = weights[0].shape[0]
        there = pl.ds(pl.multiple_of(other(0, 0, 0) * tall, tall), tall)
        for weight in weights:
            width = weight.shape[1] // 8
            pieces.append((weight, width, cols_ref.at[there, low : low + width]))
            low += width
        col_copies.extend(send_columns(pieces, col_sends, col_recvs, moves))

    def on_chip(*chip):
        where = chip_rows(*chip, rows)
        moves.later(held.at[where, :], all_ref.at[where, :])

    gather_rows(rows, held, sends, recvs, on_chip, line, send_weights)
    for one in col_copies:
        one.wait()
    moves.finish()


def gather_normed(x, gain, weights, **line):
    rows, width = x.shape
    deep = sum(weight.shape[1] for weight in weights) // 8
    return run(
        gather_normed_kernel,
        [(x, VMEM), (gain, VMEM)] + [(weight, ANY) for weight in weights],
        [
            (jax.ShapeDtypeStruct((8 * rows, width), bf16), ANY),
            (jax.ShapeDtypeStruct((8 * weights[0].shape[0], deep), bf16), ANY),
        ],
        gather_scratch(rows, width, 4 + len(weights))
        + [pltpu.SemaphoreType.DMA((len(weights), 7))] * 2,
        line.pop("number"),
        (0, 150 * rows * width * 2, 0),
        **line,
    )


def columns_kernel(rows_here, ins, outs, scratch, line):
    (cols_ref,) = outs
    sends, recvs, sems = scratch
    moves = Moves(sems)
    barrier = pltpu.get_barrier_semaphore()
    for flip in EVERYONE:
        pl.semaphore_signal(barrier, inc=1, device_id={"grp": other(*flip)}, device_id_type=MESH)
    pl.semaphore_wait(barrier, 7)
    first = pl.multiple_of(lax.axis_index("rep") * rows_here, rows_here)
    me = other(0, 0, 0)
    pieces, low = [], 0
    for weight in ins:
        width = weight.shape[1] // 8
        pieces.append(
            (weight.at[pl.ds(first, rows_here), :], width, cols_ref.at[me, :, low : low + width])
        )
        low += width
    for one in send_columns(pieces, sends, recvs, moves):
        one.wait()
    moves.finish()


def columns_of_some(weights, rows_here, number):
    deep = sum(weight.shape[1] for weight in weights) // 8
    return run(
        functools.partial(columns_kernel, rows_here),
        [(weight, ANY) for weight in weights],
        [(jax.ShapeDtypeStruct((8, rows_here, deep), bf16), ANY)],
        [pltpu.SemaphoreType.DMA((len(weights), 7))] * 2
        + [pltpu.SemaphoreType.DMA((len(weights),))],
        number, (0, 50 * 8 * rows_here * deep, 0),
    )[0]


def feed_forward_kernel(tile, ins, outs, scratch, line):
    mid_ref, gain_ref, spread_ref, rest_ref = ins
    all_ref, hidden_ref, up_part_ref, gate_part_ref, whole_ref = outs
    held, sends, recvs, sems, weight, hidden, up_part, gate_part = scratch
    rows = mid_ref.shape[0]
    inner = hidden.shape[1]
    moves = Moves(sems)
    planes, _, tall, deep = spread_ref.shape
    loads = [
        moves.start(spread_ref.at[z], weight.at[:, z * tall : (z + 1) * tall, :])
        for z in range(planes)
    ]
    loads.append(moves.start(rest_ref, weight.at[:, planes * tall :, :]))

    def fill():
        held[own_rows(rows), :] = rms_normed(mid_ref[...], gain_ref[...]).astype(bf16)

    greet_group(line, between=fill)

    def on_chip(*chip):
        where = chip_rows(*chip, rows)
        moves.later(held.at[where, :], all_ref.at[where, :])
        if chip == SIBLING:
            for one in loads:
                one.wait()
            moves.later(weight, whole_ref)

        def column(t, _):
            cols = pl.ds(pl.multiple_of(t * tile, tile), tile)
            up_cols = pl.ds(pl.multiple_of(inner + t * tile, tile), tile)
            lhs = held[where, :]
            gate = matmul_f32(lhs, weight[:, :, cols].reshape(-1, tile))
            up = matmul_f32(lhs, weight[:, :, up_cols].reshape(-1, tile))
            sigma = 1.0 / (1.0 + jnp.exp(-gate))
            swish = gate * sigma
            hidden[where, cols] = (swish * up).astype(bf16)
            up_part[where, cols] = swish.astype(bf16)
            gate_part[where, cols] = (up * sigma * (1.0 + gate * (1.0 - sigma))).astype(bf16)
            return 0

        lax.fori_loop(0, inner // tile, column, 0)
        for src, dst in ((hidden, hidden_ref), (up_part, up_part_ref), (gate_part, gate_part_ref)):
            moves.later(src.at[where, :], dst.at[where, :])

    gather_rows(rows, held, sends, recvs, on_chip, line)
    moves.finish()


def feed_forward(mid, gain, spread, rest, **line):
    rows, width = mid.shape
    inner = rest.shape[2] // 2
    weight = (8, width // 8, 2 * inner)
    tall = jax.ShapeDtypeStruct((8 * rows, inner), bf16)
    return run(
        functools.partial(feed_forward_kernel, min(256, inner)),
        [(mid, VMEM), (gain, VMEM), (spread, ANY), (rest, ANY)],
        [(jax.ShapeDtypeStruct((8 * rows, width), bf16), ANY)]
        + [(tall, ANY)] * 3
        + [(jax.ShapeDtypeStruct(weight, bf16), ANY)],
        gather_scratch(rows, width, 22)
        + [pltpu.VMEM(weight, bf16)]
        + [pltpu.VMEM((8 * rows, inner), bf16)] * 3,
        line.pop("number"),
        (32 * rows * width * inner, 150 * rows * width * 2, 8 * rows * inner),
        **line,
    )


def feed_forward_back_kernel(tile, ins, outs, scratch, line):
    grad_ref, w_ref, hidden_ref, up_part_ref, gate_part_ref = ins
    grad_gate_up_ref, down_ref = outs
    held, sends, recvs, sems, weight, hidden, up_part, gate_part, grads, down, down_low = scratch
    rows = grad_ref.shape[0]
    inner, width = weight.shape
    moves = Moves(sems)
    loads = [
        moves.start(src, dst)
        for src, dst in (
            (w_ref, weight), (hidden_ref, hidden), (up_part_ref, up_part), (gate_part_ref, gate_part)
        )
    ]
    greet_group(line)
    line.start()
    held[own_rows(rows), :] = grad_ref[...]

    def on_chip(*chip):
        where = chip_rows(*chip, rows)
        if chip == SIBLING:
            for one in loads:
                one.wait()

        def column(t, _):
            cols = pl.ds(pl.multiple_of(t * tile, tile), tile)
            up_cols = pl.ds(pl.multiple_of(inner + t * tile, tile), tile)
            incoming = held[where, :]
            grad_hidden = against_rows(incoming, weight[cols, :])
            grads[where, cols] = (grad_hidden * gate_part[where, cols].astype(f32)).astype(bf16)
            grads[where, up_cols] = (grad_hidden * up_part[where, cols].astype(f32)).astype(bf16)
            term = over_tokens(hidden[where, cols], incoming)
            if chip == SIBLING:
                down[cols, :] = term
            elif chip == ACROSS:
                down_low[cols, :] = (down[cols, :] + term).astype(bf16)
            else:
                down[cols, :] += term
            return 0

        lax.fori_loop(0, inner // tile, column, 0)
        moves.later(grads.at[where, :], grad_gate_up_ref.at[where, :])

    gather_rows(rows, held, sends, recvs, on_chip, line)
    moves.later(down_low, down_ref)
    moves.finish()


def feed_forward_back(grad, w_down, hidden, up_part, gate_part, **line):
    rows, width = grad.shape
    inner = w_down.shape[0]
    return run(
        functools.partial(feed_forward_back_kernel, min(256, inner)),
        [(grad, VMEM)] + [(array, ANY) for array in (w_down, hidden, up_part, gate_part)],
        [
            (jax.ShapeDtypeStruct((8 * rows, 2 * inner), bf16), ANY),
            (jax.ShapeDtypeStruct((inner, width), bf16), ANY),
        ],
        gather_scratch(rows, width, 9)
        + [pltpu.VMEM(w_down.shape, bf16)]
        + [pltpu.VMEM((8 * rows, inner), bf16)] * 3
        + [
            pltpu.VMEM((8 * rows, 2 * inner), bf16),
            pltpu.VMEM(w_down.shape, f32),
            pltpu.VMEM(w_down.shape, bf16),
        ],
        line.pop("number"),
        (32 * rows * width * inner, 150 * rows * width * 2, 0),
        vmem=62,
        **line,
    )


def attended_back_kernel(ins, outs, scratch, line):
    grad_ref, w_ref, attended_ref = ins
    grad_attended_ref, out_term_ref = outs
    held, sends, recvs, sems, total = scratch
    rows = grad_ref.shape[0]
    moves = Moves(sems)
    greet_group(line)
    line.start()
    held[own_rows(rows), :] = grad_ref[...]

    def on_chip(*chip):
        where = chip_rows(*chip, rows)
        incoming = held[where, :]
        grad_attended_ref[where, :] = against_rows(incoming, w_ref[...]).astype(bf16)
        term = over_tokens(attended_ref[where, :], incoming)
        if chip == SIBLING:
            total[...] = term
        elif chip == ACROSS:
            out_term_ref[...] = (total[...] + term).astype(bf16)
        else:
            total[...] += term

    gather_rows(rows, held, sends, recvs, on_chip, line)
    moves.finish()


def attended_back(grad, w_out, attended, **line):
    rows, width = grad.shape
    return run(
        attended_back_kernel,
        [(array, VMEM) for array in (grad, w_out, attended)],
        [
            (jax.ShapeDtypeStruct(attended.shape, bf16), VMEM),
            (jax.ShapeDtypeStruct(w_out.shape, bf16), VMEM),
        ],
        gather_scratch(rows, width, 1) + [pltpu.VMEM(w_out.shape, f32)],
        line.pop("number"),
        (32 * rows * width * w_out.shape[0], 150 * rows * width * 2, 0),
        **line,
    )


class WeightTerm:
    def __init__(self, rows_ref, columns_ref, term_ref, scratch):
        self.rows_ref, self.columns_ref, self.term_ref = rows_ref, columns_ref, term_ref
        self.loaded, self.ready, self.sems = scratch
        self.tile = self.loaded.shape[2]
        for number in (0, 1):
            self.load(number).start()

    def load(self, number):
        cols = slice(number * self.tile, (number + 1) * self.tile)
        return pltpu.make_async_copy(
            self.rows_ref.at[:, cols], self.loaded.at[number % 2], self.sems.at[0, number % 2]
        )

    def store(self, number):
        return pltpu.make_async_copy(
            self.ready.at[number % 2], self.term_ref.at[number], self.sems.at[1, number % 2]
        )

    def work(self, numbers):
        for number in numbers:
            at = number % 2
            self.load(number).wait()
            if number >= 2:
                self.store(number - 2).wait()
            width = self.columns_ref.shape[1]
            step = min(256, width)

            def column(t, _):
                cols = pl.ds(pl.multiple_of(t * step, step), step)
                term = over_tokens(self.loaded[at], self.columns_ref[:, cols])
                self.ready[at, :, cols] = term.astype(bf16)
                return 0

            lax.fori_loop(0, width // step, column, 0)
            self.store(number).start()
            if number + 2 < 8:
                self.load(number + 2).start()

    def finish(self):
        for number in (6, 7):
            self.store(number).wait()


def scatter_kernel(turned, tile, extra, ins, outs, scratch, line):
    out_ref = outs[0]
    part, to_s, from_s, to_chip, held, relay, last, sends, recvs = scratch[:9]
    a_ref, b_ref, loads = scratch[-3:]
    loading = [
        pltpu.make_async_copy(src, dst, loads.at[number])
        for number, (src, dst) in enumerate(((ins[1], b_ref), (ins[0], a_ref)))
    ]
    for one in loading:
        one.start()
    rows, width = out_ref.shape
    half = rows // 2
    _, _, core = place_in_group()
    greet_group(line)
    line.start()
    if extra:
        columns_ref = a_ref
        if extra == "loaded":
            columns_ref = scratch[12]
            columns_copy = pltpu.make_async_copy(ins[3], columns_ref, scratch[13].at[0])
            columns_copy.start()
        term = WeightTerm(ins[2], columns_ref, outs[1], scratch[9:12])
    for one in loading:
        one.wait()
    own_at = pl.multiple_of(core * rows, rows)
    other_at = pl.multiple_of((1 - core) * rows, rows)
    started = []

    def send(number, src, dst, target):
        one = pltpu.make_async_remote_copy(
            src_ref=src, dst_ref=dst, send_sem=sends.at[number], recv_sem=recvs.at[number],
            device_id={"grp": other(*target)}, device_id_type=MESH,
        )
        one.start()
        started.append(one)
        return one

    def landed(number, where):
        pltpu.make_async_remote_copy(
            src_ref=where, dst_ref=where, send_sem=sends.at[number], recv_sem=recvs.at[number],
            device_id={"grp": other(0, 0, 1)}, device_id_type=MESH,
        ).wait_recv()

    to_sib, to_x, to_y = (0, 0, 1), (0, 1, 0), (1, 0, 0)

    def make(number, chip):
        where = chip_rows(*chip, rows)

        def column(t, _):
            cols = pl.ds(pl.multiple_of(t * tile, tile), tile)
            lhs = a_ref[where, :]
            if turned:
                part[:, cols] = against_rows(lhs, b_ref[cols, :])
            else:
                part[:, cols] = matmul_f32(lhs, b_ref[:, cols])
            return 0

        lax.fori_loop(0, width // tile, column, 0)
        to_s[number] = part[pl.ds(other_at, rows), :].astype(bf16)
        send(number, to_s.at[number], from_s.at[number], to_sib)

    def own(low, number):
        at = pl.ds(pl.multiple_of(core * rows + low * half, half), half)
        return part[at, :] + from_s[number, low * half : (low + 1) * half, :].astype(f32)

    first, second = slice(0, half), slice(half, rows)
    make(0, ACROSS)
    landed(0, from_s.at[0])
    to_chip[0, first, :] = own(0, 0).astype(bf16)
    send(4, to_chip.at[0, first, :], relay.at[0], to_x)
    to_chip[0, second, :] = own(1, 0).astype(bf16)
    send(5, to_chip.at[0, second, :], relay.at[1], to_y)
    make(1, ALONG_X)
    landed(1, from_s.at[1])
    to_chip[1, first, :] = own(0, 1).astype(bf16)
    send(6, to_chip.at[1, first, :], last.at[0, first, :], to_x)
    held[0] = own(1, 1)
    line.step()
    make(2, ALONG_Y)
    landed(2, from_s.at[2])
    to_chip[2, second, :] = own(1, 2).astype(bf16)
    send(7, to_chip.at[2, second, :], last.at[1, second, :], to_y)
    held[1] = own(0, 2)
    if extra:
        if extra == "loaded":
            columns_copy.wait()
        term.work((0, 1, 2))
    landed(5, relay.at[1])
    to_chip[1, second, :] = (held[0] + relay[1].astype(f32)).astype(bf16)
    send(8, to_chip.at[1, second, :], last.at[0, second, :], to_x)
    landed(4, relay.at[0])
    to_chip[2, first, :] = (held[1] + relay[0].astype(f32)).astype(bf16)
    send(9, to_chip.at[2, first, :], last.at[1, first, :], to_y)
    line.step()
    make(3, SIBLING)
    if extra:
        term.work((3, 4))
        line.step()
        term.work((5, 6, 7))
    landed(3, from_s.at[3])
    for low in (0, 1):
        out_ref[low * half : (low + 1) * half, :] = own(low, 3)
    landed(6, last.at[0, first, :])
    out_ref[first, :] += last[0, first, :].astype(f32)
    landed(7, last.at[1, second, :])
    out_ref[second, :] += last[1, second, :].astype(f32)
    line.step()
    landed(8, last.at[0, second, :])
    out_ref[second, :] += last[0, second, :].astype(f32)
    landed(9, last.at[1, first, :])
    out_ref[first, :] += last[1, first, :].astype(f32)
    for one in started:
        one.wait_send()
    if extra:
        term.finish()
    line.end()


def product_scattered(a, b, turned, extra=None, **line):
    length, depth = a.shape
    width = b.shape[0] if turned else b.shape[1]
    rows = length // 8
    tile = min(256, width)
    ins = [(a, ANY), (b, ANY)]
    outs = [(jax.ShapeDtypeStruct((rows, width), f32), VMEM)]
    scratch = [
        pltpu.VMEM((2 * rows, width), f32),
        pltpu.VMEM((4, rows, width), bf16),
        pltpu.VMEM((4, rows, width), bf16),
        pltpu.VMEM((3, rows, width), bf16),
        pltpu.VMEM((2, rows // 2, width), f32),
        pltpu.VMEM((2, rows // 2, width), bf16),
        pltpu.VMEM((2, rows, width), bf16),
        pltpu.SemaphoreType.DMA((10,)),
        pltpu.SemaphoreType.DMA((10,)),
    ]
    flops, kind = 2 * length * depth * width, None
    if extra:
        first, second = extra
        kind = "own" if second is None else "loaded"
        ins.append((first, ANY))
        columns = a if second is None else second
        tall = first.shape[1] // 8
        outs.append((jax.ShapeDtypeStruct((8, tall, columns.shape[1]), bf16), ANY))
        scratch += [
            pltpu.VMEM((2, length, tall), bf16),
            pltpu.VMEM((2, tall, columns.shape[1]), bf16),
            pltpu.SemaphoreType.DMA((2, 2)),
        ]
        if second is not None:
            ins.append((second, ANY))
            scratch += [pltpu.VMEM(second.shape, bf16), pltpu.SemaphoreType.DMA((1,))]
        flops += 2 * length * first.shape[1] * columns.shape[1]
    scratch += [
        pltpu.VMEM(a.shape, bf16), pltpu.VMEM(b.shape, bf16), pltpu.SemaphoreType.DMA((2,))
    ]
    return run(
        functools.partial(scatter_kernel, turned, tile, kind), ins, outs, scratch,
        line.pop("number"), (flops, 150 * rows * width * 2, 0), vmem=60, **line,
    )


def tail_kernel(ready, later, ins, outs, scratch, line):
    qkv_ref, gains_ref = ins[:2]
    chunk_refs = dict(zip(ready, ins[2:]))
    gate_ref, up_ref, qkv_rows_ref, gains_out_ref = outs
    from_group, mine, from_rep, sends, recvs, chunk_sems, local = scratch
    me, rank = other(0, 0, 0), lax.axis_index("rep")
    inner = gate_ref.shape[1] // 8
    part = qkv_ref.shape[-1]
    high = line.outs[later[0]].shape[1]
    barrier = pltpu.get_barrier_semaphore()
    for flip in range(1, 4):
        pl.semaphore_signal(
            barrier, inc=1, device_id={"rep": (rank + flip) % 4}, device_id_type=MESH
        )
    for flip in EVERYONE:
        pl.semaphore_signal(barrier, inc=1, device_id={"grp": other(*flip)}, device_id_type=MESH)
    pl.semaphore_wait(barrier, 10)
    waits, moves = [], Moves(local)
    line.refs["qkv"] = qkv_rows_ref

    def send(kind, number, src, dst, device):
        return pltpu.make_async_remote_copy(
            src_ref=src, dst_ref=dst, send_sem=sends.at[kind, number],
            recv_sem=recvs.at[kind, number], device_id=device, device_id_type=MESH,
        )

    own_qkv = qkv_rows_ref.at[me // 4, :, :, pl.ds(pl.multiple_of((me % 4) * part, part), part)]
    qkv_copies, gain_copies = [], []
    for number, flip in enumerate(EVERYONE):
        target = other(*flip)
        qkv_copies.append(send(0, number, qkv_ref.at[target], own_qkv, {"grp": target}))
        qkv_copies[-1].start()
    moves.later(qkv_ref.at[me], own_qkv)
    line.start()
    for number, flip in enumerate(EVERYONE):
        target = other(*flip)
        gain_copies.append(
            send(1, number, gains_ref.at[target], from_group.at[me], {"grp": target})
        )
        gain_copies[-1].start()
    from_group[me] = gains_ref[me]

    def spread(chunk):
        src = chunk_refs[chunk] if chunk in chunk_refs else line.outs[chunk]
        number = chunk - DOWN
        rows = slice(number * high, (number + 1) * high)
        cols = pl.ds(pl.multiple_of(me * inner, inner), inner)
        for which, dst in enumerate((gate_ref, up_ref)):
            there = dst.at[rows, cols]
            for flip in EVERYONE:
                target = other(*flip)
                pltpu.make_async_remote_copy(
                    src_ref=src.at[target, :, which * inner : (which + 1) * inner], dst_ref=there,
                    send_sem=chunk_sems.at[0, which, number], recv_sem=chunk_sems.at[1, which, number],
                    device_id={"grp": target}, device_id_type=MESH,
                ).start()
            moves.later(src.at[me, :, which * inner : (which + 1) * inner], there)
            seven = dst.at[rows, : 7 * inner]
            waits.append(
                pltpu.make_async_remote_copy(
                    src_ref=seven, dst_ref=seven, send_sem=chunk_sems.at[0, which, number],
                    recv_sem=chunk_sems.at[1, which, number],
                    device_id={"grp": other(0, 0, 1)}, device_id_type=MESH,
                )
            )

    for chunk in ready:
        spread(chunk)
    for one in gain_copies:
        one.wait()
    mine[rank] = sum(from_group[g] for g in range(8))
    rep_copies = []
    for step in range(1, 4):
        target = (rank + step) % 4
        rep_copies.append(
            send(2, step, mine.at[rank], from_rep.at[step], {"rep": target})
        )
        rep_copies[-1].start()
    for step, one in zip(range(1, 4), rep_copies):
        one.wait()
        mine[(rank + 4 - step) % 4] = from_rep[step]
    gains_out_ref[...] = (mine[0] + mine[1]) + (mine[2] + mine[3])
    for number in range(1, line.ticks):
        if line.first + number + 1 == CHUNKS - QKV:
            for one in qkv_copies:
                one.wait()
            moves.open.pop(0).wait()
        line.step()
        chunk = line.first + number - 5
        if chunk in later:
            spread(chunk)
    line.end()
    for one in waits:
        one.wait_send()
        one.wait_recv()
    moves.finish()


def tail(qkv_term, gains, chunks, inner, number, sums, ticks, arrays, picks):
    first = sums.tick
    ready = sorted(chunks)
    later = [c for c in line_slots(first, ticks) if c < DOWN + GATE_UP]
    _, high, width = sums.shape
    wide = jax.ShapeDtypeStruct((GATE_UP * high, 8 * inner), bf16)
    moved = jax.ShapeDtypeStruct((2, 8, 2 * high, width), bf16)
    picks = dict(picks)
    for n in range(QKV):
        picks[CHUNKS - QKV + n] = (
            "qkv",
            lambda ref, n=n: ref.at[n // 2, :, (n % 2) * high : (n % 2 + 1) * high, :],
        )
    return run(
        functools.partial(tail_kernel, ready, later),
        [(qkv_term, ANY), (gains, VMEM)] + [(chunks[c], ANY) for c in ready],
        [(wide, ANY), (wide, ANY), (moved, ANY), (jax.ShapeDtypeStruct(gains.shape[1:], f32), VMEM)],
        [
            pltpu.VMEM(gains.shape, f32),
            pltpu.VMEM((4,) + gains.shape[1:], f32),
            pltpu.VMEM((4,) + gains.shape[1:], f32),
            pltpu.SemaphoreType.DMA((3, 7)),
            pltpu.SemaphoreType.DMA((3, 7)),
            pltpu.SemaphoreType.DMA((2, 2, GATE_UP)),
            pltpu.SemaphoreType.DMA((1 + 2 * GATE_UP,)),
        ],
        number, (0, 200 * 8 * high * width * 2, 0), sums=sums, ticks=ticks, arrays=arrays, picks=picks,
    )


def finish_kernel(heads, *refs):
    chunks, rest = refs[: DOWN + OUT + QKV], refs[DOWN + OUT + QKV :]
    gate_rows, up_rows = rest[:2]
    query, key, value, out, gate, up, down = rest[2:9]
    low, wide, load_sems, store_sems = rest[9:]
    _, high, width = chunks[0].shape
    depth = low.shape[0]

    def half(number):
        return slice(number * high, (number + 1) * high)

    whole = slice(0, width)
    jobs = [(ref, [(whole, down.at[number])]) for number, ref in enumerate(chunks[:DOWN])]
    for ref, into in ((gate_rows, gate), (up_rows, up)):
        for low_col in range(0, ref.shape[2], width):
            cols = slice(low_col, low_col + width)
            for number in (0, 1):
                where = (slice(None), half(number), cols)
                jobs.append((ref.at[where], [(whole, into.at[where])]))
    for number, ref in enumerate(chunks[DOWN : DOWN + OUT]):
        jobs.append((ref, [(whole, out.at[:, half(number), :])]))
    part = (heads + 2) * HD
    for number, ref in enumerate(chunks[DOWN + OUT :]):
        stores = []
        for place in range(width // part):
            at, device = place * part, (number // 2) * (width // part) + place
            for into, first, size in (
                (query, 0, heads * HD), (key, heads * HD, HD), (value, (heads + 1) * HD, HD)
            ):
                there = into.at[:, half(number % 2), device * size : (device + 1) * size]
                stores.append((slice(at + first, at + first + size), there))
        jobs.append((ref, stores))

    def load(number):
        at = number % depth
        return pltpu.make_async_copy(jobs[number][0], low.at[at], load_sems.at[at])

    def stores(number):
        at = number % depth
        return [
            pltpu.make_async_copy(wide.at[at, :, :, cols], into, store_sems.at[at, which])
            for which, (cols, into) in enumerate(jobs[number][1])
        ]

    for number in range(depth - 1):
        load(number).start()
    for number in range(len(jobs)):
        if number + depth - 1 < len(jobs):
            load(number + depth - 1).start()
        load(number).wait()
        if number >= depth:
            for one in stores(number - depth):
                one.wait()

        def cast(g, _, at=number % depth):
            wide[at, g] = low[at, g].astype(f32)
            return 0

        lax.fori_loop(0, low.shape[1], cast, 0)
        for one in stores(number):
            one.start()
    for number in range(len(jobs) - depth, len(jobs)):
        for one in stores(number):
            one.wait()


def finish(chunks, gate_rows, up_rows, heads):
    eight, high, width = chunks[0].shape
    rows, wide = gate_rows.shape

    def split(columns):
        return jax.ShapeDtypeStruct((eight, rows // eight, columns), f32)

    shapes = [split(columns) for columns in (8 * heads * HD, 8 * HD, 8 * HD, width, wide, wide)]
    shapes.append(jax.ShapeDtypeStruct((DOWN, eight, high, width), f32))
    depth = 4
    results = pl.pallas_call(
        functools.partial(finish_kernel, heads),
        out_shape=tuple(shapes),
        in_specs=[pl.BlockSpec(memory_space=pl.ANY)] * (len(chunks) + 2),
        out_specs=tuple([pl.BlockSpec(memory_space=pl.ANY)] * 7),
        scratch_shapes=[
            pltpu.VMEM((depth, eight, high, width), bf16),
            pltpu.VMEM((depth, eight, high, width), f32),
            pltpu.SemaphoreType.DMA((depth,)),
            pltpu.SemaphoreType.DMA((depth, 12)),
        ],
        compiler_params=pltpu.CompilerParams(vmem_limit_bytes=60 * 2**20),
        cost_estimate=pl.CostEstimate(
            flops=0, bytes_accessed=6 * CHUNKS * eight * high * width, transcendentals=0
        ),
    )(
        *chunks, gate_rows.reshape(eight, rows // eight, wide),
        up_rows.reshape(eight, rows // eight, wide),
    )
    flat = [result.reshape(rows, -1) for result in results[:6]]
    return flat + [results[6].reshape(DOWN * eight * high, width)]


def sum_over_sequences(term):
    return lax.psum(term, "rep").astype(f32)


def on_device(
    layer_input,
    cotangent,
    cut_order,
    piece_ids,
    w_query,
    w_key,
    w_value,
    w_out,
    w_gate,
    w_up,
    w_down,
    gain_attn,
    gain_ffn,
):
    groups = lax.axis_size("grp")
    reps = lax.axis_size("rep")
    own_index = lax.axis_index("grp")
    _, local_rows, model_width = layer_input.shape
    length = piece_ids.shape[1]
    rows_here = w_query.shape[0]
    q_width = w_query.shape[1]
    kv_heads = w_key.shape[1] // HD
    heads = q_width // HD // groups
    copies = groups // kv_heads
    hidden_here = w_down.shape[0]
    piece_col = jnp.broadcast_to(piece_ids.reshape(length, 1), (length, HD))
    cosine, sine = turn_tables(length)

    near = groups == 8 and reps == 4 and copies == 1

    def gather(rows):
        return lax.all_gather(rows, "grp", axis=0, tiled=True)

    def scatter(first, second, turned):
        term = against_rows(first, second) if turned else matmul_f32(first, second)
        return lax.psum_scatter(
            term.astype(bf16), "grp", scatter_dimension=0, tiled=True
        ).astype(f32)

    def to_columns(parts):
        return lax.all_to_all(parts, "grp", 1, 0, tiled=True).reshape(-1, parts.shape[-1])

    def per_group(weight):
        return weight.reshape(rows_here, groups, -1)

    def per_kv_head(weight):
        return jnp.repeat(weight.reshape(rows_here, kv_heads, HD), copies, axis=1)

    x_rows = layer_input.reshape(local_rows, model_width)
    x_flat = x_rows.astype(f32)
    inv_one = lax.rsqrt(jnp.mean(x_flat * x_flat, -1, keepdims=True) + EPS)
    unit_one = x_flat * inv_one
    attn_gain, ffn_gain = gain_attn.reshape(1, -1), gain_ffn.reshape(1, -1)
    if near:
        share = rows_here // (4 * reps) * 3
        spread = columns_of_some((w_gate, w_up), share, 11)
        x_first, spread = lax.optimization_barrier((x_rows, spread))
        spread = lax.all_gather(spread, "rep", axis=0)
        normed_one, cols_qkv = gather_normed(
            x_first, attn_gain, (w_query, w_key, w_value), number=1
        )
        last_gate, last_up, normed_one = lax.optimization_barrier(
            (w_gate[reps * share :], w_up[reps * share :], normed_one)
        )
        rest = to_columns(
            jnp.concatenate(
                [part.reshape(rows_here - reps * share, groups, -1) for part in (last_gate, last_up)],
                -1,
            )
        ).reshape(groups, rows_here - reps * share, -1)
    else:
        normed_one = gather(rms_normed(x_flat, attn_gain).astype(bf16))
        cols_qkv = to_columns(
            jnp.concatenate([per_group(w_query), per_kv_head(w_key), per_kv_head(w_value)], -1)
        )
        cols_gate_up = to_columns(jnp.concatenate([per_group(w_gate), per_group(w_up)], -1))
    qkv = matmul_f32(normed_one, cols_qkv)
    attended, query, key, value, lse, attended_placed = attend(
        cut_order, qkv, cosine, sine, piece_ids, piece_col, heads
    )
    if near:
        out_sum = product_scattered(attended, w_out, False, number=2)[0]
    else:
        out_sum = scatter(attended, w_out, False)
    mid = x_flat + out_sum
    inv_two = lax.rsqrt(jnp.mean(mid * mid, -1, keepdims=True) + EPS)
    unit_two = mid * inv_two
    grad_out = cotangent.reshape(local_rows, model_width)

    def finish_two(grad_two):
        return norm_back(grad_out.astype(f32), grad_two, unit_two, inv_two, gain_ffn)

    def finish_one(grad_mid, grad_one):
        grad_input, gain_term = norm_back(grad_mid, grad_one, unit_one, inv_one, gain_attn)
        return grad_input.astype(bf16).reshape(layer_input.shape), gain_term

    def back_through_attention(grad_attended, **line):
        return attend_back(
            cut_order, grad_attended, attended_placed, query, key, value, lse, cosine, sine,
            piece_ids, piece_col, heads, **line,
        )

    def result_of(down_sum):
        return (mid + down_sum).astype(bf16).reshape(layer_input.shape)

    q_here = heads * HD
    if near:
        normed_two, hidden, up_part, gate_part, cols_gate_up = feed_forward(
            mid, ffn_gain, spread, rest, number=3
        )
        cols_gate_up = cols_gate_up.reshape(model_width, -1)
        grad_gate_up, down_term = feed_forward_back(
            grad_out, w_down, hidden, up_part, gate_part, number=4
        )
        high = rows_here // GATE_UP
        sums = Sums((8, high, model_width))
        terms = {"down": down_term.reshape((DOWN,) + sums.shape)}

        def pick_whole(number):
            return "down", lambda ref: ref.at[number]

        def pick_rows(name, number):
            return name, lambda ref: ref.at[:, number * high : (number + 1) * high, :]

        picks = [pick_whole(n) for n in range(DOWN)]
        picks += [pick_rows("gate_up", n) for n in range(GATE_UP)]
        picks += [pick_rows("out", n) for n in range(OUT)]

        def line(number, ticks):
            names = sorted(
                {picks[t][0] for t in range(sums.tick, sums.tick + ticks) if t < len(picks)}
            )
            return dict(
                number=number, ticks=ticks, sums=sums, picks=dict(enumerate(picks)),
                arrays=[(name, terms[name]) for name in names],
            )

        down_sum, terms["gate_up"] = product_scattered(
            hidden, w_down, False, extra=(normed_two, grad_gate_up), **line(5, 4)
        )
        result = result_of(down_sum)
        grad_two = product_scattered(grad_gate_up, cols_gate_up, True, **line(6, 4))[0]
        grad_mid, gain_ffn_term = finish_two(grad_two)
        grad_attended, out_term = attended_back(
            grad_mid.astype(bf16), w_out, attended, **line(7, 4)
        )
        terms["out"] = out_term.reshape(8, OUT * high, model_width)
        grad_qkv = back_through_attention(grad_attended, **line(8, 2))
        grad_one, qkv_term = product_scattered(
            grad_qkv, cols_qkv, True, extra=(normed_one, None), **line(9, 4)
        )
        grad_x, gain_attn_term = finish_one(grad_mid, grad_one)
        gains = jnp.stack([gain_attn_term, gain_ffn_term]).reshape(2, groups, rows_here)
        gains = jnp.pad(jnp.moveaxis(gains, 0, 1), ((0, 0), (0, 6), (0, 0)))
        rest = line(10, CHUNKS + 4 - sums.tick)
        gate_rows, up_rows, qkv_rows, own_gains = tail(
            qkv_term.reshape(8, 8, 2 * high, -1), gains,
            {c: sums.done[c] for c in sums.done if c >= DOWN}, hidden_here, **rest,
        )
        straight = [n for n in range(CHUNKS) if n < DOWN or n >= DOWN + GATE_UP]
        weight_grads = finish([sums.done[n] for n in straight], gate_rows, up_rows, heads)
        return (result, grad_x) + tuple(weight_grads) + (own_gains[0], own_gains[1])

    normed_two = gather((unit_two * ffn_gain).astype(bf16))
    grad_all = gather(grad_out)
    gate_up = matmul_f32(normed_two, cols_gate_up)
    gate_proj, up_proj = gate_up[:, :hidden_here], gate_up[:, hidden_here:]
    sigmoid_gate = jax.nn.sigmoid(gate_proj)
    swish = gate_proj * sigmoid_gate
    hidden = (swish * up_proj).astype(bf16)
    gate_part = up_proj * sigmoid_gate * (1.0 + gate_proj * (1.0 - sigmoid_gate))
    down_term = over_tokens(hidden, grad_all).astype(bf16)
    grad_hidden = against_rows(grad_all, w_down)
    grad_gate_up = jnp.concatenate([grad_hidden * gate_part, grad_hidden * swish], 1).astype(bf16)
    grad_mid, gain_ffn_term = finish_two(scatter(grad_gate_up, cols_gate_up, True))
    grad_mid_low = gather(grad_mid.astype(bf16))
    grad_qkv = back_through_attention(against_rows(grad_mid_low, w_out).astype(bf16))
    grad_x, gain_attn_term = finish_one(grad_mid, scatter(grad_qkv, cols_qkv, True))

    def to_rows(term):
        return lax.all_to_all(
            term.astype(bf16).reshape(groups, rows_here, -1), "grp", 0, 0, tiled=True
        )

    def whole_rows(term):
        return jnp.moveaxis(term, 0, 1).reshape(rows_here, -1)

    def kv_rows(term):
        return jnp.sum(
            jnp.moveaxis(term, 0, 1).reshape(rows_here, kv_heads, copies, HD), 2
        ).reshape(rows_here, -1)

    gate_up_term = sum_over_sequences(to_rows(over_tokens(normed_two, grad_gate_up)))
    out_term = sum_over_sequences(over_tokens(attended, grad_mid_low).astype(bf16))
    qkv_term = sum_over_sequences(to_rows(over_tokens(normed_one, grad_qkv)))
    gain_total = lax.psum(jnp.stack([gain_attn_term, gain_ffn_term]), ("grp", "rep"))
    own_gains = lax.dynamic_slice_in_dim(gain_total, own_index * rows_here, rows_here, 1)
    return (
        result_of(scatter(hidden, w_down, False)),
        grad_x,
        whole_rows(qkv_term[..., :q_here]),
        kv_rows(qkv_term[..., q_here : q_here + HD]),
        kv_rows(qkv_term[..., q_here + HD :]),
        out_term,
        whole_rows(gate_up_term[..., :hidden_here]),
        whole_rows(gate_up_term[..., hidden_here:]),
        sum_over_sequences(down_term),
        own_gains[0],
        own_gains[1],
    )


def solution(mesh):
    tokens, table, rows, whole = P("rep", "grp", None), P("rep", None), P("grp", None), P()
    return jax.shard_map(
        on_device,
        mesh=mesh,
        in_specs=(tokens, tokens, table, table) + (rows,) * 7 + (whole,) * 2,
        out_specs=(tokens, tokens) + (rows,) * 7 + (P("grp"),) * 2,
        check_vma=False,
    )
```

```python
import functools

import jax
import jax.numpy as jnp
import numpy as np
from jax import lax
from jax.experimental import pallas as pl
from jax.experimental.pallas import tpu as pltpu
from jax.sharding import PartitionSpec as P

HD = 128
EPS = 1e-05
ROPE_BASE = 1000000.0
SCORE_SCALE = HD**-0.5
LOG2E = 1.4426950408889634
TO_EXP2 = SCORE_SCALE * LOG2E
NEG = -1e30

MESH = pl.DeviceIdType.MESH
f32 = jnp.float32
bf16 = jnp.bfloat16


def matmul_f32(first, second):
    return jnp.dot(first, second, preferred_element_type=f32)


def against_rows(first, second):
    return lax.dot_general(first, second, (((1,), (1,)), ((), ())), preferred_element_type=f32)


def over_tokens(first, second):
    return lax.dot_general(first, second, (((0,), (0,)), ((), ())), preferred_element_type=f32)


def turn_tables(length):
    half_size = HD // 2
    inverse = np.float32(ROPE_BASE) ** (-(np.arange(half_size, dtype=np.float32) * 2) / HD)
    angles = np.arange(length, dtype=np.float32)[:, None] * inverse.astype(np.float32)
    cosine, sine = np.cos(angles), np.sin(angles)
    tables = np.concatenate([cosine, cosine], -1), np.concatenate([-sine, sine], -1)
    return tuple(jnp.asarray(table.astype(np.float32)) for table in tables)


def norm_back(upstream, grad_normed, unit_rows, inv_root, gain):
    scaled = grad_normed * gain
    center_term = jnp.mean(scaled * unit_rows, -1, keepdims=True)
    return (
        upstream + inv_root * (scaled - unit_rows * center_term),
        jnp.sum(grad_normed * unit_rows, 0),
    )


def fold_lanes(values, op):
    out = values[:, :HD]
    for at in range(HD, values.shape[1], HD):
        out = op(out, values[:, at : at + HD])
    return out


def as_row(column):
    return jnp.broadcast_to(column, (column.shape[0], HD)).T[0:1, :]


def attend_kernel(
    heads, cuts, block,
    order_ref, qkv_ref, cos_ref, sin_ref, piece_ref, piece_col_ref,
    out_ref, q_ref, k_ref, v_ref, lse_ref, placed,
    scores,
):
    length = qkv_ref.shape[0]
    cut = length // cuts
    blocks = length // block

    def place_cut(r, _):
        src = pl.ds(pl.multiple_of(r * cut, cut), cut)
        dst = pl.ds(pl.multiple_of(order_ref[0, r] * cut, cut), cut)
        cosine, sine = cos_ref[dst, :], sin_ref[dst, :]
        for h in range(heads + 1):
            part = qkv_ref[src, h * HD : (h + 1) * HD]
            turned = (part * cosine + pltpu.roll(part, HD // 2, 1) * sine).astype(bf16)
            if h < heads:
                q_ref[h, dst, :] = turned
            else:
                k_ref[dst, :] = turned
        v_ref[dst, :] = qkv_ref[src, (heads + 1) * HD :].astype(bf16)
        return 0

    lax.fori_loop(0, cuts, place_cut, 0)

    def one_block(i, _):
        rows = pl.ds(pl.multiple_of(i * block, block), block)
        query = q_ref[:, rows, :].reshape(heads * block, HD)

        def score(j, high):
            cols = pl.ds(pl.multiple_of(j * block, block), block)
            tile = against_rows(query, k_ref[cols, :])
            scores[j] = tile
            return jnp.maximum(high, fold_lanes(tile, jnp.maximum))

        high = lax.fori_loop(0, i, score, jnp.full((heads * block, HD), NEG, f32))
        tile = against_rows(query, k_ref[rows, :])
        q_at = lax.broadcasted_iota(jnp.int32, (block, block), 0)
        k_at = lax.broadcasted_iota(jnp.int32, (block, block), 1)
        q_piece, k_piece = piece_col_ref[rows, 0:1], piece_ref[0:1, rows]
        allowed = (k_at <= q_at) | ((q_piece != 0) & (q_piece == k_piece))
        tile = jnp.concatenate(
            [jnp.where(allowed, tile[h * block : (h + 1) * block], NEG) for h in range(heads)], 0
        )
        scores[i] = tile
        high = jnp.max(jnp.maximum(high, fold_lanes(tile, jnp.maximum)), 1, keepdims=True)

        def weigh(j, state):
            total, mixed = state
            cols = pl.ds(pl.multiple_of(j * block, block), block)
            prob = jnp.exp2((scores[j] - high) * TO_EXP2)
            total = total + fold_lanes(prob, jnp.add)
            return total, mixed + matmul_f32(prob.astype(bf16), v_ref[cols, :])

        zero = jnp.zeros((heads * block, HD), f32)
        total, mixed = lax.fori_loop(0, i + 1, weigh, (zero, zero))
        total = jnp.sum(total, 1, keepdims=True)
        mixed = (mixed / total).astype(bf16)
        log_total = high * TO_EXP2 + jnp.log2(total)
        for h in range(heads):
            placed[rows, h * HD : (h + 1) * HD] = mixed[h * block : (h + 1) * block]
            lse_ref[h : h + 1, rows] = as_row(log_total[h * block : (h + 1) * block])
        return 0

    lax.fori_loop(0, blocks, one_block, 0)

    def store_cut(r, _):
        dst = pl.ds(pl.multiple_of(r * cut, cut), cut)
        src = pl.ds(pl.multiple_of(order_ref[0, r] * cut, cut), cut)
        out_ref[dst, :] = placed[src, :]
        return 0

    lax.fori_loop(0, cuts, store_cut, 0)


def vmem_specs(count):
    return [pl.BlockSpec(memory_space=pltpu.VMEM)] * count


def attend(order, qkv, cosine, sine, piece, piece_col, heads):
    length = qkv.shape[0]
    block = min(512, length)
    return pl.pallas_call(
        functools.partial(attend_kernel, heads, order.shape[1], block),
        out_shape=(
            jax.ShapeDtypeStruct((length, heads * HD), bf16),
            jax.ShapeDtypeStruct((heads, length, HD), bf16),
            jax.ShapeDtypeStruct((length, HD), bf16),
            jax.ShapeDtypeStruct((length, HD), bf16),
            jax.ShapeDtypeStruct((heads, length), f32),
            jax.ShapeDtypeStruct((length, heads * HD), bf16),
        ),
        in_specs=[pl.BlockSpec(memory_space=pltpu.SMEM)] + vmem_specs(5),
        out_specs=tuple(vmem_specs(6)),
        scratch_shapes=[pltpu.VMEM((length // block, heads * block, block), f32)],
        compiler_params=pltpu.CompilerParams(vmem_limit_bytes=60 * 2**20),
        cost_estimate=pl.CostEstimate(
            flops=3 * heads * length * length * HD, bytes_accessed=10 * length * HD * heads * 4,
            transcendentals=heads * length * length // 2,
        ),
    )(order, qkv, cosine, sine, piece, piece_col)


DOWN, GATE_UP, OUT, QKV = 8, 16, 2, 8
CHUNKS = DOWN + GATE_UP + OUT + QKV


def is_chunk(number):
    return 0 <= number < CHUNKS


def chunk_shape(shape, number):
    return shape[:2] + (shape[2] // 2,) if number >= CHUNKS - QKV else shape


def is_middle():
    rank = lax.axis_index("rep")
    return (rank == 1) | (rank == 2)


def is_end():
    rank = lax.axis_index("rep")
    return (rank == 0) | (rank == 3)


class NoLine:
    ticks = 0

    def signal(self, barrier):
        pass

    def greet(self, barrier, others):
        if others:
            pl.semaphore_wait(barrier, others)

    def start(self):
        pass

    def step(self):
        pass

    def end(self):
        pass


class Line:
    def __init__(self, first, ticks, picks, refs, outs, scratch):
        self.first, self.ticks, self.picks, self.refs, self.outs = first, ticks, picks, refs, outs
        (
            self.inward, self.across, self.own, self.pair, self.total, self.sems, self.local,
            self.carries,
        ) = scratch
        rank = lax.axis_index("rep")
        self.partner = {"rep": rank + 1 - 2 * (rank % 2)}
        self.peer = {"rep": 3 - rank}
        self.now = 0
        self.kept = []

    def signal(self, barrier):
        pl.semaphore_signal(barrier, inc=1, device_id=self.partner, device_id_type=MESH)

        @pl.when(is_middle())
        def _():
            pl.semaphore_signal(barrier, inc=1, device_id=self.peer, device_id_type=MESH)

    def greet(self, barrier, others):
        @pl.when(is_middle())
        def _():
            pl.semaphore_wait(barrier, others + 2)

        @pl.when(is_end())
        def _():
            pl.semaphore_wait(barrier, others + 1)

    def remote(self, hop, number, src, dst, device):
        return pltpu.make_async_remote_copy(
            src_ref=src, dst_ref=dst, send_sem=self.sems.at[0, hop, number],
            recv_sem=self.sems.at[1, hop, number], device_id=device, device_id_type=MESH,
        )

    def part(self, ref, at, chunk):
        width = chunk_shape(ref.shape[1:], chunk)[2]
        return ref.at[at] if width == ref.shape[3] else ref.at[at, :, :, :width]

    def hops(self, number):
        tick = self.first + number
        term = pair = total = None
        if is_chunk(tick):
            which, pick = self.picks[tick]
            term = (
                lambda: self.remote(
                    0, number, pick(self.refs[which]), self.part(self.inward, number, tick), self.partner
                ),
                lambda: pltpu.make_async_copy(
                    pick(self.refs[which]), self.part(self.own, tick % 2, tick), self.local.at[0, number]
                ),
            )
        if is_chunk(tick - 2):
            before = (
                self.refs[f"pair{number}"]
                if number < 2
                else self.part(self.pair, (tick - 2) % 3, tick - 2)
            )
            pair = (
                lambda: self.remote(1, number, before, self.part(self.across, number, tick - 2), self.peer),
                lambda: pltpu.make_async_copy(
                    before, self.part(self.pair, (tick - 2) % 3, tick - 2), self.carries.at[number]
                ),
            )
        if is_chunk(tick - 4):
            done = (
                self.refs[f"total{number}"]
                if number < 2
                else self.part(self.total, (tick - 4) % 3, tick - 4)
            )
            slot = self.outs[tick - 4]
            total = (
                lambda: self.remote(2, number, done, slot, self.partner),
                lambda: pltpu.make_async_copy(done, slot, self.local.at[1, number]),
            )
        return term, pair, total

    def open(self, number):
        term, pair, total = self.hops(number)

        @pl.when(is_end())
        def _():
            if term:
                term[0]().start()

        @pl.when(is_middle())
        def _():
            if pair:
                pair[0]().start()
            if total:
                total[0]().start()
            if term:
                term[1]().start()
            if total:
                total[1]().start()
            if pair and number < 2:
                pair[1]().start()

    def close(self, number):
        term, pair, total = self.hops(number)

        @pl.when(is_end())
        def _():
            if term:
                term[0]().wait_send()
            if total:
                total[0]().wait_recv()

        @pl.when(is_middle())
        def _():
            if total:
                total[0]().wait_send()
                total[1]().wait()
            if pair:
                pair[0]().wait_send()
                pair[0]().wait_recv()
            if term:
                term[0]().wait_recv()

    def add(self, number):
        term, pair, _ = self.hops(number)
        tick = self.first + number

        def sum_of(into, first, second):
            def one(g, _):
                into[g] = (first[g].astype(f32) + second[g].astype(f32)).astype(bf16)
                return 0

            lax.fori_loop(0, into.shape[0], one, 0)

        @pl.when(is_middle())
        def _():
            if pair:
                if number < 2:
                    pair[1]().wait()
                sum_of(
                    self.part(self.total, (tick - 2) % 3, tick - 2),
                    self.part(self.pair, (tick - 2) % 3, tick - 2),
                    self.part(self.across, number, tick - 2),
                )
            if term:
                term[1]().wait()
                sum_of(
                    self.part(self.pair, tick % 3, tick), self.part(self.own, tick % 2, tick),
                    self.part(self.inward, number, tick),
                )

    def keep(self, number):
        tick = self.first + number
        which = number - (self.ticks - 2)
        made = []
        if is_chunk(tick):
            made.append((self.pair.at[tick % 3], self.outs[f"pair{which}"], 2 + which))
        if is_chunk(tick - 2):
            made.append((self.total.at[(tick - 2) % 3], self.outs[f"total{which}"], 4 + which))
        copies = [
            lambda src=src, dst=dst, at=at: pltpu.make_async_copy(src, dst, self.carries.at[at])
            for src, dst, at in made
        ]

        @pl.when(is_middle())
        def _():
            for copy in copies:
                copy().start()

        self.kept += copies

    def start(self):
        self.open(0)
        if self.ticks > 1:
            self.open(1)

    def step(self):
        if self.now + 2 < self.ticks:
            self.settle()
            self.open(self.now + 1)

    def settle(self):
        self.close(self.now)
        self.add(self.now)
        if self.now >= self.ticks - 2:
            self.keep(self.now)
        self.now += 1

    def end(self):
        while self.now + 2 < self.ticks:
            self.step()
        while self.now < self.ticks:
            self.settle()

        @pl.when(is_middle())
        def _():
            for copy in self.kept:
                copy().wait()


def line_slots(first, ticks):
    return [t - 4 for t in range(first, first + ticks) if is_chunk(t - 4)]


class Sums:
    def __init__(self, shape):
        self.shape, self.tick, self.kept, self.done = shape, 0, {}, {}


def run(kernel, ins, outs, scratch, number, cost, sums=None, ticks=0, arrays=(), picks=None, vmem=58):
    ins, outs, scratch = list(ins), list(outs), list(scratch)
    counts = (len(ins), len(outs), len(scratch))
    first = sums.tick if ticks else 0
    names_in, names_out = [], []
    if ticks:
        last = first + ticks - 1
        for name, array in arrays:
            names_in.append(name)
            ins.append((array, pl.ANY))
        for which in (0, 1):
            for name, chunk_at in ((f"pair{which}", first - 2), (f"total{which}", first - 4)):
                if is_chunk(chunk_at + which):
                    names_in.append(name)
                    ins.append((sums.kept[name], pl.ANY))
        names_out = line_slots(first, ticks)
        for which in (0, 1):
            for name, chunk_at in ((f"pair{which}", last - 1), (f"total{which}", last - 3)):
                if is_chunk(chunk_at + which):
                    names_out.append(name)
        slots = line_slots(first, ticks)
        outs += [
            (
                jax.ShapeDtypeStruct(
                    chunk_shape(sums.shape, name) if name in slots else sums.shape, bf16
                ),
                pl.ANY,
            )
            for name in names_out
        ]
        scratch += [
            pltpu.VMEM((ticks,) + sums.shape, bf16),
            pltpu.VMEM((ticks,) + sums.shape, bf16),
            pltpu.VMEM((2,) + sums.shape, bf16),
            pltpu.VMEM((3,) + sums.shape, bf16),
            pltpu.VMEM((3,) + sums.shape, bf16),
            pltpu.SemaphoreType.DMA((2, 3, ticks)),
            pltpu.SemaphoreType.DMA((2, ticks)),
            pltpu.SemaphoreType.DMA((6,)),
        ]

    def body(*refs):
        in_refs, rest = refs[: len(ins)], refs[len(ins) :]
        out_refs, scratch_refs = rest[: len(outs)], rest[len(outs) :]
        line = NoLine()
        if ticks:
            line = Line(
                first, ticks, picks, dict(zip(names_in, in_refs[counts[0] :])),
                dict(zip(names_out, out_refs[counts[1] :])), scratch_refs[counts[2] :],
            )
        kernel(in_refs[: counts[0]], out_refs[: counts[1]], scratch_refs[: counts[2]], line)

    results = pl.pallas_call(
        body,
        out_shape=tuple(shape for shape, _ in outs),
        in_specs=[pl.BlockSpec(memory_space=space) for _, space in ins],
        out_specs=tuple(pl.BlockSpec(memory_space=space) for _, space in outs),
        scratch_shapes=scratch,
        compiler_params=pltpu.CompilerParams(
            vmem_limit_bytes=vmem * 2**20,
            **({} if number is None else {"collective_id": number, "has_side_effects": True}),
        ),
        cost_estimate=pl.CostEstimate(
            flops=cost[0], bytes_accessed=cost[1], transcendentals=cost[2]
        ),
    )(*[array for array, _ in ins])
    for name, result in zip(names_out, results[counts[1] :]):
        if name in line_slots(first, ticks):
            sums.done[name] = result
        else:
            sums.kept[name] = result
    if ticks:
        sums.tick += ticks
    return results[: counts[1]]


SMEM, VMEM, ANY = pltpu.SMEM, pltpu.VMEM, pl.ANY


def attend_back_kernel(
    heads, block, ins, outs, scratch, line
):
    grad_ref, out_ref, q_ref, k_ref, v_ref, lse_ref, cos_ref, sin_ref, piece_ref, piece_col_ref = ins
    (grad_qkv_ref,) = outs
    grads, centers, grad_q = scratch
    if line.ticks:
        line.signal(pltpu.get_barrier_semaphore())
        line.greet(pltpu.get_barrier_semaphore(), 0)
        line.start()
    length = grad_ref.shape[0]
    blocks = length // block

    def take_block(i, _):
        rows = pl.ds(pl.multiple_of(i * block, block), block)
        for h in range(heads):
            grad = grad_ref[rows, h * HD : (h + 1) * HD].astype(bf16)
            grads[h, rows, :] = grad
            product = grad.astype(f32) * out_ref[rows, h * HD : (h + 1) * HD].astype(f32)
            centers[h, rows, :] = jnp.broadcast_to(
                jnp.sum(product, 1, keepdims=True), (block, HD)
            )
        return 0

    lax.fori_loop(0, blocks, take_block, 0)
    grad_q[...] = jnp.zeros_like(grad_q)

    def key_block(j, _):
        cols = pl.ds(pl.multiple_of(j * block, block), block)
        key, value = k_ref[cols, :], v_ref[cols, :]

        def one(i, state, diagonal):
            grad_key, grad_value = state
            rows = pl.ds(pl.multiple_of(i * block, block), block)
            for h in range(heads):
                query, grad = q_ref[h, rows, :], grads[h, rows, :]
                log_total = lse_ref[h : h + 1, rows]
                center = centers[h, rows, :].T[0:1, :]
                prob = jnp.exp2(against_rows(key, query) * TO_EXP2 - log_total)
                if diagonal:
                    k_at = lax.broadcasted_iota(jnp.int32, (block, block), 0)
                    q_at = lax.broadcasted_iota(jnp.int32, (block, block), 1)
                    k_piece, q_piece = piece_col_ref[cols, 0:1], piece_ref[0:1, cols]
                    allowed = (k_at <= q_at) | ((q_piece != 0) & (q_piece == k_piece))
                    prob = jnp.where(allowed, prob, 0.0)
                grad_prob = against_rows(value, grad)
                grad_score = (prob * (grad_prob - center)).astype(bf16)
                grad_value = grad_value + matmul_f32(prob.astype(bf16), grad)
                grad_key = grad_key + matmul_f32(grad_score, query)
                grad_q[h, rows, :] += over_tokens(grad_score, key)
            return grad_key, grad_value

        zero = jnp.zeros((block, HD), f32)
        state = one(j, (zero, zero), True)
        grad_key, grad_value = lax.fori_loop(
            j + 1, blocks, functools.partial(one, diagonal=False), state
        )
        grad_key = grad_key * SCORE_SCALE
        grad_key = grad_key * cos_ref[cols, :] - pltpu.roll(grad_key, HD // 2, 1) * sin_ref[cols, :]
        grad_qkv_ref[cols, heads * HD : (heads + 1) * HD] = grad_key.astype(bf16)
        grad_qkv_ref[cols, (heads + 1) * HD :] = grad_value.astype(bf16)
        return 0

    for j in range(min(2, blocks - 1)):
        lax.fori_loop(j, j + 1, key_block, 0)
        line.step()
    lax.fori_loop(min(2, blocks - 1), blocks, key_block, 0)

    def turn_back(i, _):
        rows = pl.ds(pl.multiple_of(i * block, block), block)
        for h in range(heads):
            grad = grad_q[h, rows, :] * SCORE_SCALE
            grad = grad * cos_ref[rows, :] - pltpu.roll(grad, HD // 2, 1) * sin_ref[rows, :]
            grad_qkv_ref[rows, h * HD : (h + 1) * HD] = grad.astype(bf16)
        return 0

    lax.fori_loop(0, blocks, turn_back, 0)
    line.end()


def take_cuts_kernel(cuts, holder_ref, rows_ref, out_ref):
    cut = out_ref.shape[0] // cuts

    def one(p, _):
        src = pl.ds(pl.multiple_of(holder_ref[0, p] * cut, cut), cut)
        out_ref[pl.ds(pl.multiple_of(p * cut, cut), cut), :] = rows_ref[src, :]
        return 0

    lax.fori_loop(0, cuts, one, 0)


def take_cuts(holder, rows):
    return pl.pallas_call(
        functools.partial(take_cuts_kernel, holder.shape[1]),
        out_shape=jax.ShapeDtypeStruct(rows.shape, rows.dtype),
        in_specs=[pl.BlockSpec(memory_space=pltpu.SMEM)] + vmem_specs(1),
        out_specs=pl.BlockSpec(memory_space=pltpu.VMEM),
        cost_estimate=pl.CostEstimate(
            flops=0, bytes_accessed=2 * rows.size * rows.dtype.itemsize, transcendentals=0
        ),
    )(holder, rows)


def attend_back(
    order, grad, out, query, key, value, lse, cosine, sine, piece, piece_col, heads, **line
):
    cuts = jnp.arange(order.shape[1], dtype=order.dtype)
    holder = jnp.sum(jnp.where(order[0][None, :] == cuts[:, None], cuts[None, :], 0), 1)[None, :]
    length = grad.shape[0]
    block = min(512, length)
    tall = [take_cuts(holder, grad), out, query, key, value, lse, cosine, sine, piece, piece_col]
    grad_qkv = run(
        functools.partial(attend_back_kernel, heads, block),
        [(array, VMEM) for array in tall],
        [(jax.ShapeDtypeStruct((length, (heads + 2) * HD), bf16), VMEM)],
        [
            pltpu.VMEM((heads, length, HD), bf16),
            pltpu.VMEM((heads, length, HD), f32),
            pltpu.VMEM((heads, length, HD), f32),
        ],
        line.pop("number", None),
        (8 * heads * length * length * HD, 14 * length * HD * heads * 4, heads * length * length // 2),
        **line,
    )[0]
    return take_cuts(order, grad_qkv)


def place_in_group():
    me = lax.axis_index("grp")
    return me // 4, (me // 2) % 2, me % 2


def other(flip_y, flip_x, flip_core):
    y, x, core = place_in_group()
    return ((y + flip_y) % 2) * 4 + ((x + flip_x) % 2) * 2 + (core + flip_core) % 2


def chip_rows(flip_y, flip_x, rows):
    y, x, _ = place_in_group()
    first = (((y + flip_y) % 2) * 2 + (x + flip_x) % 2) * (2 * rows)
    return pl.ds(pl.multiple_of(first, 2 * rows), 2 * rows)


NEIGHBOURS = ((0, 0, 1), (0, 1, 0), (1, 0, 0))
EVERYONE = tuple((n // 4, (n // 2) % 2, n % 2) for n in range(1, 8))


def greet_group(line, flips=NEIGHBOURS, between=None):
    barrier = pltpu.get_barrier_semaphore()
    for flip in flips:
        pl.semaphore_signal(barrier, inc=1, device_id={"grp": other(*flip)}, device_id_type=MESH)
    line.signal(barrier)
    if between:
        between()
    line.greet(barrier, len(flips))


SIBLING, ALONG_X, ALONG_Y, ACROSS = (0, 0), (0, 1), (1, 0), (1, 1)


def gather_rows(rows, all_ref, sends, recvs, on_chip, line, then=None):
    half = rows // 2

    def block(chip, core, part=None):
        first = other(*chip, core) * rows
        if part is None:
            return pl.ds(pl.multiple_of(first, rows), rows)
        return pl.ds(pl.multiple_of(first + part * half, half), half)

    def copy(number, chip, core, part, target):
        where = all_ref.at[block(chip, core, part), :]
        return pltpu.make_async_remote_copy(
            src_ref=where, dst_ref=where, send_sem=sends.at[number], recv_sem=recvs.at[number],
            device_id={"grp": other(*target)}, device_id_type=MESH,
        )

    def landed(number, chip, core, part):
        where = all_ref.at[block(chip, core, part), :]
        pltpu.make_async_remote_copy(
            src_ref=where, dst_ref=where, send_sem=sends.at[number], recv_sem=recvs.at[number],
            device_id={"grp": other(0, 0, 1)}, device_id_type=MESH,
        ).wait_recv()

    to_s, to_x, to_y = (0, 0, 1), (0, 1, 0), (1, 0, 0)
    started = []

    def send(*what):
        one = copy(*what)
        one.start()
        started.append(one)

    send(1, SIBLING, 0, 1, to_x)
    send(3, SIBLING, 0, 0, to_y)
    send(0, SIBLING, 0, None, to_s)
    send(2, SIBLING, 0, 0, to_x)
    send(4, SIBLING, 0, 1, to_y)
    if then:
        then()
    landed(0, SIBLING, 1, None)
    on_chip(*SIBLING)
    landed(1, ALONG_X, 0, 1)
    send(6, ALONG_X, 0, 1, to_y)
    landed(3, ALONG_Y, 0, 0)
    send(5, ALONG_Y, 0, 0, to_x)
    send(7, ALONG_X, 0, 1, to_s)
    send(8, ALONG_Y, 0, 0, to_s)
    line.step()
    landed(2, ALONG_X, 0, 0)
    send(9, ALONG_X, 0, 0, to_s)
    landed(4, ALONG_Y, 0, 1)
    send(10, ALONG_Y, 0, 1, to_s)
    line.step()
    landed(7, ALONG_X, 1, 1)
    landed(9, ALONG_X, 1, 0)
    on_chip(*ALONG_X)
    landed(5, ACROSS, 0, 0)
    send(11, ACROSS, 0, 0, to_s)
    landed(6, ACROSS, 0, 1)
    send(12, ACROSS, 0, 1, to_s)
    line.step()
    landed(8, ALONG_Y, 1, 0)
    landed(10, ALONG_Y, 1, 1)
    on_chip(*ALONG_Y)
    landed(11, ACROSS, 1, 0)
    landed(12, ACROSS, 1, 1)
    on_chip(*ACROSS)
    for one in started:
        one.wait_send()
    line.end()


GATHER_COPIES = 13


def rms_normed(values, gain):
    return values * lax.rsqrt(jnp.mean(values * values, -1, keepdims=True) + EPS) * gain


class Moves:
    def __init__(self, sems):
        self.sems, self.count, self.open = sems, 0, []

    def start(self, src, dst):
        one = pltpu.make_async_copy(src, dst, self.sems.at[self.count])
        self.count += 1
        one.start()
        return one

    def later(self, src, dst):
        self.open.append(self.start(src, dst))

    def finish(self):
        for one in self.open:
            one.wait()


def gather_scratch(rows, width, moves):
    return [
        pltpu.VMEM((8 * rows, width), bf16),
        pltpu.SemaphoreType.DMA((GATHER_COPIES,)),
        pltpu.SemaphoreType.DMA((GATHER_COPIES,)),
        pltpu.SemaphoreType.DMA((moves,)),
    ]


def own_rows(rows):
    return pl.ds(pl.multiple_of(other(0, 0, 0) * rows, rows), rows)


def send_columns(pieces, sends, recvs, moves):
    copies = []
    for which, (rows_ref, width, there) in enumerate(pieces):
        for number, flip in enumerate(EVERYONE):
            target = other(*flip)
            cols = pl.ds(pl.multiple_of(target * width, width), width)
            one = pltpu.make_async_remote_copy(
                src_ref=rows_ref.at[:, cols], dst_ref=there,
                send_sem=sends.at[which, number], recv_sem=recvs.at[which, number],
                device_id={"grp": target}, device_id_type=MESH,
            )
            one.start()
            copies.append(one)
        mine = pl.ds(pl.multiple_of(other(0, 0, 0) * width, width), width)
        moves.later(rows_ref.at[:, mine], there)
    return copies


def gather_normed_kernel(ins, outs, scratch, line):
    x_ref, gain_ref = ins[:2]
    weights = ins[2:]
    all_ref, cols_ref = outs
    held, sends, recvs, sems, col_sends, col_recvs = scratch
    rows = x_ref.shape[0]
    moves = Moves(sems)

    def fill():
        held[own_rows(rows), :] = rms_normed(x_ref[...].astype(f32), gain_ref[...]).astype(bf16)

    greet_group(line, EVERYONE, fill)
    col_copies = []

    def send_weights():
        pieces, low = [], 0
        tall = weights[0].shape[0]
        there = pl.ds(pl.multiple_of(other(0, 0, 0) * tall, tall), tall)
        for weight in weights:
            width = weight.shape[1] // 8
            pieces.append((weight, width, cols_ref.at[there, low : low + width]))
            low += width
        col_copies.extend(send_columns(pieces, col_sends, col_recvs, moves))

    def on_chip(*chip):
        where = chip_rows(*chip, rows)
        moves.later(held.at[where, :], all_ref.at[where, :])

    gather_rows(rows, held, sends, recvs, on_chip, line, send_weights)
    for one in col_copies:
        one.wait()
    moves.finish()


def gather_normed(x, gain, weights, **line):
    rows, width = x.shape
    deep = sum(weight.shape[1] for weight in weights) // 8
    return run(
        gather_normed_kernel,
        [(x, VMEM), (gain, VMEM)] + [(weight, ANY) for weight in weights],
        [
            (jax.ShapeDtypeStruct((8 * rows, width), bf16), ANY),
            (jax.ShapeDtypeStruct((8 * weights[0].shape[0], deep), bf16), ANY),
        ],
        gather_scratch(rows, width, 4 + len(weights))
        + [pltpu.SemaphoreType.DMA((len(weights), 7))] * 2,
        line.pop("number"),
        (0, 150 * rows * width * 2, 0),
        **line,
    )


def columns_kernel(rows_here, ins, outs, scratch, line):
    (cols_ref,) = outs
    sends, recvs, sems = scratch
    moves = Moves(sems)
    barrier = pltpu.get_barrier_semaphore()
    for flip in EVERYONE:
        pl.semaphore_signal(barrier, inc=1, device_id={"grp": other(*flip)}, device_id_type=MESH)
    pl.semaphore_wait(barrier, 7)
    first = pl.multiple_of(lax.axis_index("rep") * rows_here, rows_here)
    me = other(0, 0, 0)
    pieces, low = [], 0
    for weight in ins:
        width = weight.shape[1] // 8
        pieces.append(
            (weight.at[pl.ds(first, rows_here), :], width, cols_ref.at[me, :, low : low + width])
        )
        low += width
    for one in send_columns(pieces, sends, recvs, moves):
        one.wait()
    moves.finish()


def columns_of_some(weights, rows_here, number):
    deep = sum(weight.shape[1] for weight in weights) // 8
    return run(
        functools.partial(columns_kernel, rows_here),
        [(weight, ANY) for weight in weights],
        [(jax.ShapeDtypeStruct((8, rows_here, deep), bf16), ANY)],
        [pltpu.SemaphoreType.DMA((len(weights), 7))] * 2
        + [pltpu.SemaphoreType.DMA((len(weights),))],
        number, (0, 50 * 8 * rows_here * deep, 0),
    )[0]


def feed_forward_kernel(tile, ins, outs, scratch, line):
    mid_ref, gain_ref, spread_ref, rest_ref = ins
    all_ref, hidden_ref, up_part_ref, gate_part_ref, whole_ref = outs
    held, sends, recvs, sems, weight, hidden, up_part, gate_part = scratch
    rows = mid_ref.shape[0]
    inner = hidden.shape[1]
    moves = Moves(sems)
    planes, _, tall, deep = spread_ref.shape
    loads = [
        moves.start(spread_ref.at[z], weight.at[:, z * tall : (z + 1) * tall, :])
        for z in range(planes)
    ]
    loads.append(moves.start(rest_ref, weight.at[:, planes * tall :, :]))

    def fill():
        held[own_rows(rows), :] = rms_normed(mid_ref[...], gain_ref[...]).astype(bf16)

    greet_group(line, between=fill)

    def on_chip(*chip):
        where = chip_rows(*chip, rows)
        moves.later(held.at[where, :], all_ref.at[where, :])
        if chip == SIBLING:
            for one in loads:
                one.wait()
            moves.later(weight, whole_ref)

        def column(t, _):
            cols = pl.ds(pl.multiple_of(t * tile, tile), tile)
            up_cols = pl.ds(pl.multiple_of(inner + t * tile, tile), tile)
            lhs = held[where, :]
            gate = matmul_f32(lhs, weight[:, :, cols].reshape(-1, tile))
            up = matmul_f32(lhs, weight[:, :, up_cols].reshape(-1, tile))
            sigma = 1.0 / (1.0 + jnp.exp(-gate))
            swish = gate * sigma
            hidden[where, cols] = (swish * up).astype(bf16)
            up_part[where, cols] = swish.astype(bf16)
            gate_part[where, cols] = (up * sigma * (1.0 + gate * (1.0 - sigma))).astype(bf16)
            return 0

        lax.fori_loop(0, inner // tile, column, 0)
        for src, dst in ((hidden, hidden_ref), (up_part, up_part_ref), (gate_part, gate_part_ref)):
            moves.later(src.at[where, :], dst.at[where, :])

    gather_rows(rows, held, sends, recvs, on_chip, line)
    moves.finish()


def feed_forward(mid, gain, spread, rest, **line):
    rows, width = mid.shape
    inner = rest.shape[2] // 2
    weight = (8, width // 8, 2 * inner)
    tall = jax.ShapeDtypeStruct((8 * rows, inner), bf16)
    return run(
        functools.partial(feed_forward_kernel, min(256, inner)),
        [(mid, VMEM), (gain, VMEM), (spread, ANY), (rest, ANY)],
        [(jax.ShapeDtypeStruct((8 * rows, width), bf16), ANY)]
        + [(tall, ANY)] * 3
        + [(jax.ShapeDtypeStruct(weight, bf16), ANY)],
        gather_scratch(rows, width, 22)
        + [pltpu.VMEM(weight, bf16)]
        + [pltpu.VMEM((8 * rows, inner), bf16)] * 3,
        line.pop("number"),
        (32 * rows * width * inner, 150 * rows * width * 2, 8 * rows * inner),
        **line,
    )


def feed_forward_back_kernel(tile, ins, outs, scratch, line):
    grad_ref, w_ref, hidden_ref, up_part_ref, gate_part_ref = ins
    grad_gate_up_ref, down_ref = outs
    held, sends, recvs, sems, weight, hidden, up_part, gate_part, grads, down, down_low = scratch
    rows = grad_ref.shape[0]
    inner, width = weight.shape
    moves = Moves(sems)
    loads = [
        moves.start(src, dst)
        for src, dst in (
            (w_ref, weight), (hidden_ref, hidden), (up_part_ref, up_part), (gate_part_ref, gate_part)
        )
    ]
    greet_group(line)
    line.start()
    held[own_rows(rows), :] = grad_ref[...].astype(bf16)

    def on_chip(*chip):
        where = chip_rows(*chip, rows)
        if chip == SIBLING:
            for one in loads:
                one.wait()

        def column(t, _):
            cols = pl.ds(pl.multiple_of(t * tile, tile), tile)
            up_cols = pl.ds(pl.multiple_of(inner + t * tile, tile), tile)
            incoming = held[where, :]
            grad_hidden = against_rows(incoming, weight[cols, :])
            grads[where, cols] = (grad_hidden * gate_part[where, cols].astype(f32)).astype(bf16)
            grads[where, up_cols] = (grad_hidden * up_part[where, cols].astype(f32)).astype(bf16)
            term = over_tokens(hidden[where, cols], incoming)
            if chip == SIBLING:
                down[cols, :] = term
            elif chip == ACROSS:
                down_low[cols, :] = (down[cols, :] + term).astype(bf16)
            else:
                down[cols, :] += term
            return 0

        lax.fori_loop(0, inner // tile, column, 0)
        moves.later(grads.at[where, :], grad_gate_up_ref.at[where, :])

    gather_rows(rows, held, sends, recvs, on_chip, line)
    moves.later(down_low, down_ref)
    moves.finish()


def feed_forward_back(grad, w_down, hidden, up_part, gate_part, **line):
    rows, width = grad.shape
    inner = w_down.shape[0]
    return run(
        functools.partial(feed_forward_back_kernel, min(256, inner)),
        [(grad, VMEM)] + [(array, ANY) for array in (w_down, hidden, up_part, gate_part)],
        [
            (jax.ShapeDtypeStruct((8 * rows, 2 * inner), bf16), ANY),
            (jax.ShapeDtypeStruct((inner, width), bf16), ANY),
        ],
        gather_scratch(rows, width, 9)
        + [pltpu.VMEM(w_down.shape, bf16)]
        + [pltpu.VMEM((8 * rows, inner), bf16)] * 3
        + [
            pltpu.VMEM((8 * rows, 2 * inner), bf16),
            pltpu.VMEM(w_down.shape, f32),
            pltpu.VMEM(w_down.shape, bf16),
        ],
        line.pop("number"),
        (32 * rows * width * inner, 150 * rows * width * 2, 0),
        vmem=62,
        **line,
    )


def attended_back_kernel(ins, outs, scratch, line):
    grad_ref, w_ref, attended_ref = ins
    grad_attended_ref, out_term_ref = outs
    held, sends, recvs, sems, total = scratch
    rows = grad_ref.shape[0]
    moves = Moves(sems)
    greet_group(line)
    line.start()
    held[own_rows(rows), :] = grad_ref[...].astype(bf16)

    def on_chip(*chip):
        where = chip_rows(*chip, rows)
        incoming = held[where, :]
        grad_attended_ref[where, :] = against_rows(incoming, w_ref[...]).astype(bf16)
        term = over_tokens(attended_ref[where, :], incoming)
        if chip == SIBLING:
            total[...] = term
        elif chip == ACROSS:
            out_term_ref[...] = (total[...] + term).astype(bf16)
        else:
            total[...] += term

    gather_rows(rows, held, sends, recvs, on_chip, line)
    moves.finish()


def attended_back(grad, w_out, attended, **line):
    rows, width = grad.shape
    return run(
        attended_back_kernel,
        [(array, VMEM) for array in (grad, w_out, attended)],
        [
            (jax.ShapeDtypeStruct(attended.shape, bf16), VMEM),
            (jax.ShapeDtypeStruct(w_out.shape, bf16), VMEM),
        ],
        gather_scratch(rows, width, 1) + [pltpu.VMEM(w_out.shape, f32)],
        line.pop("number"),
        (32 * rows * width * w_out.shape[0], 150 * rows * width * 2, 0),
        **line,
    )


class WeightTerm:
    def __init__(self, rows_ref, columns_ref, term_ref, scratch):
        self.rows_ref, self.columns_ref, self.term_ref = rows_ref, columns_ref, term_ref
        self.loaded, self.ready, self.sems = scratch
        self.tile = self.loaded.shape[2]
        for number in (0, 1):
            self.load(number).start()

    def load(self, number):
        cols = slice(number * self.tile, (number + 1) * self.tile)
        return pltpu.make_async_copy(
            self.rows_ref.at[:, cols], self.loaded.at[number % 2], self.sems.at[0, number % 2]
        )

    def store(self, number):
        return pltpu.make_async_copy(
            self.ready.at[number % 2], self.term_ref.at[number], self.sems.at[1, number % 2]
        )

    def work(self, numbers):
        for number in numbers:
            at = number % 2
            self.load(number).wait()
            if number >= 2:
                self.store(number - 2).wait()
            width = self.columns_ref.shape[1]
            step = min(256, width)

            def column(t, _):
                cols = pl.ds(pl.multiple_of(t * step, step), step)
                term = over_tokens(self.loaded[at], self.columns_ref[:, cols])
                self.ready[at, :, cols] = term.astype(bf16)
                return 0

            lax.fori_loop(0, width // step, column, 0)
            self.store(number).start()
            if number + 2 < 8:
                self.load(number + 2).start()

    def finish(self):
        for number in (6, 7):
            self.store(number).wait()


def scatter_kernel(turned, tile, extra, after, ins, outs, scratch, line):
    out_ref = outs[0] if after == "base" else scratch[-4]
    finals = ins[len(ins) - {"base": 1, "cast": 1, "back": 3}[after] :]
    part, to_s, from_s, to_chip, held, relay, last, sends, recvs = scratch[:9]
    a_ref, b_ref, loads = scratch[-3:]
    loading = [
        pltpu.make_async_copy(src, dst, loads.at[number])
        for number, (src, dst) in enumerate(((ins[1], b_ref), (ins[0], a_ref)))
    ]
    for one in loading:
        one.start()
    rows, width = out_ref.shape
    half = rows // 2
    _, _, core = place_in_group()
    greet_group(line)
    line.start()
    if extra:
        columns_ref = a_ref
        if extra == "loaded":
            columns_ref = scratch[12]
            columns_copy = pltpu.make_async_copy(ins[3], columns_ref, scratch[13].at[0])
            columns_copy.start()
        term = WeightTerm(ins[2], columns_ref, outs[-1], scratch[9:12])
    for one in loading:
        one.wait()
    own_at = pl.multiple_of(core * rows, rows)
    other_at = pl.multiple_of((1 - core) * rows, rows)
    started = []

    def send(number, src, dst, target):
        one = pltpu.make_async_remote_copy(
            src_ref=src, dst_ref=dst, send_sem=sends.at[number], recv_sem=recvs.at[number],
            device_id={"grp": other(*target)}, device_id_type=MESH,
        )
        one.start()
        started.append(one)
        return one

    def landed(number, where):
        pltpu.make_async_remote_copy(
            src_ref=where, dst_ref=where, send_sem=sends.at[number], recv_sem=recvs.at[number],
            device_id={"grp": other(0, 0, 1)}, device_id_type=MESH,
        ).wait_recv()

    to_sib, to_x, to_y = (0, 0, 1), (0, 1, 0), (1, 0, 0)

    def make(number, chip):
        where = chip_rows(*chip, rows)

        def column(t, _):
            cols = pl.ds(pl.multiple_of(t * tile, tile), tile)
            lhs = a_ref[where, :]
            if turned:
                part[:, cols] = against_rows(lhs, b_ref[cols, :])
            else:
                part[:, cols] = matmul_f32(lhs, b_ref[:, cols])
            return 0

        lax.fori_loop(0, width // tile, column, 0)
        to_s[number] = part[pl.ds(other_at, rows), :].astype(bf16)
        send(number, to_s.at[number], from_s.at[number], to_sib)

    def own(low, number):
        at = pl.ds(pl.multiple_of(core * rows + low * half, half), half)
        return part[at, :] + from_s[number, low * half : (low + 1) * half, :].astype(f32)

    first, second = slice(0, half), slice(half, rows)
    make(0, ACROSS)
    landed(0, from_s.at[0])
    to_chip[0, first, :] = own(0, 0).astype(bf16)
    send(4, to_chip.at[0, first, :], relay.at[0], to_x)
    to_chip[0, second, :] = own(1, 0).astype(bf16)
    send(5, to_chip.at[0, second, :], relay.at[1], to_y)
    make(1, ALONG_X)
    landed(1, from_s.at[1])
    to_chip[1, first, :] = own(0, 1).astype(bf16)
    send(6, to_chip.at[1, first, :], last.at[0, first, :], to_x)
    held[0] = own(1, 1)
    line.step()
    make(2, ALONG_Y)
    landed(2, from_s.at[2])
    to_chip[2, second, :] = own(1, 2).astype(bf16)
    send(7, to_chip.at[2, second, :], last.at[1, second, :], to_y)
    held[1] = own(0, 2)
    if extra:
        if extra == "loaded":
            columns_copy.wait()
        term.work((0, 1, 2))
    landed(5, relay.at[1])
    to_chip[1, second, :] = (held[0] + relay[1].astype(f32)).astype(bf16)
    send(8, to_chip.at[1, second, :], last.at[0, second, :], to_x)
    landed(4, relay.at[0])
    to_chip[2, first, :] = (held[1] + relay[0].astype(f32)).astype(bf16)
    send(9, to_chip.at[2, first, :], last.at[1, first, :], to_y)
    line.step()
    make(3, SIBLING)
    if extra:
        term.work((3, 4))
        line.step()
        term.work((5, 6, 7))
    landed(3, from_s.at[3])
    for low in (0, 1):
        at = slice(low * half, (low + 1) * half)
        if after == "back":
            out_ref[at, :] = own(low, 3)
        else:
            out_ref[at, :] = own(low, 3) + finals[0][at, :].astype(f32)
    landed(6, last.at[0, first, :])
    out_ref[first, :] += last[0, first, :].astype(f32)
    landed(7, last.at[1, second, :])
    out_ref[second, :] += last[1, second, :].astype(f32)
    line.step()
    landed(8, last.at[0, second, :])
    out_ref[second, :] += last[0, second, :].astype(f32)
    landed(9, last.at[1, first, :])
    out_ref[first, :] += last[1, first, :].astype(f32)
    if after == "cast":
        outs[0][...] = out_ref[...].astype(outs[0].dtype)
    if after == "back":
        upstream_ref, rows_ref, gain_ref = finals
        some = min(64, rows)

        def norm_rows(number, gain_term):
            at = pl.ds(pl.multiple_of(number * some, some), some)
            values, incoming = rows_ref[at, :].astype(f32), out_ref[at, :]
            inv = lax.rsqrt(jnp.mean(values * values, -1, keepdims=True) + EPS)
            grad, term = norm_back(
                upstream_ref[at, :].astype(f32), incoming, values * inv, inv, gain_ref[...]
            )
            outs[0][at, :] = grad.astype(outs[0].dtype)
            return gain_term + term[None, :]

        outs[1][...] = lax.fori_loop(0, rows // some, norm_rows, jnp.zeros((1, width), f32))
    for one in started:
        one.wait_send()
    if extra:
        term.finish()
    line.end()


def product_scattered(a, b, turned, extra=None, base=None, back=None, dtype=f32, **line):
    length, depth = a.shape
    width = b.shape[0] if turned else b.shape[1]
    rows = length // 8
    tile = min(256, width)
    ins = [(a, ANY), (b, ANY)]
    outs = [(jax.ShapeDtypeStruct((rows, width), dtype), VMEM)]
    after = "back" if back else "base" if dtype == f32 else "cast"
    if back:
        outs.append((jax.ShapeDtypeStruct((1, width), f32), VMEM))
    scratch = [
        pltpu.VMEM((2 * rows, width), f32),
        pltpu.VMEM((4, rows, width), bf16),
        pltpu.VMEM((4, rows, width), bf16),
        pltpu.VMEM((3, rows, width), bf16),
        pltpu.VMEM((2, rows // 2, width), f32),
        pltpu.VMEM((2, rows // 2, width), bf16),
        pltpu.VMEM((2, rows, width), bf16),
        pltpu.SemaphoreType.DMA((10,)),
        pltpu.SemaphoreType.DMA((10,)),
    ]
    flops, kind = 2 * length * depth * width, None
    if extra:
        first, second = extra
        kind = "own" if second is None else "loaded"
        ins.append((first, ANY))
        columns = a if second is None else second
        tall = first.shape[1] // 8
        outs.append((jax.ShapeDtypeStruct((8, tall, columns.shape[1]), bf16), ANY))
        scratch += [
            pltpu.VMEM((2, length, tall), bf16),
            pltpu.VMEM((2, tall, columns.shape[1]), bf16),
            pltpu.SemaphoreType.DMA((2, 2)),
        ]
        if second is not None:
            ins.append((second, ANY))
            scratch += [pltpu.VMEM(second.shape, bf16), pltpu.SemaphoreType.DMA((1,))]
        flops += 2 * length * first.shape[1] * columns.shape[1]
    ins += [(array, VMEM) for array in (back or (base,))]
    if after != "base":
        scratch.append(pltpu.VMEM((rows, width), f32))
    scratch += [
        pltpu.VMEM(a.shape, bf16), pltpu.VMEM(b.shape, bf16), pltpu.SemaphoreType.DMA((2,))
    ]
    return run(
        functools.partial(scatter_kernel, turned, tile, kind, after), ins, outs, scratch,
        line.pop("number"), (flops, 150 * rows * width * 2, 0), vmem=61, **line,
    )


def tail_kernel(ready, later, ins, outs, scratch, line):
    qkv_ref, gains_ref = ins[:2]
    chunk_refs = dict(zip(ready, ins[2:]))
    gate_ref, up_ref, qkv_rows_ref, gains_out_ref = outs
    from_group, mine, from_rep, sends, recvs, chunk_sems, local = scratch
    me, rank = other(0, 0, 0), lax.axis_index("rep")
    inner = gate_ref.shape[1] // 8
    part = qkv_ref.shape[-1]
    high = line.outs[later[0]].shape[1]
    barrier = pltpu.get_barrier_semaphore()
    for flip in range(1, 4):
        pl.semaphore_signal(
            barrier, inc=1, device_id={"rep": (rank + flip) % 4}, device_id_type=MESH
        )
    for flip in EVERYONE:
        pl.semaphore_signal(barrier, inc=1, device_id={"grp": other(*flip)}, device_id_type=MESH)
    pl.semaphore_wait(barrier, 10)
    waits, moves = [], Moves(local)
    line.refs["qkv"] = qkv_rows_ref

    def send(kind, number, src, dst, device):
        return pltpu.make_async_remote_copy(
            src_ref=src, dst_ref=dst, send_sem=sends.at[kind, number],
            recv_sem=recvs.at[kind, number], device_id=device, device_id_type=MESH,
        )

    own_qkv = qkv_rows_ref.at[me // 4, :, :, pl.ds(pl.multiple_of((me % 4) * part, part), part)]
    qkv_copies, gain_copies = [], []
    for number, flip in enumerate(EVERYONE):
        target = other(*flip)
        qkv_copies.append(send(0, number, qkv_ref.at[target], own_qkv, {"grp": target}))
        qkv_copies[-1].start()
    moves.later(qkv_ref.at[me], own_qkv)
    line.start()
    for number, flip in enumerate(EVERYONE):
        target = other(*flip)
        gain_copies.append(
            send(1, number, gains_ref.at[target], from_group.at[me], {"grp": target})
        )
        gain_copies[-1].start()
    from_group[me] = gains_ref[me]

    def spread(chunk):
        src = chunk_refs[chunk] if chunk in chunk_refs else line.outs[chunk]
        number = chunk - DOWN
        rows = slice(number * high, (number + 1) * high)
        cols = pl.ds(pl.multiple_of(me * inner, inner), inner)
        for which, dst in enumerate((gate_ref, up_ref)):
            there = dst.at[rows, cols]
            for flip in EVERYONE:
                target = other(*flip)
                pltpu.make_async_remote_copy(
                    src_ref=src.at[target, :, which * inner : (which + 1) * inner], dst_ref=there,
                    send_sem=chunk_sems.at[0, which, number], recv_sem=chunk_sems.at[1, which, number],
                    device_id={"grp": target}, device_id_type=MESH,
                ).start()
            moves.later(src.at[me, :, which * inner : (which + 1) * inner], there)
            seven = dst.at[rows, : 7 * inner]
            waits.append(
                pltpu.make_async_remote_copy(
                    src_ref=seven, dst_ref=seven, send_sem=chunk_sems.at[0, which, number],
                    recv_sem=chunk_sems.at[1, which, number],
                    device_id={"grp": other(0, 0, 1)}, device_id_type=MESH,
                )
            )

    for chunk in ready:
        spread(chunk)
    for one in gain_copies:
        one.wait()
    mine[rank] = sum(from_group[g] for g in range(8))
    rep_copies = []
    for step in range(1, 4):
        target = (rank + step) % 4
        rep_copies.append(
            send(2, step, mine.at[rank], from_rep.at[step], {"rep": target})
        )
        rep_copies[-1].start()
    for step, one in zip(range(1, 4), rep_copies):
        one.wait()
        mine[(rank + 4 - step) % 4] = from_rep[step]
    gains_out_ref[...] = (mine[0] + mine[1]) + (mine[2] + mine[3])
    for number in range(1, line.ticks):
        if line.first + number + 1 == CHUNKS - QKV:
            for one in qkv_copies:
                one.wait()
            moves.open.pop(0).wait()
        line.step()
        chunk = line.first + number - 5
        if chunk in later:
            spread(chunk)
    line.end()
    for one in waits:
        one.wait_send()
        one.wait_recv()
    moves.finish()


def tail(qkv_term, gains, chunks, inner, number, sums, ticks, arrays, picks):
    first = sums.tick
    ready = sorted(chunks)
    later = [c for c in line_slots(first, ticks) if c < DOWN + GATE_UP]
    _, high, width = sums.shape
    wide = jax.ShapeDtypeStruct((GATE_UP * high, 8 * inner), bf16)
    moved = jax.ShapeDtypeStruct((2, 8, 2 * high, width), bf16)
    picks = dict(picks)
    for n in range(QKV):
        picks[CHUNKS - QKV + n] = (
            "qkv",
            lambda ref, n=n: ref.at[
                n // 4, :, n // 2 % 2 * high : (n // 2 % 2 + 1) * high,
                n % 2 * (width // 2) : (n % 2 + 1) * (width // 2),
            ],
        )
    return run(
        functools.partial(tail_kernel, ready, later),
        [(qkv_term, ANY), (gains, VMEM)] + [(chunks[c], ANY) for c in ready],
        [(wide, ANY), (wide, ANY), (moved, ANY), (jax.ShapeDtypeStruct(gains.shape[1:], f32), VMEM)],
        [
            pltpu.VMEM(gains.shape, f32),
            pltpu.VMEM((4,) + gains.shape[1:], f32),
            pltpu.VMEM((4,) + gains.shape[1:], f32),
            pltpu.SemaphoreType.DMA((3, 7)),
            pltpu.SemaphoreType.DMA((3, 7)),
            pltpu.SemaphoreType.DMA((2, 2, GATE_UP)),
            pltpu.SemaphoreType.DMA((1 + 2 * GATE_UP,)),
        ],
        number, (0, 200 * 8 * high * width * 2, 0), sums=sums, ticks=ticks, arrays=arrays, picks=picks,
    )


def finish_kernel(heads, *refs):
    chunks, rest = refs[: DOWN + OUT + QKV], refs[DOWN + OUT + QKV :]
    gate_rows, up_rows = rest[:2]
    query, key, value, out, gate, up, down = rest[2:9]
    low, wide, load_sems, store_sems = rest[9:]
    _, high, width = chunks[0].shape
    depth = low.shape[0]

    def half(number):
        return slice(number * high, (number + 1) * high)

    whole = slice(0, width)
    jobs = [(ref, [(whole, down.at[number])]) for number, ref in enumerate(chunks[:DOWN])]
    for ref, into in ((gate_rows, gate), (up_rows, up)):
        for low_col in range(0, ref.shape[2], width):
            cols = slice(low_col, low_col + width)
            for number in (0, 1):
                where = (slice(None), half(number), cols)
                jobs.append((ref.at[where], [(whole, into.at[where])]))
    for number, ref in enumerate(chunks[DOWN : DOWN + OUT]):
        jobs.append((ref, [(whole, out.at[:, half(number), :])]))
    part = (heads + 2) * HD
    for number, ref in enumerate(chunks[DOWN + OUT :]):
        stores = []
        places = ref.shape[2] // part
        for place in range(places):
            at, device = place * part, (number // 4 * 2 + number % 2) * places + place
            for into, first, size in (
                (query, 0, heads * HD), (key, heads * HD, HD), (value, (heads + 1) * HD, HD)
            ):
                there = into.at[:, half(number // 2 % 2), device * size : (device + 1) * size]
                stores.append((slice(at + first, at + first + size), there))
        jobs.append((ref, stores))

    def load(number):
        at, ref = number % depth, jobs[number][0]
        return pltpu.make_async_copy(ref, low.at[at, :, :, : ref.shape[2]], load_sems.at[at])

    def stores(number):
        at = number % depth
        return [
            pltpu.make_async_copy(wide.at[at, :, :, cols], into, store_sems.at[at, which])
            for which, (cols, into) in enumerate(jobs[number][1])
        ]

    for number in range(depth - 1):
        load(number).start()
    for number in range(len(jobs)):
        if number + depth - 1 < len(jobs):
            load(number + depth - 1).start()
        load(number).wait()
        if number >= depth:
            for one in stores(number - depth):
                one.wait()

        def cast(g, _, at=number % depth, cols=slice(0, jobs[number][0].shape[2])):
            wide[at, g, :, cols] = low[at, g, :, cols].astype(f32)
            return 0

        lax.fori_loop(0, low.shape[1], cast, 0)
        for one in stores(number):
            one.start()
    for number in range(len(jobs) - depth, len(jobs)):
        for one in stores(number):
            one.wait()


def finish(chunks, gate_rows, up_rows, heads):
    eight, high, width = chunks[0].shape
    rows, wide = gate_rows.shape

    def split(columns):
        return jax.ShapeDtypeStruct((eight, rows // eight, columns), f32)

    shapes = [split(columns) for columns in (8 * heads * HD, 8 * HD, 8 * HD, width, wide, wide)]
    shapes.append(jax.ShapeDtypeStruct((DOWN, eight, high, width), f32))
    depth = 6
    results = pl.pallas_call(
        functools.partial(finish_kernel, heads),
        out_shape=tuple(shapes),
        in_specs=[pl.BlockSpec(memory_space=pl.ANY)] * (len(chunks) + 2),
        out_specs=tuple([pl.BlockSpec(memory_space=pl.ANY)] * 7),
        scratch_shapes=[
            pltpu.VMEM((depth, eight, high, width), bf16),
            pltpu.VMEM((depth, eight, high, width), f32),
            pltpu.SemaphoreType.DMA((depth,)),
            pltpu.SemaphoreType.DMA((depth, 12)),
        ],
        compiler_params=pltpu.CompilerParams(vmem_limit_bytes=60 * 2**20),
        cost_estimate=pl.CostEstimate(
            flops=0, bytes_accessed=6 * CHUNKS * eight * high * width, transcendentals=0
        ),
    )(
        *chunks, gate_rows.reshape(eight, rows // eight, wide),
        up_rows.reshape(eight, rows // eight, wide),
    )
    flat = [result.reshape(rows, -1) for result in results[:6]]
    return flat + [results[6].reshape(DOWN * eight * high, width)]


def sum_over_sequences(term):
    return lax.psum(term, "rep").astype(f32)


def on_device(
    layer_input,
    cotangent,
    cut_order,
    piece_ids,
    w_query,
    w_key,
    w_value,
    w_out,
    w_gate,
    w_up,
    w_down,
    gain_attn,
    gain_ffn,
):
    groups = lax.axis_size("grp")
    reps = lax.axis_size("rep")
    own_index = lax.axis_index("grp")
    _, local_rows, model_width = layer_input.shape
    length = piece_ids.shape[1]
    rows_here = w_query.shape[0]
    q_width = w_query.shape[1]
    kv_heads = w_key.shape[1] // HD
    heads = q_width // HD // groups
    copies = groups // kv_heads
    hidden_here = w_down.shape[0]
    piece_col = jnp.broadcast_to(piece_ids.reshape(length, 1), (length, HD))
    cosine, sine = turn_tables(length)

    near = groups == 8 and reps == 4 and copies == 1

    def gather(rows):
        return lax.all_gather(rows, "grp", axis=0, tiled=True)

    def scatter(first, second, turned):
        term = against_rows(first, second) if turned else matmul_f32(first, second)
        return lax.psum_scatter(
            term.astype(bf16), "grp", scatter_dimension=0, tiled=True
        ).astype(f32)

    def to_columns(parts):
        return lax.all_to_all(parts, "grp", 1, 0, tiled=True).reshape(-1, parts.shape[-1])

    def per_group(weight):
        return weight.reshape(rows_here, groups, -1)

    def per_kv_head(weight):
        return jnp.repeat(weight.reshape(rows_here, kv_heads, HD), copies, axis=1)

    x_rows = layer_input.reshape(local_rows, model_width)
    x_flat = x_rows.astype(f32)
    inv_one = lax.rsqrt(jnp.mean(x_flat * x_flat, -1, keepdims=True) + EPS)
    unit_one = x_flat * inv_one
    attn_gain, ffn_gain = gain_attn.reshape(1, -1), gain_ffn.reshape(1, -1)
    if near:
        share = rows_here // (4 * reps) * 3
        spread = columns_of_some((w_gate, w_up), share, 11)
        x_first, spread = lax.optimization_barrier((x_rows, spread))
        spread = lax.all_gather(spread, "rep", axis=0)
        normed_one, cols_qkv = gather_normed(
            x_first, attn_gain, (w_query, w_key, w_value), number=1
        )
        last_gate, last_up, normed_one = lax.optimization_barrier(
            (w_gate[reps * share :], w_up[reps * share :], normed_one)
        )
        rest = to_columns(
            jnp.concatenate(
                [part.reshape(rows_here - reps * share, groups, -1) for part in (last_gate, last_up)],
                -1,
            )
        ).reshape(groups, rows_here - reps * share, -1)
    else:
        normed_one = gather(rms_normed(x_flat, attn_gain).astype(bf16))
        cols_qkv = to_columns(
            jnp.concatenate([per_group(w_query), per_kv_head(w_key), per_kv_head(w_value)], -1)
        )
        cols_gate_up = to_columns(jnp.concatenate([per_group(w_gate), per_group(w_up)], -1))
    qkv = matmul_f32(normed_one, cols_qkv)
    attended, query, key, value, lse, attended_placed = attend(
        cut_order, qkv, cosine, sine, piece_ids, piece_col, heads
    )
    if near:
        mid = product_scattered(attended, w_out, False, base=x_rows, number=2)[0]
    else:
        mid = x_flat + scatter(attended, w_out, False)
    grad_out = cotangent.reshape(local_rows, model_width)

    def back_through_attention(grad_attended, **line):
        return attend_back(
            cut_order, grad_attended, attended_placed, query, key, value, lse, cosine, sine,
            piece_ids, piece_col, heads, **line,
        )

    q_here = heads * HD
    if near:
        normed_two, hidden, up_part, gate_part, cols_gate_up = feed_forward(
            mid, ffn_gain, spread, rest, number=3
        )
        cols_gate_up = cols_gate_up.reshape(model_width, -1)
        grad_gate_up, down_term = feed_forward_back(
            grad_out, w_down, hidden, up_part, gate_part, number=4
        )
        high = rows_here // GATE_UP
        sums = Sums((8, high, model_width))
        terms = {"down": down_term.reshape((DOWN,) + sums.shape)}

        def pick_whole(number):
            return "down", lambda ref: ref.at[number]

        def pick_rows(name, number):
            return name, lambda ref: ref.at[:, number * high : (number + 1) * high, :]

        picks = [pick_whole(n) for n in range(DOWN)]
        picks += [pick_rows("gate_up", n) for n in range(GATE_UP)]
        picks += [pick_rows("out", n) for n in range(OUT)]

        def line(number, ticks):
            names = sorted(
                {picks[t][0] for t in range(sums.tick, sums.tick + ticks) if t < len(picks)}
            )
            return dict(
                number=number, ticks=ticks, sums=sums, picks=dict(enumerate(picks)),
                arrays=[(name, terms[name]) for name in names],
            )

        result, terms["gate_up"] = product_scattered(
            hidden, w_down, False, extra=(normed_two, grad_gate_up), base=mid, dtype=bf16,
            **line(5, 5),
        )
        grad_mid, gain_ffn_term = product_scattered(
            grad_gate_up, cols_gate_up, True, back=(grad_out, mid, ffn_gain), **line(6, 5)
        )
        grad_attended, out_term = attended_back(grad_mid, w_out, attended, **line(7, 4))
        terms["out"] = out_term.reshape(8, OUT * high, model_width)
        grad_qkv = back_through_attention(grad_attended, **line(8, 3))
        grad_x, gain_attn_term, qkv_term = product_scattered(
            grad_qkv, cols_qkv, True, extra=(normed_one, None), dtype=bf16,
            back=(grad_mid, x_rows, attn_gain), **line(9, 4),
        )
        gains = jnp.stack([gain_attn_term, gain_ffn_term]).reshape(2, groups, rows_here)
        gains = jnp.pad(jnp.moveaxis(gains, 0, 1), ((0, 0), (0, 6), (0, 0)))
        rest = line(10, CHUNKS + 4 - sums.tick)
        gate_rows, up_rows, qkv_rows, own_gains = tail(
            qkv_term.reshape(8, 8, 2 * high, -1), gains,
            {c: sums.done[c] for c in sums.done if c >= DOWN}, hidden_here, **rest,
        )
        straight = [n for n in range(CHUNKS) if n < DOWN or n >= DOWN + GATE_UP]
        weight_grads = finish([sums.done[n] for n in straight], gate_rows, up_rows, heads)
        shaped = tuple(rows.reshape(layer_input.shape) for rows in (result, grad_x))
        return shaped + tuple(weight_grads) + (own_gains[0], own_gains[1])

    unit_one = x_flat * inv_one
    inv_two = lax.rsqrt(jnp.mean(mid * mid, -1, keepdims=True) + EPS)
    unit_two = mid * inv_two
    normed_two = gather((unit_two * ffn_gain).astype(bf16))
    grad_all = gather(grad_out)
    gate_up = matmul_f32(normed_two, cols_gate_up)
    gate_proj, up_proj = gate_up[:, :hidden_here], gate_up[:, hidden_here:]
    sigmoid_gate = jax.nn.sigmoid(gate_proj)
    swish = gate_proj * sigmoid_gate
    hidden = (swish * up_proj).astype(bf16)
    gate_part = up_proj * sigmoid_gate * (1.0 + gate_proj * (1.0 - sigmoid_gate))
    down_term = over_tokens(hidden, grad_all).astype(bf16)
    grad_hidden = against_rows(grad_all, w_down)
    grad_gate_up = jnp.concatenate([grad_hidden * gate_part, grad_hidden * swish], 1).astype(bf16)
    grad_mid, gain_ffn_term = norm_back(
        grad_out.astype(f32), scatter(grad_gate_up, cols_gate_up, True), unit_two, inv_two, gain_ffn
    )
    grad_mid_low = gather(grad_mid.astype(bf16))
    grad_qkv = back_through_attention(against_rows(grad_mid_low, w_out).astype(bf16))
    grad_x, gain_attn_term = norm_back(
        grad_mid, scatter(grad_qkv, cols_qkv, True), unit_one, inv_one, gain_attn
    )

    def to_rows(term):
        return lax.all_to_all(
            term.astype(bf16).reshape(groups, rows_here, -1), "grp", 0, 0, tiled=True
        )

    def whole_rows(term):
        return jnp.moveaxis(term, 0, 1).reshape(rows_here, -1)

    def kv_rows(term):
        return jnp.sum(
            jnp.moveaxis(term, 0, 1).reshape(rows_here, kv_heads, copies, HD), 2
        ).reshape(rows_here, -1)

    gate_up_term = sum_over_sequences(to_rows(over_tokens(normed_two, grad_gate_up)))
    out_term = sum_over_sequences(over_tokens(attended, grad_mid_low).astype(bf16))
    qkv_term = sum_over_sequences(to_rows(over_tokens(normed_one, grad_qkv)))
    gain_total = lax.psum(jnp.stack([gain_attn_term, gain_ffn_term]), ("grp", "rep"))
    own_gains = lax.dynamic_slice_in_dim(gain_total, own_index * rows_here, rows_here, 1)
    return (
        (mid + scatter(hidden, w_down, False)).astype(bf16).reshape(layer_input.shape),
        grad_x.astype(bf16).reshape(layer_input.shape),
        whole_rows(qkv_term[..., :q_here]),
        kv_rows(qkv_term[..., q_here : q_here + HD]),
        kv_rows(qkv_term[..., q_here + HD :]),
        out_term,
        whole_rows(gate_up_term[..., :hidden_here]),
        whole_rows(gate_up_term[..., hidden_here:]),
        sum_over_sequences(down_term),
        own_gains[0],
        own_gains[1],
    )


def solution(mesh):
    tokens, table, rows, whole = P("rep", "grp", None), P("rep", None), P("grp", None), P()
    return jax.shard_map(
        on_device,
        mesh=mesh,
        in_specs=(tokens, tokens, table, table) + (rows,) * 7 + (whole,) * 2,
        out_specs=(tokens, tokens) + (rows,) * 7 + (P("grp"),) * 2,
        check_vma=False,
    )
```

```python
import functools

import jax
import jax.numpy as jnp
import numpy as np
from jax import lax
from jax.experimental import pallas as pl
from jax.experimental.pallas import tpu as pltpu
from jax.sharding import PartitionSpec as P

HD = 128
EPS = 1e-05
ROPE_BASE = 1000000.0
SCORE_SCALE = HD**-0.5
LOG2E = 1.4426950408889634
TO_EXP2 = SCORE_SCALE * LOG2E
NEG = -1e30

MESH = pl.DeviceIdType.MESH
f32 = jnp.float32
bf16 = jnp.bfloat16


def matmul_f32(first, second):
    return jnp.dot(first, second, preferred_element_type=f32)


def against_rows(first, second):
    return lax.dot_general(first, second, (((1,), (1,)), ((), ())), preferred_element_type=f32)


def over_tokens(first, second):
    return lax.dot_general(first, second, (((0,), (0,)), ((), ())), preferred_element_type=f32)


def turn_tables(length):
    half_size = HD // 2
    inverse = np.float32(ROPE_BASE) ** (-(np.arange(half_size, dtype=np.float32) * 2) / HD)
    angles = np.arange(length, dtype=np.float32)[:, None] * inverse.astype(np.float32)
    cosine, sine = np.cos(angles), np.sin(angles)
    tables = np.concatenate([cosine, cosine], -1), np.concatenate([-sine, sine], -1)
    return tuple(jnp.asarray(table.astype(np.float32)) for table in tables)


def norm_back(upstream, grad_normed, unit_rows, inv_root, gain):
    scaled = grad_normed * gain
    center_term = jnp.mean(scaled * unit_rows, -1, keepdims=True)
    return (
        upstream + inv_root * (scaled - unit_rows * center_term),
        jnp.sum(grad_normed * unit_rows, 0),
    )


def fold_lanes(values, op):
    out = values[:, :HD]
    for at in range(HD, values.shape[1], HD):
        out = op(out, values[:, at : at + HD])
    return out


def as_column(row):
    return jnp.broadcast_to(row, (HD, row.shape[1])).T[:, 0:1]


def as_row(column):
    return jnp.broadcast_to(column, (column.shape[0], HD)).T[0:1, :]


def attend_kernel(
    heads, cuts, block,
    order_ref, rows_hbm, weight_hbm, cos_ref, sin_ref, piece_ref,
    out_ref, q_ref, k_ref, v_ref, lse_ref, placed,
    scores, rows_ref, weight_ref, qkv_ref, sems,
):
    length = rows_ref.shape[0]
    cut = length // cuts
    blocks = length // block
    loads = [pltpu.make_async_copy(weight_hbm, weight_ref, sems.at[blocks])]
    for i in range(blocks):
        at = slice(i * block, (i + 1) * block)
        loads.append(pltpu.make_async_copy(rows_hbm.at[at, :], rows_ref.at[at, :], sems.at[i]))
    for load in loads:
        load.start()

    def place_cut(r, first):
        src = pl.ds(pl.multiple_of(r * cut, cut), cut)
        dst = pl.ds(pl.multiple_of(order_ref[0, first + r] * cut, cut), cut)
        cosine, sine = cos_ref[dst, :], sin_ref[dst, :]
        for h in range(heads + 1):
            part = qkv_ref[src, h * HD : (h + 1) * HD]
            turned = (part * cosine + pltpu.roll(part, HD // 2, 1) * sine).astype(bf16)
            if h < heads:
                q_ref[h, dst, :] = turned
            else:
                k_ref[dst, :] = turned
        v_ref[dst, :] = qkv_ref[src, (heads + 1) * HD :].astype(bf16)
        return first

    loads[0].wait()
    for i in range(blocks):
        loads[1 + i].wait()
        qkv_ref[...] = matmul_f32(rows_ref[i * block : (i + 1) * block, :], weight_ref[...])
        lax.fori_loop(0, block // cut, place_cut, i * (block // cut))

    def one_block(i, _):
        rows = pl.ds(pl.multiple_of(i * block, block), block)
        query = q_ref[:, rows, :].reshape(heads * block, HD)

        def score(j, high):
            cols = pl.ds(pl.multiple_of(j * block, block), block)
            tile = against_rows(query, k_ref[cols, :])
            scores[j] = tile
            return jnp.maximum(high, fold_lanes(tile, jnp.maximum))

        high = lax.fori_loop(0, i, score, jnp.full((heads * block, HD), NEG, f32))
        tile = against_rows(query, k_ref[rows, :])
        q_at = lax.broadcasted_iota(jnp.int32, (block, block), 0)
        k_at = lax.broadcasted_iota(jnp.int32, (block, block), 1)
        k_piece = piece_ref[0:1, rows].astype(f32)
        q_piece = as_column(k_piece)
        allowed = (k_at <= q_at) | ((q_piece != 0) & (q_piece == k_piece))
        tile = jnp.concatenate(
            [jnp.where(allowed, tile[h * block : (h + 1) * block], NEG) for h in range(heads)], 0
        )
        scores[i] = tile
        high = jnp.max(jnp.maximum(high, fold_lanes(tile, jnp.maximum)), 1, keepdims=True)

        def weigh(j, state):
            total, mixed = state
            cols = pl.ds(pl.multiple_of(j * block, block), block)
            prob = jnp.exp2((scores[j] - high) * TO_EXP2)
            total = total + fold_lanes(prob, jnp.add)
            return total, mixed + matmul_f32(prob.astype(bf16), v_ref[cols, :])

        zero = jnp.zeros((heads * block, HD), f32)
        total, mixed = lax.fori_loop(0, i + 1, weigh, (zero, zero))
        total = jnp.sum(total, 1, keepdims=True)
        mixed = (mixed / total).astype(bf16)
        log_total = high * TO_EXP2 + jnp.log2(total)
        for h in range(heads):
            placed[rows, h * HD : (h + 1) * HD] = mixed[h * block : (h + 1) * block]
            lse_ref[h : h + 1, rows] = as_row(log_total[h * block : (h + 1) * block])
        return 0

    lax.fori_loop(0, blocks, one_block, 0)

    def store_cut(r, _):
        dst = pl.ds(pl.multiple_of(r * cut, cut), cut)
        src = pl.ds(pl.multiple_of(order_ref[0, r] * cut, cut), cut)
        out_ref[dst, :] = placed[src, :]
        return 0

    lax.fori_loop(0, cuts, store_cut, 0)


def vmem_specs(count):
    return [pl.BlockSpec(memory_space=pltpu.VMEM)] * count


def attend(order, rows, weight, cosine, sine, piece, heads):
    length, width = rows.shape
    block = min(512, length)
    return pl.pallas_call(
        functools.partial(attend_kernel, heads, order.shape[1], block),
        out_shape=(
            jax.ShapeDtypeStruct((length, heads * HD), bf16),
            jax.ShapeDtypeStruct((heads, length, HD), bf16),
            jax.ShapeDtypeStruct((length, HD), bf16),
            jax.ShapeDtypeStruct((length, HD), bf16),
            jax.ShapeDtypeStruct((heads, length), f32),
            jax.ShapeDtypeStruct((length, heads * HD), bf16),
        ),
        in_specs=[pl.BlockSpec(memory_space=pltpu.SMEM)]
        + [pl.BlockSpec(memory_space=pl.ANY)] * 2
        + vmem_specs(3),
        out_specs=tuple(vmem_specs(6)),
        scratch_shapes=[
            pltpu.VMEM((length // block, heads * block, block), f32),
            pltpu.VMEM(rows.shape, bf16),
            pltpu.VMEM(weight.shape, bf16),
            pltpu.VMEM((block, weight.shape[1]), f32),
            pltpu.SemaphoreType.DMA((length // block + 1,)),
        ],
        compiler_params=pltpu.CompilerParams(vmem_limit_bytes=60 * 2**20),
        cost_estimate=pl.CostEstimate(
            flops=3 * heads * length * length * HD + 2 * length * width * weight.shape[1],
            bytes_accessed=10 * length * HD * heads * 4 + rows.size * 2,
            transcendentals=heads * length * length // 2,
        ),
    )(order, rows, weight, cosine, sine, piece)


DOWN, GATE_UP, OUT, QKV = 8, 16, 2, 12
CHUNKS = DOWN + GATE_UP + OUT + QKV


def is_chunk(number):
    return 0 <= number < CHUNKS


def chunk_shape(shape, number):
    left = CHUNKS - number
    return shape[:2] + (shape[2] // (4 if left <= 8 else 2 if left <= QKV else 1),)


def qkv_parts(width):
    return [
        (half, low, n * (width // parts), width // parts)
        for half, parts in ((0, 2), (1, 4))
        for low in (0, 1)
        for n in range(parts)
    ]


def is_middle():
    rank = lax.axis_index("rep")
    return (rank == 1) | (rank == 2)


def is_end():
    rank = lax.axis_index("rep")
    return (rank == 0) | (rank == 3)


class NoLine:
    ticks = 0

    def signal(self, barrier):
        pass

    def greet(self, barrier, others):
        if others:
            pl.semaphore_wait(barrier, others)

    def start(self):
        pass

    def step(self):
        pass

    def end(self):
        pass


class Line:
    def __init__(self, first, ticks, picks, refs, outs, scratch):
        self.first, self.ticks, self.picks, self.refs, self.outs = first, ticks, picks, refs, outs
        (
            self.inward, self.across, self.own, self.pair, self.total, self.sems, self.local,
            self.carries,
        ) = scratch
        rank = lax.axis_index("rep")
        self.partner = {"rep": rank + 1 - 2 * (rank % 2)}
        self.peer = {"rep": 3 - rank}
        self.now = 0
        self.kept = []

    def signal(self, barrier):
        pl.semaphore_signal(barrier, inc=1, device_id=self.partner, device_id_type=MESH)

        @pl.when(is_middle())
        def _():
            pl.semaphore_signal(barrier, inc=1, device_id=self.peer, device_id_type=MESH)

    def greet(self, barrier, others):
        @pl.when(is_middle())
        def _():
            pl.semaphore_wait(barrier, others + 2)

        @pl.when(is_end())
        def _():
            pl.semaphore_wait(barrier, others + 1)

    def remote(self, hop, number, src, dst, device):
        return pltpu.make_async_remote_copy(
            src_ref=src, dst_ref=dst, send_sem=self.sems.at[0, hop, number],
            recv_sem=self.sems.at[1, hop, number], device_id=device, device_id_type=MESH,
        )

    def part(self, ref, at, chunk):
        width = chunk_shape(ref.shape[1:], chunk)[2]
        return ref.at[at] if width == ref.shape[3] else ref.at[at, :, :, :width]

    def hops(self, number):
        tick = self.first + number
        term = pair = total = None
        if is_chunk(tick):
            which, pick = self.picks[tick]
            term = (
                lambda: self.remote(
                    0, number, pick(self.refs[which]), self.part(self.inward, number, tick), self.partner
                ),
                lambda: pltpu.make_async_copy(
                    pick(self.refs[which]), self.part(self.own, tick % 2, tick), self.local.at[0, number]
                ),
            )
        if is_chunk(tick - 2):
            before = (
                self.refs[f"pair{number}"]
                if number < 2
                else self.part(self.pair, (tick - 2) % 3, tick - 2)
            )
            pair = (
                lambda: self.remote(1, number, before, self.part(self.across, number, tick - 2), self.peer),
                lambda: pltpu.make_async_copy(
                    before, self.part(self.pair, (tick - 2) % 3, tick - 2), self.carries.at[number]
                ),
            )
        if is_chunk(tick - 4):
            done = (
                self.refs[f"total{number}"]
                if number < 2
                else self.part(self.total, (tick - 4) % 3, tick - 4)
            )
            slot = self.outs[tick - 4]
            total = (
                lambda: self.remote(2, number, done, slot, self.partner),
                lambda: pltpu.make_async_copy(done, slot, self.local.at[1, number]),
            )
        return term, pair, total

    def open(self, number):
        term, pair, total = self.hops(number)

        @pl.when(is_end())
        def _():
            if term:
                term[0]().start()

        @pl.when(is_middle())
        def _():
            if pair:
                pair[0]().start()
            if total:
                total[0]().start()
            if term:
                term[1]().start()
            if total:
                total[1]().start()
            if pair and number < 2:
                pair[1]().start()

    def close(self, number):
        term, pair, total = self.hops(number)

        @pl.when(is_end())
        def _():
            if term:
                term[0]().wait_send()
            if total:
                total[0]().wait_recv()

        @pl.when(is_middle())
        def _():
            if total:
                total[0]().wait_send()
                total[1]().wait()
            if pair:
                pair[0]().wait_send()
                pair[0]().wait_recv()
            if term:
                term[0]().wait_recv()

    def add(self, number):
        term, pair, _ = self.hops(number)
        tick = self.first + number

        def sum_of(into, first, second):
            def one(g, _):
                into[g] = (first[g].astype(f32) + second[g].astype(f32)).astype(bf16)
                return 0

            lax.fori_loop(0, into.shape[0], one, 0)

        @pl.when(is_middle())
        def _():
            if pair:
                if number < 2:
                    pair[1]().wait()
                sum_of(
                    self.part(self.total, (tick - 2) % 3, tick - 2),
                    self.part(self.pair, (tick - 2) % 3, tick - 2),
                    self.part(self.across, number, tick - 2),
                )
            if term:
                term[1]().wait()
                sum_of(
                    self.part(self.pair, tick % 3, tick), self.part(self.own, tick % 2, tick),
                    self.part(self.inward, number, tick),
                )

    def keep(self, number):
        tick = self.first + number
        which = number - (self.ticks - 2)
        made = []
        if is_chunk(tick):
            made.append((self.pair.at[tick % 3], self.outs[f"pair{which}"], 2 + which))
        if is_chunk(tick - 2):
            made.append((self.total.at[(tick - 2) % 3], self.outs[f"total{which}"], 4 + which))
        copies = [
            lambda src=src, dst=dst, at=at: pltpu.make_async_copy(src, dst, self.carries.at[at])
            for src, dst, at in made
        ]

        @pl.when(is_middle())
        def _():
            for copy in copies:
                copy().start()

        self.kept += copies

    def start(self):
        self.open(0)
        if self.ticks > 1:
            self.open(1)

    def step(self):
        if self.now + 2 < self.ticks:
            self.settle()
            self.open(self.now + 1)

    def settle(self):
        self.close(self.now)
        self.add(self.now)
        if self.now >= self.ticks - 2:
            self.keep(self.now)
        self.now += 1

    def end(self):
        while self.now + 2 < self.ticks:
            self.step()
        while self.now < self.ticks:
            self.settle()

        @pl.when(is_middle())
        def _():
            for copy in self.kept:
                copy().wait()


def line_slots(first, ticks):
    return [t - 4 for t in range(first, first + ticks) if is_chunk(t - 4)]


class Sums:
    def __init__(self, shape):
        self.shape, self.tick, self.kept, self.done = shape, 0, {}, {}


def run(kernel, ins, outs, scratch, number, cost, sums=None, ticks=0, arrays=(), picks=None, vmem=58):
    ins, outs, scratch = list(ins), list(outs), list(scratch)
    counts = (len(ins), len(outs), len(scratch))
    first = sums.tick if ticks else 0
    names_in, names_out = [], []
    if ticks:
        last = first + ticks - 1
        for name, array in arrays:
            names_in.append(name)
            ins.append((array, pl.ANY))
        for which in (0, 1):
            for name, chunk_at in ((f"pair{which}", first - 2), (f"total{which}", first - 4)):
                if is_chunk(chunk_at + which):
                    names_in.append(name)
                    ins.append((sums.kept[name], pl.ANY))
        names_out = line_slots(first, ticks)
        for which in (0, 1):
            for name, chunk_at in ((f"pair{which}", last - 1), (f"total{which}", last - 3)):
                if is_chunk(chunk_at + which):
                    names_out.append(name)
        slots = line_slots(first, ticks)
        outs += [
            (
                jax.ShapeDtypeStruct(
                    chunk_shape(sums.shape, name) if name in slots else sums.shape, bf16
                ),
                pl.ANY,
            )
            for name in names_out
        ]
        scratch += [
            pltpu.VMEM((ticks,) + sums.shape, bf16),
            pltpu.VMEM((ticks,) + sums.shape, bf16),
            pltpu.VMEM((2,) + sums.shape, bf16),
            pltpu.VMEM((3,) + sums.shape, bf16),
            pltpu.VMEM((3,) + sums.shape, bf16),
            pltpu.SemaphoreType.DMA((2, 3, ticks)),
            pltpu.SemaphoreType.DMA((2, ticks)),
            pltpu.SemaphoreType.DMA((6,)),
        ]

    def body(*refs):
        in_refs, rest = refs[: len(ins)], refs[len(ins) :]
        out_refs, scratch_refs = rest[: len(outs)], rest[len(outs) :]
        line = NoLine()
        if ticks:
            line = Line(
                first, ticks, picks, dict(zip(names_in, in_refs[counts[0] :])),
                dict(zip(names_out, out_refs[counts[1] :])), scratch_refs[counts[2] :],
            )
        kernel(in_refs[: counts[0]], out_refs[: counts[1]], scratch_refs[: counts[2]], line)

    results = pl.pallas_call(
        body,
        out_shape=tuple(shape for shape, _ in outs),
        in_specs=[pl.BlockSpec(memory_space=space) for _, space in ins],
        out_specs=tuple(pl.BlockSpec(memory_space=space) for _, space in outs),
        scratch_shapes=scratch,
        compiler_params=pltpu.CompilerParams(
            vmem_limit_bytes=vmem * 2**20,
            **({} if number is None else {"collective_id": number, "has_side_effects": True}),
        ),
        cost_estimate=pl.CostEstimate(
            flops=cost[0], bytes_accessed=cost[1], transcendentals=cost[2]
        ),
    )(*[array for array, _ in ins])
    for name, result in zip(names_out, results[counts[1] :]):
        if name in line_slots(first, ticks):
            sums.done[name] = result
        else:
            sums.kept[name] = result
    if ticks:
        sums.tick += ticks
    return results[: counts[1]]


SMEM, VMEM, ANY = pltpu.SMEM, pltpu.VMEM, pl.ANY


def attend_back_kernel(
    heads, block, ins, outs, scratch, line
):
    grad_ref, out_ref, q_ref, k_ref, v_ref, lse_ref, cos_ref, sin_ref, piece_ref = ins
    (grad_qkv_ref,) = outs
    grads, centers, grad_q = scratch
    if line.ticks:
        line.signal(pltpu.get_barrier_semaphore())
        line.greet(pltpu.get_barrier_semaphore(), 0)
        line.start()
    length = grad_ref.shape[0]
    blocks = length // block

    def take_block(i, _):
        rows = pl.ds(pl.multiple_of(i * block, block), block)
        for h in range(heads):
            grad = grad_ref[rows, h * HD : (h + 1) * HD].astype(bf16)
            grads[h, rows, :] = grad
            product = grad.astype(f32) * out_ref[rows, h * HD : (h + 1) * HD].astype(f32)
            centers[h, rows, :] = jnp.broadcast_to(
                jnp.sum(product, 1, keepdims=True), (block, HD)
            )
        return 0

    lax.fori_loop(0, blocks, take_block, 0)
    grad_q[...] = jnp.zeros_like(grad_q)

    def key_block(j, _):
        cols = pl.ds(pl.multiple_of(j * block, block), block)
        key, value = k_ref[cols, :], v_ref[cols, :]

        def one(i, state, diagonal):
            grad_key, grad_value = state
            rows = pl.ds(pl.multiple_of(i * block, block), block)
            for h in range(heads):
                query, grad = q_ref[h, rows, :], grads[h, rows, :]
                log_total = lse_ref[h : h + 1, rows]
                center = centers[h, rows, :].T[0:1, :]
                prob = jnp.exp2(against_rows(key, query) * TO_EXP2 - log_total)
                if diagonal:
                    k_at = lax.broadcasted_iota(jnp.int32, (block, block), 0)
                    q_at = lax.broadcasted_iota(jnp.int32, (block, block), 1)
                    q_piece = piece_ref[0:1, cols].astype(f32)
                    k_piece = as_column(q_piece)
                    allowed = (k_at <= q_at) | ((q_piece != 0) & (q_piece == k_piece))
                    prob = jnp.where(allowed, prob, 0.0)
                grad_prob = against_rows(value, grad)
                grad_score = (prob * (grad_prob - center)).astype(bf16)
                grad_value = grad_value + matmul_f32(prob.astype(bf16), grad)
                grad_key = grad_key + matmul_f32(grad_score, query)
                grad_q[h, rows, :] += over_tokens(grad_score, key)
            return grad_key, grad_value

        zero = jnp.zeros((block, HD), f32)
        state = one(j, (zero, zero), True)
        grad_key, grad_value = lax.fori_loop(
            j + 1, blocks, functools.partial(one, diagonal=False), state
        )
        grad_key = grad_key * SCORE_SCALE
        grad_key = grad_key * cos_ref[cols, :] - pltpu.roll(grad_key, HD // 2, 1) * sin_ref[cols, :]
        grad_qkv_ref[cols, heads * HD : (heads + 1) * HD] = grad_key.astype(bf16)
        grad_qkv_ref[cols, (heads + 1) * HD :] = grad_value.astype(bf16)
        return 0

    for j in range(min(2, blocks - 1)):
        lax.fori_loop(j, j + 1, key_block, 0)
        line.step()
    lax.fori_loop(min(2, blocks - 1), blocks, key_block, 0)

    def turn_back(i, _):
        rows = pl.ds(pl.multiple_of(i * block, block), block)
        for h in range(heads):
            grad = grad_q[h, rows, :] * SCORE_SCALE
            grad = grad * cos_ref[rows, :] - pltpu.roll(grad, HD // 2, 1) * sin_ref[rows, :]
            grad_qkv_ref[rows, h * HD : (h + 1) * HD] = grad.astype(bf16)
        return 0

    lax.fori_loop(0, blocks, turn_back, 0)
    line.end()


def take_cuts_kernel(cuts, holder_ref, rows_ref, out_ref):
    cut = out_ref.shape[0] // cuts

    def one(p, _):
        src = pl.ds(pl.multiple_of(holder_ref[0, p] * cut, cut), cut)
        out_ref[pl.ds(pl.multiple_of(p * cut, cut), cut), :] = rows_ref[src, :]
        return 0

    lax.fori_loop(0, cuts, one, 0)


def take_cuts(holder, rows):
    return pl.pallas_call(
        functools.partial(take_cuts_kernel, holder.shape[1]),
        out_shape=jax.ShapeDtypeStruct(rows.shape, rows.dtype),
        in_specs=[pl.BlockSpec(memory_space=pltpu.SMEM)] + vmem_specs(1),
        out_specs=pl.BlockSpec(memory_space=pltpu.VMEM),
        cost_estimate=pl.CostEstimate(
            flops=0, bytes_accessed=2 * rows.size * rows.dtype.itemsize, transcendentals=0
        ),
    )(holder, rows)


def attend_back(
    order, grad, out, query, key, value, lse, cosine, sine, piece, heads, **line
):
    cuts = jnp.arange(order.shape[1], dtype=order.dtype)
    holder = jnp.sum(jnp.where(order[0][None, :] == cuts[:, None], cuts[None, :], 0), 1)[None, :]
    length = grad.shape[0]
    block = min(512, length)
    tall = [take_cuts(holder, grad), out, query, key, value, lse, cosine, sine, piece]
    grad_qkv = run(
        functools.partial(attend_back_kernel, heads, block),
        [(array, VMEM) for array in tall],
        [(jax.ShapeDtypeStruct((length, (heads + 2) * HD), bf16), VMEM)],
        [
            pltpu.VMEM((heads, length, HD), bf16),
            pltpu.VMEM((heads, length, HD), f32),
            pltpu.VMEM((heads, length, HD), f32),
        ],
        line.pop("number", None),
        (8 * heads * length * length * HD, 14 * length * HD * heads * 4, heads * length * length // 2),
        **line,
    )[0]
    return take_cuts(order, grad_qkv)


def place_in_group():
    me = lax.axis_index("grp")
    return me // 4, (me // 2) % 2, me % 2


def other(flip_y, flip_x, flip_core):
    y, x, core = place_in_group()
    return ((y + flip_y) % 2) * 4 + ((x + flip_x) % 2) * 2 + (core + flip_core) % 2


def chip_rows(flip_y, flip_x, rows):
    y, x, _ = place_in_group()
    first = (((y + flip_y) % 2) * 2 + (x + flip_x) % 2) * (2 * rows)
    return pl.ds(pl.multiple_of(first, 2 * rows), 2 * rows)


NEIGHBOURS = ((0, 0, 1), (0, 1, 0), (1, 0, 0))
EVERYONE = tuple((n // 4, (n // 2) % 2, n % 2) for n in range(1, 8))


def greet_group(line, flips=NEIGHBOURS, between=None):
    barrier = pltpu.get_barrier_semaphore()
    for flip in flips:
        pl.semaphore_signal(barrier, inc=1, device_id={"grp": other(*flip)}, device_id_type=MESH)
    line.signal(barrier)
    if between:
        between()
    line.greet(barrier, len(flips))


SIBLING, ALONG_X, ALONG_Y, ACROSS = (0, 0), (0, 1), (1, 0), (1, 1)


class Gather:
    TO_S, TO_X, TO_Y = (0, 0, 1), (0, 1, 0), (1, 0, 0)

    def __init__(self, rows, all_ref, sends, recvs):
        self.rows, self.all_ref, self.sends, self.recvs = rows, all_ref, sends, recvs
        self.started = []

    def copy(self, number, chip, core, part, target):
        first = other(*chip, core) * self.rows
        if part is None:
            where = pl.ds(pl.multiple_of(first, self.rows), self.rows)
        else:
            half = self.rows // 2
            where = pl.ds(pl.multiple_of(first + part * half, half), half)
        where = self.all_ref.at[where, :]
        return pltpu.make_async_remote_copy(
            src_ref=where, dst_ref=where, send_sem=self.sends.at[number],
            recv_sem=self.recvs.at[number], device_id={"grp": other(*target)}, device_id_type=MESH,
        )

    def send(self, *what):
        one = self.copy(*what)
        one.start()
        self.started.append(one)

    def landed(self, number, chip, core, part):
        self.copy(number, chip, core, part, self.TO_S).wait_recv()

    def send_own(self):
        self.send(1, SIBLING, 0, 1, self.TO_X)
        self.send(3, SIBLING, 0, 0, self.TO_Y)
        self.send(0, SIBLING, 0, None, self.TO_S)
        self.send(2, SIBLING, 0, 0, self.TO_X)
        self.send(4, SIBLING, 0, 1, self.TO_Y)

    def sibling(self):
        self.landed(0, SIBLING, 1, None)

    def relay(self):
        self.landed(1, ALONG_X, 0, 1)
        self.send(6, ALONG_X, 0, 1, self.TO_Y)
        self.landed(3, ALONG_Y, 0, 0)
        self.send(5, ALONG_Y, 0, 0, self.TO_X)
        self.send(7, ALONG_X, 0, 1, self.TO_S)
        self.send(8, ALONG_Y, 0, 0, self.TO_S)

    def pass_second(self):
        self.landed(2, ALONG_X, 0, 0)
        self.send(9, ALONG_X, 0, 0, self.TO_S)
        self.landed(4, ALONG_Y, 0, 1)
        self.send(10, ALONG_Y, 0, 1, self.TO_S)

    def along_x(self):
        self.landed(7, ALONG_X, 1, 1)
        self.landed(9, ALONG_X, 1, 0)

    def pass_across(self):
        self.landed(5, ACROSS, 0, 0)
        self.send(11, ACROSS, 0, 0, self.TO_S)
        self.landed(6, ACROSS, 0, 1)
        self.send(12, ACROSS, 0, 1, self.TO_S)

    def along_y(self):
        self.landed(8, ALONG_Y, 1, 0)
        self.landed(10, ALONG_Y, 1, 1)

    def across(self):
        self.landed(11, ACROSS, 1, 0)
        self.landed(12, ACROSS, 1, 1)

    def finish(self):
        for one in self.started:
            one.wait_send()


def gather_rows(rows, all_ref, sends, recvs, on_chip, line, then=None):
    rows_of = Gather(rows, all_ref, sends, recvs)
    rows_of.send_own()
    if then:
        then()
    rows_of.sibling()
    on_chip(*SIBLING)
    rows_of.relay()
    line.step()
    rows_of.pass_second()
    line.step()
    rows_of.along_x()
    on_chip(*ALONG_X)
    rows_of.pass_across()
    line.step()
    rows_of.along_y()
    on_chip(*ALONG_Y)
    rows_of.across()
    on_chip(*ACROSS)
    rows_of.finish()
    line.end()


GATHER_COPIES = 13


def rms_normed(values, gain):
    return values * lax.rsqrt(jnp.mean(values * values, -1, keepdims=True) + EPS) * gain


class Moves:
    def __init__(self, sems):
        self.sems, self.count, self.open = sems, 0, []

    def start(self, src, dst):
        one = pltpu.make_async_copy(src, dst, self.sems.at[self.count])
        self.count += 1
        one.start()
        return one

    def later(self, src, dst):
        self.open.append(self.start(src, dst))

    def finish(self):
        for one in self.open:
            one.wait()


def gather_scratch(rows, width, moves):
    return [
        pltpu.VMEM((8 * rows, width), bf16),
        pltpu.SemaphoreType.DMA((GATHER_COPIES,)),
        pltpu.SemaphoreType.DMA((GATHER_COPIES,)),
        pltpu.SemaphoreType.DMA((moves,)),
    ]


def own_rows(rows):
    return pl.ds(pl.multiple_of(other(0, 0, 0) * rows, rows), rows)


def send_columns(pieces, sends, recvs, moves):
    copies = []
    for which, (rows_ref, width, there) in enumerate(pieces):
        for number, flip in enumerate(EVERYONE):
            target = other(*flip)
            cols = pl.ds(pl.multiple_of(target * width, width), width)
            one = pltpu.make_async_remote_copy(
                src_ref=rows_ref.at[:, cols], dst_ref=there,
                send_sem=sends.at[which, number], recv_sem=recvs.at[which, number],
                device_id={"grp": target}, device_id_type=MESH,
            )
            one.start()
            copies.append(one)
        mine = pl.ds(pl.multiple_of(other(0, 0, 0) * width, width), width)
        moves.later(rows_ref.at[:, mine], there)
    return copies


def gather_normed_kernel(ins, outs, scratch, line):
    x_ref, gain_ref = ins[:2]
    weights = ins[2:]
    all_ref, cols_ref = outs
    held, sends, recvs, sems, col_sends, col_recvs = scratch
    rows = x_ref.shape[0]
    moves = Moves(sems)

    def fill():
        held[own_rows(rows), :] = rms_normed(x_ref[...].astype(f32), gain_ref[...]).astype(bf16)

    greet_group(line, EVERYONE, fill)
    col_copies = []

    def send_weights():
        pieces, low = [], 0
        tall = weights[0].shape[0]
        there = pl.ds(pl.multiple_of(other(0, 0, 0) * tall, tall), tall)
        for weight in weights:
            width = weight.shape[1] // 8
            pieces.append((weight, width, cols_ref.at[there, low : low + width]))
            low += width
        col_copies.extend(send_columns(pieces, col_sends, col_recvs, moves))

    def on_chip(*chip):
        where = chip_rows(*chip, rows)
        moves.later(held.at[where, :], all_ref.at[where, :])

    gather_rows(rows, held, sends, recvs, on_chip, line, send_weights)
    for one in col_copies:
        one.wait()
    moves.finish()


def gather_normed(x, gain, weights, **line):
    rows, width = x.shape
    deep = sum(weight.shape[1] for weight in weights) // 8
    return run(
        gather_normed_kernel,
        [(x, VMEM), (gain, VMEM)] + [(weight, ANY) for weight in weights],
        [
            (jax.ShapeDtypeStruct((8 * rows, width), bf16), ANY),
            (jax.ShapeDtypeStruct((8 * weights[0].shape[0], deep), bf16), ANY),
        ],
        gather_scratch(rows, width, 4 + len(weights))
        + [pltpu.SemaphoreType.DMA((len(weights), 7))] * 2,
        line.pop("number"),
        (0, 150 * rows * width * 2, 0),
        **line,
    )


def columns_kernel(rows_here, ins, outs, scratch, line):
    (cols_ref,) = outs
    sends, recvs, sems = scratch
    moves = Moves(sems)
    barrier = pltpu.get_barrier_semaphore()
    for flip in EVERYONE:
        pl.semaphore_signal(barrier, inc=1, device_id={"grp": other(*flip)}, device_id_type=MESH)
    pl.semaphore_wait(barrier, 7)
    first = pl.multiple_of(lax.axis_index("rep") * rows_here, rows_here)
    me = other(0, 0, 0)
    pieces, low = [], 0
    for weight in ins:
        width = weight.shape[1] // 8
        pieces.append(
            (weight.at[pl.ds(first, rows_here), :], width, cols_ref.at[me, :, low : low + width])
        )
        low += width
    for one in send_columns(pieces, sends, recvs, moves):
        one.wait()
    moves.finish()


def columns_of_some(weights, rows_here, number):
    deep = sum(weight.shape[1] for weight in weights) // 8
    return run(
        functools.partial(columns_kernel, rows_here),
        [(weight, ANY) for weight in weights],
        [(jax.ShapeDtypeStruct((8, rows_here, deep), bf16), ANY)],
        [pltpu.SemaphoreType.DMA((len(weights), 7))] * 2
        + [pltpu.SemaphoreType.DMA((len(weights),))],
        number, (0, 50 * 8 * rows_here * deep, 0),
    )[0]


def feed_forward_kernel(tile, ins, outs, scratch, line):
    mid_ref, gain_ref, grad_ref, spread_ref, rest_ref, w_down_ref = ins
    all_ref, hidden_ref, whole_ref, grad_gate_up_ref, down_ref = outs
    held, grads_held, sends, recvs, grad_sends, grad_recvs, sems = scratch[:7]
    weight, w_down, hidden, up_part, gate_part, grads, down = scratch[7:]
    rows = mid_ref.shape[0]
    inner = hidden.shape[1]
    moves = Moves(sems)
    planes, _, tall, _ = spread_ref.shape
    loads = [
        moves.start(spread_ref.at[z], weight.at[:, z * tall : (z + 1) * tall, :])
        for z in range(planes)
    ]
    loads.append(moves.start(rest_ref, weight.at[:, planes * tall :, :]))
    down_load = moves.start(w_down_ref, w_down)

    def fill():
        held[own_rows(rows), :] = rms_normed(mid_ref[...], gain_ref[...]).astype(bf16)
        grads_held[own_rows(rows), :] = grad_ref[...]

    greet_group(line, between=fill)
    first = Gather(rows, held, sends, recvs)
    second = Gather(rows, grads_held, grad_sends, grad_recvs)
    stored = []

    def forward(*chip):
        where = chip_rows(*chip, rows)
        moves.later(held.at[where, :], all_ref.at[where, :])

        def column(t, _):
            cols = pl.ds(pl.multiple_of(t * tile, tile), tile)
            up_cols = pl.ds(pl.multiple_of(inner + t * tile, tile), tile)
            lhs = held[where, :]
            gate = matmul_f32(lhs, weight[:, :, cols].reshape(-1, tile))
            up = matmul_f32(lhs, weight[:, :, up_cols].reshape(-1, tile))
            sigma = 1.0 / (1.0 + jnp.exp(-gate))
            swish = gate * sigma
            hidden[where, cols] = (swish * up).astype(bf16)
            up_part[where, cols] = swish.astype(bf16)
            gate_part[where, cols] = (up * sigma * (1.0 + gate * (1.0 - sigma))).astype(bf16)
            return 0

        lax.fori_loop(0, inner // tile, column, 0)
        moves.later(hidden.at[where, :], hidden_ref.at[where, :])

    def backward(*chip):
        where = chip_rows(*chip, rows)
        slot = len(stored) % 2
        if len(stored) >= 2:
            stored[len(stored) - 2].wait()

        def column(t, _):
            cols = pl.ds(pl.multiple_of(t * tile, tile), tile)
            up_cols = pl.ds(pl.multiple_of(inner + t * tile, tile), tile)
            incoming = grads_held[where, :]
            grad_hidden = against_rows(incoming, w_down[cols, :])
            grads[slot, :, cols] = (grad_hidden * gate_part[where, cols].astype(f32)).astype(bf16)
            grads[slot, :, up_cols] = (grad_hidden * up_part[where, cols].astype(f32)).astype(bf16)
            term = over_tokens(hidden[where, cols], incoming)
            if chip == SIBLING:
                down[cols, :] = term
            elif chip == ACROSS:
                weight[t] = (down[cols, :] + term).astype(bf16)
            else:
                down[cols, :] += term
            return 0

        lax.fori_loop(0, inner // tile, column, 0)
        stored.append(moves.start(grads.at[slot], grad_gate_up_ref.at[where, :]))

    first.send_own()
    for one in loads:
        one.wait()
    whole = moves.start(weight, whole_ref)
    first.sibling()
    forward(*SIBLING)
    first.relay()
    first.pass_second()
    second.send_own()
    first.along_x()
    forward(*ALONG_X)
    first.pass_across()
    first.along_y()
    forward(*ALONG_Y)
    second.relay()
    first.across()
    forward(*ACROSS)
    down_load.wait()
    second.sibling()
    backward(*SIBLING)
    second.pass_second()
    second.along_x()
    backward(*ALONG_X)
    second.pass_across()
    second.along_y()
    backward(*ALONG_Y)
    second.across()
    whole.wait()
    backward(*ACROSS)
    moves.later(weight.at[: inner // tile], down_ref)
    first.finish()
    second.finish()
    for one in stored[-2:]:
        one.wait()
    moves.finish()


def feed_forward(mid, gain, grad, spread, rest, w_down, **line):
    rows, width = mid.shape
    inner = w_down.shape[0]
    weight = (8, width // 8, 2 * inner)
    return run(
        functools.partial(feed_forward_kernel, weight[1]),
        [(mid, VMEM), (gain, VMEM), (grad, VMEM), (spread, ANY), (rest, ANY), (w_down, ANY)],
        [
            (jax.ShapeDtypeStruct((8 * rows, width), bf16), ANY),
            (jax.ShapeDtypeStruct((8 * rows, inner), bf16), ANY),
            (jax.ShapeDtypeStruct(weight, bf16), ANY),
            (jax.ShapeDtypeStruct((8 * rows, 2 * inner), bf16), ANY),
            (jax.ShapeDtypeStruct((inner // weight[1], weight[1], width), bf16), ANY),
        ],
        [pltpu.VMEM((8 * rows, width), bf16)] * 2
        + [pltpu.SemaphoreType.DMA((GATHER_COPIES,))] * 4
        + [pltpu.SemaphoreType.DMA((20,))]
        + [pltpu.VMEM(weight, bf16), pltpu.VMEM(w_down.shape, bf16)]
        + [pltpu.VMEM((8 * rows, inner), bf16)] * 3
        + [
            pltpu.VMEM((2, 2 * rows, 2 * inner), bf16),
            pltpu.VMEM(w_down.shape, f32),
        ],
        line.pop("number"),
        (64 * rows * width * inner, 300 * rows * width * 2, 8 * rows * inner),
        vmem=61,
        **line,
    )


def attended_back_kernel(ins, outs, scratch, line):
    grad_ref, w_ref, attended_ref = ins
    grad_attended_ref, out_term_ref = outs
    held, sends, recvs, sems, total = scratch
    rows = grad_ref.shape[0]
    moves = Moves(sems)
    greet_group(line)
    line.start()
    held[own_rows(rows), :] = grad_ref[...].astype(bf16)

    def on_chip(*chip):
        where = chip_rows(*chip, rows)
        incoming = held[where, :]
        grad_attended_ref[where, :] = against_rows(incoming, w_ref[...]).astype(bf16)
        term = over_tokens(attended_ref[where, :], incoming)
        if chip == SIBLING:
            total[...] = term
        elif chip == ACROSS:
            out_term_ref[...] = (total[...] + term).astype(bf16)
        else:
            total[...] += term

    gather_rows(rows, held, sends, recvs, on_chip, line)
    moves.finish()


def attended_back(grad, w_out, attended, **line):
    rows, width = grad.shape
    return run(
        attended_back_kernel,
        [(array, VMEM) for array in (grad, w_out, attended)],
        [
            (jax.ShapeDtypeStruct(attended.shape, bf16), VMEM),
            (jax.ShapeDtypeStruct(w_out.shape, bf16), VMEM),
        ],
        gather_scratch(rows, width, 1) + [pltpu.VMEM(w_out.shape, f32)],
        line.pop("number"),
        (32 * rows * width * w_out.shape[0], 150 * rows * width * 2, 0),
        **line,
    )


class WeightTerm:
    def __init__(self, rows_ref, columns_ref, term_ref, scratch):
        self.rows_ref, self.columns_ref, self.term_ref = rows_ref, columns_ref, term_ref
        self.loaded, self.ready, self.sems = scratch
        self.tile = self.loaded.shape[2]
        for number in (0, 1):
            self.load(number).start()

    def load(self, number):
        cols = slice(number * self.tile, (number + 1) * self.tile)
        return pltpu.make_async_copy(
            self.rows_ref.at[:, cols], self.loaded.at[number % 2], self.sems.at[0, number % 2]
        )

    def store(self, number):
        return pltpu.make_async_copy(
            self.ready.at[number % 2], self.term_ref.at[number], self.sems.at[1, number % 2]
        )

    def work(self, numbers):
        for number in numbers:
            at = number % 2
            self.load(number).wait()
            if number >= 2:
                self.store(number - 2).wait()
            width = self.columns_ref.shape[1]
            step = min(256, width)

            def column(t, _):
                cols = pl.ds(pl.multiple_of(t * step, step), step)
                term = over_tokens(self.loaded[at], self.columns_ref[:, cols])
                self.ready[at, :, cols] = term.astype(bf16)
                return 0

            lax.fori_loop(0, width // step, column, 0)
            self.store(number).start()
            if number + 2 < 8:
                self.load(number + 2).start()

    def finish(self):
        for number in (6, 7):
            self.store(number).wait()


def scatter_kernel(turned, tile, extra, after, ins, outs, scratch, line):
    out_ref = outs[0] if after == "base" else scratch[-4]
    finals = ins[len(ins) - {"base": 1, "cast": 1, "back": 3}[after] :]
    part, to_s, from_s, to_chip, held, relay, last, sends, recvs = scratch[:9]
    a_ref, b_ref, loads = scratch[-3:]
    loading = [
        pltpu.make_async_copy(src, dst, loads.at[number])
        for number, (src, dst) in enumerate(((ins[1], b_ref), (ins[0], a_ref)))
    ]
    for one in loading:
        one.start()
    rows, width = out_ref.shape
    half = rows // 2
    _, _, core = place_in_group()
    greet_group(line)
    line.start()
    if extra:
        columns_ref = a_ref
        if extra == "loaded":
            columns_ref = scratch[12]
            columns_copy = pltpu.make_async_copy(ins[3], columns_ref, scratch[13].at[0])
            columns_copy.start()
        term = WeightTerm(ins[2], columns_ref, outs[-1], scratch[9:12])
    for one in loading:
        one.wait()
    own_at = pl.multiple_of(core * rows, rows)
    other_at = pl.multiple_of((1 - core) * rows, rows)
    started = []

    def send(number, src, dst, target):
        one = pltpu.make_async_remote_copy(
            src_ref=src, dst_ref=dst, send_sem=sends.at[number], recv_sem=recvs.at[number],
            device_id={"grp": other(*target)}, device_id_type=MESH,
        )
        one.start()
        started.append(one)
        return one

    def landed(number, where):
        pltpu.make_async_remote_copy(
            src_ref=where, dst_ref=where, send_sem=sends.at[number], recv_sem=recvs.at[number],
            device_id={"grp": other(0, 0, 1)}, device_id_type=MESH,
        ).wait_recv()

    to_sib, to_x, to_y = (0, 0, 1), (0, 1, 0), (1, 0, 0)

    def make(number, chip):
        where = chip_rows(*chip, rows)

        def column(t, _):
            cols = pl.ds(pl.multiple_of(t * tile, tile), tile)
            lhs = a_ref[where, :]
            if turned:
                part[:, cols] = against_rows(lhs, b_ref[cols, :])
            else:
                part[:, cols] = matmul_f32(lhs, b_ref[:, cols])
            return 0

        lax.fori_loop(0, width // tile, column, 0)
        to_s[number] = part[pl.ds(other_at, rows), :].astype(bf16)
        send(number, to_s.at[number], from_s.at[number], to_sib)

    def own(low, number):
        at = pl.ds(pl.multiple_of(core * rows + low * half, half), half)
        return part[at, :] + from_s[number, low * half : (low + 1) * half, :].astype(f32)

    first, second = slice(0, half), slice(half, rows)
    make(0, ACROSS)
    landed(0, from_s.at[0])
    to_chip[0, first, :] = own(0, 0).astype(bf16)
    send(4, to_chip.at[0, first, :], relay.at[0], to_x)
    to_chip[0, second, :] = own(1, 0).astype(bf16)
    send(5, to_chip.at[0, second, :], relay.at[1], to_y)
    make(1, ALONG_X)
    landed(1, from_s.at[1])
    to_chip[1, first, :] = own(0, 1).astype(bf16)
    send(6, to_chip.at[1, first, :], last.at[0, first, :], to_x)
    held[0] = own(1, 1)
    line.step()
    make(2, ALONG_Y)
    landed(2, from_s.at[2])
    to_chip[2, second, :] = own(1, 2).astype(bf16)
    send(7, to_chip.at[2, second, :], last.at[1, second, :], to_y)
    held[1] = own(0, 2)
    if extra:
        if extra == "loaded":
            columns_copy.wait()
        term.work((0, 1, 2))
    landed(5, relay.at[1])
    to_chip[1, second, :] = (held[0] + relay[1].astype(f32)).astype(bf16)
    send(8, to_chip.at[1, second, :], last.at[0, second, :], to_x)
    landed(4, relay.at[0])
    to_chip[2, first, :] = (held[1] + relay[0].astype(f32)).astype(bf16)
    send(9, to_chip.at[2, first, :], last.at[1, first, :], to_y)
    line.step()
    make(3, SIBLING)
    if extra:
        term.work((3, 4))
        line.step()
        term.work((5, 6, 7))
    landed(3, from_s.at[3])
    for low in (0, 1):
        at = slice(low * half, (low + 1) * half)
        if after == "back":
            out_ref[at, :] = own(low, 3)
        else:
            out_ref[at, :] = own(low, 3) + finals[0][at, :].astype(f32)
    landed(6, last.at[0, first, :])
    out_ref[first, :] += last[0, first, :].astype(f32)
    landed(7, last.at[1, second, :])
    out_ref[second, :] += last[1, second, :].astype(f32)
    line.step()
    landed(8, last.at[0, second, :])
    out_ref[second, :] += last[0, second, :].astype(f32)
    landed(9, last.at[1, first, :])
    out_ref[first, :] += last[1, first, :].astype(f32)
    if after == "cast":
        outs[0][...] = out_ref[...].astype(outs[0].dtype)
    if after == "back":
        upstream_ref, rows_ref, gain_ref = finals
        some = min(64, rows)

        def norm_rows(number, gain_term):
            at = pl.ds(pl.multiple_of(number * some, some), some)
            values, incoming = rows_ref[at, :].astype(f32), out_ref[at, :]
            inv = lax.rsqrt(jnp.mean(values * values, -1, keepdims=True) + EPS)
            grad, term = norm_back(
                upstream_ref[at, :].astype(f32), incoming, values * inv, inv, gain_ref[...]
            )
            outs[0][at, :] = grad.astype(outs[0].dtype)
            return gain_term + term[None, :]

        outs[1][...] = lax.fori_loop(0, rows // some, norm_rows, jnp.zeros((1, width), f32))
    for one in started:
        one.wait_send()
    if extra:
        term.finish()
    line.end()


def product_scattered(a, b, turned, extra=None, base=None, back=None, dtype=f32, **line):
    length, depth = a.shape
    width = b.shape[0] if turned else b.shape[1]
    rows = length // 8
    tile = min(256, width)
    ins = [(a, ANY), (b, ANY)]
    outs = [(jax.ShapeDtypeStruct((rows, width), dtype), VMEM)]
    after = "back" if back else "base" if dtype == f32 else "cast"
    if back:
        outs.append((jax.ShapeDtypeStruct((1, width), f32), VMEM))
    scratch = [
        pltpu.VMEM((2 * rows, width), f32),
        pltpu.VMEM((4, rows, width), bf16),
        pltpu.VMEM((4, rows, width), bf16),
        pltpu.VMEM((3, rows, width), bf16),
        pltpu.VMEM((2, rows // 2, width), f32),
        pltpu.VMEM((2, rows // 2, width), bf16),
        pltpu.VMEM((2, rows, width), bf16),
        pltpu.SemaphoreType.DMA((10,)),
        pltpu.SemaphoreType.DMA((10,)),
    ]
    flops, kind = 2 * length * depth * width, None
    if extra:
        first, second = extra
        kind = "own" if second is None else "loaded"
        ins.append((first, ANY))
        columns = a if second is None else second
        tall = first.shape[1] // 8
        outs.append((jax.ShapeDtypeStruct((8, tall, columns.shape[1]), bf16), ANY))
        scratch += [
            pltpu.VMEM((2, length, tall), bf16),
            pltpu.VMEM((2, tall, columns.shape[1]), bf16),
            pltpu.SemaphoreType.DMA((2, 2)),
        ]
        if second is not None:
            ins.append((second, ANY))
            scratch += [pltpu.VMEM(second.shape, bf16), pltpu.SemaphoreType.DMA((1,))]
        flops += 2 * length * first.shape[1] * columns.shape[1]
    ins += [(array, VMEM) for array in (back or (base,))]
    if after != "base":
        scratch.append(pltpu.VMEM((rows, width), f32))
    scratch += [
        pltpu.VMEM(a.shape, bf16), pltpu.VMEM(b.shape, bf16), pltpu.SemaphoreType.DMA((2,))
    ]
    return run(
        functools.partial(scatter_kernel, turned, tile, kind, after), ins, outs, scratch,
        line.pop("number"), (flops, 150 * rows * width * 2, 0), vmem=61, **line,
    )


def tail_kernel(ready, later, ins, outs, scratch, line):
    qkv_ref, gains_ref = ins[:2]
    chunk_refs = dict(zip(ready, ins[2:]))
    gate_ref, up_ref, qkv_rows_ref, gains_out_ref = outs
    from_group, mine, from_rep, sends, recvs, chunk_sems, local = scratch
    me, rank = other(0, 0, 0), lax.axis_index("rep")
    inner = gate_ref.shape[1] // 8
    part = qkv_ref.shape[-1]
    high = line.outs[later[0]].shape[1]
    barrier = pltpu.get_barrier_semaphore()
    for flip in range(1, 4):
        pl.semaphore_signal(
            barrier, inc=1, device_id={"rep": (rank + flip) % 4}, device_id_type=MESH
        )
    for flip in EVERYONE:
        pl.semaphore_signal(barrier, inc=1, device_id={"grp": other(*flip)}, device_id_type=MESH)
    pl.semaphore_wait(barrier, 10)
    waits, moves = [], Moves(local)
    line.refs["qkv"] = qkv_rows_ref

    def send(kind, number, src, dst, device):
        return pltpu.make_async_remote_copy(
            src_ref=src, dst_ref=dst, send_sem=sends.at[kind, number],
            recv_sem=recvs.at[kind, number], device_id=device, device_id_type=MESH,
        )

    own_qkv = qkv_rows_ref.at[me // 4, :, :, pl.ds(pl.multiple_of((me % 4) * part, part), part)]
    qkv_copies, gain_copies = [], []
    for number, flip in enumerate(EVERYONE):
        target = other(*flip)
        qkv_copies.append(send(0, number, qkv_ref.at[target], own_qkv, {"grp": target}))
        qkv_copies[-1].start()
    moves.later(qkv_ref.at[me], own_qkv)
    line.start()
    for number, flip in enumerate(EVERYONE):
        target = other(*flip)
        gain_copies.append(
            send(1, number, gains_ref.at[target], from_group.at[me], {"grp": target})
        )
        gain_copies[-1].start()
    from_group[me] = gains_ref[me]

    def spread(chunk):
        src = chunk_refs[chunk] if chunk in chunk_refs else line.outs[chunk]
        number = chunk - DOWN
        rows = slice(number * high, (number + 1) * high)
        cols = pl.ds(pl.multiple_of(me * inner, inner), inner)
        for which, dst in enumerate((gate_ref, up_ref)):
            there = dst.at[rows, cols]
            for flip in EVERYONE:
                target = other(*flip)
                pltpu.make_async_remote_copy(
                    src_ref=src.at[target, :, which * inner : (which + 1) * inner], dst_ref=there,
                    send_sem=chunk_sems.at[0, which, number], recv_sem=chunk_sems.at[1, which, number],
                    device_id={"grp": target}, device_id_type=MESH,
                ).start()
            moves.later(src.at[me, :, which * inner : (which + 1) * inner], there)
            seven = dst.at[rows, : 7 * inner]
            waits.append(
                pltpu.make_async_remote_copy(
                    src_ref=seven, dst_ref=seven, send_sem=chunk_sems.at[0, which, number],
                    recv_sem=chunk_sems.at[1, which, number],
                    device_id={"grp": other(0, 0, 1)}, device_id_type=MESH,
                )
            )

    for chunk in ready:
        spread(chunk)
    for one in gain_copies:
        one.wait()
    mine[rank] = sum(from_group[g] for g in range(8))
    rep_copies = []
    for step in range(1, 4):
        target = (rank + step) % 4
        rep_copies.append(
            send(2, step, mine.at[rank], from_rep.at[step], {"rep": target})
        )
        rep_copies[-1].start()
    for step, one in zip(range(1, 4), rep_copies):
        one.wait()
        mine[(rank + 4 - step) % 4] = from_rep[step]
    gains_out_ref[...] = (mine[0] + mine[1]) + (mine[2] + mine[3])
    for number in range(1, line.ticks):
        if line.first + number + 1 == CHUNKS - QKV:
            for one in qkv_copies:
                one.wait()
            moves.open.pop(0).wait()
        line.step()
        chunk = line.first + number - 5
        if chunk in later:
            spread(chunk)
    line.end()
    for one in waits:
        one.wait_send()
        one.wait_recv()
    moves.finish()


def tail(qkv_term, gains, chunks, inner, number, sums, ticks, arrays, picks):
    first = sums.tick
    ready = sorted(chunks)
    later = [c for c in line_slots(first, ticks) if c < DOWN + GATE_UP]
    _, high, width = sums.shape
    wide = jax.ShapeDtypeStruct((GATE_UP * high, 8 * inner), bf16)
    moved = jax.ShapeDtypeStruct((2, 8, 2 * high, width), bf16)
    picks = dict(picks)
    for n, (half, low, column, columns) in enumerate(qkv_parts(width)):
        where = (half, slice(None), slice(low * high, (low + 1) * high), slice(column, column + columns))
        picks[CHUNKS - QKV + n] = ("qkv", lambda ref, where=where: ref.at[where])
    return run(
        functools.partial(tail_kernel, ready, later),
        [(qkv_term, ANY), (gains, VMEM)] + [(chunks[c], ANY) for c in ready],
        [(wide, ANY), (wide, ANY), (moved, ANY), (jax.ShapeDtypeStruct(gains.shape[1:], f32), VMEM)],
        [
            pltpu.VMEM(gains.shape, f32),
            pltpu.VMEM((4,) + gains.shape[1:], f32),
            pltpu.VMEM((4,) + gains.shape[1:], f32),
            pltpu.SemaphoreType.DMA((3, 7)),
            pltpu.SemaphoreType.DMA((3, 7)),
            pltpu.SemaphoreType.DMA((2, 2, GATE_UP)),
            pltpu.SemaphoreType.DMA((1 + 2 * GATE_UP,)),
        ],
        number, (0, 200 * 8 * high * width * 2, 0), sums=sums, ticks=ticks, arrays=arrays, picks=picks,
    )


def finish_kernel(heads, *refs):
    chunks, rest = refs[: DOWN + OUT + QKV], refs[DOWN + OUT + QKV :]
    gate_rows, up_rows = rest[:2]
    query, key, value, out, gate, up, down = rest[2:9]
    low, wide, load_sems, store_sems = rest[9:]
    _, high, width = chunks[0].shape
    depth = low.shape[0]

    def half(number):
        return slice(number * high, (number + 1) * high)

    whole = slice(0, width)
    jobs = [(ref, [(whole, down.at[number])]) for number, ref in enumerate(chunks[:DOWN])]
    for ref, into in ((gate_rows, gate), (up_rows, up)):
        for low_col in range(0, ref.shape[2], width):
            cols = slice(low_col, low_col + width)
            for number in (0, 1):
                where = (slice(None), half(number), cols)
                jobs.append((ref.at[where], [(whole, into.at[where])]))
    for number, ref in enumerate(chunks[DOWN : DOWN + OUT]):
        jobs.append((ref, [(whole, out.at[:, half(number), :])]))
    part = (heads + 2) * HD
    for ref, (devices, low_rows, column, columns) in zip(chunks[DOWN + OUT :], qkv_parts(width)):
        stores = []
        for place in range(columns // part):
            at, device = place * part, devices * (width // part) + column // part + place
            for into, first, size in (
                (query, 0, heads * HD), (key, heads * HD, HD), (value, (heads + 1) * HD, HD)
            ):
                there = into.at[:, half(low_rows), device * size : (device + 1) * size]
                stores.append((slice(at + first, at + first + size), there))
        jobs.append((ref, stores))

    def load(number):
        at, ref = number % depth, jobs[number][0]
        return pltpu.make_async_copy(ref, low.at[at, :, :, : ref.shape[2]], load_sems.at[at])

    def stores(number):
        at = number % depth
        return [
            pltpu.make_async_copy(wide.at[at, :, :, cols], into, store_sems.at[at, which])
            for which, (cols, into) in enumerate(jobs[number][1])
        ]

    for number in range(depth - 1):
        load(number).start()
    for number in range(len(jobs)):
        if number + depth - 1 < len(jobs):
            load(number + depth - 1).start()
        load(number).wait()
        if number >= depth:
            for one in stores(number - depth):
                one.wait()

        def cast(g, _, at=number % depth, cols=slice(0, jobs[number][0].shape[2])):
            wide[at, g, :, cols] = low[at, g, :, cols].astype(f32)
            return 0

        lax.fori_loop(0, low.shape[1], cast, 0)
        for one in stores(number):
            one.start()
    for number in range(len(jobs) - depth, len(jobs)):
        for one in stores(number):
            one.wait()


def finish(chunks, gate_rows, up_rows, heads):
    eight, high, width = chunks[0].shape
    rows, wide = gate_rows.shape

    def split(columns):
        return jax.ShapeDtypeStruct((eight, rows // eight, columns), f32)

    shapes = [split(columns) for columns in (8 * heads * HD, 8 * HD, 8 * HD, width, wide, wide)]
    shapes.append(jax.ShapeDtypeStruct((DOWN, eight, high, width), f32))
    depth = 6
    results = pl.pallas_call(
        functools.partial(finish_kernel, heads),
        out_shape=tuple(shapes),
        in_specs=[pl.BlockSpec(memory_space=pl.ANY)] * (len(chunks) + 2),
        out_specs=tuple([pl.BlockSpec(memory_space=pl.ANY)] * 7),
        scratch_shapes=[
            pltpu.VMEM((depth, eight, high, width), bf16),
            pltpu.VMEM((depth, eight, high, width), f32),
            pltpu.SemaphoreType.DMA((depth,)),
            pltpu.SemaphoreType.DMA((depth, 12)),
        ],
        compiler_params=pltpu.CompilerParams(vmem_limit_bytes=60 * 2**20),
        cost_estimate=pl.CostEstimate(
            flops=0, bytes_accessed=6 * CHUNKS * eight * high * width, transcendentals=0
        ),
    )(
        *chunks, gate_rows.reshape(eight, rows // eight, wide),
        up_rows.reshape(eight, rows // eight, wide),
    )
    flat = [result.reshape(rows, -1) for result in results[:6]]
    return flat + [results[6].reshape(DOWN * eight * high, width)]


def sum_over_sequences(term):
    return lax.psum(term, "rep").astype(f32)


def on_device(
    layer_input,
    cotangent,
    cut_order,
    piece_ids,
    w_query,
    w_key,
    w_value,
    w_out,
    w_gate,
    w_up,
    w_down,
    gain_attn,
    gain_ffn,
):
    groups = lax.axis_size("grp")
    reps = lax.axis_size("rep")
    own_index = lax.axis_index("grp")
    _, local_rows, model_width = layer_input.shape
    length = piece_ids.shape[1]
    rows_here = w_query.shape[0]
    q_width = w_query.shape[1]
    kv_heads = w_key.shape[1] // HD
    heads = q_width // HD // groups
    copies = groups // kv_heads
    hidden_here = w_down.shape[0]
    cosine, sine = turn_tables(length)

    near = groups == 8 and reps == 4 and copies == 1

    def gather(rows):
        return lax.all_gather(rows, "grp", axis=0, tiled=True)

    def scatter(first, second, turned):
        term = against_rows(first, second) if turned else matmul_f32(first, second)
        return lax.psum_scatter(
            term.astype(bf16), "grp", scatter_dimension=0, tiled=True
        ).astype(f32)

    def to_columns(parts):
        return lax.all_to_all(parts, "grp", 1, 0, tiled=True).reshape(-1, parts.shape[-1])

    def per_group(weight):
        return weight.reshape(rows_here, groups, -1)

    def per_kv_head(weight):
        return jnp.repeat(weight.reshape(rows_here, kv_heads, HD), copies, axis=1)

    x_rows = layer_input.reshape(local_rows, model_width)
    x_flat = x_rows.astype(f32)
    inv_one = lax.rsqrt(jnp.mean(x_flat * x_flat, -1, keepdims=True) + EPS)
    unit_one = x_flat * inv_one
    attn_gain, ffn_gain = gain_attn.reshape(1, -1), gain_ffn.reshape(1, -1)
    if near:
        share = rows_here // (4 * reps) * 3
        spread = columns_of_some((w_gate, w_up), share, 11)
        x_first, spread = lax.optimization_barrier((x_rows, spread))
        spread = lax.all_gather(spread, "rep", axis=0)
        normed_one, cols_qkv = gather_normed(
            x_first, attn_gain, (w_query, w_key, w_value), number=1
        )
        last_gate, last_up, normed_one = lax.optimization_barrier(
            (w_gate[reps * share :], w_up[reps * share :], normed_one)
        )
        rest = to_columns(
            jnp.concatenate(
                [part.reshape(rows_here - reps * share, groups, -1) for part in (last_gate, last_up)],
                -1,
            )
        ).reshape(groups, rows_here - reps * share, -1)
    else:
        normed_one = gather(rms_normed(x_flat, attn_gain).astype(bf16))
        cols_qkv = to_columns(
            jnp.concatenate([per_group(w_query), per_kv_head(w_key), per_kv_head(w_value)], -1)
        )
        cols_gate_up = to_columns(jnp.concatenate([per_group(w_gate), per_group(w_up)], -1))
    attended, query, key, value, lse, attended_placed = attend(
        cut_order, normed_one, cols_qkv, cosine, sine, piece_ids, heads
    )
    if near:
        mid = product_scattered(attended, w_out, False, base=x_rows, number=2)[0]
    else:
        mid = x_flat + scatter(attended, w_out, False)
    grad_out = cotangent.reshape(local_rows, model_width)

    def back_through_attention(grad_attended, **line):
        return attend_back(
            cut_order, grad_attended, attended_placed, query, key, value, lse, cosine, sine,
            piece_ids, heads, **line,
        )

    q_here = heads * HD
    if near:
        normed_two, hidden, cols_gate_up, grad_gate_up, down_term = feed_forward(
            mid, ffn_gain, grad_out, spread, rest, w_down, number=3
        )
        cols_gate_up = cols_gate_up.reshape(model_width, -1)
        high = rows_here // GATE_UP
        sums = Sums((8, high, model_width))
        terms = {"down": down_term.reshape((DOWN,) + sums.shape)}

        def pick_whole(number):
            return "down", lambda ref: ref.at[number]

        def pick_rows(name, number):
            return name, lambda ref: ref.at[:, number * high : (number + 1) * high, :]

        picks = [pick_whole(n) for n in range(DOWN)]
        picks += [pick_rows("gate_up", n) for n in range(GATE_UP)]
        picks += [pick_rows("out", n) for n in range(OUT)]

        def line(number, ticks):
            names = sorted(
                {picks[t][0] for t in range(sums.tick, sums.tick + ticks) if t < len(picks)}
            )
            return dict(
                number=number, ticks=ticks, sums=sums, picks=dict(enumerate(picks)),
                arrays=[(name, terms[name]) for name in names],
            )

        result, terms["gate_up"] = product_scattered(
            hidden, w_down, False, extra=(normed_two, grad_gate_up), base=mid, dtype=bf16,
            **line(5, 5),
        )
        grad_mid, gain_ffn_term = product_scattered(
            grad_gate_up, cols_gate_up, True, back=(grad_out, mid, ffn_gain), **line(6, 5)
        )
        grad_attended, out_term = attended_back(grad_mid, w_out, attended, **line(7, 4))
        terms["out"] = out_term.reshape(8, OUT * high, model_width)
        grad_qkv = back_through_attention(grad_attended, **line(8, 3))
        grad_x, gain_attn_term, qkv_term = product_scattered(
            grad_qkv, cols_qkv, True, extra=(normed_one, None), dtype=bf16,
            back=(grad_mid, x_rows, attn_gain), **line(9, 4),
        )
        gains = jnp.stack([gain_attn_term, gain_ffn_term]).reshape(2, groups, rows_here)
        gains = jnp.pad(jnp.moveaxis(gains, 0, 1), ((0, 0), (0, 6), (0, 0)))
        rest = line(10, CHUNKS + 4 - sums.tick)
        gate_rows, up_rows, qkv_rows, own_gains = tail(
            qkv_term.reshape(8, 8, 2 * high, -1), gains,
            {c: sums.done[c] for c in sums.done if c >= DOWN}, hidden_here, **rest,
        )
        straight = [n for n in range(CHUNKS) if n < DOWN or n >= DOWN + GATE_UP]
        weight_grads = finish([sums.done[n] for n in straight], gate_rows, up_rows, heads)
        shaped = tuple(rows.reshape(layer_input.shape) for rows in (result, grad_x))
        return shaped + tuple(weight_grads) + (own_gains[0], own_gains[1])

    unit_one = x_flat * inv_one
    inv_two = lax.rsqrt(jnp.mean(mid * mid, -1, keepdims=True) + EPS)
    unit_two = mid * inv_two
    normed_two = gather((unit_two * ffn_gain).astype(bf16))
    grad_all = gather(grad_out)
    gate_up = matmul_f32(normed_two, cols_gate_up)
    gate_proj, up_proj = gate_up[:, :hidden_here], gate_up[:, hidden_here:]
    sigmoid_gate = jax.nn.sigmoid(gate_proj)
    swish = gate_proj * sigmoid_gate
    hidden = (swish * up_proj).astype(bf16)
    gate_part = up_proj * sigmoid_gate * (1.0 + gate_proj * (1.0 - sigmoid_gate))
    down_term = over_tokens(hidden, grad_all).astype(bf16)
    grad_hidden = against_rows(grad_all, w_down)
    grad_gate_up = jnp.concatenate([grad_hidden * gate_part, grad_hidden * swish], 1).astype(bf16)
    grad_mid, gain_ffn_term = norm_back(
        grad_out.astype(f32), scatter(grad_gate_up, cols_gate_up, True), unit_two, inv_two, gain_ffn
    )
    grad_mid_low = gather(grad_mid.astype(bf16))
    grad_qkv = back_through_attention(against_rows(grad_mid_low, w_out).astype(bf16))
    grad_x, gain_attn_term = norm_back(
        grad_mid, scatter(grad_qkv, cols_qkv, True), unit_one, inv_one, gain_attn
    )

    def to_rows(term):
        return lax.all_to_all(
            term.astype(bf16).reshape(groups, rows_here, -1), "grp", 0, 0, tiled=True
        )

    def whole_rows(term):
        return jnp.moveaxis(term, 0, 1).reshape(rows_here, -1)

    def kv_rows(term):
        return jnp.sum(
            jnp.moveaxis(term, 0, 1).reshape(rows_here, kv_heads, copies, HD), 2
        ).reshape(rows_here, -1)

    gate_up_term = sum_over_sequences(to_rows(over_tokens(normed_two, grad_gate_up)))
    out_term = sum_over_sequences(over_tokens(attended, grad_mid_low).astype(bf16))
    qkv_term = sum_over_sequences(to_rows(over_tokens(normed_one, grad_qkv)))
    gain_total = lax.psum(jnp.stack([gain_attn_term, gain_ffn_term]), ("grp", "rep"))
    own_gains = lax.dynamic_slice_in_dim(gain_total, own_index * rows_here, rows_here, 1)
    return (
        (mid + scatter(hidden, w_down, False)).astype(bf16).reshape(layer_input.shape),
        grad_x.astype(bf16).reshape(layer_input.shape),
        whole_rows(qkv_term[..., :q_here]),
        kv_rows(qkv_term[..., q_here : q_here + HD]),
        kv_rows(qkv_term[..., q_here + HD :]),
        out_term,
        whole_rows(gate_up_term[..., :hidden_here]),
        whole_rows(gate_up_term[..., hidden_here:]),
        sum_over_sequences(down_term),
        own_gains[0],
        own_gains[1],
    )


def solution(mesh):
    tokens, table, rows, whole = P("rep", "grp", None), P("rep", None), P("grp", None), P()
    return jax.shard_map(
        on_device,
        mesh=mesh,
        in_specs=(tokens, tokens, table, table) + (rows,) * 7 + (whole,) * 2,
        out_specs=(tokens, tokens) + (rows,) * 7 + (P("grp"),) * 2,
        check_vma=False,
    )
```

```python
import functools

import jax
import jax.numpy as jnp
import numpy as np
from jax import lax
from jax.experimental import pallas as pl
from jax.experimental.pallas import tpu as pltpu
from jax.sharding import PartitionSpec as P

HD = 128
EPS = 1e-05
ROPE_BASE = 1000000.0
SCORE_SCALE = HD**-0.5
LOG2E = 1.4426950408889634
TO_EXP2 = SCORE_SCALE * LOG2E
NEG = -1e30

MESH = pl.DeviceIdType.MESH
f32 = jnp.float32
bf16 = jnp.bfloat16


def matmul_f32(first, second):
    return jnp.dot(first, second, preferred_element_type=f32)


def against_rows(first, second):
    return lax.dot_general(first, second, (((1,), (1,)), ((), ())), preferred_element_type=f32)


def over_tokens(first, second):
    return lax.dot_general(first, second, (((0,), (0,)), ((), ())), preferred_element_type=f32)


def turn_tables(length):
    half_size = HD // 2
    inverse = np.float32(ROPE_BASE) ** (-(np.arange(half_size, dtype=np.float32) * 2) / HD)
    angles = np.arange(length, dtype=np.float32)[:, None] * inverse.astype(np.float32)
    cosine, sine = np.cos(angles), np.sin(angles)
    tables = np.concatenate([cosine, cosine], -1), np.concatenate([-sine, sine], -1)
    return tuple(jnp.asarray(table.astype(np.float32)) for table in tables)


def norm_back(upstream, grad_normed, unit_rows, inv_root, gain):
    scaled = grad_normed * gain
    center_term = jnp.mean(scaled * unit_rows, -1, keepdims=True)
    return (
        upstream + inv_root * (scaled - unit_rows * center_term),
        jnp.sum(grad_normed * unit_rows, 0),
    )


def fold_lanes(values, op):
    out = values[:, :HD]
    for at in range(HD, values.shape[1], HD):
        out = op(out, values[:, at : at + HD])
    return out


def as_column(row):
    return jnp.broadcast_to(row, (HD, row.shape[1])).T[:, 0:1]


def as_row(column):
    return jnp.broadcast_to(column, (column.shape[0], HD)).T[0:1, :]


def attend_kernel(
    heads, cuts, block,
    order_ref, rows_hbm, weight_hbm, cos_ref, sin_ref, piece_ref,
    out_ref, q_ref, k_ref, v_ref, lse_ref, placed,
    scores, rows_ref, weight_ref, qkv_ref, sems,
):
    length = rows_ref.shape[0]
    cut = length // cuts
    blocks = length // block
    loads = [pltpu.make_async_copy(weight_hbm, weight_ref, sems.at[blocks])]
    for i in range(blocks):
        at = slice(i * block, (i + 1) * block)
        loads.append(pltpu.make_async_copy(rows_hbm.at[at, :], rows_ref.at[at, :], sems.at[i]))
    for load in loads:
        load.start()

    def place_cut(r, first):
        src = pl.ds(pl.multiple_of(r * cut, cut), cut)
        dst = pl.ds(pl.multiple_of(order_ref[0, first + r] * cut, cut), cut)
        cosine, sine = cos_ref[dst, :], sin_ref[dst, :]
        for h in range(heads + 1):
            part = qkv_ref[src, h * HD : (h + 1) * HD]
            turned = (part * cosine + pltpu.roll(part, HD // 2, 1) * sine).astype(bf16)
            if h < heads:
                q_ref[h, dst, :] = turned
            else:
                k_ref[dst, :] = turned
        v_ref[dst, :] = qkv_ref[src, (heads + 1) * HD :].astype(bf16)
        return first

    loads[0].wait()
    for i in range(blocks):
        loads[1 + i].wait()
        qkv_ref[...] = matmul_f32(rows_ref[i * block : (i + 1) * block, :], weight_ref[...])
        lax.fori_loop(0, block // cut, place_cut, i * (block // cut))

    def one_block(i, _):
        rows = pl.ds(pl.multiple_of(i * block, block), block)
        query = q_ref[:, rows, :].reshape(heads * block, HD)

        def score(j, high):
            cols = pl.ds(pl.multiple_of(j * block, block), block)
            tile = against_rows(query, k_ref[cols, :])
            scores[j] = tile
            return jnp.maximum(high, fold_lanes(tile, jnp.maximum))

        high = lax.fori_loop(0, i, score, jnp.full((heads * block, HD), NEG, f32))
        tile = against_rows(query, k_ref[rows, :])
        q_at = lax.broadcasted_iota(jnp.int32, (block, block), 0)
        k_at = lax.broadcasted_iota(jnp.int32, (block, block), 1)
        k_piece = piece_ref[0:1, rows].astype(f32)
        q_piece = as_column(k_piece)
        allowed = (k_at <= q_at) | ((q_piece != 0) & (q_piece == k_piece))
        tile = jnp.concatenate(
            [jnp.where(allowed, tile[h * block : (h + 1) * block], NEG) for h in range(heads)], 0
        )
        scores[i] = tile
        high = jnp.max(jnp.maximum(high, fold_lanes(tile, jnp.maximum)), 1, keepdims=True)

        def weigh(j, state):
            total, mixed = state
            cols = pl.ds(pl.multiple_of(j * block, block), block)
            prob = jnp.exp2((scores[j] - high) * TO_EXP2)
            total = total + fold_lanes(prob, jnp.add)
            return total, mixed + matmul_f32(prob.astype(bf16), v_ref[cols, :])

        zero = jnp.zeros((heads * block, HD), f32)
        total, mixed = lax.fori_loop(0, i + 1, weigh, (zero, zero))
        total = jnp.sum(total, 1, keepdims=True)
        mixed = (mixed / total).astype(bf16)
        log_total = high * TO_EXP2 + jnp.log2(total)
        for h in range(heads):
            placed[rows, h * HD : (h + 1) * HD] = mixed[h * block : (h + 1) * block]
            lse_ref[h : h + 1, rows] = as_row(log_total[h * block : (h + 1) * block])
        return 0

    lax.fori_loop(0, blocks, one_block, 0)

    def store_cut(r, _):
        dst = pl.ds(pl.multiple_of(r * cut, cut), cut)
        src = pl.ds(pl.multiple_of(order_ref[0, r] * cut, cut), cut)
        out_ref[dst, :] = placed[src, :]
        return 0

    lax.fori_loop(0, cuts, store_cut, 0)


def vmem_specs(count):
    return [pl.BlockSpec(memory_space=pltpu.VMEM)] * count


def attend(order, rows, weight, cosine, sine, piece, heads):
    length, width = rows.shape
    block = min(512, length)
    return pl.pallas_call(
        functools.partial(attend_kernel, heads, order.shape[1], block),
        out_shape=(
            jax.ShapeDtypeStruct((length, heads * HD), bf16),
            jax.ShapeDtypeStruct((heads, length, HD), bf16),
            jax.ShapeDtypeStruct((length, HD), bf16),
            jax.ShapeDtypeStruct((length, HD), bf16),
            jax.ShapeDtypeStruct((heads, length), f32),
            jax.ShapeDtypeStruct((length, heads * HD), bf16),
        ),
        in_specs=[pl.BlockSpec(memory_space=pltpu.SMEM)]
        + [pl.BlockSpec(memory_space=pl.ANY)] * 2
        + vmem_specs(3),
        out_specs=tuple(vmem_specs(6)),
        scratch_shapes=[
            pltpu.VMEM((length // block, heads * block, block), f32),
            pltpu.VMEM(rows.shape, bf16),
            pltpu.VMEM(weight.shape, bf16),
            pltpu.VMEM((block, weight.shape[1]), f32),
            pltpu.SemaphoreType.DMA((length // block + 1,)),
        ],
        compiler_params=pltpu.CompilerParams(vmem_limit_bytes=60 * 2**20),
        cost_estimate=pl.CostEstimate(
            flops=3 * heads * length * length * HD + 2 * length * width * weight.shape[1],
            bytes_accessed=10 * length * HD * heads * 4 + rows.size * 2,
            transcendentals=heads * length * length // 2,
        ),
    )(order, rows, weight, cosine, sine, piece)


DOWN, GATE_UP, OUT, QKV = 16, 32, 4, 8
CHUNKS = DOWN + GATE_UP + OUT + QKV
LAG = 3


def is_chunk(number):
    return 0 <= number < CHUNKS


def is_middle():
    rank = lax.axis_index("rep")
    return (rank == 1) | (rank == 2)


def is_end():
    rank = lax.axis_index("rep")
    return (rank == 0) | (rank == 3)


class NoLine:
    ticks = 0

    def signal(self, barrier):
        pass

    def greet(self, barrier, others):
        if others:
            pl.semaphore_wait(barrier, others)

    def start(self):
        pass

    def step(self, times=1):
        pass

    def end(self):
        pass


class Line:
    def __init__(self, first, ticks, picks, refs, outs, scratch):
        self.first, self.ticks, self.picks, self.refs, self.outs = first, ticks, picks, refs, outs
        (
            self.inward, self.across, self.own, self.pair, self.total, self.sems, self.local,
            self.carries,
        ) = scratch
        rank = lax.axis_index("rep")
        self.partner = {"rep": rank + 1 - 2 * (rank % 2)}
        self.peer = {"rep": 3 - rank}
        self.now = 0
        self.kept = []

    def signal(self, barrier):
        pl.semaphore_signal(barrier, inc=1, device_id=self.partner, device_id_type=MESH)

        @pl.when(is_middle())
        def _():
            pl.semaphore_signal(barrier, inc=1, device_id=self.peer, device_id_type=MESH)

    def greet(self, barrier, others):
        @pl.when(is_middle())
        def _():
            pl.semaphore_wait(barrier, others + 2)

        @pl.when(is_end())
        def _():
            pl.semaphore_wait(barrier, others + 1)

    def remote(self, hop, number, src, dst, device):
        return pltpu.make_async_remote_copy(
            src_ref=src, dst_ref=dst, send_sem=self.sems.at[0, hop, number],
            recv_sem=self.sems.at[1, hop, number], device_id=device, device_id_type=MESH,
        )

    def hops(self, number):
        tick = self.first + number
        term = pair = total = None
        if is_chunk(tick):
            which, pick = self.picks[tick]
            term = (
                lambda: self.remote(
                    0, number, pick(self.refs[which]), self.inward.at[number], self.partner
                ),
                lambda: pltpu.make_async_copy(
                    pick(self.refs[which]), self.own.at[tick % LAG], self.local.at[0, number]
                ),
            )
        if is_chunk(tick - LAG):
            held = self.pair.at[(tick - LAG) % (LAG + 1)]
            before = self.refs[f"pair{number}"] if number < LAG else held
            pair = (
                lambda: self.remote(1, number, before, self.across.at[number], self.peer),
                lambda: pltpu.make_async_copy(before, held, self.carries.at[0, number]),
            )
        if is_chunk(tick - 2 * LAG):
            held_total = self.total.at[(tick - 2 * LAG) % (LAG + 1)]
            done = self.refs[f"total{number}"] if number < LAG else held_total
            slot = self.outs[tick - 2 * LAG]
            total = (
                lambda: self.remote(2, number, done, slot, self.partner),
                lambda: pltpu.make_async_copy(done, slot, self.local.at[1, number]),
            )
        return term, pair, total

    def open(self, number):
        term, pair, total = self.hops(number)

        @pl.when(is_end())
        def _():
            if term:
                term[0]().start()

        @pl.when(is_middle())
        def _():
            if pair:
                pair[0]().start()
            if total:
                total[0]().start()
            if term:
                term[1]().start()
            if total:
                total[1]().start()
            if pair and number < LAG:
                pair[1]().start()

    def close(self, number):
        term, pair, total = self.hops(number)

        @pl.when(is_end())
        def _():
            if term:
                term[0]().wait_send()
            if total:
                total[0]().wait_recv()

        @pl.when(is_middle())
        def _():
            if total:
                total[0]().wait_send()
                total[1]().wait()
            if pair:
                pair[0]().wait_send()
                pair[0]().wait_recv()
            if term:
                term[0]().wait_recv()

    def add(self, number):
        term, pair, _ = self.hops(number)
        tick = self.first + number

        def sum_of(into, first, second):
            def one(g, _):
                into[g] = (first[g].astype(f32) + second[g].astype(f32)).astype(bf16)
                return 0

            lax.fori_loop(0, into.shape[0], one, 0)

        @pl.when(is_middle())
        def _():
            if pair:
                if number < LAG:
                    pair[1]().wait()
                before = tick - LAG
                sum_of(
                    self.total.at[before % (LAG + 1)], self.pair.at[before % (LAG + 1)],
                    self.across.at[number],
                )
            if term:
                term[1]().wait()
                sum_of(self.pair.at[tick % (LAG + 1)], self.own.at[tick % LAG], self.inward.at[number])

    def keep(self, number):
        tick = self.first + number
        which = number - (self.ticks - LAG)
        made = []
        if is_chunk(tick):
            made.append((self.pair.at[tick % (LAG + 1)], self.outs[f"pair{which}"], (1, which)))
        if is_chunk(tick - LAG):
            held = self.total.at[(tick - LAG) % (LAG + 1)]
            made.append((held, self.outs[f"total{which}"], (2, which)))
        copies = [
            lambda src=src, dst=dst, at=at: pltpu.make_async_copy(src, dst, self.carries.at[*at])
            for src, dst, at in made
        ]

        @pl.when(is_middle())
        def _():
            for copy in copies:
                copy().start()

        self.kept += copies

    def start(self):
        for number in range(LAG):
            self.open(number)

    def step(self, times=1):
        for _ in range(times):
            if self.now + LAG < self.ticks:
                self.settle()
                self.open(self.now + LAG - 1)

    def settle(self):
        self.close(self.now)
        self.add(self.now)
        if self.now >= self.ticks - LAG:
            self.keep(self.now)
        self.now += 1

    def end(self):
        while self.now + LAG < self.ticks:
            self.step()
        while self.now < self.ticks:
            self.settle()

        @pl.when(is_middle())
        def _():
            for copy in self.kept:
                copy().wait()


def line_slots(first, ticks):
    return [t - 2 * LAG for t in range(first, first + ticks) if is_chunk(t - 2 * LAG)]


class Sums:
    def __init__(self, shape):
        self.shape, self.tick, self.kept, self.done = shape, 0, {}, {}


def run(kernel, ins, outs, scratch, number, cost, sums=None, ticks=0, arrays=(), picks=None, vmem=58):
    ins, outs, scratch = list(ins), list(outs), list(scratch)
    counts = (len(ins), len(outs), len(scratch))
    first = sums.tick if ticks else 0
    names_in, names_out = [], []
    if ticks:
        for name, array in arrays:
            names_in.append(name)
            ins.append((array, pl.ANY))
        for which in range(LAG):
            for name, chunk_at in ((f"pair{which}", first - LAG), (f"total{which}", first - 2 * LAG)):
                if is_chunk(chunk_at + which):
                    names_in.append(name)
                    ins.append((sums.kept[name], pl.ANY))
        names_out = line_slots(first, ticks)
        after = first + ticks
        for which in range(LAG):
            for name, chunk_at in ((f"pair{which}", after - LAG), (f"total{which}", after - 2 * LAG)):
                if is_chunk(chunk_at + which):
                    names_out.append(name)
        outs += [(jax.ShapeDtypeStruct(sums.shape, bf16), pl.ANY)] * len(names_out)
        scratch += [
            pltpu.VMEM((ticks,) + sums.shape, bf16),
            pltpu.VMEM((ticks,) + sums.shape, bf16),
            pltpu.VMEM((LAG,) + sums.shape, bf16),
            pltpu.VMEM((LAG + 1,) + sums.shape, bf16),
            pltpu.VMEM((LAG + 1,) + sums.shape, bf16),
            pltpu.SemaphoreType.DMA((2, 3, ticks)),
            pltpu.SemaphoreType.DMA((2, ticks)),
            pltpu.SemaphoreType.DMA((3, LAG)),
        ]

    def body(*refs):
        in_refs, rest = refs[: len(ins)], refs[len(ins) :]
        out_refs, scratch_refs = rest[: len(outs)], rest[len(outs) :]
        line = NoLine()
        if ticks:
            line = Line(
                first, ticks, picks, dict(zip(names_in, in_refs[counts[0] :])),
                dict(zip(names_out, out_refs[counts[1] :])), scratch_refs[counts[2] :],
            )
        kernel(in_refs[: counts[0]], out_refs[: counts[1]], scratch_refs[: counts[2]], line)

    results = pl.pallas_call(
        body,
        out_shape=tuple(shape for shape, _ in outs),
        in_specs=[pl.BlockSpec(memory_space=space) for _, space in ins],
        out_specs=tuple(pl.BlockSpec(memory_space=space) for _, space in outs),
        scratch_shapes=scratch,
        compiler_params=pltpu.CompilerParams(
            vmem_limit_bytes=vmem * 2**20,
            **({} if number is None else {"collective_id": number, "has_side_effects": True}),
        ),
        cost_estimate=pl.CostEstimate(
            flops=cost[0], bytes_accessed=cost[1], transcendentals=cost[2]
        ),
    )(*[array for array, _ in ins])
    for name, result in zip(names_out, results[counts[1] :]):
        if name in line_slots(first, ticks):
            sums.done[name] = result
        else:
            sums.kept[name] = result
    if ticks:
        sums.tick += ticks
    return results[: counts[1]]


SMEM, VMEM, ANY = pltpu.SMEM, pltpu.VMEM, pl.ANY


def attend_back_kernel(
    heads, block, ins, outs, scratch, line
):
    grad_ref, out_ref, q_ref, k_ref, v_ref, lse_ref, cos_ref, sin_ref, piece_ref = ins
    (grad_qkv_ref,) = outs
    grads, centers, grad_q = scratch
    if line.ticks:
        line.signal(pltpu.get_barrier_semaphore())
        line.greet(pltpu.get_barrier_semaphore(), 0)
        line.start()
    length = grad_ref.shape[0]
    blocks = length // block

    def take_block(i, _):
        rows = pl.ds(pl.multiple_of(i * block, block), block)
        for h in range(heads):
            grad = grad_ref[rows, h * HD : (h + 1) * HD].astype(bf16)
            grads[h, rows, :] = grad
            product = grad.astype(f32) * out_ref[rows, h * HD : (h + 1) * HD].astype(f32)
            centers[h, rows, :] = jnp.broadcast_to(
                jnp.sum(product, 1, keepdims=True), (block, HD)
            )
        return 0

    lax.fori_loop(0, blocks, take_block, 0)
    grad_q[...] = jnp.zeros_like(grad_q)

    def key_block(j, _):
        cols = pl.ds(pl.multiple_of(j * block, block), block)
        key, value = k_ref[cols, :], v_ref[cols, :]

        def one(i, state, diagonal):
            grad_key, grad_value = state
            rows = pl.ds(pl.multiple_of(i * block, block), block)
            for h in range(heads):
                query, grad = q_ref[h, rows, :], grads[h, rows, :]
                log_total = lse_ref[h : h + 1, rows]
                center = centers[h, rows, :].T[0:1, :]
                prob = jnp.exp2(against_rows(key, query) * TO_EXP2 - log_total)
                if diagonal:
                    k_at = lax.broadcasted_iota(jnp.int32, (block, block), 0)
                    q_at = lax.broadcasted_iota(jnp.int32, (block, block), 1)
                    q_piece = piece_ref[0:1, cols].astype(f32)
                    k_piece = as_column(q_piece)
                    allowed = (k_at <= q_at) | ((q_piece != 0) & (q_piece == k_piece))
                    prob = jnp.where(allowed, prob, 0.0)
                grad_prob = against_rows(value, grad)
                grad_score = (prob * (grad_prob - center)).astype(bf16)
                grad_value = grad_value + matmul_f32(prob.astype(bf16), grad)
                grad_key = grad_key + matmul_f32(grad_score, query)
                grad_q[h, rows, :] += over_tokens(grad_score, key)
            return grad_key, grad_value

        zero = jnp.zeros((block, HD), f32)
        state = one(j, (zero, zero), True)
        grad_key, grad_value = lax.fori_loop(
            j + 1, blocks, functools.partial(one, diagonal=False), state
        )
        grad_key = grad_key * SCORE_SCALE
        grad_key = grad_key * cos_ref[cols, :] - pltpu.roll(grad_key, HD // 2, 1) * sin_ref[cols, :]
        grad_qkv_ref[cols, heads * HD : (heads + 1) * HD] = grad_key.astype(bf16)
        grad_qkv_ref[cols, (heads + 1) * HD :] = grad_value.astype(bf16)
        return 0

    for j in range(min(2, blocks - 1)):
        lax.fori_loop(j, j + 1, key_block, 0)
        line.step(1 + j)
    lax.fori_loop(min(2, blocks - 1), blocks, key_block, 0)

    def turn_back(i, _):
        rows = pl.ds(pl.multiple_of(i * block, block), block)
        for h in range(heads):
            grad = grad_q[h, rows, :] * SCORE_SCALE
            grad = grad * cos_ref[rows, :] - pltpu.roll(grad, HD // 2, 1) * sin_ref[rows, :]
            grad_qkv_ref[rows, h * HD : (h + 1) * HD] = grad.astype(bf16)
        return 0

    lax.fori_loop(0, blocks, turn_back, 0)
    line.end()


def take_cuts_kernel(cuts, holder_ref, rows_ref, out_ref):
    cut = out_ref.shape[0] // cuts

    def one(p, _):
        src = pl.ds(pl.multiple_of(holder_ref[0, p] * cut, cut), cut)
        out_ref[pl.ds(pl.multiple_of(p * cut, cut), cut), :] = rows_ref[src, :]
        return 0

    lax.fori_loop(0, cuts, one, 0)


def take_cuts(holder, rows):
    return pl.pallas_call(
        functools.partial(take_cuts_kernel, holder.shape[1]),
        out_shape=jax.ShapeDtypeStruct(rows.shape, rows.dtype),
        in_specs=[pl.BlockSpec(memory_space=pltpu.SMEM)] + vmem_specs(1),
        out_specs=pl.BlockSpec(memory_space=pltpu.VMEM),
        cost_estimate=pl.CostEstimate(
            flops=0, bytes_accessed=2 * rows.size * rows.dtype.itemsize, transcendentals=0
        ),
    )(holder, rows)


def attend_back(
    order, grad, out, query, key, value, lse, cosine, sine, piece, heads, **line
):
    cuts = jnp.arange(order.shape[1], dtype=order.dtype)
    holder = jnp.sum(jnp.where(order[0][None, :] == cuts[:, None], cuts[None, :], 0), 1)[None, :]
    length = grad.shape[0]
    block = min(512, length)
    tall = [take_cuts(holder, grad), out, query, key, value, lse, cosine, sine, piece]
    grad_qkv = run(
        functools.partial(attend_back_kernel, heads, block),
        [(array, VMEM) for array in tall],
        [(jax.ShapeDtypeStruct((length, (heads + 2) * HD), bf16), VMEM)],
        [
            pltpu.VMEM((heads, length, HD), bf16),
            pltpu.VMEM((heads, length, HD), f32),
            pltpu.VMEM((heads, length, HD), f32),
        ],
        line.pop("number", None),
        (8 * heads * length * length * HD, 14 * length * HD * heads * 4, heads * length * length // 2),
        **line,
    )[0]
    return take_cuts(order, grad_qkv)


def place_in_group():
    me = lax.axis_index("grp")
    return me // 4, (me // 2) % 2, me % 2


def other(flip_y, flip_x, flip_core):
    y, x, core = place_in_group()
    return ((y + flip_y) % 2) * 4 + ((x + flip_x) % 2) * 2 + (core + flip_core) % 2


def chip_rows(flip_y, flip_x, rows):
    y, x, _ = place_in_group()
    first = (((y + flip_y) % 2) * 2 + (x + flip_x) % 2) * (2 * rows)
    return pl.ds(pl.multiple_of(first, 2 * rows), 2 * rows)


NEIGHBOURS = ((0, 0, 1), (0, 1, 0), (1, 0, 0))
EVERYONE = tuple((n // 4, (n // 2) % 2, n % 2) for n in range(1, 8))


def greet_group(line, flips=NEIGHBOURS, between=None):
    barrier = pltpu.get_barrier_semaphore()
    for flip in flips:
        pl.semaphore_signal(barrier, inc=1, device_id={"grp": other(*flip)}, device_id_type=MESH)
    line.signal(barrier)
    if between:
        between()
    line.greet(barrier, len(flips))


SIBLING, ALONG_X, ALONG_Y, ACROSS = (0, 0), (0, 1), (1, 0), (1, 1)


class Gather:
    TO_S, TO_X, TO_Y = (0, 0, 1), (0, 1, 0), (1, 0, 0)

    def __init__(self, rows, all_ref, sends, recvs):
        self.rows, self.all_ref, self.sends, self.recvs = rows, all_ref, sends, recvs
        self.started = []

    def copy(self, number, chip, core, part, target):
        first = other(*chip, core) * self.rows
        if part is None:
            where = pl.ds(pl.multiple_of(first, self.rows), self.rows)
        else:
            half = self.rows // 2
            where = pl.ds(pl.multiple_of(first + part * half, half), half)
        where = self.all_ref.at[where, :]
        return pltpu.make_async_remote_copy(
            src_ref=where, dst_ref=where, send_sem=self.sends.at[number],
            recv_sem=self.recvs.at[number], device_id={"grp": other(*target)}, device_id_type=MESH,
        )

    def send(self, *what):
        one = self.copy(*what)
        one.start()
        self.started.append(one)

    def landed(self, number, chip, core, part):
        self.copy(number, chip, core, part, self.TO_S).wait_recv()

    def send_own(self):
        self.send(1, SIBLING, 0, 1, self.TO_X)
        self.send(3, SIBLING, 0, 0, self.TO_Y)
        self.send(0, SIBLING, 0, None, self.TO_S)
        self.send(2, SIBLING, 0, 0, self.TO_X)
        self.send(4, SIBLING, 0, 1, self.TO_Y)

    def sibling(self):
        self.landed(0, SIBLING, 1, None)

    def relay(self):
        self.landed(1, ALONG_X, 0, 1)
        self.send(6, ALONG_X, 0, 1, self.TO_Y)
        self.landed(3, ALONG_Y, 0, 0)
        self.send(5, ALONG_Y, 0, 0, self.TO_X)
        self.send(7, ALONG_X, 0, 1, self.TO_S)
        self.send(8, ALONG_Y, 0, 0, self.TO_S)

    def pass_second(self):
        self.landed(2, ALONG_X, 0, 0)
        self.send(9, ALONG_X, 0, 0, self.TO_S)
        self.landed(4, ALONG_Y, 0, 1)
        self.send(10, ALONG_Y, 0, 1, self.TO_S)

    def along_x(self):
        self.landed(7, ALONG_X, 1, 1)
        self.landed(9, ALONG_X, 1, 0)

    def pass_across(self):
        self.landed(5, ACROSS, 0, 0)
        self.send(11, ACROSS, 0, 0, self.TO_S)
        self.landed(6, ACROSS, 0, 1)
        self.send(12, ACROSS, 0, 1, self.TO_S)

    def along_y(self):
        self.landed(8, ALONG_Y, 1, 0)
        self.landed(10, ALONG_Y, 1, 1)

    def across(self):
        self.landed(11, ACROSS, 1, 0)
        self.landed(12, ACROSS, 1, 1)

    def finish(self):
        for one in self.started:
            one.wait_send()


def gather_rows(rows, all_ref, sends, recvs, on_chip, line, then=None):
    rows_of = Gather(rows, all_ref, sends, recvs)
    rows_of.send_own()
    if then:
        then()
    rows_of.sibling()
    on_chip(*SIBLING)
    rows_of.relay()
    line.step(2)
    rows_of.pass_second()
    line.step(2)
    rows_of.along_x()
    on_chip(*ALONG_X)
    rows_of.pass_across()
    line.step()
    rows_of.along_y()
    on_chip(*ALONG_Y)
    rows_of.across()
    on_chip(*ACROSS)
    rows_of.finish()
    line.end()


GATHER_COPIES = 13


def rms_normed(values, gain):
    return values * lax.rsqrt(jnp.mean(values * values, -1, keepdims=True) + EPS) * gain


class Moves:
    def __init__(self, sems):
        self.sems, self.count, self.open = sems, 0, []

    def start(self, src, dst):
        one = pltpu.make_async_copy(src, dst, self.sems.at[self.count])
        self.count += 1
        one.start()
        return one

    def later(self, src, dst):
        self.open.append(self.start(src, dst))

    def finish(self):
        for one in self.open:
            one.wait()


def gather_scratch(rows, width, moves):
    return [
        pltpu.VMEM((8 * rows, width), bf16),
        pltpu.SemaphoreType.DMA((GATHER_COPIES,)),
        pltpu.SemaphoreType.DMA((GATHER_COPIES,)),
        pltpu.SemaphoreType.DMA((moves,)),
    ]


def own_rows(rows):
    return pl.ds(pl.multiple_of(other(0, 0, 0) * rows, rows), rows)


def send_columns(pieces, sends, recvs, moves):
    copies = []
    for which, (rows_ref, width, there) in enumerate(pieces):
        for number, flip in enumerate(EVERYONE):
            target = other(*flip)
            cols = pl.ds(pl.multiple_of(target * width, width), width)
            one = pltpu.make_async_remote_copy(
                src_ref=rows_ref.at[:, cols], dst_ref=there,
                send_sem=sends.at[which, number], recv_sem=recvs.at[which, number],
                device_id={"grp": target}, device_id_type=MESH,
            )
            one.start()
            copies.append(one)
        mine = pl.ds(pl.multiple_of(other(0, 0, 0) * width, width), width)
        moves.later(rows_ref.at[:, mine], there)
    return copies


def gather_normed_kernel(ins, outs, scratch, line):
    x_ref, gain_ref = ins[:2]
    weights = ins[2:]
    all_ref, cols_ref = outs
    held, sends, recvs, sems, col_sends, col_recvs = scratch
    rows = x_ref.shape[0]
    moves = Moves(sems)

    def fill():
        held[own_rows(rows), :] = rms_normed(x_ref[...].astype(f32), gain_ref[...]).astype(bf16)

    greet_group(line, EVERYONE, fill)
    col_copies = []

    def send_weights():
        pieces, low = [], 0
        tall = weights[0].shape[0]
        there = pl.ds(pl.multiple_of(other(0, 0, 0) * tall, tall), tall)
        for weight in weights:
            width = weight.shape[1] // 8
            pieces.append((weight, width, cols_ref.at[there, low : low + width]))
            low += width
        col_copies.extend(send_columns(pieces, col_sends, col_recvs, moves))

    def on_chip(*chip):
        where = chip_rows(*chip, rows)
        moves.later(held.at[where, :], all_ref.at[where, :])

    gather_rows(rows, held, sends, recvs, on_chip, line, send_weights)
    for one in col_copies:
        one.wait()
    moves.finish()


def gather_normed(x, gain, weights, **line):
    rows, width = x.shape
    deep = sum(weight.shape[1] for weight in weights) // 8
    return run(
        gather_normed_kernel,
        [(x, VMEM), (gain, VMEM)] + [(weight, ANY) for weight in weights],
        [
            (jax.ShapeDtypeStruct((8 * rows, width), bf16), ANY),
            (jax.ShapeDtypeStruct((8 * weights[0].shape[0], deep), bf16), ANY),
        ],
        gather_scratch(rows, width, 4 + len(weights))
        + [pltpu.SemaphoreType.DMA((len(weights), 7))] * 2,
        line.pop("number"),
        (0, 150 * rows * width * 2, 0),
        **line,
    )


def columns_kernel(rows_here, ins, outs, scratch, line):
    (cols_ref,) = outs
    sends, recvs, sems = scratch
    moves = Moves(sems)
    barrier = pltpu.get_barrier_semaphore()
    for flip in EVERYONE:
        pl.semaphore_signal(barrier, inc=1, device_id={"grp": other(*flip)}, device_id_type=MESH)
    pl.semaphore_wait(barrier, 7)
    first = pl.multiple_of(lax.axis_index("rep") * rows_here, rows_here)
    me = other(0, 0, 0)
    pieces, low = [], 0
    for weight in ins:
        width = weight.shape[1] // 8
        pieces.append(
            (weight.at[pl.ds(first, rows_here), :], width, cols_ref.at[me, :, low : low + width])
        )
        low += width
    for one in send_columns(pieces, sends, recvs, moves):
        one.wait()
    moves.finish()


def columns_of_some(weights, rows_here, number):
    deep = sum(weight.shape[1] for weight in weights) // 8
    return run(
        functools.partial(columns_kernel, rows_here),
        [(weight, ANY) for weight in weights],
        [(jax.ShapeDtypeStruct((8, rows_here, deep), bf16), ANY)],
        [pltpu.SemaphoreType.DMA((len(weights), 7))] * 2
        + [pltpu.SemaphoreType.DMA((len(weights),))],
        number, (0, 50 * 8 * rows_here * deep, 0),
    )[0]


def feed_forward_kernel(tile, ins, outs, scratch, line):
    mid_ref, gain_ref, grad_ref, spread_ref, rest_ref, w_down_ref = ins
    all_ref, hidden_ref, whole_ref, grad_gate_up_ref, down_ref = outs
    held, grads_held, sends, recvs, grad_sends, grad_recvs, sems = scratch[:7]
    weight, w_down, hidden, up_part, gate_part, grads, down = scratch[7:]
    rows = mid_ref.shape[0]
    inner = hidden.shape[1]
    moves = Moves(sems)
    planes, _, tall, _ = spread_ref.shape
    loads = [
        moves.start(spread_ref.at[z], weight.at[:, z * tall : (z + 1) * tall, :])
        for z in range(planes)
    ]
    loads.append(moves.start(rest_ref, weight.at[:, planes * tall :, :]))
    down_load = moves.start(w_down_ref, w_down)

    def fill():
        held[own_rows(rows), :] = rms_normed(mid_ref[...], gain_ref[...]).astype(bf16)
        grads_held[own_rows(rows), :] = grad_ref[...]

    greet_group(line, between=fill)
    first = Gather(rows, held, sends, recvs)
    second = Gather(rows, grads_held, grad_sends, grad_recvs)
    stored = []

    def forward(*chip):
        where = chip_rows(*chip, rows)
        moves.later(held.at[where, :], all_ref.at[where, :])

        def column(t, _):
            cols = pl.ds(pl.multiple_of(t * tile, tile), tile)
            up_cols = pl.ds(pl.multiple_of(inner + t * tile, tile), tile)
            lhs = held[where, :]
            gate = matmul_f32(lhs, weight[:, :, cols].reshape(-1, tile))
            up = matmul_f32(lhs, weight[:, :, up_cols].reshape(-1, tile))
            sigma = 1.0 / (1.0 + jnp.exp(-gate))
            swish = gate * sigma
            hidden[where, cols] = (swish * up).astype(bf16)
            up_part[where, cols] = swish.astype(bf16)
            gate_part[where, cols] = (up * sigma * (1.0 + gate * (1.0 - sigma))).astype(bf16)
            return 0

        lax.fori_loop(0, inner // tile, column, 0)
        moves.later(hidden.at[where, :], hidden_ref.at[where, :])

    def backward(*chip):
        where = chip_rows(*chip, rows)
        slot = len(stored) % 2
        if len(stored) >= 2:
            stored[len(stored) - 2].wait()

        def column(t, _):
            cols = pl.ds(pl.multiple_of(t * tile, tile), tile)
            up_cols = pl.ds(pl.multiple_of(inner + t * tile, tile), tile)
            incoming = grads_held[where, :]
            grad_hidden = against_rows(incoming, w_down[cols, :])
            grads[slot, :, cols] = (grad_hidden * gate_part[where, cols].astype(f32)).astype(bf16)
            grads[slot, :, up_cols] = (grad_hidden * up_part[where, cols].astype(f32)).astype(bf16)
            term = over_tokens(hidden[where, cols], incoming)
            if chip == SIBLING:
                down[cols, :] = term
            elif chip == ACROSS:
                weight[t] = (down[cols, :] + term).astype(bf16)
            else:
                down[cols, :] += term
            return 0

        lax.fori_loop(0, inner // tile, column, 0)
        stored.append(moves.start(grads.at[slot], grad_gate_up_ref.at[where, :]))

    first.send_own()
    for one in loads:
        one.wait()
    whole = moves.start(weight, whole_ref)
    first.sibling()
    forward(*SIBLING)
    first.relay()
    first.pass_second()
    second.send_own()
    first.along_x()
    forward(*ALONG_X)
    first.pass_across()
    first.along_y()
    forward(*ALONG_Y)
    second.relay()
    first.across()
    forward(*ACROSS)
    down_load.wait()
    second.sibling()
    backward(*SIBLING)
    second.pass_second()
    second.along_x()
    backward(*ALONG_X)
    second.pass_across()
    second.along_y()
    backward(*ALONG_Y)
    second.across()
    whole.wait()
    backward(*ACROSS)
    moves.later(weight.at[: inner // tile], down_ref)
    first.finish()
    second.finish()
    for one in stored[-2:]:
        one.wait()
    moves.finish()


def feed_forward(mid, gain, grad, spread, rest, w_down, **line):
    rows, width = mid.shape
    inner = w_down.shape[0]
    weight = (8, width // 8, 2 * inner)
    return run(
        functools.partial(feed_forward_kernel, weight[1]),
        [(mid, VMEM), (gain, VMEM), (grad, VMEM), (spread, ANY), (rest, ANY), (w_down, ANY)],
        [
            (jax.ShapeDtypeStruct((8 * rows, width), bf16), ANY),
            (jax.ShapeDtypeStruct((8 * rows, inner), bf16), ANY),
            (jax.ShapeDtypeStruct(weight, bf16), ANY),
            (jax.ShapeDtypeStruct((8 * rows, 2 * inner), bf16), ANY),
            (jax.ShapeDtypeStruct((inner // weight[1], weight[1], width), bf16), ANY),
        ],
        [pltpu.VMEM((8 * rows, width), bf16)] * 2
        + [pltpu.SemaphoreType.DMA((GATHER_COPIES,))] * 4
        + [pltpu.SemaphoreType.DMA((20,))]
        + [pltpu.VMEM(weight, bf16), pltpu.VMEM(w_down.shape, bf16)]
        + [pltpu.VMEM((8 * rows, inner), bf16)] * 3
        + [
            pltpu.VMEM((2, 2 * rows, 2 * inner), bf16),
            pltpu.VMEM(w_down.shape, f32),
        ],
        line.pop("number"),
        (64 * rows * width * inner, 300 * rows * width * 2, 8 * rows * inner),
        vmem=61,
        **line,
    )


def attended_back_kernel(ins, outs, scratch, line):
    grad_ref, w_ref, attended_ref = ins
    grad_attended_ref, out_term_ref = outs
    held, sends, recvs, sems, total = scratch
    rows = grad_ref.shape[0]
    moves = Moves(sems)
    greet_group(line)
    line.start()
    held[own_rows(rows), :] = grad_ref[...].astype(bf16)

    def on_chip(*chip):
        where = chip_rows(*chip, rows)
        incoming = held[where, :]
        grad_attended_ref[where, :] = against_rows(incoming, w_ref[...]).astype(bf16)
        term = over_tokens(attended_ref[where, :], incoming)
        if chip == SIBLING:
            total[...] = term
        elif chip == ACROSS:
            out_term_ref[...] = (total[...] + term).astype(bf16)
        else:
            total[...] += term

    gather_rows(rows, held, sends, recvs, on_chip, line)
    moves.finish()


def attended_back(grad, w_out, attended, **line):
    rows, width = grad.shape
    return run(
        attended_back_kernel,
        [(array, VMEM) for array in (grad, w_out, attended)],
        [
            (jax.ShapeDtypeStruct(attended.shape, bf16), VMEM),
            (jax.ShapeDtypeStruct(w_out.shape, bf16), VMEM),
        ],
        gather_scratch(rows, width, 1) + [pltpu.VMEM(w_out.shape, f32)],
        line.pop("number"),
        (32 * rows * width * w_out.shape[0], 150 * rows * width * 2, 0),
        **line,
    )


class WeightTerm:
    def __init__(self, rows_ref, columns_ref, term_ref, scratch):
        self.rows_ref, self.columns_ref, self.term_ref = rows_ref, columns_ref, term_ref
        self.loaded, self.ready, self.sems = scratch
        self.tile = self.loaded.shape[2]
        for number in (0, 1):
            self.load(number).start()

    def load(self, number):
        cols = slice(number * self.tile, (number + 1) * self.tile)
        return pltpu.make_async_copy(
            self.rows_ref.at[:, cols], self.loaded.at[number % 2], self.sems.at[0, number % 2]
        )

    def store(self, number):
        return pltpu.make_async_copy(
            self.ready.at[number % 2], self.term_ref.at[number], self.sems.at[1, number % 2]
        )

    def work(self, numbers):
        for number in numbers:
            at = number % 2
            self.load(number).wait()
            if number >= 2:
                self.store(number - 2).wait()
            width = self.columns_ref.shape[1]
            step = min(256, width)

            def column(t, _):
                cols = pl.ds(pl.multiple_of(t * step, step), step)
                term = over_tokens(self.loaded[at], self.columns_ref[:, cols])
                self.ready[at, :, cols] = term.astype(bf16)
                return 0

            lax.fori_loop(0, width // step, column, 0)
            self.store(number).start()
            if number + 2 < 8:
                self.load(number + 2).start()

    def finish(self):
        for number in (6, 7):
            self.store(number).wait()


def scatter_kernel(turned, tile, extra, after, steps, ins, outs, scratch, line):
    out_ref = outs[0] if after == "base" else scratch[-4]
    finals = ins[len(ins) - {"base": 1, "cast": 1, "back": 3}[after] :]
    part, to_s, from_s, to_chip, held, relay, last, sends, recvs = scratch[:9]
    a_ref, b_ref, loads = scratch[-3:]
    loading = [
        pltpu.make_async_copy(src, dst, loads.at[number])
        for number, (src, dst) in enumerate(((ins[1], b_ref), (ins[0], a_ref)))
    ]
    for one in loading:
        one.start()
    rows, width = out_ref.shape
    half = rows // 2
    _, _, core = place_in_group()
    greet_group(line)
    line.start()
    if extra:
        columns_ref = a_ref
        if extra == "loaded":
            columns_ref = scratch[12]
            columns_copy = pltpu.make_async_copy(ins[3], columns_ref, scratch[13].at[0])
            columns_copy.start()
        term = WeightTerm(ins[2], columns_ref, outs[-1], scratch[9:12])
    for one in loading:
        one.wait()
    own_at = pl.multiple_of(core * rows, rows)
    other_at = pl.multiple_of((1 - core) * rows, rows)
    started = []

    def send(number, src, dst, target):
        one = pltpu.make_async_remote_copy(
            src_ref=src, dst_ref=dst, send_sem=sends.at[number], recv_sem=recvs.at[number],
            device_id={"grp": other(*target)}, device_id_type=MESH,
        )
        one.start()
        started.append(one)
        return one

    def landed(number, where):
        pltpu.make_async_remote_copy(
            src_ref=where, dst_ref=where, send_sem=sends.at[number], recv_sem=recvs.at[number],
            device_id={"grp": other(0, 0, 1)}, device_id_type=MESH,
        ).wait_recv()

    to_sib, to_x, to_y = (0, 0, 1), (0, 1, 0), (1, 0, 0)

    def make(number, chip):
        where = chip_rows(*chip, rows)

        def column(t, _):
            cols = pl.ds(pl.multiple_of(t * tile, tile), tile)
            lhs = a_ref[where, :]
            if turned:
                part[:, cols] = against_rows(lhs, b_ref[cols, :])
            else:
                part[:, cols] = matmul_f32(lhs, b_ref[:, cols])
            return 0

        lax.fori_loop(0, width // tile, column, 0)
        to_s[number] = part[pl.ds(other_at, rows), :].astype(bf16)
        send(number, to_s.at[number], from_s.at[number], to_sib)

    def own(low, number):
        at = pl.ds(pl.multiple_of(core * rows + low * half, half), half)
        return part[at, :] + from_s[number, low * half : (low + 1) * half, :].astype(f32)

    first, second = slice(0, half), slice(half, rows)
    step = lambda point: line.step(steps.get(point, 0))
    make(0, ACROSS)
    landed(0, from_s.at[0])
    to_chip[0, first, :] = own(0, 0).astype(bf16)
    send(4, to_chip.at[0, first, :], relay.at[0], to_x)
    to_chip[0, second, :] = own(1, 0).astype(bf16)
    send(5, to_chip.at[0, second, :], relay.at[1], to_y)
    step("across")
    make(1, ALONG_X)
    landed(1, from_s.at[1])
    to_chip[1, first, :] = own(0, 1).astype(bf16)
    send(6, to_chip.at[1, first, :], last.at[0, first, :], to_x)
    held[0] = own(1, 1)
    step("x")
    make(2, ALONG_Y)
    landed(2, from_s.at[2])
    to_chip[2, second, :] = own(1, 2).astype(bf16)
    send(7, to_chip.at[2, second, :], last.at[1, second, :], to_y)
    held[1] = own(0, 2)
    step("y")
    if extra:
        if extra == "loaded":
            columns_copy.wait()
        term.work((0, 1, 2))
        step("work")
    landed(5, relay.at[1])
    to_chip[1, second, :] = (held[0] + relay[1].astype(f32)).astype(bf16)
    send(8, to_chip.at[1, second, :], last.at[0, second, :], to_x)
    landed(4, relay.at[0])
    to_chip[2, first, :] = (held[1] + relay[0].astype(f32)).astype(bf16)
    send(9, to_chip.at[2, first, :], last.at[1, first, :], to_y)
    step("relayed")
    make(3, SIBLING)
    step("sibling")
    if extra:
        term.work((3, 4))
        step("work2")
        term.work((5, 6, 7))
        step("work3")
    landed(3, from_s.at[3])
    for low in (0, 1):
        at = slice(low * half, (low + 1) * half)
        if after == "back":
            out_ref[at, :] = own(low, 3)
        else:
            out_ref[at, :] = own(low, 3) + finals[0][at, :].astype(f32)
    landed(6, last.at[0, first, :])
    out_ref[first, :] += last[0, first, :].astype(f32)
    landed(7, last.at[1, second, :])
    out_ref[second, :] += last[1, second, :].astype(f32)
    step("halves")
    landed(8, last.at[0, second, :])
    out_ref[second, :] += last[0, second, :].astype(f32)
    landed(9, last.at[1, first, :])
    out_ref[first, :] += last[1, first, :].astype(f32)
    if after == "cast":
        outs[0][...] = out_ref[...].astype(outs[0].dtype)
    if after == "back":
        upstream_ref, rows_ref, gain_ref = finals
        some = min(64, rows)

        def norm_rows(number, gain_term):
            at = pl.ds(pl.multiple_of(number * some, some), some)
            values, incoming = rows_ref[at, :].astype(f32), out_ref[at, :]
            inv = lax.rsqrt(jnp.mean(values * values, -1, keepdims=True) + EPS)
            grad, term = norm_back(
                upstream_ref[at, :].astype(f32), incoming, values * inv, inv, gain_ref[...]
            )
            outs[0][at, :] = grad.astype(outs[0].dtype)
            return gain_term + term[None, :]

        outs[1][...] = lax.fori_loop(0, rows // some, norm_rows, jnp.zeros((1, width), f32))
    for one in started:
        one.wait_send()
    if extra:
        term.finish()
    line.end()


def product_scattered(
    a, b, turned, extra=None, base=None, back=None, dtype=f32, steps=None, **line
):
    length, depth = a.shape
    width = b.shape[0] if turned else b.shape[1]
    rows = length // 8
    tile = min(256, width)
    ins = [(a, ANY), (b, ANY)]
    outs = [(jax.ShapeDtypeStruct((rows, width), dtype), VMEM)]
    after = "back" if back else "base" if dtype == f32 else "cast"
    if back:
        outs.append((jax.ShapeDtypeStruct((1, width), f32), VMEM))
    scratch = [
        pltpu.VMEM((2 * rows, width), f32),
        pltpu.VMEM((4, rows, width), bf16),
        pltpu.VMEM((4, rows, width), bf16),
        pltpu.VMEM((3, rows, width), bf16),
        pltpu.VMEM((2, rows // 2, width), f32),
        pltpu.VMEM((2, rows // 2, width), bf16),
        pltpu.VMEM((2, rows, width), bf16),
        pltpu.SemaphoreType.DMA((10,)),
        pltpu.SemaphoreType.DMA((10,)),
    ]
    flops, kind = 2 * length * depth * width, None
    if extra:
        first, second = extra
        kind = "own" if second is None else "loaded"
        ins.append((first, ANY))
        columns = a if second is None else second
        tall = first.shape[1] // 8
        outs.append((jax.ShapeDtypeStruct((8, tall, columns.shape[1]), bf16), ANY))
        scratch += [
            pltpu.VMEM((2, length, tall), bf16),
            pltpu.VMEM((2, tall, columns.shape[1]), bf16),
            pltpu.SemaphoreType.DMA((2, 2)),
        ]
        if second is not None:
            ins.append((second, ANY))
            scratch += [pltpu.VMEM(second.shape, bf16), pltpu.SemaphoreType.DMA((1,))]
        flops += 2 * length * first.shape[1] * columns.shape[1]
    ins += [(array, VMEM) for array in (back or (base,))]
    if after != "base":
        scratch.append(pltpu.VMEM((rows, width), f32))
    scratch += [
        pltpu.VMEM(a.shape, bf16), pltpu.VMEM(b.shape, bf16), pltpu.SemaphoreType.DMA((2,))
    ]
    return run(
        functools.partial(scatter_kernel, turned, tile, kind, after, steps or {}), ins, outs, scratch,
        line.pop("number"), (flops, 150 * rows * width * 2, 0), vmem=61, **line,
    )


def tail_kernel(ready, later, ins, outs, scratch, line):
    qkv_ref, gains_ref = ins[:2]
    chunk_refs = dict(zip(ready, ins[2:]))
    gate_ref, up_ref, qkv_rows_ref, gains_out_ref = outs
    from_group, mine, from_rep, sends, recvs, chunk_sems, local = scratch
    me, rank = other(0, 0, 0), lax.axis_index("rep")
    inner = gate_ref.shape[1] // 8
    part = qkv_ref.shape[-1]
    high = line.outs[later[0]].shape[1]
    barrier = pltpu.get_barrier_semaphore()
    for flip in range(1, 4):
        pl.semaphore_signal(
            barrier, inc=1, device_id={"rep": (rank + flip) % 4}, device_id_type=MESH
        )
    for flip in EVERYONE:
        pl.semaphore_signal(barrier, inc=1, device_id={"grp": other(*flip)}, device_id_type=MESH)
    pl.semaphore_wait(barrier, 10)
    waits, moves = [], Moves(local)
    line.refs["qkv"] = qkv_rows_ref

    def send(kind, number, src, dst, device):
        return pltpu.make_async_remote_copy(
            src_ref=src, dst_ref=dst, send_sem=sends.at[kind, number],
            recv_sem=recvs.at[kind, number], device_id=device, device_id_type=MESH,
        )

    own_qkv = qkv_rows_ref.at[me // 4, :, :, pl.ds(pl.multiple_of((me % 4) * part, part), part)]
    qkv_copies, gain_copies = [], []
    for number, flip in enumerate(EVERYONE):
        target = other(*flip)
        qkv_copies.append(send(0, number, qkv_ref.at[target], own_qkv, {"grp": target}))
        qkv_copies[-1].start()
    moves.later(qkv_ref.at[me], own_qkv)
    line.start()
    for number, flip in enumerate(EVERYONE):
        target = other(*flip)
        gain_copies.append(
            send(1, number, gains_ref.at[target], from_group.at[me], {"grp": target})
        )
        gain_copies[-1].start()
    from_group[me] = gains_ref[me]

    def spread(chunk):
        src = chunk_refs[chunk] if chunk in chunk_refs else line.outs[chunk]
        number = chunk - DOWN
        rows = slice(number // 2 * high, (number // 2 + 1) * high)
        dst = (gate_ref, up_ref)[number % 2]
        there = dst.at[rows, pl.ds(pl.multiple_of(me * inner, inner), inner)]
        for flip in EVERYONE:
            target = other(*flip)
            pltpu.make_async_remote_copy(
                src_ref=src.at[target], dst_ref=there, send_sem=chunk_sems.at[0, number],
                recv_sem=chunk_sems.at[1, number], device_id={"grp": target}, device_id_type=MESH,
            ).start()
        moves.later(src.at[me], there)
        seven = dst.at[rows, : 7 * inner]
        waits.append(
            pltpu.make_async_remote_copy(
                src_ref=seven, dst_ref=seven, send_sem=chunk_sems.at[0, number],
                recv_sem=chunk_sems.at[1, number], device_id={"grp": other(0, 0, 1)},
                device_id_type=MESH,
            )
        )

    for chunk in ready:
        spread(chunk)
    for one in gain_copies:
        one.wait()
    mine[rank] = sum(from_group[g] for g in range(8))
    rep_copies = []
    for step in range(1, 4):
        target = (rank + step) % 4
        rep_copies.append(
            send(2, step, mine.at[rank], from_rep.at[step], {"rep": target})
        )
        rep_copies[-1].start()
    for step, one in zip(range(1, 4), rep_copies):
        one.wait()
        mine[(rank + 4 - step) % 4] = from_rep[step]
    gains_out_ref[...] = (mine[0] + mine[1]) + (mine[2] + mine[3])
    for settled in range(line.ticks - LAG):
        if line.first + settled + LAG == CHUNKS - QKV:
            for one in qkv_copies:
                one.wait()
            moves.open.pop(0).wait()
        line.step()
        chunk = line.first + settled - 2 * LAG
        if chunk in later:
            spread(chunk)
    line.end()
    for one in waits:
        one.wait_send()
        one.wait_recv()
    moves.finish()


def tail(qkv_term, gains, chunks, inner, number, sums, ticks, arrays, picks):
    first = sums.tick
    ready = sorted(chunks)
    later = [c for c in line_slots(first, ticks) if c < DOWN + GATE_UP]
    _, high, width = sums.shape
    wide = jax.ShapeDtypeStruct((GATE_UP // 2 * high, 8 * inner), bf16)
    moved = jax.ShapeDtypeStruct((2, 8, 2 * high, 2 * width), bf16)
    picks = dict(picks)
    for n in range(QKV):
        where = (
            n // 4, slice(None), slice(n // 2 % 2 * high, (n // 2 % 2 + 1) * high),
            slice(n % 2 * width, (n % 2 + 1) * width),
        )
        picks[CHUNKS - QKV + n] = ("qkv", lambda ref, where=where: ref.at[where])
    return run(
        functools.partial(tail_kernel, ready, later),
        [(qkv_term, ANY), (gains, VMEM)] + [(chunks[c], ANY) for c in ready],
        [(wide, ANY), (wide, ANY), (moved, ANY), (jax.ShapeDtypeStruct(gains.shape[1:], f32), VMEM)],
        [
            pltpu.VMEM(gains.shape, f32),
            pltpu.VMEM((4,) + gains.shape[1:], f32),
            pltpu.VMEM((4,) + gains.shape[1:], f32),
            pltpu.SemaphoreType.DMA((3, 7)),
            pltpu.SemaphoreType.DMA((3, 7)),
            pltpu.SemaphoreType.DMA((2, GATE_UP)),
            pltpu.SemaphoreType.DMA((1 + GATE_UP,)),
        ],
        number, (0, 200 * 8 * high * width * 2, 0), sums=sums, ticks=ticks, arrays=arrays, picks=picks,
    )


def finish_kernel(heads, *refs):
    chunks, rest = refs[: DOWN + OUT + QKV], refs[DOWN + OUT + QKV :]
    gate_rows, up_rows = rest[:2]
    query, key, value, out, gate, up, down = rest[2:9]
    low, wide, load_sems, store_sems = rest[9:]
    _, high, width = chunks[0].shape
    depth = low.shape[0]

    def half(number):
        return slice(number * high, (number + 1) * high)

    def side(number):
        return slice(number * width, (number + 1) * width)

    jobs = []
    for n, ref in enumerate(chunks[:DOWN]):
        jobs.append((ref, [(slice(0, width), down.at[n // 2, :, :, side(n % 2)])]))
    for ref, into in ((gate_rows, gate), (up_rows, up)):
        for low_col in range(0, ref.shape[2], low.shape[3]):
            for number in (0, 1):
                where = (slice(None), half(number), slice(low_col, low_col + low.shape[3]))
                jobs.append((ref.at[where], [(slice(0, low.shape[3]), into.at[where])]))
    for n, ref in enumerate(chunks[DOWN : DOWN + OUT]):
        jobs.append((ref, [(slice(0, width), out.at[:, half(n // 2), side(n % 2)])]))
    part = (heads + 2) * HD
    for n, ref in enumerate(chunks[DOWN + OUT :]):
        stores = []
        for place in range(width // part):
            at, device = place * part, (n // 4 * 2 + n % 2) * (width // part) + place
            for into, first, size in (
                (query, 0, heads * HD), (key, heads * HD, HD), (value, (heads + 1) * HD, HD)
            ):
                there = into.at[:, half(n // 2 % 2), device * size : (device + 1) * size]
                stores.append((slice(at + first, at + first + size), there))
        jobs.append((ref, stores))

    def load(number):
        at, ref = number % depth, jobs[number][0]
        return pltpu.make_async_copy(ref, low.at[at, :, :, : ref.shape[2]], load_sems.at[at])

    def stores(number):
        at = number % depth
        return [
            pltpu.make_async_copy(wide.at[at, :, :, cols], into, store_sems.at[at, which])
            for which, (cols, into) in enumerate(jobs[number][1])
        ]

    for number in range(depth - 1):
        load(number).start()
    for number in range(len(jobs)):
        if number + depth - 1 < len(jobs):
            load(number + depth - 1).start()
        load(number).wait()
        if number >= depth:
            for one in stores(number - depth):
                one.wait()

        def cast(g, _, at=number % depth, cols=slice(0, jobs[number][0].shape[2])):
            wide[at, g, :, cols] = low[at, g, :, cols].astype(f32)
            return 0

        lax.fori_loop(0, low.shape[1], cast, 0)
        for one in stores(number):
            one.start()
    for number in range(len(jobs) - depth, len(jobs)):
        for one in stores(number):
            one.wait()


def finish(chunks, gate_rows, up_rows, heads):
    eight, high, width = chunks[0].shape
    width = 2 * width
    rows, wide = gate_rows.shape

    def split(columns):
        return jax.ShapeDtypeStruct((eight, rows // eight, columns), f32)

    shapes = [split(columns) for columns in (8 * heads * HD, 8 * HD, 8 * HD, width, wide, wide)]
    shapes.append(jax.ShapeDtypeStruct((DOWN // 2, eight, high, width), f32))
    depth = 6
    results = pl.pallas_call(
        functools.partial(finish_kernel, heads),
        out_shape=tuple(shapes),
        in_specs=[pl.BlockSpec(memory_space=pl.ANY)] * (len(chunks) + 2),
        out_specs=tuple([pl.BlockSpec(memory_space=pl.ANY)] * 7),
        scratch_shapes=[
            pltpu.VMEM((depth, eight, high, width), bf16),
            pltpu.VMEM((depth, eight, high, width), f32),
            pltpu.SemaphoreType.DMA((depth,)),
            pltpu.SemaphoreType.DMA((depth, 12)),
        ],
        compiler_params=pltpu.CompilerParams(vmem_limit_bytes=60 * 2**20),
        cost_estimate=pl.CostEstimate(
            flops=0, bytes_accessed=3 * CHUNKS * eight * high * width, transcendentals=0
        ),
    )(
        *chunks, gate_rows.reshape(eight, rows // eight, wide),
        up_rows.reshape(eight, rows // eight, wide),
    )
    flat = [result.reshape(rows, -1) for result in results[:6]]
    return flat + [results[6].reshape(-1, width)]


def sum_over_sequences(term):
    return lax.psum(term, "rep").astype(f32)


def on_device(
    layer_input,
    cotangent,
    cut_order,
    piece_ids,
    w_query,
    w_key,
    w_value,
    w_out,
    w_gate,
    w_up,
    w_down,
    gain_attn,
    gain_ffn,
):
    groups = lax.axis_size("grp")
    reps = lax.axis_size("rep")
    own_index = lax.axis_index("grp")
    _, local_rows, model_width = layer_input.shape
    length = piece_ids.shape[1]
    rows_here = w_query.shape[0]
    q_width = w_query.shape[1]
    kv_heads = w_key.shape[1] // HD
    heads = q_width // HD // groups
    copies = groups // kv_heads
    hidden_here = w_down.shape[0]
    cosine, sine = turn_tables(length)

    near = groups == 8 and reps == 4 and copies == 1 and 2 * hidden_here == model_width

    def gather(rows):
        return lax.all_gather(rows, "grp", axis=0, tiled=True)

    def scatter(first, second, turned):
        term = against_rows(first, second) if turned else matmul_f32(first, second)
        return lax.psum_scatter(
            term.astype(bf16), "grp", scatter_dimension=0, tiled=True
        ).astype(f32)

    def to_columns(parts):
        return lax.all_to_all(parts, "grp", 1, 0, tiled=True).reshape(-1, parts.shape[-1])

    def per_group(weight):
        return weight.reshape(rows_here, groups, -1)

    def per_kv_head(weight):
        return jnp.repeat(weight.reshape(rows_here, kv_heads, HD), copies, axis=1)

    x_rows = layer_input.reshape(local_rows, model_width)
    x_flat = x_rows.astype(f32)
    inv_one = lax.rsqrt(jnp.mean(x_flat * x_flat, -1, keepdims=True) + EPS)
    unit_one = x_flat * inv_one
    attn_gain, ffn_gain = gain_attn.reshape(1, -1), gain_ffn.reshape(1, -1)
    if near:
        share = rows_here // (4 * reps) * 3
        spread = columns_of_some((w_gate, w_up), share, 11)
        x_first, spread = lax.optimization_barrier((x_rows, spread))
        spread = lax.all_gather(spread, "rep", axis=0)
        normed_one, cols_qkv = gather_normed(
            x_first, attn_gain, (w_query, w_key, w_value), number=1
        )
        last_gate, last_up, normed_one = lax.optimization_barrier(
            (w_gate[reps * share :], w_up[reps * share :], normed_one)
        )
        rest = to_columns(
            jnp.concatenate(
                [part.reshape(rows_here - reps * share, groups, -1) for part in (last_gate, last_up)],
                -1,
            )
        ).reshape(groups, rows_here - reps * share, -1)
    else:
        normed_one = gather(rms_normed(x_flat, attn_gain).astype(bf16))
        cols_qkv = to_columns(
            jnp.concatenate([per_group(w_query), per_kv_head(w_key), per_kv_head(w_value)], -1)
        )
        cols_gate_up = to_columns(jnp.concatenate([per_group(w_gate), per_group(w_up)], -1))
    attended, query, key, value, lse, attended_placed = attend(
        cut_order, normed_one, cols_qkv, cosine, sine, piece_ids, heads
    )
    if near:
        mid = product_scattered(attended, w_out, False, base=x_rows, number=2)[0]
    else:
        mid = x_flat + scatter(attended, w_out, False)
    grad_out = cotangent.reshape(local_rows, model_width)

    def back_through_attention(grad_attended, **line):
        return attend_back(
            cut_order, grad_attended, attended_placed, query, key, value, lse, cosine, sine,
            piece_ids, heads, **line,
        )

    q_here = heads * HD
    if near:
        normed_two, hidden, cols_gate_up, grad_gate_up, down_term = feed_forward(
            mid, ffn_gain, grad_out, spread, rest, w_down, number=3
        )
        cols_gate_up = cols_gate_up.reshape(model_width, -1)
        high, half_width = 2 * rows_here // GATE_UP, model_width // 2
        sums = Sums((8, high, half_width))
        terms = {"down": down_term.reshape(DOWN // 2, 8, high, model_width)}

        def pick_whole(n):
            return "down", lambda ref: ref.at[n // 2, :, :, n % 2 * half_width : (n % 2 + 1) * half_width]

        def pick_rows(name, n):
            rows, side = n // 2 * high, n % 2 * half_width
            return name, lambda ref: ref.at[:, rows : rows + high, side : side + half_width]

        picks = [pick_whole(n) for n in range(DOWN)]
        picks += [pick_rows("gate_up", n) for n in range(GATE_UP)]
        picks += [pick_rows("out", n) for n in range(OUT)]

        def line(number, ticks):
            names = sorted(
                {picks[t][0] for t in range(sums.tick, sums.tick + ticks) if t < len(picks)}
            )
            return dict(
                number=number, ticks=ticks, sums=sums, picks=dict(enumerate(picks)),
                arrays=[(name, terms[name]) for name in names],
            )

        result, terms["gate_up"] = product_scattered(
            hidden, w_down, False, extra=(normed_two, grad_gate_up), base=mid, dtype=bf16,
            steps={"x": 1, "y": 1, "work": 1, "relayed": 1, "work2": 1, "work3": 2}, **line(5, 10),
        )
        grad_mid, gain_ffn_term = product_scattered(
            grad_gate_up, cols_gate_up, True, back=(grad_out, mid, ffn_gain),
            steps={"across": 1, "x": 1, "y": 1, "relayed": 1, "sibling": 1, "halves": 1}, **line(6, 10),
        )
        grad_attended, out_term = attended_back(grad_mid, w_out, attended, **line(7, 8))
        terms["out"] = out_term.reshape(8, OUT // 2 * high, model_width)
        grad_qkv = back_through_attention(grad_attended, **line(8, 6))
        grad_x, gain_attn_term, qkv_term = product_scattered(
            grad_qkv, cols_qkv, True, extra=(normed_one, None), dtype=bf16,
            back=(grad_mid, x_rows, attn_gain),
            steps={"y": 1, "work": 1, "relayed": 2, "work2": 1, "work3": 1}, **line(9, 8),
        )
        gains = jnp.stack([gain_attn_term, gain_ffn_term]).reshape(2, groups, rows_here)
        gains = jnp.pad(jnp.moveaxis(gains, 0, 1), ((0, 0), (0, 6), (0, 0)))
        rest = line(10, CHUNKS + 2 * LAG - sums.tick)
        gate_rows, up_rows, qkv_rows, own_gains = tail(
            qkv_term.reshape(8, 8, 2 * high, -1), gains,
            {c: sums.done[c] for c in sums.done if c >= DOWN}, hidden_here, **rest,
        )
        straight = [n for n in range(CHUNKS) if n < DOWN or n >= DOWN + GATE_UP]
        weight_grads = finish([sums.done[n] for n in straight], gate_rows, up_rows, heads)
        shaped = tuple(rows.reshape(layer_input.shape) for rows in (result, grad_x))
        return shaped + tuple(weight_grads) + (own_gains[0], own_gains[1])

    unit_one = x_flat * inv_one
    inv_two = lax.rsqrt(jnp.mean(mid * mid, -1, keepdims=True) + EPS)
    unit_two = mid * inv_two
    normed_two = gather((unit_two * ffn_gain).astype(bf16))
    grad_all = gather(grad_out)
    gate_up = matmul_f32(normed_two, cols_gate_up)
    gate_proj, up_proj = gate_up[:, :hidden_here], gate_up[:, hidden_here:]
    sigmoid_gate = jax.nn.sigmoid(gate_proj)
    swish = gate_proj * sigmoid_gate
    hidden = (swish * up_proj).astype(bf16)
    gate_part = up_proj * sigmoid_gate * (1.0 + gate_proj * (1.0 - sigmoid_gate))
    down_term = over_tokens(hidden, grad_all).astype(bf16)
    grad_hidden = against_rows(grad_all, w_down)
    grad_gate_up = jnp.concatenate([grad_hidden * gate_part, grad_hidden * swish], 1).astype(bf16)
    grad_mid, gain_ffn_term = norm_back(
        grad_out.astype(f32), scatter(grad_gate_up, cols_gate_up, True), unit_two, inv_two, gain_ffn
    )
    grad_mid_low = gather(grad_mid.astype(bf16))
    grad_qkv = back_through_attention(against_rows(grad_mid_low, w_out).astype(bf16))
    grad_x, gain_attn_term = norm_back(
        grad_mid, scatter(grad_qkv, cols_qkv, True), unit_one, inv_one, gain_attn
    )

    def to_rows(term):
        return lax.all_to_all(
            term.astype(bf16).reshape(groups, rows_here, -1), "grp", 0, 0, tiled=True
        )

    def whole_rows(term):
        return jnp.moveaxis(term, 0, 1).reshape(rows_here, -1)

    def kv_rows(term):
        return jnp.sum(
            jnp.moveaxis(term, 0, 1).reshape(rows_here, kv_heads, copies, HD), 2
        ).reshape(rows_here, -1)

    gate_up_term = sum_over_sequences(to_rows(over_tokens(normed_two, grad_gate_up)))
    out_term = sum_over_sequences(over_tokens(attended, grad_mid_low).astype(bf16))
    qkv_term = sum_over_sequences(to_rows(over_tokens(normed_one, grad_qkv)))
    gain_total = lax.psum(jnp.stack([gain_attn_term, gain_ffn_term]), ("grp", "rep"))
    own_gains = lax.dynamic_slice_in_dim(gain_total, own_index * rows_here, rows_here, 1)
    return (
        (mid + scatter(hidden, w_down, False)).astype(bf16).reshape(layer_input.shape),
        grad_x.astype(bf16).reshape(layer_input.shape),
        whole_rows(qkv_term[..., :q_here]),
        kv_rows(qkv_term[..., q_here : q_here + HD]),
        kv_rows(qkv_term[..., q_here + HD :]),
        out_term,
        whole_rows(gate_up_term[..., :hidden_here]),
        whole_rows(gate_up_term[..., hidden_here:]),
        sum_over_sequences(down_term),
        own_gains[0],
        own_gains[1],
    )


def solution(mesh):
    tokens, table, rows, whole = P("rep", "grp", None), P("rep", None), P("grp", None), P()
    return jax.shard_map(
        on_device,
        mesh=mesh,
        in_specs=(tokens, tokens, table, table) + (rows,) * 7 + (whole,) * 2,
        out_specs=(tokens, tokens) + (rows,) * 7 + (P("grp"),) * 2,
        check_vma=False,
    )
```

```python
import functools

import jax
import jax.numpy as jnp
import numpy as np
from jax import lax
from jax.experimental import pallas as pl
from jax.experimental.pallas import tpu as pltpu
from jax.sharding import PartitionSpec as P

HD = 128
EPS = 1e-05
ROPE_BASE = 1000000.0
SCORE_SCALE = HD**-0.5
LOG2E = 1.4426950408889634
TO_EXP2 = SCORE_SCALE * LOG2E
NEG = -1e30

MESH = pl.DeviceIdType.MESH
f32 = jnp.float32
bf16 = jnp.bfloat16


def matmul_f32(first, second):
    return jnp.dot(first, second, preferred_element_type=f32)


def against_rows(first, second):
    return lax.dot_general(first, second, (((1,), (1,)), ((), ())), preferred_element_type=f32)


def over_tokens(first, second):
    return lax.dot_general(first, second, (((0,), (0,)), ((), ())), preferred_element_type=f32)


def turn_tables(length):
    half_size = HD // 2
    inverse = np.float32(ROPE_BASE) ** (-(np.arange(half_size, dtype=np.float32) * 2) / HD)
    angles = np.arange(length, dtype=np.float32)[:, None] * inverse.astype(np.float32)
    cosine, sine = np.cos(angles), np.sin(angles)
    tables = np.concatenate([cosine, cosine], -1), np.concatenate([-sine, sine], -1)
    return tuple(jnp.asarray(table.astype(np.float32)) for table in tables)


def norm_back(upstream, grad_normed, unit_rows, inv_root, gain):
    scaled = grad_normed * gain
    center_term = jnp.mean(scaled * unit_rows, -1, keepdims=True)
    return (
        upstream + inv_root * (scaled - unit_rows * center_term),
        jnp.sum(grad_normed * unit_rows, 0),
    )


def fold_lanes(values, op):
    out = values[:, :HD]
    for at in range(HD, values.shape[1], HD):
        out = op(out, values[:, at : at + HD])
    return out


def as_column(row):
    return jnp.broadcast_to(row, (HD, row.shape[1])).T[:, 0:1]


def as_row(column):
    return jnp.broadcast_to(column, (column.shape[0], HD)).T[0:1, :]


def attend_kernel(
    heads, cuts, block,
    order_ref, rows_hbm, weight_hbm, cos_ref, sin_ref, piece_ref,
    out_ref, q_ref, k_ref, v_ref, lse_ref, placed,
    scores, rows_ref, weight_ref, qkv_ref, sems,
):
    length = rows_ref.shape[0]
    cut = length // cuts
    blocks = length // block
    loads = [pltpu.make_async_copy(weight_hbm, weight_ref, sems.at[blocks])]
    for i in range(blocks):
        at = slice(i * block, (i + 1) * block)
        loads.append(pltpu.make_async_copy(rows_hbm.at[at, :], rows_ref.at[at, :], sems.at[i]))
    for load in loads:
        load.start()

    def place_cut(r, first):
        src = pl.ds(pl.multiple_of(r * cut, cut), cut)
        dst = pl.ds(pl.multiple_of(order_ref[0, first + r] * cut, cut), cut)
        cosine, sine = cos_ref[dst, :], sin_ref[dst, :]
        for h in range(heads + 1):
            part = qkv_ref[src, h * HD : (h + 1) * HD]
            turned = (part * cosine + pltpu.roll(part, HD // 2, 1) * sine).astype(bf16)
            if h < heads:
                q_ref[h, dst, :] = turned
            else:
                k_ref[dst, :] = turned
        v_ref[dst, :] = qkv_ref[src, (heads + 1) * HD :].astype(bf16)
        return first

    loads[0].wait()
    for i in range(blocks):
        loads[1 + i].wait()
        qkv_ref[...] = matmul_f32(rows_ref[i * block : (i + 1) * block, :], weight_ref[...])
        lax.fori_loop(0, block // cut, place_cut, i * (block // cut))

    def one_block(i, _):
        rows = pl.ds(pl.multiple_of(i * block, block), block)
        query = q_ref[:, rows, :].reshape(heads * block, HD)

        def score(j, high):
            cols = pl.ds(pl.multiple_of(j * block, block), block)
            tile = against_rows(query, k_ref[cols, :])
            scores[j] = tile
            return jnp.maximum(high, fold_lanes(tile, jnp.maximum))

        high = lax.fori_loop(0, i, score, jnp.full((heads * block, HD), NEG, f32))
        tile = against_rows(query, k_ref[rows, :])
        q_at = lax.broadcasted_iota(jnp.int32, (block, block), 0)
        k_at = lax.broadcasted_iota(jnp.int32, (block, block), 1)
        k_piece = piece_ref[0:1, rows].astype(f32)
        q_piece = as_column(k_piece)
        allowed = (k_at <= q_at) | ((q_piece != 0) & (q_piece == k_piece))
        tile = jnp.concatenate(
            [jnp.where(allowed, tile[h * block : (h + 1) * block], NEG) for h in range(heads)], 0
        )
        scores[i] = tile
        high = jnp.max(jnp.maximum(high, fold_lanes(tile, jnp.maximum)), 1, keepdims=True)

        def weigh(j, state):
            total, mixed = state
            cols = pl.ds(pl.multiple_of(j * block, block), block)
            prob = jnp.exp2((scores[j] - high) * TO_EXP2)
            total = total + fold_lanes(prob, jnp.add)
            return total, mixed + matmul_f32(prob.astype(bf16), v_ref[cols, :])

        zero = jnp.zeros((heads * block, HD), f32)
        total, mixed = lax.fori_loop(0, i + 1, weigh, (zero, zero))
        total = jnp.sum(total, 1, keepdims=True)
        mixed = (mixed / total).astype(bf16)
        log_total = high * TO_EXP2 + jnp.log2(total)
        for h in range(heads):
            placed[rows, h * HD : (h + 1) * HD] = mixed[h * block : (h + 1) * block]
            lse_ref[h : h + 1, rows] = as_row(log_total[h * block : (h + 1) * block])
        return 0

    lax.fori_loop(0, blocks, one_block, 0)

    def store_cut(r, _):
        dst = pl.ds(pl.multiple_of(r * cut, cut), cut)
        src = pl.ds(pl.multiple_of(order_ref[0, r] * cut, cut), cut)
        out_ref[dst, :] = placed[src, :]
        return 0

    lax.fori_loop(0, cuts, store_cut, 0)


def vmem_specs(count):
    return [pl.BlockSpec(memory_space=pltpu.VMEM)] * count


def attend(order, rows, weight, cosine, sine, piece, heads):
    length, width = rows.shape
    block = min(512, length)
    return pl.pallas_call(
        functools.partial(attend_kernel, heads, order.shape[1], block),
        out_shape=(
            jax.ShapeDtypeStruct((length, heads * HD), bf16),
            jax.ShapeDtypeStruct((heads, length, HD), bf16),
            jax.ShapeDtypeStruct((length, HD), bf16),
            jax.ShapeDtypeStruct((length, HD), bf16),
            jax.ShapeDtypeStruct((heads, length), f32),
            jax.ShapeDtypeStruct((length, heads * HD), bf16),
        ),
        in_specs=[pl.BlockSpec(memory_space=pltpu.SMEM)]
        + [pl.BlockSpec(memory_space=pl.ANY)] * 2
        + vmem_specs(3),
        out_specs=tuple(vmem_specs(6)),
        scratch_shapes=[
            pltpu.VMEM((length // block, heads * block, block), f32),
            pltpu.VMEM(rows.shape, bf16),
            pltpu.VMEM(weight.shape, bf16),
            pltpu.VMEM((block, weight.shape[1]), f32),
            pltpu.SemaphoreType.DMA((length // block + 1,)),
        ],
        compiler_params=pltpu.CompilerParams(vmem_limit_bytes=60 * 2**20),
        cost_estimate=pl.CostEstimate(
            flops=3 * heads * length * length * HD + 2 * length * width * weight.shape[1],
            bytes_accessed=10 * length * HD * heads * 4 + rows.size * 2,
            transcendentals=heads * length * length // 2,
        ),
    )(order, rows, weight, cosine, sine, piece)


DOWN, GATE_UP, OUT, QKV = 16, 32, 4, 8
CHUNKS = DOWN + GATE_UP + OUT + QKV
LAG = 3


def is_chunk(number):
    return 0 <= number < CHUNKS


def is_middle():
    rank = lax.axis_index("rep")
    return (rank == 1) | (rank == 2)


def is_end():
    rank = lax.axis_index("rep")
    return (rank == 0) | (rank == 3)


class NoLine:
    ticks = 0

    def signal(self, barrier):
        pass

    def greet(self, barrier, others):
        if others:
            pl.semaphore_wait(barrier, others)

    def start(self):
        pass

    def step(self, times=1):
        pass

    def end(self):
        pass


class Line:
    def __init__(self, first, ticks, picks, refs, outs, scratch):
        self.first, self.ticks, self.picks, self.refs, self.outs = first, ticks, picks, refs, outs
        (
            self.inward, self.across, self.own, self.pair, self.total, self.sems, self.local,
            self.carries,
        ) = scratch
        rank = lax.axis_index("rep")
        self.partner = {"rep": rank + 1 - 2 * (rank % 2)}
        self.peer = {"rep": 3 - rank}
        self.now = 0
        self.kept = []

    def signal(self, barrier):
        pl.semaphore_signal(barrier, inc=1, device_id=self.partner, device_id_type=MESH)

        @pl.when(is_middle())
        def _():
            pl.semaphore_signal(barrier, inc=1, device_id=self.peer, device_id_type=MESH)

    def greet(self, barrier, others):
        @pl.when(is_middle())
        def _():
            pl.semaphore_wait(barrier, others + 2)

        @pl.when(is_end())
        def _():
            pl.semaphore_wait(barrier, others + 1)

    def remote(self, hop, number, src, dst, device):
        return pltpu.make_async_remote_copy(
            src_ref=src, dst_ref=dst, send_sem=self.sems.at[0, hop, number],
            recv_sem=self.sems.at[1, hop, number], device_id=device, device_id_type=MESH,
        )

    def hops(self, number):
        tick = self.first + number
        term = pair = total = None
        if is_chunk(tick):
            which, pick = self.picks[tick]
            term = (
                lambda: self.remote(
                    0, number, pick(self.refs[which]), self.inward.at[number], self.partner
                ),
                lambda: pltpu.make_async_copy(
                    pick(self.refs[which]), self.own.at[tick % LAG], self.local.at[0, number]
                ),
            )
        if is_chunk(tick - LAG):
            held = self.pair.at[(tick - LAG) % (LAG + 1)]
            before = self.refs[f"pair{number}"] if number < LAG else held
            pair = (
                lambda: self.remote(1, number, before, self.across.at[number], self.peer),
                lambda: pltpu.make_async_copy(before, held, self.carries.at[0, number]),
            )
        if is_chunk(tick - 2 * LAG):
            held_total = self.total.at[(tick - 2 * LAG) % (LAG + 1)]
            done = self.refs[f"total{number}"] if number < LAG else held_total
            slot = self.outs[tick - 2 * LAG]
            total = (
                lambda: self.remote(2, number, done, slot, self.partner),
                lambda: pltpu.make_async_copy(done, slot, self.local.at[1, number]),
            )
        return term, pair, total

    def open(self, number):
        term, pair, total = self.hops(number)

        @pl.when(is_end())
        def _():
            if term:
                term[0]().start()

        @pl.when(is_middle())
        def _():
            if pair:
                pair[0]().start()
            if total:
                total[0]().start()
            if term:
                term[1]().start()
            if total:
                total[1]().start()
            if pair and number < LAG:
                pair[1]().start()

    def close(self, number):
        term, pair, total = self.hops(number)

        @pl.when(is_end())
        def _():
            if term:
                term[0]().wait_send()
            if total:
                total[0]().wait_recv()

        @pl.when(is_middle())
        def _():
            if total:
                total[0]().wait_send()
                total[1]().wait()
            if pair:
                pair[0]().wait_send()
                pair[0]().wait_recv()
            if term:
                term[0]().wait_recv()

    def add(self, number):
        term, pair, _ = self.hops(number)
        tick = self.first + number

        def sum_of(into, first, second):
            def one(g, _):
                into[g] = (first[g].astype(f32) + second[g].astype(f32)).astype(bf16)
                return 0

            lax.fori_loop(0, into.shape[0], one, 0)

        @pl.when(is_middle())
        def _():
            if pair:
                if number < LAG:
                    pair[1]().wait()
                before = tick - LAG
                sum_of(
                    self.total.at[before % (LAG + 1)], self.pair.at[before % (LAG + 1)],
                    self.across.at[number],
                )
            if term:
                term[1]().wait()
                sum_of(self.pair.at[tick % (LAG + 1)], self.own.at[tick % LAG], self.inward.at[number])

    def keep(self, number):
        tick = self.first + number
        which = number - (self.ticks - LAG)
        made = []
        if is_chunk(tick):
            made.append((self.pair.at[tick % (LAG + 1)], self.outs[f"pair{which}"], (1, which)))
        if is_chunk(tick - LAG):
            held = self.total.at[(tick - LAG) % (LAG + 1)]
            made.append((held, self.outs[f"total{which}"], (2, which)))
        copies = [
            lambda src=src, dst=dst, at=at: pltpu.make_async_copy(src, dst, self.carries.at[*at])
            for src, dst, at in made
        ]

        @pl.when(is_middle())
        def _():
            for copy in copies:
                copy().start()

        self.kept += copies

    def start(self):
        for number in range(LAG):
            self.open(number)

    def step(self, times=1):
        for _ in range(times):
            if self.now + LAG < self.ticks:
                self.settle()
                self.open(self.now + LAG - 1)

    def settle(self):
        self.close(self.now)
        self.add(self.now)
        if self.now >= self.ticks - LAG:
            self.keep(self.now)
        self.now += 1

    def end(self):
        while self.now + LAG < self.ticks:
            self.step()
        while self.now < self.ticks:
            self.settle()

        @pl.when(is_middle())
        def _():
            for copy in self.kept:
                copy().wait()


def line_slots(first, ticks):
    return [t - 2 * LAG for t in range(first, first + ticks) if is_chunk(t - 2 * LAG)]


class Sums:
    def __init__(self, shape):
        self.shape, self.tick, self.kept, self.done = shape, 0, {}, {}


def run(kernel, ins, outs, scratch, number, cost, sums=None, ticks=0, arrays=(), picks=None, vmem=58):
    ins, outs, scratch = list(ins), list(outs), list(scratch)
    counts = (len(ins), len(outs), len(scratch))
    first = sums.tick if ticks else 0
    names_in, names_out = [], []
    if ticks:
        for name, array in arrays:
            names_in.append(name)
            ins.append((array, pl.ANY))
        for which in range(LAG):
            for name, chunk_at in ((f"pair{which}", first - LAG), (f"total{which}", first - 2 * LAG)):
                if is_chunk(chunk_at + which):
                    names_in.append(name)
                    ins.append((sums.kept[name], pl.ANY))
        names_out = line_slots(first, ticks)
        after = first + ticks
        for which in range(LAG):
            for name, chunk_at in ((f"pair{which}", after - LAG), (f"total{which}", after - 2 * LAG)):
                if is_chunk(chunk_at + which):
                    names_out.append(name)
        outs += [(jax.ShapeDtypeStruct(sums.shape, bf16), pl.ANY)] * len(names_out)
        scratch += [
            pltpu.VMEM((ticks,) + sums.shape, bf16),
            pltpu.VMEM((ticks,) + sums.shape, bf16),
            pltpu.VMEM((LAG,) + sums.shape, bf16),
            pltpu.VMEM((LAG + 1,) + sums.shape, bf16),
            pltpu.VMEM((LAG + 1,) + sums.shape, bf16),
            pltpu.SemaphoreType.DMA((2, 3, ticks)),
            pltpu.SemaphoreType.DMA((2, ticks)),
            pltpu.SemaphoreType.DMA((3, LAG)),
        ]

    def body(*refs):
        in_refs, rest = refs[: len(ins)], refs[len(ins) :]
        out_refs, scratch_refs = rest[: len(outs)], rest[len(outs) :]
        line = NoLine()
        if ticks:
            line = Line(
                first, ticks, picks, dict(zip(names_in, in_refs[counts[0] :])),
                dict(zip(names_out, out_refs[counts[1] :])), scratch_refs[counts[2] :],
            )
        kernel(in_refs[: counts[0]], out_refs[: counts[1]], scratch_refs[: counts[2]], line)

    results = pl.pallas_call(
        body,
        out_shape=tuple(shape for shape, _ in outs),
        in_specs=[pl.BlockSpec(memory_space=space) for _, space in ins],
        out_specs=tuple(pl.BlockSpec(memory_space=space) for _, space in outs),
        scratch_shapes=scratch,
        compiler_params=pltpu.CompilerParams(
            vmem_limit_bytes=vmem * 2**20,
            **({} if number is None else {"collective_id": number, "has_side_effects": True}),
        ),
        cost_estimate=pl.CostEstimate(
            flops=cost[0], bytes_accessed=cost[1], transcendentals=cost[2]
        ),
    )(*[array for array, _ in ins])
    for name, result in zip(names_out, results[counts[1] :]):
        if name in line_slots(first, ticks):
            sums.done[name] = result
        else:
            sums.kept[name] = result
    if ticks:
        sums.tick += ticks
    return results[: counts[1]]


SMEM, VMEM, ANY = pltpu.SMEM, pltpu.VMEM, pl.ANY


def attend_back_kernel(
    heads, block, ins, outs, scratch, line
):
    grad_ref, out_ref, q_ref, k_ref, v_ref, lse_ref, cos_ref, sin_ref, piece_ref, place_ref = ins
    (grad_qkv_ref,) = outs
    grads, centers, grad_q, placed = scratch
    if line.ticks:
        line.signal(pltpu.get_barrier_semaphore())
        line.greet(pltpu.get_barrier_semaphore(), 0)
        line.start()
    length = grad_ref.shape[0]
    blocks = length // block

    def take_block(i, _):
        rows = pl.ds(pl.multiple_of(i * block, block), block)
        position = lax.broadcasted_iota(jnp.int32, (block, length), 0) + i * block
        chosen = jnp.where(place_ref[...] == position, 1.0, 0.0).astype(bf16)
        taken = matmul_f32(chosen, grad_ref[...]).astype(bf16)
        for h in range(heads):
            grad = taken[:, h * HD : (h + 1) * HD]
            grads[h, rows, :] = grad
            product = grad.astype(f32) * out_ref[rows, h * HD : (h + 1) * HD].astype(f32)
            centers[h, rows, :] = jnp.broadcast_to(
                jnp.sum(product, 1, keepdims=True), (block, HD)
            )
        return 0

    lax.fori_loop(0, blocks, take_block, 0)
    grad_q[...] = jnp.zeros_like(grad_q)

    def key_block(j, _):
        cols = pl.ds(pl.multiple_of(j * block, block), block)
        key, value = k_ref[cols, :], v_ref[cols, :]

        def one(i, state, diagonal):
            grad_key, grad_value = state
            rows = pl.ds(pl.multiple_of(i * block, block), block)
            for h in range(heads):
                query, grad = q_ref[h, rows, :], grads[h, rows, :]
                log_total = lse_ref[h : h + 1, rows]
                center = centers[h, rows, :].T[0:1, :]
                prob = jnp.exp2(against_rows(key, query) * TO_EXP2 - log_total)
                if diagonal:
                    k_at = lax.broadcasted_iota(jnp.int32, (block, block), 0)
                    q_at = lax.broadcasted_iota(jnp.int32, (block, block), 1)
                    q_piece = piece_ref[0:1, cols].astype(f32)
                    k_piece = as_column(q_piece)
                    allowed = (k_at <= q_at) | ((q_piece != 0) & (q_piece == k_piece))
                    prob = jnp.where(allowed, prob, 0.0)
                grad_prob = against_rows(value, grad)
                grad_score = (prob * (grad_prob - center)).astype(bf16)
                grad_value = grad_value + matmul_f32(prob.astype(bf16), grad)
                grad_key = grad_key + matmul_f32(grad_score, query)
                grad_q[h, rows, :] += over_tokens(grad_score, key)
            return grad_key, grad_value

        zero = jnp.zeros((block, HD), f32)
        state = one(j, (zero, zero), True)
        grad_key, grad_value = lax.fori_loop(
            j + 1, blocks, functools.partial(one, diagonal=False), state
        )
        grad_key = grad_key * SCORE_SCALE
        grad_key = grad_key * cos_ref[cols, :] - pltpu.roll(grad_key, HD // 2, 1) * sin_ref[cols, :]
        placed[cols, heads * HD : (heads + 1) * HD] = grad_key.astype(bf16)
        placed[cols, (heads + 1) * HD :] = grad_value.astype(bf16)
        return 0

    for j in range(min(2, blocks - 1)):
        lax.fori_loop(j, j + 1, key_block, 0)
        line.step(1 + j)
    lax.fori_loop(min(2, blocks - 1), blocks, key_block, 0)

    def turn_back(i, _):
        rows = pl.ds(pl.multiple_of(i * block, block), block)
        for h in range(heads):
            grad = grad_q[h, rows, :] * SCORE_SCALE
            grad = grad * cos_ref[rows, :] - pltpu.roll(grad, HD // 2, 1) * sin_ref[rows, :]
            placed[rows, h * HD : (h + 1) * HD] = grad.astype(bf16)
        return 0

    lax.fori_loop(0, blocks, turn_back, 0)
    line.step()

    def store_block(i, _):
        rows = pl.ds(pl.multiple_of(i * block, block), block)
        place = as_column(place_ref[0:1, rows].astype(f32)).astype(jnp.int32)
        position = lax.broadcasted_iota(jnp.int32, (block, length), 1)
        chosen = jnp.where(place == position, 1.0, 0.0).astype(bf16)
        grad_qkv_ref[rows, :] = matmul_f32(chosen, placed[...]).astype(bf16)
        return 0

    lax.fori_loop(0, blocks, store_block, 0)
    line.end()


def attend_back(
    order, grad, out, query, key, value, lse, cosine, sine, piece, heads, **line
):
    length = grad.shape[0]
    block = min(512, length)
    cut = length // order.shape[1]
    place = (order.reshape(-1, 1) * cut + jnp.arange(cut, dtype=order.dtype)).reshape(1, length)
    tall = [grad, out, query, key, value, lse, cosine, sine, piece, place]
    return run(
        functools.partial(attend_back_kernel, heads, block),
        [(array, VMEM) for array in tall],
        [(jax.ShapeDtypeStruct((length, (heads + 2) * HD), bf16), VMEM)],
        [
            pltpu.VMEM((heads, length, HD), bf16),
            pltpu.VMEM((heads, length, HD), f32),
            pltpu.VMEM((heads, length, HD), f32),
            pltpu.VMEM((length, (heads + 2) * HD), bf16),
        ],
        line.pop("number", None),
        (8 * heads * length * length * HD, 14 * length * HD * heads * 4, heads * length * length // 2),
        **line,
    )[0]


def place_in_group():
    me = lax.axis_index("grp")
    return me // 4, (me // 2) % 2, me % 2


def other(flip_y, flip_x, flip_core):
    y, x, core = place_in_group()
    return ((y + flip_y) % 2) * 4 + ((x + flip_x) % 2) * 2 + (core + flip_core) % 2


def chip_rows(flip_y, flip_x, rows):
    y, x, _ = place_in_group()
    first = (((y + flip_y) % 2) * 2 + (x + flip_x) % 2) * (2 * rows)
    return pl.ds(pl.multiple_of(first, 2 * rows), 2 * rows)


NEIGHBOURS = ((0, 0, 1), (0, 1, 0), (1, 0, 0))
EVERYONE = tuple((n // 4, (n // 2) % 2, n % 2) for n in range(1, 8))


def greet_group(line, flips=NEIGHBOURS, between=None):
    barrier = pltpu.get_barrier_semaphore()
    for flip in flips:
        pl.semaphore_signal(barrier, inc=1, device_id={"grp": other(*flip)}, device_id_type=MESH)
    line.signal(barrier)
    if between:
        between()
    line.greet(barrier, len(flips))


SIBLING, ALONG_X, ALONG_Y, ACROSS = (0, 0), (0, 1), (1, 0), (1, 1)


class Gather:
    TO_S, TO_X, TO_Y = (0, 0, 1), (0, 1, 0), (1, 0, 0)

    def __init__(self, rows, all_ref, sends, recvs):
        self.rows, self.all_ref, self.sends, self.recvs = rows, all_ref, sends, recvs
        self.started = []

    def copy(self, number, chip, core, part, target):
        first = other(*chip, core) * self.rows
        if part is None:
            where = pl.ds(pl.multiple_of(first, self.rows), self.rows)
        else:
            half = self.rows // 2
            where = pl.ds(pl.multiple_of(first + part * half, half), half)
        where = self.all_ref.at[where, :]
        return pltpu.make_async_remote_copy(
            src_ref=where, dst_ref=where, send_sem=self.sends.at[number],
            recv_sem=self.recvs.at[number], device_id={"grp": other(*target)}, device_id_type=MESH,
        )

    def send(self, *what):
        one = self.copy(*what)
        one.start()
        self.started.append(one)

    def landed(self, number, chip, core, part):
        self.copy(number, chip, core, part, self.TO_S).wait_recv()

    def send_own(self):
        self.send(1, SIBLING, 0, 1, self.TO_X)
        self.send(3, SIBLING, 0, 0, self.TO_Y)
        self.send(0, SIBLING, 0, None, self.TO_S)
        self.send(2, SIBLING, 0, 0, self.TO_X)
        self.send(4, SIBLING, 0, 1, self.TO_Y)

    def sibling(self):
        self.landed(0, SIBLING, 1, None)

    def relay(self):
        self.landed(1, ALONG_X, 0, 1)
        self.send(6, ALONG_X, 0, 1, self.TO_Y)
        self.landed(3, ALONG_Y, 0, 0)
        self.send(5, ALONG_Y, 0, 0, self.TO_X)
        self.send(7, ALONG_X, 0, 1, self.TO_S)
        self.send(8, ALONG_Y, 0, 0, self.TO_S)

    def pass_second(self):
        self.landed(2, ALONG_X, 0, 0)
        self.send(9, ALONG_X, 0, 0, self.TO_S)
        self.landed(4, ALONG_Y, 0, 1)
        self.send(10, ALONG_Y, 0, 1, self.TO_S)

    def along_x(self):
        self.landed(7, ALONG_X, 1, 1)
        self.landed(9, ALONG_X, 1, 0)

    def pass_across(self):
        self.landed(5, ACROSS, 0, 0)
        self.send(11, ACROSS, 0, 0, self.TO_S)
        self.landed(6, ACROSS, 0, 1)
        self.send(12, ACROSS, 0, 1, self.TO_S)

    def along_y(self):
        self.landed(8, ALONG_Y, 1, 0)
        self.landed(10, ALONG_Y, 1, 1)

    def across(self):
        self.landed(11, ACROSS, 1, 0)
        self.landed(12, ACROSS, 1, 1)

    def finish(self):
        for one in self.started:
            one.wait_send()


def gather_rows(rows, all_ref, sends, recvs, on_chip, line, then=None):
    rows_of = Gather(rows, all_ref, sends, recvs)
    rows_of.send_own()
    if then:
        then()
    rows_of.sibling()
    on_chip(*SIBLING)
    rows_of.relay()
    line.step(2)
    rows_of.pass_second()
    line.step(2)
    rows_of.along_x()
    on_chip(*ALONG_X)
    rows_of.pass_across()
    line.step()
    rows_of.along_y()
    on_chip(*ALONG_Y)
    rows_of.across()
    on_chip(*ACROSS)
    rows_of.finish()
    line.end()


GATHER_COPIES = 13


def rms_normed(values, gain):
    return values * lax.rsqrt(jnp.mean(values * values, -1, keepdims=True) + EPS) * gain


class Moves:
    def __init__(self, sems):
        self.sems, self.count, self.open = sems, 0, []

    def start(self, src, dst):
        one = pltpu.make_async_copy(src, dst, self.sems.at[self.count])
        self.count += 1
        one.start()
        return one

    def later(self, src, dst):
        self.open.append(self.start(src, dst))

    def finish(self):
        for one in self.open:
            one.wait()


def gather_scratch(rows, width, moves):
    return [
        pltpu.VMEM((8 * rows, width), bf16),
        pltpu.SemaphoreType.DMA((GATHER_COPIES,)),
        pltpu.SemaphoreType.DMA((GATHER_COPIES,)),
        pltpu.SemaphoreType.DMA((moves,)),
    ]


def own_rows(rows):
    return pl.ds(pl.multiple_of(other(0, 0, 0) * rows, rows), rows)


def send_columns(pieces, sends, recvs, moves):
    copies = []
    for which, (rows_ref, width, there) in enumerate(pieces):
        for number, flip in enumerate(EVERYONE):
            target = other(*flip)
            cols = pl.ds(pl.multiple_of(target * width, width), width)
            one = pltpu.make_async_remote_copy(
                src_ref=rows_ref.at[:, cols], dst_ref=there,
                send_sem=sends.at[which, number], recv_sem=recvs.at[which, number],
                device_id={"grp": target}, device_id_type=MESH,
            )
            one.start()
            copies.append(one)
        mine = pl.ds(pl.multiple_of(other(0, 0, 0) * width, width), width)
        moves.later(rows_ref.at[:, mine], there)
    return copies


def gather_normed_kernel(ins, outs, scratch, line):
    x_ref, gain_ref = ins[:2]
    weights = ins[2:]
    all_ref, cols_ref = outs
    held, sends, recvs, sems, col_sends, col_recvs = scratch
    rows = x_ref.shape[0]
    moves = Moves(sems)

    def fill():
        held[own_rows(rows), :] = rms_normed(x_ref[...].astype(f32), gain_ref[...]).astype(bf16)

    greet_group(line, EVERYONE, fill)
    col_copies = []

    def send_weights():
        pieces, low = [], 0
        tall = weights[0].shape[0]
        there = pl.ds(pl.multiple_of(other(0, 0, 0) * tall, tall), tall)
        for weight in weights:
            width = weight.shape[1] // 8
            pieces.append((weight, width, cols_ref.at[there, low : low + width]))
            low += width
        col_copies.extend(send_columns(pieces, col_sends, col_recvs, moves))

    def on_chip(*chip):
        where = chip_rows(*chip, rows)
        moves.later(held.at[where, :], all_ref.at[where, :])

    gather_rows(rows, held, sends, recvs, on_chip, line, send_weights)
    for one in col_copies:
        one.wait()
    moves.finish()


def gather_normed(x, gain, weights, **line):
    rows, width = x.shape
    deep = sum(weight.shape[1] for weight in weights) // 8
    return run(
        gather_normed_kernel,
        [(x, VMEM), (gain, VMEM)] + [(weight, ANY) for weight in weights],
        [
            (jax.ShapeDtypeStruct((8 * rows, width), bf16), ANY),
            (jax.ShapeDtypeStruct((8 * weights[0].shape[0], deep), bf16), ANY),
        ],
        gather_scratch(rows, width, 4 + len(weights))
        + [pltpu.SemaphoreType.DMA((len(weights), 7))] * 2,
        line.pop("number"),
        (0, 150 * rows * width * 2, 0),
        **line,
    )


def columns_kernel(rows_here, ins, outs, scratch, line):
    (cols_ref,) = outs
    sends, recvs, sems = scratch
    moves = Moves(sems)
    barrier = pltpu.get_barrier_semaphore()
    for flip in EVERYONE:
        pl.semaphore_signal(barrier, inc=1, device_id={"grp": other(*flip)}, device_id_type=MESH)
    pl.semaphore_wait(barrier, 7)
    first = pl.multiple_of(lax.axis_index("rep") * rows_here, rows_here)
    me = other(0, 0, 0)
    pieces, low = [], 0
    for weight in ins:
        width = weight.shape[1] // 8
        pieces.append(
            (weight.at[pl.ds(first, rows_here), :], width, cols_ref.at[me, :, low : low + width])
        )
        low += width
    for one in send_columns(pieces, sends, recvs, moves):
        one.wait()
    moves.finish()


def columns_of_some(weights, rows_here, number):
    deep = sum(weight.shape[1] for weight in weights) // 8
    return run(
        functools.partial(columns_kernel, rows_here),
        [(weight, ANY) for weight in weights],
        [(jax.ShapeDtypeStruct((8, rows_here, deep), bf16), ANY)],
        [pltpu.SemaphoreType.DMA((len(weights), 7))] * 2
        + [pltpu.SemaphoreType.DMA((len(weights),))],
        number, (0, 50 * 8 * rows_here * deep, 0),
    )[0]


def feed_forward_kernel(tile, ins, outs, scratch, line):
    mid_ref, gain_ref, grad_ref, spread_ref, rest_ref, w_down_ref = ins
    all_ref, hidden_ref, whole_ref, grad_gate_up_ref, down_ref = outs
    held, grads_held, sends, recvs, grad_sends, grad_recvs, sems = scratch[:7]
    weight, w_down, hidden, up_part, gate_part, grads, down = scratch[7:]
    rows = mid_ref.shape[0]
    inner = hidden.shape[1]
    moves = Moves(sems)
    planes, _, tall, _ = spread_ref.shape
    loads = [
        moves.start(spread_ref.at[z], weight.at[:, z * tall : (z + 1) * tall, :])
        for z in range(planes)
    ]
    loads.append(moves.start(rest_ref, weight.at[:, planes * tall :, :]))
    down_load = moves.start(w_down_ref, w_down)

    def fill():
        held[own_rows(rows), :] = rms_normed(mid_ref[...], gain_ref[...]).astype(bf16)
        grads_held[own_rows(rows), :] = grad_ref[...]

    greet_group(line, between=fill)
    first = Gather(rows, held, sends, recvs)
    second = Gather(rows, grads_held, grad_sends, grad_recvs)
    stored = []

    def forward(*chip):
        where = chip_rows(*chip, rows)
        moves.later(held.at[where, :], all_ref.at[where, :])

        def column(t, _):
            cols = pl.ds(pl.multiple_of(t * tile, tile), tile)
            up_cols = pl.ds(pl.multiple_of(inner + t * tile, tile), tile)
            lhs = held[where, :]
            gate = matmul_f32(lhs, weight[:, :, cols].reshape(-1, tile))
            up = matmul_f32(lhs, weight[:, :, up_cols].reshape(-1, tile))
            sigma = 1.0 / (1.0 + jnp.exp(-gate))
            swish = gate * sigma
            hidden[where, cols] = (swish * up).astype(bf16)
            up_part[where, cols] = swish.astype(bf16)
            gate_part[where, cols] = (up * sigma * (1.0 + gate * (1.0 - sigma))).astype(bf16)
            return 0

        lax.fori_loop(0, inner // tile, column, 0)
        moves.later(hidden.at[where, :], hidden_ref.at[where, :])

    def backward(*chip):
        where = chip_rows(*chip, rows)
        slot = len(stored) % 2
        if len(stored) >= 2:
            stored[len(stored) - 2].wait()

        def column(t, _):
            cols = pl.ds(pl.multiple_of(t * tile, tile), tile)
            up_cols = pl.ds(pl.multiple_of(inner + t * tile, tile), tile)
            incoming = grads_held[where, :]
            grad_hidden = against_rows(incoming, w_down[cols, :])
            grads[slot, :, cols] = (grad_hidden * gate_part[where, cols].astype(f32)).astype(bf16)
            grads[slot, :, up_cols] = (grad_hidden * up_part[where, cols].astype(f32)).astype(bf16)
            term = over_tokens(hidden[where, cols], incoming)
            if chip == SIBLING:
                down[cols, :] = term
            elif chip == ACROSS:
                weight[t] = (down[cols, :] + term).astype(bf16)
            else:
                down[cols, :] += term
            return 0

        lax.fori_loop(0, inner // tile, column, 0)
        stored.append(moves.start(grads.at[slot], grad_gate_up_ref.at[where, :]))

    first.send_own()
    for one in loads:
        one.wait()
    whole = moves.start(weight, whole_ref)
    first.sibling()
    forward(*SIBLING)
    first.relay()
    first.pass_second()
    second.send_own()
    first.along_x()
    forward(*ALONG_X)
    first.pass_across()
    first.along_y()
    forward(*ALONG_Y)
    second.relay()
    first.across()
    forward(*ACROSS)
    down_load.wait()
    second.sibling()
    backward(*SIBLING)
    second.pass_second()
    second.along_x()
    backward(*ALONG_X)
    second.pass_across()
    second.along_y()
    backward(*ALONG_Y)
    second.across()
    whole.wait()
    backward(*ACROSS)
    moves.later(weight.at[: inner // tile], down_ref)
    first.finish()
    second.finish()
    for one in stored[-2:]:
        one.wait()
    moves.finish()


def feed_forward(mid, gain, grad, spread, rest, w_down, **line):
    rows, width = mid.shape
    inner = w_down.shape[0]
    weight = (8, width // 8, 2 * inner)
    return run(
        functools.partial(feed_forward_kernel, weight[1]),
        [(mid, VMEM), (gain, VMEM), (grad, VMEM), (spread, ANY), (rest, ANY), (w_down, ANY)],
        [
            (jax.ShapeDtypeStruct((8 * rows, width), bf16), ANY),
            (jax.ShapeDtypeStruct((8 * rows, inner), bf16), ANY),
            (jax.ShapeDtypeStruct(weight, bf16), ANY),
            (jax.ShapeDtypeStruct((8 * rows, 2 * inner), bf16), ANY),
            (jax.ShapeDtypeStruct((inner // weight[1], weight[1], width), bf16), ANY),
        ],
        [pltpu.VMEM((8 * rows, width), bf16)] * 2
        + [pltpu.SemaphoreType.DMA((GATHER_COPIES,))] * 4
        + [pltpu.SemaphoreType.DMA((20,))]
        + [pltpu.VMEM(weight, bf16), pltpu.VMEM(w_down.shape, bf16)]
        + [pltpu.VMEM((8 * rows, inner), bf16)] * 3
        + [
            pltpu.VMEM((2, 2 * rows, 2 * inner), bf16),
            pltpu.VMEM(w_down.shape, f32),
        ],
        line.pop("number"),
        (64 * rows * width * inner, 300 * rows * width * 2, 8 * rows * inner),
        vmem=63,
        **line,
    )


def attended_back_kernel(ins, outs, scratch, line):
    grad_ref, w_ref, attended_ref = ins
    grad_attended_ref, out_term_ref = outs
    held, sends, recvs, sems, total = scratch
    rows = grad_ref.shape[0]
    moves = Moves(sems)
    greet_group(line)
    line.start()
    held[own_rows(rows), :] = grad_ref[...].astype(bf16)

    def on_chip(*chip):
        where = chip_rows(*chip, rows)
        incoming = held[where, :]
        grad_attended_ref[where, :] = against_rows(incoming, w_ref[...]).astype(bf16)
        term = over_tokens(attended_ref[where, :], incoming)
        if chip == SIBLING:
            total[...] = term
        elif chip == ACROSS:
            out_term_ref[...] = (total[...] + term).astype(bf16)
        else:
            total[...] += term

    gather_rows(rows, held, sends, recvs, on_chip, line)
    moves.finish()


def attended_back(grad, w_out, attended, **line):
    rows, width = grad.shape
    return run(
        attended_back_kernel,
        [(array, VMEM) for array in (grad, w_out, attended)],
        [
            (jax.ShapeDtypeStruct(attended.shape, bf16), VMEM),
            (jax.ShapeDtypeStruct(w_out.shape, bf16), VMEM),
        ],
        gather_scratch(rows, width, 1) + [pltpu.VMEM(w_out.shape, f32)],
        line.pop("number"),
        (32 * rows * width * w_out.shape[0], 150 * rows * width * 2, 0),
        **line,
    )


class WeightTerm:
    def __init__(self, rows_ref, columns_ref, term_ref, scratch):
        self.rows_ref, self.columns_ref, self.term_ref = rows_ref, columns_ref, term_ref
        self.loaded, self.flipped, self.ready, self.sems = scratch
        self.tile = self.loaded.shape[2]
        for number in (0, 1):
            self.load(number).start()

    def load(self, number):
        cols = slice(number * self.tile, (number + 1) * self.tile)
        return pltpu.make_async_copy(
            self.rows_ref.at[:, cols], self.loaded.at[number % 2], self.sems.at[0, number % 2]
        )

    def store(self, number):
        return pltpu.make_async_copy(
            self.ready.at[number % 2], self.term_ref.at[number], self.sems.at[1, number % 2]
        )

    def work(self, numbers):
        for number in numbers:
            at = number % 2
            self.load(number).wait()
            if number >= 2:
                self.store(number - 2).wait()
            width = self.columns_ref.shape[1]
            step = min(256, width)
            self.flipped[...] = self.loaded[at].T

            def column(t, _):
                cols = pl.ds(pl.multiple_of(t * step, step), step)
                term = matmul_f32(self.flipped[...], self.columns_ref[:, cols])
                self.ready[at, :, cols] = term.astype(bf16)
                return 0

            lax.fori_loop(0, width // step, column, 0)
            self.store(number).start()
            if number + 2 < 8:
                self.load(number + 2).start()

    def finish(self):
        for number in (6, 7):
            self.store(number).wait()


def scatter_kernel(turned, tile, extra, after, steps, ins, outs, scratch, line):
    out_ref = outs[0] if after == "base" else scratch[-4]
    finals = ins[len(ins) - {"base": 1, "cast": 1, "back": 3}[after] :]
    part, to_s, from_s, to_chip, held, relay, last, sends, recvs = scratch[:9]
    a_ref, b_ref, loads = scratch[-3:]
    loading = [
        pltpu.make_async_copy(src, dst, loads.at[number])
        for number, (src, dst) in enumerate(((ins[1], b_ref), (ins[0], a_ref)))
    ]
    for one in loading:
        one.start()
    rows, width = out_ref.shape
    half = rows // 2
    _, _, core = place_in_group()
    greet_group(line)
    line.start()
    if extra:
        columns_ref = a_ref
        if extra == "loaded":
            columns_ref = scratch[13]
            columns_copy = pltpu.make_async_copy(ins[3], columns_ref, scratch[14].at[0])
            columns_copy.start()
        term = WeightTerm(ins[2], columns_ref, outs[-1], scratch[9:13])
    for one in loading:
        one.wait()
    own_at = pl.multiple_of(core * rows, rows)
    other_at = pl.multiple_of((1 - core) * rows, rows)
    started = []

    def send(number, src, dst, target):
        one = pltpu.make_async_remote_copy(
            src_ref=src, dst_ref=dst, send_sem=sends.at[number], recv_sem=recvs.at[number],
            device_id={"grp": other(*target)}, device_id_type=MESH,
        )
        one.start()
        started.append(one)
        return one

    def landed(number, where):
        pltpu.make_async_remote_copy(
            src_ref=where, dst_ref=where, send_sem=sends.at[number], recv_sem=recvs.at[number],
            device_id={"grp": other(0, 0, 1)}, device_id_type=MESH,
        ).wait_recv()

    to_sib, to_x, to_y = (0, 0, 1), (0, 1, 0), (1, 0, 0)

    def make(number, chip):
        where = chip_rows(*chip, rows)

        def column(t, _):
            cols = pl.ds(pl.multiple_of(t * tile, tile), tile)
            lhs = a_ref[where, :]
            if turned:
                part[:, cols] = against_rows(lhs, b_ref[cols, :])
            else:
                part[:, cols] = matmul_f32(lhs, b_ref[:, cols])
            return 0

        lax.fori_loop(0, width // tile, column, 0)
        to_s[number] = part[pl.ds(other_at, rows), :].astype(bf16)
        send(number, to_s.at[number], from_s.at[number], to_sib)

    def own(low, number):
        at = pl.ds(pl.multiple_of(core * rows + low * half, half), half)
        return part[at, :] + from_s[number, low * half : (low + 1) * half, :].astype(f32)

    first, second = slice(0, half), slice(half, rows)
    step = lambda point: line.step(steps.get(point, 0))
    make(0, ACROSS)
    landed(0, from_s.at[0])
    to_chip[0, first, :] = own(0, 0).astype(bf16)
    send(4, to_chip.at[0, first, :], relay.at[0], to_x)
    to_chip[0, second, :] = own(1, 0).astype(bf16)
    send(5, to_chip.at[0, second, :], relay.at[1], to_y)
    step("across")
    make(1, ALONG_X)
    landed(1, from_s.at[1])
    to_chip[1, first, :] = own(0, 1).astype(bf16)
    send(6, to_chip.at[1, first, :], last.at[0, first, :], to_x)
    held[0] = own(1, 1)
    step("x")
    make(2, ALONG_Y)
    landed(2, from_s.at[2])
    to_chip[2, second, :] = own(1, 2).astype(bf16)
    send(7, to_chip.at[2, second, :], last.at[1, second, :], to_y)
    held[1] = own(0, 2)
    step("y")
    if extra:
        if extra == "loaded":
            columns_copy.wait()
        term.work((0, 1, 2))
        step("work")
    landed(5, relay.at[1])
    to_chip[1, second, :] = (held[0] + relay[1].astype(f32)).astype(bf16)
    send(8, to_chip.at[1, second, :], last.at[0, second, :], to_x)
    landed(4, relay.at[0])
    to_chip[2, first, :] = (held[1] + relay[0].astype(f32)).astype(bf16)
    send(9, to_chip.at[2, first, :], last.at[1, first, :], to_y)
    step("relayed")
    make(3, SIBLING)
    step("sibling")
    if extra:
        term.work((3, 4))
        step("work2")
        term.work((5, 6, 7))
        step("work3")
    landed(3, from_s.at[3])
    for low in (0, 1):
        at = slice(low * half, (low + 1) * half)
        if after == "back":
            out_ref[at, :] = own(low, 3)
        else:
            out_ref[at, :] = own(low, 3) + finals[0][at, :].astype(f32)
    landed(6, last.at[0, first, :])
    out_ref[first, :] += last[0, first, :].astype(f32)
    landed(7, last.at[1, second, :])
    out_ref[second, :] += last[1, second, :].astype(f32)
    step("halves")
    landed(8, last.at[0, second, :])
    out_ref[second, :] += last[0, second, :].astype(f32)
    landed(9, last.at[1, first, :])
    out_ref[first, :] += last[1, first, :].astype(f32)
    if after == "cast":
        outs[0][...] = out_ref[...].astype(outs[0].dtype)
    if after == "back":
        upstream_ref, rows_ref, gain_ref = finals
        some = min(64, rows)

        def norm_rows(number, gain_term):
            at = pl.ds(pl.multiple_of(number * some, some), some)
            values, incoming = rows_ref[at, :].astype(f32), out_ref[at, :]
            inv = lax.rsqrt(jnp.mean(values * values, -1, keepdims=True) + EPS)
            grad, term = norm_back(
                upstream_ref[at, :].astype(f32), incoming, values * inv, inv, gain_ref[...]
            )
            outs[0][at, :] = grad.astype(outs[0].dtype)
            return gain_term + term[None, :]

        outs[1][...] = lax.fori_loop(0, rows // some, norm_rows, jnp.zeros((1, width), f32))
    for one in started:
        one.wait_send()
    if extra:
        term.finish()
    line.end()


def product_scattered(
    a, b, turned, extra=None, base=None, back=None, dtype=f32, steps=None, **line
):
    length, depth = a.shape
    width = b.shape[0] if turned else b.shape[1]
    rows = length // 8
    tile = min(256, width)
    ins = [(a, ANY), (b, ANY)]
    outs = [(jax.ShapeDtypeStruct((rows, width), dtype), VMEM)]
    after = "back" if back else "base" if dtype == f32 else "cast"
    if back:
        outs.append((jax.ShapeDtypeStruct((1, width), f32), VMEM))
    scratch = [
        pltpu.VMEM((2 * rows, width), f32),
        pltpu.VMEM((4, rows, width), bf16),
        pltpu.VMEM((4, rows, width), bf16),
        pltpu.VMEM((3, rows, width), bf16),
        pltpu.VMEM((2, rows // 2, width), f32),
        pltpu.VMEM((2, rows // 2, width), bf16),
        pltpu.VMEM((2, rows, width), bf16),
        pltpu.SemaphoreType.DMA((10,)),
        pltpu.SemaphoreType.DMA((10,)),
    ]
    flops, kind = 2 * length * depth * width, None
    if extra:
        first, second = extra
        kind = "own" if second is None else "loaded"
        ins.append((first, ANY))
        columns = a if second is None else second
        tall = first.shape[1] // 8
        outs.append((jax.ShapeDtypeStruct((8, tall, columns.shape[1]), bf16), ANY))
        scratch += [
            pltpu.VMEM((2, length, tall), bf16),
            pltpu.VMEM((tall, length), bf16),
            pltpu.VMEM((2, tall, columns.shape[1]), bf16),
            pltpu.SemaphoreType.DMA((2, 2)),
        ]
        if second is not None:
            ins.append((second, ANY))
            scratch += [pltpu.VMEM(second.shape, bf16), pltpu.SemaphoreType.DMA((1,))]
        flops += 2 * length * first.shape[1] * columns.shape[1]
    ins += [(array, VMEM) for array in (back or (base,))]
    if after != "base":
        scratch.append(pltpu.VMEM((rows, width), f32))
    scratch += [
        pltpu.VMEM(a.shape, bf16), pltpu.VMEM(b.shape, bf16), pltpu.SemaphoreType.DMA((2,))
    ]
    return run(
        functools.partial(scatter_kernel, turned, tile, kind, after, steps or {}), ins, outs, scratch,
        line.pop("number"), (flops, 150 * rows * width * 2, 0), vmem=61, **line,
    )


def tail_kernel(ready, later, ins, outs, scratch, line):
    qkv_ref, gains_ref = ins[:2]
    chunk_refs = dict(zip(ready, ins[2:]))
    gate_ref, up_ref, qkv_rows_ref, gains_out_ref = outs
    from_group, mine, from_rep, sends, recvs, chunk_sems, local = scratch
    me, rank = other(0, 0, 0), lax.axis_index("rep")
    inner = gate_ref.shape[1] // 8
    part = qkv_ref.shape[-1]
    high = line.outs[later[0]].shape[1]
    barrier = pltpu.get_barrier_semaphore()
    for flip in range(1, 4):
        pl.semaphore_signal(
            barrier, inc=1, device_id={"rep": (rank + flip) % 4}, device_id_type=MESH
        )
    for flip in EVERYONE:
        pl.semaphore_signal(barrier, inc=1, device_id={"grp": other(*flip)}, device_id_type=MESH)
    pl.semaphore_wait(barrier, 10)
    waits, moves = [], Moves(local)
    line.refs["qkv"] = qkv_rows_ref

    def send(kind, number, src, dst, device):
        return pltpu.make_async_remote_copy(
            src_ref=src, dst_ref=dst, send_sem=sends.at[kind, number],
            recv_sem=recvs.at[kind, number], device_id=device, device_id_type=MESH,
        )

    own_qkv = qkv_rows_ref.at[me // 4, :, :, pl.ds(pl.multiple_of((me % 4) * part, part), part)]
    qkv_copies, gain_copies = [], []
    for number, flip in enumerate(EVERYONE):
        target = other(*flip)
        qkv_copies.append(send(0, number, qkv_ref.at[target], own_qkv, {"grp": target}))
        qkv_copies[-1].start()
    moves.later(qkv_ref.at[me], own_qkv)
    line.start()
    for number, flip in enumerate(EVERYONE):
        target = other(*flip)
        gain_copies.append(
            send(1, number, gains_ref.at[target], from_group.at[me], {"grp": target})
        )
        gain_copies[-1].start()
    from_group[me] = gains_ref[me]

    def spread(chunk):
        src = chunk_refs[chunk] if chunk in chunk_refs else line.outs[chunk]
        number = chunk - DOWN
        rows = slice(number // 2 * high, (number // 2 + 1) * high)
        dst = (gate_ref, up_ref)[number % 2]
        there = dst.at[rows, pl.ds(pl.multiple_of(me * inner, inner), inner)]
        for flip in EVERYONE:
            target = other(*flip)
            pltpu.make_async_remote_copy(
                src_ref=src.at[target], dst_ref=there, send_sem=chunk_sems.at[0, number],
                recv_sem=chunk_sems.at[1, number], device_id={"grp": target}, device_id_type=MESH,
            ).start()
        moves.later(src.at[me], there)
        seven = dst.at[rows, : 7 * inner]
        waits.append(
            pltpu.make_async_remote_copy(
                src_ref=seven, dst_ref=seven, send_sem=chunk_sems.at[0, number],
                recv_sem=chunk_sems.at[1, number], device_id={"grp": other(0, 0, 1)},
                device_id_type=MESH,
            )
        )

    for chunk in ready:
        spread(chunk)
    for one in gain_copies:
        one.wait()
    mine[rank] = sum(from_group[g] for g in range(8))
    rep_copies = []
    for step in range(1, 4):
        target = (rank + step) % 4
        rep_copies.append(
            send(2, step, mine.at[rank], from_rep.at[step], {"rep": target})
        )
        rep_copies[-1].start()
    for step, one in zip(range(1, 4), rep_copies):
        one.wait()
        mine[(rank + 4 - step) % 4] = from_rep[step]
    gains_out_ref[...] = (mine[0] + mine[1]) + (mine[2] + mine[3])
    for settled in range(line.ticks - LAG):
        if line.first + settled + LAG == CHUNKS - QKV:
            for one in qkv_copies:
                one.wait()
            moves.open.pop(0).wait()
        line.step()
        chunk = line.first + settled - 2 * LAG
        if chunk in later:
            spread(chunk)
    line.end()
    for one in waits:
        one.wait_send()
        one.wait_recv()
    moves.finish()


def tail(qkv_term, gains, chunks, inner, number, sums, ticks, arrays, picks):
    first = sums.tick
    ready = sorted(chunks)
    later = [c for c in line_slots(first, ticks) if c < DOWN + GATE_UP]
    _, high, width = sums.shape
    wide = jax.ShapeDtypeStruct((GATE_UP // 2 * high, 8 * inner), bf16)
    moved = jax.ShapeDtypeStruct((2, 8, 2 * high, 2 * width), bf16)
    picks = dict(picks)
    for n in range(QKV):
        where = (
            n // 4, slice(None), slice(n // 2 % 2 * high, (n // 2 % 2 + 1) * high),
            slice(n % 2 * width, (n % 2 + 1) * width),
        )
        picks[CHUNKS - QKV + n] = ("qkv", lambda ref, where=where: ref.at[where])
    return run(
        functools.partial(tail_kernel, ready, later),
        [(qkv_term, ANY), (gains, VMEM)] + [(chunks[c], ANY) for c in ready],
        [(wide, ANY), (wide, ANY), (moved, ANY), (jax.ShapeDtypeStruct(gains.shape[1:], f32), VMEM)],
        [
            pltpu.VMEM(gains.shape, f32),
            pltpu.VMEM((4,) + gains.shape[1:], f32),
            pltpu.VMEM((4,) + gains.shape[1:], f32),
            pltpu.SemaphoreType.DMA((3, 7)),
            pltpu.SemaphoreType.DMA((3, 7)),
            pltpu.SemaphoreType.DMA((2, GATE_UP)),
            pltpu.SemaphoreType.DMA((1 + GATE_UP,)),
        ],
        number, (0, 200 * 8 * high * width * 2, 0), sums=sums, ticks=ticks, arrays=arrays, picks=picks,
    )


def finish_kernel(heads, *refs):
    chunks, rest = refs[: DOWN + OUT + QKV], refs[DOWN + OUT + QKV :]
    gate_rows, up_rows = rest[:2]
    query, key, value, out, gate, up, down = rest[2:9]
    low, wide, load_sems, store_sems = rest[9:]
    _, high, width = chunks[0].shape
    depth = low.shape[0]

    def half(number):
        return slice(number * high, (number + 1) * high)

    def side(number):
        return slice(number * width, (number + 1) * width)

    jobs = []
    for n, ref in enumerate(chunks[:DOWN]):
        jobs.append((ref, [(slice(0, width), down.at[n // 2, :, :, side(n % 2)])]))
    for ref, into in ((gate_rows, gate), (up_rows, up)):
        for low_col in range(0, ref.shape[2], low.shape[3]):
            for number in (0, 1):
                where = (slice(None), half(number), slice(low_col, low_col + low.shape[3]))
                jobs.append((ref.at[where], [(slice(0, low.shape[3]), into.at[where])]))
    for n, ref in enumerate(chunks[DOWN : DOWN + OUT]):
        jobs.append((ref, [(slice(0, width), out.at[:, half(n // 2), side(n % 2)])]))
    part = (heads + 2) * HD
    for n, ref in enumerate(chunks[DOWN + OUT :]):
        stores = []
        for place in range(width // part):
            at, device = place * part, (n // 4 * 2 + n % 2) * (width // part) + place
            for into, first, size in (
                (query, 0, heads * HD), (key, heads * HD, HD), (value, (heads + 1) * HD, HD)
            ):
                there = into.at[:, half(n // 2 % 2), device * size : (device + 1) * size]
                stores.append((slice(at + first, at + first + size), there))
        jobs.append((ref, stores))

    def load(number):
        at, ref = number % depth, jobs[number][0]
        return pltpu.make_async_copy(ref, low.at[at, :, :, : ref.shape[2]], load_sems.at[at])

    def stores(number):
        at = number % depth
        return [
            pltpu.make_async_copy(wide.at[at, :, :, cols], into, store_sems.at[at, which])
            for which, (cols, into) in enumerate(jobs[number][1])
        ]

    for number in range(depth - 1):
        load(number).start()
    for number in range(len(jobs)):
        if number + depth - 1 < len(jobs):
            load(number + depth - 1).start()
        load(number).wait()
        if number >= depth:
            for one in stores(number - depth):
                one.wait()

        def cast(g, _, at=number % depth, cols=slice(0, jobs[number][0].shape[2])):
            wide[at, g, :, cols] = low[at, g, :, cols].astype(f32)
            return 0

        lax.fori_loop(0, low.shape[1], cast, 0)
        for one in stores(number):
            one.start()
    for number in range(len(jobs) - depth, len(jobs)):
        for one in stores(number):
            one.wait()


def finish(chunks, gate_rows, up_rows, heads):
    eight, high, width = chunks[0].shape
    width = 2 * width
    rows, wide = gate_rows.shape

    def split(columns):
        return jax.ShapeDtypeStruct((eight, rows // eight, columns), f32)

    shapes = [split(columns) for columns in (8 * heads * HD, 8 * HD, 8 * HD, width, wide, wide)]
    shapes.append(jax.ShapeDtypeStruct((DOWN // 2, eight, high, width), f32))
    depth = 6
    results = pl.pallas_call(
        functools.partial(finish_kernel, heads),
        out_shape=tuple(shapes),
        in_specs=[pl.BlockSpec(memory_space=pl.ANY)] * (len(chunks) + 2),
        out_specs=tuple([pl.BlockSpec(memory_space=pl.ANY)] * 7),
        scratch_shapes=[
            pltpu.VMEM((depth, eight, high, width), bf16),
            pltpu.VMEM((depth, eight, high, width), f32),
            pltpu.SemaphoreType.DMA((depth,)),
            pltpu.SemaphoreType.DMA((depth, 12)),
        ],
        compiler_params=pltpu.CompilerParams(vmem_limit_bytes=60 * 2**20),
        cost_estimate=pl.CostEstimate(
            flops=0, bytes_accessed=3 * CHUNKS * eight * high * width, transcendentals=0
        ),
    )(
        *chunks, gate_rows.reshape(eight, rows // eight, wide),
        up_rows.reshape(eight, rows // eight, wide),
    )
    flat = [result.reshape(rows, -1) for result in results[:6]]
    return flat + [results[6].reshape(-1, width)]


def sum_over_sequences(term):
    return lax.psum(term, "rep").astype(f32)


def on_device(
    layer_input,
    cotangent,
    cut_order,
    piece_ids,
    w_query,
    w_key,
    w_value,
    w_out,
    w_gate,
    w_up,
    w_down,
    gain_attn,
    gain_ffn,
):
    groups = lax.axis_size("grp")
    reps = lax.axis_size("rep")
    own_index = lax.axis_index("grp")
    _, local_rows, model_width = layer_input.shape
    length = piece_ids.shape[1]
    rows_here = w_query.shape[0]
    q_width = w_query.shape[1]
    kv_heads = w_key.shape[1] // HD
    heads = q_width // HD // groups
    copies = groups // kv_heads
    hidden_here = w_down.shape[0]
    cosine, sine = turn_tables(length)

    near = groups == 8 and reps == 4 and copies == 1 and 2 * hidden_here == model_width

    def gather(rows):
        return lax.all_gather(rows, "grp", axis=0, tiled=True)

    def scatter(first, second, turned):
        term = against_rows(first, second) if turned else matmul_f32(first, second)
        return lax.psum_scatter(
            term.astype(bf16), "grp", scatter_dimension=0, tiled=True
        ).astype(f32)

    def to_columns(parts):
        return lax.all_to_all(parts, "grp", 1, 0, tiled=True).reshape(-1, parts.shape[-1])

    def per_group(weight):
        return weight.reshape(rows_here, groups, -1)

    def per_kv_head(weight):
        return jnp.repeat(weight.reshape(rows_here, kv_heads, HD), copies, axis=1)

    x_rows = layer_input.reshape(local_rows, model_width)
    x_flat = x_rows.astype(f32)
    inv_one = lax.rsqrt(jnp.mean(x_flat * x_flat, -1, keepdims=True) + EPS)
    unit_one = x_flat * inv_one
    attn_gain, ffn_gain = gain_attn.reshape(1, -1), gain_ffn.reshape(1, -1)
    if near:
        share = rows_here // (4 * reps) * 3
        spread = columns_of_some((w_gate, w_up), share, 11)
        x_first, spread = lax.optimization_barrier((x_rows, spread))
        spread = lax.all_gather(spread, "rep", axis=0)
        normed_one, cols_qkv = gather_normed(
            x_first, attn_gain, (w_query, w_key, w_value), number=1
        )
        last_gate, last_up, normed_one = lax.optimization_barrier(
            (w_gate[reps * share :], w_up[reps * share :], normed_one)
        )
        rest = to_columns(
            jnp.concatenate(
                [part.reshape(rows_here - reps * share, groups, -1) for part in (last_gate, last_up)],
                -1,
            )
        ).reshape(groups, rows_here - reps * share, -1)
    else:
        normed_one = gather(rms_normed(x_flat, attn_gain).astype(bf16))
        cols_qkv = to_columns(
            jnp.concatenate([per_group(w_query), per_kv_head(w_key), per_kv_head(w_value)], -1)
        )
        cols_gate_up = to_columns(jnp.concatenate([per_group(w_gate), per_group(w_up)], -1))
    attended, query, key, value, lse, attended_placed = attend(
        cut_order, normed_one, cols_qkv, cosine, sine, piece_ids, heads
    )
    if near:
        mid = product_scattered(attended, w_out, False, base=x_rows, number=2)[0]
    else:
        mid = x_flat + scatter(attended, w_out, False)
    grad_out = cotangent.reshape(local_rows, model_width)

    def back_through_attention(grad_attended, **line):
        return attend_back(
            cut_order, grad_attended, attended_placed, query, key, value, lse, cosine, sine,
            piece_ids, heads, **line,
        )

    q_here = heads * HD
    if near:
        normed_two, hidden, cols_gate_up, grad_gate_up, down_term = feed_forward(
            mid, ffn_gain, grad_out, spread, rest, w_down, number=3
        )
        cols_gate_up = cols_gate_up.reshape(model_width, -1)
        high, half_width = 2 * rows_here // GATE_UP, model_width // 2
        sums = Sums((8, high, half_width))
        terms = {"down": down_term.reshape(DOWN // 2, 8, high, model_width)}

        def pick_whole(n):
            return "down", lambda ref: ref.at[n // 2, :, :, n % 2 * half_width : (n % 2 + 1) * half_width]

        def pick_rows(name, n):
            rows, side = n // 2 * high, n % 2 * half_width
            return name, lambda ref: ref.at[:, rows : rows + high, side : side + half_width]

        picks = [pick_whole(n) for n in range(DOWN)]
        picks += [pick_rows("gate_up", n) for n in range(GATE_UP)]
        picks += [pick_rows("out", n) for n in range(OUT)]

        def line(number, ticks):
            names = sorted(
                {picks[t][0] for t in range(sums.tick, sums.tick + ticks) if t < len(picks)}
            )
            return dict(
                number=number, ticks=ticks, sums=sums, picks=dict(enumerate(picks)),
                arrays=[(name, terms[name]) for name in names],
            )

        result, terms["gate_up"] = product_scattered(
            hidden, w_down, False, extra=(normed_two, grad_gate_up), base=mid, dtype=bf16,
            steps={"x": 1, "y": 1, "work": 1, "relayed": 1, "sibling": 1, "work2": 1, "work3": 1}, **line(5, 10),
        )
        grad_mid, gain_ffn_term = product_scattered(
            grad_gate_up, cols_gate_up, True, back=(grad_out, mid, ffn_gain),
            steps={"across": 1, "x": 1, "y": 1, "relayed": 1, "sibling": 1, "halves": 1}, **line(6, 10),
        )
        grad_attended, out_term = attended_back(grad_mid, w_out, attended, **line(7, 8))
        terms["out"] = out_term.reshape(8, OUT // 2 * high, model_width)
        grad_qkv = back_through_attention(grad_attended, **line(8, 7))
        grad_x, gain_attn_term, qkv_term = product_scattered(
            grad_qkv, cols_qkv, True, extra=(normed_one, None), dtype=bf16,
            back=(grad_mid, x_rows, attn_gain),
            steps={"y": 1, "work": 1, "relayed": 2, "work2": 1, "work3": 1}, **line(9, 8),
        )
        gains = jnp.stack([gain_attn_term, gain_ffn_term]).reshape(2, groups, rows_here)
        gains = jnp.pad(jnp.moveaxis(gains, 0, 1), ((0, 0), (0, 6), (0, 0)))
        rest = line(10, CHUNKS + 2 * LAG - sums.tick)
        gate_rows, up_rows, qkv_rows, own_gains = tail(
            qkv_term.reshape(8, 8, 2 * high, -1), gains,
            {c: sums.done[c] for c in sums.done if c >= DOWN}, hidden_here, **rest,
        )
        straight = [n for n in range(CHUNKS) if n < DOWN or n >= DOWN + GATE_UP]
        weight_grads = finish([sums.done[n] for n in straight], gate_rows, up_rows, heads)
        shaped = tuple(rows.reshape(layer_input.shape) for rows in (result, grad_x))
        return shaped + tuple(weight_grads) + (own_gains[0], own_gains[1])

    unit_one = x_flat * inv_one
    inv_two = lax.rsqrt(jnp.mean(mid * mid, -1, keepdims=True) + EPS)
    unit_two = mid * inv_two
    normed_two = gather((unit_two * ffn_gain).astype(bf16))
    grad_all = gather(grad_out)
    gate_up = matmul_f32(normed_two, cols_gate_up)
    gate_proj, up_proj = gate_up[:, :hidden_here], gate_up[:, hidden_here:]
    sigmoid_gate = jax.nn.sigmoid(gate_proj)
    swish = gate_proj * sigmoid_gate
    hidden = (swish * up_proj).astype(bf16)
    gate_part = up_proj * sigmoid_gate * (1.0 + gate_proj * (1.0 - sigmoid_gate))
    down_term = over_tokens(hidden, grad_all).astype(bf16)
    grad_hidden = against_rows(grad_all, w_down)
    grad_gate_up = jnp.concatenate([grad_hidden * gate_part, grad_hidden * swish], 1).astype(bf16)
    grad_mid, gain_ffn_term = norm_back(
        grad_out.astype(f32), scatter(grad_gate_up, cols_gate_up, True), unit_two, inv_two, gain_ffn
    )
    grad_mid_low = gather(grad_mid.astype(bf16))
    grad_qkv = back_through_attention(against_rows(grad_mid_low, w_out).astype(bf16))
    grad_x, gain_attn_term = norm_back(
        grad_mid, scatter(grad_qkv, cols_qkv, True), unit_one, inv_one, gain_attn
    )

    def to_rows(term):
        return lax.all_to_all(
            term.astype(bf16).reshape(groups, rows_here, -1), "grp", 0, 0, tiled=True
        )

    def whole_rows(term):
        return jnp.moveaxis(term, 0, 1).reshape(rows_here, -1)

    def kv_rows(term):
        return jnp.sum(
            jnp.moveaxis(term, 0, 1).reshape(rows_here, kv_heads, copies, HD), 2
        ).reshape(rows_here, -1)

    gate_up_term = sum_over_sequences(to_rows(over_tokens(normed_two, grad_gate_up)))
    out_term = sum_over_sequences(over_tokens(attended, grad_mid_low).astype(bf16))
    qkv_term = sum_over_sequences(to_rows(over_tokens(normed_one, grad_qkv)))
    gain_total = lax.psum(jnp.stack([gain_attn_term, gain_ffn_term]), ("grp", "rep"))
    own_gains = lax.dynamic_slice_in_dim(gain_total, own_index * rows_here, rows_here, 1)
    return (
        (mid + scatter(hidden, w_down, False)).astype(bf16).reshape(layer_input.shape),
        grad_x.astype(bf16).reshape(layer_input.shape),
        whole_rows(qkv_term[..., :q_here]),
        kv_rows(qkv_term[..., q_here : q_here + HD]),
        kv_rows(qkv_term[..., q_here + HD :]),
        out_term,
        whole_rows(gate_up_term[..., :hidden_here]),
        whole_rows(gate_up_term[..., hidden_here:]),
        sum_over_sequences(down_term),
        own_gains[0],
        own_gains[1],
    )


def solution(mesh):
    tokens, table, rows, whole = P("rep", "grp", None), P("rep", None), P("grp", None), P()
    return jax.shard_map(
        on_device,
        mesh=mesh,
        in_specs=(tokens, tokens, table, table) + (rows,) * 7 + (whole,) * 2,
        out_specs=(tokens, tokens) + (rows,) * 7 + (P("grp"),) * 2,
        check_vma=False,
    )
```

```python
import functools

import jax
import jax.numpy as jnp
import numpy as np
from jax import lax
from jax.experimental import pallas as pl
from jax.experimental.pallas import tpu as pltpu
from jax.sharding import PartitionSpec as P

HD = 128
EPS = 1e-05
ROPE_BASE = 1000000.0
SCORE_SCALE = HD**-0.5
LOG2E = 1.4426950408889634
TO_EXP2 = SCORE_SCALE * LOG2E
NEG = -1e30

MESH = pl.DeviceIdType.MESH
f32 = jnp.float32
bf16 = jnp.bfloat16


def matmul_f32(first, second):
    return jnp.dot(first, second, preferred_element_type=f32)


def against_rows(first, second):
    return lax.dot_general(first, second, (((1,), (1,)), ((), ())), preferred_element_type=f32)


def over_tokens(first, second):
    return lax.dot_general(first, second, (((0,), (0,)), ((), ())), preferred_element_type=f32)


def turn_tables(length):
    half_size = HD // 2
    inverse = np.float32(ROPE_BASE) ** (-(np.arange(half_size, dtype=np.float32) * 2) / HD)
    angles = np.arange(length, dtype=np.float32)[:, None] * inverse.astype(np.float32)
    cosine, sine = np.cos(angles), np.sin(angles)
    tables = np.concatenate([cosine, cosine], -1), np.concatenate([-sine, sine], -1)
    return tuple(jnp.asarray(table.astype(np.float32)) for table in tables)


def norm_back(upstream, grad_normed, unit_rows, inv_root, gain):
    scaled = grad_normed * gain
    center_term = jnp.mean(scaled * unit_rows, -1, keepdims=True)
    return (
        upstream + inv_root * (scaled - unit_rows * center_term),
        jnp.sum(grad_normed * unit_rows, 0),
    )


def fold_lanes(values, op):
    out = values[:, :HD]
    for at in range(HD, values.shape[1], HD):
        out = op(out, values[:, at : at + HD])
    return out


def as_column(row):
    return jnp.broadcast_to(row, (HD, row.shape[1])).T[:, 0:1]


def as_row(column):
    return jnp.broadcast_to(column, (column.shape[0], HD)).T[0:1, :]


def attend_kernel(
    heads, cuts, block,
    order_ref, rows_hbm, weight_hbm, cos_ref, sin_ref, piece_ref,
    out_ref, q_ref, k_ref, v_ref, lse_ref, placed,
    scores, rows_ref, weight_ref, qkv_ref, sems,
):
    length = rows_ref.shape[0]
    cut = length // cuts
    blocks = length // block
    loads = [pltpu.make_async_copy(weight_hbm, weight_ref, sems.at[blocks])]
    for i in range(blocks):
        at = slice(i * block, (i + 1) * block)
        loads.append(pltpu.make_async_copy(rows_hbm.at[at, :], rows_ref.at[at, :], sems.at[i]))
    for load in loads:
        load.start()

    def place_cut(r, first):
        src = pl.ds(pl.multiple_of(r * cut, cut), cut)
        dst = pl.ds(pl.multiple_of(order_ref[0, first + r] * cut, cut), cut)
        cosine, sine = cos_ref[dst, :], sin_ref[dst, :]
        for h in range(heads + 1):
            part = qkv_ref[src, h * HD : (h + 1) * HD]
            turned = (part * cosine + pltpu.roll(part, HD // 2, 1) * sine).astype(bf16)
            if h < heads:
                q_ref[h, dst, :] = turned
            else:
                k_ref[dst, :] = turned
        v_ref[dst, :] = qkv_ref[src, (heads + 1) * HD :].astype(bf16)
        return first

    loads[0].wait()
    for i in range(blocks):
        loads[1 + i].wait()
        qkv_ref[...] = matmul_f32(rows_ref[i * block : (i + 1) * block, :], weight_ref[...])
        lax.fori_loop(0, block // cut, place_cut, i * (block // cut))

    def one_block(i, _):
        rows = pl.ds(pl.multiple_of(i * block, block), block)
        query = q_ref[:, rows, :].reshape(heads * block, HD)

        def score(j, high):
            cols = pl.ds(pl.multiple_of(j * block, block), block)
            tile = against_rows(query, k_ref[cols, :])
            scores[j] = tile
            return jnp.maximum(high, fold_lanes(tile, jnp.maximum))

        high = lax.fori_loop(0, i, score, jnp.full((heads * block, HD), NEG, f32))
        tile = against_rows(query, k_ref[rows, :])
        q_at = lax.broadcasted_iota(jnp.int32, (block, block), 0)
        k_at = lax.broadcasted_iota(jnp.int32, (block, block), 1)
        k_piece = piece_ref[0:1, rows].astype(f32)
        q_piece = as_column(k_piece)
        allowed = (k_at <= q_at) | ((q_piece != 0) & (q_piece == k_piece))
        tile = jnp.concatenate(
            [jnp.where(allowed, tile[h * block : (h + 1) * block], NEG) for h in range(heads)], 0
        )
        scores[i] = tile
        high = jnp.max(jnp.maximum(high, fold_lanes(tile, jnp.maximum)), 1, keepdims=True)

        def weigh(j, state):
            total, mixed = state
            cols = pl.ds(pl.multiple_of(j * block, block), block)
            prob = jnp.exp2((scores[j] - high) * TO_EXP2)
            total = total + fold_lanes(prob, jnp.add)
            return total, mixed + matmul_f32(prob.astype(bf16), v_ref[cols, :])

        zero = jnp.zeros((heads * block, HD), f32)
        total, mixed = lax.fori_loop(0, i + 1, weigh, (zero, zero))
        total = jnp.sum(total, 1, keepdims=True)
        mixed = (mixed / total).astype(bf16)
        log_total = high * TO_EXP2 + jnp.log2(total)
        for h in range(heads):
            placed[rows, h * HD : (h + 1) * HD] = mixed[h * block : (h + 1) * block]
            lse_ref[h : h + 1, rows] = as_row(log_total[h * block : (h + 1) * block])
        return 0

    lax.fori_loop(0, blocks, one_block, 0)

    def store_cut(r, _):
        dst = pl.ds(pl.multiple_of(r * cut, cut), cut)
        src = pl.ds(pl.multiple_of(order_ref[0, r] * cut, cut), cut)
        out_ref[dst, :] = placed[src, :]
        return 0

    lax.fori_loop(0, cuts, store_cut, 0)


def vmem_specs(count):
    return [pl.BlockSpec(memory_space=pltpu.VMEM)] * count


def attend(order, rows, weight, cosine, sine, piece, heads):
    length, width = rows.shape
    block = min(512, length)
    return pl.pallas_call(
        functools.partial(attend_kernel, heads, order.shape[1], block),
        out_shape=(
            jax.ShapeDtypeStruct((length, heads * HD), bf16),
            jax.ShapeDtypeStruct((heads, length, HD), bf16),
            jax.ShapeDtypeStruct((length, HD), bf16),
            jax.ShapeDtypeStruct((length, HD), bf16),
            jax.ShapeDtypeStruct((heads, length), f32),
            jax.ShapeDtypeStruct((length, heads * HD), bf16),
        ),
        in_specs=[pl.BlockSpec(memory_space=pltpu.SMEM)]
        + [pl.BlockSpec(memory_space=pl.ANY)] * 2
        + vmem_specs(3),
        out_specs=tuple(vmem_specs(6)),
        scratch_shapes=[
            pltpu.VMEM((length // block, heads * block, block), f32),
            pltpu.VMEM(rows.shape, bf16),
            pltpu.VMEM(weight.shape, bf16),
            pltpu.VMEM((block, weight.shape[1]), f32),
            pltpu.SemaphoreType.DMA((length // block + 1,)),
        ],
        compiler_params=pltpu.CompilerParams(vmem_limit_bytes=60 * 2**20),
        cost_estimate=pl.CostEstimate(
            flops=3 * heads * length * length * HD + 2 * length * width * weight.shape[1],
            bytes_accessed=10 * length * HD * heads * 4 + rows.size * 2,
            transcendentals=heads * length * length // 2,
        ),
    )(order, rows, weight, cosine, sine, piece)


DOWN, GATE_UP, OUT, QKV = 16, 32, 4, 8
CHUNKS = DOWN + GATE_UP + OUT + QKV
LAG = 3


def is_chunk(number):
    return 0 <= number < CHUNKS


def is_middle():
    rank = lax.axis_index("rep")
    return (rank == 1) | (rank == 2)


def is_end():
    rank = lax.axis_index("rep")
    return (rank == 0) | (rank == 3)


class NoLine:
    ticks = 0

    def signal(self, barrier):
        pass

    def greet(self, barrier, others):
        if others:
            pl.semaphore_wait(barrier, others)

    def start(self):
        pass

    def step(self, times=1):
        pass

    def end(self):
        pass


class Line:
    def __init__(self, first, ticks, picks, refs, outs, scratch):
        self.first, self.ticks, self.picks, self.refs, self.outs = first, ticks, picks, refs, outs
        (
            self.inward, self.across, self.own, self.pair, self.total, self.sems, self.local,
            self.carries,
        ) = scratch
        rank = lax.axis_index("rep")
        self.partner = {"rep": rank + 1 - 2 * (rank % 2)}
        self.peer = {"rep": 3 - rank}
        self.now = 0
        self.kept = []

    def signal(self, barrier):
        pl.semaphore_signal(barrier, inc=1, device_id=self.partner, device_id_type=MESH)

        @pl.when(is_middle())
        def _():
            pl.semaphore_signal(barrier, inc=1, device_id=self.peer, device_id_type=MESH)

    def greet(self, barrier, others):
        @pl.when(is_middle())
        def _():
            pl.semaphore_wait(barrier, others + 2)

        @pl.when(is_end())
        def _():
            pl.semaphore_wait(barrier, others + 1)

    def remote(self, hop, number, src, dst, device):
        return pltpu.make_async_remote_copy(
            src_ref=src, dst_ref=dst, send_sem=self.sems.at[0, hop, number],
            recv_sem=self.sems.at[1, hop, number], device_id=device, device_id_type=MESH,
        )

    def hops(self, number):
        tick = self.first + number
        term = pair = total = None
        if is_chunk(tick):
            which, pick = self.picks[tick]
            term = (
                lambda: self.remote(
                    0, number, pick(self.refs[which]), self.inward.at[number], self.partner
                ),
                lambda: pltpu.make_async_copy(
                    pick(self.refs[which]), self.own.at[tick % LAG], self.local.at[0, number]
                ),
            )
        if is_chunk(tick - LAG):
            held = self.pair.at[(tick - LAG) % (LAG + 1)]
            before = self.refs[f"pair{number}"] if number < LAG else held
            pair = (
                lambda: self.remote(1, number, before, self.across.at[number], self.peer),
                lambda: pltpu.make_async_copy(before, held, self.carries.at[0, number]),
            )
        if is_chunk(tick - 2 * LAG):
            held_total = self.total.at[(tick - 2 * LAG) % (LAG + 1)]
            done = self.refs[f"total{number}"] if number < LAG else held_total
            slot = self.outs[tick - 2 * LAG]
            total = (
                lambda: self.remote(2, number, done, slot, self.partner),
                lambda: pltpu.make_async_copy(done, slot, self.local.at[1, number]),
            )
        return term, pair, total

    def open(self, number):
        term, pair, total = self.hops(number)

        @pl.when(is_end())
        def _():
            if term:
                term[0]().start()

        @pl.when(is_middle())
        def _():
            if pair:
                pair[0]().start()
            if total:
                total[0]().start()
            if term:
                term[1]().start()
            if total:
                total[1]().start()
            if pair and number < LAG:
                pair[1]().start()

    def close(self, number):
        term, pair, total = self.hops(number)

        @pl.when(is_end())
        def _():
            if term:
                term[0]().wait_send()
            if total:
                total[0]().wait_recv()

        @pl.when(is_middle())
        def _():
            if total:
                total[0]().wait_send()
                total[1]().wait()
            if pair:
                pair[0]().wait_send()
                pair[0]().wait_recv()
            if term:
                term[0]().wait_recv()

    def add(self, number):
        term, pair, _ = self.hops(number)
        tick = self.first + number

        def sum_of(into, first, second):
            def one(g, _):
                into[g] = (first[g].astype(f32) + second[g].astype(f32)).astype(bf16)
                return 0

            lax.fori_loop(0, into.shape[0], one, 0)

        @pl.when(is_middle())
        def _():
            if pair:
                if number < LAG:
                    pair[1]().wait()
                before = tick - LAG
                sum_of(
                    self.total.at[before % (LAG + 1)], self.pair.at[before % (LAG + 1)],
                    self.across.at[number],
                )
            if term:
                term[1]().wait()
                sum_of(self.pair.at[tick % (LAG + 1)], self.own.at[tick % LAG], self.inward.at[number])

    def keep(self, number):
        tick = self.first + number
        which = number - (self.ticks - LAG)
        made = []
        if is_chunk(tick):
            made.append((self.pair.at[tick % (LAG + 1)], self.outs[f"pair{which}"], (1, which)))
        if is_chunk(tick - LAG):
            held = self.total.at[(tick - LAG) % (LAG + 1)]
            made.append((held, self.outs[f"total{which}"], (2, which)))
        copies = [
            lambda src=src, dst=dst, at=at: pltpu.make_async_copy(src, dst, self.carries.at[*at])
            for src, dst, at in made
        ]

        @pl.when(is_middle())
        def _():
            for copy in copies:
                copy().start()

        self.kept += copies

    def start(self):
        for number in range(LAG):
            self.open(number)

    def step(self, times=1):
        for _ in range(times):
            if self.now + LAG < self.ticks:
                self.settle()
                self.open(self.now + LAG - 1)

    def settle(self):
        self.close(self.now)
        self.add(self.now)
        if self.now >= self.ticks - LAG:
            self.keep(self.now)
        self.now += 1

    def end(self):
        while self.now + LAG < self.ticks:
            self.step()
        while self.now < self.ticks:
            self.settle()

        @pl.when(is_middle())
        def _():
            for copy in self.kept:
                copy().wait()


def line_slots(first, ticks):
    return [t - 2 * LAG for t in range(first, first + ticks) if is_chunk(t - 2 * LAG)]


class Sums:
    def __init__(self, shape):
        self.shape, self.tick, self.kept, self.done = shape, 0, {}, {}


def run(kernel, ins, outs, scratch, number, cost, sums=None, ticks=0, arrays=(), picks=None, vmem=58):
    ins, outs, scratch = list(ins), list(outs), list(scratch)
    counts = (len(ins), len(outs), len(scratch))
    first = sums.tick if ticks else 0
    names_in, names_out = [], []
    if ticks:
        for name, array in arrays:
            names_in.append(name)
            ins.append((array, pl.ANY))
        for which in range(LAG):
            for name, chunk_at in ((f"pair{which}", first - LAG), (f"total{which}", first - 2 * LAG)):
                if is_chunk(chunk_at + which):
                    names_in.append(name)
                    ins.append((sums.kept[name], pl.ANY))
        names_out = line_slots(first, ticks)
        after = first + ticks
        for which in range(LAG):
            for name, chunk_at in ((f"pair{which}", after - LAG), (f"total{which}", after - 2 * LAG)):
                if is_chunk(chunk_at + which):
                    names_out.append(name)
        outs += [(jax.ShapeDtypeStruct(sums.shape, bf16), pl.ANY)] * len(names_out)
        scratch += [
            pltpu.VMEM((ticks,) + sums.shape, bf16),
            pltpu.VMEM((ticks,) + sums.shape, bf16),
            pltpu.VMEM((LAG,) + sums.shape, bf16),
            pltpu.VMEM((LAG + 1,) + sums.shape, bf16),
            pltpu.VMEM((LAG + 1,) + sums.shape, bf16),
            pltpu.SemaphoreType.DMA((2, 3, ticks)),
            pltpu.SemaphoreType.DMA((2, ticks)),
            pltpu.SemaphoreType.DMA((3, LAG)),
        ]

    def body(*refs):
        in_refs, rest = refs[: len(ins)], refs[len(ins) :]
        out_refs, scratch_refs = rest[: len(outs)], rest[len(outs) :]
        line = NoLine()
        if ticks:
            line = Line(
                first, ticks, picks, dict(zip(names_in, in_refs[counts[0] :])),
                dict(zip(names_out, out_refs[counts[1] :])), scratch_refs[counts[2] :],
            )
        kernel(in_refs[: counts[0]], out_refs[: counts[1]], scratch_refs[: counts[2]], line)

    results = pl.pallas_call(
        body,
        out_shape=tuple(shape for shape, _ in outs),
        in_specs=[pl.BlockSpec(memory_space=space) for _, space in ins],
        out_specs=tuple(pl.BlockSpec(memory_space=space) for _, space in outs),
        scratch_shapes=scratch,
        compiler_params=pltpu.CompilerParams(
            vmem_limit_bytes=vmem * 2**20,
            **({} if number is None else {"collective_id": number, "has_side_effects": True}),
        ),
        cost_estimate=pl.CostEstimate(
            flops=cost[0], bytes_accessed=cost[1], transcendentals=cost[2]
        ),
    )(*[array for array, _ in ins])
    for name, result in zip(names_out, results[counts[1] :]):
        if name in line_slots(first, ticks):
            sums.done[name] = result
        else:
            sums.kept[name] = result
    if ticks:
        sums.tick += ticks
    return results[: counts[1]]


SMEM, VMEM, ANY = pltpu.SMEM, pltpu.VMEM, pl.ANY


def attend_back_kernel(
    heads, block, ins, outs, scratch, line
):
    grad_ref, out_ref, q_ref, k_ref, v_ref, lse_ref, cos_ref, sin_ref, piece_ref, place_ref = ins
    (grad_qkv_ref,) = outs
    grads, centers, grad_q, placed = scratch
    if line.ticks:
        line.signal(pltpu.get_barrier_semaphore())
        line.greet(pltpu.get_barrier_semaphore(), 0)
        line.start()
    length = grad_ref.shape[0]
    blocks = length // block

    def take_block(i, _):
        rows = pl.ds(pl.multiple_of(i * block, block), block)
        position = lax.broadcasted_iota(jnp.int32, (block, length), 0) + i * block
        chosen = jnp.where(place_ref[...] == position, 1.0, 0.0).astype(bf16)
        taken = matmul_f32(chosen, grad_ref[...]).astype(bf16)
        for h in range(heads):
            grad = taken[:, h * HD : (h + 1) * HD]
            grads[h, rows, :] = grad
            product = grad.astype(f32) * out_ref[rows, h * HD : (h + 1) * HD].astype(f32)
            centers[h, rows, :] = jnp.broadcast_to(
                jnp.sum(product, 1, keepdims=True), (block, HD)
            )
        return 0

    lax.fori_loop(0, blocks, take_block, 0)
    grad_q[...] = jnp.zeros_like(grad_q)

    def key_block(j, _):
        cols = pl.ds(pl.multiple_of(j * block, block), block)
        key, value = k_ref[cols, :], v_ref[cols, :]

        def one(i, state, diagonal):
            grad_key, grad_value = state
            rows = pl.ds(pl.multiple_of(i * block, block), block)
            for h in range(heads):
                query, grad = q_ref[h, rows, :], grads[h, rows, :]
                log_total = lse_ref[h : h + 1, rows]
                center = centers[h, rows, :].T[0:1, :]
                prob = jnp.exp2(against_rows(key, query) * TO_EXP2 - log_total)
                if diagonal:
                    k_at = lax.broadcasted_iota(jnp.int32, (block, block), 0)
                    q_at = lax.broadcasted_iota(jnp.int32, (block, block), 1)
                    q_piece = piece_ref[0:1, cols].astype(f32)
                    k_piece = as_column(q_piece)
                    allowed = (k_at <= q_at) | ((q_piece != 0) & (q_piece == k_piece))
                    prob = jnp.where(allowed, prob, 0.0)
                grad_prob = against_rows(value, grad)
                grad_score = (prob * (grad_prob - center)).astype(bf16)
                grad_value = grad_value + matmul_f32(prob.astype(bf16), grad)
                grad_key = grad_key + matmul_f32(grad_score, query)
                grad_q[h, rows, :] += over_tokens(grad_score, key)
            return grad_key, grad_value

        zero = jnp.zeros((block, HD), f32)
        state = one(j, (zero, zero), True)
        grad_key, grad_value = lax.fori_loop(
            j + 1, blocks, functools.partial(one, diagonal=False), state
        )
        grad_key = grad_key * SCORE_SCALE
        grad_key = grad_key * cos_ref[cols, :] - pltpu.roll(grad_key, HD // 2, 1) * sin_ref[cols, :]
        placed[cols, heads * HD : (heads + 1) * HD] = grad_key.astype(bf16)
        placed[cols, (heads + 1) * HD :] = grad_value.astype(bf16)
        return 0

    for j in range(min(2, blocks - 1)):
        lax.fori_loop(j, j + 1, key_block, 0)
        line.step(1 + j)
    lax.fori_loop(min(2, blocks - 1), blocks, key_block, 0)

    def turn_back(i, _):
        rows = pl.ds(pl.multiple_of(i * block, block), block)
        for h in range(heads):
            grad = grad_q[h, rows, :] * SCORE_SCALE
            grad = grad * cos_ref[rows, :] - pltpu.roll(grad, HD // 2, 1) * sin_ref[rows, :]
            placed[rows, h * HD : (h + 1) * HD] = grad.astype(bf16)
        return 0

    lax.fori_loop(0, blocks, turn_back, 0)
    line.step()

    def store_block(i, _):
        rows = pl.ds(pl.multiple_of(i * block, block), block)
        place = as_column(place_ref[0:1, rows].astype(f32)).astype(jnp.int32)
        position = lax.broadcasted_iota(jnp.int32, (block, length), 1)
        chosen = jnp.where(place == position, 1.0, 0.0).astype(bf16)
        grad_qkv_ref[rows, :] = matmul_f32(chosen, placed[...]).astype(bf16)
        return 0

    lax.fori_loop(0, blocks, store_block, 0)
    line.end()


def attend_back(
    order, grad, out, query, key, value, lse, cosine, sine, piece, heads, **line
):
    length = grad.shape[0]
    block = min(512, length)
    cut = length // order.shape[1]
    place = (order.reshape(-1, 1) * cut + jnp.arange(cut, dtype=order.dtype)).reshape(1, length)
    tall = [grad, out, query, key, value, lse, cosine, sine, piece, place]
    return run(
        functools.partial(attend_back_kernel, heads, block),
        [(array, VMEM) for array in tall],
        [(jax.ShapeDtypeStruct((length, (heads + 2) * HD), bf16), VMEM)],
        [
            pltpu.VMEM((heads, length, HD), bf16),
            pltpu.VMEM((heads, length, HD), f32),
            pltpu.VMEM((heads, length, HD), f32),
            pltpu.VMEM((length, (heads + 2) * HD), bf16),
        ],
        line.pop("number", None),
        (8 * heads * length * length * HD, 14 * length * HD * heads * 4, heads * length * length // 2),
        **line,
    )[0]


def place_in_group():
    me = lax.axis_index("grp")
    return me // 4, (me // 2) % 2, me % 2


def other(flip_y, flip_x, flip_core):
    y, x, core = place_in_group()
    return ((y + flip_y) % 2) * 4 + ((x + flip_x) % 2) * 2 + (core + flip_core) % 2


def chip_rows(flip_y, flip_x, rows):
    y, x, _ = place_in_group()
    first = (((y + flip_y) % 2) * 2 + (x + flip_x) % 2) * (2 * rows)
    return pl.ds(pl.multiple_of(first, 2 * rows), 2 * rows)


NEIGHBOURS = ((0, 0, 1), (0, 1, 0), (1, 0, 0))
EVERYONE = tuple((n // 4, (n // 2) % 2, n % 2) for n in range(1, 8))


def greet_group(line, flips=NEIGHBOURS, between=None):
    barrier = pltpu.get_barrier_semaphore()
    for flip in flips:
        pl.semaphore_signal(barrier, inc=1, device_id={"grp": other(*flip)}, device_id_type=MESH)
    line.signal(barrier)
    if between:
        between()
    line.greet(barrier, len(flips))


SIBLING, ALONG_X, ALONG_Y, ACROSS = (0, 0), (0, 1), (1, 0), (1, 1)


class Gather:
    TO_S, TO_X, TO_Y = (0, 0, 1), (0, 1, 0), (1, 0, 0)

    def __init__(self, rows, all_ref, sends, recvs):
        self.rows, self.all_ref, self.sends, self.recvs = rows, all_ref, sends, recvs
        self.started = []

    def copy(self, number, chip, core, part, target):
        first = other(*chip, core) * self.rows
        if part is None:
            where = pl.ds(pl.multiple_of(first, self.rows), self.rows)
        else:
            half = self.rows // 2
            where = pl.ds(pl.multiple_of(first + part * half, half), half)
        where = self.all_ref.at[where, :]
        return pltpu.make_async_remote_copy(
            src_ref=where, dst_ref=where, send_sem=self.sends.at[number],
            recv_sem=self.recvs.at[number], device_id={"grp": other(*target)}, device_id_type=MESH,
        )

    def send(self, *what):
        one = self.copy(*what)
        one.start()
        self.started.append(one)

    def landed(self, number, chip, core, part):
        self.copy(number, chip, core, part, self.TO_S).wait_recv()

    def send_own(self):
        self.send(1, SIBLING, 0, 1, self.TO_X)
        self.send(3, SIBLING, 0, 0, self.TO_Y)
        self.send(0, SIBLING, 0, None, self.TO_S)
        self.send(2, SIBLING, 0, 0, self.TO_X)
        self.send(4, SIBLING, 0, 1, self.TO_Y)

    def sibling(self):
        self.landed(0, SIBLING, 1, None)

    def relay(self):
        self.landed(1, ALONG_X, 0, 1)
        self.send(6, ALONG_X, 0, 1, self.TO_Y)
        self.landed(3, ALONG_Y, 0, 0)
        self.send(5, ALONG_Y, 0, 0, self.TO_X)
        self.send(7, ALONG_X, 0, 1, self.TO_S)
        self.send(8, ALONG_Y, 0, 0, self.TO_S)

    def pass_second(self):
        self.landed(2, ALONG_X, 0, 0)
        self.send(9, ALONG_X, 0, 0, self.TO_S)
        self.landed(4, ALONG_Y, 0, 1)
        self.send(10, ALONG_Y, 0, 1, self.TO_S)

    def along_x(self):
        self.landed(7, ALONG_X, 1, 1)
        self.landed(9, ALONG_X, 1, 0)

    def pass_across(self):
        self.landed(5, ACROSS, 0, 0)
        self.send(11, ACROSS, 0, 0, self.TO_S)
        self.landed(6, ACROSS, 0, 1)
        self.send(12, ACROSS, 0, 1, self.TO_S)

    def along_y(self):
        self.landed(8, ALONG_Y, 1, 0)
        self.landed(10, ALONG_Y, 1, 1)

    def across(self):
        self.landed(11, ACROSS, 1, 0)
        self.landed(12, ACROSS, 1, 1)

    def finish(self):
        for one in self.started:
            one.wait_send()


def gather_rows(rows, all_ref, sends, recvs, on_chip, line, then=None):
    rows_of = Gather(rows, all_ref, sends, recvs)
    rows_of.send_own()
    if then:
        then()
    rows_of.sibling()
    on_chip(*SIBLING)
    rows_of.relay()
    line.step(2)
    rows_of.pass_second()
    line.step(2)
    rows_of.along_x()
    on_chip(*ALONG_X)
    rows_of.pass_across()
    line.step()
    rows_of.along_y()
    on_chip(*ALONG_Y)
    rows_of.across()
    on_chip(*ACROSS)
    rows_of.finish()
    line.end()


GATHER_COPIES = 13


def rms_normed(values, gain):
    return values * lax.rsqrt(jnp.mean(values * values, -1, keepdims=True) + EPS) * gain


class Moves:
    def __init__(self, sems):
        self.sems, self.count, self.open = sems, 0, []

    def start(self, src, dst):
        one = pltpu.make_async_copy(src, dst, self.sems.at[self.count])
        self.count += 1
        one.start()
        return one

    def later(self, src, dst):
        self.open.append(self.start(src, dst))

    def finish(self):
        for one in self.open:
            one.wait()


def gather_scratch(rows, width, moves):
    return [
        pltpu.VMEM((8 * rows, width), bf16),
        pltpu.SemaphoreType.DMA((GATHER_COPIES,)),
        pltpu.SemaphoreType.DMA((GATHER_COPIES,)),
        pltpu.SemaphoreType.DMA((moves,)),
    ]


def own_rows(rows):
    return pl.ds(pl.multiple_of(other(0, 0, 0) * rows, rows), rows)


def send_columns(pieces, sends, recvs, moves):
    copies = []
    for which, (rows_ref, width, there) in enumerate(pieces):
        for number, flip in enumerate(EVERYONE):
            target = other(*flip)
            cols = pl.ds(pl.multiple_of(target * width, width), width)
            one = pltpu.make_async_remote_copy(
                src_ref=rows_ref.at[:, cols], dst_ref=there,
                send_sem=sends.at[which, number], recv_sem=recvs.at[which, number],
                device_id={"grp": target}, device_id_type=MESH,
            )
            one.start()
            copies.append(one)
        mine = pl.ds(pl.multiple_of(other(0, 0, 0) * width, width), width)
        moves.later(rows_ref.at[:, mine], there)
    return copies


def gather_normed_kernel(ins, outs, scratch, line):
    x_ref, gain_ref = ins[:2]
    weights = ins[2:]
    all_ref, cols_ref = outs
    held, sends, recvs, sems, col_sends, col_recvs = scratch
    rows = x_ref.shape[0]
    moves = Moves(sems)

    def fill():
        held[own_rows(rows), :] = rms_normed(x_ref[...].astype(f32), gain_ref[...]).astype(bf16)

    greet_group(line, EVERYONE, fill)
    col_copies = []

    def send_weights():
        pieces, low = [], 0
        tall = weights[0].shape[0]
        there = pl.ds(pl.multiple_of(other(0, 0, 0) * tall, tall), tall)
        for weight in weights:
            width = weight.shape[1] // 8
            pieces.append((weight, width, cols_ref.at[there, low : low + width]))
            low += width
        col_copies.extend(send_columns(pieces, col_sends, col_recvs, moves))

    def on_chip(*chip):
        where = chip_rows(*chip, rows)
        moves.later(held.at[where, :], all_ref.at[where, :])

    gather_rows(rows, held, sends, recvs, on_chip, line, send_weights)
    for one in col_copies:
        one.wait()
    moves.finish()


def gather_normed(x, gain, weights, **line):
    rows, width = x.shape
    deep = sum(weight.shape[1] for weight in weights) // 8
    return run(
        gather_normed_kernel,
        [(x, VMEM), (gain, VMEM)] + [(weight, ANY) for weight in weights],
        [
            (jax.ShapeDtypeStruct((8 * rows, width), bf16), ANY),
            (jax.ShapeDtypeStruct((8 * weights[0].shape[0], deep), bf16), ANY),
        ],
        gather_scratch(rows, width, 4 + len(weights))
        + [pltpu.SemaphoreType.DMA((len(weights), 7))] * 2,
        line.pop("number"),
        (0, 150 * rows * width * 2, 0),
        **line,
    )


def columns_kernel(rows_here, ins, outs, scratch, line):
    (cols_ref,) = outs
    sends, recvs, sems = scratch
    moves = Moves(sems)
    barrier = pltpu.get_barrier_semaphore()
    for flip in EVERYONE:
        pl.semaphore_signal(barrier, inc=1, device_id={"grp": other(*flip)}, device_id_type=MESH)
    pl.semaphore_wait(barrier, 7)
    first = pl.multiple_of(lax.axis_index("rep") * rows_here, rows_here)
    me = other(0, 0, 0)
    pieces, low = [], 0
    for weight in ins:
        width = weight.shape[1] // 8
        pieces.append(
            (weight.at[pl.ds(first, rows_here), :], width, cols_ref.at[me, :, low : low + width])
        )
        low += width
    for one in send_columns(pieces, sends, recvs, moves):
        one.wait()
    moves.finish()


def columns_of_some(weights, rows_here, number):
    deep = sum(weight.shape[1] for weight in weights) // 8
    return run(
        functools.partial(columns_kernel, rows_here),
        [(weight, ANY) for weight in weights],
        [(jax.ShapeDtypeStruct((8, rows_here, deep), bf16), ANY)],
        [pltpu.SemaphoreType.DMA((len(weights), 7))] * 2
        + [pltpu.SemaphoreType.DMA((len(weights),))],
        number, (0, 50 * 8 * rows_here * deep, 0),
    )[0]


def feed_forward_kernel(tile, ins, outs, scratch, line):
    mid_ref, gain_ref, grad_ref, spread_ref, rest_ref, w_down_ref = ins
    all_ref, hidden_ref, whole_ref, grad_gate_up_ref, down_ref = outs
    held, grads_held, sends, recvs, grad_sends, grad_recvs, sems = scratch[:7]
    weight, w_down, hidden, up_part, gate_part, grads, down = scratch[7:]
    rows = mid_ref.shape[0]
    inner = hidden.shape[1]
    moves = Moves(sems)
    planes, _, tall, _ = spread_ref.shape
    loads = [
        moves.start(spread_ref.at[z], weight.at[:, z * tall : (z + 1) * tall, :])
        for z in range(planes)
    ]
    loads.append(moves.start(rest_ref, weight.at[:, planes * tall :, :]))
    down_load = moves.start(w_down_ref, w_down)

    def fill():
        held[own_rows(rows), :] = rms_normed(mid_ref[...], gain_ref[...]).astype(bf16)
        grads_held[own_rows(rows), :] = grad_ref[...]

    greet_group(line, between=fill)
    first = Gather(rows, held, sends, recvs)
    second = Gather(rows, grads_held, grad_sends, grad_recvs)
    stored = []

    def forward(*chip):
        where = chip_rows(*chip, rows)
        moves.later(held.at[where, :], all_ref.at[where, :])

        def column(t, _):
            cols = pl.ds(pl.multiple_of(t * tile, tile), tile)
            up_cols = pl.ds(pl.multiple_of(inner + t * tile, tile), tile)
            lhs = held[where, :]
            gate = matmul_f32(lhs, weight[:, :, cols].reshape(-1, tile))
            up = matmul_f32(lhs, weight[:, :, up_cols].reshape(-1, tile))
            sigma = 1.0 / (1.0 + jnp.exp(-gate))
            swish = gate * sigma
            hidden[where, cols] = (swish * up).astype(bf16)
            up_part[where, cols] = swish.astype(bf16)
            gate_part[where, cols] = (up * sigma * (1.0 + gate * (1.0 - sigma))).astype(bf16)
            return 0

        lax.fori_loop(0, inner // tile, column, 0)
        moves.later(hidden.at[where, :], hidden_ref.at[where, :])

    def backward(*chip):
        where = chip_rows(*chip, rows)
        slot = len(stored) % 2
        if len(stored) >= 2:
            stored[len(stored) - 2].wait()

        def column(t, _):
            cols = pl.ds(pl.multiple_of(t * tile, tile), tile)
            up_cols = pl.ds(pl.multiple_of(inner + t * tile, tile), tile)
            incoming = grads_held[where, :]
            grad_hidden = against_rows(incoming, w_down[cols, :])
            grads[slot, :, cols] = (grad_hidden * gate_part[where, cols].astype(f32)).astype(bf16)
            grads[slot, :, up_cols] = (grad_hidden * up_part[where, cols].astype(f32)).astype(bf16)
            term = over_tokens(hidden[where, cols], incoming)
            if chip == SIBLING:
                down[cols, :] = term
            elif chip == ACROSS:
                weight[t] = (down[cols, :] + term).astype(bf16)
            else:
                down[cols, :] += term
            return 0

        lax.fori_loop(0, inner // tile, column, 0)
        stored.append(moves.start(grads.at[slot], grad_gate_up_ref.at[where, :]))

    first.send_own()
    for one in loads:
        one.wait()
    whole = moves.start(weight, whole_ref)
    first.sibling()
    forward(*SIBLING)
    first.relay()
    first.pass_second()
    second.send_own()
    first.along_x()
    forward(*ALONG_X)
    first.pass_across()
    first.along_y()
    forward(*ALONG_Y)
    second.relay()
    first.across()
    forward(*ACROSS)
    down_load.wait()
    second.sibling()
    backward(*SIBLING)
    second.pass_second()
    second.along_x()
    backward(*ALONG_X)
    second.pass_across()
    second.along_y()
    backward(*ALONG_Y)
    second.across()
    whole.wait()
    backward(*ACROSS)
    moves.later(weight.at[: inner // tile], down_ref)
    first.finish()
    second.finish()
    for one in stored[-2:]:
        one.wait()
    moves.finish()


def feed_forward(mid, gain, grad, spread, rest, w_down, **line):
    rows, width = mid.shape
    inner = w_down.shape[0]
    weight = (8, width // 8, 2 * inner)
    return run(
        functools.partial(feed_forward_kernel, weight[1]),
        [(mid, VMEM), (gain, VMEM), (grad, VMEM), (spread, ANY), (rest, ANY), (w_down, ANY)],
        [
            (jax.ShapeDtypeStruct((8 * rows, width), bf16), ANY),
            (jax.ShapeDtypeStruct((8 * rows, inner), bf16), ANY),
            (jax.ShapeDtypeStruct(weight, bf16), ANY),
            (jax.ShapeDtypeStruct((8 * rows, 2 * inner), bf16), ANY),
            (jax.ShapeDtypeStruct((inner // weight[1], weight[1], width), bf16), ANY),
        ],
        [pltpu.VMEM((8 * rows, width), bf16)] * 2
        + [pltpu.SemaphoreType.DMA((GATHER_COPIES,))] * 4
        + [pltpu.SemaphoreType.DMA((20,))]
        + [pltpu.VMEM(weight, bf16), pltpu.VMEM(w_down.shape, bf16)]
        + [pltpu.VMEM((8 * rows, inner), bf16)] * 3
        + [
            pltpu.VMEM((2, 2 * rows, 2 * inner), bf16),
            pltpu.VMEM(w_down.shape, f32),
        ],
        line.pop("number"),
        (64 * rows * width * inner, 300 * rows * width * 2, 8 * rows * inner),
        vmem=63,
        **line,
    )


def attended_back_kernel(ins, outs, scratch, line):
    grad_ref, w_ref, attended_ref = ins
    grad_attended_ref, out_term_ref = outs
    held, sends, recvs, sems, total = scratch
    rows = grad_ref.shape[0]
    moves = Moves(sems)
    greet_group(line)
    line.start()
    held[own_rows(rows), :] = grad_ref[...].astype(bf16)

    def on_chip(*chip):
        where = chip_rows(*chip, rows)
        incoming = held[where, :]
        grad_attended_ref[where, :] = against_rows(incoming, w_ref[...]).astype(bf16)
        term = over_tokens(attended_ref[where, :], incoming)
        if chip == SIBLING:
            total[...] = term
        elif chip == ACROSS:
            out_term_ref[...] = (total[...] + term).astype(bf16)
        else:
            total[...] += term

    gather_rows(rows, held, sends, recvs, on_chip, line)
    moves.finish()


def attended_back(grad, w_out, attended, **line):
    rows, width = grad.shape
    return run(
        attended_back_kernel,
        [(array, VMEM) for array in (grad, w_out, attended)],
        [
            (jax.ShapeDtypeStruct(attended.shape, bf16), VMEM),
            (jax.ShapeDtypeStruct(w_out.shape, bf16), VMEM),
        ],
        gather_scratch(rows, width, 1) + [pltpu.VMEM(w_out.shape, f32)],
        line.pop("number"),
        (32 * rows * width * w_out.shape[0], 150 * rows * width * 2, 0),
        **line,
    )


class WeightTerm:
    def __init__(self, rows_ref, columns_ref, term_ref, scratch):
        self.rows_ref, self.columns_ref, self.term_ref = rows_ref, columns_ref, term_ref
        self.loaded, self.flipped, self.ready, self.sems = scratch
        self.tile = self.loaded.shape[2]
        for number in (0, 1):
            self.load(number).start()

    def load(self, number):
        cols = slice(number * self.tile, (number + 1) * self.tile)
        return pltpu.make_async_copy(
            self.rows_ref.at[:, cols], self.loaded.at[number % 2], self.sems.at[0, number % 2]
        )

    def store(self, number):
        return pltpu.make_async_copy(
            self.ready.at[number % 2], self.term_ref.at[number], self.sems.at[1, number % 2]
        )

    def work(self, numbers):
        for number in numbers:
            at = number % 2
            self.load(number).wait()
            if number >= 2:
                self.store(number - 2).wait()
            width = self.columns_ref.shape[1]
            step = min(256, width)
            self.flipped[...] = self.loaded[at].T

            def column(t, _):
                cols = pl.ds(pl.multiple_of(t * step, step), step)
                term = matmul_f32(self.flipped[...], self.columns_ref[:, cols])
                self.ready[at, :, cols] = term.astype(bf16)
                return 0

            lax.fori_loop(0, width // step, column, 0)
            self.store(number).start()
            if number + 2 < 8:
                self.load(number + 2).start()

    def finish(self):
        for number in (6, 7):
            self.store(number).wait()


UNITS = (
    (ACROSS, 0), (ACROSS, 1), (ALONG_X, 0), (ALONG_Y, 1), (ALONG_X, 1), (ALONG_Y, 0),
    (SIBLING, 0), (SIBLING, 1),
)


def scatter_kernel(turned, extra, after, steps, ins, outs, scratch, line):
    out_ref = outs[0] if after == "base" else scratch[-4]
    finals = ins[len(ins) - {"base": 1, "cast": 1, "back": 3}[after] :]
    part, to_s, from_s, to_link, relay, last, sends, recvs = scratch[:8]
    a_ref, b_ref, load_sems = scratch[-3:]
    rows, width = out_ref.shape
    half = width // 2
    _, _, core = place_in_group()
    loading = {}

    def load(name, src, dst):
        loading[name] = pltpu.make_async_copy(src, dst, load_sems.at[len(loading)])
        loading[name].start()

    def load_weight(h):
        where = (slice(h * half, (h + 1) * half), slice(None))
        where = where if turned else where[::-1]
        load(h, ins[1].at[where], b_ref.at[where])

    def load_rows(chip):
        where = chip_rows(*chip, rows)
        load(chip, ins[0].at[where, :], a_ref.at[where, :])

    load_weight(0)
    load_rows(ACROSS)
    load_weight(1)
    for chip in (ALONG_X, ALONG_Y, SIBLING):
        load_rows(chip)
    greet_group(line)
    line.start()
    if extra:
        columns_ref = a_ref
        if extra == "loaded":
            columns_ref = scratch[12]
            load("columns", ins[3], columns_ref)
        term = WeightTerm(ins[2], columns_ref, outs[-1], scratch[8:12])
    own_at = pl.multiple_of(core * rows, rows)
    other_at = pl.multiple_of((1 - core) * rows, rows)
    to_sib, to_x, to_y = (0, 0, 1), (0, 1, 0), (1, 0, 0)
    started = []

    def ready(*names):
        for name in names:
            if name in loading:
                loading.pop(name).wait()
                loading[name, "done"] = None

    def send(number, src, dst, target):
        one = pltpu.make_async_remote_copy(
            src_ref=src, dst_ref=dst, send_sem=sends.at[number], recv_sem=recvs.at[number],
            device_id={"grp": other(*target)}, device_id_type=MESH,
        )
        one.start()
        started.append(one)

    def landed(number, where):
        pltpu.make_async_remote_copy(
            src_ref=where, dst_ref=where, send_sem=sends.at[number], recv_sem=recvs.at[number],
            device_id={"grp": other(0, 0, 1)}, device_id_type=MESH,
        ).wait_recv()

    def make(n):
        chip, h = UNITS[n]
        ready(h, chip)
        lhs = a_ref[chip_rows(*chip, rows), :]
        cols = slice(h * half, (h + 1) * half)
        if turned:
            part[n % 2] = against_rows(lhs, b_ref[cols, :])
        else:
            part[n % 2] = matmul_f32(lhs, b_ref[:, cols])
        to_s[n] = part[n % 2, pl.ds(other_at, rows), :].astype(bf16)
        send(n, to_s.at[n], from_s.at[n], to_sib)

    def own(n):
        landed(n, from_s.at[n])
        return part[n % 2, pl.ds(own_at, rows), :] + from_s[n].astype(f32)

    def finish(n):
        _, h = UNITS[n]
        if n < 2:
            to_link[n] = own(n).astype(bf16)
            send(8 + n, to_link.at[n], relay.at[n], (to_x, to_y)[n])
        elif n < 4:
            to_link[n] = own(n).astype(bf16)
            send(8 + n, to_link.at[n], last.at[(None, None, 0, 3)[n]], (to_x, to_y)[n - 2])
        elif n < 6:
            total = own(n)
            landed(8 + h, relay.at[h])
            to_link[n] = (total + relay[h].astype(f32)).astype(bf16)
            send(8 + n, to_link.at[n], last.at[(1, 2)[n - 4]], (to_x, to_y)[n - 4])
        else:
            cols = slice(h * half, (h + 1) * half)
            if after == "back":
                out_ref[:, cols] = own(n)
            else:
                out_ref[:, cols] = own(n) + finals[0][:, cols].astype(f32)
        line.step(steps.get(n, 0))

    def work(numbers, point):
        if extra:
            ready("columns")
            if columns_ref is a_ref:
                ready(*(chip for chip, _ in UNITS))
            term.work(numbers)
        line.step(steps.get(point, 0))

    make(0)
    make(1)
    finish(0)
    make(2)
    finish(1)
    make(3)
    finish(2)
    make(4)
    finish(3)
    make(5)
    work((0, 1), "early")
    finish(4)
    make(6)
    finish(5)
    make(7)
    finish(6)
    finish(7)
    work((2, 3), "late")
    work((4, 5), "later")
    work((6, 7), "latest")
    for number, slot, h in ((10, 0, 0), (11, 3, 1), (12, 1, 1), (13, 2, 0)):
        cols = slice(h * half, (h + 1) * half)
        landed(number, last.at[slot])
        out_ref[:, cols] += last[slot].astype(f32)
        line.step(steps.get(number, 0))
    if after == "cast":
        outs[0][...] = out_ref[...].astype(outs[0].dtype)
    if after == "back":
        upstream_ref, rows_ref, gain_ref = finals
        some = min(64, rows)

        def norm_rows(number, gain_term):
            at = pl.ds(pl.multiple_of(number * some, some), some)
            values, incoming = rows_ref[at, :].astype(f32), out_ref[at, :]
            inv = lax.rsqrt(jnp.mean(values * values, -1, keepdims=True) + EPS)
            grad, gain_part = norm_back(
                upstream_ref[at, :].astype(f32), incoming, values * inv, inv, gain_ref[...]
            )
            outs[0][at, :] = grad.astype(outs[0].dtype)
            return gain_term + gain_part[None, :]

        outs[1][...] = lax.fori_loop(0, rows // some, norm_rows, jnp.zeros((1, width), f32))
    for one in started:
        one.wait_send()
    if extra:
        term.finish()
    line.end()


def product_scattered(
    a, b, turned, extra=None, base=None, back=None, dtype=f32, steps=None, **line
):
    length, depth = a.shape
    width = b.shape[0] if turned else b.shape[1]
    rows = length // 8
    ins = [(a, ANY), (b, ANY)]
    outs = [(jax.ShapeDtypeStruct((rows, width), dtype), VMEM)]
    after = "back" if back else "base" if dtype == f32 else "cast"
    if back:
        outs.append((jax.ShapeDtypeStruct((1, width), f32), VMEM))
    piece = (rows, width // 2)
    scratch = [
        pltpu.VMEM((2, 2 * rows, width // 2), f32),
        pltpu.VMEM((8,) + piece, bf16),
        pltpu.VMEM((8,) + piece, bf16),
        pltpu.VMEM((6,) + piece, bf16),
        pltpu.VMEM((2,) + piece, bf16),
        pltpu.VMEM((4,) + piece, bf16),
        pltpu.SemaphoreType.DMA((14,)),
        pltpu.SemaphoreType.DMA((14,)),
    ]
    flops, kind = 2 * length * depth * width, None
    if extra:
        first, second = extra
        kind = "own" if second is None else "loaded"
        ins.append((first, ANY))
        columns = a if second is None else second
        tall = first.shape[1] // 8
        outs.append((jax.ShapeDtypeStruct((8, tall, columns.shape[1]), bf16), ANY))
        scratch += [
            pltpu.VMEM((2, length, tall), bf16),
            pltpu.VMEM((tall, length), bf16),
            pltpu.VMEM((2, tall, columns.shape[1]), bf16),
            pltpu.SemaphoreType.DMA((2, 2)),
        ]
        if second is not None:
            ins.append((second, ANY))
            scratch.append(pltpu.VMEM(second.shape, bf16))
        flops += 2 * length * first.shape[1] * columns.shape[1]
    ins += [(array, VMEM) for array in (back or (base,))]
    if after != "base":
        scratch.append(pltpu.VMEM((rows, width), f32))
    scratch += [
        pltpu.VMEM(a.shape, bf16), pltpu.VMEM(b.shape, bf16), pltpu.SemaphoreType.DMA((7,))
    ]
    return run(
        functools.partial(scatter_kernel, turned, kind, after, steps or {}), ins, outs, scratch,
        line.pop("number"), (flops, 150 * rows * width * 2, 0), vmem=61, **line,
    )


def tail_kernel(ready, later, ins, outs, scratch, line):
    qkv_ref, gains_ref = ins[:2]
    chunk_refs = dict(zip(ready, ins[2:]))
    gate_ref, up_ref, qkv_rows_ref, gains_out_ref = outs
    from_group, mine, from_rep, sends, recvs, chunk_sems, local = scratch
    me, rank = other(0, 0, 0), lax.axis_index("rep")
    inner = gate_ref.shape[1] // 8
    part = qkv_ref.shape[-1]
    high = line.outs[later[0]].shape[1]
    barrier = pltpu.get_barrier_semaphore()
    for flip in range(1, 4):
        pl.semaphore_signal(
            barrier, inc=1, device_id={"rep": (rank + flip) % 4}, device_id_type=MESH
        )
    for flip in EVERYONE:
        pl.semaphore_signal(barrier, inc=1, device_id={"grp": other(*flip)}, device_id_type=MESH)
    pl.semaphore_wait(barrier, 10)
    waits, moves = [], Moves(local)
    line.refs["qkv"] = qkv_rows_ref

    def send(kind, number, src, dst, device):
        return pltpu.make_async_remote_copy(
            src_ref=src, dst_ref=dst, send_sem=sends.at[kind, number],
            recv_sem=recvs.at[kind, number], device_id=device, device_id_type=MESH,
        )

    own_qkv = qkv_rows_ref.at[me // 4, :, :, pl.ds(pl.multiple_of((me % 4) * part, part), part)]
    qkv_copies, gain_copies = [], []
    for number, flip in enumerate(EVERYONE):
        target = other(*flip)
        qkv_copies.append(send(0, number, qkv_ref.at[target], own_qkv, {"grp": target}))
        qkv_copies[-1].start()
    moves.later(qkv_ref.at[me], own_qkv)
    line.start()
    for number, flip in enumerate(EVERYONE):
        target = other(*flip)
        gain_copies.append(
            send(1, number, gains_ref.at[target], from_group.at[me], {"grp": target})
        )
        gain_copies[-1].start()
    from_group[me] = gains_ref[me]

    def spread(chunk):
        src = chunk_refs[chunk] if chunk in chunk_refs else line.outs[chunk]
        number = chunk - DOWN
        rows = slice(number // 2 * high, (number // 2 + 1) * high)
        dst = (gate_ref, up_ref)[number % 2]
        there = dst.at[rows, pl.ds(pl.multiple_of(me * inner, inner), inner)]
        for flip in EVERYONE:
            target = other(*flip)
            pltpu.make_async_remote_copy(
                src_ref=src.at[target], dst_ref=there, send_sem=chunk_sems.at[0, number],
                recv_sem=chunk_sems.at[1, number], device_id={"grp": target}, device_id_type=MESH,
            ).start()
        moves.later(src.at[me], there)
        seven = dst.at[rows, : 7 * inner]
        waits.append(
            pltpu.make_async_remote_copy(
                src_ref=seven, dst_ref=seven, send_sem=chunk_sems.at[0, number],
                recv_sem=chunk_sems.at[1, number], device_id={"grp": other(0, 0, 1)},
                device_id_type=MESH,
            )
        )

    for chunk in ready:
        spread(chunk)
    for one in gain_copies:
        one.wait()
    mine[rank] = sum(from_group[g] for g in range(8))
    rep_copies = []
    for step in range(1, 4):
        target = (rank + step) % 4
        rep_copies.append(
            send(2, step, mine.at[rank], from_rep.at[step], {"rep": target})
        )
        rep_copies[-1].start()
    for step, one in zip(range(1, 4), rep_copies):
        one.wait()
        mine[(rank + 4 - step) % 4] = from_rep[step]
    gains_out_ref[...] = (mine[0] + mine[1]) + (mine[2] + mine[3])
    for settled in range(line.ticks - LAG):
        if line.first + settled + LAG == CHUNKS - QKV:
            for one in qkv_copies:
                one.wait()
            moves.open.pop(0).wait()
        line.step()
        chunk = line.first + settled - 2 * LAG
        if chunk in later:
            spread(chunk)
    line.end()
    for one in waits:
        one.wait_send()
        one.wait_recv()
    moves.finish()


def tail(qkv_term, gains, chunks, inner, number, sums, ticks, arrays, picks):
    first = sums.tick
    ready = sorted(chunks)
    later = [c for c in line_slots(first, ticks) if c < DOWN + GATE_UP]
    _, high, width = sums.shape
    wide = jax.ShapeDtypeStruct((GATE_UP // 2 * high, 8 * inner), bf16)
    moved = jax.ShapeDtypeStruct((2, 8, 2 * high, 2 * width), bf16)
    picks = dict(picks)
    for n in range(QKV):
        where = (
            n // 4, slice(None), slice(n // 2 % 2 * high, (n // 2 % 2 + 1) * high),
            slice(n % 2 * width, (n % 2 + 1) * width),
        )
        picks[CHUNKS - QKV + n] = ("qkv", lambda ref, where=where: ref.at[where])
    return run(
        functools.partial(tail_kernel, ready, later),
        [(qkv_term, ANY), (gains, VMEM)] + [(chunks[c], ANY) for c in ready],
        [(wide, ANY), (wide, ANY), (moved, ANY), (jax.ShapeDtypeStruct(gains.shape[1:], f32), VMEM)],
        [
            pltpu.VMEM(gains.shape, f32),
            pltpu.VMEM((4,) + gains.shape[1:], f32),
            pltpu.VMEM((4,) + gains.shape[1:], f32),
            pltpu.SemaphoreType.DMA((3, 7)),
            pltpu.SemaphoreType.DMA((3, 7)),
            pltpu.SemaphoreType.DMA((2, GATE_UP)),
            pltpu.SemaphoreType.DMA((1 + GATE_UP,)),
        ],
        number, (0, 200 * 8 * high * width * 2, 0), sums=sums, ticks=ticks, arrays=arrays, picks=picks,
    )


def finish_kernel(heads, *refs):
    chunks, rest = refs[: DOWN + OUT + QKV], refs[DOWN + OUT + QKV :]
    gate_rows, up_rows = rest[:2]
    query, key, value, out, gate, up, down = rest[2:9]
    low, wide, load_sems, store_sems = rest[9:]
    _, high, width = chunks[0].shape
    depth = low.shape[0]

    def half(number):
        return slice(number * high, (number + 1) * high)

    def side(number):
        return slice(number * width, (number + 1) * width)

    jobs = []
    for n, ref in enumerate(chunks[:DOWN]):
        jobs.append((ref, [(slice(0, width), down.at[n // 2, :, :, side(n % 2)])]))
    for ref, into in ((gate_rows, gate), (up_rows, up)):
        for low_col in range(0, ref.shape[2], low.shape[3]):
            for number in (0, 1):
                where = (slice(None), half(number), slice(low_col, low_col + low.shape[3]))
                jobs.append((ref.at[where], [(slice(0, low.shape[3]), into.at[where])]))
    for n, ref in enumerate(chunks[DOWN : DOWN + OUT]):
        jobs.append((ref, [(slice(0, width), out.at[:, half(n // 2), side(n % 2)])]))
    part = (heads + 2) * HD
    for n, ref in enumerate(chunks[DOWN + OUT :]):
        stores = []
        for place in range(width // part):
            at, device = place * part, (n // 4 * 2 + n % 2) * (width // part) + place
            for into, first, size in (
                (query, 0, heads * HD), (key, heads * HD, HD), (value, (heads + 1) * HD, HD)
            ):
                there = into.at[:, half(n // 2 % 2), device * size : (device + 1) * size]
                stores.append((slice(at + first, at + first + size), there))
        jobs.append((ref, stores))

    def load(number):
        at, ref = number % depth, jobs[number][0]
        return pltpu.make_async_copy(ref, low.at[at, :, :, : ref.shape[2]], load_sems.at[at])

    def stores(number):
        at = number % depth
        return [
            pltpu.make_async_copy(wide.at[at, :, :, cols], into, store_sems.at[at, which])
            for which, (cols, into) in enumerate(jobs[number][1])
        ]

    for number in range(depth - 1):
        load(number).start()
    for number in range(len(jobs)):
        if number + depth - 1 < len(jobs):
            load(number + depth - 1).start()
        load(number).wait()
        if number >= depth:
            for one in stores(number - depth):
                one.wait()

        def cast(g, _, at=number % depth, cols=slice(0, jobs[number][0].shape[2])):
            wide[at, g, :, cols] = low[at, g, :, cols].astype(f32)
            return 0

        lax.fori_loop(0, low.shape[1], cast, 0)
        for one in stores(number):
            one.start()
    for number in range(len(jobs) - depth, len(jobs)):
        for one in stores(number):
            one.wait()


def finish(chunks, gate_rows, up_rows, heads):
    eight, high, width = chunks[0].shape
    width = 2 * width
    rows, wide = gate_rows.shape

    def split(columns):
        return jax.ShapeDtypeStruct((eight, rows // eight, columns), f32)

    shapes = [split(columns) for columns in (8 * heads * HD, 8 * HD, 8 * HD, width, wide, wide)]
    shapes.append(jax.ShapeDtypeStruct((DOWN // 2, eight, high, width), f32))
    depth = 6
    results = pl.pallas_call(
        functools.partial(finish_kernel, heads),
        out_shape=tuple(shapes),
        in_specs=[pl.BlockSpec(memory_space=pl.ANY)] * (len(chunks) + 2),
        out_specs=tuple([pl.BlockSpec(memory_space=pl.ANY)] * 7),
        scratch_shapes=[
            pltpu.VMEM((depth, eight, high, width), bf16),
            pltpu.VMEM((depth, eight, high, width), f32),
            pltpu.SemaphoreType.DMA((depth,)),
            pltpu.SemaphoreType.DMA((depth, 12)),
        ],
        compiler_params=pltpu.CompilerParams(vmem_limit_bytes=60 * 2**20),
        cost_estimate=pl.CostEstimate(
            flops=0, bytes_accessed=3 * CHUNKS * eight * high * width, transcendentals=0
        ),
    )(
        *chunks, gate_rows.reshape(eight, rows // eight, wide),
        up_rows.reshape(eight, rows // eight, wide),
    )
    flat = [result.reshape(rows, -1) for result in results[:6]]
    return flat + [results[6].reshape(-1, width)]


def sum_over_sequences(term):
    return lax.psum(term, "rep").astype(f32)


def on_device(
    layer_input,
    cotangent,
    cut_order,
    piece_ids,
    w_query,
    w_key,
    w_value,
    w_out,
    w_gate,
    w_up,
    w_down,
    gain_attn,
    gain_ffn,
):
    groups = lax.axis_size("grp")
    reps = lax.axis_size("rep")
    own_index = lax.axis_index("grp")
    _, local_rows, model_width = layer_input.shape
    length = piece_ids.shape[1]
    rows_here = w_query.shape[0]
    q_width = w_query.shape[1]
    kv_heads = w_key.shape[1] // HD
    heads = q_width // HD // groups
    copies = groups // kv_heads
    hidden_here = w_down.shape[0]
    cosine, sine = turn_tables(length)

    near = groups == 8 and reps == 4 and copies == 1 and 2 * hidden_here == model_width

    def gather(rows):
        return lax.all_gather(rows, "grp", axis=0, tiled=True)

    def scatter(first, second, turned):
        term = against_rows(first, second) if turned else matmul_f32(first, second)
        return lax.psum_scatter(
            term.astype(bf16), "grp", scatter_dimension=0, tiled=True
        ).astype(f32)

    def to_columns(parts):
        return lax.all_to_all(parts, "grp", 1, 0, tiled=True).reshape(-1, parts.shape[-1])

    def per_group(weight):
        return weight.reshape(rows_here, groups, -1)

    def per_kv_head(weight):
        return jnp.repeat(weight.reshape(rows_here, kv_heads, HD), copies, axis=1)

    x_rows = layer_input.reshape(local_rows, model_width)
    x_flat = x_rows.astype(f32)
    inv_one = lax.rsqrt(jnp.mean(x_flat * x_flat, -1, keepdims=True) + EPS)
    unit_one = x_flat * inv_one
    attn_gain, ffn_gain = gain_attn.reshape(1, -1), gain_ffn.reshape(1, -1)
    if near:
        share = rows_here // (4 * reps) * 3
        spread = columns_of_some((w_gate, w_up), share, 11)
        x_first, spread = lax.optimization_barrier((x_rows, spread))
        spread = lax.all_gather(spread, "rep", axis=0)
        normed_one, cols_qkv = gather_normed(
            x_first, attn_gain, (w_query, w_key, w_value), number=1
        )
        last_gate, last_up, normed_one = lax.optimization_barrier(
            (w_gate[reps * share :], w_up[reps * share :], normed_one)
        )
        rest = to_columns(
            jnp.concatenate(
                [part.reshape(rows_here - reps * share, groups, -1) for part in (last_gate, last_up)],
                -1,
            )
        ).reshape(groups, rows_here - reps * share, -1)
    else:
        normed_one = gather(rms_normed(x_flat, attn_gain).astype(bf16))
        cols_qkv = to_columns(
            jnp.concatenate([per_group(w_query), per_kv_head(w_key), per_kv_head(w_value)], -1)
        )
        cols_gate_up = to_columns(jnp.concatenate([per_group(w_gate), per_group(w_up)], -1))
    attended, query, key, value, lse, attended_placed = attend(
        cut_order, normed_one, cols_qkv, cosine, sine, piece_ids, heads
    )
    if near:
        mid = product_scattered(attended, w_out, False, base=x_rows, number=2)[0]
    else:
        mid = x_flat + scatter(attended, w_out, False)
    grad_out = cotangent.reshape(local_rows, model_width)

    def back_through_attention(grad_attended, **line):
        return attend_back(
            cut_order, grad_attended, attended_placed, query, key, value, lse, cosine, sine,
            piece_ids, heads, **line,
        )

    q_here = heads * HD
    if near:
        normed_two, hidden, cols_gate_up, grad_gate_up, down_term = feed_forward(
            mid, ffn_gain, grad_out, spread, rest, w_down, number=3
        )
        cols_gate_up = cols_gate_up.reshape(model_width, -1)
        high, half_width = 2 * rows_here // GATE_UP, model_width // 2
        sums = Sums((8, high, half_width))
        terms = {"down": down_term.reshape(DOWN // 2, 8, high, model_width)}

        def pick_whole(n):
            return "down", lambda ref: ref.at[n // 2, :, :, n % 2 * half_width : (n % 2 + 1) * half_width]

        def pick_rows(name, n):
            rows, side = n // 2 * high, n % 2 * half_width
            return name, lambda ref: ref.at[:, rows : rows + high, side : side + half_width]

        picks = [pick_whole(n) for n in range(DOWN)]
        picks += [pick_rows("gate_up", n) for n in range(GATE_UP)]
        picks += [pick_rows("out", n) for n in range(OUT)]

        def line(number, ticks):
            names = sorted(
                {picks[t][0] for t in range(sums.tick, sums.tick + ticks) if t < len(picks)}
            )
            return dict(
                number=number, ticks=ticks, sums=sums, picks=dict(enumerate(picks)),
                arrays=[(name, terms[name]) for name in names],
            )

        result, terms["gate_up"] = product_scattered(
            hidden, w_down, False, extra=(normed_two, grad_gate_up), base=mid, dtype=bf16,
            steps={1: 1, 3: 1, "early": 1, 7: 1, "late": 1, "later": 1, "latest": 1}, **line(5, 9),
        )
        grad_mid, gain_ffn_term = product_scattered(
            grad_gate_up, cols_gate_up, True, back=(grad_out, mid, ffn_gain),
            steps={0: 1, 2: 1, 3: 1, 4: 1, 5: 1, 7: 1, 12: 1}, **line(6, 10),
        )
        grad_attended, out_term = attended_back(grad_mid, w_out, attended, **line(7, 8))
        terms["out"] = out_term.reshape(8, OUT // 2 * high, model_width)
        grad_qkv = back_through_attention(grad_attended, **line(8, 7))
        grad_x, gain_attn_term, qkv_term = product_scattered(
            grad_qkv, cols_qkv, True, extra=(normed_one, None), dtype=bf16,
            back=(grad_mid, x_rows, attn_gain),
            steps={3: 1, "early": 1, 5: 1, "late": 1, "latest": 1}, **line(9, 8),
        )
        gains = jnp.stack([gain_attn_term, gain_ffn_term]).reshape(2, groups, rows_here)
        gains = jnp.pad(jnp.moveaxis(gains, 0, 1), ((0, 0), (0, 6), (0, 0)))
        rest = line(10, CHUNKS + 2 * LAG - sums.tick)
        gate_rows, up_rows, qkv_rows, own_gains = tail(
            qkv_term.reshape(8, 8, 2 * high, -1), gains,
            {c: sums.done[c] for c in sums.done if c >= DOWN}, hidden_here, **rest,
        )
        straight = [n for n in range(CHUNKS) if n < DOWN or n >= DOWN + GATE_UP]
        weight_grads = finish([sums.done[n] for n in straight], gate_rows, up_rows, heads)
        shaped = tuple(rows.reshape(layer_input.shape) for rows in (result, grad_x))
        return shaped + tuple(weight_grads) + (own_gains[0], own_gains[1])

    unit_one = x_flat * inv_one
    inv_two = lax.rsqrt(jnp.mean(mid * mid, -1, keepdims=True) + EPS)
    unit_two = mid * inv_two
    normed_two = gather((unit_two * ffn_gain).astype(bf16))
    grad_all = gather(grad_out)
    gate_up = matmul_f32(normed_two, cols_gate_up)
    gate_proj, up_proj = gate_up[:, :hidden_here], gate_up[:, hidden_here:]
    sigmoid_gate = jax.nn.sigmoid(gate_proj)
    swish = gate_proj * sigmoid_gate
    hidden = (swish * up_proj).astype(bf16)
    gate_part = up_proj * sigmoid_gate * (1.0 + gate_proj * (1.0 - sigmoid_gate))
    down_term = over_tokens(hidden, grad_all).astype(bf16)
    grad_hidden = against_rows(grad_all, w_down)
    grad_gate_up = jnp.concatenate([grad_hidden * gate_part, grad_hidden * swish], 1).astype(bf16)
    grad_mid, gain_ffn_term = norm_back(
        grad_out.astype(f32), scatter(grad_gate_up, cols_gate_up, True), unit_two, inv_two, gain_ffn
    )
    grad_mid_low = gather(grad_mid.astype(bf16))
    grad_qkv = back_through_attention(against_rows(grad_mid_low, w_out).astype(bf16))
    grad_x, gain_attn_term = norm_back(
        grad_mid, scatter(grad_qkv, cols_qkv, True), unit_one, inv_one, gain_attn
    )

    def to_rows(term):
        return lax.all_to_all(
            term.astype(bf16).reshape(groups, rows_here, -1), "grp", 0, 0, tiled=True
        )

    def whole_rows(term):
        return jnp.moveaxis(term, 0, 1).reshape(rows_here, -1)

    def kv_rows(term):
        return jnp.sum(
            jnp.moveaxis(term, 0, 1).reshape(rows_here, kv_heads, copies, HD), 2
        ).reshape(rows_here, -1)

    gate_up_term = sum_over_sequences(to_rows(over_tokens(normed_two, grad_gate_up)))
    out_term = sum_over_sequences(over_tokens(attended, grad_mid_low).astype(bf16))
    qkv_term = sum_over_sequences(to_rows(over_tokens(normed_one, grad_qkv)))
    gain_total = lax.psum(jnp.stack([gain_attn_term, gain_ffn_term]), ("grp", "rep"))
    own_gains = lax.dynamic_slice_in_dim(gain_total, own_index * rows_here, rows_here, 1)
    return (
        (mid + scatter(hidden, w_down, False)).astype(bf16).reshape(layer_input.shape),
        grad_x.astype(bf16).reshape(layer_input.shape),
        whole_rows(qkv_term[..., :q_here]),
        kv_rows(qkv_term[..., q_here : q_here + HD]),
        kv_rows(qkv_term[..., q_here + HD :]),
        out_term,
        whole_rows(gate_up_term[..., :hidden_here]),
        whole_rows(gate_up_term[..., hidden_here:]),
        sum_over_sequences(down_term),
        own_gains[0],
        own_gains[1],
    )


def solution(mesh):
    tokens, table, rows, whole = P("rep", "grp", None), P("rep", None), P("grp", None), P()
    return jax.shard_map(
        on_device,
        mesh=mesh,
        in_specs=(tokens, tokens, table, table) + (rows,) * 7 + (whole,) * 2,
        out_specs=(tokens, tokens) + (rows,) * 7 + (P("grp"),) * 2,
        check_vma=False,
    )
```

```python
import functools

import jax
import jax.numpy as jnp
import numpy as np
from jax import lax
from jax.experimental import pallas as pl
from jax.experimental.pallas import tpu as pltpu
from jax.sharding import PartitionSpec as P

HD = 128
EPS = 1e-05
ROPE_BASE = 1000000.0
SCORE_SCALE = HD**-0.5
LOG2E = 1.4426950408889634
TO_EXP2 = SCORE_SCALE * LOG2E
NEG = -1e30

MESH = pl.DeviceIdType.MESH
f32 = jnp.float32
bf16 = jnp.bfloat16


def matmul_f32(first, second):
    return jnp.dot(first, second, preferred_element_type=f32)


def against_rows(first, second):
    return lax.dot_general(first, second, (((1,), (1,)), ((), ())), preferred_element_type=f32)


def over_tokens(first, second):
    return lax.dot_general(first, second, (((0,), (0,)), ((), ())), preferred_element_type=f32)


def turn_tables(length):
    half_size = HD // 2
    inverse = np.float32(ROPE_BASE) ** (-(np.arange(half_size, dtype=np.float32) * 2) / HD)
    angles = np.arange(length, dtype=np.float32)[:, None] * inverse.astype(np.float32)
    cosine, sine = np.cos(angles), np.sin(angles)
    tables = np.concatenate([cosine, cosine], -1), np.concatenate([-sine, sine], -1)
    return tuple(jnp.asarray(table.astype(np.float32)) for table in tables)


def norm_back(upstream, grad_normed, unit_rows, inv_root, gain):
    scaled = grad_normed * gain
    center_term = jnp.mean(scaled * unit_rows, -1, keepdims=True)
    return (
        upstream + inv_root * (scaled - unit_rows * center_term),
        jnp.sum(grad_normed * unit_rows, 0),
    )


def fold_lanes(values, op):
    out = values[:, :HD]
    for at in range(HD, values.shape[1], HD):
        out = op(out, values[:, at : at + HD])
    return out


def as_column(row):
    return jnp.broadcast_to(row, (HD, row.shape[1])).T[:, 0:1]


def as_row(column):
    return jnp.broadcast_to(column, (column.shape[0], HD)).T[0:1, :]


def attend_kernel(
    heads, cuts, block,
    order_ref, rows_hbm, weight_hbm, cos_ref, sin_ref, piece_ref,
    out_ref, q_ref, k_ref, v_ref, lse_ref, placed,
    scores, rows_ref, weight_ref, qkv_ref, sems,
):
    length = rows_ref.shape[0]
    cut = length // cuts
    blocks = length // block
    loads = [pltpu.make_async_copy(weight_hbm, weight_ref, sems.at[blocks])]
    for i in range(blocks):
        at = slice(i * block, (i + 1) * block)
        loads.append(pltpu.make_async_copy(rows_hbm.at[at, :], rows_ref.at[at, :], sems.at[i]))
    for load in loads:
        load.start()

    def place_cut(r, first):
        src = pl.ds(pl.multiple_of(r * cut, cut), cut)
        dst = pl.ds(pl.multiple_of(order_ref[0, first + r] * cut, cut), cut)
        cosine, sine = cos_ref[dst, :], sin_ref[dst, :]
        for h in range(heads + 1):
            part = qkv_ref[src, h * HD : (h + 1) * HD]
            turned = (part * cosine + pltpu.roll(part, HD // 2, 1) * sine).astype(bf16)
            if h < heads:
                q_ref[h, dst, :] = turned
            else:
                k_ref[dst, :] = turned
        v_ref[dst, :] = qkv_ref[src, (heads + 1) * HD :].astype(bf16)
        return first

    loads[0].wait()
    for i in range(blocks):
        loads[1 + i].wait()
        qkv_ref[...] = matmul_f32(rows_ref[i * block : (i + 1) * block, :], weight_ref[...])
        lax.fori_loop(0, block // cut, place_cut, i * (block // cut))

    def one_block(i, _):
        rows = pl.ds(pl.multiple_of(i * block, block), block)
        query = q_ref[:, rows, :].reshape(heads * block, HD)

        def score(j, high):
            cols = pl.ds(pl.multiple_of(j * block, block), block)
            tile = against_rows(query, k_ref[cols, :])
            scores[j] = tile
            return jnp.maximum(high, fold_lanes(tile, jnp.maximum))

        high = lax.fori_loop(0, i, score, jnp.full((heads * block, HD), NEG, f32))
        tile = against_rows(query, k_ref[rows, :])
        q_at = lax.broadcasted_iota(jnp.int32, (block, block), 0)
        k_at = lax.broadcasted_iota(jnp.int32, (block, block), 1)
        k_piece = piece_ref[0:1, rows].astype(f32)
        q_piece = as_column(k_piece)
        allowed = (k_at <= q_at) | ((q_piece != 0) & (q_piece == k_piece))
        tile = jnp.concatenate(
            [jnp.where(allowed, tile[h * block : (h + 1) * block], NEG) for h in range(heads)], 0
        )
        scores[i] = tile
        high = jnp.max(jnp.maximum(high, fold_lanes(tile, jnp.maximum)), 1, keepdims=True)

        def weigh(j, state):
            total, mixed = state
            cols = pl.ds(pl.multiple_of(j * block, block), block)
            prob = jnp.exp2((scores[j] - high) * TO_EXP2)
            total = total + fold_lanes(prob, jnp.add)
            return total, mixed + matmul_f32(prob.astype(bf16), v_ref[cols, :])

        zero = jnp.zeros((heads * block, HD), f32)
        total, mixed = lax.fori_loop(0, i + 1, weigh, (zero, zero))
        total = jnp.sum(total, 1, keepdims=True)
        mixed = (mixed / total).astype(bf16)
        log_total = high * TO_EXP2 + jnp.log2(total)
        for h in range(heads):
            placed[rows, h * HD : (h + 1) * HD] = mixed[h * block : (h + 1) * block]
            lse_ref[h : h + 1, rows] = as_row(log_total[h * block : (h + 1) * block])
        return 0

    lax.fori_loop(0, blocks, one_block, 0)

    def store_cut(r, _):
        dst = pl.ds(pl.multiple_of(r * cut, cut), cut)
        src = pl.ds(pl.multiple_of(order_ref[0, r] * cut, cut), cut)
        out_ref[dst, :] = placed[src, :]
        return 0

    lax.fori_loop(0, cuts, store_cut, 0)


def vmem_specs(count):
    return [pl.BlockSpec(memory_space=pltpu.VMEM)] * count


def attend(order, rows, weight, cosine, sine, piece, heads):
    length, width = rows.shape
    block = min(512, length)
    return pl.pallas_call(
        functools.partial(attend_kernel, heads, order.shape[1], block),
        out_shape=(
            jax.ShapeDtypeStruct((length, heads * HD), bf16),
            jax.ShapeDtypeStruct((heads, length, HD), bf16),
            jax.ShapeDtypeStruct((length, HD), bf16),
            jax.ShapeDtypeStruct((length, HD), bf16),
            jax.ShapeDtypeStruct((heads, length), f32),
            jax.ShapeDtypeStruct((length, heads * HD), bf16),
        ),
        in_specs=[pl.BlockSpec(memory_space=pltpu.SMEM)]
        + [pl.BlockSpec(memory_space=pl.ANY)] * 2
        + vmem_specs(3),
        out_specs=tuple(vmem_specs(6)),
        scratch_shapes=[
            pltpu.VMEM((length // block, heads * block, block), f32),
            pltpu.VMEM(rows.shape, bf16),
            pltpu.VMEM(weight.shape, bf16),
            pltpu.VMEM((block, weight.shape[1]), f32),
            pltpu.SemaphoreType.DMA((length // block + 1,)),
        ],
        compiler_params=pltpu.CompilerParams(vmem_limit_bytes=60 * 2**20),
        cost_estimate=pl.CostEstimate(
            flops=3 * heads * length * length * HD + 2 * length * width * weight.shape[1],
            bytes_accessed=10 * length * HD * heads * 4 + rows.size * 2,
            transcendentals=heads * length * length // 2,
        ),
    )(order, rows, weight, cosine, sine, piece)


DOWN, GATE_UP, OUT, QKV = 16, 32, 4, 8
CHUNKS = DOWN + GATE_UP + OUT + QKV
LAG = 3


def is_chunk(number):
    return 0 <= number < CHUNKS


def is_middle():
    rank = lax.axis_index("rep")
    return (rank == 1) | (rank == 2)


def is_end():
    rank = lax.axis_index("rep")
    return (rank == 0) | (rank == 3)


class NoLine:
    ticks = 0

    def signal(self, barrier):
        pass

    def greet(self, barrier, others):
        if others:
            pl.semaphore_wait(barrier, others)

    def start(self):
        pass

    def step(self, times=1):
        pass

    def end(self):
        pass


class Line:
    def __init__(self, first, ticks, picks, refs, outs, scratch):
        self.first, self.ticks, self.picks, self.refs, self.outs = first, ticks, picks, refs, outs
        (
            self.inward, self.across, self.own, self.pair, self.total, self.sems, self.local,
            self.carries,
        ) = scratch
        rank = lax.axis_index("rep")
        self.partner = {"rep": rank + 1 - 2 * (rank % 2)}
        self.peer = {"rep": 3 - rank}
        self.now = 0
        self.kept = []

    def signal(self, barrier):
        pl.semaphore_signal(barrier, inc=1, device_id=self.partner, device_id_type=MESH)

        @pl.when(is_middle())
        def _():
            pl.semaphore_signal(barrier, inc=1, device_id=self.peer, device_id_type=MESH)

    def greet(self, barrier, others):
        @pl.when(is_middle())
        def _():
            pl.semaphore_wait(barrier, others + 2)

        @pl.when(is_end())
        def _():
            pl.semaphore_wait(barrier, others + 1)

    def remote(self, hop, number, src, dst, device):
        return pltpu.make_async_remote_copy(
            src_ref=src, dst_ref=dst, send_sem=self.sems.at[0, hop, number],
            recv_sem=self.sems.at[1, hop, number], device_id=device, device_id_type=MESH,
        )

    def hops(self, number):
        tick = self.first + number
        term = pair = total = None
        if is_chunk(tick):
            which, pick = self.picks[tick]
            term = (
                lambda: self.remote(
                    0, number, pick(self.refs[which]), self.inward.at[number], self.partner
                ),
                lambda: pltpu.make_async_copy(
                    pick(self.refs[which]), self.own.at[tick % LAG], self.local.at[0, number]
                ),
            )
        if is_chunk(tick - LAG):
            held = self.pair.at[(tick - LAG) % (LAG + 1)]
            before = self.refs[f"pair{number}"] if number < LAG else held
            pair = (
                lambda: self.remote(1, number, before, self.across.at[number], self.peer),
                lambda: pltpu.make_async_copy(before, held, self.carries.at[0, number]),
            )
        if is_chunk(tick - 2 * LAG):
            held_total = self.total.at[(tick - 2 * LAG) % (LAG + 1)]
            done = self.refs[f"total{number}"] if number < LAG else held_total
            slot = self.outs[tick - 2 * LAG]
            total = (
                lambda: self.remote(2, number, done, slot, self.partner),
                lambda: pltpu.make_async_copy(done, slot, self.local.at[1, number]),
            )
        return term, pair, total

    def open(self, number):
        term, pair, total = self.hops(number)

        @pl.when(is_end())
        def _():
            if term:
                term[0]().start()

        @pl.when(is_middle())
        def _():
            if pair:
                pair[0]().start()
            if total:
                total[0]().start()
            if term:
                term[1]().start()
            if total:
                total[1]().start()
            if pair and number < LAG:
                pair[1]().start()

    def close(self, number):
        term, pair, total = self.hops(number)

        @pl.when(is_end())
        def _():
            if term:
                term[0]().wait_send()
            if total:
                total[0]().wait_recv()

        @pl.when(is_middle())
        def _():
            if total:
                total[0]().wait_send()
                total[1]().wait()
            if pair:
                pair[0]().wait_send()
                pair[0]().wait_recv()
            if term:
                term[0]().wait_recv()

    def add(self, number):
        term, pair, _ = self.hops(number)
        tick = self.first + number

        def sum_of(into, first, second):
            def one(g, _):
                into[g] = (first[g].astype(f32) + second[g].astype(f32)).astype(bf16)
                return 0

            lax.fori_loop(0, into.shape[0], one, 0)

        @pl.when(is_middle())
        def _():
            if pair:
                if number < LAG:
                    pair[1]().wait()
                before = tick - LAG
                sum_of(
                    self.total.at[before % (LAG + 1)], self.pair.at[before % (LAG + 1)],
                    self.across.at[number],
                )
            if term:
                term[1]().wait()
                sum_of(self.pair.at[tick % (LAG + 1)], self.own.at[tick % LAG], self.inward.at[number])

    def keep(self, number):
        tick = self.first + number
        which = number - (self.ticks - LAG)
        made = []
        if is_chunk(tick):
            made.append((self.pair.at[tick % (LAG + 1)], self.outs[f"pair{which}"], (1, which)))
        if is_chunk(tick - LAG):
            held = self.total.at[(tick - LAG) % (LAG + 1)]
            made.append((held, self.outs[f"total{which}"], (2, which)))
        copies = [
            lambda src=src, dst=dst, at=at: pltpu.make_async_copy(src, dst, self.carries.at[*at])
            for src, dst, at in made
        ]

        @pl.when(is_middle())
        def _():
            for copy in copies:
                copy().start()

        self.kept += copies

    def start(self):
        for number in range(LAG):
            self.open(number)

    def step(self, times=1):
        for _ in range(times):
            if self.now + LAG < self.ticks:
                self.settle()
                self.open(self.now + LAG - 1)

    def settle(self):
        self.close(self.now)
        self.add(self.now)
        if self.now >= self.ticks - LAG:
            self.keep(self.now)
        self.now += 1

    def end(self):
        while self.now + LAG < self.ticks:
            self.step()
        while self.now < self.ticks:
            self.settle()

        @pl.when(is_middle())
        def _():
            for copy in self.kept:
                copy().wait()


def line_slots(first, ticks):
    return [t - 2 * LAG for t in range(first, first + ticks) if is_chunk(t - 2 * LAG)]


class Sums:
    def __init__(self, shape):
        self.shape, self.tick, self.kept, self.done = shape, 0, {}, {}


def run(kernel, ins, outs, scratch, number, cost, sums=None, ticks=0, arrays=(), picks=None, vmem=58):
    ins, outs, scratch = list(ins), list(outs), list(scratch)
    counts = (len(ins), len(outs), len(scratch))
    first = sums.tick if ticks else 0
    names_in, names_out = [], []
    if ticks:
        for name, array in arrays:
            names_in.append(name)
            ins.append((array, pl.ANY))
        for which in range(LAG):
            for name, chunk_at in ((f"pair{which}", first - LAG), (f"total{which}", first - 2 * LAG)):
                if is_chunk(chunk_at + which):
                    names_in.append(name)
                    ins.append((sums.kept[name], pl.ANY))
        names_out = line_slots(first, ticks)
        after = first + ticks
        for which in range(LAG):
            for name, chunk_at in ((f"pair{which}", after - LAG), (f"total{which}", after - 2 * LAG)):
                if is_chunk(chunk_at + which):
                    names_out.append(name)
        outs += [(jax.ShapeDtypeStruct(sums.shape, bf16), pl.ANY)] * len(names_out)
        scratch += [
            pltpu.VMEM((ticks,) + sums.shape, bf16),
            pltpu.VMEM((ticks,) + sums.shape, bf16),
            pltpu.VMEM((LAG,) + sums.shape, bf16),
            pltpu.VMEM((LAG + 1,) + sums.shape, bf16),
            pltpu.VMEM((LAG + 1,) + sums.shape, bf16),
            pltpu.SemaphoreType.DMA((2, 3, ticks)),
            pltpu.SemaphoreType.DMA((2, ticks)),
            pltpu.SemaphoreType.DMA((3, LAG)),
        ]

    def body(*refs):
        in_refs, rest = refs[: len(ins)], refs[len(ins) :]
        out_refs, scratch_refs = rest[: len(outs)], rest[len(outs) :]
        line = NoLine()
        if ticks:
            line = Line(
                first, ticks, picks, dict(zip(names_in, in_refs[counts[0] :])),
                dict(zip(names_out, out_refs[counts[1] :])), scratch_refs[counts[2] :],
            )
        kernel(in_refs[: counts[0]], out_refs[: counts[1]], scratch_refs[: counts[2]], line)

    results = pl.pallas_call(
        body,
        out_shape=tuple(shape for shape, _ in outs),
        in_specs=[pl.BlockSpec(memory_space=space) for _, space in ins],
        out_specs=tuple(pl.BlockSpec(memory_space=space) for _, space in outs),
        scratch_shapes=scratch,
        compiler_params=pltpu.CompilerParams(
            vmem_limit_bytes=vmem * 2**20,
            **({} if number is None else {"collective_id": number, "has_side_effects": True}),
        ),
        cost_estimate=pl.CostEstimate(
            flops=cost[0], bytes_accessed=cost[1], transcendentals=cost[2]
        ),
    )(*[array for array, _ in ins])
    for name, result in zip(names_out, results[counts[1] :]):
        if name in line_slots(first, ticks):
            sums.done[name] = result
        else:
            sums.kept[name] = result
    if ticks:
        sums.tick += ticks
    return results[: counts[1]]


SMEM, VMEM, ANY = pltpu.SMEM, pltpu.VMEM, pl.ANY


def attend_back_kernel(
    heads, block, ins, outs, scratch, line, entered=False
):
    grad_ref, out_ref, q_ref, k_ref, v_ref, lse_ref, cos_ref, sin_ref, piece_ref, place_ref = ins
    (grad_qkv_ref,) = outs
    grads, centers, grad_q, placed = scratch
    if line.ticks and not entered:
        line.signal(pltpu.get_barrier_semaphore())
        line.greet(pltpu.get_barrier_semaphore(), 0)
        line.start()
    length = grad_ref.shape[0]
    blocks = length // block

    def take_block(i, _):
        rows = pl.ds(pl.multiple_of(i * block, block), block)
        position = lax.broadcasted_iota(jnp.int32, (block, length), 0) + i * block
        chosen = jnp.where(place_ref[...] == position, 1.0, 0.0).astype(bf16)
        taken = matmul_f32(chosen, grad_ref[...]).astype(bf16)
        for h in range(heads):
            grad = taken[:, h * HD : (h + 1) * HD]
            grads[h, rows, :] = grad
            product = grad.astype(f32) * out_ref[rows, h * HD : (h + 1) * HD].astype(f32)
            centers[h, rows, :] = jnp.broadcast_to(
                jnp.sum(product, 1, keepdims=True), (block, HD)
            )
        return 0

    lax.fori_loop(0, blocks, take_block, 0)
    line.step()
    grad_q[...] = jnp.zeros_like(grad_q)

    def key_block(j, _):
        cols = pl.ds(pl.multiple_of(j * block, block), block)
        key, value = k_ref[cols, :], v_ref[cols, :]

        def one(i, state, diagonal):
            grad_key, grad_value = state
            rows = pl.ds(pl.multiple_of(i * block, block), block)
            for h in range(heads):
                query, grad = q_ref[h, rows, :], grads[h, rows, :]
                log_total = lse_ref[h : h + 1, rows]
                center = centers[h, rows, :].T[0:1, :]
                prob = jnp.exp2(against_rows(key, query) * TO_EXP2 - log_total)
                if diagonal:
                    k_at = lax.broadcasted_iota(jnp.int32, (block, block), 0)
                    q_at = lax.broadcasted_iota(jnp.int32, (block, block), 1)
                    q_piece = piece_ref[0:1, cols].astype(f32)
                    k_piece = as_column(q_piece)
                    allowed = (k_at <= q_at) | ((q_piece != 0) & (q_piece == k_piece))
                    prob = jnp.where(allowed, prob, 0.0)
                grad_prob = against_rows(value, grad)
                grad_score = (prob * (grad_prob - center)).astype(bf16)
                grad_value = grad_value + matmul_f32(prob.astype(bf16), grad)
                grad_key = grad_key + matmul_f32(grad_score, query)
                grad_q[h, rows, :] += over_tokens(grad_score, key)
            return grad_key, grad_value

        zero = jnp.zeros((block, HD), f32)
        state = one(j, (zero, zero), True)
        grad_key, grad_value = lax.fori_loop(
            j + 1, blocks, functools.partial(one, diagonal=False), state
        )
        grad_key = grad_key * SCORE_SCALE
        grad_key = grad_key * cos_ref[cols, :] - pltpu.roll(grad_key, HD // 2, 1) * sin_ref[cols, :]
        placed[cols, heads * HD : (heads + 1) * HD] = grad_key.astype(bf16)
        placed[cols, (heads + 1) * HD :] = grad_value.astype(bf16)
        return 0

    for j in range(min(2, blocks - 1)):
        lax.fori_loop(j, j + 1, key_block, 0)
        line.step(2 - j)
    lax.fori_loop(min(2, blocks - 1), blocks, key_block, 0)

    def turn_back(i, _):
        rows = pl.ds(pl.multiple_of(i * block, block), block)
        for h in range(heads):
            grad = grad_q[h, rows, :] * SCORE_SCALE
            grad = grad * cos_ref[rows, :] - pltpu.roll(grad, HD // 2, 1) * sin_ref[rows, :]
            placed[rows, h * HD : (h + 1) * HD] = grad.astype(bf16)
        return 0

    lax.fori_loop(0, blocks, turn_back, 0)
    line.step()

    def store_block(i, _):
        rows = pl.ds(pl.multiple_of(i * block, block), block)
        place = as_column(place_ref[0:1, rows].astype(f32)).astype(jnp.int32)
        position = lax.broadcasted_iota(jnp.int32, (block, length), 1)
        chosen = jnp.where(place == position, 1.0, 0.0).astype(bf16)
        grad_qkv_ref[rows, :] = matmul_f32(chosen, placed[...]).astype(bf16)
        return 0

    lax.fori_loop(0, blocks, store_block, 0)
    line.end()


def attend_back_operands(order, out, query, key, value, lse, cosine, sine, piece, heads):
    length = out.shape[0]
    cut = length // order.shape[1]
    place = (order.reshape(-1, 1) * cut + jnp.arange(cut, dtype=order.dtype)).reshape(1, length)
    scratch = [
        pltpu.VMEM((heads, length, HD), bf16),
        pltpu.VMEM((heads, length, HD), f32),
        pltpu.VMEM((heads, length, HD), f32),
        pltpu.VMEM((length, (heads + 2) * HD), bf16),
    ]
    return [out, query, key, value, lse, cosine, sine, piece, place], scratch


def attend_back(grad, operands, scratch, heads):
    length = grad.shape[0]
    return run(
        functools.partial(attend_back_kernel, heads, min(512, length)),
        [(array, VMEM) for array in [grad] + operands],
        [(jax.ShapeDtypeStruct((length, (heads + 2) * HD), bf16), VMEM)],
        scratch,
        None,
        (8 * heads * length * length * HD, 14 * length * HD * heads * 4, heads * length * length // 2),
    )[0]


def place_in_group():
    me = lax.axis_index("grp")
    return me // 4, (me // 2) % 2, me % 2


def other(flip_y, flip_x, flip_core):
    y, x, core = place_in_group()
    return ((y + flip_y) % 2) * 4 + ((x + flip_x) % 2) * 2 + (core + flip_core) % 2


def chip_rows(flip_y, flip_x, rows):
    y, x, _ = place_in_group()
    first = (((y + flip_y) % 2) * 2 + (x + flip_x) % 2) * (2 * rows)
    return pl.ds(pl.multiple_of(first, 2 * rows), 2 * rows)


NEIGHBOURS = ((0, 0, 1), (0, 1, 0), (1, 0, 0))
EVERYONE = tuple((n // 4, (n // 2) % 2, n % 2) for n in range(1, 8))


def greet_group(line, flips=NEIGHBOURS, between=None):
    barrier = pltpu.get_barrier_semaphore()
    for flip in flips:
        pl.semaphore_signal(barrier, inc=1, device_id={"grp": other(*flip)}, device_id_type=MESH)
    line.signal(barrier)
    if between:
        between()
    line.greet(barrier, len(flips))


SIBLING, ALONG_X, ALONG_Y, ACROSS = (0, 0), (0, 1), (1, 0), (1, 1)


class Gather:
    TO_S, TO_X, TO_Y = (0, 0, 1), (0, 1, 0), (1, 0, 0)

    def __init__(self, rows, all_ref, sends, recvs):
        self.rows, self.all_ref, self.sends, self.recvs = rows, all_ref, sends, recvs
        self.started = []

    def copy(self, number, chip, core, part, target):
        first = other(*chip, core) * self.rows
        if part is None:
            where = pl.ds(pl.multiple_of(first, self.rows), self.rows)
        else:
            half = self.rows // 2
            where = pl.ds(pl.multiple_of(first + part * half, half), half)
        where = self.all_ref.at[where, :]
        return pltpu.make_async_remote_copy(
            src_ref=where, dst_ref=where, send_sem=self.sends.at[number],
            recv_sem=self.recvs.at[number], device_id={"grp": other(*target)}, device_id_type=MESH,
        )

    def send(self, *what):
        one = self.copy(*what)
        one.start()
        self.started.append(one)

    def landed(self, number, chip, core, part):
        self.copy(number, chip, core, part, self.TO_S).wait_recv()

    def send_own(self):
        self.send(1, SIBLING, 0, 1, self.TO_X)
        self.send(3, SIBLING, 0, 0, self.TO_Y)
        self.send(0, SIBLING, 0, None, self.TO_S)
        self.send(2, SIBLING, 0, 0, self.TO_X)
        self.send(4, SIBLING, 0, 1, self.TO_Y)

    def sibling(self):
        self.landed(0, SIBLING, 1, None)

    def relay(self):
        self.landed(1, ALONG_X, 0, 1)
        self.send(6, ALONG_X, 0, 1, self.TO_Y)
        self.landed(3, ALONG_Y, 0, 0)
        self.send(5, ALONG_Y, 0, 0, self.TO_X)
        self.send(7, ALONG_X, 0, 1, self.TO_S)
        self.send(8, ALONG_Y, 0, 0, self.TO_S)

    def pass_second(self):
        self.landed(2, ALONG_X, 0, 0)
        self.send(9, ALONG_X, 0, 0, self.TO_S)
        self.landed(4, ALONG_Y, 0, 1)
        self.send(10, ALONG_Y, 0, 1, self.TO_S)

    def along_x(self):
        self.landed(7, ALONG_X, 1, 1)
        self.landed(9, ALONG_X, 1, 0)

    def pass_across(self):
        self.landed(5, ACROSS, 0, 0)
        self.send(11, ACROSS, 0, 0, self.TO_S)
        self.landed(6, ACROSS, 0, 1)
        self.send(12, ACROSS, 0, 1, self.TO_S)

    def along_y(self):
        self.landed(8, ALONG_Y, 1, 0)
        self.landed(10, ALONG_Y, 1, 1)

    def across(self):
        self.landed(11, ACROSS, 1, 0)
        self.landed(12, ACROSS, 1, 1)

    def finish(self):
        for one in self.started:
            one.wait_send()


def gather_rows(rows, all_ref, sends, recvs, on_chip, line, then=None, final=True):
    rows_of = Gather(rows, all_ref, sends, recvs)
    rows_of.send_own()
    if then:
        then()
    rows_of.sibling()
    on_chip(*SIBLING)
    rows_of.relay()
    line.step(2)
    rows_of.pass_second()
    line.step(2)
    rows_of.along_x()
    on_chip(*ALONG_X)
    rows_of.pass_across()
    line.step(2)
    rows_of.along_y()
    on_chip(*ALONG_Y)
    rows_of.across()
    on_chip(*ACROSS)
    rows_of.finish()
    if final:
        line.end()
    else:
        line.step()


GATHER_COPIES = 13


def rms_normed(values, gain):
    return values * lax.rsqrt(jnp.mean(values * values, -1, keepdims=True) + EPS) * gain


class Moves:
    def __init__(self, sems):
        self.sems, self.count, self.open = sems, 0, []

    def start(self, src, dst):
        one = pltpu.make_async_copy(src, dst, self.sems.at[self.count])
        self.count += 1
        one.start()
        return one

    def later(self, src, dst):
        self.open.append(self.start(src, dst))

    def finish(self):
        for one in self.open:
            one.wait()


def gather_scratch(rows, width, moves):
    return [
        pltpu.VMEM((8 * rows, width), bf16),
        pltpu.SemaphoreType.DMA((GATHER_COPIES,)),
        pltpu.SemaphoreType.DMA((GATHER_COPIES,)),
        pltpu.SemaphoreType.DMA((moves,)),
    ]


def own_rows(rows):
    return pl.ds(pl.multiple_of(other(0, 0, 0) * rows, rows), rows)


def send_columns(pieces, sends, recvs, moves):
    copies = []
    for which, (rows_ref, width, there) in enumerate(pieces):
        for number, flip in enumerate(EVERYONE):
            target = other(*flip)
            cols = pl.ds(pl.multiple_of(target * width, width), width)
            one = pltpu.make_async_remote_copy(
                src_ref=rows_ref.at[:, cols], dst_ref=there,
                send_sem=sends.at[which, number], recv_sem=recvs.at[which, number],
                device_id={"grp": target}, device_id_type=MESH,
            )
            one.start()
            copies.append(one)
        mine = pl.ds(pl.multiple_of(other(0, 0, 0) * width, width), width)
        moves.later(rows_ref.at[:, mine], there)
    return copies


def gather_normed_kernel(ins, outs, scratch, line):
    x_ref, gain_ref = ins[:2]
    weights = ins[2:]
    all_ref, cols_ref = outs
    held, sends, recvs, sems, col_sends, col_recvs = scratch
    rows = x_ref.shape[0]
    moves = Moves(sems)

    def fill():
        held[own_rows(rows), :] = rms_normed(x_ref[...].astype(f32), gain_ref[...]).astype(bf16)

    greet_group(line, EVERYONE, fill)
    col_copies = []

    def send_weights():
        pieces, low = [], 0
        tall = weights[0].shape[0]
        there = pl.ds(pl.multiple_of(other(0, 0, 0) * tall, tall), tall)
        for weight in weights:
            width = weight.shape[1] // 8
            pieces.append((weight, width, cols_ref.at[there, low : low + width]))
            low += width
        col_copies.extend(send_columns(pieces, col_sends, col_recvs, moves))

    def on_chip(*chip):
        where = chip_rows(*chip, rows)
        moves.later(held.at[where, :], all_ref.at[where, :])

    gather_rows(rows, held, sends, recvs, on_chip, line, send_weights)
    for one in col_copies:
        one.wait()
    moves.finish()


def gather_normed(x, gain, weights, **line):
    rows, width = x.shape
    deep = sum(weight.shape[1] for weight in weights) // 8
    return run(
        gather_normed_kernel,
        [(x, VMEM), (gain, VMEM)] + [(weight, ANY) for weight in weights],
        [
            (jax.ShapeDtypeStruct((8 * rows, width), bf16), ANY),
            (jax.ShapeDtypeStruct((8 * weights[0].shape[0], deep), bf16), ANY),
        ],
        gather_scratch(rows, width, 4 + len(weights))
        + [pltpu.SemaphoreType.DMA((len(weights), 7))] * 2,
        line.pop("number"),
        (0, 150 * rows * width * 2, 0),
        **line,
    )


def columns_kernel(rows_here, ins, outs, scratch, line):
    (cols_ref,) = outs
    sends, recvs, sems = scratch
    moves = Moves(sems)
    barrier = pltpu.get_barrier_semaphore()
    for flip in EVERYONE:
        pl.semaphore_signal(barrier, inc=1, device_id={"grp": other(*flip)}, device_id_type=MESH)
    pl.semaphore_wait(barrier, 7)
    first = pl.multiple_of(lax.axis_index("rep") * rows_here, rows_here)
    me = other(0, 0, 0)
    pieces, low = [], 0
    for weight in ins:
        width = weight.shape[1] // 8
        pieces.append(
            (weight.at[pl.ds(first, rows_here), :], width, cols_ref.at[me, :, low : low + width])
        )
        low += width
    for one in send_columns(pieces, sends, recvs, moves):
        one.wait()
    moves.finish()


def columns_of_some(weights, rows_here, number):
    deep = sum(weight.shape[1] for weight in weights) // 8
    return run(
        functools.partial(columns_kernel, rows_here),
        [(weight, ANY) for weight in weights],
        [(jax.ShapeDtypeStruct((8, rows_here, deep), bf16), ANY)],
        [pltpu.SemaphoreType.DMA((len(weights), 7))] * 2
        + [pltpu.SemaphoreType.DMA((len(weights),))],
        number, (0, 50 * 8 * rows_here * deep, 0),
    )[0]


def feed_forward_kernel(tile, ins, outs, scratch, line):
    mid_ref, gain_ref, grad_ref, spread_ref, rest_ref, w_down_ref = ins
    all_ref, hidden_ref, whole_ref, grad_gate_up_ref, down_ref = outs
    held, grads_held, sends, recvs, grad_sends, grad_recvs, sems = scratch[:7]
    weight, w_down, hidden, up_part, gate_part, grads, down = scratch[7:]
    rows = mid_ref.shape[0]
    inner = hidden.shape[1]
    moves = Moves(sems)
    planes, _, tall, _ = spread_ref.shape
    loads = [
        moves.start(spread_ref.at[z], weight.at[:, z * tall : (z + 1) * tall, :])
        for z in range(planes)
    ]
    loads.append(moves.start(rest_ref, weight.at[:, planes * tall :, :]))
    down_load = moves.start(w_down_ref, w_down)

    def fill():
        held[own_rows(rows), :] = rms_normed(mid_ref[...], gain_ref[...]).astype(bf16)
        grads_held[own_rows(rows), :] = grad_ref[...]

    greet_group(line, between=fill)
    first = Gather(rows, held, sends, recvs)
    second = Gather(rows, grads_held, grad_sends, grad_recvs)
    stored = []

    def forward(*chip):
        where = chip_rows(*chip, rows)
        moves.later(held.at[where, :], all_ref.at[where, :])

        def column(t, _):
            cols = pl.ds(pl.multiple_of(t * tile, tile), tile)
            up_cols = pl.ds(pl.multiple_of(inner + t * tile, tile), tile)
            lhs = held[where, :]
            gate = matmul_f32(lhs, weight[:, :, cols].reshape(-1, tile))
            up = matmul_f32(lhs, weight[:, :, up_cols].reshape(-1, tile))
            sigma = 1.0 / (1.0 + jnp.exp(-gate))
            swish = gate * sigma
            hidden[where, cols] = (swish * up).astype(bf16)
            up_part[where, cols] = swish.astype(bf16)
            gate_part[where, cols] = (up * sigma * (1.0 + gate * (1.0 - sigma))).astype(bf16)
            return 0

        lax.fori_loop(0, inner // tile, column, 0)
        moves.later(hidden.at[where, :], hidden_ref.at[where, :])

    def backward(*chip):
        where = chip_rows(*chip, rows)
        slot = len(stored) % 2
        if len(stored) >= 2:
            stored[len(stored) - 2].wait()

        def column(t, _):
            cols = pl.ds(pl.multiple_of(t * tile, tile), tile)
            up_cols = pl.ds(pl.multiple_of(inner + t * tile, tile), tile)
            incoming = grads_held[where, :]
            grad_hidden = against_rows(incoming, w_down[cols, :])
            grads[slot, :, cols] = (grad_hidden * gate_part[where, cols].astype(f32)).astype(bf16)
            grads[slot, :, up_cols] = (grad_hidden * up_part[where, cols].astype(f32)).astype(bf16)
            term = over_tokens(hidden[where, cols], incoming)
            if chip == SIBLING:
                down[cols, :] = term
            elif chip == ACROSS:
                weight[t] = (down[cols, :] + term).astype(bf16)
            else:
                down[cols, :] += term
            return 0

        lax.fori_loop(0, inner // tile, column, 0)
        stored.append(moves.start(grads.at[slot], grad_gate_up_ref.at[where, :]))

    first.send_own()
    for one in loads:
        one.wait()
    whole = moves.start(weight, whole_ref)
    first.sibling()
    forward(*SIBLING)
    first.relay()
    first.pass_second()
    second.send_own()
    first.along_x()
    forward(*ALONG_X)
    first.pass_across()
    first.along_y()
    forward(*ALONG_Y)
    second.relay()
    first.across()
    forward(*ACROSS)
    down_load.wait()
    second.sibling()
    backward(*SIBLING)
    second.pass_second()
    second.along_x()
    backward(*ALONG_X)
    second.pass_across()
    second.along_y()
    backward(*ALONG_Y)
    second.across()
    whole.wait()
    backward(*ACROSS)
    moves.later(weight.at[: inner // tile], down_ref)
    first.finish()
    second.finish()
    for one in stored[-2:]:
        one.wait()
    moves.finish()


def feed_forward(mid, gain, grad, spread, rest, w_down, **line):
    rows, width = mid.shape
    inner = w_down.shape[0]
    weight = (8, width // 8, 2 * inner)
    return run(
        functools.partial(feed_forward_kernel, weight[1]),
        [(mid, VMEM), (gain, VMEM), (grad, VMEM), (spread, ANY), (rest, ANY), (w_down, ANY)],
        [
            (jax.ShapeDtypeStruct((8 * rows, width), bf16), ANY),
            (jax.ShapeDtypeStruct((8 * rows, inner), bf16), ANY),
            (jax.ShapeDtypeStruct(weight, bf16), ANY),
            (jax.ShapeDtypeStruct((8 * rows, 2 * inner), bf16), ANY),
            (jax.ShapeDtypeStruct((inner // weight[1], weight[1], width), bf16), ANY),
        ],
        [pltpu.VMEM((8 * rows, width), bf16)] * 2
        + [pltpu.SemaphoreType.DMA((GATHER_COPIES,))] * 4
        + [pltpu.SemaphoreType.DMA((20,))]
        + [pltpu.VMEM(weight, bf16), pltpu.VMEM(w_down.shape, bf16)]
        + [pltpu.VMEM((8 * rows, inner), bf16)] * 3
        + [
            pltpu.VMEM((2, 2 * rows, 2 * inner), bf16),
            pltpu.VMEM(w_down.shape, f32),
        ],
        line.pop("number"),
        (64 * rows * width * inner, 300 * rows * width * 2, 8 * rows * inner),
        vmem=63,
        **line,
    )


def attention_back_kernel(heads, block, ins, outs, scratch, line):
    grad_ref, w_ref, attended_ref = ins[:3]
    grad_qkv_ref, out_term_ref = outs
    held, sends, recvs, sems, total, grad_attended_ref = scratch[:6]
    rows = grad_ref.shape[0]
    moves = Moves(sems)
    greet_group(line)
    line.start()
    held[own_rows(rows), :] = grad_ref[...].astype(bf16)

    def on_chip(*chip):
        where = chip_rows(*chip, rows)
        incoming = held[where, :]
        grad_attended_ref[where, :] = against_rows(incoming, w_ref[...]).astype(bf16)
        term = over_tokens(attended_ref[where, :], incoming)
        if chip == SIBLING:
            total[...] = term
        elif chip == ACROSS:
            out_term_ref[...] = (total[...] + term).astype(bf16)
        else:
            total[...] += term

    gather_rows(rows, held, sends, recvs, on_chip, line, final=False)
    moves.finish()
    attend_back_kernel(
        heads, block, (grad_attended_ref,) + tuple(ins[3:]), (grad_qkv_ref,), scratch[6:], line,
        entered=True,
    )


def attention_back(grad, w_out, attended, back_ins, back_scratch, heads, **line):
    rows, width = grad.shape
    length = 8 * rows
    return run(
        functools.partial(attention_back_kernel, heads, min(512, length)),
        [(array, VMEM) for array in [grad, w_out, attended] + back_ins],
        [
            (jax.ShapeDtypeStruct((length, (heads + 2) * HD), bf16), VMEM),
            (jax.ShapeDtypeStruct(w_out.shape, bf16), VMEM),
        ],
        gather_scratch(rows, width, 1)
        + [pltpu.VMEM(w_out.shape, f32), pltpu.VMEM(attended.shape, bf16)]
        + back_scratch,
        line.pop("number"),
        (
            32 * rows * width * w_out.shape[0] + 8 * heads * length * length * HD,
            250 * rows * width * 2, heads * length * length // 2,
        ),
        **line,
    )


class WeightTerm:
    def __init__(self, rows_ref, columns_ref, term_ref, scratch):
        self.rows_ref, self.columns_ref, self.term_ref = rows_ref, columns_ref, term_ref
        self.loaded, self.flipped, self.ready, self.sems = scratch
        self.tile = self.loaded.shape[2]
        for number in (0, 1):
            self.load(number).start()

    def load(self, number):
        cols = slice(number * self.tile, (number + 1) * self.tile)
        return pltpu.make_async_copy(
            self.rows_ref.at[:, cols], self.loaded.at[number % 2], self.sems.at[0, number % 2]
        )

    def store(self, number):
        return pltpu.make_async_copy(
            self.ready.at[number % 2], self.term_ref.at[number], self.sems.at[1, number % 2]
        )

    def work(self, numbers):
        for number in numbers:
            at = number % 2
            self.load(number).wait()
            if number >= 2:
                self.store(number - 2).wait()
            width = self.columns_ref.shape[1]
            step = min(256, width)
            self.flipped[...] = self.loaded[at].T

            def column(t, _):
                cols = pl.ds(pl.multiple_of(t * step, step), step)
                term = matmul_f32(self.flipped[...], self.columns_ref[:, cols])
                self.ready[at, :, cols] = term.astype(bf16)
                return 0

            lax.fori_loop(0, width // step, column, 0)
            self.store(number).start()
            if number + 2 < 8:
                self.load(number + 2).start()

    def finish(self):
        for number in (6, 7):
            self.store(number).wait()


UNITS = (
    (ACROSS, 0), (ACROSS, 1), (ALONG_X, 0), (ALONG_Y, 1), (ALONG_X, 1), (ALONG_Y, 0),
    (SIBLING, 0), (SIBLING, 1),
)


def scatter_kernel(turned, extra, after, steps, ins, outs, scratch, line):
    out_ref = outs[0] if after == "base" else scratch[-4]
    finals = ins[len(ins) - {"base": 1, "cast": 1, "back": 3}[after] :]
    part, to_s, from_s, to_link, relay, last, sends, recvs = scratch[:8]
    a_ref, b_ref, load_sems = scratch[-3:]
    rows, width = out_ref.shape
    half = width // 2
    _, _, core = place_in_group()
    loading = {}

    def load(name, src, dst):
        loading[name] = pltpu.make_async_copy(src, dst, load_sems.at[len(loading)])
        loading[name].start()

    def load_weight(h):
        where = (slice(h * half, (h + 1) * half), slice(None))
        where = where if turned else where[::-1]
        load(h, ins[1].at[where], b_ref.at[where])

    def load_rows(chip):
        where = chip_rows(*chip, rows)
        load(chip, ins[0].at[where, :], a_ref.at[where, :])

    load_weight(0)
    load_rows(ACROSS)
    load_weight(1)
    for chip in (ALONG_X, ALONG_Y, SIBLING):
        load_rows(chip)
    greet_group(line)
    line.start()
    if extra:
        columns_ref = a_ref
        if extra == "loaded":
            columns_ref = scratch[12]
            load("columns", ins[3], columns_ref)
        term = WeightTerm(ins[2], columns_ref, outs[-1], scratch[8:12])
    own_at = pl.multiple_of(core * rows, rows)
    other_at = pl.multiple_of((1 - core) * rows, rows)
    to_sib, to_x, to_y = (0, 0, 1), (0, 1, 0), (1, 0, 0)
    started = []

    def ready(*names):
        for name in names:
            if name in loading:
                loading.pop(name).wait()
                loading[name, "done"] = None

    def send(number, src, dst, target):
        one = pltpu.make_async_remote_copy(
            src_ref=src, dst_ref=dst, send_sem=sends.at[number], recv_sem=recvs.at[number],
            device_id={"grp": other(*target)}, device_id_type=MESH,
        )
        one.start()
        started.append(one)

    def landed(number, where):
        pltpu.make_async_remote_copy(
            src_ref=where, dst_ref=where, send_sem=sends.at[number], recv_sem=recvs.at[number],
            device_id={"grp": other(0, 0, 1)}, device_id_type=MESH,
        ).wait_recv()

    def make(n):
        chip, h = UNITS[n]
        ready(h, chip)
        lhs = a_ref[chip_rows(*chip, rows), :]
        cols = slice(h * half, (h + 1) * half)
        if turned:
            part[n % 2] = against_rows(lhs, b_ref[cols, :])
        else:
            part[n % 2] = matmul_f32(lhs, b_ref[:, cols])
        to_s[n] = part[n % 2, pl.ds(other_at, rows), :].astype(bf16)
        send(n, to_s.at[n], from_s.at[n], to_sib)

    def own(n):
        landed(n, from_s.at[n])
        return part[n % 2, pl.ds(own_at, rows), :] + from_s[n].astype(f32)

    def finish(n):
        _, h = UNITS[n]
        if n < 2:
            to_link[n] = own(n).astype(bf16)
            send(8 + n, to_link.at[n], relay.at[n], (to_x, to_y)[n])
        elif n < 4:
            to_link[n] = own(n).astype(bf16)
            send(8 + n, to_link.at[n], last.at[(None, None, 0, 3)[n]], (to_x, to_y)[n - 2])
        elif n < 6:
            total = own(n)
            landed(8 + h, relay.at[h])
            to_link[n] = (total + relay[h].astype(f32)).astype(bf16)
            send(8 + n, to_link.at[n], last.at[(1, 2)[n - 4]], (to_x, to_y)[n - 4])
        else:
            cols = slice(h * half, (h + 1) * half)
            if after == "back":
                out_ref[:, cols] = own(n)
            else:
                out_ref[:, cols] = own(n) + finals[0][:, cols].astype(f32)
        line.step(steps.get(n, 0))

    def work(numbers, point):
        if extra:
            ready("columns")
            if columns_ref is a_ref:
                ready(*(chip for chip, _ in UNITS))
            term.work(numbers)
        line.step(steps.get(point, 0))

    make(0)
    make(1)
    finish(0)
    make(2)
    finish(1)
    make(3)
    finish(2)
    make(4)
    finish(3)
    make(5)
    work((0, 1), "early")
    finish(4)
    make(6)
    finish(5)
    make(7)
    finish(6)
    finish(7)
    work((2, 3), "late")
    work((4, 5), "later")
    work((6, 7), "latest")
    for number, slot, h in ((10, 0, 0), (11, 3, 1), (12, 1, 1), (13, 2, 0)):
        cols = slice(h * half, (h + 1) * half)
        landed(number, last.at[slot])
        out_ref[:, cols] += last[slot].astype(f32)
        line.step(steps.get(number, 0))
    if after == "cast":
        outs[0][...] = out_ref[...].astype(outs[0].dtype)
    if after == "back":
        upstream_ref, rows_ref, gain_ref = finals
        some = min(64, rows)

        def norm_rows(number, gain_term):
            at = pl.ds(pl.multiple_of(number * some, some), some)
            values, incoming = rows_ref[at, :].astype(f32), out_ref[at, :]
            inv = lax.rsqrt(jnp.mean(values * values, -1, keepdims=True) + EPS)
            grad, gain_part = norm_back(
                upstream_ref[at, :].astype(f32), incoming, values * inv, inv, gain_ref[...]
            )
            outs[0][at, :] = grad.astype(outs[0].dtype)
            return gain_term + gain_part[None, :]

        outs[1][...] = lax.fori_loop(0, rows // some, norm_rows, jnp.zeros((1, width), f32))
    for one in started:
        one.wait_send()
    if extra:
        term.finish()
    line.end()


def product_scattered(
    a, b, turned, extra=None, base=None, back=None, dtype=f32, steps=None, **line
):
    length, depth = a.shape
    width = b.shape[0] if turned else b.shape[1]
    rows = length // 8
    ins = [(a, ANY), (b, ANY)]
    outs = [(jax.ShapeDtypeStruct((rows, width), dtype), VMEM)]
    after = "back" if back else "base" if dtype == f32 else "cast"
    if back:
        outs.append((jax.ShapeDtypeStruct((1, width), f32), VMEM))
    piece = (rows, width // 2)
    scratch = [
        pltpu.VMEM((2, 2 * rows, width // 2), f32),
        pltpu.VMEM((8,) + piece, bf16),
        pltpu.VMEM((8,) + piece, bf16),
        pltpu.VMEM((6,) + piece, bf16),
        pltpu.VMEM((2,) + piece, bf16),
        pltpu.VMEM((4,) + piece, bf16),
        pltpu.SemaphoreType.DMA((14,)),
        pltpu.SemaphoreType.DMA((14,)),
    ]
    flops, kind = 2 * length * depth * width, None
    if extra:
        first, second = extra
        kind = "own" if second is None else "loaded"
        ins.append((first, ANY))
        columns = a if second is None else second
        tall = first.shape[1] // 8
        outs.append((jax.ShapeDtypeStruct((8, tall, columns.shape[1]), bf16), ANY))
        scratch += [
            pltpu.VMEM((2, length, tall), bf16),
            pltpu.VMEM((tall, length), bf16),
            pltpu.VMEM((2, tall, columns.shape[1]), bf16),
            pltpu.SemaphoreType.DMA((2, 2)),
        ]
        if second is not None:
            ins.append((second, ANY))
            scratch.append(pltpu.VMEM(second.shape, bf16))
        flops += 2 * length * first.shape[1] * columns.shape[1]
    ins += [(array, VMEM) for array in (back or (base,))]
    if after != "base":
        scratch.append(pltpu.VMEM((rows, width), f32))
    scratch += [
        pltpu.VMEM(a.shape, bf16), pltpu.VMEM(b.shape, bf16), pltpu.SemaphoreType.DMA((7,))
    ]
    return run(
        functools.partial(scatter_kernel, turned, kind, after, steps or {}), ins, outs, scratch,
        line.pop("number"), (flops, 150 * rows * width * 2, 0), vmem=61, **line,
    )


def tail_kernel(ready, later, ins, outs, scratch, line):
    qkv_ref, gains_ref = ins[:2]
    chunk_refs = dict(zip(ready, ins[2:]))
    gate_ref, up_ref, qkv_rows_ref, gains_out_ref = outs
    from_group, mine, from_rep, sends, recvs, chunk_sems, local = scratch
    me, rank = other(0, 0, 0), lax.axis_index("rep")
    inner = gate_ref.shape[1] // 8
    part = qkv_ref.shape[-1]
    high = line.outs[later[0]].shape[1]
    barrier = pltpu.get_barrier_semaphore()
    for flip in range(1, 4):
        pl.semaphore_signal(
            barrier, inc=1, device_id={"rep": (rank + flip) % 4}, device_id_type=MESH
        )
    for flip in EVERYONE:
        pl.semaphore_signal(barrier, inc=1, device_id={"grp": other(*flip)}, device_id_type=MESH)
    pl.semaphore_wait(barrier, 10)
    waits, moves = [], Moves(local)
    line.refs["qkv"] = qkv_rows_ref

    def send(kind, number, src, dst, device):
        return pltpu.make_async_remote_copy(
            src_ref=src, dst_ref=dst, send_sem=sends.at[kind, number],
            recv_sem=recvs.at[kind, number], device_id=device, device_id_type=MESH,
        )

    own_qkv = qkv_rows_ref.at[me // 4, :, :, pl.ds(pl.multiple_of((me % 4) * part, part), part)]
    qkv_copies, gain_copies = [], []
    for number, flip in enumerate(EVERYONE):
        target = other(*flip)
        qkv_copies.append(send(0, number, qkv_ref.at[target], own_qkv, {"grp": target}))
        qkv_copies[-1].start()
    moves.later(qkv_ref.at[me], own_qkv)
    line.start()
    for number, flip in enumerate(EVERYONE):
        target = other(*flip)
        gain_copies.append(
            send(1, number, gains_ref.at[target], from_group.at[me], {"grp": target})
        )
        gain_copies[-1].start()
    from_group[me] = gains_ref[me]

    def spread(chunk):
        src = chunk_refs[chunk] if chunk in chunk_refs else line.outs[chunk]
        number = chunk - DOWN
        rows = slice(number // 2 * high, (number // 2 + 1) * high)
        dst = (gate_ref, up_ref)[number % 2]
        there = dst.at[rows, pl.ds(pl.multiple_of(me * inner, inner), inner)]
        for flip in EVERYONE:
            target = other(*flip)
            pltpu.make_async_remote_copy(
                src_ref=src.at[target], dst_ref=there, send_sem=chunk_sems.at[0, number],
                recv_sem=chunk_sems.at[1, number], device_id={"grp": target}, device_id_type=MESH,
            ).start()
        moves.later(src.at[me], there)
        seven = dst.at[rows, : 7 * inner]
        waits.append(
            pltpu.make_async_remote_copy(
                src_ref=seven, dst_ref=seven, send_sem=chunk_sems.at[0, number],
                recv_sem=chunk_sems.at[1, number], device_id={"grp": other(0, 0, 1)},
                device_id_type=MESH,
            )
        )

    for chunk in ready:
        spread(chunk)
    for one in gain_copies:
        one.wait()
    mine[rank] = sum(from_group[g] for g in range(8))
    rep_copies = []
    for step in range(1, 4):
        target = (rank + step) % 4
        rep_copies.append(
            send(2, step, mine.at[rank], from_rep.at[step], {"rep": target})
        )
        rep_copies[-1].start()
    for step, one in zip(range(1, 4), rep_copies):
        one.wait()
        mine[(rank + 4 - step) % 4] = from_rep[step]
    gains_out_ref[...] = (mine[0] + mine[1]) + (mine[2] + mine[3])
    for settled in range(line.ticks - LAG):
        if line.first + settled + LAG == CHUNKS - QKV:
            for one in qkv_copies:
                one.wait()
            moves.open.pop(0).wait()
        line.step()
        chunk = line.first + settled - 2 * LAG
        if chunk in later:
            spread(chunk)
    line.end()
    for one in waits:
        one.wait_send()
        one.wait_recv()
    moves.finish()


def tail(qkv_term, gains, chunks, inner, number, sums, ticks, arrays, picks):
    first = sums.tick
    ready = sorted(chunks)
    later = [c for c in line_slots(first, ticks) if c < DOWN + GATE_UP]
    _, high, width = sums.shape
    wide = jax.ShapeDtypeStruct((GATE_UP // 2 * high, 8 * inner), bf16)
    moved = jax.ShapeDtypeStruct((2, 8, 2 * high, 2 * width), bf16)
    picks = dict(picks)
    for n in range(QKV):
        where = (
            n // 4, slice(None), slice(n // 2 % 2 * high, (n // 2 % 2 + 1) * high),
            slice(n % 2 * width, (n % 2 + 1) * width),
        )
        picks[CHUNKS - QKV + n] = ("qkv", lambda ref, where=where: ref.at[where])
    return run(
        functools.partial(tail_kernel, ready, later),
        [(qkv_term, ANY), (gains, VMEM)] + [(chunks[c], ANY) for c in ready],
        [(wide, ANY), (wide, ANY), (moved, ANY), (jax.ShapeDtypeStruct(gains.shape[1:], f32), VMEM)],
        [
            pltpu.VMEM(gains.shape, f32),
            pltpu.VMEM((4,) + gains.shape[1:], f32),
            pltpu.VMEM((4,) + gains.shape[1:], f32),
            pltpu.SemaphoreType.DMA((3, 7)),
            pltpu.SemaphoreType.DMA((3, 7)),
            pltpu.SemaphoreType.DMA((2, GATE_UP)),
            pltpu.SemaphoreType.DMA((1 + GATE_UP,)),
        ],
        number, (0, 200 * 8 * high * width * 2, 0), sums=sums, ticks=ticks, arrays=arrays, picks=picks,
    )


def finish_kernel(heads, *refs):
    chunks, rest = refs[: DOWN + OUT + QKV], refs[DOWN + OUT + QKV :]
    gate_rows, up_rows = rest[:2]
    query, key, value, out, gate, up, down = rest[2:9]
    low, wide, load_sems, store_sems = rest[9:]
    _, high, width = chunks[0].shape
    depth = low.shape[0]

    def half(number):
        return slice(number * high, (number + 1) * high)

    def side(number):
        return slice(number * width, (number + 1) * width)

    jobs = []
    for n, ref in enumerate(chunks[:DOWN]):
        jobs.append((ref, [(slice(0, width), down.at[n // 2, :, :, side(n % 2)])]))
    for ref, into in ((gate_rows, gate), (up_rows, up)):
        for low_col in range(0, ref.shape[2], low.shape[3]):
            for number in (0, 1):
                where = (slice(None), half(number), slice(low_col, low_col + low.shape[3]))
                jobs.append((ref.at[where], [(slice(0, low.shape[3]), into.at[where])]))
    for n, ref in enumerate(chunks[DOWN : DOWN + OUT]):
        jobs.append((ref, [(slice(0, width), out.at[:, half(n // 2), side(n % 2)])]))
    part = (heads + 2) * HD
    for n, ref in enumerate(chunks[DOWN + OUT :]):
        stores = []
        for place in range(width // part):
            at, device = place * part, (n // 4 * 2 + n % 2) * (width // part) + place
            for into, first, size in (
                (query, 0, heads * HD), (key, heads * HD, HD), (value, (heads + 1) * HD, HD)
            ):
                there = into.at[:, half(n // 2 % 2), device * size : (device + 1) * size]
                stores.append((slice(at + first, at + first + size), there))
        jobs.append((ref, stores))

    def load(number):
        at, ref = number % depth, jobs[number][0]
        return pltpu.make_async_copy(ref, low.at[at, :, :, : ref.shape[2]], load_sems.at[at])

    def stores(number):
        at = number % depth
        return [
            pltpu.make_async_copy(wide.at[at, :, :, cols], into, store_sems.at[at, which])
            for which, (cols, into) in enumerate(jobs[number][1])
        ]

    for number in range(depth - 1):
        load(number).start()
    for number in range(len(jobs)):
        if number + depth - 1 < len(jobs):
            load(number + depth - 1).start()
        load(number).wait()
        if number >= depth:
            for one in stores(number - depth):
                one.wait()

        def cast(g, _, at=number % depth, cols=slice(0, jobs[number][0].shape[2])):
            wide[at, g, :, cols] = low[at, g, :, cols].astype(f32)
            return 0

        lax.fori_loop(0, low.shape[1], cast, 0)
        for one in stores(number):
            one.start()
    for number in range(len(jobs) - depth, len(jobs)):
        for one in stores(number):
            one.wait()


def finish(chunks, gate_rows, up_rows, heads):
    eight, high, width = chunks[0].shape
    width = 2 * width
    rows, wide = gate_rows.shape

    def split(columns):
        return jax.ShapeDtypeStruct((eight, rows // eight, columns), f32)

    shapes = [split(columns) for columns in (8 * heads * HD, 8 * HD, 8 * HD, width, wide, wide)]
    shapes.append(jax.ShapeDtypeStruct((DOWN // 2, eight, high, width), f32))
    depth = 6
    results = pl.pallas_call(
        functools.partial(finish_kernel, heads),
        out_shape=tuple(shapes),
        in_specs=[pl.BlockSpec(memory_space=pl.ANY)] * (len(chunks) + 2),
        out_specs=tuple([pl.BlockSpec(memory_space=pl.ANY)] * 7),
        scratch_shapes=[
            pltpu.VMEM((depth, eight, high, width), bf16),
            pltpu.VMEM((depth, eight, high, width), f32),
            pltpu.SemaphoreType.DMA((depth,)),
            pltpu.SemaphoreType.DMA((depth, 12)),
        ],
        compiler_params=pltpu.CompilerParams(vmem_limit_bytes=60 * 2**20),
        cost_estimate=pl.CostEstimate(
            flops=0, bytes_accessed=3 * CHUNKS * eight * high * width, transcendentals=0
        ),
    )(
        *chunks, gate_rows.reshape(eight, rows // eight, wide),
        up_rows.reshape(eight, rows // eight, wide),
    )
    flat = [result.reshape(rows, -1) for result in results[:6]]
    return flat + [results[6].reshape(-1, width)]


def sum_over_sequences(term):
    return lax.psum(term, "rep").astype(f32)


def on_device(
    layer_input,
    cotangent,
    cut_order,
    piece_ids,
    w_query,
    w_key,
    w_value,
    w_out,
    w_gate,
    w_up,
    w_down,
    gain_attn,
    gain_ffn,
):
    groups = lax.axis_size("grp")
    reps = lax.axis_size("rep")
    own_index = lax.axis_index("grp")
    _, local_rows, model_width = layer_input.shape
    length = piece_ids.shape[1]
    rows_here = w_query.shape[0]
    q_width = w_query.shape[1]
    kv_heads = w_key.shape[1] // HD
    heads = q_width // HD // groups
    copies = groups // kv_heads
    hidden_here = w_down.shape[0]
    cosine, sine = turn_tables(length)

    near = groups == 8 and reps == 4 and copies == 1 and 2 * hidden_here == model_width

    def gather(rows):
        return lax.all_gather(rows, "grp", axis=0, tiled=True)

    def scatter(first, second, turned):
        term = against_rows(first, second) if turned else matmul_f32(first, second)
        return lax.psum_scatter(
            term.astype(bf16), "grp", scatter_dimension=0, tiled=True
        ).astype(f32)

    def to_columns(parts):
        return lax.all_to_all(parts, "grp", 1, 0, tiled=True).reshape(-1, parts.shape[-1])

    def per_group(weight):
        return weight.reshape(rows_here, groups, -1)

    def per_kv_head(weight):
        return jnp.repeat(weight.reshape(rows_here, kv_heads, HD), copies, axis=1)

    x_rows = layer_input.reshape(local_rows, model_width)
    x_flat = x_rows.astype(f32)
    inv_one = lax.rsqrt(jnp.mean(x_flat * x_flat, -1, keepdims=True) + EPS)
    unit_one = x_flat * inv_one
    attn_gain, ffn_gain = gain_attn.reshape(1, -1), gain_ffn.reshape(1, -1)
    if near:
        share = rows_here // (4 * reps) * 3
        spread = columns_of_some((w_gate, w_up), share, 11)
        x_first, spread = lax.optimization_barrier((x_rows, spread))
        spread = lax.all_gather(spread, "rep", axis=0)
        normed_one, cols_qkv = gather_normed(
            x_first, attn_gain, (w_query, w_key, w_value), number=1
        )
        last_gate, last_up, normed_one = lax.optimization_barrier(
            (w_gate[reps * share :], w_up[reps * share :], normed_one)
        )
        rest = to_columns(
            jnp.concatenate(
                [part.reshape(rows_here - reps * share, groups, -1) for part in (last_gate, last_up)],
                -1,
            )
        ).reshape(groups, rows_here - reps * share, -1)
    else:
        normed_one = gather(rms_normed(x_flat, attn_gain).astype(bf16))
        cols_qkv = to_columns(
            jnp.concatenate([per_group(w_query), per_kv_head(w_key), per_kv_head(w_value)], -1)
        )
        cols_gate_up = to_columns(jnp.concatenate([per_group(w_gate), per_group(w_up)], -1))
    attended, query, key, value, lse, attended_placed = attend(
        cut_order, normed_one, cols_qkv, cosine, sine, piece_ids, heads
    )
    if near:
        mid = product_scattered(attended, w_out, False, base=x_rows, number=2)[0]
    else:
        mid = x_flat + scatter(attended, w_out, False)
    grad_out = cotangent.reshape(local_rows, model_width)

    back_ins, back_scratch = attend_back_operands(
        cut_order, attended_placed, query, key, value, lse, cosine, sine, piece_ids, heads
    )
    q_here = heads * HD
    if near:
        normed_two, hidden, cols_gate_up, grad_gate_up, down_term = feed_forward(
            mid, ffn_gain, grad_out, spread, rest, w_down, number=3
        )
        cols_gate_up = cols_gate_up.reshape(model_width, -1)
        high, half_width = 2 * rows_here // GATE_UP, model_width // 2
        sums = Sums((8, high, half_width))
        terms = {"down": down_term.reshape(DOWN // 2, 8, high, model_width)}

        def pick_whole(n):
            return "down", lambda ref: ref.at[n // 2, :, :, n % 2 * half_width : (n % 2 + 1) * half_width]

        def pick_rows(name, n):
            rows, side = n // 2 * high, n % 2 * half_width
            return name, lambda ref: ref.at[:, rows : rows + high, side : side + half_width]

        picks = [pick_whole(n) for n in range(DOWN)]
        picks += [pick_rows("gate_up", n) for n in range(GATE_UP)]
        picks += [pick_rows("out", n) for n in range(OUT)]

        def line(number, ticks):
            names = sorted(
                {picks[t][0] for t in range(sums.tick, sums.tick + ticks) if t < len(picks)}
            )
            return dict(
                number=number, ticks=ticks, sums=sums, picks=dict(enumerate(picks)),
                arrays=[(name, terms[name]) for name in names],
            )

        result, terms["gate_up"] = product_scattered(
            hidden, w_down, False, extra=(normed_two, grad_gate_up), base=mid, dtype=bf16,
            steps={1: 1, 3: 1, "early": 1, 7: 1, "late": 1, "later": 1, "latest": 1}, **line(5, 9),
        )
        grad_mid, gain_ffn_term = product_scattered(
            grad_gate_up, cols_gate_up, True, back=(grad_out, mid, ffn_gain),
            steps={0: 1, 2: 1, 3: 1, 4: 1, 5: 1, 7: 1, 12: 1}, **line(6, 10),
        )
        grad_qkv, out_term = attention_back(
            grad_mid, w_out, attended, back_ins, back_scratch, heads, **line(7, 15)
        )
        terms["out"] = out_term.reshape(8, OUT // 2 * high, model_width)
        grad_x, gain_attn_term, qkv_term = product_scattered(
            grad_qkv, cols_qkv, True, extra=(normed_one, None), dtype=bf16,
            back=(grad_mid, x_rows, attn_gain),
            steps={3: 1, "early": 1, 5: 1, "late": 1, "latest": 1}, **line(9, 8),
        )
        gains = jnp.stack([gain_attn_term, gain_ffn_term]).reshape(2, groups, rows_here)
        gains = jnp.pad(jnp.moveaxis(gains, 0, 1), ((0, 0), (0, 6), (0, 0)))
        rest = line(10, CHUNKS + 2 * LAG - sums.tick)
        gate_rows, up_rows, qkv_rows, own_gains = tail(
            qkv_term.reshape(8, 8, 2 * high, -1), gains,
            {c: sums.done[c] for c in sums.done if c >= DOWN}, hidden_here, **rest,
        )
        straight = [n for n in range(CHUNKS) if n < DOWN or n >= DOWN + GATE_UP]
        weight_grads = finish([sums.done[n] for n in straight], gate_rows, up_rows, heads)
        shaped = tuple(rows.reshape(layer_input.shape) for rows in (result, grad_x))
        return shaped + tuple(weight_grads) + (own_gains[0], own_gains[1])

    unit_one = x_flat * inv_one
    inv_two = lax.rsqrt(jnp.mean(mid * mid, -1, keepdims=True) + EPS)
    unit_two = mid * inv_two
    normed_two = gather((unit_two * ffn_gain).astype(bf16))
    grad_all = gather(grad_out)
    gate_up = matmul_f32(normed_two, cols_gate_up)
    gate_proj, up_proj = gate_up[:, :hidden_here], gate_up[:, hidden_here:]
    sigmoid_gate = jax.nn.sigmoid(gate_proj)
    swish = gate_proj * sigmoid_gate
    hidden = (swish * up_proj).astype(bf16)
    gate_part = up_proj * sigmoid_gate * (1.0 + gate_proj * (1.0 - sigmoid_gate))
    down_term = over_tokens(hidden, grad_all).astype(bf16)
    grad_hidden = against_rows(grad_all, w_down)
    grad_gate_up = jnp.concatenate([grad_hidden * gate_part, grad_hidden * swish], 1).astype(bf16)
    grad_mid, gain_ffn_term = norm_back(
        grad_out.astype(f32), scatter(grad_gate_up, cols_gate_up, True), unit_two, inv_two, gain_ffn
    )
    grad_mid_low = gather(grad_mid.astype(bf16))
    grad_attended = against_rows(grad_mid_low, w_out).astype(bf16)
    grad_qkv = attend_back(grad_attended, back_ins, back_scratch, heads)
    grad_x, gain_attn_term = norm_back(
        grad_mid, scatter(grad_qkv, cols_qkv, True), unit_one, inv_one, gain_attn
    )

    def to_rows(term):
        return lax.all_to_all(
            term.astype(bf16).reshape(groups, rows_here, -1), "grp", 0, 0, tiled=True
        )

    def whole_rows(term):
        return jnp.moveaxis(term, 0, 1).reshape(rows_here, -1)

    def kv_rows(term):
        return jnp.sum(
            jnp.moveaxis(term, 0, 1).reshape(rows_here, kv_heads, copies, HD), 2
        ).reshape(rows_here, -1)

    gate_up_term = sum_over_sequences(to_rows(over_tokens(normed_two, grad_gate_up)))
    out_term = sum_over_sequences(over_tokens(attended, grad_mid_low).astype(bf16))
    qkv_term = sum_over_sequences(to_rows(over_tokens(normed_one, grad_qkv)))
    gain_total = lax.psum(jnp.stack([gain_attn_term, gain_ffn_term]), ("grp", "rep"))
    own_gains = lax.dynamic_slice_in_dim(gain_total, own_index * rows_here, rows_here, 1)
    return (
        (mid + scatter(hidden, w_down, False)).astype(bf16).reshape(layer_input.shape),
        grad_x.astype(bf16).reshape(layer_input.shape),
        whole_rows(qkv_term[..., :q_here]),
        kv_rows(qkv_term[..., q_here : q_here + HD]),
        kv_rows(qkv_term[..., q_here + HD :]),
        out_term,
        whole_rows(gate_up_term[..., :hidden_here]),
        whole_rows(gate_up_term[..., hidden_here:]),
        sum_over_sequences(down_term),
        own_gains[0],
        own_gains[1],
    )


def solution(mesh):
    tokens, table, rows, whole = P("rep", "grp", None), P("rep", None), P("grp", None), P()
    return jax.shard_map(
        on_device,
        mesh=mesh,
        in_specs=(tokens, tokens, table, table) + (rows,) * 7 + (whole,) * 2,
        out_specs=(tokens, tokens) + (rows,) * 7 + (P("grp"),) * 2,
        check_vma=False,
    )
```

```python
import functools

import jax
import jax.numpy as jnp
import numpy as np
from jax import lax
from jax.experimental import pallas as pl
from jax.experimental.pallas import tpu as pltpu
from jax.sharding import PartitionSpec as P

HD = 128
EPS = 1e-05
ROPE_BASE = 1000000.0
SCORE_SCALE = HD**-0.5
LOG2E = 1.4426950408889634
TO_EXP2 = SCORE_SCALE * LOG2E
NEG = -1e30

MESH = pl.DeviceIdType.MESH
f32 = jnp.float32
bf16 = jnp.bfloat16


def matmul_f32(first, second):
    return jnp.dot(first, second, preferred_element_type=f32)


def against_rows(first, second):
    return lax.dot_general(first, second, (((1,), (1,)), ((), ())), preferred_element_type=f32)


def over_tokens(first, second):
    return lax.dot_general(first, second, (((0,), (0,)), ((), ())), preferred_element_type=f32)


def turn_tables(length):
    half_size = HD // 2
    inverse = np.float32(ROPE_BASE) ** (-(np.arange(half_size, dtype=np.float32) * 2) / HD)
    angles = np.arange(length, dtype=np.float32)[:, None] * inverse.astype(np.float32)
    cosine, sine = np.cos(angles), np.sin(angles)
    tables = np.concatenate([cosine, cosine], -1), np.concatenate([-sine, sine], -1)
    return tuple(jnp.asarray(table.astype(np.float32)) for table in tables)


def norm_back(upstream, grad_normed, unit_rows, inv_root, gain):
    scaled = grad_normed * gain
    center_term = jnp.mean(scaled * unit_rows, -1, keepdims=True)
    return (
        upstream + inv_root * (scaled - unit_rows * center_term),
        jnp.sum(grad_normed * unit_rows, 0),
    )


def fold_lanes(values, op):
    out = values[:, :HD]
    for at in range(HD, values.shape[1], HD):
        out = op(out, values[:, at : at + HD])
    return out


def as_column(row):
    return jnp.broadcast_to(row, (HD, row.shape[1])).T[:, 0:1]


def as_row(column):
    return jnp.broadcast_to(column, (column.shape[0], HD)).T[0:1, :]


def attend_kernel(
    heads, cuts, block,
    order_ref, rows_hbm, weight_hbm, cos_ref, sin_ref, piece_ref,
    out_ref, q_ref, k_ref, v_ref, lse_ref, placed,
    scores, rows_ref, weight_ref, qkv_ref, sems,
):
    length = rows_ref.shape[0]
    cut = length // cuts
    blocks = length // block
    loads = [pltpu.make_async_copy(weight_hbm, weight_ref, sems.at[blocks])]
    for i in range(blocks):
        at = slice(i * block, (i + 1) * block)
        loads.append(pltpu.make_async_copy(rows_hbm.at[at, :], rows_ref.at[at, :], sems.at[i]))
    for load in loads:
        load.start()

    def place_cut(r, first):
        src = pl.ds(pl.multiple_of(r * cut, cut), cut)
        dst = pl.ds(pl.multiple_of(order_ref[0, first + r] * cut, cut), cut)
        cosine, sine = cos_ref[dst, :], sin_ref[dst, :]
        for h in range(heads + 1):
            part = qkv_ref[src, h * HD : (h + 1) * HD]
            turned = (part * cosine + pltpu.roll(part, HD // 2, 1) * sine).astype(bf16)
            if h < heads:
                q_ref[h, dst, :] = turned
            else:
                k_ref[dst, :] = turned
        v_ref[dst, :] = qkv_ref[src, (heads + 1) * HD :].astype(bf16)
        return first

    loads[0].wait()
    for i in range(blocks):
        loads[1 + i].wait()
        qkv_ref[...] = matmul_f32(rows_ref[i * block : (i + 1) * block, :], weight_ref[...])
        lax.fori_loop(0, block // cut, place_cut, i * (block // cut))

    def one_block(i, _):
        rows = pl.ds(pl.multiple_of(i * block, block), block)
        query = q_ref[:, rows, :].reshape(heads * block, HD)

        def score(j, high):
            cols = pl.ds(pl.multiple_of(j * block, block), block)
            tile = against_rows(query, k_ref[cols, :])
            scores[j] = tile
            return jnp.maximum(high, fold_lanes(tile, jnp.maximum))

        high = lax.fori_loop(0, i, score, jnp.full((heads * block, HD), NEG, f32))
        tile = against_rows(query, k_ref[rows, :])
        q_at = lax.broadcasted_iota(jnp.int32, (block, block), 0)
        k_at = lax.broadcasted_iota(jnp.int32, (block, block), 1)
        k_piece = piece_ref[0:1, rows].astype(f32)
        q_piece = as_column(k_piece)
        allowed = (k_at <= q_at) | ((q_piece != 0) & (q_piece == k_piece))
        tile = jnp.concatenate(
            [jnp.where(allowed, tile[h * block : (h + 1) * block], NEG) for h in range(heads)], 0
        )
        scores[i] = tile
        high = jnp.max(jnp.maximum(high, fold_lanes(tile, jnp.maximum)), 1, keepdims=True)

        def weigh(j, state):
            total, mixed = state
            cols = pl.ds(pl.multiple_of(j * block, block), block)
            prob = jnp.exp2((scores[j] - high) * TO_EXP2)
            total = total + fold_lanes(prob, jnp.add)
            return total, mixed + matmul_f32(prob.astype(bf16), v_ref[cols, :])

        zero = jnp.zeros((heads * block, HD), f32)
        total, mixed = lax.fori_loop(0, i + 1, weigh, (zero, zero))
        total = jnp.sum(total, 1, keepdims=True)
        mixed = (mixed / total).astype(bf16)
        log_total = high * TO_EXP2 + jnp.log2(total)
        for h in range(heads):
            placed[rows, h * HD : (h + 1) * HD] = mixed[h * block : (h + 1) * block]
            lse_ref[h : h + 1, rows] = as_row(log_total[h * block : (h + 1) * block])
        return 0

    lax.fori_loop(0, blocks, one_block, 0)

    def store_cut(r, _):
        dst = pl.ds(pl.multiple_of(r * cut, cut), cut)
        src = pl.ds(pl.multiple_of(order_ref[0, r] * cut, cut), cut)
        out_ref[dst, :] = placed[src, :]
        return 0

    lax.fori_loop(0, cuts, store_cut, 0)


def vmem_specs(count):
    return [pl.BlockSpec(memory_space=pltpu.VMEM)] * count


def attend(order, rows, weight, cosine, sine, piece, heads):
    length, width = rows.shape
    block = min(512, length)
    return pl.pallas_call(
        functools.partial(attend_kernel, heads, order.shape[1], block),
        out_shape=(
            jax.ShapeDtypeStruct((length, heads * HD), bf16),
            jax.ShapeDtypeStruct((heads, length, HD), bf16),
            jax.ShapeDtypeStruct((length, HD), bf16),
            jax.ShapeDtypeStruct((length, HD), bf16),
            jax.ShapeDtypeStruct((heads, length), f32),
            jax.ShapeDtypeStruct((length, heads * HD), bf16),
        ),
        in_specs=[pl.BlockSpec(memory_space=pltpu.SMEM)]
        + [pl.BlockSpec(memory_space=pl.ANY)] * 2
        + vmem_specs(3),
        out_specs=tuple(vmem_specs(6)),
        scratch_shapes=[
            pltpu.VMEM((length // block, heads * block, block), f32),
            pltpu.VMEM(rows.shape, bf16),
            pltpu.VMEM(weight.shape, bf16),
            pltpu.VMEM((block, weight.shape[1]), f32),
            pltpu.SemaphoreType.DMA((length // block + 1,)),
        ],
        compiler_params=pltpu.CompilerParams(vmem_limit_bytes=60 * 2**20),
        cost_estimate=pl.CostEstimate(
            flops=3 * heads * length * length * HD + 2 * length * width * weight.shape[1],
            bytes_accessed=10 * length * HD * heads * 4 + rows.size * 2,
            transcendentals=heads * length * length // 2,
        ),
    )(order, rows, weight, cosine, sine, piece)


DOWN, GATE_UP, OUT, QKV = 16, 32, 4, 8
CHUNKS = DOWN + GATE_UP + OUT + QKV
LAG = 3


def is_chunk(number):
    return 0 <= number < CHUNKS


def is_middle():
    rank = lax.axis_index("rep")
    return (rank == 1) | (rank == 2)


def is_end():
    rank = lax.axis_index("rep")
    return (rank == 0) | (rank == 3)


class NoLine:
    ticks = 0

    def signal(self, barrier):
        pass

    def greet(self, barrier, others):
        if others:
            pl.semaphore_wait(barrier, others)

    def start(self):
        pass

    def step(self, times=1):
        pass

    def end(self):
        pass


class Line:
    def __init__(self, first, ticks, picks, refs, outs, scratch):
        self.first, self.ticks, self.picks, self.refs, self.outs = first, ticks, picks, refs, outs
        (
            self.inward, self.across, self.own, self.pair, self.total, self.sems, self.local,
            self.carries,
        ) = scratch
        rank = lax.axis_index("rep")
        self.partner = {"rep": rank + 1 - 2 * (rank % 2)}
        self.peer = {"rep": 3 - rank}
        self.now = 0
        self.kept = []

    def signal(self, barrier):
        pl.semaphore_signal(barrier, inc=1, device_id=self.partner, device_id_type=MESH)

        @pl.when(is_middle())
        def _():
            pl.semaphore_signal(barrier, inc=1, device_id=self.peer, device_id_type=MESH)

    def greet(self, barrier, others):
        @pl.when(is_middle())
        def _():
            pl.semaphore_wait(barrier, others + 2)

        @pl.when(is_end())
        def _():
            pl.semaphore_wait(barrier, others + 1)

    def remote(self, hop, number, src, dst, device):
        return pltpu.make_async_remote_copy(
            src_ref=src, dst_ref=dst, send_sem=self.sems.at[0, hop, number],
            recv_sem=self.sems.at[1, hop, number], device_id=device, device_id_type=MESH,
        )

    def hops(self, number):
        tick = self.first + number
        term = pair = total = None
        if is_chunk(tick):
            which, pick = self.picks[tick]
            term = (
                lambda: self.remote(
                    0, number, pick(self.refs[which]), self.inward.at[number], self.partner
                ),
                lambda: pltpu.make_async_copy(
                    pick(self.refs[which]), self.own.at[tick % LAG], self.local.at[0, number]
                ),
            )
        if is_chunk(tick - LAG):
            held = self.pair.at[(tick - LAG) % (LAG + 1)]
            before = self.refs[f"pair{number}"] if number < LAG else held
            pair = (
                lambda: self.remote(1, number, before, self.across.at[number], self.peer),
                lambda: pltpu.make_async_copy(before, held, self.carries.at[0, number]),
            )
        if is_chunk(tick - 2 * LAG):
            held_total = self.total.at[(tick - 2 * LAG) % (LAG + 1)]
            done = self.refs[f"total{number}"] if number < LAG else held_total
            slot = self.outs[tick - 2 * LAG]
            total = (
                lambda: self.remote(2, number, done, slot, self.partner),
                lambda: pltpu.make_async_copy(done, slot, self.local.at[1, number]),
            )
        return term, pair, total

    def open(self, number):
        term, pair, total = self.hops(number)

        @pl.when(is_end())
        def _():
            if term:
                term[0]().start()

        @pl.when(is_middle())
        def _():
            if pair:
                pair[0]().start()
            if total:
                total[0]().start()
            if term:
                term[1]().start()
            if total:
                total[1]().start()
            if pair and number < LAG:
                pair[1]().start()

    def close(self, number):
        term, pair, total = self.hops(number)

        @pl.when(is_end())
        def _():
            if term:
                term[0]().wait_send()
            if total:
                total[0]().wait_recv()

        @pl.when(is_middle())
        def _():
            if total:
                total[0]().wait_send()
                total[1]().wait()
            if pair:
                pair[0]().wait_send()
                pair[0]().wait_recv()
            if term:
                term[0]().wait_recv()

    def add(self, number):
        term, pair, _ = self.hops(number)
        tick = self.first + number

        def sum_of(into, first, second):
            def one(g, _):
                into[g] = (first[g].astype(f32) + second[g].astype(f32)).astype(bf16)
                return 0

            lax.fori_loop(0, into.shape[0], one, 0)

        @pl.when(is_middle())
        def _():
            if pair:
                if number < LAG:
                    pair[1]().wait()
                before = tick - LAG
                sum_of(
                    self.total.at[before % (LAG + 1)], self.pair.at[before % (LAG + 1)],
                    self.across.at[number],
                )
            if term:
                term[1]().wait()
                sum_of(self.pair.at[tick % (LAG + 1)], self.own.at[tick % LAG], self.inward.at[number])

    def keep(self, number):
        tick = self.first + number
        which = number - (self.ticks - LAG)
        made = []
        if is_chunk(tick):
            made.append((self.pair.at[tick % (LAG + 1)], self.outs[f"pair{which}"], (1, which)))
        if is_chunk(tick - LAG):
            held = self.total.at[(tick - LAG) % (LAG + 1)]
            made.append((held, self.outs[f"total{which}"], (2, which)))
        copies = [
            lambda src=src, dst=dst, at=at: pltpu.make_async_copy(src, dst, self.carries.at[*at])
            for src, dst, at in made
        ]

        @pl.when(is_middle())
        def _():
            for copy in copies:
                copy().start()

        self.kept += copies

    def start(self):
        for number in range(LAG):
            self.open(number)

    def step(self, times=1):
        for _ in range(times):
            if self.now + LAG < self.ticks:
                self.settle()
                self.open(self.now + LAG - 1)

    def settle(self):
        self.close(self.now)
        self.add(self.now)
        if self.now >= self.ticks - LAG:
            self.keep(self.now)
        self.now += 1

    def end(self):
        while self.now + LAG < self.ticks:
            self.step()
        while self.now < self.ticks:
            self.settle()

        @pl.when(is_middle())
        def _():
            for copy in self.kept:
                copy().wait()


def line_slots(first, ticks):
    return [t - 2 * LAG for t in range(first, first + ticks) if is_chunk(t - 2 * LAG)]


class Sums:
    def __init__(self, shape):
        self.shape, self.tick, self.kept, self.done = shape, 0, {}, {}


def run(kernel, ins, outs, scratch, number, cost, sums=None, ticks=0, arrays=(), picks=None, vmem=58):
    ins, outs, scratch = list(ins), list(outs), list(scratch)
    counts = (len(ins), len(outs), len(scratch))
    first = sums.tick if ticks else 0
    names_in, names_out = [], []
    if ticks:
        for name, array in arrays:
            names_in.append(name)
            ins.append((array, pl.ANY))
        for which in range(LAG):
            for name, chunk_at in ((f"pair{which}", first - LAG), (f"total{which}", first - 2 * LAG)):
                if is_chunk(chunk_at + which):
                    names_in.append(name)
                    ins.append((sums.kept[name], pl.ANY))
        names_out = line_slots(first, ticks)
        after = first + ticks
        for which in range(LAG):
            for name, chunk_at in ((f"pair{which}", after - LAG), (f"total{which}", after - 2 * LAG)):
                if is_chunk(chunk_at + which):
                    names_out.append(name)
        outs += [(jax.ShapeDtypeStruct(sums.shape, bf16), pl.ANY)] * len(names_out)
        scratch += [
            pltpu.VMEM((ticks,) + sums.shape, bf16),
            pltpu.VMEM((ticks,) + sums.shape, bf16),
            pltpu.VMEM((LAG,) + sums.shape, bf16),
            pltpu.VMEM((LAG + 1,) + sums.shape, bf16),
            pltpu.VMEM((LAG + 1,) + sums.shape, bf16),
            pltpu.SemaphoreType.DMA((2, 3, ticks)),
            pltpu.SemaphoreType.DMA((2, ticks)),
            pltpu.SemaphoreType.DMA((3, LAG)),
        ]

    def body(*refs):
        in_refs, rest = refs[: len(ins)], refs[len(ins) :]
        out_refs, scratch_refs = rest[: len(outs)], rest[len(outs) :]
        line = NoLine()
        if ticks:
            line = Line(
                first, ticks, picks, dict(zip(names_in, in_refs[counts[0] :])),
                dict(zip(names_out, out_refs[counts[1] :])), scratch_refs[counts[2] :],
            )
        kernel(in_refs[: counts[0]], out_refs[: counts[1]], scratch_refs[: counts[2]], line)

    results = pl.pallas_call(
        body,
        out_shape=tuple(shape for shape, _ in outs),
        in_specs=[pl.BlockSpec(memory_space=space) for _, space in ins],
        out_specs=tuple(pl.BlockSpec(memory_space=space) for _, space in outs),
        scratch_shapes=scratch,
        compiler_params=pltpu.CompilerParams(
            vmem_limit_bytes=vmem * 2**20,
            **({} if number is None else {"collective_id": number, "has_side_effects": True}),
        ),
        cost_estimate=pl.CostEstimate(
            flops=cost[0], bytes_accessed=cost[1], transcendentals=cost[2]
        ),
    )(*[array for array, _ in ins])
    for name, result in zip(names_out, results[counts[1] :]):
        if name in line_slots(first, ticks):
            sums.done[name] = result
        else:
            sums.kept[name] = result
    if ticks:
        sums.tick += ticks
    return results[: counts[1]]


SMEM, VMEM, ANY = pltpu.SMEM, pltpu.VMEM, pl.ANY


def attend_back_kernel(
    heads, block, ins, outs, scratch, line, entered=False
):
    grad_ref, out_ref, q_ref, k_ref, v_ref, lse_ref, cos_ref, sin_ref, piece_ref, place_ref = ins
    (grad_qkv_ref,) = outs
    grads, centers, grad_q, placed = scratch
    if line.ticks and not entered:
        line.signal(pltpu.get_barrier_semaphore())
        line.greet(pltpu.get_barrier_semaphore(), 0)
        line.start()
    length = grad_ref.shape[0]
    blocks = length // block

    def take_block(i, _):
        rows = pl.ds(pl.multiple_of(i * block, block), block)
        position = lax.broadcasted_iota(jnp.int32, (block, length), 0) + i * block
        chosen = jnp.where(place_ref[...] == position, 1.0, 0.0).astype(bf16)
        taken = matmul_f32(chosen, grad_ref[...]).astype(bf16)
        for h in range(heads):
            grad = taken[:, h * HD : (h + 1) * HD]
            grads[h, rows, :] = grad
            product = grad.astype(f32) * out_ref[rows, h * HD : (h + 1) * HD].astype(f32)
            centers[h, rows, :] = jnp.broadcast_to(
                jnp.sum(product, 1, keepdims=True), (block, HD)
            )
        return 0

    lax.fori_loop(0, blocks, take_block, 0)
    line.step()
    grad_q[...] = jnp.zeros_like(grad_q)

    def key_block(j, _):
        cols = pl.ds(pl.multiple_of(j * block, block), block)
        key, value = k_ref[cols, :], v_ref[cols, :]

        def one(i, state, diagonal):
            grad_key, grad_value = state
            rows = pl.ds(pl.multiple_of(i * block, block), block)
            for h in range(heads):
                query, grad = q_ref[h, rows, :], grads[h, rows, :]
                log_total = lse_ref[h : h + 1, rows]
                center = centers[h, rows, :].T[0:1, :]
                prob = jnp.exp2(against_rows(key, query) * TO_EXP2 - log_total)
                if diagonal:
                    k_at = lax.broadcasted_iota(jnp.int32, (block, block), 0)
                    q_at = lax.broadcasted_iota(jnp.int32, (block, block), 1)
                    q_piece = piece_ref[0:1, cols].astype(f32)
                    k_piece = as_column(q_piece)
                    allowed = (k_at <= q_at) | ((q_piece != 0) & (q_piece == k_piece))
                    prob = jnp.where(allowed, prob, 0.0)
                grad_prob = against_rows(value, grad)
                grad_score = (prob * (grad_prob - center)).astype(bf16)
                grad_value = grad_value + matmul_f32(prob.astype(bf16), grad)
                grad_key = grad_key + matmul_f32(grad_score, query)
                grad_q[h, rows, :] += over_tokens(grad_score, key)
            return grad_key, grad_value

        zero = jnp.zeros((block, HD), f32)
        state = one(j, (zero, zero), True)
        grad_key, grad_value = lax.fori_loop(
            j + 1, blocks, functools.partial(one, diagonal=False), state
        )
        grad_key = grad_key * SCORE_SCALE
        grad_key = grad_key * cos_ref[cols, :] - pltpu.roll(grad_key, HD // 2, 1) * sin_ref[cols, :]
        placed[cols, heads * HD : (heads + 1) * HD] = grad_key.astype(bf16)
        placed[cols, (heads + 1) * HD :] = grad_value.astype(bf16)
        return 0

    for j in range(min(2, blocks - 1)):
        lax.fori_loop(j, j + 1, key_block, 0)
        line.step(2 - j)
    lax.fori_loop(min(2, blocks - 1), blocks, key_block, 0)

    def turn_back(i, _):
        rows = pl.ds(pl.multiple_of(i * block, block), block)
        for h in range(heads):
            grad = grad_q[h, rows, :] * SCORE_SCALE
            grad = grad * cos_ref[rows, :] - pltpu.roll(grad, HD // 2, 1) * sin_ref[rows, :]
            placed[rows, h * HD : (h + 1) * HD] = grad.astype(bf16)
        return 0

    lax.fori_loop(0, blocks, turn_back, 0)
    line.step()

    def store_block(i, _):
        rows = pl.ds(pl.multiple_of(i * block, block), block)
        place = as_column(place_ref[0:1, rows].astype(f32)).astype(jnp.int32)
        position = lax.broadcasted_iota(jnp.int32, (block, length), 1)
        chosen = jnp.where(place == position, 1.0, 0.0).astype(bf16)
        grad_qkv_ref[rows, :] = matmul_f32(chosen, placed[...]).astype(bf16)
        return 0

    lax.fori_loop(0, blocks, store_block, 0)
    line.end()


def attend_back_operands(order, out, query, key, value, lse, cosine, sine, piece, heads):
    length = out.shape[0]
    cut = length // order.shape[1]
    place = (order.reshape(-1, 1) * cut + jnp.arange(cut, dtype=order.dtype)).reshape(1, length)
    scratch = [
        pltpu.VMEM((heads, length, HD), bf16),
        pltpu.VMEM((heads, length, HD), f32),
        pltpu.VMEM((heads, length, HD), f32),
        pltpu.VMEM((length, (heads + 2) * HD), bf16),
    ]
    return [out, query, key, value, lse, cosine, sine, piece, place], scratch


def attend_back(grad, operands, scratch, heads):
    length = grad.shape[0]
    return run(
        functools.partial(attend_back_kernel, heads, min(512, length)),
        [(array, VMEM) for array in [grad] + operands],
        [(jax.ShapeDtypeStruct((length, (heads + 2) * HD), bf16), VMEM)],
        scratch,
        None,
        (8 * heads * length * length * HD, 14 * length * HD * heads * 4, heads * length * length // 2),
    )[0]


def place_in_group():
    me = lax.axis_index("grp")
    return me // 4, (me // 2) % 2, me % 2


def other(flip_y, flip_x, flip_core):
    y, x, core = place_in_group()
    return ((y + flip_y) % 2) * 4 + ((x + flip_x) % 2) * 2 + (core + flip_core) % 2


def chip_rows(flip_y, flip_x, rows):
    y, x, _ = place_in_group()
    first = (((y + flip_y) % 2) * 2 + (x + flip_x) % 2) * (2 * rows)
    return pl.ds(pl.multiple_of(first, 2 * rows), 2 * rows)


NEIGHBOURS = ((0, 0, 1), (0, 1, 0), (1, 0, 0))
EVERYONE = tuple((n // 4, (n // 2) % 2, n % 2) for n in range(1, 8))


def greet_group(line, flips=NEIGHBOURS, between=None):
    barrier = pltpu.get_barrier_semaphore()
    for flip in flips:
        pl.semaphore_signal(barrier, inc=1, device_id={"grp": other(*flip)}, device_id_type=MESH)
    line.signal(barrier)
    if between:
        between()
    line.greet(barrier, len(flips))


SIBLING, ALONG_X, ALONG_Y, ACROSS = (0, 0), (0, 1), (1, 0), (1, 1)


class Gather:
    TO_S, TO_X, TO_Y = (0, 0, 1), (0, 1, 0), (1, 0, 0)

    def __init__(self, rows, all_ref, sends, recvs):
        self.rows, self.all_ref, self.sends, self.recvs = rows, all_ref, sends, recvs
        self.started = []

    def copy(self, number, chip, core, part, target):
        first = other(*chip, core) * self.rows
        if part is None:
            where = pl.ds(pl.multiple_of(first, self.rows), self.rows)
        else:
            half = self.rows // 2
            where = pl.ds(pl.multiple_of(first + part * half, half), half)
        where = self.all_ref.at[where, :]
        return pltpu.make_async_remote_copy(
            src_ref=where, dst_ref=where, send_sem=self.sends.at[number],
            recv_sem=self.recvs.at[number], device_id={"grp": other(*target)}, device_id_type=MESH,
        )

    def send(self, *what):
        one = self.copy(*what)
        one.start()
        self.started.append(one)

    def landed(self, number, chip, core, part):
        self.copy(number, chip, core, part, self.TO_S).wait_recv()

    def send_own(self):
        self.send(1, SIBLING, 0, 1, self.TO_X)
        self.send(3, SIBLING, 0, 0, self.TO_Y)
        self.send(0, SIBLING, 0, None, self.TO_S)
        self.send(2, SIBLING, 0, 0, self.TO_X)
        self.send(4, SIBLING, 0, 1, self.TO_Y)

    def sibling(self):
        self.landed(0, SIBLING, 1, None)

    def relay(self):
        self.landed(1, ALONG_X, 0, 1)
        self.send(6, ALONG_X, 0, 1, self.TO_Y)
        self.landed(3, ALONG_Y, 0, 0)
        self.send(5, ALONG_Y, 0, 0, self.TO_X)
        self.send(7, ALONG_X, 0, 1, self.TO_S)
        self.send(8, ALONG_Y, 0, 0, self.TO_S)

    def pass_second(self):
        self.landed(2, ALONG_X, 0, 0)
        self.send(9, ALONG_X, 0, 0, self.TO_S)
        self.landed(4, ALONG_Y, 0, 1)
        self.send(10, ALONG_Y, 0, 1, self.TO_S)

    def along_x(self):
        self.landed(7, ALONG_X, 1, 1)
        self.landed(9, ALONG_X, 1, 0)

    def pass_across(self):
        self.landed(5, ACROSS, 0, 0)
        self.send(11, ACROSS, 0, 0, self.TO_S)
        self.landed(6, ACROSS, 0, 1)
        self.send(12, ACROSS, 0, 1, self.TO_S)

    def along_y(self):
        self.landed(8, ALONG_Y, 1, 0)
        self.landed(10, ALONG_Y, 1, 1)

    def across(self):
        self.landed(11, ACROSS, 1, 0)
        self.landed(12, ACROSS, 1, 1)

    def finish(self):
        for one in self.started:
            one.wait_send()


def gather_rows(rows, all_ref, sends, recvs, on_chip, line, then=None, final=True):
    rows_of = Gather(rows, all_ref, sends, recvs)
    rows_of.send_own()
    if then:
        then()
    rows_of.sibling()
    on_chip(*SIBLING)
    rows_of.relay()
    line.step(2)
    rows_of.pass_second()
    line.step(2)
    rows_of.along_x()
    on_chip(*ALONG_X)
    rows_of.pass_across()
    line.step(2)
    rows_of.along_y()
    on_chip(*ALONG_Y)
    rows_of.across()
    on_chip(*ACROSS)
    rows_of.finish()
    if final:
        line.end()
    else:
        line.step()


GATHER_COPIES = 13


def rms_normed(values, gain):
    return values * lax.rsqrt(jnp.mean(values * values, -1, keepdims=True) + EPS) * gain


class Moves:
    def __init__(self, sems):
        self.sems, self.count, self.open = sems, 0, []

    def start(self, src, dst):
        one = pltpu.make_async_copy(src, dst, self.sems.at[self.count])
        self.count += 1
        one.start()
        return one

    def later(self, src, dst):
        self.open.append(self.start(src, dst))

    def finish(self):
        for one in self.open:
            one.wait()


def gather_scratch(rows, width, moves):
    return [
        pltpu.VMEM((8 * rows, width), bf16),
        pltpu.SemaphoreType.DMA((GATHER_COPIES,)),
        pltpu.SemaphoreType.DMA((GATHER_COPIES,)),
        pltpu.SemaphoreType.DMA((moves,)),
    ]


def own_rows(rows):
    return pl.ds(pl.multiple_of(other(0, 0, 0) * rows, rows), rows)


def send_columns(pieces, sends, recvs, moves):
    copies = []
    for which, (rows_ref, width, there) in enumerate(pieces):
        for number, flip in enumerate(EVERYONE):
            target = other(*flip)
            cols = pl.ds(pl.multiple_of(target * width, width), width)
            one = pltpu.make_async_remote_copy(
                src_ref=rows_ref.at[:, cols], dst_ref=there,
                send_sem=sends.at[which, number], recv_sem=recvs.at[which, number],
                device_id={"grp": target}, device_id_type=MESH,
            )
            one.start()
            copies.append(one)
        mine = pl.ds(pl.multiple_of(other(0, 0, 0) * width, width), width)
        moves.later(rows_ref.at[:, mine], there)
    return copies


def gather_normed_kernel(ins, outs, scratch, line):
    x_ref, gain_ref = ins[:2]
    weights = ins[2:]
    all_ref, cols_ref = outs
    held, sends, recvs, sems, col_sends, col_recvs = scratch
    rows = x_ref.shape[0]
    moves = Moves(sems)

    def fill():
        held[own_rows(rows), :] = rms_normed(x_ref[...].astype(f32), gain_ref[...]).astype(bf16)

    greet_group(line, EVERYONE, fill)
    col_copies = []

    def send_weights():
        pieces, low = [], 0
        tall = weights[0].shape[0]
        there = pl.ds(pl.multiple_of(other(0, 0, 0) * tall, tall), tall)
        for weight in weights:
            width = weight.shape[1] // 8
            pieces.append((weight, width, cols_ref.at[there, low : low + width]))
            low += width
        col_copies.extend(send_columns(pieces, col_sends, col_recvs, moves))

    def on_chip(*chip):
        where = chip_rows(*chip, rows)
        moves.later(held.at[where, :], all_ref.at[where, :])

    gather_rows(rows, held, sends, recvs, on_chip, line, send_weights)
    for one in col_copies:
        one.wait()
    moves.finish()


def gather_normed(x, gain, weights, **line):
    rows, width = x.shape
    deep = sum(weight.shape[1] for weight in weights) // 8
    return run(
        gather_normed_kernel,
        [(x, VMEM), (gain, VMEM)] + [(weight, ANY) for weight in weights],
        [
            (jax.ShapeDtypeStruct((8 * rows, width), bf16), ANY),
            (jax.ShapeDtypeStruct((8 * weights[0].shape[0], deep), bf16), ANY),
        ],
        gather_scratch(rows, width, 4 + len(weights))
        + [pltpu.SemaphoreType.DMA((len(weights), 7))] * 2,
        line.pop("number"),
        (0, 150 * rows * width * 2, 0),
        **line,
    )


def columns_kernel(rows_here, ins, outs, scratch, line):
    cols_ref, packed_ref = outs
    sends, recvs, sems = scratch
    moves = Moves(sems)
    barrier = pltpu.get_barrier_semaphore()
    for flip in EVERYONE:
        pl.semaphore_signal(barrier, inc=1, device_id={"grp": other(*flip)}, device_id_type=MESH)
    pl.semaphore_wait(barrier, 7)
    first = pl.multiple_of(lax.axis_index("rep") * rows_here, rows_here)
    me = other(0, 0, 0)
    pieces, low = [], 0
    for weight in ins:
        width = weight.shape[1] // 8
        pieces.append(
            (weight.at[pl.ds(first, rows_here), :], width, cols_ref.at[me, :, low : low + width])
        )
        low += width
    copies = send_columns(pieces, sends, recvs, moves)
    low = 0
    for weight in ins:
        width = weight.shape[1] // 8
        for device in range(8):
            moves.later(
                weight.at[weight.shape[0] - packed_ref.shape[1] :, device * width : (device + 1) * width],
                packed_ref.at[device, :, low : low + width],
            )
        low += width
    for one in copies:
        one.wait()
    moves.finish()


def columns_of_some(weights, rows_here, rest, number):
    deep = sum(weight.shape[1] for weight in weights) // 8
    return run(
        functools.partial(columns_kernel, rows_here),
        [(weight, ANY) for weight in weights],
        [
            (jax.ShapeDtypeStruct((8, rows_here, deep), bf16), ANY),
            (jax.ShapeDtypeStruct((8, rest, deep), bf16), ANY),
        ],
        [pltpu.SemaphoreType.DMA((len(weights), 7))] * 2
        + [pltpu.SemaphoreType.DMA((9 * len(weights),))],
        number, (0, 50 * 8 * rows_here * deep, 0),
    )


def feed_forward_kernel(tile, ins, outs, scratch, line):
    mid_ref, gain_ref, grad_ref, spread_ref, rest_ref, w_down_ref = ins
    all_ref, hidden_ref, whole_ref, grad_gate_up_ref, down_ref = outs
    held, grads_held, sends, recvs, grad_sends, grad_recvs, sems = scratch[:7]
    weight, w_down, hidden, up_part, gate_part, grads, down = scratch[7:]
    rows = mid_ref.shape[0]
    inner = hidden.shape[1]
    moves = Moves(sems)
    planes, _, tall, _ = spread_ref.shape
    loads = [
        moves.start(spread_ref.at[z], weight.at[:, z * tall : (z + 1) * tall, :])
        for z in range(planes)
    ]
    loads.append(moves.start(rest_ref, weight.at[:, planes * tall :, :]))
    down_load = moves.start(w_down_ref, w_down)

    def fill():
        held[own_rows(rows), :] = rms_normed(mid_ref[...], gain_ref[...]).astype(bf16)
        grads_held[own_rows(rows), :] = grad_ref[...]

    greet_group(line, between=fill)
    first = Gather(rows, held, sends, recvs)
    second = Gather(rows, grads_held, grad_sends, grad_recvs)
    stored = []

    def forward(*chip):
        where = chip_rows(*chip, rows)
        moves.later(held.at[where, :], all_ref.at[where, :])

        def column(t, _):
            cols = pl.ds(pl.multiple_of(t * tile, tile), tile)
            up_cols = pl.ds(pl.multiple_of(inner + t * tile, tile), tile)
            lhs = held[where, :]
            gate = matmul_f32(lhs, weight[:, :, cols].reshape(-1, tile))
            up = matmul_f32(lhs, weight[:, :, up_cols].reshape(-1, tile))
            sigma = 1.0 / (1.0 + jnp.exp(-gate))
            swish = gate * sigma
            hidden[where, cols] = (swish * up).astype(bf16)
            up_part[where, cols] = swish.astype(bf16)
            gate_part[where, cols] = (up * sigma * (1.0 + gate * (1.0 - sigma))).astype(bf16)
            return 0

        lax.fori_loop(0, inner // tile, column, 0)
        moves.later(hidden.at[where, :], hidden_ref.at[where, :])

    def backward(*chip):
        where = chip_rows(*chip, rows)
        slot = len(stored) % 2
        if len(stored) >= 2:
            stored[len(stored) - 2].wait()

        def column(t, _):
            cols = pl.ds(pl.multiple_of(t * tile, tile), tile)
            up_cols = pl.ds(pl.multiple_of(inner + t * tile, tile), tile)
            incoming = grads_held[where, :]
            grad_hidden = against_rows(incoming, w_down[cols, :])
            grads[slot, :, cols] = (grad_hidden * gate_part[where, cols].astype(f32)).astype(bf16)
            grads[slot, :, up_cols] = (grad_hidden * up_part[where, cols].astype(f32)).astype(bf16)
            term = over_tokens(hidden[where, cols], incoming)
            if chip == SIBLING:
                down[cols, :] = term
            elif chip == ACROSS:
                weight[t] = (down[cols, :] + term).astype(bf16)
            else:
                down[cols, :] += term
            return 0

        lax.fori_loop(0, inner // tile, column, 0)
        stored.append(moves.start(grads.at[slot], grad_gate_up_ref.at[where, :]))

    first.send_own()
    for one in loads:
        one.wait()
    whole = moves.start(weight, whole_ref)
    first.sibling()
    forward(*SIBLING)
    first.relay()
    first.pass_second()
    second.send_own()
    first.along_x()
    forward(*ALONG_X)
    first.pass_across()
    first.along_y()
    forward(*ALONG_Y)
    second.relay()
    first.across()
    forward(*ACROSS)
    down_load.wait()
    second.sibling()
    backward(*SIBLING)
    second.pass_second()
    second.along_x()
    backward(*ALONG_X)
    second.pass_across()
    second.along_y()
    backward(*ALONG_Y)
    second.across()
    whole.wait()
    backward(*ACROSS)
    moves.later(weight.at[: inner // tile], down_ref)
    first.finish()
    second.finish()
    for one in stored[-2:]:
        one.wait()
    moves.finish()


def feed_forward(mid, gain, grad, spread, rest, w_down, **line):
    rows, width = mid.shape
    inner = w_down.shape[0]
    weight = (8, width // 8, 2 * inner)
    return run(
        functools.partial(feed_forward_kernel, weight[1]),
        [(mid, VMEM), (gain, VMEM), (grad, VMEM), (spread, ANY), (rest, ANY), (w_down, ANY)],
        [
            (jax.ShapeDtypeStruct((8 * rows, width), bf16), ANY),
            (jax.ShapeDtypeStruct((8 * rows, inner), bf16), ANY),
            (jax.ShapeDtypeStruct(weight, bf16), ANY),
            (jax.ShapeDtypeStruct((8 * rows, 2 * inner), bf16), ANY),
            (jax.ShapeDtypeStruct((inner // weight[1], weight[1], width), bf16), ANY),
        ],
        [pltpu.VMEM((8 * rows, width), bf16)] * 2
        + [pltpu.SemaphoreType.DMA((GATHER_COPIES,))] * 4
        + [pltpu.SemaphoreType.DMA((20,))]
        + [pltpu.VMEM(weight, bf16), pltpu.VMEM(w_down.shape, bf16)]
        + [pltpu.VMEM((8 * rows, inner), bf16)] * 3
        + [
            pltpu.VMEM((2, 2 * rows, 2 * inner), bf16),
            pltpu.VMEM(w_down.shape, f32),
        ],
        line.pop("number"),
        (64 * rows * width * inner, 300 * rows * width * 2, 8 * rows * inner),
        vmem=63,
        **line,
    )


def attention_back_kernel(heads, block, ins, outs, scratch, line):
    grad_ref, w_ref, attended_ref = ins[:3]
    grad_qkv_ref, out_term_ref = outs
    held, sends, recvs, sems, total, grad_attended_ref = scratch[:6]
    rows = grad_ref.shape[0]
    moves = Moves(sems)
    greet_group(line)
    line.start()
    held[own_rows(rows), :] = grad_ref[...].astype(bf16)

    def on_chip(*chip):
        where = chip_rows(*chip, rows)
        incoming = held[where, :]
        grad_attended_ref[where, :] = against_rows(incoming, w_ref[...]).astype(bf16)
        term = over_tokens(attended_ref[where, :], incoming)
        if chip == SIBLING:
            total[...] = term
        elif chip == ACROSS:
            out_term_ref[...] = (total[...] + term).astype(bf16)
        else:
            total[...] += term

    gather_rows(rows, held, sends, recvs, on_chip, line, final=False)
    moves.finish()
    attend_back_kernel(
        heads, block, (grad_attended_ref,) + tuple(ins[3:]), (grad_qkv_ref,), scratch[6:], line,
        entered=True,
    )


def attention_back(grad, w_out, attended, back_ins, back_scratch, heads, **line):
    rows, width = grad.shape
    length = 8 * rows
    return run(
        functools.partial(attention_back_kernel, heads, min(512, length)),
        [(array, VMEM) for array in [grad, w_out, attended] + back_ins],
        [
            (jax.ShapeDtypeStruct((length, (heads + 2) * HD), bf16), VMEM),
            (jax.ShapeDtypeStruct(w_out.shape, bf16), VMEM),
        ],
        gather_scratch(rows, width, 1)
        + [pltpu.VMEM(w_out.shape, f32), pltpu.VMEM(attended.shape, bf16)]
        + back_scratch,
        line.pop("number"),
        (
            32 * rows * width * w_out.shape[0] + 8 * heads * length * length * HD,
            250 * rows * width * 2, heads * length * length // 2,
        ),
        **line,
    )


class WeightTerm:
    def __init__(self, rows_ref, columns_ref, term_ref, scratch):
        self.rows_ref, self.columns_ref, self.term_ref = rows_ref, columns_ref, term_ref
        self.loaded, self.flipped, self.ready, self.sems = scratch
        self.tile = self.loaded.shape[2]
        for number in (0, 1):
            self.load(number).start()

    def load(self, number):
        cols = slice(number * self.tile, (number + 1) * self.tile)
        return pltpu.make_async_copy(
            self.rows_ref.at[:, cols], self.loaded.at[number % 2], self.sems.at[0, number % 2]
        )

    def store(self, number):
        return pltpu.make_async_copy(
            self.ready.at[number % 2], self.term_ref.at[number], self.sems.at[1, number % 2]
        )

    def work(self, numbers):
        for number in numbers:
            at = number % 2
            self.load(number).wait()
            if number >= 2:
                self.store(number - 2).wait()
            width = self.columns_ref.shape[1]
            step = min(256, width)
            self.flipped[...] = self.loaded[at].T

            def column(t, _):
                cols = pl.ds(pl.multiple_of(t * step, step), step)
                term = matmul_f32(self.flipped[...], self.columns_ref[:, cols])
                self.ready[at, :, cols] = term.astype(bf16)
                return 0

            lax.fori_loop(0, width // step, column, 0)
            self.store(number).start()
            if number + 2 < 8:
                self.load(number + 2).start()

    def finish(self):
        for number in (6, 7):
            self.store(number).wait()


UNITS = (
    (ACROSS, 0), (ACROSS, 1), (ALONG_X, 0), (ALONG_Y, 1), (ALONG_X, 1), (ALONG_Y, 0),
    (SIBLING, 0), (SIBLING, 1),
)


def scatter_kernel(turned, extra, after, steps, ins, outs, scratch, line):
    out_ref = outs[0] if after == "base" else scratch[-4]
    finals = ins[len(ins) - {"base": 1, "cast": 1, "back": 3}[after] :]
    part, to_s, from_s, to_link, relay, last, sends, recvs = scratch[:8]
    a_ref, b_ref, load_sems = scratch[-3:]
    rows, width = out_ref.shape
    half = width // 2
    _, _, core = place_in_group()
    loading = {}

    def load(name, src, dst):
        loading[name] = pltpu.make_async_copy(src, dst, load_sems.at[len(loading)])
        loading[name].start()

    def load_weight(h):
        where = (slice(h * half, (h + 1) * half), slice(None))
        where = where if turned else where[::-1]
        load(h, ins[1].at[where], b_ref.at[where])

    def load_rows(chip):
        where = chip_rows(*chip, rows)
        load(chip, ins[0].at[where, :], a_ref.at[where, :])

    load_weight(0)
    load_rows(ACROSS)
    load_weight(1)
    for chip in (ALONG_X, ALONG_Y, SIBLING):
        load_rows(chip)
    greet_group(line)
    line.start()
    if extra:
        columns_ref = a_ref
        if extra == "loaded":
            columns_ref = scratch[12]
            load("columns", ins[3], columns_ref)
        term = WeightTerm(ins[2], columns_ref, outs[-1], scratch[8:12])
    own_at = pl.multiple_of(core * rows, rows)
    other_at = pl.multiple_of((1 - core) * rows, rows)
    to_sib, to_x, to_y = (0, 0, 1), (0, 1, 0), (1, 0, 0)
    started = []

    def ready(*names):
        for name in names:
            if name in loading:
                loading.pop(name).wait()
                loading[name, "done"] = None

    def send(number, src, dst, target):
        one = pltpu.make_async_remote_copy(
            src_ref=src, dst_ref=dst, send_sem=sends.at[number], recv_sem=recvs.at[number],
            device_id={"grp": other(*target)}, device_id_type=MESH,
        )
        one.start()
        started.append(one)

    def landed(number, where):
        pltpu.make_async_remote_copy(
            src_ref=where, dst_ref=where, send_sem=sends.at[number], recv_sem=recvs.at[number],
            device_id={"grp": other(0, 0, 1)}, device_id_type=MESH,
        ).wait_recv()

    def make(n):
        chip, h = UNITS[n]
        ready(h, chip)
        lhs = a_ref[chip_rows(*chip, rows), :]
        cols = slice(h * half, (h + 1) * half)
        if turned:
            part[n % 2] = against_rows(lhs, b_ref[cols, :])
        else:
            part[n % 2] = matmul_f32(lhs, b_ref[:, cols])
        to_s[n] = part[n % 2, pl.ds(other_at, rows), :].astype(bf16)
        send(n, to_s.at[n], from_s.at[n], to_sib)

    def own(n):
        landed(n, from_s.at[n])
        return part[n % 2, pl.ds(own_at, rows), :] + from_s[n].astype(f32)

    def finish(n):
        _, h = UNITS[n]
        if n < 2:
            to_link[n] = own(n).astype(bf16)
            send(8 + n, to_link.at[n], relay.at[n], (to_x, to_y)[n])
        elif n < 4:
            to_link[n] = own(n).astype(bf16)
            send(8 + n, to_link.at[n], last.at[(None, None, 0, 3)[n]], (to_x, to_y)[n - 2])
        elif n < 6:
            total = own(n)
            landed(8 + h, relay.at[h])
            to_link[n] = (total + relay[h].astype(f32)).astype(bf16)
            send(8 + n, to_link.at[n], last.at[(1, 2)[n - 4]], (to_x, to_y)[n - 4])
        else:
            cols = slice(h * half, (h + 1) * half)
            if after == "back":
                out_ref[:, cols] = own(n)
            else:
                out_ref[:, cols] = own(n) + finals[0][:, cols].astype(f32)
        line.step(steps.get(n, 0))

    def work(numbers, point):
        if extra:
            ready("columns")
            if columns_ref is a_ref:
                ready(*(chip for chip, _ in UNITS))
            term.work(numbers)
        line.step(steps.get(point, 0))

    make(0)
    make(1)
    finish(0)
    make(2)
    finish(1)
    make(3)
    finish(2)
    make(4)
    finish(3)
    make(5)
    work((0, 1), "early")
    finish(4)
    make(6)
    finish(5)
    make(7)
    finish(6)
    finish(7)
    work((2, 3), "late")
    work((4, 5), "later")
    work((6, 7), "latest")
    for number, slot, h in ((10, 0, 0), (11, 3, 1), (12, 1, 1), (13, 2, 0)):
        cols = slice(h * half, (h + 1) * half)
        landed(number, last.at[slot])
        out_ref[:, cols] += last[slot].astype(f32)
        line.step(steps.get(number, 0))
    if after == "cast":
        outs[0][...] = out_ref[...].astype(outs[0].dtype)
    if after == "back":
        upstream_ref, rows_ref, gain_ref = finals
        some = min(64, rows)

        def norm_rows(number, gain_term):
            at = pl.ds(pl.multiple_of(number * some, some), some)
            values, incoming = rows_ref[at, :].astype(f32), out_ref[at, :]
            inv = lax.rsqrt(jnp.mean(values * values, -1, keepdims=True) + EPS)
            grad, gain_part = norm_back(
                upstream_ref[at, :].astype(f32), incoming, values * inv, inv, gain_ref[...]
            )
            outs[0][at, :] = grad.astype(outs[0].dtype)
            return gain_term + gain_part[None, :]

        outs[1][...] = lax.fori_loop(0, rows // some, norm_rows, jnp.zeros((1, width), f32))
    for one in started:
        one.wait_send()
    if extra:
        term.finish()
    line.end()


def product_scattered(
    a, b, turned, extra=None, base=None, back=None, dtype=f32, steps=None, **line
):
    length, depth = a.shape
    width = b.shape[0] if turned else b.shape[1]
    rows = length // 8
    ins = [(a, ANY), (b, ANY)]
    outs = [(jax.ShapeDtypeStruct((rows, width), dtype), VMEM)]
    after = "back" if back else "base" if dtype == f32 else "cast"
    if back:
        outs.append((jax.ShapeDtypeStruct((1, width), f32), VMEM))
    piece = (rows, width // 2)
    scratch = [
        pltpu.VMEM((2, 2 * rows, width // 2), f32),
        pltpu.VMEM((8,) + piece, bf16),
        pltpu.VMEM((8,) + piece, bf16),
        pltpu.VMEM((6,) + piece, bf16),
        pltpu.VMEM((2,) + piece, bf16),
        pltpu.VMEM((4,) + piece, bf16),
        pltpu.SemaphoreType.DMA((14,)),
        pltpu.SemaphoreType.DMA((14,)),
    ]
    flops, kind = 2 * length * depth * width, None
    if extra:
        first, second = extra
        kind = "own" if second is None else "loaded"
        ins.append((first, ANY))
        columns = a if second is None else second
        tall = first.shape[1] // 8
        outs.append((jax.ShapeDtypeStruct((8, tall, columns.shape[1]), bf16), ANY))
        scratch += [
            pltpu.VMEM((2, length, tall), bf16),
            pltpu.VMEM((tall, length), bf16),
            pltpu.VMEM((2, tall, columns.shape[1]), bf16),
            pltpu.SemaphoreType.DMA((2, 2)),
        ]
        if second is not None:
            ins.append((second, ANY))
            scratch.append(pltpu.VMEM(second.shape, bf16))
        flops += 2 * length * first.shape[1] * columns.shape[1]
    ins += [(array, VMEM) for array in (back or (base,))]
    if after != "base":
        scratch.append(pltpu.VMEM((rows, width), f32))
    scratch += [
        pltpu.VMEM(a.shape, bf16), pltpu.VMEM(b.shape, bf16), pltpu.SemaphoreType.DMA((7,))
    ]
    return run(
        functools.partial(scatter_kernel, turned, kind, after, steps or {}), ins, outs, scratch,
        line.pop("number"), (flops, 150 * rows * width * 2, 0), vmem=61, **line,
    )


def tail_kernel(ready, later, ins, outs, scratch, line):
    qkv_ref, gains_ref = ins[:2]
    chunk_refs = dict(zip(ready, ins[2:]))
    gate_ref, up_ref, qkv_rows_ref, gains_out_ref = outs
    from_group, mine, from_rep, sends, recvs, chunk_sems, local = scratch
    me, rank = other(0, 0, 0), lax.axis_index("rep")
    inner = gate_ref.shape[1] // 8
    part = qkv_ref.shape[-1]
    high = line.outs[later[0]].shape[1]
    barrier = pltpu.get_barrier_semaphore()
    for flip in range(1, 4):
        pl.semaphore_signal(
            barrier, inc=1, device_id={"rep": (rank + flip) % 4}, device_id_type=MESH
        )
    for flip in EVERYONE:
        pl.semaphore_signal(barrier, inc=1, device_id={"grp": other(*flip)}, device_id_type=MESH)
    pl.semaphore_wait(barrier, 10)
    waits, moves = [], Moves(local)
    line.refs["qkv"] = qkv_rows_ref

    def send(kind, number, src, dst, device):
        return pltpu.make_async_remote_copy(
            src_ref=src, dst_ref=dst, send_sem=sends.at[kind, number],
            recv_sem=recvs.at[kind, number], device_id=device, device_id_type=MESH,
        )

    own_qkv = qkv_rows_ref.at[me // 4, :, :, pl.ds(pl.multiple_of((me % 4) * part, part), part)]
    qkv_copies, gain_copies = [], []
    for number, flip in enumerate(EVERYONE):
        target = other(*flip)
        qkv_copies.append(send(0, number, qkv_ref.at[target], own_qkv, {"grp": target}))
        qkv_copies[-1].start()
    moves.later(qkv_ref.at[me], own_qkv)
    line.start()
    for number, flip in enumerate(EVERYONE):
        target = other(*flip)
        gain_copies.append(
            send(1, number, gains_ref.at[target], from_group.at[me], {"grp": target})
        )
        gain_copies[-1].start()
    from_group[me] = gains_ref[me]

    def spread(chunk):
        src = chunk_refs[chunk] if chunk in chunk_refs else line.outs[chunk]
        number = chunk - DOWN
        rows = slice(number // 2 * high, (number // 2 + 1) * high)
        dst = (gate_ref, up_ref)[number % 2]
        there = dst.at[rows, pl.ds(pl.multiple_of(me * inner, inner), inner)]
        for flip in EVERYONE:
            target = other(*flip)
            pltpu.make_async_remote_copy(
                src_ref=src.at[target], dst_ref=there, send_sem=chunk_sems.at[0, number],
                recv_sem=chunk_sems.at[1, number], device_id={"grp": target}, device_id_type=MESH,
            ).start()
        moves.later(src.at[me], there)
        seven = dst.at[rows, : 7 * inner]
        waits.append(
            pltpu.make_async_remote_copy(
                src_ref=seven, dst_ref=seven, send_sem=chunk_sems.at[0, number],
                recv_sem=chunk_sems.at[1, number], device_id={"grp": other(0, 0, 1)},
                device_id_type=MESH,
            )
        )

    for chunk in ready:
        spread(chunk)
    for one in gain_copies:
        one.wait()
    mine[rank] = sum(from_group[g] for g in range(8))
    rep_copies = []
    for step in range(1, 4):
        target = (rank + step) % 4
        rep_copies.append(
            send(2, step, mine.at[rank], from_rep.at[step], {"rep": target})
        )
        rep_copies[-1].start()
    for step, one in zip(range(1, 4), rep_copies):
        one.wait()
        mine[(rank + 4 - step) % 4] = from_rep[step]
    gains_out_ref[...] = (mine[0] + mine[1]) + (mine[2] + mine[3])
    for settled in range(line.ticks - LAG):
        if line.first + settled + LAG == CHUNKS - QKV:
            for one in qkv_copies:
                one.wait()
            moves.open.pop(0).wait()
        line.step()
        chunk = line.first + settled - 2 * LAG
        if chunk in later:
            spread(chunk)
    line.end()
    for one in waits:
        one.wait_send()
        one.wait_recv()
    moves.finish()


def tail(qkv_term, gains, chunks, inner, number, sums, ticks, arrays, picks):
    first = sums.tick
    ready = sorted(chunks)
    later = [c for c in line_slots(first, ticks) if c < DOWN + GATE_UP]
    _, high, width = sums.shape
    wide = jax.ShapeDtypeStruct((GATE_UP // 2 * high, 8 * inner), bf16)
    moved = jax.ShapeDtypeStruct((2, 8, 2 * high, 2 * width), bf16)
    picks = dict(picks)
    for n in range(QKV):
        where = (
            n // 4, slice(None), slice(n // 2 % 2 * high, (n // 2 % 2 + 1) * high),
            slice(n % 2 * width, (n % 2 + 1) * width),
        )
        picks[CHUNKS - QKV + n] = ("qkv", lambda ref, where=where: ref.at[where])
    return run(
        functools.partial(tail_kernel, ready, later),
        [(qkv_term, ANY), (gains, VMEM)] + [(chunks[c], ANY) for c in ready],
        [(wide, ANY), (wide, ANY), (moved, ANY), (jax.ShapeDtypeStruct(gains.shape[1:], f32), VMEM)],
        [
            pltpu.VMEM(gains.shape, f32),
            pltpu.VMEM((4,) + gains.shape[1:], f32),
            pltpu.VMEM((4,) + gains.shape[1:], f32),
            pltpu.SemaphoreType.DMA((3, 7)),
            pltpu.SemaphoreType.DMA((3, 7)),
            pltpu.SemaphoreType.DMA((2, GATE_UP)),
            pltpu.SemaphoreType.DMA((1 + GATE_UP,)),
        ],
        number, (0, 200 * 8 * high * width * 2, 0), sums=sums, ticks=ticks, arrays=arrays, picks=picks,
    )


def finish_kernel(heads, *refs):
    chunks, rest = refs[: DOWN + OUT + QKV], refs[DOWN + OUT + QKV :]
    gate_rows, up_rows = rest[:2]
    kept = [
        pltpu.make_async_copy(src, dst, rest[-1].at[number])
        for number, (src, dst) in enumerate(zip(rest[2:4], rest[11:13]))
    ]
    for one in kept:
        one.start()
    query, key, value, out, gate, up, down = rest[4:11]
    low, wide, load_sems, store_sems = rest[13:17]
    _, high, width = chunks[0].shape
    depth = low.shape[0]

    def half(number):
        return slice(number * high, (number + 1) * high)

    def side(number):
        return slice(number * width, (number + 1) * width)

    jobs = []
    for n, ref in enumerate(chunks[:DOWN]):
        jobs.append((ref, [(slice(0, width), down.at[n // 2, :, :, side(n % 2)])]))
    for ref, into in ((gate_rows, gate), (up_rows, up)):
        for low_col in range(0, ref.shape[2], low.shape[3]):
            for number in (0, 1):
                where = (slice(None), half(number), slice(low_col, low_col + low.shape[3]))
                jobs.append((ref.at[where], [(slice(0, low.shape[3]), into.at[where])]))
    for n, ref in enumerate(chunks[DOWN : DOWN + OUT]):
        jobs.append((ref, [(slice(0, width), out.at[:, half(n // 2), side(n % 2)])]))
    part = (heads + 2) * HD
    for n, ref in enumerate(chunks[DOWN + OUT :]):
        stores = []
        for place in range(width // part):
            at, device = place * part, (n // 4 * 2 + n % 2) * (width // part) + place
            for into, first, size in (
                (query, 0, heads * HD), (key, heads * HD, HD), (value, (heads + 1) * HD, HD)
            ):
                there = into.at[:, half(n // 2 % 2), device * size : (device + 1) * size]
                stores.append((slice(at + first, at + first + size), there))
        jobs.append((ref, stores))

    def load(number):
        at, ref = number % depth, jobs[number][0]
        return pltpu.make_async_copy(ref, low.at[at, :, :, : ref.shape[2]], load_sems.at[at])

    def stores(number):
        at = number % depth
        return [
            pltpu.make_async_copy(wide.at[at, :, :, cols], into, store_sems.at[at, which])
            for which, (cols, into) in enumerate(jobs[number][1])
        ]

    for number in range(depth - 1):
        load(number).start()
    for number in range(len(jobs)):
        if number + depth - 1 < len(jobs):
            load(number + depth - 1).start()
        load(number).wait()
        if number >= depth:
            for one in stores(number - depth):
                one.wait()

        def cast(g, _, at=number % depth, cols=slice(0, jobs[number][0].shape[2])):
            wide[at, g, :, cols] = low[at, g, :, cols].astype(f32)
            return 0

        lax.fori_loop(0, low.shape[1], cast, 0)
        for one in stores(number):
            one.start()
    for number in range(len(jobs) - depth, len(jobs)):
        for one in stores(number):
            one.wait()
    for one in kept:
        one.wait()


def finish(chunks, gate_rows, up_rows, others, heads):
    eight, high, width = chunks[0].shape
    width = 2 * width
    rows, wide = gate_rows.shape

    def split(columns):
        return jax.ShapeDtypeStruct((eight, rows // eight, columns), f32)

    shapes = [split(columns) for columns in (8 * heads * HD, 8 * HD, 8 * HD, width, wide, wide)]
    shapes.append(jax.ShapeDtypeStruct((DOWN // 2, eight, high, width), f32))
    depth = 12
    results = pl.pallas_call(
        functools.partial(finish_kernel, heads),
        out_shape=tuple(shapes) + tuple(jax.ShapeDtypeStruct(x.shape, x.dtype) for x in others),
        in_specs=[pl.BlockSpec(memory_space=pl.ANY)] * (len(chunks) + 4),
        out_specs=tuple([pl.BlockSpec(memory_space=pl.ANY)] * 9),
        scratch_shapes=[
            pltpu.VMEM((depth, eight, high, width), bf16),
            pltpu.VMEM((depth, eight, high, width), f32),
            pltpu.SemaphoreType.DMA((depth,)),
            pltpu.SemaphoreType.DMA((depth, 12)),
            pltpu.SemaphoreType.DMA((2,)),
        ],
        compiler_params=pltpu.CompilerParams(vmem_limit_bytes=60 * 2**20),
        cost_estimate=pl.CostEstimate(
            flops=0, bytes_accessed=3 * CHUNKS * eight * high * width, transcendentals=0
        ),
    )(
        *chunks, gate_rows.reshape(eight, rows // eight, wide),
        up_rows.reshape(eight, rows // eight, wide), *others,
    )
    flat = [result.reshape(rows, -1) for result in results[:6]]
    return flat + [results[6].reshape(-1, width)], results[7:]


def sum_over_sequences(term):
    return lax.psum(term, "rep").astype(f32)


def on_device(
    layer_input,
    cotangent,
    cut_order,
    piece_ids,
    w_query,
    w_key,
    w_value,
    w_out,
    w_gate,
    w_up,
    w_down,
    gain_attn,
    gain_ffn,
):
    groups = lax.axis_size("grp")
    reps = lax.axis_size("rep")
    own_index = lax.axis_index("grp")
    _, local_rows, model_width = layer_input.shape
    length = piece_ids.shape[1]
    rows_here = w_query.shape[0]
    q_width = w_query.shape[1]
    kv_heads = w_key.shape[1] // HD
    heads = q_width // HD // groups
    copies = groups // kv_heads
    hidden_here = w_down.shape[0]
    cosine, sine = turn_tables(length)

    near = groups == 8 and reps == 4 and copies == 1 and 2 * hidden_here == model_width

    def gather(rows):
        return lax.all_gather(rows, "grp", axis=0, tiled=True)

    def scatter(first, second, turned):
        term = against_rows(first, second) if turned else matmul_f32(first, second)
        return lax.psum_scatter(
            term.astype(bf16), "grp", scatter_dimension=0, tiled=True
        ).astype(f32)

    def to_columns(parts):
        return lax.all_to_all(parts, "grp", 1, 0, tiled=True).reshape(-1, parts.shape[-1])

    def per_group(weight):
        return weight.reshape(rows_here, groups, -1)

    def per_kv_head(weight):
        return jnp.repeat(weight.reshape(rows_here, kv_heads, HD), copies, axis=1)

    x_rows = layer_input.reshape(local_rows, model_width)
    x_flat = x_rows.astype(f32)
    inv_one = lax.rsqrt(jnp.mean(x_flat * x_flat, -1, keepdims=True) + EPS)
    unit_one = x_flat * inv_one
    attn_gain, ffn_gain = gain_attn.reshape(1, -1), gain_ffn.reshape(1, -1)
    if near:
        share = rows_here // (4 * reps) * 3
        spread, rest = columns_of_some((w_gate, w_up), share, rows_here - reps * share, 11)
        x_first, spread, rest = lax.optimization_barrier((x_rows, spread, rest))
        spread = lax.all_gather(spread, "rep", axis=0)
        normed_one, cols_qkv = gather_normed(
            x_first, attn_gain, (w_query, w_key, w_value), number=1
        )
        rest, normed_one = lax.optimization_barrier((rest, normed_one))
        rest = lax.all_to_all(rest, "grp", 0, 0, tiled=True)
    else:
        normed_one = gather(rms_normed(x_flat, attn_gain).astype(bf16))
        cols_qkv = to_columns(
            jnp.concatenate([per_group(w_query), per_kv_head(w_key), per_kv_head(w_value)], -1)
        )
        cols_gate_up = to_columns(jnp.concatenate([per_group(w_gate), per_group(w_up)], -1))
    attended, query, key, value, lse, attended_placed = attend(
        cut_order, normed_one, cols_qkv, cosine, sine, piece_ids, heads
    )
    if near:
        mid = product_scattered(attended, w_out, False, base=x_rows, number=2)[0]
    else:
        mid = x_flat + scatter(attended, w_out, False)
    grad_out = cotangent.reshape(local_rows, model_width)

    back_ins, back_scratch = attend_back_operands(
        cut_order, attended_placed, query, key, value, lse, cosine, sine, piece_ids, heads
    )
    q_here = heads * HD
    if near:
        normed_two, hidden, cols_gate_up, grad_gate_up, down_term = feed_forward(
            mid, ffn_gain, grad_out, spread, rest, w_down, number=3
        )
        cols_gate_up = cols_gate_up.reshape(model_width, -1)
        high, half_width = 2 * rows_here // GATE_UP, model_width // 2
        sums = Sums((8, high, half_width))
        terms = {"down": down_term.reshape(DOWN // 2, 8, high, model_width)}

        def pick_whole(n):
            return "down", lambda ref: ref.at[n // 2, :, :, n % 2 * half_width : (n % 2 + 1) * half_width]

        def pick_rows(name, n):
            rows, side = n // 2 * high, n % 2 * half_width
            return name, lambda ref: ref.at[:, rows : rows + high, side : side + half_width]

        picks = [pick_whole(n) for n in range(DOWN)]
        picks += [pick_rows("gate_up", n) for n in range(GATE_UP)]
        picks += [pick_rows("out", n) for n in range(OUT)]

        def line(number, ticks):
            names = sorted(
                {picks[t][0] for t in range(sums.tick, sums.tick + ticks) if t < len(picks)}
            )
            return dict(
                number=number, ticks=ticks, sums=sums, picks=dict(enumerate(picks)),
                arrays=[(name, terms[name]) for name in names],
            )

        result, terms["gate_up"] = product_scattered(
            hidden, w_down, False, extra=(normed_two, grad_gate_up), base=mid, dtype=bf16,
            steps={1: 1, 3: 1, "early": 1, 7: 1, "late": 1, "later": 1, "latest": 1}, **line(5, 9),
        )
        grad_mid, gain_ffn_term = product_scattered(
            grad_gate_up, cols_gate_up, True, back=(grad_out, mid, ffn_gain),
            steps={0: 1, 2: 1, 3: 1, 4: 1, 5: 1, 7: 1, 12: 1}, **line(6, 10),
        )
        grad_qkv, out_term = attention_back(
            grad_mid, w_out, attended, back_ins, back_scratch, heads, **line(7, 15)
        )
        terms["out"] = out_term.reshape(8, OUT // 2 * high, model_width)
        grad_x, gain_attn_term, qkv_term = product_scattered(
            grad_qkv, cols_qkv, True, extra=(normed_one, None), dtype=bf16,
            back=(grad_mid, x_rows, attn_gain),
            steps={3: 1, "early": 1, 5: 1, "late": 1, "latest": 1}, **line(9, 8),
        )
        gains = jnp.stack([gain_attn_term, gain_ffn_term]).reshape(2, groups, rows_here)
        gains = jnp.pad(jnp.moveaxis(gains, 0, 1), ((0, 0), (0, 6), (0, 0)))
        rest = line(10, CHUNKS + 2 * LAG - sums.tick)
        gate_rows, up_rows, qkv_rows, own_gains = tail(
            qkv_term.reshape(8, 8, 2 * high, -1), gains,
            {c: sums.done[c] for c in sums.done if c >= DOWN}, hidden_here, **rest,
        )
        straight = [n for n in range(CHUNKS) if n < DOWN or n >= DOWN + GATE_UP]
        weight_grads, shaped = finish(
            [sums.done[n] for n in straight], gate_rows, up_rows, (result, grad_x), heads
        )
        shaped = tuple(rows.reshape(layer_input.shape) for rows in shaped)
        return shaped + tuple(weight_grads) + (own_gains[0], own_gains[1])

    unit_one = x_flat * inv_one
    inv_two = lax.rsqrt(jnp.mean(mid * mid, -1, keepdims=True) + EPS)
    unit_two = mid * inv_two
    normed_two = gather((unit_two * ffn_gain).astype(bf16))
    grad_all = gather(grad_out)
    gate_up = matmul_f32(normed_two, cols_gate_up)
    gate_proj, up_proj = gate_up[:, :hidden_here], gate_up[:, hidden_here:]
    sigmoid_gate = jax.nn.sigmoid(gate_proj)
    swish = gate_proj * sigmoid_gate
    hidden = (swish * up_proj).astype(bf16)
    gate_part = up_proj * sigmoid_gate * (1.0 + gate_proj * (1.0 - sigmoid_gate))
    down_term = over_tokens(hidden, grad_all).astype(bf16)
    grad_hidden = against_rows(grad_all, w_down)
    grad_gate_up = jnp.concatenate([grad_hidden * gate_part, grad_hidden * swish], 1).astype(bf16)
    grad_mid, gain_ffn_term = norm_back(
        grad_out.astype(f32), scatter(grad_gate_up, cols_gate_up, True), unit_two, inv_two, gain_ffn
    )
    grad_mid_low = gather(grad_mid.astype(bf16))
    grad_attended = against_rows(grad_mid_low, w_out).astype(bf16)
    grad_qkv = attend_back(grad_attended, back_ins, back_scratch, heads)
    grad_x, gain_attn_term = norm_back(
        grad_mid, scatter(grad_qkv, cols_qkv, True), unit_one, inv_one, gain_attn
    )

    def to_rows(term):
        return lax.all_to_all(
            term.astype(bf16).reshape(groups, rows_here, -1), "grp", 0, 0, tiled=True
        )

    def whole_rows(term):
        return jnp.moveaxis(term, 0, 1).reshape(rows_here, -1)

    def kv_rows(term):
        return jnp.sum(
            jnp.moveaxis(term, 0, 1).reshape(rows_here, kv_heads, copies, HD), 2
        ).reshape(rows_here, -1)

    gate_up_term = sum_over_sequences(to_rows(over_tokens(normed_two, grad_gate_up)))
    out_term = sum_over_sequences(over_tokens(attended, grad_mid_low).astype(bf16))
    qkv_term = sum_over_sequences(to_rows(over_tokens(normed_one, grad_qkv)))
    gain_total = lax.psum(jnp.stack([gain_attn_term, gain_ffn_term]), ("grp", "rep"))
    own_gains = lax.dynamic_slice_in_dim(gain_total, own_index * rows_here, rows_here, 1)
    return (
        (mid + scatter(hidden, w_down, False)).astype(bf16).reshape(layer_input.shape),
        grad_x.astype(bf16).reshape(layer_input.shape),
        whole_rows(qkv_term[..., :q_here]),
        kv_rows(qkv_term[..., q_here : q_here + HD]),
        kv_rows(qkv_term[..., q_here + HD :]),
        out_term,
        whole_rows(gate_up_term[..., :hidden_here]),
        whole_rows(gate_up_term[..., hidden_here:]),
        sum_over_sequences(down_term),
        own_gains[0],
        own_gains[1],
    )


def solution(mesh):
    tokens, table, rows, whole = P("rep", "grp", None), P("rep", None), P("grp", None), P()
    return jax.shard_map(
        on_device,
        mesh=mesh,
        in_specs=(tokens, tokens, table, table) + (rows,) * 7 + (whole,) * 2,
        out_specs=(tokens, tokens) + (rows,) * 7 + (P("grp"),) * 2,
        check_vma=False,
    )
```

```python
import functools

import jax
import jax.numpy as jnp
import numpy as np
from jax import lax
from jax.experimental import pallas as pl
from jax.experimental.pallas import tpu as pltpu
from jax.sharding import PartitionSpec as P

HD = 128
EPS = 1e-05
ROPE_BASE = 1000000.0
SCORE_SCALE = HD**-0.5
LOG2E = 1.4426950408889634
TO_EXP2 = SCORE_SCALE * LOG2E
NEG = -1e30

MESH = pl.DeviceIdType.MESH
f32 = jnp.float32
bf16 = jnp.bfloat16


def matmul_f32(first, second):
    return jnp.dot(first, second, preferred_element_type=f32)


def against_rows(first, second):
    return lax.dot_general(first, second, (((1,), (1,)), ((), ())), preferred_element_type=f32)


def over_tokens(first, second):
    return lax.dot_general(first, second, (((0,), (0,)), ((), ())), preferred_element_type=f32)


def turn_tables(length):
    half_size = HD // 2
    inverse = np.float32(ROPE_BASE) ** (-(np.arange(half_size, dtype=np.float32) * 2) / HD)
    angles = np.arange(length, dtype=np.float32)[:, None] * inverse.astype(np.float32)
    cosine, sine = np.cos(angles), np.sin(angles)
    tables = np.concatenate([cosine, cosine], -1), np.concatenate([-sine, sine], -1)
    return tuple(jnp.asarray(table.astype(np.float32)) for table in tables)


def norm_back(upstream, grad_normed, unit_rows, inv_root, gain):
    scaled = grad_normed * gain
    center_term = jnp.mean(scaled * unit_rows, -1, keepdims=True)
    return (
        upstream + inv_root * (scaled - unit_rows * center_term),
        jnp.sum(grad_normed * unit_rows, 0),
    )


def fold_lanes(values, op):
    out = values[:, :HD]
    for at in range(HD, values.shape[1], HD):
        out = op(out, values[:, at : at + HD])
    return out


def as_column(row):
    return jnp.broadcast_to(row, (HD, row.shape[1])).T[:, 0:1]


def as_row(column):
    return jnp.broadcast_to(column, (column.shape[0], HD)).T[0:1, :]


def attend_kernel(
    heads, cuts, block,
    order_ref, rows_hbm, weight_hbm, cos_ref, sin_ref, piece_ref,
    out_ref, q_ref, k_ref, v_ref, lse_ref, placed,
    scores, rows_ref, weight_ref, qkv_ref, sems,
):
    length = rows_ref.shape[0]
    cut = length // cuts
    blocks = length // block
    loads = [pltpu.make_async_copy(weight_hbm, weight_ref, sems.at[blocks])]
    for i in range(blocks):
        at = slice(i * block, (i + 1) * block)
        loads.append(pltpu.make_async_copy(rows_hbm.at[at, :], rows_ref.at[at, :], sems.at[i]))
    for load in loads:
        load.start()

    def place_cut(r, first):
        src = pl.ds(pl.multiple_of(r * cut, cut), cut)
        dst = pl.ds(pl.multiple_of(order_ref[0, first + r] * cut, cut), cut)
        cosine, sine = cos_ref[dst, :], sin_ref[dst, :]
        for h in range(heads + 1):
            part = qkv_ref[src, h * HD : (h + 1) * HD]
            turned = (part * cosine + pltpu.roll(part, HD // 2, 1) * sine).astype(bf16)
            if h < heads:
                q_ref[h, dst, :] = turned
            else:
                k_ref[dst, :] = turned
        v_ref[dst, :] = qkv_ref[src, (heads + 1) * HD :].astype(bf16)
        return first

    loads[0].wait()
    for i in range(blocks):
        loads[1 + i].wait()
        qkv_ref[...] = matmul_f32(rows_ref[i * block : (i + 1) * block, :], weight_ref[...])
        lax.fori_loop(0, block // cut, place_cut, i * (block // cut))

    def one_block(i, _):
        rows = pl.ds(pl.multiple_of(i * block, block), block)
        query = q_ref[:, rows, :].reshape(heads * block, HD)

        def score(j, high):
            cols = pl.ds(pl.multiple_of(j * block, block), block)
            tile = against_rows(query, k_ref[cols, :])
            scores[j] = tile
            return jnp.maximum(high, fold_lanes(tile, jnp.maximum))

        high = lax.fori_loop(0, i, score, jnp.full((heads * block, HD), NEG, f32))
        tile = against_rows(query, k_ref[rows, :])
        q_at = lax.broadcasted_iota(jnp.int32, (block, block), 0)
        k_at = lax.broadcasted_iota(jnp.int32, (block, block), 1)
        k_piece = piece_ref[0:1, rows].astype(f32)
        q_piece = as_column(k_piece)
        allowed = (k_at <= q_at) | ((q_piece != 0) & (q_piece == k_piece))
        tile = jnp.concatenate(
            [jnp.where(allowed, tile[h * block : (h + 1) * block], NEG) for h in range(heads)], 0
        )
        scores[i] = tile
        high = jnp.max(jnp.maximum(high, fold_lanes(tile, jnp.maximum)), 1, keepdims=True)

        def weigh(j, state):
            total, mixed = state
            cols = pl.ds(pl.multiple_of(j * block, block), block)
            prob = jnp.exp2((scores[j] - high) * TO_EXP2)
            total = total + fold_lanes(prob, jnp.add)
            return total, mixed + matmul_f32(prob.astype(bf16), v_ref[cols, :])

        zero = jnp.zeros((heads * block, HD), f32)
        total, mixed = lax.fori_loop(0, i + 1, weigh, (zero, zero))
        total = jnp.sum(total, 1, keepdims=True)
        mixed = (mixed / total).astype(bf16)
        log_total = high * TO_EXP2 + jnp.log2(total)
        for h in range(heads):
            placed[rows, h * HD : (h + 1) * HD] = mixed[h * block : (h + 1) * block]
            lse_ref[h : h + 1, rows] = as_row(log_total[h * block : (h + 1) * block])
        return 0

    lax.fori_loop(0, blocks, one_block, 0)

    def store_cut(r, _):
        dst = pl.ds(pl.multiple_of(r * cut, cut), cut)
        src = pl.ds(pl.multiple_of(order_ref[0, r] * cut, cut), cut)
        out_ref[dst, :] = placed[src, :]
        return 0

    lax.fori_loop(0, cuts, store_cut, 0)


def vmem_specs(count):
    return [pl.BlockSpec(memory_space=pltpu.VMEM)] * count


def attend(order, rows, weight, cosine, sine, piece, heads):
    length, width = rows.shape
    block = min(512, length)
    return pl.pallas_call(
        functools.partial(attend_kernel, heads, order.shape[1], block),
        out_shape=(
            jax.ShapeDtypeStruct((length, heads * HD), bf16),
            jax.ShapeDtypeStruct((heads, length, HD), bf16),
            jax.ShapeDtypeStruct((length, HD), bf16),
            jax.ShapeDtypeStruct((length, HD), bf16),
            jax.ShapeDtypeStruct((heads, length), f32),
            jax.ShapeDtypeStruct((length, heads * HD), bf16),
        ),
        in_specs=[pl.BlockSpec(memory_space=pltpu.SMEM)]
        + [pl.BlockSpec(memory_space=pl.ANY)] * 2
        + vmem_specs(3),
        out_specs=tuple(vmem_specs(6)),
        scratch_shapes=[
            pltpu.VMEM((length // block, heads * block, block), f32),
            pltpu.VMEM(rows.shape, bf16),
            pltpu.VMEM(weight.shape, bf16),
            pltpu.VMEM((block, weight.shape[1]), f32),
            pltpu.SemaphoreType.DMA((length // block + 1,)),
        ],
        compiler_params=pltpu.CompilerParams(vmem_limit_bytes=60 * 2**20),
        cost_estimate=pl.CostEstimate(
            flops=3 * heads * length * length * HD + 2 * length * width * weight.shape[1],
            bytes_accessed=10 * length * HD * heads * 4 + rows.size * 2,
            transcendentals=heads * length * length // 2,
        ),
    )(order, rows, weight, cosine, sine, piece)


DOWN, GATE_UP, OUT, QKV = 16, 32, 4, 8
CHUNKS = DOWN + GATE_UP + OUT + QKV
LAG = 3


def is_chunk(number):
    return 0 <= number < CHUNKS


def is_middle():
    rank = lax.axis_index("rep")
    return (rank == 1) | (rank == 2)


def is_end():
    rank = lax.axis_index("rep")
    return (rank == 0) | (rank == 3)


class NoLine:
    ticks = 0

    def signal(self, barrier):
        pass

    def greet(self, barrier, others):
        if others:
            pl.semaphore_wait(barrier, others)

    def start(self):
        pass

    def step(self, times=1):
        pass

    def end(self):
        pass


class Line:
    def __init__(self, first, ticks, picks, refs, outs, scratch):
        self.first, self.ticks, self.picks, self.refs, self.outs = first, ticks, picks, refs, outs
        (
            self.inward, self.across, self.own, self.pair, self.total, self.sems, self.local,
            self.carries,
        ) = scratch
        rank = lax.axis_index("rep")
        self.partner = {"rep": rank + 1 - 2 * (rank % 2)}
        self.peer = {"rep": 3 - rank}
        self.now = 0
        self.kept = []

    def signal(self, barrier):
        pl.semaphore_signal(barrier, inc=1, device_id=self.partner, device_id_type=MESH)

        @pl.when(is_middle())
        def _():
            pl.semaphore_signal(barrier, inc=1, device_id=self.peer, device_id_type=MESH)

    def greet(self, barrier, others):
        @pl.when(is_middle())
        def _():
            pl.semaphore_wait(barrier, others + 2)

        @pl.when(is_end())
        def _():
            pl.semaphore_wait(barrier, others + 1)

    def remote(self, hop, number, src, dst, device):
        return pltpu.make_async_remote_copy(
            src_ref=src, dst_ref=dst, send_sem=self.sems.at[0, hop, number],
            recv_sem=self.sems.at[1, hop, number], device_id=device, device_id_type=MESH,
        )

    def hops(self, number):
        tick = self.first + number
        term = pair = total = None
        if is_chunk(tick):
            which, pick = self.picks[tick]
            term = (
                lambda: self.remote(
                    0, number, pick(self.refs[which]), self.inward.at[number], self.partner
                ),
                lambda: pltpu.make_async_copy(
                    pick(self.refs[which]), self.own.at[tick % LAG], self.local.at[0, number]
                ),
            )
        if is_chunk(tick - LAG):
            held = self.pair.at[(tick - LAG) % (LAG + 1)]
            before = self.refs[f"pair{number}"] if number < LAG else held
            pair = (
                lambda: self.remote(1, number, before, self.across.at[number], self.peer),
                lambda: pltpu.make_async_copy(before, held, self.carries.at[0, number]),
            )
        if is_chunk(tick - 2 * LAG):
            held_total = self.total.at[(tick - 2 * LAG) % (LAG + 1)]
            done = self.refs[f"total{number}"] if number < LAG else held_total
            slot = self.outs[tick - 2 * LAG]
            total = (
                lambda: self.remote(2, number, done, slot, self.partner),
                lambda: pltpu.make_async_copy(held_total, slot, self.local.at[1, number]),
                lambda: pltpu.make_async_copy(done, held_total, self.carries.at[3, number]),
            )
        return term, pair, total

    def open(self, number):
        term, pair, total = self.hops(number)

        @pl.when(is_end())
        def _():
            if term:
                term[0]().start()

        @pl.when(is_middle())
        def _():
            if pair:
                pair[0]().start()
            if total:
                total[0]().start()
            if term:
                term[1]().start()
            if total:
                total[2 if number < LAG else 1]().start()
            if pair and number < LAG:
                pair[1]().start()

    def close(self, number):
        term, pair, total = self.hops(number)

        @pl.when(is_end())
        def _():
            if term:
                term[0]().wait_send()
            if total:
                total[0]().wait_recv()

        @pl.when(is_middle())
        def _():
            if total:
                total[0]().wait_send()
                if number >= LAG:
                    total[1]().wait()
            if pair:
                pair[0]().wait_send()
                pair[0]().wait_recv()
            if term:
                term[0]().wait_recv()

    def add(self, number):
        term, pair, total = self.hops(number)
        tick = self.first + number

        def sum_of(into, first, second):
            def one(g, _):
                into[g] = (first[g].astype(f32) + second[g].astype(f32)).astype(bf16)
                return 0

            lax.fori_loop(0, into.shape[0], one, 0)

        @pl.when(is_middle())
        def _():
            if total and number < LAG:
                total[2]().wait()
                total[1]().start()
            if pair:
                if number < LAG:
                    pair[1]().wait()
                before = tick - LAG
                sum_of(
                    self.total.at[before % (LAG + 1)], self.pair.at[before % (LAG + 1)],
                    self.across.at[number],
                )
            if term:
                term[1]().wait()
                sum_of(self.pair.at[tick % (LAG + 1)], self.own.at[tick % LAG], self.inward.at[number])
            if total and number < LAG:
                total[1]().wait()

    def keep(self, number):
        tick = self.first + number
        which = number - (self.ticks - LAG)
        made = []
        if is_chunk(tick):
            made.append((self.pair.at[tick % (LAG + 1)], self.outs[f"pair{which}"], (1, which)))
        if is_chunk(tick - LAG):
            held = self.total.at[(tick - LAG) % (LAG + 1)]
            made.append((held, self.outs[f"total{which}"], (2, which)))
        copies = [
            lambda src=src, dst=dst, at=at: pltpu.make_async_copy(src, dst, self.carries.at[*at])
            for src, dst, at in made
        ]

        @pl.when(is_middle())
        def _():
            for copy in copies:
                copy().start()

        self.kept += copies

    def start(self):
        for number in range(LAG):
            self.open(number)

    def step(self, times=1):
        for _ in range(times):
            if self.now + LAG < self.ticks:
                self.settle()
                self.open(self.now + LAG - 1)

    def settle(self):
        self.close(self.now)
        self.add(self.now)
        if self.now >= self.ticks - LAG:
            self.keep(self.now)
        self.now += 1

    def end(self):
        while self.now + LAG < self.ticks:
            self.step()
        while self.now < self.ticks:
            self.settle()

        @pl.when(is_middle())
        def _():
            for copy in self.kept:
                copy().wait()


def line_slots(first, ticks):
    return [t - 2 * LAG for t in range(first, first + ticks) if is_chunk(t - 2 * LAG)]


class Sums:
    def __init__(self, shape):
        self.shape, self.tick, self.kept, self.done = shape, 0, {}, {}


def run(kernel, ins, outs, scratch, number, cost, sums=None, ticks=0, arrays=(), picks=None, vmem=58):
    ins, outs, scratch = list(ins), list(outs), list(scratch)
    counts = (len(ins), len(outs), len(scratch))
    first = sums.tick if ticks else 0
    names_in, names_out = [], []
    if ticks:
        for name, array in arrays:
            names_in.append(name)
            ins.append((array, pl.ANY))
        for which in range(LAG):
            for name, chunk_at in ((f"pair{which}", first - LAG), (f"total{which}", first - 2 * LAG)):
                if is_chunk(chunk_at + which):
                    names_in.append(name)
                    ins.append((sums.kept[name], pl.ANY))
        names_out = line_slots(first, ticks)
        after = first + ticks
        for which in range(LAG):
            for name, chunk_at in ((f"pair{which}", after - LAG), (f"total{which}", after - 2 * LAG)):
                if is_chunk(chunk_at + which):
                    names_out.append(name)
        outs += [(jax.ShapeDtypeStruct(sums.shape, bf16), pl.ANY)] * len(names_out)
        scratch += [
            pltpu.VMEM((ticks,) + sums.shape, bf16),
            pltpu.VMEM((ticks,) + sums.shape, bf16),
            pltpu.VMEM((LAG,) + sums.shape, bf16),
            pltpu.VMEM((LAG + 1,) + sums.shape, bf16),
            pltpu.VMEM((LAG + 1,) + sums.shape, bf16),
            pltpu.SemaphoreType.DMA((2, 3, ticks)),
            pltpu.SemaphoreType.DMA((2, ticks)),
            pltpu.SemaphoreType.DMA((4, LAG)),
        ]

    def body(*refs):
        in_refs, rest = refs[: len(ins)], refs[len(ins) :]
        out_refs, scratch_refs = rest[: len(outs)], rest[len(outs) :]
        line = NoLine()
        if ticks:
            line = Line(
                first, ticks, picks, dict(zip(names_in, in_refs[counts[0] :])),
                dict(zip(names_out, out_refs[counts[1] :])), scratch_refs[counts[2] :],
            )
        kernel(in_refs[: counts[0]], out_refs[: counts[1]], scratch_refs[: counts[2]], line)

    results = pl.pallas_call(
        body,
        out_shape=tuple(shape for shape, _ in outs),
        in_specs=[pl.BlockSpec(memory_space=space) for _, space in ins],
        out_specs=tuple(pl.BlockSpec(memory_space=space) for _, space in outs),
        scratch_shapes=scratch,
        compiler_params=pltpu.CompilerParams(
            vmem_limit_bytes=vmem * 2**20,
            **({} if number is None else {"collective_id": number, "has_side_effects": True}),
        ),
        cost_estimate=pl.CostEstimate(
            flops=cost[0], bytes_accessed=cost[1], transcendentals=cost[2]
        ),
    )(*[array for array, _ in ins])
    for name, result in zip(names_out, results[counts[1] :]):
        if name in line_slots(first, ticks):
            sums.done[name] = result
        else:
            sums.kept[name] = result
    if ticks:
        sums.tick += ticks
    return results[: counts[1]]


SMEM, VMEM, ANY = pltpu.SMEM, pltpu.VMEM, pl.ANY


def attend_back_kernel(
    heads, block, ins, outs, scratch, line, entered=False
):
    grad_ref, out_ref, q_ref, k_ref, v_ref, lse_ref, cos_ref, sin_ref, piece_ref, place_ref = ins
    (grad_qkv_ref,) = outs
    grads, centers, grad_q, placed = scratch
    if line.ticks and not entered:
        line.signal(pltpu.get_barrier_semaphore())
        line.greet(pltpu.get_barrier_semaphore(), 0)
        line.start()
    length = grad_ref.shape[0]
    blocks = length // block

    def take_block(i, _):
        rows = pl.ds(pl.multiple_of(i * block, block), block)
        position = lax.broadcasted_iota(jnp.int32, (block, length), 0) + i * block
        chosen = jnp.where(place_ref[...] == position, 1.0, 0.0).astype(bf16)
        taken = matmul_f32(chosen, grad_ref[...]).astype(bf16)
        for h in range(heads):
            grad = taken[:, h * HD : (h + 1) * HD]
            grads[h, rows, :] = grad
            product = grad.astype(f32) * out_ref[rows, h * HD : (h + 1) * HD].astype(f32)
            centers[h, rows, :] = jnp.broadcast_to(
                jnp.sum(product, 1, keepdims=True), (block, HD)
            )
        return 0

    lax.fori_loop(0, blocks, take_block, 0)
    line.step()
    grad_q[...] = jnp.zeros_like(grad_q)

    def key_block(j, _):
        cols = pl.ds(pl.multiple_of(j * block, block), block)
        key, value = k_ref[cols, :], v_ref[cols, :]

        def one(i, state, diagonal):
            grad_key, grad_value = state
            rows = pl.ds(pl.multiple_of(i * block, block), block)
            for h in range(heads):
                query, grad = q_ref[h, rows, :], grads[h, rows, :]
                log_total = lse_ref[h : h + 1, rows]
                center = centers[h, rows, :].T[0:1, :]
                prob = jnp.exp2(against_rows(key, query) * TO_EXP2 - log_total)
                if diagonal:
                    k_at = lax.broadcasted_iota(jnp.int32, (block, block), 0)
                    q_at = lax.broadcasted_iota(jnp.int32, (block, block), 1)
                    q_piece = piece_ref[0:1, cols].astype(f32)
                    k_piece = as_column(q_piece)
                    allowed = (k_at <= q_at) | ((q_piece != 0) & (q_piece == k_piece))
                    prob = jnp.where(allowed, prob, 0.0)
                grad_prob = against_rows(value, grad)
                grad_score = (prob * (grad_prob - center)).astype(bf16)
                grad_value = grad_value + matmul_f32(prob.astype(bf16), grad)
                grad_key = grad_key + matmul_f32(grad_score, query)
                grad_q[h, rows, :] += over_tokens(grad_score, key)
            return grad_key, grad_value

        zero = jnp.zeros((block, HD), f32)
        state = one(j, (zero, zero), True)
        grad_key, grad_value = lax.fori_loop(
            j + 1, blocks, functools.partial(one, diagonal=False), state
        )
        grad_key = grad_key * SCORE_SCALE
        grad_key = grad_key * cos_ref[cols, :] - pltpu.roll(grad_key, HD // 2, 1) * sin_ref[cols, :]
        placed[cols, heads * HD : (heads + 1) * HD] = grad_key.astype(bf16)
        placed[cols, (heads + 1) * HD :] = grad_value.astype(bf16)
        return 0

    for j in range(min(2, blocks - 1)):
        lax.fori_loop(j, j + 1, key_block, 0)
        line.step(2 - j)
    lax.fori_loop(min(2, blocks - 1), blocks, key_block, 0)

    def turn_back(i, _):
        rows = pl.ds(pl.multiple_of(i * block, block), block)
        for h in range(heads):
            grad = grad_q[h, rows, :] * SCORE_SCALE
            grad = grad * cos_ref[rows, :] - pltpu.roll(grad, HD // 2, 1) * sin_ref[rows, :]
            placed[rows, h * HD : (h + 1) * HD] = grad.astype(bf16)
        return 0

    lax.fori_loop(0, blocks, turn_back, 0)
    line.step()

    def store_block(i, _):
        rows = pl.ds(pl.multiple_of(i * block, block), block)
        place = as_column(place_ref[0:1, rows].astype(f32)).astype(jnp.int32)
        position = lax.broadcasted_iota(jnp.int32, (block, length), 1)
        chosen = jnp.where(place == position, 1.0, 0.0).astype(bf16)
        grad_qkv_ref[rows, :] = matmul_f32(chosen, placed[...]).astype(bf16)
        return 0

    lax.fori_loop(0, blocks, store_block, 0)
    line.end()


def attend_back_operands(order, out, query, key, value, lse, cosine, sine, piece, heads):
    length = out.shape[0]
    cut = length // order.shape[1]
    place = (order.reshape(-1, 1) * cut + jnp.arange(cut, dtype=order.dtype)).reshape(1, length)
    scratch = [
        pltpu.VMEM((heads, length, HD), bf16),
        pltpu.VMEM((heads, length, HD), f32),
        pltpu.VMEM((heads, length, HD), f32),
        pltpu.VMEM((length, (heads + 2) * HD), bf16),
    ]
    return [out, query, key, value, lse, cosine, sine, piece, place], scratch


def attend_back(grad, operands, scratch, heads):
    length = grad.shape[0]
    return run(
        functools.partial(attend_back_kernel, heads, min(512, length)),
        [(array, VMEM) for array in [grad] + operands],
        [(jax.ShapeDtypeStruct((length, (heads + 2) * HD), bf16), VMEM)],
        scratch,
        None,
        (8 * heads * length * length * HD, 14 * length * HD * heads * 4, heads * length * length // 2),
    )[0]


def place_in_group():
    me = lax.axis_index("grp")
    return me // 4, (me // 2) % 2, me % 2


def other(flip_y, flip_x, flip_core):
    y, x, core = place_in_group()
    return ((y + flip_y) % 2) * 4 + ((x + flip_x) % 2) * 2 + (core + flip_core) % 2


def chip_rows(flip_y, flip_x, rows):
    y, x, _ = place_in_group()
    first = (((y + flip_y) % 2) * 2 + (x + flip_x) % 2) * (2 * rows)
    return pl.ds(pl.multiple_of(first, 2 * rows), 2 * rows)


NEIGHBOURS = ((0, 0, 1), (0, 1, 0), (1, 0, 0))
EVERYONE = tuple((n // 4, (n // 2) % 2, n % 2) for n in range(1, 8))


def greet_group(line, flips=NEIGHBOURS, between=None):
    barrier = pltpu.get_barrier_semaphore()
    for flip in flips:
        pl.semaphore_signal(barrier, inc=1, device_id={"grp": other(*flip)}, device_id_type=MESH)
    line.signal(barrier)
    if between:
        between()
    line.greet(barrier, len(flips))


SIBLING, ALONG_X, ALONG_Y, ACROSS = (0, 0), (0, 1), (1, 0), (1, 1)


class Gather:
    TO_S, TO_X, TO_Y = (0, 0, 1), (0, 1, 0), (1, 0, 0)

    def __init__(self, rows, all_ref, sends, recvs):
        self.rows, self.all_ref, self.sends, self.recvs = rows, all_ref, sends, recvs
        self.started = []

    def copy(self, number, chip, core, part, target):
        first = other(*chip, core) * self.rows
        if part is None:
            where = pl.ds(pl.multiple_of(first, self.rows), self.rows)
        else:
            half = self.rows // 2
            where = pl.ds(pl.multiple_of(first + part * half, half), half)
        where = self.all_ref.at[where, :]
        return pltpu.make_async_remote_copy(
            src_ref=where, dst_ref=where, send_sem=self.sends.at[number],
            recv_sem=self.recvs.at[number], device_id={"grp": other(*target)}, device_id_type=MESH,
        )

    def send(self, *what):
        one = self.copy(*what)
        one.start()
        self.started.append(one)

    def landed(self, number, chip, core, part):
        self.copy(number, chip, core, part, self.TO_S).wait_recv()

    def send_own(self):
        self.send(1, SIBLING, 0, 1, self.TO_X)
        self.send(3, SIBLING, 0, 0, self.TO_Y)
        self.send(0, SIBLING, 0, None, self.TO_S)
        self.send(2, SIBLING, 0, 0, self.TO_X)
        self.send(4, SIBLING, 0, 1, self.TO_Y)

    def sibling(self):
        self.landed(0, SIBLING, 1, None)

    def relay(self):
        self.landed(1, ALONG_X, 0, 1)
        self.send(6, ALONG_X, 0, 1, self.TO_Y)
        self.landed(3, ALONG_Y, 0, 0)
        self.send(5, ALONG_Y, 0, 0, self.TO_X)
        self.send(7, ALONG_X, 0, 1, self.TO_S)
        self.send(8, ALONG_Y, 0, 0, self.TO_S)

    def pass_second(self):
        self.landed(2, ALONG_X, 0, 0)
        self.send(9, ALONG_X, 0, 0, self.TO_S)
        self.landed(4, ALONG_Y, 0, 1)
        self.send(10, ALONG_Y, 0, 1, self.TO_S)

    def along_x(self):
        self.landed(7, ALONG_X, 1, 1)
        self.landed(9, ALONG_X, 1, 0)

    def pass_across(self):
        self.landed(5, ACROSS, 0, 0)
        self.send(11, ACROSS, 0, 0, self.TO_S)
        self.landed(6, ACROSS, 0, 1)
        self.send(12, ACROSS, 0, 1, self.TO_S)

    def along_y(self):
        self.landed(8, ALONG_Y, 1, 0)
        self.landed(10, ALONG_Y, 1, 1)

    def across(self):
        self.landed(11, ACROSS, 1, 0)
        self.landed(12, ACROSS, 1, 1)

    def finish(self):
        for one in self.started:
            one.wait_send()


def gather_rows(rows, all_ref, sends, recvs, on_chip, line, then=None, final=True):
    rows_of = Gather(rows, all_ref, sends, recvs)
    rows_of.send_own()
    if then:
        then()
    rows_of.sibling()
    on_chip(*SIBLING)
    rows_of.relay()
    line.step(2)
    rows_of.pass_second()
    line.step(2)
    rows_of.along_x()
    on_chip(*ALONG_X)
    rows_of.pass_across()
    line.step(2)
    rows_of.along_y()
    on_chip(*ALONG_Y)
    rows_of.across()
    on_chip(*ACROSS)
    rows_of.finish()
    if final:
        line.end()
    else:
        line.step()


GATHER_COPIES = 13


def rms_normed(values, gain):
    return values * lax.rsqrt(jnp.mean(values * values, -1, keepdims=True) + EPS) * gain


class Moves:
    def __init__(self, sems):
        self.sems, self.count, self.open = sems, 0, []

    def start(self, src, dst):
        one = pltpu.make_async_copy(src, dst, self.sems.at[self.count])
        self.count += 1
        one.start()
        return one

    def later(self, src, dst):
        self.open.append(self.start(src, dst))

    def finish(self):
        for one in self.open:
            one.wait()


def gather_scratch(rows, width, moves):
    return [
        pltpu.VMEM((8 * rows, width), bf16),
        pltpu.SemaphoreType.DMA((GATHER_COPIES,)),
        pltpu.SemaphoreType.DMA((GATHER_COPIES,)),
        pltpu.SemaphoreType.DMA((moves,)),
    ]


def own_rows(rows):
    return pl.ds(pl.multiple_of(other(0, 0, 0) * rows, rows), rows)


def send_columns(pieces, sends, recvs, moves):
    copies = []
    for which, (rows_ref, width, there) in enumerate(pieces):
        for number, flip in enumerate(EVERYONE):
            target = other(*flip)
            cols = pl.ds(pl.multiple_of(target * width, width), width)
            one = pltpu.make_async_remote_copy(
                src_ref=rows_ref.at[:, cols], dst_ref=there,
                send_sem=sends.at[which, number], recv_sem=recvs.at[which, number],
                device_id={"grp": target}, device_id_type=MESH,
            )
            one.start()
            copies.append(one)
        mine = pl.ds(pl.multiple_of(other(0, 0, 0) * width, width), width)
        moves.later(rows_ref.at[:, mine], there)
    return copies


def gather_normed_kernel(ins, outs, scratch, line):
    x_ref, gain_ref = ins[:2]
    weights = ins[2:]
    all_ref, cols_ref = outs
    held, sends, recvs, sems, col_sends, col_recvs = scratch
    rows = x_ref.shape[0]
    moves = Moves(sems)

    def fill():
        held[own_rows(rows), :] = rms_normed(x_ref[...].astype(f32), gain_ref[...]).astype(bf16)

    greet_group(line, EVERYONE, fill)
    col_copies = []

    def send_weights():
        pieces, low = [], 0
        tall = weights[0].shape[0]
        there = pl.ds(pl.multiple_of(other(0, 0, 0) * tall, tall), tall)
        for weight in weights:
            width = weight.shape[1] // 8
            pieces.append((weight, width, cols_ref.at[there, low : low + width]))
            low += width
        col_copies.extend(send_columns(pieces, col_sends, col_recvs, moves))

    def on_chip(*chip):
        where = chip_rows(*chip, rows)
        moves.later(held.at[where, :], all_ref.at[where, :])

    gather_rows(rows, held, sends, recvs, on_chip, line, send_weights)
    for one in col_copies:
        one.wait()
    moves.finish()


def gather_normed(x, gain, weights, **line):
    rows, width = x.shape
    deep = sum(weight.shape[1] for weight in weights) // 8
    return run(
        gather_normed_kernel,
        [(x, VMEM), (gain, VMEM)] + [(weight, ANY) for weight in weights],
        [
            (jax.ShapeDtypeStruct((8 * rows, width), bf16), ANY),
            (jax.ShapeDtypeStruct((8 * weights[0].shape[0], deep), bf16), ANY),
        ],
        gather_scratch(rows, width, 4 + len(weights))
        + [pltpu.SemaphoreType.DMA((len(weights), 7))] * 2,
        line.pop("number"),
        (0, 150 * rows * width * 2, 0),
        **line,
    )


def columns_kernel(rows_here, ins, outs, scratch, line):
    (cols_ref,) = outs
    sends, recvs, sems = scratch
    moves = Moves(sems)
    barrier = pltpu.get_barrier_semaphore()
    for flip in EVERYONE:
        pl.semaphore_signal(barrier, inc=1, device_id={"grp": other(*flip)}, device_id_type=MESH)
    pl.semaphore_wait(barrier, 7)
    first = pl.multiple_of(lax.axis_index("rep") * rows_here, rows_here)
    me = other(0, 0, 0)
    pieces, low = [], 0
    for weight in ins:
        width = weight.shape[1] // 8
        pieces.append(
            (weight.at[pl.ds(first, rows_here), :], width, cols_ref.at[me, :, low : low + width])
        )
        low += width
    for one in send_columns(pieces, sends, recvs, moves):
        one.wait()
    moves.finish()


def columns_of_some(weights, rows_here, number):
    deep = sum(weight.shape[1] for weight in weights) // 8
    return run(
        functools.partial(columns_kernel, rows_here),
        [(weight, ANY) for weight in weights],
        [(jax.ShapeDtypeStruct((8, rows_here, deep), bf16), ANY)],
        [pltpu.SemaphoreType.DMA((len(weights), 7))] * 2
        + [pltpu.SemaphoreType.DMA((len(weights),))],
        number, (0, 50 * 8 * rows_here * deep, 0),
    )[0]


def feed_forward_kernel(tile, ins, outs, scratch, line):
    mid_ref, gain_ref, grad_ref, spread_ref, rest_ref, w_down_ref = ins
    all_ref, hidden_ref, whole_ref, grad_gate_up_ref, down_ref = outs
    held, grads_held, sends, recvs, grad_sends, grad_recvs, sems = scratch[:7]
    weight, w_down, hidden, up_part, gate_part, grads, down = scratch[7:]
    rows = mid_ref.shape[0]
    inner = hidden.shape[1]
    moves = Moves(sems)
    planes, _, tall, _ = spread_ref.shape
    loads = [
        moves.start(spread_ref.at[z], weight.at[:, z * tall : (z + 1) * tall, :])
        for z in range(planes)
    ]
    loads.append(moves.start(rest_ref, weight.at[:, planes * tall :, :]))
    down_load = moves.start(w_down_ref, w_down)

    def fill():
        held[own_rows(rows), :] = rms_normed(mid_ref[...], gain_ref[...]).astype(bf16)
        grads_held[own_rows(rows), :] = grad_ref[...]

    greet_group(line, between=fill)
    first = Gather(rows, held, sends, recvs)
    second = Gather(rows, grads_held, grad_sends, grad_recvs)
    stored = []

    def forward(*chip):
        where = chip_rows(*chip, rows)
        moves.later(held.at[where, :], all_ref.at[where, :])

        def column(t, _):
            cols = pl.ds(pl.multiple_of(t * tile, tile), tile)
            up_cols = pl.ds(pl.multiple_of(inner + t * tile, tile), tile)
            lhs = held[where, :]
            gate = matmul_f32(lhs, weight[:, :, cols].reshape(-1, tile))
            up = matmul_f32(lhs, weight[:, :, up_cols].reshape(-1, tile))
            sigma = 1.0 / (1.0 + jnp.exp(-gate))
            swish = gate * sigma
            hidden[where, cols] = (swish * up).astype(bf16)
            up_part[where, cols] = swish.astype(bf16)
            gate_part[where, cols] = (up * sigma * (1.0 + gate * (1.0 - sigma))).astype(bf16)
            return 0

        lax.fori_loop(0, inner // tile, column, 0)
        moves.later(hidden.at[where, :], hidden_ref.at[where, :])

    def backward(*chip):
        where = chip_rows(*chip, rows)
        slot = len(stored) % 2
        if len(stored) >= 2:
            stored[len(stored) - 2].wait()

        def column(t, _):
            cols = pl.ds(pl.multiple_of(t * tile, tile), tile)
            up_cols = pl.ds(pl.multiple_of(inner + t * tile, tile), tile)
            incoming = grads_held[where, :]
            grad_hidden = against_rows(incoming, w_down[cols, :])
            grads[slot, :, cols] = (grad_hidden * gate_part[where, cols].astype(f32)).astype(bf16)
            grads[slot, :, up_cols] = (grad_hidden * up_part[where, cols].astype(f32)).astype(bf16)
            term = over_tokens(hidden[where, cols], incoming)
            if chip == SIBLING:
                down[cols, :] = term
            elif chip == ACROSS:
                weight[t] = (down[cols, :] + term).astype(bf16)
            else:
                down[cols, :] += term
            return 0

        lax.fori_loop(0, inner // tile, column, 0)
        stored.append(moves.start(grads.at[slot], grad_gate_up_ref.at[where, :]))

    first.send_own()
    for one in loads:
        one.wait()
    whole = moves.start(weight, whole_ref)
    first.sibling()
    forward(*SIBLING)
    first.relay()
    first.pass_second()
    second.send_own()
    first.along_x()
    forward(*ALONG_X)
    first.pass_across()
    first.along_y()
    forward(*ALONG_Y)
    second.relay()
    first.across()
    forward(*ACROSS)
    down_load.wait()
    second.sibling()
    backward(*SIBLING)
    second.pass_second()
    second.along_x()
    backward(*ALONG_X)
    second.pass_across()
    second.along_y()
    backward(*ALONG_Y)
    second.across()
    whole.wait()
    backward(*ACROSS)
    moves.later(weight.at[: inner // tile], down_ref)
    first.finish()
    second.finish()
    for one in stored[-2:]:
        one.wait()
    moves.finish()


def feed_forward(mid, gain, grad, spread, rest, w_down, **line):
    rows, width = mid.shape
    inner = w_down.shape[0]
    weight = (8, width // 8, 2 * inner)
    return run(
        functools.partial(feed_forward_kernel, weight[1]),
        [(mid, VMEM), (gain, VMEM), (grad, VMEM), (spread, ANY), (rest, ANY), (w_down, ANY)],
        [
            (jax.ShapeDtypeStruct((8 * rows, width), bf16), ANY),
            (jax.ShapeDtypeStruct((8 * rows, inner), bf16), ANY),
            (jax.ShapeDtypeStruct(weight, bf16), ANY),
            (jax.ShapeDtypeStruct((8 * rows, 2 * inner), bf16), ANY),
            (jax.ShapeDtypeStruct((inner // weight[1], weight[1], width), bf16), ANY),
        ],
        [pltpu.VMEM((8 * rows, width), bf16)] * 2
        + [pltpu.SemaphoreType.DMA((GATHER_COPIES,))] * 4
        + [pltpu.SemaphoreType.DMA((20,))]
        + [pltpu.VMEM(weight, bf16), pltpu.VMEM(w_down.shape, bf16)]
        + [pltpu.VMEM((8 * rows, inner), bf16)] * 3
        + [
            pltpu.VMEM((2, 2 * rows, 2 * inner), bf16),
            pltpu.VMEM(w_down.shape, f32),
        ],
        line.pop("number"),
        (64 * rows * width * inner, 300 * rows * width * 2, 8 * rows * inner),
        vmem=63,
        **line,
    )


def attention_back_kernel(heads, block, ins, outs, scratch, line):
    grad_ref, w_ref, attended_ref = ins[:3]
    grad_qkv_ref, out_term_ref = outs
    held, sends, recvs, sems, total, grad_attended_ref = scratch[:6]
    rows = grad_ref.shape[0]
    moves = Moves(sems)
    greet_group(line)
    line.start()
    held[own_rows(rows), :] = grad_ref[...].astype(bf16)

    def on_chip(*chip):
        where = chip_rows(*chip, rows)
        incoming = held[where, :]
        grad_attended_ref[where, :] = against_rows(incoming, w_ref[...]).astype(bf16)
        term = over_tokens(attended_ref[where, :], incoming)
        if chip == SIBLING:
            total[...] = term
        elif chip == ACROSS:
            out_term_ref[...] = (total[...] + term).astype(bf16)
        else:
            total[...] += term

    gather_rows(rows, held, sends, recvs, on_chip, line, final=False)
    moves.finish()
    attend_back_kernel(
        heads, block, (grad_attended_ref,) + tuple(ins[3:]), (grad_qkv_ref,), scratch[6:], line,
        entered=True,
    )


def attention_back(grad, w_out, attended, back_ins, back_scratch, heads, **line):
    rows, width = grad.shape
    length = 8 * rows
    return run(
        functools.partial(attention_back_kernel, heads, min(512, length)),
        [(array, VMEM) for array in [grad, w_out, attended] + back_ins],
        [
            (jax.ShapeDtypeStruct((length, (heads + 2) * HD), bf16), VMEM),
            (jax.ShapeDtypeStruct(w_out.shape, bf16), VMEM),
        ],
        gather_scratch(rows, width, 1)
        + [pltpu.VMEM(w_out.shape, f32), pltpu.VMEM(attended.shape, bf16)]
        + back_scratch,
        line.pop("number"),
        (
            32 * rows * width * w_out.shape[0] + 8 * heads * length * length * HD,
            250 * rows * width * 2, heads * length * length // 2,
        ),
        **line,
    )


class WeightTerm:
    def __init__(self, rows_ref, columns_ref, term_ref, scratch):
        self.rows_ref, self.columns_ref, self.term_ref = rows_ref, columns_ref, term_ref
        self.loaded, self.flipped, self.ready, self.sems = scratch
        self.tile = self.loaded.shape[2]
        for number in (0, 1):
            self.load(number).start()

    def load(self, number):
        cols = slice(number * self.tile, (number + 1) * self.tile)
        return pltpu.make_async_copy(
            self.rows_ref.at[:, cols], self.loaded.at[number % 2], self.sems.at[0, number % 2]
        )

    def store(self, number):
        return pltpu.make_async_copy(
            self.ready.at[number % 2], self.term_ref.at[number], self.sems.at[1, number % 2]
        )

    def work(self, numbers):
        for number in numbers:
            at = number % 2
            self.load(number).wait()
            if number >= 2:
                self.store(number - 2).wait()
            width = self.columns_ref.shape[1]
            step = min(256, width)
            self.flipped[...] = self.loaded[at].T

            def column(t, _):
                cols = pl.ds(pl.multiple_of(t * step, step), step)
                term = matmul_f32(self.flipped[...], self.columns_ref[:, cols])
                self.ready[at, :, cols] = term.astype(bf16)
                return 0

            lax.fori_loop(0, width // step, column, 0)
            self.store(number).start()
            if number + 2 < 8:
                self.load(number + 2).start()

    def finish(self):
        for number in (6, 7):
            self.store(number).wait()


UNITS = (
    (ACROSS, 0), (ACROSS, 1), (ALONG_X, 0), (ALONG_Y, 1), (ALONG_X, 1), (ALONG_Y, 0),
    (SIBLING, 0), (SIBLING, 1),
)


def scatter_kernel(turned, extra, after, steps, ins, outs, scratch, line):
    out_ref = outs[0] if after == "base" else scratch[-4]
    finals = ins[len(ins) - {"base": 1, "cast": 1, "back": 3}[after] :]
    part, to_s, from_s, to_link, relay, last, sends, recvs = scratch[:8]
    a_ref, b_ref, load_sems = scratch[-3:]
    rows, width = out_ref.shape
    half = width // 2
    _, _, core = place_in_group()
    loading = {}

    def load(name, src, dst):
        loading[name] = pltpu.make_async_copy(src, dst, load_sems.at[len(loading)])
        loading[name].start()

    def load_weight(h):
        where = (slice(h * half, (h + 1) * half), slice(None))
        where = where if turned else where[::-1]
        load(h, ins[1].at[where], b_ref.at[where])

    def load_rows(chip):
        where = chip_rows(*chip, rows)
        load(chip, ins[0].at[where, :], a_ref.at[where, :])

    load_weight(0)
    load_rows(ACROSS)
    load_weight(1)
    for chip in (ALONG_X, ALONG_Y, SIBLING):
        load_rows(chip)
    greet_group(line)
    line.start()
    if extra:
        columns_ref = a_ref
        if extra == "loaded":
            columns_ref = scratch[12]
            load("columns", ins[3], columns_ref)
        term = WeightTerm(ins[2], columns_ref, outs[-1], scratch[8:12])
    own_at = pl.multiple_of(core * rows, rows)
    other_at = pl.multiple_of((1 - core) * rows, rows)
    to_sib, to_x, to_y = (0, 0, 1), (0, 1, 0), (1, 0, 0)
    started = []

    def ready(*names):
        for name in names:
            if name in loading:
                loading.pop(name).wait()
                loading[name, "done"] = None

    def send(number, src, dst, target):
        one = pltpu.make_async_remote_copy(
            src_ref=src, dst_ref=dst, send_sem=sends.at[number], recv_sem=recvs.at[number],
            device_id={"grp": other(*target)}, device_id_type=MESH,
        )
        one.start()
        started.append(one)

    def landed(number, where):
        pltpu.make_async_remote_copy(
            src_ref=where, dst_ref=where, send_sem=sends.at[number], recv_sem=recvs.at[number],
            device_id={"grp": other(0, 0, 1)}, device_id_type=MESH,
        ).wait_recv()

    def make(n):
        chip, h = UNITS[n]
        ready(h, chip)
        lhs = a_ref[chip_rows(*chip, rows), :]
        cols = slice(h * half, (h + 1) * half)
        if turned:
            part[n % 2] = against_rows(lhs, b_ref[cols, :])
        else:
            part[n % 2] = matmul_f32(lhs, b_ref[:, cols])
        to_s[n] = part[n % 2, pl.ds(other_at, rows), :].astype(bf16)
        send(n, to_s.at[n], from_s.at[n], to_sib)

    def own(n):
        landed(n, from_s.at[n])
        return part[n % 2, pl.ds(own_at, rows), :] + from_s[n].astype(f32)

    def finish(n):
        _, h = UNITS[n]
        if n < 2:
            to_link[n] = own(n).astype(bf16)
            send(8 + n, to_link.at[n], relay.at[n], (to_x, to_y)[n])
        elif n < 4:
            to_link[n] = own(n).astype(bf16)
            send(8 + n, to_link.at[n], last.at[(None, None, 0, 3)[n]], (to_x, to_y)[n - 2])
        elif n < 6:
            total = own(n)
            landed(8 + h, relay.at[h])
            to_link[n] = (total + relay[h].astype(f32)).astype(bf16)
            send(8 + n, to_link.at[n], last.at[(1, 2)[n - 4]], (to_x, to_y)[n - 4])
        else:
            cols = slice(h * half, (h + 1) * half)
            if after == "back":
                out_ref[:, cols] = own(n)
            else:
                out_ref[:, cols] = own(n) + finals[0][:, cols].astype(f32)
        line.step(steps.get(n, 0))

    def work(numbers, point):
        if extra:
            ready("columns")
            if columns_ref is a_ref:
                ready(*(chip for chip, _ in UNITS))
            term.work(numbers)
        line.step(steps.get(point, 0))

    make(0)
    make(1)
    finish(0)
    make(2)
    finish(1)
    make(3)
    finish(2)
    make(4)
    finish(3)
    make(5)
    work((0, 1), "early")
    finish(4)
    make(6)
    finish(5)
    make(7)
    finish(6)
    finish(7)
    work((2, 3), "late")
    work((4, 5), "later")
    work((6, 7), "latest")
    for number, slot, h in ((10, 0, 0), (11, 3, 1), (12, 1, 1), (13, 2, 0)):
        cols = slice(h * half, (h + 1) * half)
        landed(number, last.at[slot])
        out_ref[:, cols] += last[slot].astype(f32)
        line.step(steps.get(number, 0))
    if after == "cast":
        outs[0][...] = out_ref[...].astype(outs[0].dtype)
    if after == "back":
        upstream_ref, rows_ref, gain_ref = finals
        some = min(64, rows)

        def norm_rows(number, gain_term):
            at = pl.ds(pl.multiple_of(number * some, some), some)
            values, incoming = rows_ref[at, :].astype(f32), out_ref[at, :]
            inv = lax.rsqrt(jnp.mean(values * values, -1, keepdims=True) + EPS)
            grad, gain_part = norm_back(
                upstream_ref[at, :].astype(f32), incoming, values * inv, inv, gain_ref[...]
            )
            outs[0][at, :] = grad.astype(outs[0].dtype)
            return gain_term + gain_part[None, :]

        outs[1][...] = lax.fori_loop(0, rows // some, norm_rows, jnp.zeros((1, width), f32))
    for one in started:
        one.wait_send()
    if extra:
        term.finish()
    line.end()


def product_scattered(
    a, b, turned, extra=None, base=None, back=None, dtype=f32, steps=None, **line
):
    length, depth = a.shape
    width = b.shape[0] if turned else b.shape[1]
    rows = length // 8
    ins = [(a, ANY), (b, ANY)]
    outs = [(jax.ShapeDtypeStruct((rows, width), dtype), VMEM)]
    after = "back" if back else "base" if dtype == f32 else "cast"
    if back:
        outs.append((jax.ShapeDtypeStruct((1, width), f32), VMEM))
    piece = (rows, width // 2)
    scratch = [
        pltpu.VMEM((2, 2 * rows, width // 2), f32),
        pltpu.VMEM((8,) + piece, bf16),
        pltpu.VMEM((8,) + piece, bf16),
        pltpu.VMEM((6,) + piece, bf16),
        pltpu.VMEM((2,) + piece, bf16),
        pltpu.VMEM((4,) + piece, bf16),
        pltpu.SemaphoreType.DMA((14,)),
        pltpu.SemaphoreType.DMA((14,)),
    ]
    flops, kind = 2 * length * depth * width, None
    if extra:
        first, second = extra
        kind = "own" if second is None else "loaded"
        ins.append((first, ANY))
        columns = a if second is None else second
        tall = first.shape[1] // 8
        outs.append((jax.ShapeDtypeStruct((8, tall, columns.shape[1]), bf16), ANY))
        scratch += [
            pltpu.VMEM((2, length, tall), bf16),
            pltpu.VMEM((tall, length), bf16),
            pltpu.VMEM((2, tall, columns.shape[1]), bf16),
            pltpu.SemaphoreType.DMA((2, 2)),
        ]
        if second is not None:
            ins.append((second, ANY))
            scratch.append(pltpu.VMEM(second.shape, bf16))
        flops += 2 * length * first.shape[1] * columns.shape[1]
    ins += [(array, VMEM) for array in (back or (base,))]
    if after != "base":
        scratch.append(pltpu.VMEM((rows, width), f32))
    scratch += [
        pltpu.VMEM(a.shape, bf16), pltpu.VMEM(b.shape, bf16), pltpu.SemaphoreType.DMA((7,))
    ]
    return run(
        functools.partial(scatter_kernel, turned, kind, after, steps or {}), ins, outs, scratch,
        line.pop("number"), (flops, 150 * rows * width * 2, 0), vmem=61, **line,
    )


def tail_kernel(ready, later, ins, outs, scratch, line):
    qkv_ref, gains_ref = ins[:2]
    chunk_refs = dict(zip(ready, ins[2:]))
    gate_ref, up_ref, qkv_rows_ref, gains_out_ref = outs
    from_group, mine, from_rep, sends, recvs, chunk_sems, local = scratch
    me, rank = other(0, 0, 0), lax.axis_index("rep")
    inner = gate_ref.shape[1] // 8
    part = qkv_ref.shape[-1]
    high = line.outs[later[0]].shape[1]
    barrier = pltpu.get_barrier_semaphore()
    for flip in range(1, 4):
        pl.semaphore_signal(
            barrier, inc=1, device_id={"rep": (rank + flip) % 4}, device_id_type=MESH
        )
    for flip in EVERYONE:
        pl.semaphore_signal(barrier, inc=1, device_id={"grp": other(*flip)}, device_id_type=MESH)
    pl.semaphore_wait(barrier, 10)
    waits, moves = [], Moves(local)
    line.refs["qkv"] = qkv_rows_ref

    def send(kind, number, src, dst, device):
        return pltpu.make_async_remote_copy(
            src_ref=src, dst_ref=dst, send_sem=sends.at[kind, number],
            recv_sem=recvs.at[kind, number], device_id=device, device_id_type=MESH,
        )

    own_qkv = qkv_rows_ref.at[me // 4, :, :, pl.ds(pl.multiple_of((me % 4) * part, part), part)]
    qkv_copies, gain_copies = [], []
    for number, flip in enumerate(EVERYONE):
        target = other(*flip)
        qkv_copies.append(send(0, number, qkv_ref.at[target], own_qkv, {"grp": target}))
        qkv_copies[-1].start()
    moves.later(qkv_ref.at[me], own_qkv)
    line.start()
    for number, flip in enumerate(EVERYONE):
        target = other(*flip)
        gain_copies.append(
            send(1, number, gains_ref.at[target], from_group.at[me], {"grp": target})
        )
        gain_copies[-1].start()
    from_group[me] = gains_ref[me]

    def spread(chunk):
        src = chunk_refs[chunk] if chunk in chunk_refs else line.outs[chunk]
        number = chunk - DOWN
        rows = slice(number // 2 * high, (number // 2 + 1) * high)
        dst = (gate_ref, up_ref)[number % 2]
        there = dst.at[rows, pl.ds(pl.multiple_of(me * inner, inner), inner)]
        for flip in EVERYONE:
            target = other(*flip)
            pltpu.make_async_remote_copy(
                src_ref=src.at[target], dst_ref=there, send_sem=chunk_sems.at[0, number],
                recv_sem=chunk_sems.at[1, number], device_id={"grp": target}, device_id_type=MESH,
            ).start()
        moves.later(src.at[me], there)
        seven = dst.at[rows, : 7 * inner]
        waits.append(
            pltpu.make_async_remote_copy(
                src_ref=seven, dst_ref=seven, send_sem=chunk_sems.at[0, number],
                recv_sem=chunk_sems.at[1, number], device_id={"grp": other(0, 0, 1)},
                device_id_type=MESH,
            )
        )

    for chunk in ready:
        spread(chunk)
    for one in gain_copies:
        one.wait()
    mine[rank] = sum(from_group[g] for g in range(8))
    rep_copies = []
    for step in range(1, 4):
        target = (rank + step) % 4
        rep_copies.append(
            send(2, step, mine.at[rank], from_rep.at[step], {"rep": target})
        )
        rep_copies[-1].start()
    for step, one in zip(range(1, 4), rep_copies):
        one.wait()
        mine[(rank + 4 - step) % 4] = from_rep[step]
    gains_out_ref[...] = (mine[0] + mine[1]) + (mine[2] + mine[3])
    for settled in range(line.ticks - LAG):
        if line.first + settled + LAG == CHUNKS - QKV:
            for one in qkv_copies:
                one.wait()
            moves.open.pop(0).wait()
        line.step()
        chunk = line.first + settled - 2 * LAG
        if chunk in later:
            spread(chunk)
    line.end()
    for one in waits:
        one.wait_send()
        one.wait_recv()
    moves.finish()


def tail(qkv_term, gains, chunks, inner, number, sums, ticks, arrays, picks):
    first = sums.tick
    ready = sorted(chunks)
    later = [c for c in line_slots(first, ticks) if c < DOWN + GATE_UP]
    _, high, width = sums.shape
    wide = jax.ShapeDtypeStruct((GATE_UP // 2 * high, 8 * inner), bf16)
    moved = jax.ShapeDtypeStruct((2, 8, 2 * high, 2 * width), bf16)
    picks = dict(picks)
    for n in range(QKV):
        where = (
            n // 4, slice(None), slice(n // 2 % 2 * high, (n // 2 % 2 + 1) * high),
            slice(n % 2 * width, (n % 2 + 1) * width),
        )
        picks[CHUNKS - QKV + n] = ("qkv", lambda ref, where=where: ref.at[where])
    return run(
        functools.partial(tail_kernel, ready, later),
        [(qkv_term, ANY), (gains, VMEM)] + [(chunks[c], ANY) for c in ready],
        [(wide, ANY), (wide, ANY), (moved, ANY), (jax.ShapeDtypeStruct(gains.shape[1:], f32), VMEM)],
        [
            pltpu.VMEM(gains.shape, f32),
            pltpu.VMEM((4,) + gains.shape[1:], f32),
            pltpu.VMEM((4,) + gains.shape[1:], f32),
            pltpu.SemaphoreType.DMA((3, 7)),
            pltpu.SemaphoreType.DMA((3, 7)),
            pltpu.SemaphoreType.DMA((2, GATE_UP)),
            pltpu.SemaphoreType.DMA((1 + GATE_UP,)),
        ],
        number, (0, 200 * 8 * high * width * 2, 0), sums=sums, ticks=ticks, arrays=arrays, picks=picks,
    )


def finish_kernel(heads, *refs):
    chunks, rest = refs[: DOWN + OUT + QKV], refs[DOWN + OUT + QKV :]
    gate_rows, up_rows = rest[:2]
    query, key, value, out, gate, up, down = rest[2:9]
    low, wide, load_sems, store_sems = rest[9:]
    _, high, width = chunks[0].shape
    depth = low.shape[0]

    def half(number):
        return slice(number * high, (number + 1) * high)

    def side(number):
        return slice(number * width, (number + 1) * width)

    jobs = []
    for n, ref in enumerate(chunks[:DOWN]):
        jobs.append((ref, [(slice(0, width), down.at[n // 2, :, :, side(n % 2)])]))
    for ref, into in ((gate_rows, gate), (up_rows, up)):
        for low_col in range(0, ref.shape[2], low.shape[3]):
            for number in (0, 1):
                where = (slice(None), half(number), slice(low_col, low_col + low.shape[3]))
                jobs.append((ref.at[where], [(slice(0, low.shape[3]), into.at[where])]))
    for n, ref in enumerate(chunks[DOWN : DOWN + OUT]):
        jobs.append((ref, [(slice(0, width), out.at[:, half(n // 2), side(n % 2)])]))
    part = (heads + 2) * HD
    for n, ref in enumerate(chunks[DOWN + OUT :]):
        stores = []
        for place in range(width // part):
            at, device = place * part, (n // 4 * 2 + n % 2) * (width // part) + place
            for into, first, size in (
                (query, 0, heads * HD), (key, heads * HD, HD), (value, (heads + 1) * HD, HD)
            ):
                there = into.at[:, half(n // 2 % 2), device * size : (device + 1) * size]
                stores.append((slice(at + first, at + first + size), there))
        jobs.append((ref, stores))

    def load(number):
        at, ref = number % depth, jobs[number][0]
        return pltpu.make_async_copy(ref, low.at[at, :, :, : ref.shape[2]], load_sems.at[at])

    def stores(number):
        at = number % depth
        return [
            pltpu.make_async_copy(wide.at[at, :, :, cols], into, store_sems.at[at, which])
            for which, (cols, into) in enumerate(jobs[number][1])
        ]

    for number in range(depth - 1):
        load(number).start()
    for number in range(len(jobs)):
        if number + depth - 1 < len(jobs):
            load(number + depth - 1).start()
        load(number).wait()
        if number >= depth:
            for one in stores(number - depth):
                one.wait()

        def cast(g, _, at=number % depth, cols=slice(0, jobs[number][0].shape[2])):
            wide[at, g, :, cols] = low[at, g, :, cols].astype(f32)
            return 0

        lax.fori_loop(0, low.shape[1], cast, 0)
        for one in stores(number):
            one.start()
    for number in range(len(jobs) - depth, len(jobs)):
        for one in stores(number):
            one.wait()


def finish(chunks, gate_rows, up_rows, heads):
    eight, high, width = chunks[0].shape
    width = 2 * width
    rows, wide = gate_rows.shape

    def split(columns):
        return jax.ShapeDtypeStruct((eight, rows // eight, columns), f32)

    shapes = [split(columns) for columns in (8 * heads * HD, 8 * HD, 8 * HD, width, wide, wide)]
    shapes.append(jax.ShapeDtypeStruct((DOWN // 2, eight, high, width), f32))
    depth = 12
    results = pl.pallas_call(
        functools.partial(finish_kernel, heads),
        out_shape=tuple(shapes),
        in_specs=[pl.BlockSpec(memory_space=pl.ANY)] * (len(chunks) + 2),
        out_specs=tuple([pl.BlockSpec(memory_space=pl.ANY)] * 7),
        scratch_shapes=[
            pltpu.VMEM((depth, eight, high, width), bf16),
            pltpu.VMEM((depth, eight, high, width), f32),
            pltpu.SemaphoreType.DMA((depth,)),
            pltpu.SemaphoreType.DMA((depth, 12)),
        ],
        compiler_params=pltpu.CompilerParams(vmem_limit_bytes=60 * 2**20),
        cost_estimate=pl.CostEstimate(
            flops=0, bytes_accessed=3 * CHUNKS * eight * high * width, transcendentals=0
        ),
    )(
        *chunks, gate_rows.reshape(eight, rows // eight, wide),
        up_rows.reshape(eight, rows // eight, wide),
    )
    flat = [result.reshape(rows, -1) for result in results[:6]]
    return flat + [results[6].reshape(-1, width)]


def sum_over_sequences(term):
    return lax.psum(term, "rep").astype(f32)


def on_device(
    layer_input,
    cotangent,
    cut_order,
    piece_ids,
    w_query,
    w_key,
    w_value,
    w_out,
    w_gate,
    w_up,
    w_down,
    gain_attn,
    gain_ffn,
):
    groups = lax.axis_size("grp")
    reps = lax.axis_size("rep")
    own_index = lax.axis_index("grp")
    _, local_rows, model_width = layer_input.shape
    length = piece_ids.shape[1]
    rows_here = w_query.shape[0]
    q_width = w_query.shape[1]
    kv_heads = w_key.shape[1] // HD
    heads = q_width // HD // groups
    copies = groups // kv_heads
    hidden_here = w_down.shape[0]
    cosine, sine = turn_tables(length)

    near = groups == 8 and reps == 4 and copies == 1 and 2 * hidden_here == model_width

    def gather(rows):
        return lax.all_gather(rows, "grp", axis=0, tiled=True)

    def scatter(first, second, turned):
        term = against_rows(first, second) if turned else matmul_f32(first, second)
        return lax.psum_scatter(
            term.astype(bf16), "grp", scatter_dimension=0, tiled=True
        ).astype(f32)

    def to_columns(parts):
        return lax.all_to_all(parts, "grp", 1, 0, tiled=True).reshape(-1, parts.shape[-1])

    def per_group(weight):
        return weight.reshape(rows_here, groups, -1)

    def per_kv_head(weight):
        return jnp.repeat(weight.reshape(rows_here, kv_heads, HD), copies, axis=1)

    x_rows = layer_input.reshape(local_rows, model_width)
    x_flat = x_rows.astype(f32)
    inv_one = lax.rsqrt(jnp.mean(x_flat * x_flat, -1, keepdims=True) + EPS)
    unit_one = x_flat * inv_one
    attn_gain, ffn_gain = gain_attn.reshape(1, -1), gain_ffn.reshape(1, -1)
    if near:
        share = rows_here // (4 * reps) * 3
        spread = columns_of_some((w_gate, w_up), share, 11)
        x_first, spread = lax.optimization_barrier((x_rows, spread))
        spread = lax.all_gather(spread, "rep", axis=0)
        normed_one, cols_qkv = gather_normed(
            x_first, attn_gain, (w_query, w_key, w_value), number=1
        )
        last_gate, last_up, normed_one = lax.optimization_barrier(
            (w_gate[reps * share :], w_up[reps * share :], normed_one)
        )
        rest = to_columns(
            jnp.concatenate(
                [part.reshape(rows_here - reps * share, groups, -1) for part in (last_gate, last_up)],
                -1,
            )
        ).reshape(groups, rows_here - reps * share, -1)
    else:
        normed_one = gather(rms_normed(x_flat, attn_gain).astype(bf16))
        cols_qkv = to_columns(
            jnp.concatenate([per_group(w_query), per_kv_head(w_key), per_kv_head(w_value)], -1)
        )
        cols_gate_up = to_columns(jnp.concatenate([per_group(w_gate), per_group(w_up)], -1))
    attended, query, key, value, lse, attended_placed = attend(
        cut_order, normed_one, cols_qkv, cosine, sine, piece_ids, heads
    )
    if near:
        mid = product_scattered(attended, w_out, False, base=x_rows, number=2)[0]
    else:
        mid = x_flat + scatter(attended, w_out, False)
    grad_out = cotangent.reshape(local_rows, model_width)

    back_ins, back_scratch = attend_back_operands(
        cut_order, attended_placed, query, key, value, lse, cosine, sine, piece_ids, heads
    )
    q_here = heads * HD
    if near:
        normed_two, hidden, cols_gate_up, grad_gate_up, down_term = feed_forward(
            mid, ffn_gain, grad_out, spread, rest, w_down, number=3
        )
        cols_gate_up = cols_gate_up.reshape(model_width, -1)
        high, half_width = 2 * rows_here // GATE_UP, model_width // 2
        sums = Sums((8, high, half_width))
        terms = {"down": down_term.reshape(DOWN // 2, 8, high, model_width)}

        def pick_whole(n):
            return "down", lambda ref: ref.at[n // 2, :, :, n % 2 * half_width : (n % 2 + 1) * half_width]

        def pick_rows(name, n):
            rows, side = n // 2 * high, n % 2 * half_width
            return name, lambda ref: ref.at[:, rows : rows + high, side : side + half_width]

        picks = [pick_whole(n) for n in range(DOWN)]
        picks += [pick_rows("gate_up", n) for n in range(GATE_UP)]
        picks += [pick_rows("out", n) for n in range(OUT)]

        def line(number, ticks):
            names = sorted(
                {picks[t][0] for t in range(sums.tick, sums.tick + ticks) if t < len(picks)}
            )
            return dict(
                number=number, ticks=ticks, sums=sums, picks=dict(enumerate(picks)),
                arrays=[(name, terms[name]) for name in names],
            )

        result, terms["gate_up"] = product_scattered(
            hidden, w_down, False, extra=(normed_two, grad_gate_up), base=mid, dtype=bf16,
            steps={1: 1, 3: 1, "early": 1, 7: 1, "late": 1, "later": 1, "latest": 1}, **line(5, 9),
        )
        grad_mid, gain_ffn_term = product_scattered(
            grad_gate_up, cols_gate_up, True, back=(grad_out, mid, ffn_gain),
            steps={0: 1, 2: 1, 3: 1, 4: 1, 5: 1, 7: 1, 12: 1}, **line(6, 10),
        )
        grad_qkv, out_term = attention_back(
            grad_mid, w_out, attended, back_ins, back_scratch, heads, **line(7, 15)
        )
        terms["out"] = out_term.reshape(8, OUT // 2 * high, model_width)
        grad_x, gain_attn_term, qkv_term = product_scattered(
            grad_qkv, cols_qkv, True, extra=(normed_one, None), dtype=bf16,
            back=(grad_mid, x_rows, attn_gain),
            steps={3: 1, "early": 1, 5: 1, "late": 1, "latest": 1}, **line(9, 8),
        )
        gains = jnp.stack([gain_attn_term, gain_ffn_term]).reshape(2, groups, rows_here)
        gains = jnp.pad(jnp.moveaxis(gains, 0, 1), ((0, 0), (0, 6), (0, 0)))
        rest = line(10, CHUNKS + 2 * LAG - sums.tick)
        gate_rows, up_rows, qkv_rows, own_gains = tail(
            qkv_term.reshape(8, 8, 2 * high, -1), gains,
            {c: sums.done[c] for c in sums.done if c >= DOWN}, hidden_here, **rest,
        )
        straight = [n for n in range(CHUNKS) if n < DOWN or n >= DOWN + GATE_UP]
        weight_grads = finish([sums.done[n] for n in straight], gate_rows, up_rows, heads)
        shaped = tuple(rows.reshape(layer_input.shape) for rows in (result, grad_x))
        return shaped + tuple(weight_grads) + (own_gains[0], own_gains[1])

    unit_one = x_flat * inv_one
    inv_two = lax.rsqrt(jnp.mean(mid * mid, -1, keepdims=True) + EPS)
    unit_two = mid * inv_two
    normed_two = gather((unit_two * ffn_gain).astype(bf16))
    grad_all = gather(grad_out)
    gate_up = matmul_f32(normed_two, cols_gate_up)
    gate_proj, up_proj = gate_up[:, :hidden_here], gate_up[:, hidden_here:]
    sigmoid_gate = jax.nn.sigmoid(gate_proj)
    swish = gate_proj * sigmoid_gate
    hidden = (swish * up_proj).astype(bf16)
    gate_part = up_proj * sigmoid_gate * (1.0 + gate_proj * (1.0 - sigmoid_gate))
    down_term = over_tokens(hidden, grad_all).astype(bf16)
    grad_hidden = against_rows(grad_all, w_down)
    grad_gate_up = jnp.concatenate([grad_hidden * gate_part, grad_hidden * swish], 1).astype(bf16)
    grad_mid, gain_ffn_term = norm_back(
        grad_out.astype(f32), scatter(grad_gate_up, cols_gate_up, True), unit_two, inv_two, gain_ffn
    )
    grad_mid_low = gather(grad_mid.astype(bf16))
    grad_attended = against_rows(grad_mid_low, w_out).astype(bf16)
    grad_qkv = attend_back(grad_attended, back_ins, back_scratch, heads)
    grad_x, gain_attn_term = norm_back(
        grad_mid, scatter(grad_qkv, cols_qkv, True), unit_one, inv_one, gain_attn
    )

    def to_rows(term):
        return lax.all_to_all(
            term.astype(bf16).reshape(groups, rows_here, -1), "grp", 0, 0, tiled=True
        )

    def whole_rows(term):
        return jnp.moveaxis(term, 0, 1).reshape(rows_here, -1)

    def kv_rows(term):
        return jnp.sum(
            jnp.moveaxis(term, 0, 1).reshape(rows_here, kv_heads, copies, HD), 2
        ).reshape(rows_here, -1)

    gate_up_term = sum_over_sequences(to_rows(over_tokens(normed_two, grad_gate_up)))
    out_term = sum_over_sequences(over_tokens(attended, grad_mid_low).astype(bf16))
    qkv_term = sum_over_sequences(to_rows(over_tokens(normed_one, grad_qkv)))
    gain_total = lax.psum(jnp.stack([gain_attn_term, gain_ffn_term]), ("grp", "rep"))
    own_gains = lax.dynamic_slice_in_dim(gain_total, own_index * rows_here, rows_here, 1)
    return (
        (mid + scatter(hidden, w_down, False)).astype(bf16).reshape(layer_input.shape),
        grad_x.astype(bf16).reshape(layer_input.shape),
        whole_rows(qkv_term[..., :q_here]),
        kv_rows(qkv_term[..., q_here : q_here + HD]),
        kv_rows(qkv_term[..., q_here + HD :]),
        out_term,
        whole_rows(gate_up_term[..., :hidden_here]),
        whole_rows(gate_up_term[..., hidden_here:]),
        sum_over_sequences(down_term),
        own_gains[0],
        own_gains[1],
    )


def solution(mesh):
    tokens, table, rows, whole = P("rep", "grp", None), P("rep", None), P("grp", None), P()
    return jax.shard_map(
        on_device,
        mesh=mesh,
        in_specs=(tokens, tokens, table, table) + (rows,) * 7 + (whole,) * 2,
        out_specs=(tokens, tokens) + (rows,) * 7 + (P("grp"),) * 2,
        check_vma=False,
    )
```

```python
import functools

import jax
import jax.numpy as jnp
import numpy as np
from jax import lax
from jax.experimental import pallas as pl
from jax.experimental.pallas import tpu as pltpu
from jax.sharding import PartitionSpec as P

HD = 128
EPS = 1e-05
ROPE_BASE = 1000000.0
SCORE_SCALE = HD**-0.5
LOG2E = 1.4426950408889634
TO_EXP2 = SCORE_SCALE * LOG2E
NEG = -1e30

MESH = pl.DeviceIdType.MESH
f32 = jnp.float32
bf16 = jnp.bfloat16


def matmul_f32(first, second):
    return jnp.dot(first, second, preferred_element_type=f32)


def against_rows(first, second):
    return lax.dot_general(first, second, (((1,), (1,)), ((), ())), preferred_element_type=f32)


def over_tokens(first, second):
    return lax.dot_general(first, second, (((0,), (0,)), ((), ())), preferred_element_type=f32)


def turn_tables(length):
    half_size = HD // 2
    inverse = np.float32(ROPE_BASE) ** (-(np.arange(half_size, dtype=np.float32) * 2) / HD)
    angles = np.arange(length, dtype=np.float32)[:, None] * inverse.astype(np.float32)
    cosine, sine = np.cos(angles), np.sin(angles)
    tables = np.concatenate([cosine, cosine], -1), np.concatenate([-sine, sine], -1)
    return tuple(jnp.asarray(table.astype(np.float32)) for table in tables)


def norm_back(upstream, grad_normed, unit_rows, inv_root, gain):
    scaled = grad_normed * gain
    center_term = jnp.mean(scaled * unit_rows, -1, keepdims=True)
    return (
        upstream + inv_root * (scaled - unit_rows * center_term),
        jnp.sum(grad_normed * unit_rows, 0),
    )


def fold_lanes(values, op):
    out = values[:, :HD]
    for at in range(HD, values.shape[1], HD):
        out = op(out, values[:, at : at + HD])
    return out


def as_column(row):
    return jnp.broadcast_to(row, (HD, row.shape[1])).T[:, 0:1]


def as_row(column):
    return jnp.broadcast_to(column, (column.shape[0], HD)).T[0:1, :]


def attend_kernel(
    heads, cuts, block,
    order_ref, rows_hbm, weight_hbm, cos_ref, sin_ref, piece_ref,
    out_ref, q_ref, k_ref, v_ref, lse_ref, placed,
    scores, rows_ref, weight_ref, qkv_ref, sems,
):
    length = rows_ref.shape[0]
    cut = length // cuts
    blocks = length // block
    loads = [pltpu.make_async_copy(weight_hbm, weight_ref, sems.at[blocks])]
    for i in range(blocks):
        at = slice(i * block, (i + 1) * block)
        loads.append(pltpu.make_async_copy(rows_hbm.at[at, :], rows_ref.at[at, :], sems.at[i]))
    for load in loads:
        load.start()

    def place_cut(r, first):
        src = pl.ds(pl.multiple_of(r * cut, cut), cut)
        dst = pl.ds(pl.multiple_of(order_ref[0, first + r] * cut, cut), cut)
        cosine, sine = cos_ref[dst, :], sin_ref[dst, :]
        for h in range(heads + 1):
            part = qkv_ref[src, h * HD : (h + 1) * HD]
            turned = (part * cosine + pltpu.roll(part, HD // 2, 1) * sine).astype(bf16)
            if h < heads:
                q_ref[h, dst, :] = turned
            else:
                k_ref[dst, :] = turned
        v_ref[dst, :] = qkv_ref[src, (heads + 1) * HD :].astype(bf16)
        return first

    loads[0].wait()
    for i in range(blocks):
        loads[1 + i].wait()
        qkv_ref[...] = matmul_f32(rows_ref[i * block : (i + 1) * block, :], weight_ref[...])
        lax.fori_loop(0, block // cut, place_cut, i * (block // cut))

    def one_block(i, _):
        rows = pl.ds(pl.multiple_of(i * block, block), block)
        query = q_ref[:, rows, :].reshape(heads * block, HD)

        def score(j, high):
            cols = pl.ds(pl.multiple_of(j * block, block), block)
            tile = against_rows(query, k_ref[cols, :])
            scores[j] = tile
            return jnp.maximum(high, fold_lanes(tile, jnp.maximum))

        high = lax.fori_loop(0, i, score, jnp.full((heads * block, HD), NEG, f32))
        tile = against_rows(query, k_ref[rows, :])
        q_at = lax.broadcasted_iota(jnp.int32, (block, block), 0)
        k_at = lax.broadcasted_iota(jnp.int32, (block, block), 1)
        k_piece = piece_ref[0:1, rows].astype(f32)
        q_piece = as_column(k_piece)
        allowed = (k_at <= q_at) | ((q_piece != 0) & (q_piece == k_piece))
        tile = jnp.concatenate(
            [jnp.where(allowed, tile[h * block : (h + 1) * block], NEG) for h in range(heads)], 0
        )
        scores[i] = tile
        high = jnp.max(jnp.maximum(high, fold_lanes(tile, jnp.maximum)), 1, keepdims=True)

        def weigh(j, state):
            total, mixed = state
            cols = pl.ds(pl.multiple_of(j * block, block), block)
            prob = jnp.exp2((scores[j] - high) * TO_EXP2)
            total = total + fold_lanes(prob, jnp.add)
            return total, mixed + matmul_f32(prob.astype(bf16), v_ref[cols, :])

        zero = jnp.zeros((heads * block, HD), f32)
        total, mixed = lax.fori_loop(0, i + 1, weigh, (zero, zero))
        total = jnp.sum(total, 1, keepdims=True)
        mixed = (mixed / total).astype(bf16)
        log_total = high * TO_EXP2 + jnp.log2(total)
        for h in range(heads):
            placed[rows, h * HD : (h + 1) * HD] = mixed[h * block : (h + 1) * block]
            lse_ref[h : h + 1, rows] = as_row(log_total[h * block : (h + 1) * block])
        return 0

    lax.fori_loop(0, blocks, one_block, 0)

    def store_cut(r, _):
        dst = pl.ds(pl.multiple_of(r * cut, cut), cut)
        src = pl.ds(pl.multiple_of(order_ref[0, r] * cut, cut), cut)
        out_ref[dst, :] = placed[src, :]
        return 0

    lax.fori_loop(0, cuts, store_cut, 0)


def vmem_specs(count):
    return [pl.BlockSpec(memory_space=pltpu.VMEM)] * count


def attend(order, rows, weight, cosine, sine, piece, heads):
    length, width = rows.shape
    block = min(512, length)
    return pl.pallas_call(
        functools.partial(attend_kernel, heads, order.shape[1], block),
        out_shape=(
            jax.ShapeDtypeStruct((length, heads * HD), bf16),
            jax.ShapeDtypeStruct((heads, length, HD), bf16),
            jax.ShapeDtypeStruct((length, HD), bf16),
            jax.ShapeDtypeStruct((length, HD), bf16),
            jax.ShapeDtypeStruct((heads, length), f32),
            jax.ShapeDtypeStruct((length, heads * HD), bf16),
        ),
        in_specs=[pl.BlockSpec(memory_space=pltpu.SMEM)]
        + [pl.BlockSpec(memory_space=pl.ANY)] * 2
        + vmem_specs(3),
        out_specs=tuple(vmem_specs(6)),
        scratch_shapes=[
            pltpu.VMEM((length // block, heads * block, block), f32),
            pltpu.VMEM(rows.shape, bf16),
            pltpu.VMEM(weight.shape, bf16),
            pltpu.VMEM((block, weight.shape[1]), f32),
            pltpu.SemaphoreType.DMA((length // block + 1,)),
        ],
        compiler_params=pltpu.CompilerParams(vmem_limit_bytes=60 * 2**20),
        cost_estimate=pl.CostEstimate(
            flops=3 * heads * length * length * HD + 2 * length * width * weight.shape[1],
            bytes_accessed=10 * length * HD * heads * 4 + rows.size * 2,
            transcendentals=heads * length * length // 2,
        ),
    )(order, rows, weight, cosine, sine, piece)


DOWN, GATE_UP, OUT, QKV = 16, 32, 4, 8
CHUNKS = DOWN + GATE_UP + OUT + QKV
LAG = 3


def is_chunk(number):
    return 0 <= number < CHUNKS


def is_middle():
    rank = lax.axis_index("rep")
    return (rank == 1) | (rank == 2)


def is_end():
    rank = lax.axis_index("rep")
    return (rank == 0) | (rank == 3)


class NoLine:
    ticks = 0

    def signal(self, barrier):
        pass

    def greet(self, barrier, others):
        if others:
            pl.semaphore_wait(barrier, others)

    def start(self):
        pass

    def step(self, times=1):
        pass

    def end(self):
        pass


class Line:
    def __init__(self, first, ticks, picks, refs, outs, scratch):
        self.first, self.ticks, self.picks, self.refs, self.outs = first, ticks, picks, refs, outs
        (
            self.inward, self.across, self.own, self.pair, self.total, self.sems, self.local,
            self.carries,
        ) = scratch
        rank = lax.axis_index("rep")
        self.partner = {"rep": rank + 1 - 2 * (rank % 2)}
        self.peer = {"rep": 3 - rank}
        self.now = 0
        self.kept = []

    def signal(self, barrier):
        pl.semaphore_signal(barrier, inc=1, device_id=self.partner, device_id_type=MESH)

        @pl.when(is_middle())
        def _():
            pl.semaphore_signal(barrier, inc=1, device_id=self.peer, device_id_type=MESH)

    def greet(self, barrier, others):
        @pl.when(is_middle())
        def _():
            pl.semaphore_wait(barrier, others + 2)

        @pl.when(is_end())
        def _():
            pl.semaphore_wait(barrier, others + 1)

    def remote(self, hop, number, src, dst, device):
        return pltpu.make_async_remote_copy(
            src_ref=src, dst_ref=dst, send_sem=self.sems.at[0, hop, number],
            recv_sem=self.sems.at[1, hop, number], device_id=device, device_id_type=MESH,
        )

    def hops(self, number):
        tick = self.first + number
        term = pair = total = None
        if is_chunk(tick):
            which, pick = self.picks[tick]
            term = (
                lambda: self.remote(
                    0, number, pick(self.refs[which]), self.inward.at[number], self.partner
                ),
                lambda: pltpu.make_async_copy(
                    pick(self.refs[which]), self.own.at[tick % LAG], self.local.at[0, number]
                ),
            )
        if is_chunk(tick - LAG):
            held = self.pair.at[(tick - LAG) % (LAG + 1)]
            before = self.refs[f"pair{number}"] if number < LAG else held
            pair = (
                lambda: self.remote(1, number, before, self.across.at[number], self.peer),
                lambda: pltpu.make_async_copy(before, held, self.carries.at[0, number]),
            )
        if is_chunk(tick - 2 * LAG):
            held_total = self.total.at[(tick - 2 * LAG) % (LAG + 1)]
            done = self.refs[f"total{number}"] if number < LAG else held_total
            slot = self.outs[tick - 2 * LAG]
            total = (
                lambda: self.remote(2, number, done, slot, self.partner),
                lambda: pltpu.make_async_copy(held_total, slot, self.local.at[1, number]),
                lambda: pltpu.make_async_copy(done, held_total, self.carries.at[3, number]),
            )
        return term, pair, total

    def open(self, number):
        term, pair, total = self.hops(number)

        @pl.when(is_end())
        def _():
            if term:
                term[0]().start()

        @pl.when(is_middle())
        def _():
            if pair:
                pair[0]().start()
            if total:
                total[0]().start()
            if term:
                term[1]().start()
            if total:
                total[2 if number < LAG else 1]().start()
            if pair and number < LAG:
                pair[1]().start()

    def close(self, number):
        term, pair, total = self.hops(number)

        @pl.when(is_end())
        def _():
            if term:
                term[0]().wait_send()
            if total:
                total[0]().wait_recv()

        @pl.when(is_middle())
        def _():
            if total:
                total[0]().wait_send()
                if number >= LAG:
                    total[1]().wait()
            if pair:
                pair[0]().wait_send()
                pair[0]().wait_recv()
            if term:
                term[0]().wait_recv()

    def add(self, number):
        term, pair, total = self.hops(number)
        tick = self.first + number

        def sum_of(into, first, second):
            def one(g, _):
                into[g] = (first[g].astype(f32) + second[g].astype(f32)).astype(bf16)
                return 0

            lax.fori_loop(0, into.shape[0], one, 0)

        @pl.when(is_middle())
        def _():
            if total and number < LAG:
                total[2]().wait()
                total[1]().start()
            if pair:
                if number < LAG:
                    pair[1]().wait()
                before = tick - LAG
                sum_of(
                    self.total.at[before % (LAG + 1)], self.pair.at[before % (LAG + 1)],
                    self.across.at[number],
                )
            if term:
                term[1]().wait()
                sum_of(self.pair.at[tick % (LAG + 1)], self.own.at[tick % LAG], self.inward.at[number])
            if total and number < LAG:
                total[1]().wait()

    def keep(self, number):
        tick = self.first + number
        which = number - (self.ticks - LAG)
        made = []
        if is_chunk(tick):
            made.append((self.pair.at[tick % (LAG + 1)], self.outs[f"pair{which}"], (1, which)))
        if is_chunk(tick - LAG):
            held = self.total.at[(tick - LAG) % (LAG + 1)]
            made.append((held, self.outs[f"total{which}"], (2, which)))
        copies = [
            lambda src=src, dst=dst, at=at: pltpu.make_async_copy(src, dst, self.carries.at[*at])
            for src, dst, at in made
        ]

        @pl.when(is_middle())
        def _():
            for copy in copies:
                copy().start()

        self.kept += copies

    def start(self):
        for number in range(LAG):
            self.open(number)

    def step(self, times=1):
        for _ in range(times):
            if self.now + LAG < self.ticks:
                self.settle()
                self.open(self.now + LAG - 1)

    def settle(self):
        self.close(self.now)
        self.add(self.now)
        if self.now >= self.ticks - LAG:
            self.keep(self.now)
        self.now += 1

    def end(self):
        while self.now + LAG < self.ticks:
            self.step()
        while self.now < self.ticks:
            self.settle()

        @pl.when(is_middle())
        def _():
            for copy in self.kept:
                copy().wait()


def line_slots(first, ticks):
    return [t - 2 * LAG for t in range(first, first + ticks) if is_chunk(t - 2 * LAG)]


class Sums:
    def __init__(self, shape):
        self.shape, self.tick, self.kept, self.done = shape, 0, {}, {}


def run(kernel, ins, outs, scratch, number, cost, sums=None, ticks=0, arrays=(), picks=None, vmem=58):
    ins, outs, scratch = list(ins), list(outs), list(scratch)
    counts = (len(ins), len(outs), len(scratch))
    first = sums.tick if ticks else 0
    names_in, names_out = [], []
    if ticks:
        for name, array in arrays:
            names_in.append(name)
            ins.append((array, pl.ANY))
        for which in range(LAG):
            for name, chunk_at in ((f"pair{which}", first - LAG), (f"total{which}", first - 2 * LAG)):
                if is_chunk(chunk_at + which):
                    names_in.append(name)
                    ins.append((sums.kept[name], pl.ANY))
        names_out = line_slots(first, ticks)
        after = first + ticks
        for which in range(LAG):
            for name, chunk_at in ((f"pair{which}", after - LAG), (f"total{which}", after - 2 * LAG)):
                if is_chunk(chunk_at + which):
                    names_out.append(name)
        outs += [(jax.ShapeDtypeStruct(sums.shape, bf16), pl.ANY)] * len(names_out)
        scratch += [
            pltpu.VMEM((ticks,) + sums.shape, bf16),
            pltpu.VMEM((ticks,) + sums.shape, bf16),
            pltpu.VMEM((LAG,) + sums.shape, bf16),
            pltpu.VMEM((LAG + 1,) + sums.shape, bf16),
            pltpu.VMEM((LAG + 1,) + sums.shape, bf16),
            pltpu.SemaphoreType.DMA((2, 3, ticks)),
            pltpu.SemaphoreType.DMA((2, ticks)),
            pltpu.SemaphoreType.DMA((4, LAG)),
        ]

    def body(*refs):
        in_refs, rest = refs[: len(ins)], refs[len(ins) :]
        out_refs, scratch_refs = rest[: len(outs)], rest[len(outs) :]
        line = NoLine()
        if ticks:
            line = Line(
                first, ticks, picks, dict(zip(names_in, in_refs[counts[0] :])),
                dict(zip(names_out, out_refs[counts[1] :])), scratch_refs[counts[2] :],
            )
        kernel(in_refs[: counts[0]], out_refs[: counts[1]], scratch_refs[: counts[2]], line)

    results = pl.pallas_call(
        body,
        out_shape=tuple(shape for shape, _ in outs),
        in_specs=[pl.BlockSpec(memory_space=space) for _, space in ins],
        out_specs=tuple(pl.BlockSpec(memory_space=space) for _, space in outs),
        scratch_shapes=scratch,
        compiler_params=pltpu.CompilerParams(
            vmem_limit_bytes=vmem * 2**20,
            **({} if number is None else {"collective_id": number, "has_side_effects": True}),
        ),
        cost_estimate=pl.CostEstimate(
            flops=cost[0], bytes_accessed=cost[1], transcendentals=cost[2]
        ),
    )(*[array for array, _ in ins])
    for name, result in zip(names_out, results[counts[1] :]):
        if name in line_slots(first, ticks):
            sums.done[name] = result
        else:
            sums.kept[name] = result
    if ticks:
        sums.tick += ticks
    return results[: counts[1]]


SMEM, VMEM, ANY = pltpu.SMEM, pltpu.VMEM, pl.ANY


def attend_back_kernel(
    heads, block, ins, outs, scratch, line, entered=False
):
    grad_ref, out_ref, q_ref, k_ref, v_ref, lse_ref, cos_ref, sin_ref, piece_ref, place_ref = ins
    (grad_qkv_ref,) = outs
    grads, centers, grad_q, placed = scratch
    if line.ticks and not entered:
        line.signal(pltpu.get_barrier_semaphore())
        line.greet(pltpu.get_barrier_semaphore(), 0)
        line.start()
    length = grad_ref.shape[0]
    blocks = length // block

    def take_block(i, _):
        rows = pl.ds(pl.multiple_of(i * block, block), block)
        position = lax.broadcasted_iota(jnp.int32, (block, length), 0) + i * block
        chosen = jnp.where(place_ref[...] == position, 1.0, 0.0).astype(bf16)
        taken = matmul_f32(chosen, grad_ref[...]).astype(bf16)
        for h in range(heads):
            grad = taken[:, h * HD : (h + 1) * HD]
            grads[h, rows, :] = grad
            product = grad.astype(f32) * out_ref[rows, h * HD : (h + 1) * HD].astype(f32)
            centers[h, rows, :] = jnp.broadcast_to(
                jnp.sum(product, 1, keepdims=True), (block, HD)
            )
        return 0

    lax.fori_loop(0, blocks, take_block, 0)
    line.step()
    grad_q[...] = jnp.zeros_like(grad_q)

    def key_block(j, _):
        cols = pl.ds(pl.multiple_of(j * block, block), block)
        key, value = k_ref[cols, :], v_ref[cols, :]

        def one(i, state, diagonal):
            grad_key, grad_value = state
            rows = pl.ds(pl.multiple_of(i * block, block), block)
            for h in range(heads):
                query, grad = q_ref[h, rows, :], grads[h, rows, :]
                log_total = lse_ref[h : h + 1, rows]
                center = centers[h, rows, :].T[0:1, :]
                prob = jnp.exp2(against_rows(key, query) * TO_EXP2 - log_total)
                if diagonal:
                    k_at = lax.broadcasted_iota(jnp.int32, (block, block), 0)
                    q_at = lax.broadcasted_iota(jnp.int32, (block, block), 1)
                    q_piece = piece_ref[0:1, cols].astype(f32)
                    k_piece = as_column(q_piece)
                    allowed = (k_at <= q_at) | ((q_piece != 0) & (q_piece == k_piece))
                    prob = jnp.where(allowed, prob, 0.0)
                grad_prob = against_rows(value, grad)
                grad_score = (prob * (grad_prob - center)).astype(bf16)
                grad_value = grad_value + matmul_f32(prob.astype(bf16), grad)
                grad_key = grad_key + matmul_f32(grad_score, query)
                grad_q[h, rows, :] += over_tokens(grad_score, key)
            return grad_key, grad_value

        zero = jnp.zeros((block, HD), f32)
        state = one(j, (zero, zero), True)
        grad_key, grad_value = lax.fori_loop(
            j + 1, blocks, functools.partial(one, diagonal=False), state
        )
        grad_key = grad_key * SCORE_SCALE
        grad_key = grad_key * cos_ref[cols, :] - pltpu.roll(grad_key, HD // 2, 1) * sin_ref[cols, :]
        placed[cols, heads * HD : (heads + 1) * HD] = grad_key.astype(bf16)
        placed[cols, (heads + 1) * HD :] = grad_value.astype(bf16)
        return 0

    for j in range(min(2, blocks - 1)):
        lax.fori_loop(j, j + 1, key_block, 0)
        line.step(2 - j)
    lax.fori_loop(min(2, blocks - 1), blocks, key_block, 0)

    def turn_back(i, _):
        rows = pl.ds(pl.multiple_of(i * block, block), block)
        for h in range(heads):
            grad = grad_q[h, rows, :] * SCORE_SCALE
            grad = grad * cos_ref[rows, :] - pltpu.roll(grad, HD // 2, 1) * sin_ref[rows, :]
            placed[rows, h * HD : (h + 1) * HD] = grad.astype(bf16)
        return 0

    lax.fori_loop(0, blocks, turn_back, 0)
    line.step()

    def store_block(i, _):
        rows = pl.ds(pl.multiple_of(i * block, block), block)
        place = as_column(place_ref[0:1, rows].astype(f32)).astype(jnp.int32)
        position = lax.broadcasted_iota(jnp.int32, (block, length), 1)
        chosen = jnp.where(place == position, 1.0, 0.0).astype(bf16)
        grad_qkv_ref[rows, :] = matmul_f32(chosen, placed[...]).astype(bf16)
        return 0

    lax.fori_loop(0, blocks, store_block, 0)
    line.end()


def attend_back_operands(order, out, query, key, value, lse, cosine, sine, piece, heads):
    length = out.shape[0]
    cut = length // order.shape[1]
    place = (order.reshape(-1, 1) * cut + jnp.arange(cut, dtype=order.dtype)).reshape(1, length)
    scratch = [
        pltpu.VMEM((heads, length, HD), bf16),
        pltpu.VMEM((heads, length, HD), f32),
        pltpu.VMEM((heads, length, HD), f32),
        pltpu.VMEM((length, (heads + 2) * HD), bf16),
    ]
    return [out, query, key, value, lse, cosine, sine, piece, place], scratch


def attend_back(grad, operands, scratch, heads):
    length = grad.shape[0]
    return run(
        functools.partial(attend_back_kernel, heads, min(512, length)),
        [(array, VMEM) for array in [grad] + operands],
        [(jax.ShapeDtypeStruct((length, (heads + 2) * HD), bf16), VMEM)],
        scratch,
        None,
        (8 * heads * length * length * HD, 14 * length * HD * heads * 4, heads * length * length // 2),
    )[0]


def place_in_group():
    me = lax.axis_index("grp")
    return me // 4, (me // 2) % 2, me % 2


def other(flip_y, flip_x, flip_core):
    y, x, core = place_in_group()
    return ((y + flip_y) % 2) * 4 + ((x + flip_x) % 2) * 2 + (core + flip_core) % 2


def chip_rows(flip_y, flip_x, rows):
    y, x, _ = place_in_group()
    first = (((y + flip_y) % 2) * 2 + (x + flip_x) % 2) * (2 * rows)
    return pl.ds(pl.multiple_of(first, 2 * rows), 2 * rows)


NEIGHBOURS = ((0, 0, 1), (0, 1, 0), (1, 0, 0))
EVERYONE = tuple((n // 4, (n // 2) % 2, n % 2) for n in range(1, 8))


def greet_group(line, flips=NEIGHBOURS, between=None):
    barrier = pltpu.get_barrier_semaphore()
    for flip in flips:
        pl.semaphore_signal(barrier, inc=1, device_id={"grp": other(*flip)}, device_id_type=MESH)
    line.signal(barrier)
    if between:
        between()
    line.greet(barrier, len(flips))


SIBLING, ALONG_X, ALONG_Y, ACROSS = (0, 0), (0, 1), (1, 0), (1, 1)


class Gather:
    TO_S, TO_X, TO_Y = (0, 0, 1), (0, 1, 0), (1, 0, 0)

    def __init__(self, rows, all_ref, sends, recvs):
        self.rows, self.all_ref, self.sends, self.recvs = rows, all_ref, sends, recvs
        self.started = []

    def copy(self, number, chip, core, part, target):
        first = other(*chip, core) * self.rows
        if part is None:
            where = pl.ds(pl.multiple_of(first, self.rows), self.rows)
        else:
            half = self.rows // 2
            where = pl.ds(pl.multiple_of(first + part * half, half), half)
        where = self.all_ref.at[where, :]
        return pltpu.make_async_remote_copy(
            src_ref=where, dst_ref=where, send_sem=self.sends.at[number],
            recv_sem=self.recvs.at[number], device_id={"grp": other(*target)}, device_id_type=MESH,
        )

    def send(self, *what):
        one = self.copy(*what)
        one.start()
        self.started.append(one)

    def landed(self, number, chip, core, part):
        self.copy(number, chip, core, part, self.TO_S).wait_recv()

    def send_own(self):
        self.send(1, SIBLING, 0, 1, self.TO_X)
        self.send(3, SIBLING, 0, 0, self.TO_Y)
        self.send(0, SIBLING, 0, None, self.TO_S)
        self.send(2, SIBLING, 0, 0, self.TO_X)
        self.send(4, SIBLING, 0, 1, self.TO_Y)

    def sibling(self):
        self.landed(0, SIBLING, 1, None)

    def relay(self):
        self.landed(1, ALONG_X, 0, 1)
        self.send(6, ALONG_X, 0, 1, self.TO_Y)
        self.landed(3, ALONG_Y, 0, 0)
        self.send(5, ALONG_Y, 0, 0, self.TO_X)
        self.send(7, ALONG_X, 0, 1, self.TO_S)
        self.send(8, ALONG_Y, 0, 0, self.TO_S)

    def pass_second(self):
        self.landed(2, ALONG_X, 0, 0)
        self.send(9, ALONG_X, 0, 0, self.TO_S)
        self.landed(4, ALONG_Y, 0, 1)
        self.send(10, ALONG_Y, 0, 1, self.TO_S)

    def along_x(self):
        self.landed(7, ALONG_X, 1, 1)
        self.landed(9, ALONG_X, 1, 0)

    def pass_across(self):
        self.landed(5, ACROSS, 0, 0)
        self.send(11, ACROSS, 0, 0, self.TO_S)
        self.landed(6, ACROSS, 0, 1)
        self.send(12, ACROSS, 0, 1, self.TO_S)

    def along_y(self):
        self.landed(8, ALONG_Y, 1, 0)
        self.landed(10, ALONG_Y, 1, 1)

    def across(self):
        self.landed(11, ACROSS, 1, 0)
        self.landed(12, ACROSS, 1, 1)

    def finish(self):
        for one in self.started:
            one.wait_send()


def gather_rows(rows, all_ref, sends, recvs, on_chip, line, then=None, final=True):
    rows_of = Gather(rows, all_ref, sends, recvs)
    rows_of.send_own()
    if then:
        then()
    rows_of.sibling()
    on_chip(*SIBLING)
    rows_of.relay()
    line.step(2)
    rows_of.pass_second()
    line.step(2)
    rows_of.along_x()
    on_chip(*ALONG_X)
    rows_of.pass_across()
    line.step(2)
    rows_of.along_y()
    on_chip(*ALONG_Y)
    rows_of.across()
    on_chip(*ACROSS)
    rows_of.finish()
    if final:
        line.end()
    else:
        line.step()


GATHER_COPIES = 13


def rms_normed(values, gain):
    return values * lax.rsqrt(jnp.mean(values * values, -1, keepdims=True) + EPS) * gain


class Moves:
    def __init__(self, sems):
        self.sems, self.count, self.open = sems, 0, []

    def start(self, src, dst):
        one = pltpu.make_async_copy(src, dst, self.sems.at[self.count])
        self.count += 1
        one.start()
        return one

    def later(self, src, dst):
        self.open.append(self.start(src, dst))

    def finish(self):
        for one in self.open:
            one.wait()


def gather_scratch(rows, width, moves):
    return [
        pltpu.VMEM((8 * rows, width), bf16),
        pltpu.SemaphoreType.DMA((GATHER_COPIES,)),
        pltpu.SemaphoreType.DMA((GATHER_COPIES,)),
        pltpu.SemaphoreType.DMA((moves,)),
    ]


def own_rows(rows):
    return pl.ds(pl.multiple_of(other(0, 0, 0) * rows, rows), rows)


def send_columns(pieces, sends, recvs, moves):
    copies = []
    for which, (rows_ref, width, there) in enumerate(pieces):
        for number, flip in enumerate(EVERYONE):
            target = other(*flip)
            cols = pl.ds(pl.multiple_of(target * width, width), width)
            one = pltpu.make_async_remote_copy(
                src_ref=rows_ref.at[:, cols], dst_ref=there,
                send_sem=sends.at[which, number], recv_sem=recvs.at[which, number],
                device_id={"grp": target}, device_id_type=MESH,
            )
            one.start()
            copies.append(one)
        mine = pl.ds(pl.multiple_of(other(0, 0, 0) * width, width), width)
        moves.later(rows_ref.at[:, mine], there)
    return copies


def gather_normed_kernel(ins, outs, scratch, line):
    x_ref, gain_ref = ins[:2]
    weights = ins[2:]
    all_ref, cols_ref = outs
    held, sends, recvs, sems, col_sends, col_recvs = scratch
    rows = x_ref.shape[0]
    moves = Moves(sems)

    def fill():
        held[own_rows(rows), :] = rms_normed(x_ref[...].astype(f32), gain_ref[...]).astype(bf16)

    greet_group(line, EVERYONE, fill)
    col_copies = []

    def send_weights():
        pieces, low = [], 0
        tall = weights[0].shape[0]
        there = pl.ds(pl.multiple_of(other(0, 0, 0) * tall, tall), tall)
        for weight in weights:
            width = weight.shape[1] // 8
            pieces.append((weight, width, cols_ref.at[there, low : low + width]))
            low += width
        col_copies.extend(send_columns(pieces, col_sends, col_recvs, moves))

    def on_chip(*chip):
        where = chip_rows(*chip, rows)
        moves.later(held.at[where, :], all_ref.at[where, :])

    gather_rows(rows, held, sends, recvs, on_chip, line, send_weights)
    for one in col_copies:
        one.wait()
    moves.finish()


def gather_normed(x, gain, weights, **line):
    rows, width = x.shape
    deep = sum(weight.shape[1] for weight in weights) // 8
    return run(
        gather_normed_kernel,
        [(x, VMEM), (gain, VMEM)] + [(weight, ANY) for weight in weights],
        [
            (jax.ShapeDtypeStruct((8 * rows, width), bf16), ANY),
            (jax.ShapeDtypeStruct((8 * weights[0].shape[0], deep), bf16), ANY),
        ],
        gather_scratch(rows, width, 4 + len(weights))
        + [pltpu.SemaphoreType.DMA((len(weights), 7))] * 2,
        line.pop("number"),
        (0, 150 * rows * width * 2, 0),
        **line,
    )


def columns_kernel(rows_here, ins, outs, scratch, line):
    (cols_ref,) = outs
    sends, recvs, sems = scratch
    moves = Moves(sems)
    barrier = pltpu.get_barrier_semaphore()
    for flip in EVERYONE:
        pl.semaphore_signal(barrier, inc=1, device_id={"grp": other(*flip)}, device_id_type=MESH)
    pl.semaphore_wait(barrier, 7)
    first = pl.multiple_of(lax.axis_index("rep") * rows_here, rows_here)
    me = other(0, 0, 0)
    pieces, low = [], 0
    for weight in ins:
        width = weight.shape[1] // 8
        pieces.append(
            (weight.at[pl.ds(first, rows_here), :], width, cols_ref.at[me, :, low : low + width])
        )
        low += width
    for one in send_columns(pieces, sends, recvs, moves):
        one.wait()
    moves.finish()


def columns_of_some(weights, rows_here, number):
    deep = sum(weight.shape[1] for weight in weights) // 8
    return run(
        functools.partial(columns_kernel, rows_here),
        [(weight, ANY) for weight in weights],
        [(jax.ShapeDtypeStruct((8, rows_here, deep), bf16), ANY)],
        [pltpu.SemaphoreType.DMA((len(weights), 7))] * 2
        + [pltpu.SemaphoreType.DMA((len(weights),))],
        number, (0, 50 * 8 * rows_here * deep, 0),
    )[0]


def feed_forward_kernel(tile, ins, outs, scratch, line):
    mid_ref, gain_ref, grad_ref, spread_ref, rest_ref, w_down_ref = ins
    all_ref, hidden_ref, whole_ref, grad_gate_up_ref, down_ref = outs
    held, grads_held, sends, recvs, grad_sends, grad_recvs, sems = scratch[:7]
    weight, w_down, hidden, up_part, gate_part, grads, down = scratch[7:]
    rows = mid_ref.shape[0]
    inner = hidden.shape[1]
    moves = Moves(sems)
    planes, _, tall, _ = spread_ref.shape
    loads = [
        moves.start(spread_ref.at[z], weight.at[:, z * tall : (z + 1) * tall, :])
        for z in range(planes)
    ]
    loads.append(moves.start(rest_ref, weight.at[:, planes * tall :, :]))
    down_load = moves.start(w_down_ref, w_down)

    def fill():
        held[own_rows(rows), :] = rms_normed(mid_ref[...], gain_ref[...]).astype(bf16)
        grads_held[own_rows(rows), :] = grad_ref[...]

    greet_group(line, between=fill)
    first = Gather(rows, held, sends, recvs)
    second = Gather(rows, grads_held, grad_sends, grad_recvs)
    stored = []

    def forward(*chip):
        where = chip_rows(*chip, rows)
        moves.later(held.at[where, :], all_ref.at[where, :])

        def column(t, _):
            cols = pl.ds(pl.multiple_of(t * tile, tile), tile)
            up_cols = pl.ds(pl.multiple_of(inner + t * tile, tile), tile)
            lhs = held[where, :]
            gate = matmul_f32(lhs, weight[:, :, cols].reshape(-1, tile))
            up = matmul_f32(lhs, weight[:, :, up_cols].reshape(-1, tile))
            sigma = 1.0 / (1.0 + jnp.exp(-gate))
            swish = gate * sigma
            hidden[where, cols] = (swish * up).astype(bf16)
            up_part[where, cols] = swish.astype(bf16)
            gate_part[where, cols] = (up * sigma * (1.0 + gate * (1.0 - sigma))).astype(bf16)
            return 0

        lax.fori_loop(0, inner // tile, column, 0)
        moves.later(hidden.at[where, :], hidden_ref.at[where, :])

    def backward(*chip):
        where = chip_rows(*chip, rows)
        slot = len(stored) % 2
        if len(stored) >= 2:
            stored[len(stored) - 2].wait()

        def column(t, _):
            cols = pl.ds(pl.multiple_of(t * tile, tile), tile)
            up_cols = pl.ds(pl.multiple_of(inner + t * tile, tile), tile)
            incoming = grads_held[where, :]
            grad_hidden = against_rows(incoming, w_down[cols, :])
            grads[slot, :, cols] = (grad_hidden * gate_part[where, cols].astype(f32)).astype(bf16)
            grads[slot, :, up_cols] = (grad_hidden * up_part[where, cols].astype(f32)).astype(bf16)
            term = over_tokens(hidden[where, cols], incoming)
            if chip == SIBLING:
                down[cols, :] = term
            elif chip == ACROSS:
                weight[t] = (down[cols, :] + term).astype(bf16)
            else:
                down[cols, :] += term
            return 0

        lax.fori_loop(0, inner // tile, column, 0)
        stored.append(moves.start(grads.at[slot], grad_gate_up_ref.at[where, :]))

    first.send_own()
    for one in loads:
        one.wait()
    whole = moves.start(weight, whole_ref)
    first.sibling()
    forward(*SIBLING)
    first.relay()
    first.pass_second()
    second.send_own()
    first.along_x()
    forward(*ALONG_X)
    first.pass_across()
    first.along_y()
    forward(*ALONG_Y)
    first.across()
    forward(*ACROSS)
    second.relay()
    down_load.wait()
    second.sibling()
    backward(*SIBLING)
    second.pass_second()
    second.along_x()
    backward(*ALONG_X)
    second.pass_across()
    second.along_y()
    backward(*ALONG_Y)
    second.across()
    whole.wait()
    backward(*ACROSS)
    moves.later(weight.at[: inner // tile], down_ref)
    first.finish()
    second.finish()
    for one in stored[-2:]:
        one.wait()
    moves.finish()


def feed_forward(mid, gain, grad, spread, rest, w_down, **line):
    rows, width = mid.shape
    inner = w_down.shape[0]
    weight = (8, width // 8, 2 * inner)
    return run(
        functools.partial(feed_forward_kernel, weight[1]),
        [(mid, VMEM), (gain, VMEM), (grad, VMEM), (spread, ANY), (rest, ANY), (w_down, ANY)],
        [
            (jax.ShapeDtypeStruct((8 * rows, width), bf16), ANY),
            (jax.ShapeDtypeStruct((8 * rows, inner), bf16), ANY),
            (jax.ShapeDtypeStruct(weight, bf16), ANY),
            (jax.ShapeDtypeStruct((8 * rows, 2 * inner), bf16), ANY),
            (jax.ShapeDtypeStruct((inner // weight[1], weight[1], width), bf16), ANY),
        ],
        [pltpu.VMEM((8 * rows, width), bf16)] * 2
        + [pltpu.SemaphoreType.DMA((GATHER_COPIES,))] * 4
        + [pltpu.SemaphoreType.DMA((20,))]
        + [pltpu.VMEM(weight, bf16), pltpu.VMEM(w_down.shape, bf16)]
        + [pltpu.VMEM((8 * rows, inner), bf16)] * 3
        + [
            pltpu.VMEM((2, 2 * rows, 2 * inner), bf16),
            pltpu.VMEM(w_down.shape, f32),
        ],
        line.pop("number"),
        (64 * rows * width * inner, 300 * rows * width * 2, 8 * rows * inner),
        vmem=63,
        **line,
    )


def attention_back_kernel(heads, block, ins, outs, scratch, line):
    grad_ref, w_ref, attended_ref = ins[:3]
    grad_qkv_ref, out_term_ref = outs
    held, sends, recvs, sems, total, grad_attended_ref = scratch[:6]
    rows = grad_ref.shape[0]
    moves = Moves(sems)
    greet_group(line)
    line.start()
    held[own_rows(rows), :] = grad_ref[...].astype(bf16)

    def on_chip(*chip):
        where = chip_rows(*chip, rows)
        incoming = held[where, :]
        grad_attended_ref[where, :] = against_rows(incoming, w_ref[...]).astype(bf16)
        term = over_tokens(attended_ref[where, :], incoming)
        if chip == SIBLING:
            total[...] = term
        elif chip == ACROSS:
            out_term_ref[...] = (total[...] + term).astype(bf16)
        else:
            total[...] += term

    gather_rows(rows, held, sends, recvs, on_chip, line, final=False)
    moves.finish()
    attend_back_kernel(
        heads, block, (grad_attended_ref,) + tuple(ins[3:]), (grad_qkv_ref,), scratch[6:], line,
        entered=True,
    )


def attention_back(grad, w_out, attended, back_ins, back_scratch, heads, **line):
    rows, width = grad.shape
    length = 8 * rows
    return run(
        functools.partial(attention_back_kernel, heads, min(512, length)),
        [(array, VMEM) for array in [grad, w_out, attended] + back_ins],
        [
            (jax.ShapeDtypeStruct((length, (heads + 2) * HD), bf16), VMEM),
            (jax.ShapeDtypeStruct(w_out.shape, bf16), VMEM),
        ],
        gather_scratch(rows, width, 1)
        + [pltpu.VMEM(w_out.shape, f32), pltpu.VMEM(attended.shape, bf16)]
        + back_scratch,
        line.pop("number"),
        (
            32 * rows * width * w_out.shape[0] + 8 * heads * length * length * HD,
            250 * rows * width * 2, heads * length * length // 2,
        ),
        **line,
    )


class WeightTerm:
    def __init__(self, rows_ref, columns_ref, term_ref, scratch):
        self.rows_ref, self.columns_ref, self.term_ref = rows_ref, columns_ref, term_ref
        self.loaded, self.flipped, self.ready, self.sems = scratch
        self.tile = self.loaded.shape[2]
        for number in (0, 1):
            self.load(number).start()

    def load(self, number):
        cols = slice(number * self.tile, (number + 1) * self.tile)
        return pltpu.make_async_copy(
            self.rows_ref.at[:, cols], self.loaded.at[number % 2], self.sems.at[0, number % 2]
        )

    def store(self, number):
        return pltpu.make_async_copy(
            self.ready.at[number % 2], self.term_ref.at[number], self.sems.at[1, number % 2]
        )

    def work(self, numbers):
        for number in numbers:
            at = number % 2
            self.load(number).wait()
            if number >= 2:
                self.store(number - 2).wait()
            width = self.columns_ref.shape[1]
            step = min(256, width)
            self.flipped[...] = self.loaded[at].T

            def column(t, _):
                cols = pl.ds(pl.multiple_of(t * step, step), step)
                term = matmul_f32(self.flipped[...], self.columns_ref[:, cols])
                self.ready[at, :, cols] = term.astype(bf16)
                return 0

            lax.fori_loop(0, width // step, column, 0)
            self.store(number).start()
            if number + 2 < 8:
                self.load(number + 2).start()

    def finish(self):
        for number in (6, 7):
            self.store(number).wait()


UNITS = (
    (ACROSS, 0), (ACROSS, 1), (ALONG_X, 0), (ALONG_Y, 1), (ALONG_X, 1), (ALONG_Y, 0),
    (SIBLING, 0), (SIBLING, 1),
)


def scatter_kernel(turned, extra, after, steps, ins, outs, scratch, line):
    out_ref = outs[0] if after == "base" else scratch[-4]
    finals = ins[len(ins) - {"base": 1, "cast": 1, "back": 3}[after] :]
    part, to_s, from_s, to_link, relay, last, sends, recvs = scratch[:8]
    a_ref, b_ref, load_sems = scratch[-3:]
    rows, width = out_ref.shape
    half = width // 2
    _, _, core = place_in_group()
    loading = {}

    def load(name, src, dst):
        loading[name] = pltpu.make_async_copy(src, dst, load_sems.at[len(loading)])
        loading[name].start()

    def load_weight(h):
        where = (slice(h * half, (h + 1) * half), slice(None))
        where = where if turned else where[::-1]
        load(h, ins[1].at[where], b_ref.at[where])

    def load_rows(chip):
        where = chip_rows(*chip, rows)
        load(chip, ins[0].at[where, :], a_ref.at[where, :])

    load_weight(0)
    load_rows(ACROSS)
    load_weight(1)
    for chip in (ALONG_X, ALONG_Y, SIBLING):
        load_rows(chip)
    greet_group(line)
    line.start()
    if extra:
        columns_ref = a_ref
        if extra == "loaded":
            columns_ref = scratch[12]
            load("columns", ins[3], columns_ref)
        term = WeightTerm(ins[2], columns_ref, outs[-1], scratch[8:12])
    own_at = pl.multiple_of(core * rows, rows)
    other_at = pl.multiple_of((1 - core) * rows, rows)
    to_sib, to_x, to_y = (0, 0, 1), (0, 1, 0), (1, 0, 0)
    started = []

    def ready(*names):
        for name in names:
            if name in loading:
                loading.pop(name).wait()
                loading[name, "done"] = None

    def send(number, src, dst, target):
        one = pltpu.make_async_remote_copy(
            src_ref=src, dst_ref=dst, send_sem=sends.at[number], recv_sem=recvs.at[number],
            device_id={"grp": other(*target)}, device_id_type=MESH,
        )
        one.start()
        started.append(one)

    def landed(number, where):
        pltpu.make_async_remote_copy(
            src_ref=where, dst_ref=where, send_sem=sends.at[number], recv_sem=recvs.at[number],
            device_id={"grp": other(0, 0, 1)}, device_id_type=MESH,
        ).wait_recv()

    def make(n):
        chip, h = UNITS[n]
        ready(h, chip)
        lhs = a_ref[chip_rows(*chip, rows), :]
        cols = slice(h * half, (h + 1) * half)
        if turned:
            part[n % 2] = against_rows(lhs, b_ref[cols, :])
        else:
            part[n % 2] = matmul_f32(lhs, b_ref[:, cols])
        to_s[n] = part[n % 2, pl.ds(other_at, rows), :].astype(bf16)
        send(n, to_s.at[n], from_s.at[n], to_sib)

    def own(n):
        landed(n, from_s.at[n])
        return part[n % 2, pl.ds(own_at, rows), :] + from_s[n].astype(f32)

    def finish(n):
        _, h = UNITS[n]
        if n < 2:
            to_link[n] = own(n).astype(bf16)
            send(8 + n, to_link.at[n], relay.at[n], (to_x, to_y)[n])
        elif n < 4:
            to_link[n] = own(n).astype(bf16)
            send(8 + n, to_link.at[n], last.at[(None, None, 0, 3)[n]], (to_x, to_y)[n - 2])
        elif n < 6:
            total = own(n)
            landed(8 + h, relay.at[h])
            to_link[n] = (total + relay[h].astype(f32)).astype(bf16)
            send(8 + n, to_link.at[n], last.at[(1, 2)[n - 4]], (to_x, to_y)[n - 4])
        else:
            cols = slice(h * half, (h + 1) * half)
            if after == "back":
                out_ref[:, cols] = own(n)
            else:
                out_ref[:, cols] = own(n) + finals[0][:, cols].astype(f32)
        line.step(steps.get(n, 0))

    def work(numbers, point):
        if extra:
            ready("columns")
            if columns_ref is a_ref:
                ready(*(chip for chip, _ in UNITS))
            term.work(numbers)
        line.step(steps.get(point, 0))

    make(0)
    make(1)
    finish(0)
    make(2)
    finish(1)
    make(3)
    finish(2)
    make(4)
    finish(3)
    make(5)
    work((0, 1), "early")
    finish(4)
    make(6)
    finish(5)
    make(7)
    finish(6)
    finish(7)
    work((2, 3), "late")
    work((4, 5), "later")
    work((6, 7), "latest")
    for number, slot, h in ((10, 0, 0), (11, 3, 1), (12, 1, 1), (13, 2, 0)):
        cols = slice(h * half, (h + 1) * half)
        landed(number, last.at[slot])
        out_ref[:, cols] += last[slot].astype(f32)
        line.step(steps.get(number, 0))
    if after == "cast":
        outs[0][...] = out_ref[...].astype(outs[0].dtype)
    if after == "back":
        upstream_ref, rows_ref, gain_ref = finals
        some = min(64, rows)

        def norm_rows(number, gain_term):
            at = pl.ds(pl.multiple_of(number * some, some), some)
            values, incoming = rows_ref[at, :].astype(f32), out_ref[at, :]
            inv = lax.rsqrt(jnp.mean(values * values, -1, keepdims=True) + EPS)
            grad, gain_part = norm_back(
                upstream_ref[at, :].astype(f32), incoming, values * inv, inv, gain_ref[...]
            )
            outs[0][at, :] = grad.astype(outs[0].dtype)
            return gain_term + gain_part[None, :]

        outs[1][...] = lax.fori_loop(0, rows // some, norm_rows, jnp.zeros((1, width), f32))
    for one in started:
        one.wait_send()
    if extra:
        term.finish()
    line.end()


def product_scattered(
    a, b, turned, extra=None, base=None, back=None, dtype=f32, steps=None, **line
):
    length, depth = a.shape
    width = b.shape[0] if turned else b.shape[1]
    rows = length // 8
    ins = [(a, ANY), (b, ANY)]
    outs = [(jax.ShapeDtypeStruct((rows, width), dtype), VMEM)]
    after = "back" if back else "base" if dtype == f32 else "cast"
    if back:
        outs.append((jax.ShapeDtypeStruct((1, width), f32), VMEM))
    piece = (rows, width // 2)
    scratch = [
        pltpu.VMEM((2, 2 * rows, width // 2), f32),
        pltpu.VMEM((8,) + piece, bf16),
        pltpu.VMEM((8,) + piece, bf16),
        pltpu.VMEM((6,) + piece, bf16),
        pltpu.VMEM((2,) + piece, bf16),
        pltpu.VMEM((4,) + piece, bf16),
        pltpu.SemaphoreType.DMA((14,)),
        pltpu.SemaphoreType.DMA((14,)),
    ]
    flops, kind = 2 * length * depth * width, None
    if extra:
        first, second = extra
        kind = "own" if second is None else "loaded"
        ins.append((first, ANY))
        columns = a if second is None else second
        tall = first.shape[1] // 8
        outs.append((jax.ShapeDtypeStruct((8, tall, columns.shape[1]), bf16), ANY))
        scratch += [
            pltpu.VMEM((2, length, tall), bf16),
            pltpu.VMEM((tall, length), bf16),
            pltpu.VMEM((2, tall, columns.shape[1]), bf16),
            pltpu.SemaphoreType.DMA((2, 2)),
        ]
        if second is not None:
            ins.append((second, ANY))
            scratch.append(pltpu.VMEM(second.shape, bf16))
        flops += 2 * length * first.shape[1] * columns.shape[1]
    ins += [(array, VMEM) for array in (back or (base,))]
    if after != "base":
        scratch.append(pltpu.VMEM((rows, width), f32))
    scratch += [
        pltpu.VMEM(a.shape, bf16), pltpu.VMEM(b.shape, bf16), pltpu.SemaphoreType.DMA((7,))
    ]
    return run(
        functools.partial(scatter_kernel, turned, kind, after, steps or {}), ins, outs, scratch,
        line.pop("number"), (flops, 150 * rows * width * 2, 0), vmem=61, **line,
    )


def tail_kernel(ready, later, ins, outs, scratch, line):
    qkv_ref, gains_ref = ins[:2]
    chunk_refs = dict(zip(ready, ins[2:]))
    gate_ref, up_ref, qkv_rows_ref, gains_out_ref = outs
    from_group, mine, from_rep, sends, recvs, chunk_sems, local = scratch
    me, rank = other(0, 0, 0), lax.axis_index("rep")
    inner = gate_ref.shape[1] // 8
    part = qkv_ref.shape[-1]
    high = line.outs[later[0]].shape[1]
    barrier = pltpu.get_barrier_semaphore()
    for flip in range(1, 4):
        pl.semaphore_signal(
            barrier, inc=1, device_id={"rep": (rank + flip) % 4}, device_id_type=MESH
        )
    for flip in EVERYONE:
        pl.semaphore_signal(barrier, inc=1, device_id={"grp": other(*flip)}, device_id_type=MESH)
    pl.semaphore_wait(barrier, 10)
    waits, moves = [], Moves(local)
    line.refs["qkv"] = qkv_rows_ref

    def send(kind, number, src, dst, device):
        return pltpu.make_async_remote_copy(
            src_ref=src, dst_ref=dst, send_sem=sends.at[kind, number],
            recv_sem=recvs.at[kind, number], device_id=device, device_id_type=MESH,
        )

    own_qkv = qkv_rows_ref.at[me // 4, :, :, pl.ds(pl.multiple_of((me % 4) * part, part), part)]
    qkv_copies, gain_copies = [], []
    for number, flip in enumerate(EVERYONE):
        target = other(*flip)
        qkv_copies.append(send(0, number, qkv_ref.at[target], own_qkv, {"grp": target}))
        qkv_copies[-1].start()
    moves.later(qkv_ref.at[me], own_qkv)
    line.start()
    for number, flip in enumerate(EVERYONE):
        target = other(*flip)
        gain_copies.append(
            send(1, number, gains_ref.at[target], from_group.at[me], {"grp": target})
        )
        gain_copies[-1].start()
    from_group[me] = gains_ref[me]

    def spread(chunk):
        src = chunk_refs[chunk] if chunk in chunk_refs else line.outs[chunk]
        number = chunk - DOWN
        rows = slice(number // 2 * high, (number // 2 + 1) * high)
        dst = (gate_ref, up_ref)[number % 2]
        there = dst.at[rows, pl.ds(pl.multiple_of(me * inner, inner), inner)]
        for flip in EVERYONE:
            target = other(*flip)
            pltpu.make_async_remote_copy(
                src_ref=src.at[target], dst_ref=there, send_sem=chunk_sems.at[0, number],
                recv_sem=chunk_sems.at[1, number], device_id={"grp": target}, device_id_type=MESH,
            ).start()
        moves.later(src.at[me], there)
        seven = dst.at[rows, : 7 * inner]
        waits.append(
            pltpu.make_async_remote_copy(
                src_ref=seven, dst_ref=seven, send_sem=chunk_sems.at[0, number],
                recv_sem=chunk_sems.at[1, number], device_id={"grp": other(0, 0, 1)},
                device_id_type=MESH,
            )
        )

    for chunk in ready:
        spread(chunk)
    for one in gain_copies:
        one.wait()
    mine[rank] = sum(from_group[g] for g in range(8))
    rep_copies = []
    for step in range(1, 4):
        target = (rank + step) % 4
        rep_copies.append(
            send(2, step, mine.at[rank], from_rep.at[step], {"rep": target})
        )
        rep_copies[-1].start()
    for step, one in zip(range(1, 4), rep_copies):
        one.wait()
        mine[(rank + 4 - step) % 4] = from_rep[step]
    gains_out_ref[...] = (mine[0] + mine[1]) + (mine[2] + mine[3])
    for settled in range(line.ticks - LAG):
        if line.first + settled + LAG == CHUNKS - QKV:
            for one in qkv_copies:
                one.wait()
            moves.open.pop(0).wait()
        line.step()
        chunk = line.first + settled - 2 * LAG
        if chunk in later:
            spread(chunk)
    line.end()
    for one in waits:
        one.wait_send()
        one.wait_recv()
    moves.finish()


def tail(qkv_term, gains, chunks, inner, number, sums, ticks, arrays, picks):
    first = sums.tick
    ready = sorted(chunks)
    later = [c for c in line_slots(first, ticks) if c < DOWN + GATE_UP]
    _, high, width = sums.shape
    wide = jax.ShapeDtypeStruct((GATE_UP // 2 * high, 8 * inner), bf16)
    moved = jax.ShapeDtypeStruct((2, 8, 2 * high, 2 * width), bf16)
    picks = dict(picks)
    for n in range(QKV):
        where = (
            n // 4, slice(None), slice(n // 2 % 2 * high, (n // 2 % 2 + 1) * high),
            slice(n % 2 * width, (n % 2 + 1) * width),
        )
        picks[CHUNKS - QKV + n] = ("qkv", lambda ref, where=where: ref.at[where])
    return run(
        functools.partial(tail_kernel, ready, later),
        [(qkv_term, ANY), (gains, VMEM)] + [(chunks[c], ANY) for c in ready],
        [(wide, ANY), (wide, ANY), (moved, ANY), (jax.ShapeDtypeStruct(gains.shape[1:], f32), VMEM)],
        [
            pltpu.VMEM(gains.shape, f32),
            pltpu.VMEM((4,) + gains.shape[1:], f32),
            pltpu.VMEM((4,) + gains.shape[1:], f32),
            pltpu.SemaphoreType.DMA((3, 7)),
            pltpu.SemaphoreType.DMA((3, 7)),
            pltpu.SemaphoreType.DMA((2, GATE_UP)),
            pltpu.SemaphoreType.DMA((1 + GATE_UP,)),
        ],
        number, (0, 200 * 8 * high * width * 2, 0), sums=sums, ticks=ticks, arrays=arrays, picks=picks,
    )


def finish_kernel(heads, *refs):
    chunks, rest = refs[: DOWN + OUT + QKV], refs[DOWN + OUT + QKV :]
    gate_rows, up_rows = rest[:2]
    query, key, value, out, gate, up, down = rest[2:9]
    low, wide, load_sems, store_sems = rest[9:]
    _, high, width = chunks[0].shape
    depth = low.shape[0]

    def half(number):
        return slice(number * high, (number + 1) * high)

    def side(number):
        return slice(number * width, (number + 1) * width)

    jobs = []
    for n, ref in enumerate(chunks[:DOWN]):
        jobs.append((ref, [(slice(0, width), down.at[n // 2, :, :, side(n % 2)])]))
    for ref, into in ((gate_rows, gate), (up_rows, up)):
        for low_col in range(0, ref.shape[2], low.shape[3]):
            for number in (0, 1):
                where = (slice(None), half(number), slice(low_col, low_col + low.shape[3]))
                jobs.append((ref.at[where], [(slice(0, low.shape[3]), into.at[where])]))
    for n, ref in enumerate(chunks[DOWN : DOWN + OUT]):
        jobs.append((ref, [(slice(0, width), out.at[:, half(n // 2), side(n % 2)])]))
    part = (heads + 2) * HD
    for n, ref in enumerate(chunks[DOWN + OUT :]):
        stores = []
        for place in range(width // part):
            at, device = place * part, (n // 4 * 2 + n % 2) * (width // part) + place
            for into, first, size in (
                (query, 0, heads * HD), (key, heads * HD, HD), (value, (heads + 1) * HD, HD)
            ):
                there = into.at[:, half(n // 2 % 2), device * size : (device + 1) * size]
                stores.append((slice(at + first, at + first + size), there))
        jobs.append((ref, stores))

    def load(number):
        at, ref = number % depth, jobs[number][0]
        return pltpu.make_async_copy(ref, low.at[at, :, :, : ref.shape[2]], load_sems.at[at])

    def stores(number):
        at = number % depth
        return [
            pltpu.make_async_copy(wide.at[at, :, :, cols], into, store_sems.at[at, which])
            for which, (cols, into) in enumerate(jobs[number][1])
        ]

    for number in range(depth - 1):
        load(number).start()
    for number in range(len(jobs)):
        if number + depth - 1 < len(jobs):
            load(number + depth - 1).start()
        load(number).wait()
        if number >= depth:
            for one in stores(number - depth):
                one.wait()

        def cast(g, _, at=number % depth, cols=slice(0, jobs[number][0].shape[2])):
            wide[at, g, :, cols] = low[at, g, :, cols].astype(f32)
            return 0

        lax.fori_loop(0, low.shape[1], cast, 0)
        for one in stores(number):
            one.start()
    for number in range(len(jobs) - depth, len(jobs)):
        for one in stores(number):
            one.wait()


def finish(chunks, gate_rows, up_rows, heads):
    eight, high, width = chunks[0].shape
    width = 2 * width
    rows, wide = gate_rows.shape

    def split(columns):
        return jax.ShapeDtypeStruct((eight, rows // eight, columns), f32)

    shapes = [split(columns) for columns in (8 * heads * HD, 8 * HD, 8 * HD, width, wide, wide)]
    shapes.append(jax.ShapeDtypeStruct((DOWN // 2, eight, high, width), f32))
    depth = 12
    results = pl.pallas_call(
        functools.partial(finish_kernel, heads),
        out_shape=tuple(shapes),
        in_specs=[pl.BlockSpec(memory_space=pl.ANY)] * (len(chunks) + 2),
        out_specs=tuple([pl.BlockSpec(memory_space=pl.ANY)] * 7),
        scratch_shapes=[
            pltpu.VMEM((depth, eight, high, width), bf16),
            pltpu.VMEM((depth, eight, high, width), f32),
            pltpu.SemaphoreType.DMA((depth,)),
            pltpu.SemaphoreType.DMA((depth, 12)),
        ],
        compiler_params=pltpu.CompilerParams(vmem_limit_bytes=60 * 2**20),
        cost_estimate=pl.CostEstimate(
            flops=0, bytes_accessed=3 * CHUNKS * eight * high * width, transcendentals=0
        ),
    )(
        *chunks, gate_rows.reshape(eight, rows // eight, wide),
        up_rows.reshape(eight, rows // eight, wide),
    )
    flat = [result.reshape(rows, -1) for result in results[:6]]
    return flat + [results[6].reshape(-1, width)]


def sum_over_sequences(term):
    return lax.psum(term, "rep").astype(f32)


def on_device(
    layer_input,
    cotangent,
    cut_order,
    piece_ids,
    w_query,
    w_key,
    w_value,
    w_out,
    w_gate,
    w_up,
    w_down,
    gain_attn,
    gain_ffn,
):
    groups = lax.axis_size("grp")
    reps = lax.axis_size("rep")
    own_index = lax.axis_index("grp")
    _, local_rows, model_width = layer_input.shape
    length = piece_ids.shape[1]
    rows_here = w_query.shape[0]
    q_width = w_query.shape[1]
    kv_heads = w_key.shape[1] // HD
    heads = q_width // HD // groups
    copies = groups // kv_heads
    hidden_here = w_down.shape[0]
    cosine, sine = turn_tables(length)

    near = groups == 8 and reps == 4 and copies == 1 and 2 * hidden_here == model_width

    def gather(rows):
        return lax.all_gather(rows, "grp", axis=0, tiled=True)

    def scatter(first, second, turned):
        term = against_rows(first, second) if turned else matmul_f32(first, second)
        return lax.psum_scatter(
            term.astype(bf16), "grp", scatter_dimension=0, tiled=True
        ).astype(f32)

    def to_columns(parts):
        return lax.all_to_all(parts, "grp", 1, 0, tiled=True).reshape(-1, parts.shape[-1])

    def per_group(weight):
        return weight.reshape(rows_here, groups, -1)

    def per_kv_head(weight):
        return jnp.repeat(weight.reshape(rows_here, kv_heads, HD), copies, axis=1)

    x_rows = layer_input.reshape(local_rows, model_width)
    x_flat = x_rows.astype(f32)
    inv_one = lax.rsqrt(jnp.mean(x_flat * x_flat, -1, keepdims=True) + EPS)
    unit_one = x_flat * inv_one
    attn_gain, ffn_gain = gain_attn.reshape(1, -1), gain_ffn.reshape(1, -1)
    if near:
        share = rows_here // (4 * reps) * 3
        spread = columns_of_some((w_gate, w_up), share, 11)
        x_first, spread = lax.optimization_barrier((x_rows, spread))
        spread = lax.all_gather(spread, "rep", axis=0)
        normed_one, cols_qkv = gather_normed(
            x_first, attn_gain, (w_query, w_key, w_value), number=1
        )
        last_gate, last_up, normed_one = lax.optimization_barrier(
            (w_gate[reps * share :], w_up[reps * share :], normed_one)
        )
        rest = to_columns(
            jnp.concatenate(
                [part.reshape(rows_here - reps * share, groups, -1) for part in (last_gate, last_up)],
                -1,
            )
        ).reshape(groups, rows_here - reps * share, -1)
    else:
        normed_one = gather(rms_normed(x_flat, attn_gain).astype(bf16))
        cols_qkv = to_columns(
            jnp.concatenate([per_group(w_query), per_kv_head(w_key), per_kv_head(w_value)], -1)
        )
        cols_gate_up = to_columns(jnp.concatenate([per_group(w_gate), per_group(w_up)], -1))
    attended, query, key, value, lse, attended_placed = attend(
        cut_order, normed_one, cols_qkv, cosine, sine, piece_ids, heads
    )
    if near:
        mid = product_scattered(attended, w_out, False, base=x_rows, number=2)[0]
    else:
        mid = x_flat + scatter(attended, w_out, False)
    grad_out = cotangent.reshape(local_rows, model_width)

    back_ins, back_scratch = attend_back_operands(
        cut_order, attended_placed, query, key, value, lse, cosine, sine, piece_ids, heads
    )
    q_here = heads * HD
    if near:
        normed_two, hidden, cols_gate_up, grad_gate_up, down_term = feed_forward(
            mid, ffn_gain, grad_out, spread, rest, w_down, number=3
        )
        cols_gate_up = cols_gate_up.reshape(model_width, -1)
        high, half_width = 2 * rows_here // GATE_UP, model_width // 2
        sums = Sums((8, high, half_width))
        terms = {"down": down_term.reshape(DOWN // 2, 8, high, model_width)}

        def pick_whole(n):
            return "down", lambda ref: ref.at[n // 2, :, :, n % 2 * half_width : (n % 2 + 1) * half_width]

        def pick_rows(name, n):
            rows, side = n // 2 * high, n % 2 * half_width
            return name, lambda ref: ref.at[:, rows : rows + high, side : side + half_width]

        picks = [pick_whole(n) for n in range(DOWN)]
        picks += [pick_rows("gate_up", n) for n in range(GATE_UP)]
        picks += [pick_rows("out", n) for n in range(OUT)]

        def line(number, ticks):
            names = sorted(
                {picks[t][0] for t in range(sums.tick, sums.tick + ticks) if t < len(picks)}
            )
            return dict(
                number=number, ticks=ticks, sums=sums, picks=dict(enumerate(picks)),
                arrays=[(name, terms[name]) for name in names],
            )

        result, terms["gate_up"] = product_scattered(
            hidden, w_down, False, extra=(normed_two, grad_gate_up), base=mid, dtype=bf16,
            steps={1: 1, 3: 1, "early": 1, 7: 1, "late": 1, "later": 1, "latest": 1}, **line(5, 9),
        )
        grad_mid, gain_ffn_term = product_scattered(
            grad_gate_up, cols_gate_up, True, back=(grad_out, mid, ffn_gain),
            steps={0: 1, 2: 1, 3: 1, 4: 1, 5: 1, 7: 1, 12: 1}, **line(6, 10),
        )
        grad_qkv, out_term = attention_back(
            grad_mid, w_out, attended, back_ins, back_scratch, heads, **line(7, 15)
        )
        terms["out"] = out_term.reshape(8, OUT // 2 * high, model_width)
        grad_x, gain_attn_term, qkv_term = product_scattered(
            grad_qkv, cols_qkv, True, extra=(normed_one, None), dtype=bf16,
            back=(grad_mid, x_rows, attn_gain),
            steps={3: 1, "early": 1, 5: 1, "late": 1, "latest": 1}, **line(9, 8),
        )
        gains = jnp.stack([gain_attn_term, gain_ffn_term]).reshape(2, groups, rows_here)
        gains = jnp.pad(jnp.moveaxis(gains, 0, 1), ((0, 0), (0, 6), (0, 0)))
        rest = line(10, CHUNKS + 2 * LAG - sums.tick)
        gate_rows, up_rows, qkv_rows, own_gains = tail(
            qkv_term.reshape(8, 8, 2 * high, -1), gains,
            {c: sums.done[c] for c in sums.done if c >= DOWN}, hidden_here, **rest,
        )
        straight = [n for n in range(CHUNKS) if n < DOWN or n >= DOWN + GATE_UP]
        weight_grads = finish([sums.done[n] for n in straight], gate_rows, up_rows, heads)
        shaped = tuple(rows.reshape(layer_input.shape) for rows in (result, grad_x))
        return shaped + tuple(weight_grads) + (own_gains[0], own_gains[1])

    unit_one = x_flat * inv_one
    inv_two = lax.rsqrt(jnp.mean(mid * mid, -1, keepdims=True) + EPS)
    unit_two = mid * inv_two
    normed_two = gather((unit_two * ffn_gain).astype(bf16))
    grad_all = gather(grad_out)
    gate_up = matmul_f32(normed_two, cols_gate_up)
    gate_proj, up_proj = gate_up[:, :hidden_here], gate_up[:, hidden_here:]
    sigmoid_gate = jax.nn.sigmoid(gate_proj)
    swish = gate_proj * sigmoid_gate
    hidden = (swish * up_proj).astype(bf16)
    gate_part = up_proj * sigmoid_gate * (1.0 + gate_proj * (1.0 - sigmoid_gate))
    down_term = over_tokens(hidden, grad_all).astype(bf16)
    grad_hidden = against_rows(grad_all, w_down)
    grad_gate_up = jnp.concatenate([grad_hidden * gate_part, grad_hidden * swish], 1).astype(bf16)
    grad_mid, gain_ffn_term = norm_back(
        grad_out.astype(f32), scatter(grad_gate_up, cols_gate_up, True), unit_two, inv_two, gain_ffn
    )
    grad_mid_low = gather(grad_mid.astype(bf16))
    grad_attended = against_rows(grad_mid_low, w_out).astype(bf16)
    grad_qkv = attend_back(grad_attended, back_ins, back_scratch, heads)
    grad_x, gain_attn_term = norm_back(
        grad_mid, scatter(grad_qkv, cols_qkv, True), unit_one, inv_one, gain_attn
    )

    def to_rows(term):
        return lax.all_to_all(
            term.astype(bf16).reshape(groups, rows_here, -1), "grp", 0, 0, tiled=True
        )

    def whole_rows(term):
        return jnp.moveaxis(term, 0, 1).reshape(rows_here, -1)

    def kv_rows(term):
        return jnp.sum(
            jnp.moveaxis(term, 0, 1).reshape(rows_here, kv_heads, copies, HD), 2
        ).reshape(rows_here, -1)

    gate_up_term = sum_over_sequences(to_rows(over_tokens(normed_two, grad_gate_up)))
    out_term = sum_over_sequences(over_tokens(attended, grad_mid_low).astype(bf16))
    qkv_term = sum_over_sequences(to_rows(over_tokens(normed_one, grad_qkv)))
    gain_total = lax.psum(jnp.stack([gain_attn_term, gain_ffn_term]), ("grp", "rep"))
    own_gains = lax.dynamic_slice_in_dim(gain_total, own_index * rows_here, rows_here, 1)
    return (
        (mid + scatter(hidden, w_down, False)).astype(bf16).reshape(layer_input.shape),
        grad_x.astype(bf16).reshape(layer_input.shape),
        whole_rows(qkv_term[..., :q_here]),
        kv_rows(qkv_term[..., q_here : q_here + HD]),
        kv_rows(qkv_term[..., q_here + HD :]),
        out_term,
        whole_rows(gate_up_term[..., :hidden_here]),
        whole_rows(gate_up_term[..., hidden_here:]),
        sum_over_sequences(down_term),
        own_gains[0],
        own_gains[1],
    )


def solution(mesh):
    tokens, table, rows, whole = P("rep", "grp", None), P("rep", None), P("grp", None), P()
    return jax.shard_map(
        on_device,
        mesh=mesh,
        in_specs=(tokens, tokens, table, table) + (rows,) * 7 + (whole,) * 2,
        out_specs=(tokens, tokens) + (rows,) * 7 + (P("grp"),) * 2,
        check_vma=False,
    )
```
